32 devices in a mesh: dp: 2 (over core), fsdp: 16 (over z, y, x).
Axes of the slice: x: 2, y: 2, z: 4, core: 2. Of those that a mesh axis runs over, the one named last changes fastest.
Arguments:
- table: bfloat16 [32768, 768], P(('dp', 'fsdp')), may hold values from -6 to 6
- token_ids: int32 [384, 64], P(('dp', 'fsdp')), may hold values from 0 to 32767, as said below
- sent_lengths: int32 [384], P(('dp', 'fsdp')), may hold values from 2 to 64, as said below
- pair_slot: int32 [384], replicated, may hold values from 0 to 383, as said below
- pair_lang: int32 [192], replicated, may hold values from 0 to 108, as said below
- w_query: bfloat16 [768, 768], P('fsdp'), may hold values from -0.21875 to 0.21875
- b_query: bfloat16 [768], P('fsdp'), may hold values from -3 to 3
- w_key: bfloat16 [768, 768], P('fsdp'), may hold values from -0.21875 to 0.21875
- w_value: bfloat16 [768, 768], P('fsdp'), may hold values from -0.21875 to 0.21875
- b_value: bfloat16 [768], P('fsdp'), may hold values from -3 to 3
- w_out: bfloat16 [768, 768], P('fsdp'), may hold values from -1.25 to 1.25
- b_out: bfloat16 [768], P('fsdp'), may hold values from -3 to 3
- ln1_gain: bfloat16 [768], P('fsdp'), may hold values from 0.5 to 1.5
- ln1_bias: bfloat16 [768], P('fsdp'), may hold values from -2 to 2
- w_up: bfloat16 [768, 3072], P('fsdp'), may hold values from -0.21875 to 0.21875
- b_up: bfloat16 [3072], P('fsdp'), may hold values from -3 to 3
- w_down: bfloat16 [3072, 768], P('fsdp'), may hold values from -0.109375 to 0.109375
- b_down: bfloat16 [768], P('fsdp'), may hold values from -3 to 3
- ln2_gain: bfloat16 [768], P('fsdp'), may hold values from 0.5 to 1.5
- ln2_bias: bfloat16 [768], P('fsdp'), may hold values from -2 to 2
Outputs:
- layer_out: bfloat16 [384, 64, 768], P(('dp', 'fsdp'))
- loss_value: float32 [], replicated
- table_grad: float32 [32768, 768], P(('dp', 'fsdp'))
- grad_w_query: float32 [768, 768], P('fsdp')
- grad_b_query: float32 [768], P('fsdp')
- grad_w_key: float32 [768, 768], P('fsdp')
- grad_w_value: float32 [768, 768], P('fsdp')
- grad_b_value: float32 [768], P('fsdp')
- grad_w_out: float32 [768, 768], P('fsdp')
- grad_b_out: float32 [768], P('fsdp')
- grad_ln1_gain: float32 [768], P('fsdp')
- grad_ln1_bias: float32 [768], P('fsdp')
- grad_w_up: float32 [768, 3072], P('fsdp')
- grad_b_up: float32 [3072], P('fsdp')
- grad_w_down: float32 [3072, 768], P('fsdp')
- grad_b_down: float32 [768], P('fsdp')
- grad_ln2_gain: float32 [768], P('fsdp')
- grad_ln2_bias: float32 [768], P('fsdp')
The draws below stay inside these ranges and needn't reach their ends.
Inputs may be any that keep to these rules, and one draw needn't show every extreme that they name: `token_ids`: among the 768 tokens of one device, at most 48 name rows of any one aligned block of 1024 table rows, and on every device some block is named exactly 48 times. `sent_lengths`: position 0 of a sentence is its summary token; positions at or past its length are padding. Some sentence has length exactly 64. `pair_slot`: each value appears once; slots 2 p and 2 p + 1 are the two sides of translation pair p. `pair_lang`: language pairs have uneven counts of translation pairs.
All inputs are finite; a program needn't handle non-finite values.
Results may differ from the reference program's by a relative error of at most 0.028.
The reference program's roundings to bfloat16 on the way count: a program that leaves them out, or rounds other values in their place, can miss the bound.
Values may be sent and summed in bfloat16 or wider, within the bound.
A program may use at most 192 MiB of HBM per device.

```python
import math
from functools import partial
import jax
import jax.numpy as jnp
from jax import lax

D = 768
FF = 3072
HEADS = 12
HEAD = 64
SEQ = 64
SENT_DEV = 12
VOCAB_DEV = 1024
LANGS = 109
OWNERS = 32
TOK_DEV = 768
SENTS = 384
PAIRS = 192
VOCAB = 32768
CAP = 48


def draw_token_ids(key, part):
    key = jax.random.fold_in(key, 11)
    key_forced, key_blocks = jax.random.split(key, 2)
    blocks = SENTS // SENT_DEV
    slot_total = OWNERS * CAP
    forced = jax.random.randint(key_forced, (blocks,), 0, OWNERS)

    def one_block(inner_key, owner):
        key_slots, key_order, key_rows = jax.random.split(inner_key, 3)
        others = (owner * CAP + CAP + jax.random.permutation(key_slots, slot_total - CAP)) % slot_total
        chosen = jnp.concatenate([owner * CAP + jnp.arange(CAP, dtype=jnp.int32), others[:TOK_DEV - CAP].astype(jnp.int32)])
        chosen = jax.random.permutation(key_order, chosen)
        rows_in = jax.random.randint(key_rows, (TOK_DEV,), 0, VOCAB_DEV)
        return chosen // CAP * VOCAB_DEV + rows_in
    identifiers = jax.vmap(one_block)(jax.random.split(key_blocks, blocks), forced)
    return identifiers.reshape(SENTS, SEQ).astype(jnp.int32)


def draw_sent_lengths(key, part):
    key = jax.random.fold_in(key, 23)
    key_caps, key_lens, key_pick = jax.random.split(key, 3)
    blocks = SENTS // SENT_DEV
    device_cap = jax.random.randint(key_caps, (blocks, 1), 2, SEQ + 1)
    lengths = jax.random.randint(key_lens, (blocks, SENT_DEV), 2, device_cap + 1).reshape(SENTS)
    longest = jax.random.randint(key_pick, (), 0, SENTS)
    lengths = jnp.where(jnp.arange(SENTS) == longest, SEQ, lengths)
    return lengths.astype(jnp.int32)


def draw_pair_slot(key, part):
    key = jax.random.fold_in(key, 37)
    blocks = SENTS // SENT_DEV
    half_count = SENT_DEV // 2
    device_ids = jnp.arange(blocks, dtype=jnp.int32)[:, None]
    within = jnp.arange(half_count, dtype=jnp.int32)[None, :]
    first_side = 2 * (device_ids * half_count + within)
    second_side = 2 * ((device_ids - 1) % blocks * half_count + within) + 1
    slots = jnp.concatenate([first_side, second_side], axis=1)

    def shuffle(inner_key, row):
        return jax.random.permutation(inner_key, row)
    slots = jax.vmap(shuffle)(jax.random.split(key, blocks), slots)
    return slots.reshape(SENTS).astype(jnp.int32)


def draw_pair_lang(key, part):
    key = jax.random.fold_in(key, 41)
    jitter = jax.random.randint(key, (PAIRS,), 0, PAIRS // 8 + 1)
    spot = jnp.arange(PAIRS, dtype=jnp.int32) + jitter
    language = LANGS * spot * spot // (PAIRS * PAIRS)
    return jnp.minimum(language, LANGS - 1).astype(jnp.int32)


def levels(stream_key, extent, cuts, low, largest):
    gain = 1.0
    for position, parts in cuts:
        steps = jax.random.uniform(jax.random.fold_in(jax.random.fold_in(stream_key, 6), position), (parts,), jnp.float32, low / len(cuts), largest / len(cuts))
        gain = gain * jnp.repeat(jnp.exp(steps), extent[position] // parts).reshape((-1,) + (1,) * (len(extent) - 1 - position))
    return gain


def centred(key, dims, width, limit, cuts=(), held_as=jnp.bfloat16):
    array = width * jax.random.normal(key, dims, jnp.float32)
    if cuts:
        array = array * levels(key, dims, cuts, -0.22, 0.18)
    return jnp.clip(array, -limit, limit).astype(held_as)


def setup_inputs(seed: int = 0) -> dict:
    keys = jax.random.split(jax.random.key(seed), 21)
    return {
        "table": centred(keys[0], (VOCAB, D), 1.0, 6.0, ((0, 32),)),
        "token_ids": draw_token_ids(jax.random.fold_in(keys[20], 71), 0),
        "sent_lengths": draw_sent_lengths(jax.random.fold_in(keys[20], 71), 0),
        "pair_slot": draw_pair_slot(jax.random.fold_in(keys[20], 71), 0),
        "pair_lang": draw_pair_lang(jax.random.fold_in(keys[20], 71), 0),
        "w_query": centred(keys[5], (D, D), D ** -0.5, 0.21875, ((0, 16),)),
        "b_query": centred(keys[6], (D,), 0.5, 3.0, ((0, 16),)),
        "w_key": centred(keys[7], (D, D), D ** -0.5, 0.21875, ((0, 16),)),
        "w_value": centred(keys[8], (D, D), D ** -0.5, 0.21875, ((0, 16),)),
        "b_value": centred(keys[9], (D,), 0.5, 3.0, ((0, 16),)),
        "w_out": centred(keys[10], (D, D), (2 * D // SEQ) ** -0.5, 1.25, ((0, 16),)),
        "b_out": centred(keys[11], (D,), 0.5, 3.0, ((0, 16),)),
        "ln1_gain": jnp.clip(1.0 + 0.1 * jax.random.normal(keys[12], (D,), jnp.float32), 0.5, 1.5).astype(jnp.bfloat16),
        "ln1_bias": centred(keys[13], (D,), 0.3, 2.0, ((0, 16),)),
        "w_up": centred(keys[14], (D, FF), D ** -0.5, 0.21875, ((0, 16),)),
        "b_up": centred(keys[15], (FF,), 0.5, 3.0, ((0, 16),)),
        "w_down": centred(keys[16], (FF, D), FF ** -0.5, 0.109375, ((0, 16),)),
        "b_down": centred(keys[17], (D,), 0.5, 3.0, ((0, 16),)),
        "ln2_gain": jnp.clip(1.0 + 0.1 * jax.random.normal(keys[18], (D,), jnp.float32), 0.5, 1.5).astype(jnp.bfloat16),
        "ln2_bias": centred(keys[19], (D,), 0.3, 2.0, ((0, 16),)),
    }


EPSILON = 1e-06
SCORE_SCALE = 50.0
MARGIN_WIDTH = 0.3
MASK_FLOOR = -1000000000.0
PRECISE = lax.Precision.HIGHEST

@jax.custom_vjp
def low(v):
    return lax.optimization_barrier(v.astype(jnp.bfloat16)).astype(jnp.float32)

@jax.custom_vjp
def low_back(v):
    return v

def low_keep(v):
    return (low(v), None)

def low_pass(kept, grad):
    return (grad,)

def back_keep(v):
    return (v, None)

def back_low(kept, grad):
    return (low(grad),)
low.defvjp(low_keep, low_pass)
low_back.defvjp(back_keep, back_low)

def product(left_side, right_side):
    return jnp.dot(left_side, right_side, precision=PRECISE, preferred_element_type=jnp.float32)

def layer_norm(inputs, ln_gain, ln_shift):
    row_mean = lax.optimization_barrier(jnp.mean(inputs, axis=-1, keepdims=True))
    centered = inputs - row_mean
    variance = lax.optimization_barrier(jnp.mean(centered * centered, axis=-1, keepdims=True))
    return centered * lax.rsqrt(variance + EPSILON) * ln_gain + ln_shift

def softmax_rows(scores):
    row_peak = lax.optimization_barrier(jnp.max(scores, axis=-1, keepdims=True))
    shifted = jnp.exp(scores - row_peak)
    return shifted / lax.optimization_barrier(jnp.sum(shifted, axis=-1, keepdims=True))

def sentence_block(params, inputs):
    w_query, b_query, w_key, w_value, b_value, w_out, b_out, ln1_gain, ln1_bias, w_up, b_up, w_down, b_down, ln2_gain, ln2_bias = params
    embedded, valid_mask = inputs
    sent_count, length, model_width = embedded.shape
    head_shape = (sent_count, length, HEADS, HEAD)
    queries = low_back(low(product(embedded, w_query) + b_query)).reshape(head_shape)
    keys_all = low_back(low(product(embedded, w_key))).reshape(head_shape)
    values_all = low_back(low(product(embedded, w_value) + b_value)).reshape(head_shape)
    scores = low_back(jnp.einsum('bqhd,bkhd->bhqk', queries, keys_all, precision=PRECISE) * HEAD ** (-0.5))
    scores = jnp.where(valid_mask[:, None, None, :] > 0, scores, MASK_FLOOR)
    attn_probs = low(softmax_rows(scores))
    context = jnp.einsum('bhqk,bkhd->bqhd', attn_probs, values_all, precision=PRECISE)
    context = low_back(low(context.reshape(sent_count, length, model_width)))
    attended = low_back(product(context, w_out) + b_out)
    hidden = layer_norm(embedded + attended, ln1_gain, ln1_bias)
    up_pre = low_back(product(low(hidden), w_up) + b_up)
    down_out = low_back(product(low(jax.nn.gelu(up_pre, approximate=False)), w_down) + b_down)
    second = layer_norm(hidden + down_out, ln2_gain, ln2_bias) * valid_mask[:, :, None]
    summary = second[:, 0]
    unit_vector = summary / jnp.sqrt(lax.optimization_barrier(jnp.sum(summary * summary, axis=-1, keepdims=True)) + EPSILON)
    return (low(unit_vector), second)

def model_loss(params, table_full, token_ids, valid_mask, pair_slot, sent_weight):
    embedded = table_full[token_ids]
    block_rows = math.gcd(SENTS, 64)
    blocks = SENTS // block_rows
    units, outputs = lax.map(jax.checkpoint(partial(sentence_block, params)), (embedded.reshape(blocks, block_rows, SEQ, D), valid_mask.reshape(blocks, block_rows, SEQ)))
    units = units.reshape(SENTS, D)
    raw_scores = low_back(SCORE_SCALE * product(units, units.T))
    side_of = pair_slot % 2
    pair_of = pair_slot // 2
    opposite = side_of[:, None] != side_of[None, :]
    partner = opposite & (pair_of[:, None] == pair_of[None, :])
    pair_scores = jnp.where(partner, raw_scores - SCORE_SCALE * MARGIN_WIDTH, raw_scores)
    pair_scores = jnp.where(opposite, pair_scores, MASK_FLOOR)
    log_total = jax.nn.logsumexp(pair_scores, axis=1)
    picked = lax.optimization_barrier(jnp.sum(jnp.where(partner, pair_scores, 0.0), axis=1))
    return (jnp.sum(sent_weight * (log_total - picked)), outputs.reshape(SENTS, SEQ, D))

def sentence_weights(pair_slot, pair_lang):
    per_lang = lax.optimization_barrier(jnp.sum((pair_lang[:, None] == jnp.arange(LANGS, dtype=jnp.int32)[None, :]).astype(jnp.float32), axis=0))
    per_pair = 1.0 / (2.0 * LANGS * jnp.take(per_lang, pair_lang))
    return jnp.take(per_pair, pair_slot // 2)

def reference(table, token_ids, sent_lengths, pair_slot, pair_lang, w_query, b_query, w_key, w_value, b_value, w_out, b_out, ln1_gain, ln1_bias, w_up, b_up, w_down, b_down, ln2_gain, ln2_bias):
    params = tuple((weight.astype(jnp.float32) for weight in (w_query, b_query, w_key, w_value, b_value, w_out, b_out, ln1_gain, ln1_bias, w_up, b_up, w_down, b_down, ln2_gain, ln2_bias)))
    valid_mask = (jnp.arange(SEQ, dtype=jnp.int32)[None, :] < sent_lengths[:, None]).astype(jnp.float32)
    sent_weight = sentence_weights(pair_slot, pair_lang)
    loss_value, pullback, layer_full = jax.vjp(lambda weights, table_full: model_loss(weights, table_full, token_ids, valid_mask, pair_slot, sent_weight), params, table.astype(jnp.float32), has_aux=True)
    layer_out = layer_full.astype(jnp.bfloat16)
    grads, table_grad = pullback(jnp.ones_like(loss_value))
    return (layer_out, loss_value, table_grad, grads[0], grads[1], grads[2], grads[3], grads[4], grads[5], grads[6], grads[7], grads[8], grads[9], grads[10], grads[11], grads[12], grads[13], grads[14])
```

```python
from functools import partial

import jax
import jax.numpy as jnp
from jax import lax
from jax.experimental import pallas as pl
from jax.experimental.pallas import tpu as pltpu
from jax.sharding import PartitionSpec as P

HEADS = 12
HEAD = 64
LANGS = 109


EPSILON = 1e-06
SCORE_SCALE = 50.0
MARGIN_WIDTH = 0.3
MASK_FLOOR = -1000000000.0


def contract(left_side, right_side, left_dim, right_dim):
    return lax.dot_general(
        left_side,
        right_side,
        (((left_dim,), (right_dim,)), ((), ())),
        preferred_element_type=jnp.float32,
    )


def norm_rows(inputs, ln_gain, ln_shift):
    row_mean = jnp.mean(inputs, axis=-1, keepdims=True)
    centered = inputs - row_mean
    variance = jnp.mean(centered * centered, axis=-1, keepdims=True)
    inverse = lax.rsqrt(variance + EPSILON)
    normed = centered * inverse
    return (normed * ln_gain + ln_shift, normed, inverse)


def norm_back(grad_output, normed, inverse, ln_gain):
    grad_normed = grad_output * ln_gain
    first_term = jnp.mean(grad_normed, axis=-1, keepdims=True)
    second_term = jnp.mean(grad_normed * normed, axis=-1, keepdims=True)
    grad_input = inverse * (grad_normed - first_term - normed * second_term)
    return (grad_input, jnp.sum(grad_output * normed, axis=0), jnp.sum(grad_output, axis=0))


def general_body(
    table,
    token_ids,
    sent_lengths,
    pair_slot,
    pair_lang,
    w_query,
    b_query,
    w_key,
    w_value,
    b_value,
    w_out,
    b_out,
    ln1_gain,
    ln1_bias,
    w_up,
    b_up,
    w_down,
    b_down,
    ln2_gain,
    ln2_bias,
):
    sentences, length = token_ids.shape
    tokens = sentences * length
    vocab_rows, model_width = table.shape
    owners = lax.axis_size(("dp", "fsdp"))
    dp_count = lax.axis_size("dp")
    fsdp_count = lax.axis_size("fsdp")
    capacity = max(2, 2 * tokens // owners)
    device = lax.axis_index(("dp", "fsdp"))
    score_factor = HEAD ** (-0.5)
    flat_ids = token_ids.reshape(tokens)
    owner_of = flat_ids // vocab_rows
    member = (owner_of[:, None] == jnp.arange(owners, dtype=jnp.int32)[None, :]).astype(jnp.int32)
    owner_rank = jnp.sum(jnp.cumsum(member, axis=0) * member, axis=1) - 1
    slot_of = owner_of * capacity + owner_rank
    requests = jnp.full((owners * capacity,), -1, jnp.int32).at[slot_of].set(flat_ids)
    received = lax.all_to_all(
        lax.all_to_all(
            requests.reshape(dp_count, fsdp_count, capacity),
            "dp",
            split_axis=0,
            concat_axis=0,
            tiled=True,
        ),
        "fsdp",
        split_axis=1,
        concat_axis=1,
        tiled=True,
    )
    present = received >= 0
    local_rows = jnp.where(present, received - device * vocab_rows, 0)
    found_rows = jnp.where(present[..., None], table[local_rows], jnp.zeros((), table.dtype))
    replies = lax.all_to_all(
        lax.all_to_all(found_rows, "dp", split_axis=0, concat_axis=0, tiled=True),
        "fsdp",
        split_axis=1,
        concat_axis=1,
        tiled=True,
    )
    embedded = replies.reshape(owners * capacity, model_width)[slot_of]
    gathered = (
        lax.all_gather(w_query, "fsdp", axis=0, tiled=True),
        lax.all_gather(b_query, "fsdp", axis=0, tiled=True),
        lax.all_gather(w_key, "fsdp", axis=0, tiled=True),
        lax.all_gather(w_value, "fsdp", axis=0, tiled=True),
        lax.all_gather(b_value, "fsdp", axis=0, tiled=True),
        lax.all_gather(w_out, "fsdp", axis=0, tiled=True),
        lax.all_gather(b_out, "fsdp", axis=0, tiled=True),
        lax.all_gather(ln1_gain, "fsdp", axis=0, tiled=True),
        lax.all_gather(ln1_bias, "fsdp", axis=0, tiled=True),
        lax.all_gather(w_up, "fsdp", axis=0, tiled=True),
        lax.all_gather(b_up, "fsdp", axis=0, tiled=True),
        lax.all_gather(w_down, "fsdp", axis=0, tiled=True),
        lax.all_gather(b_down, "fsdp", axis=0, tiled=True),
        lax.all_gather(ln2_gain, "fsdp", axis=0, tiled=True),
        lax.all_gather(ln2_bias, "fsdp", axis=0, tiled=True),
    )
    (
        full_wq,
        full_bq,
        full_wk,
        full_wv,
        full_bv,
        full_wo,
        full_bo,
        full_g1,
        full_s1,
        full_wup,
        full_bup,
        full_wdown,
        full_bdown,
        full_g2,
        full_s2,
    ) = gathered
    valid_mask = jnp.arange(length, dtype=jnp.int32)[None, :] < sent_lengths[:, None]
    head_shape = (sentences, length, HEADS, HEAD)
    queries = (jnp.dot(embedded, full_wq, preferred_element_type=jnp.float32) + full_bq).astype(
        jnp.bfloat16
    )
    key_heads = (
        jnp.dot(embedded, full_wk, preferred_element_type=jnp.float32)
        .astype(jnp.bfloat16)
        .reshape(head_shape)
    )
    value_heads = (
        (jnp.dot(embedded, full_wv, preferred_element_type=jnp.float32) + full_bv)
        .astype(jnp.bfloat16)
        .reshape(head_shape)
    )
    query_heads = queries.reshape(head_shape)
    scores = (
        jnp.einsum("bqhd,bkhd->bhqk", query_heads, key_heads, preferred_element_type=jnp.float32)
        * score_factor
    )
    scores = jnp.where(valid_mask[:, None, None, :], scores, MASK_FLOOR)
    row_peak = jnp.max(scores, axis=-1, keepdims=True)
    shifted = jnp.exp(scores - row_peak)
    totals = jnp.sum(shifted, axis=-1, keepdims=True)
    attn_probs = (shifted / totals).astype(jnp.bfloat16)
    context = jnp.einsum(
        "bhqk,bkhd->bqhd", attn_probs, value_heads, preferred_element_type=jnp.float32
    )
    context = context.reshape(tokens, model_width).astype(jnp.bfloat16)
    attended = jnp.dot(context, full_wo, preferred_element_type=jnp.float32) + full_bo
    hidden, normed_one, inverse_one = norm_rows(
        embedded.astype(jnp.float32) + attended, full_g1, full_s1
    )
    hidden_low = hidden.astype(jnp.bfloat16)
    up_pre = jnp.dot(hidden_low, full_wup, preferred_element_type=jnp.float32) + full_bup
    activated = jax.nn.gelu(up_pre, approximate=False).astype(jnp.bfloat16)
    down_pre = jnp.dot(activated, full_wdown, preferred_element_type=jnp.float32) + full_bdown
    normed_out, normed_two, inverse_two = norm_rows(hidden + down_pre, full_g2, full_s2)
    layer_out = jnp.where(valid_mask.reshape(tokens)[:, None], normed_out, 0.0).astype(jnp.bfloat16)
    layer_out = layer_out.reshape(sentences, length, model_width)

    def first_rows(matrix):
        return matrix.reshape(sentences, length, matrix.shape[-1])[:, 0]

    summary = first_rows(normed_out)
    magnitude = jnp.sqrt(jnp.sum(summary * summary, axis=-1, keepdims=True) + EPSILON)
    unit_vector = summary / magnitude
    unit_low = unit_vector.astype(jnp.bfloat16)
    every_unit = lax.all_gather(unit_low, ("dp", "fsdp"), axis=0, tiled=True)
    every_side = pair_slot % 2
    every_pair = pair_slot // 2
    my_slots = lax.dynamic_slice_in_dim(pair_slot, device * sentences, sentences)
    my_side = my_slots % 2
    my_pair = my_slots // 2
    lang_onehot = (pair_lang[:, None] == jnp.arange(LANGS, dtype=jnp.int32)[None, :]).astype(
        jnp.float32
    )
    per_lang = jnp.sum(lang_onehot, axis=0)
    per_pair = 1.0 / (2.0 * LANGS * jnp.sum(lang_onehot * per_lang[None, :], axis=1))
    my_weight = jnp.take(per_pair, my_pair)
    opposite = my_side[:, None] != every_side[None, :]
    partner = opposite & (my_pair[:, None] == every_pair[None, :])
    raw_scores = SCORE_SCALE * contract(unit_low, every_unit, 1, 1)
    pair_scores = jnp.where(partner, raw_scores - SCORE_SCALE * MARGIN_WIDTH, raw_scores)
    pair_scores = jnp.where(opposite, pair_scores, MASK_FLOOR)
    pair_peak = jnp.max(pair_scores, axis=1, keepdims=True)
    pair_exp = jnp.exp(pair_scores - pair_peak)
    pair_total = jnp.sum(pair_exp, axis=1, keepdims=True)
    log_total = pair_peak[:, 0] + jnp.log(pair_total[:, 0])
    picked = jnp.sum(jnp.where(partner, pair_scores, 0.0), axis=1)
    loss_value = lax.psum(jnp.sum(my_weight * (log_total - picked)), ("dp", "fsdp"))
    coefficients = (
        my_weight[:, None] * (pair_exp / pair_total - partner.astype(jnp.float32))
    ).astype(jnp.bfloat16)
    unit_grad = SCORE_SCALE * contract(coefficients, every_unit, 1, 0)
    column_terms = SCORE_SCALE * contract(coefficients, unit_low, 0, 0)
    unit_grad = unit_grad + lax.psum_scatter(
        column_terms, ("dp", "fsdp"), scatter_dimension=0, tiled=True
    )
    along = jnp.sum(unit_vector * unit_grad, axis=-1, keepdims=True)
    summary_grad = (unit_grad - unit_vector * along) / magnitude
    again_weights = (
        lax.all_gather(w_query, "fsdp", axis=0, tiled=True),
        lax.all_gather(w_key, "fsdp", axis=0, tiled=True),
        lax.all_gather(w_value, "fsdp", axis=0, tiled=True),
        lax.all_gather(w_out, "fsdp", axis=0, tiled=True),
        lax.all_gather(ln1_gain, "fsdp", axis=0, tiled=True),
        lax.all_gather(w_up, "fsdp", axis=0, tiled=True),
        lax.all_gather(w_down, "fsdp", axis=0, tiled=True),
        lax.all_gather(ln2_gain, "fsdp", axis=0, tiled=True),
    )
    again_wq, again_wk, again_wv, again_wo, again_g1, again_wup, again_wdown, again_g2 = (
        again_weights
    )
    residual_grad, grad_g2, grad_s2 = norm_back(
        summary_grad, first_rows(normed_two), first_rows(inverse_two), again_g2
    )
    down_grad = residual_grad.astype(jnp.bfloat16)
    activated_cls = first_rows(activated)
    act_grad = contract(down_grad, again_wdown, 1, 1)
    gelu_value, gelu_pull = jax.vjp(partial(jax.nn.gelu, approximate=False), first_rows(up_pre))
    up_grad = gelu_pull(act_grad)[0].astype(jnp.bfloat16)
    hidden_cls = first_rows(hidden_low)
    hidden_grad = contract(up_grad, again_wup, 1, 1) + residual_grad
    first_grad, grad_g1, grad_s1 = norm_back(
        hidden_grad, first_rows(normed_one), first_rows(inverse_one), again_g1
    )
    attend_grad = first_grad.astype(jnp.bfloat16)
    context_cls = first_rows(context)
    context_grad = (
        contract(attend_grad, again_wo, 1, 1).astype(jnp.bfloat16).reshape(sentences, HEADS, HEAD)
    )
    query_cls = query_heads[:, 0]
    cls_scores = (
        jnp.einsum("bhd,bkhd->bhk", query_cls, key_heads, preferred_element_type=jnp.float32)
        * score_factor
    )
    cls_scores = jnp.where(valid_mask[:, None, :], cls_scores, MASK_FLOOR)
    cls_probs = jnp.exp(cls_scores - row_peak[:, :, 0]) / totals[:, :, 0]
    prob_grad = jnp.einsum(
        "bhd,bkhd->bhk", context_grad, value_heads, preferred_element_type=jnp.float32
    )
    score_grad = (
        cls_probs * (prob_grad - jnp.sum(cls_probs * prob_grad, axis=-1, keepdims=True))
    ).astype(jnp.bfloat16)
    query_grad = (
        (
            jnp.einsum("bhk,bkhd->bhd", score_grad, key_heads, preferred_element_type=jnp.float32)
            * score_factor
        )
        .astype(jnp.bfloat16)
        .reshape(sentences, model_width)
    )
    key_grad = (
        (
            jnp.einsum("bhk,bhd->bkhd", score_grad, query_cls, preferred_element_type=jnp.float32)
            * score_factor
        )
        .astype(jnp.bfloat16)
        .reshape(tokens, model_width)
    )
    value_grad = (
        jnp.einsum(
            "bhk,bhd->bkhd",
            cls_probs.astype(jnp.bfloat16),
            context_grad,
            preferred_element_type=jnp.float32,
        )
        .astype(jnp.bfloat16)
        .reshape(tokens, model_width)
    )
    embedded_cls = first_rows(embedded)
    grad_wkey = contract(embedded, key_grad, 0, 0)
    grad_wvalue = contract(embedded, value_grad, 0, 0)
    grad_bvalue = jnp.sum(value_grad, axis=0, dtype=jnp.float32)
    row_grads = contract(key_grad, again_wk, 1, 1) + contract(value_grad, again_wv, 1, 1)
    summary_extra = contract(query_grad, again_wq, 1, 1) + first_grad
    row_grads = (
        row_grads.reshape(sentences, length, model_width)
        .at[:, 0]
        .add(summary_extra)
        .reshape(tokens, model_width)
    )
    outgoing = jnp.zeros((owners * capacity, model_width), jnp.float32).at[slot_of].set(row_grads)
    incoming = lax.all_to_all(
        lax.all_to_all(
            outgoing.reshape(dp_count, fsdp_count, capacity, model_width).astype(jnp.bfloat16),
            "dp",
            split_axis=0,
            concat_axis=0,
            tiled=True,
        ),
        "fsdp",
        split_axis=1,
        concat_axis=1,
        tiled=True,
    ).astype(jnp.float32)
    incoming = jnp.where(
        present.reshape(owners * capacity)[:, None],
        incoming.reshape(owners * capacity, model_width),
        0.0,
    )
    table_grad = (
        jnp.zeros((vocab_rows, model_width), jnp.float32)
        .at[local_rows.reshape(owners * capacity)]
        .add(incoming)
    )
    grad_wquery = contract(embedded_cls, query_grad, 0, 0)
    grad_bquery = jnp.sum(query_grad, axis=0, dtype=jnp.float32)
    grad_wout = contract(context_cls, attend_grad, 0, 0)
    grad_bout = jnp.sum(attend_grad, axis=0, dtype=jnp.float32)
    grad_wup = contract(hidden_cls, up_grad, 0, 0)
    grad_bup = jnp.sum(up_grad, axis=0, dtype=jnp.float32)
    grad_wdown = contract(activated_cls, down_grad, 0, 0)
    grad_bdown = jnp.sum(down_grad, axis=0, dtype=jnp.float32)
    owned_grads = (
        lax.psum_scatter(
            grad_wquery.astype(jnp.bfloat16), "fsdp", scatter_dimension=0, tiled=True
        ).astype(jnp.float32),
        lax.psum_scatter(
            grad_bquery.astype(jnp.bfloat16), "fsdp", scatter_dimension=0, tiled=True
        ).astype(jnp.float32),
        lax.psum_scatter(
            grad_wkey.astype(jnp.bfloat16), "fsdp", scatter_dimension=0, tiled=True
        ).astype(jnp.float32),
        lax.psum_scatter(
            grad_wvalue.astype(jnp.bfloat16), "fsdp", scatter_dimension=0, tiled=True
        ).astype(jnp.float32),
        lax.psum_scatter(
            grad_bvalue.astype(jnp.bfloat16), "fsdp", scatter_dimension=0, tiled=True
        ).astype(jnp.float32),
        lax.psum_scatter(
            grad_wout.astype(jnp.bfloat16), "fsdp", scatter_dimension=0, tiled=True
        ).astype(jnp.float32),
        lax.psum_scatter(
            grad_bout.astype(jnp.bfloat16), "fsdp", scatter_dimension=0, tiled=True
        ).astype(jnp.float32),
        lax.psum_scatter(
            grad_g1.astype(jnp.bfloat16), "fsdp", scatter_dimension=0, tiled=True
        ).astype(jnp.float32),
        lax.psum_scatter(
            grad_s1.astype(jnp.bfloat16), "fsdp", scatter_dimension=0, tiled=True
        ).astype(jnp.float32),
        lax.psum_scatter(
            grad_wup.astype(jnp.bfloat16), "fsdp", scatter_dimension=0, tiled=True
        ).astype(jnp.float32),
        lax.psum_scatter(
            grad_bup.astype(jnp.bfloat16), "fsdp", scatter_dimension=0, tiled=True
        ).astype(jnp.float32),
        lax.psum_scatter(
            grad_wdown.astype(jnp.bfloat16), "fsdp", scatter_dimension=0, tiled=True
        ).astype(jnp.float32),
        lax.psum_scatter(
            grad_bdown.astype(jnp.bfloat16), "fsdp", scatter_dimension=0, tiled=True
        ).astype(jnp.float32),
        lax.psum_scatter(
            grad_g2.astype(jnp.bfloat16), "fsdp", scatter_dimension=0, tiled=True
        ).astype(jnp.float32),
        lax.psum_scatter(
            grad_s2.astype(jnp.bfloat16), "fsdp", scatter_dimension=0, tiled=True
        ).astype(jnp.float32),
    )
    summed = (
        lax.psum(owned_grads[0].astype(jnp.bfloat16), "dp").astype(jnp.float32),
        lax.psum(owned_grads[1].astype(jnp.bfloat16), "dp").astype(jnp.float32),
        lax.psum(owned_grads[2].astype(jnp.bfloat16), "dp").astype(jnp.float32),
        lax.psum(owned_grads[3].astype(jnp.bfloat16), "dp").astype(jnp.float32),
        lax.psum(owned_grads[4].astype(jnp.bfloat16), "dp").astype(jnp.float32),
        lax.psum(owned_grads[5].astype(jnp.bfloat16), "dp").astype(jnp.float32),
        lax.psum(owned_grads[6].astype(jnp.bfloat16), "dp").astype(jnp.float32),
        lax.psum(owned_grads[7].astype(jnp.bfloat16), "dp").astype(jnp.float32),
        lax.psum(owned_grads[8].astype(jnp.bfloat16), "dp").astype(jnp.float32),
        lax.psum(owned_grads[9].astype(jnp.bfloat16), "dp").astype(jnp.float32),
        lax.psum(owned_grads[10].astype(jnp.bfloat16), "dp").astype(jnp.float32),
        lax.psum(owned_grads[11].astype(jnp.bfloat16), "dp").astype(jnp.float32),
        lax.psum(owned_grads[12].astype(jnp.bfloat16), "dp").astype(jnp.float32),
        lax.psum(owned_grads[13].astype(jnp.bfloat16), "dp").astype(jnp.float32),
        lax.psum(owned_grads[14].astype(jnp.bfloat16), "dp").astype(jnp.float32),
    )
    return (
        layer_out,
        loss_value,
        table_grad,
        summed[0],
        summed[1],
        summed[2],
        summed[3],
        summed[4],
        summed[5],
        summed[6],
        summed[7],
        summed[8],
        summed[9],
        summed[10],
        summed[11],
        summed[12],
        summed[13],
        summed[14],
    )


CORES = 2
PLANES = 4
LINES = 4
CHIPS = PLANES * LINES
DEVICES = CORES * CHIPS
CAPACITY = 48
PAD = 16
MESH = pl.DeviceIdType.MESH
VMEM_LIMIT = 60 * 1024 * 1024


def place():
    core = lax.axis_index("dp")
    chip = lax.axis_index("fsdp")
    along_x = chip + 1 - 2 * (chip % 2)
    along_y = chip + 2 - 4 * ((chip // 2) % 2)
    first = along_x + core * (along_y - along_x)
    second = along_y + core * (along_x - along_y)
    return core, chip, first, second


def enter():
    core, chip, _, _ = place()
    me = core * CHIPS + chip
    barrier = pltpu.get_barrier_semaphore()

    def greet(step, carry):
        other = (me + step) % DEVICES
        pl.semaphore_signal(
            barrier, inc=1, device_id=(other // CHIPS, other % CHIPS), device_id_type=MESH
        )
        return carry

    lax.fori_loop(1, DEVICES, greet, 0)
    pl.semaphore_wait(barrier, DEVICES - 1)


def remote(source, target, send_sem, recv_sem, core, chip):
    return pltpu.make_async_remote_copy(
        src_ref=source,
        dst_ref=target,
        send_sem=send_sem,
        recv_sem=recv_sem,
        device_id=(core, chip),
        device_id_type=MESH,
    )


def weight_steps(piece, send, recv):
    core, chip, first, second = place()

    def above(at, step):
        return (at + LINES * (PLANES - step)) % CHIPS

    def copy(index, at, target_core, target_chip, carried):
        part = piece(at, carried)
        return remote(part, part, send.at[index], recv.at[index], target_core, target_chip)

    def begin():
        for step in range(1, PLANES):
            copy(step - 1, chip, core, (chip + LINES * step) % CHIPS, core).start()
        copy(3, chip, core, first, core).start()
        copy(7, chip, core, second, core).start()

    def plane(step):
        def run():
            copy(step - 1, above(chip, step), core, first, core).wait_recv()
            copy(3 + step, above(chip, step), core, first, core).start()
            copy(7 + step, above(chip, step), core, second, core).start()
            copy(14 + step, above(chip, step), 1 - core, chip, core).start()

        return run

    def near(step):
        def run():
            copy(3 + step, above(first, step), core, second, core).wait_recv()
            copy(11 + step, above(first, step), core, second, core).start()
            copy(18 + step, above(first, step), 1 - core, chip, core).start()

        return run

    def far(step):
        def run():
            at = above(second, step) if step < 4 else above(first + second - chip, step - 4)
            copy(7 + step, at, core, second, core).wait_recv()
            copy(22 + step, at, 1 - core, chip, core).start()

        return run

    def finish():
        for index in range(15, 30):
            copy(index, chip, 1 - core, chip, 1 - core).wait_recv()

    def drain():
        for index in range(30):
            copy(index, chip, 1 - core, chip, core).wait_send()

    moves = [plane(step) for step in range(1, 4)]
    moves += [near(step) for step in range(4)]
    moves += [far(step) for step in range(8)]
    return begin, moves, finish, drain


def transposed(row):
    parts = []
    for start in range(0, row.shape[1], 128):
        tile = jnp.broadcast_to(row[:, start : start + 128], (128, 128))
        parts.append(jnp.transpose(tile)[:, 0:1])
    return jnp.concatenate(parts, axis=0)


def iota(shape, axis):
    return lax.broadcasted_iota(jnp.int32, shape, axis)


def fetch_kernel(
    shift,
    ids_ref,
    table_ref,
    wq_ref,
    wk_ref,
    wv_ref,
    wo_ref,
    wup_ref,
    wdown_ref,
    small_ref,
    embedded_ref,
    wa_ref,
    wb_ref,
    wc_ref,
    smalls_ref,
    every_ids,
    rank_ref,
    row_ref,
    pick_ref,
    rows_ref,
    replies_ref,
    ids_send,
    ids_recv,
    rows_send,
    rows_recv,
    small_send,
    small_recv,
    weight_send,
    weight_recv,
):
    core, chip, _, _ = place()
    me = core * CHIPS + chip
    tokens, width = embedded_ref.shape
    vocab_rows = table_ref.shape[0]
    enter()

    def ids_copy(step):
        other = (me + step) % DEVICES
        return remote(
            ids_ref,
            every_ids.at[me],
            ids_send.at[step],
            ids_recv.at[step],
            other // CHIPS,
            other % CHIPS,
        )

    lax.fori_loop(1, DEVICES, lambda step, carry: (ids_copy(step).start(), carry)[1], 0)
    every_ids[me] = ids_ref[...]

    depth = wq_ref.shape[0]
    deep = wdown_ref.shape[0]
    mine = pl.ds(pl.multiple_of(chip * depth, 16), depth)
    wa_ref[mine, 0:width] = wq_ref[...]
    wa_ref[mine, width : 2 * width] = wk_ref[...]
    wa_ref[mine, 2 * width : 3 * width] = wv_ref[...]
    wa_ref[mine, 3 * width : 4 * width] = wo_ref[...]
    wb_ref[mine, :] = wup_ref[...]
    wc_ref[pl.ds(pl.multiple_of(chip * deep, 16), deep), :] = wdown_ref[...]
    smalls_ref[:, pl.ds(pl.multiple_of(chip * 128, 128), 128)] = small_ref[...]

    def block(ref, rows, columns):
        def piece(at, carried):
            return ref.at[
                pl.ds(pl.multiple_of(at * rows, 16), rows),
                pl.ds(pl.multiple_of(carried * columns, 128), columns),
            ]

        return piece

    groups = [
        weight_steps(block(wa_ref, depth, 2 * width), weight_send.at[0], weight_recv.at[0]),
        weight_steps(block(wb_ref, depth, 2 * width), weight_send.at[1], weight_recv.at[1]),
        weight_steps(block(wc_ref, deep, width // 2), weight_send.at[2], weight_recv.at[2]),
    ]
    groups[0][0]()

    def small_copy(step):
        part = smalls_ref.at[:, pl.ds(pl.multiple_of(chip * 128, 128), 128)]
        return remote(
            part, part, small_send.at[step], small_recv.at[step], core, (chip + step) % CHIPS
        )

    lax.fori_loop(1, CHIPS, lambda step, carry: (small_copy(step).start(), carry)[1], 0)

    own_row = jnp.concatenate([ids_ref[j : j + 1, :] for j in range(tokens // 128)], axis=1)
    owner_row = lax.shift_right_logical(own_row, shift).astype(jnp.float32)
    owner_col = transposed(owner_row)
    earlier = (owner_row == owner_col) & (iota((tokens, tokens), 1) < iota((tokens, tokens), 0))
    own_rank = jnp.sum(earlier.astype(jnp.float32), axis=1, keepdims=True)
    own_slot = (owner_col * CAPACITY + own_rank).astype(jnp.int32)

    lax.fori_loop(1, DEVICES, lambda step, carry: (ids_copy(step).wait_recv(), carry)[1], 0)
    all_ids = jnp.concatenate([every_ids[:, j, :] for j in range(tokens // 128)], axis=1)
    asked = lax.shift_right_logical(all_ids, shift) == me
    ahead = (iota((tokens, tokens), 0) < iota((tokens, tokens), 1)).astype(jnp.bfloat16)
    ranks = jnp.dot(asked.astype(jnp.bfloat16), ahead, preferred_element_type=jnp.float32)
    rank_ref[...] = jnp.where(asked, ranks, -1.0)
    row_ref[...] = (all_ids & (vocab_rows - 1)).astype(jnp.float32) + 1.0

    def rows_copy(step):
        other = (me + step) % DEVICES
        return remote(
            rows_ref.at[pl.ds(pl.multiple_of(step * CAPACITY, 16), CAPACITY)],
            replies_ref.at[pl.ds(pl.multiple_of(me * CAPACITY, 16), CAPACITY)],
            rows_send.at[step],
            rows_recv.at[step],
            other // CHIPS,
            other % CHIPS,
        )

    group = DEVICES // 4
    for quarter in range(4):

        def pick(index, carry):
            source = (me + quarter * group + index) % DEVICES
            rank = rank_ref[pl.ds(source, 1), :]
            row = row_ref[pl.ds(source, 1), :]
            here = iota((CAPACITY, tokens), 0).astype(jnp.float32) == rank
            found = jnp.sum(jnp.where(here, row, 0.0), axis=1, keepdims=True) - 1.0
            chosen = iota((CAPACITY, vocab_rows), 1).astype(jnp.float32) == found
            pick_ref[pl.ds(pl.multiple_of(index * CAPACITY, 16), CAPACITY), :] = chosen.astype(
                jnp.bfloat16
            )
            return carry

        lax.fori_loop(0, group, pick, 0)
        rows_ref[quarter * group * CAPACITY : (quarter + 1) * group * CAPACITY, :] = jnp.dot(
            pick_ref[...], table_ref[...], preferred_element_type=jnp.float32
        ).astype(jnp.bfloat16)
        lax.fori_loop(
            max(1, quarter * group),
            (quarter + 1) * group,
            lambda step, carry: (rows_copy(step).start(), carry)[1],
            0,
        )
    replies_ref[pl.ds(pl.multiple_of(me * CAPACITY, 16), CAPACITY), :] = rows_ref[0:CAPACITY, :]

    groups[1][0]()
    for move in groups[0][1]:
        move()
    groups[2][0]()
    for move in groups[1][1]:
        move()
    for move in groups[2][1]:
        move()
    lax.fori_loop(1, DEVICES, lambda step, carry: (rows_copy(step).wait_recv(), carry)[1], 0)
    for start in range(0, tokens, 256):
        slots = iota((256, DEVICES * CAPACITY), 1)
        order = (own_slot[start : start + 256, :] == slots).astype(jnp.bfloat16)
        embedded_ref[start : start + 256, :] = jnp.dot(
            order, replies_ref[...], preferred_element_type=jnp.float32
        ).astype(jnp.bfloat16)
    lax.fori_loop(1, CHIPS, lambda step, carry: (small_copy(step).wait(), carry)[1], 0)
    for part in groups:
        part[2]()

    def drain(step, carry):
        ids_copy(step).wait_send()
        rows_copy(step).wait_send()
        return carry

    lax.fori_loop(1, DEVICES, drain, 0)
    for part in groups:
        part[3]()


def fetch(ids, table, weights, small):
    tokens = 768
    width = table.shape[1]
    wide = weights[4].shape[1]
    low = jnp.bfloat16
    dma = pltpu.SemaphoreType.DMA
    shift = table.shape[0].bit_length() - 1
    vmem = pl.BlockSpec(memory_space=pltpu.VMEM)
    return pl.pallas_call(
        partial(fetch_kernel, shift),
        out_shape=(
            jax.ShapeDtypeStruct((tokens, width), low),
            jax.ShapeDtypeStruct((width, 4 * width), low),
            jax.ShapeDtypeStruct((width, wide), low),
            jax.ShapeDtypeStruct((wide, width), low),
            jax.ShapeDtypeStruct((PAD, CHIPS * 128), low),
            jax.ShapeDtypeStruct((DEVICES, 8, 128), jnp.int32),
        ),
        in_specs=[vmem] * 9,
        out_specs=[vmem] * 6,
        scratch_shapes=[
            pltpu.VMEM((DEVICES, tokens), jnp.float32),
            pltpu.VMEM((DEVICES, tokens), jnp.float32),
            pltpu.VMEM((DEVICES // 4 * CAPACITY, table.shape[0]), low),
            pltpu.VMEM((DEVICES * CAPACITY, width), low),
            pltpu.VMEM((DEVICES * CAPACITY, width), low),
            dma((DEVICES,)),
            dma((DEVICES,)),
            dma((DEVICES,)),
            dma((DEVICES,)),
            dma((CHIPS,)),
            dma((CHIPS,)),
            dma((3, 30)),
            dma((3, 30)),
        ],
        compiler_params=pltpu.CompilerParams(
            collective_id=0, has_side_effects=True, vmem_limit_bytes=VMEM_LIMIT
        ),
        name="fetch",
    )(ids, table, *weights, small)


def gather_steps(buffer, send, recv):
    core, chip, first, second = place()
    plane, line = chip // LINES, chip % LINES
    line_first, line_second = first % LINES, second % LINES
    line_far = line_first + line_second - line
    half = buffer.shape[-1] // 2
    columns = pl.ds(pl.multiple_of(core * half, 128), half)
    others = pl.ds(pl.multiple_of((1 - core) * half, 128), half)

    def copy(index, part, to_core, to_chip):
        return remote(part, part, send.at[index], recv.at[index], to_core, to_chip)

    def own(at):
        return buffer.at[at, plane, line]

    def chip_part(at_plane, at_line, which):
        return buffer.at[:, at_plane, at_line, :, which]

    def line_part(at_line, which):
        return buffer.at[:, :, at_line, :, which]

    def run():
        copy(0, own(core), 1 - core, chip).start()
        copy(0, own(1 - core), 1 - core, chip).wait_recv()
        for step in range(1, PLANES):
            part = chip_part(plane, line, columns)
            copy(step, part, core, (chip + LINES * step) % CHIPS).start()
        for step in range(1, PLANES):
            part = chip_part((plane + PLANES - step) % PLANES, line, columns)
            copy(step, part, core, chip).wait_recv()
            copy(6 + step, part, 1 - core, chip).start()
        copy(4, line_part(line, columns), core, first).start()
        copy(5, line_part(line, columns), core, second).start()
        copy(4, line_part(line_first, columns), core, first).wait_recv()
        copy(6, line_part(line_first, columns), core, second).start()
        copy(10, line_part(line_first, columns), 1 - core, chip).start()
        copy(5, line_part(line_second, columns), core, second).wait_recv()
        copy(11, line_part(line_second, columns), 1 - core, chip).start()
        copy(6, line_part(line_far, columns), core, second).wait_recv()
        copy(12, line_part(line_far, columns), 1 - core, chip).start()
        for step in range(1, PLANES):
            part = chip_part((plane + PLANES - step) % PLANES, line, others)
            copy(6 + step, part, 1 - core, chip).wait_recv()
        copy(10, line_part(line_second, others), 1 - core, chip).wait_recv()
        copy(11, line_part(line_first, others), 1 - core, chip).wait_recv()
        copy(12, line_part(line_far, others), 1 - core, chip).wait_recv()

    def drain():
        copy(0, own(core), 1 - core, chip).wait_send()
        for index in [1, 2, 3, 7, 8, 9]:
            copy(index, chip_part(plane, line, columns), 1 - core, chip).wait_send()
        for index in [4, 5, 6, 10, 11, 12]:
            copy(index, line_part(line, columns), 1 - core, chip).wait_send()

    return run, drain


def gather_kernel(own_ref, all_ref, send, recv):
    core, chip, _, _ = place()
    all_ref[core, chip // LINES, chip % LINES] = own_ref[...]
    enter()
    run, drain = gather_steps(all_ref, send, recv)
    run()
    drain()


def gather(own):
    rows, width = own.shape
    dma = pltpu.SemaphoreType.DMA
    vmem = pl.BlockSpec(memory_space=pltpu.VMEM)
    return pl.pallas_call(
        gather_kernel,
        out_shape=jax.ShapeDtypeStruct((CORES, PLANES, LINES, rows, width), own.dtype),
        in_specs=[vmem],
        out_specs=vmem,
        scratch_shapes=[dma((13,)), dma((13,))],
        compiler_params=pltpu.CompilerParams(
            collective_id=1, has_side_effects=True, vmem_limit_bytes=VMEM_LIMIT
        ),
        name="gather_units",
    )(own).reshape(DEVICES * rows, width)


def exchange_kernel(
    own_ref, left_ref, tall_ref, coef_ref, all_ref, left_out, tall_out, coef_out, *sems
):
    core, chip, _, _ = place()
    me = core * CHIPS + chip
    all_ref[core, chip // LINES, chip % LINES] = own_ref[...]
    left_out[me] = left_ref[chip]
    tall_out[me] = tall_ref[chip]
    coef_out[me] = coef_ref[me]
    enter()
    run, drain = gather_steps(all_ref, sems[0], sems[1])

    def copies(step):
        other = (me + step) % DEVICES
        to_core, to_chip = other // CHIPS, other % CHIPS
        return [
            remote(
                coef_ref.at[other],
                coef_out.at[me],
                sems[2].at[step],
                sems[3].at[step],
                to_core,
                to_chip,
            ),
            remote(
                left_ref.at[to_chip],
                left_out.at[me],
                sems[4].at[step],
                sems[5].at[step],
                to_core,
                to_chip,
            ),
            remote(
                tall_ref.at[to_chip],
                tall_out.at[me],
                sems[6].at[step],
                sems[7].at[step],
                to_core,
                to_chip,
            ),
        ]

    def begin(step, carry):
        for one in copies(step):
            one.start()
        return carry

    def end(step, carry):
        for one in copies(step):
            one.wait()
        return carry

    lax.fori_loop(1, DEVICES, begin, 0)
    run()
    lax.fori_loop(1, DEVICES, end, 0)
    drain()


def exchange(own, left, tall, coefs):
    rows, width = own.shape
    dma = pltpu.SemaphoreType.DMA
    vmem = pl.BlockSpec(memory_space=pltpu.VMEM)
    low = own.dtype
    got = pl.pallas_call(
        exchange_kernel,
        out_shape=(
            jax.ShapeDtypeStruct((CORES, PLANES, LINES, rows, width), low),
            jax.ShapeDtypeStruct((DEVICES,) + left.shape[1:], low),
            jax.ShapeDtypeStruct((DEVICES,) + tall.shape[1:], low),
            jax.ShapeDtypeStruct(coefs.shape, low),
        ),
        in_specs=[vmem] * 4,
        out_specs=[vmem] * 4,
        scratch_shapes=[dma((13,))] * 2 + [dma((DEVICES,))] * 6,
        compiler_params=pltpu.CompilerParams(
            collective_id=2, has_side_effects=True, vmem_limit_bytes=VMEM_LIMIT
        ),
        name="exchange",
    )(own, left, tall, coefs)
    return (got[0].reshape(DEVICES * rows, width),) + tuple(got[1:])


def block_body(
    table,
    token_ids,
    sent_lengths,
    pair_slot,
    pair_lang,
    w_query,
    b_query,
    w_key,
    w_value,
    b_value,
    w_out,
    b_out,
    ln1_gain,
    ln1_bias,
    w_up,
    b_up,
    w_down,
    b_down,
    ln2_gain,
    ln2_bias,
):
    low, wide = jnp.bfloat16, jnp.float32
    sentences, length = token_ids.shape
    tokens = sentences * length
    vocab_rows, width = table.shape
    hidden_width = w_up.shape[1]
    depth, deep = w_query.shape[0], w_down.shape[0]
    core = lax.axis_index("dp")
    chip = lax.axis_index("fsdp")
    me = core * CHIPS + chip
    score_factor = HEAD ** (-0.5)
    ids = jnp.pad(token_ids.reshape(tokens // 128, 128), ((0, 8 - tokens // 128), (0, 0)))
    vectors = jnp.stack(
        [b_query, b_value, b_out, ln1_gain, ln1_bias, b_down, ln2_gain, ln2_bias]
    )
    small = jnp.concatenate([vectors, b_up.reshape(deep // depth, depth)])
    small = jnp.pad(small, ((0, PAD - small.shape[0]), (0, 128 - depth)))
    embedded, wa, full_wup, full_wdown, smalls, every_ids = fetch(
        ids, table, (w_query, w_key, w_value, w_out, w_up, w_down), small
    )
    smalls = smalls.reshape(PAD, CHIPS, 128)[:, :, :depth]
    full_bq, full_bv, full_bo, full_g1, full_s1, full_bdown, full_g2, full_s2 = (
        smalls[:8].reshape(8, width).astype(wide)
    )
    full_bup = jnp.transpose(smalls[8 : 8 + deep // depth], (1, 0, 2)).reshape(hidden_width)
    full_bup = full_bup.astype(wide)
    full_wq, full_wk, full_wv, full_wo = (
        wa[:, k * width : (k + 1) * width] for k in range(4)
    )

    valid_mask = jnp.arange(length, dtype=jnp.int32)[None, :] < sent_lengths[:, None]
    head_shape = (sentences, length, HEADS, HEAD)
    queries = (jnp.dot(embedded, full_wq, preferred_element_type=wide) + full_bq).astype(low)
    keys = jnp.dot(embedded, full_wk, preferred_element_type=wide).astype(low)
    values = (jnp.dot(embedded, full_wv, preferred_element_type=wide) + full_bv).astype(low)
    query_heads = queries.reshape(head_shape)
    key_heads = keys.reshape(head_shape)
    value_heads = values.reshape(head_shape)
    scores = (
        jnp.einsum("bqhd,bkhd->bhqk", query_heads, key_heads, preferred_element_type=wide)
        * score_factor
    )
    scores = jnp.where(valid_mask[:, None, None, :], scores, MASK_FLOOR)
    row_peak = jnp.max(scores, axis=-1, keepdims=True)
    shifted = jnp.exp(scores - row_peak)
    totals = jnp.sum(shifted, axis=-1, keepdims=True)
    attn_probs = (shifted / totals).astype(low)
    context = jnp.einsum("bhqk,bkhd->bqhd", attn_probs, value_heads, preferred_element_type=wide)
    context = context.reshape(tokens, width).astype(low)
    attended = jnp.dot(context, full_wo, preferred_element_type=wide) + full_bo
    hidden, normed_one, inverse_one = norm_rows(
        embedded.astype(wide) + attended, full_g1, full_s1
    )
    hidden_low = hidden.astype(low)
    up_pre = jnp.dot(hidden_low, full_wup, preferred_element_type=wide) + full_bup
    activated = jax.nn.gelu(up_pre, approximate=False).astype(low)
    down_pre = jnp.dot(activated, full_wdown, preferred_element_type=wide) + full_bdown
    normed_out, normed_two, inverse_two = norm_rows(hidden + down_pre, full_g2, full_s2)
    layer_out = jnp.where(valid_mask.reshape(tokens)[:, None], normed_out, 0.0).astype(low)
    layer_out = layer_out.reshape(sentences, length, width)

    def first_rows(matrix):
        return matrix.reshape(sentences, length, matrix.shape[-1])[:, 0]

    def padded(matrix):
        return jnp.pad(matrix, ((0, PAD - sentences), (0, 0)))

    def unpadded(matrix):
        return matrix.reshape(DEVICES, PAD, -1)[:, :sentences].reshape(DEVICES * sentences, -1)

    summary = first_rows(normed_out)
    magnitude = jnp.sqrt(jnp.sum(summary * summary, axis=-1, keepdims=True) + EPSILON)
    unit_vector = summary / magnitude
    unit_low = unit_vector.astype(low)
    every_unit = unpadded(gather(padded(unit_low)))

    side, pair = pair_slot % 2, pair_slot // 2
    lang_onehot = (pair_lang[:, None] == jnp.arange(LANGS, dtype=jnp.int32)[None, :]).astype(wide)
    per_lang = jnp.sum(lang_onehot, axis=0)
    per_pair = 1.0 / (2.0 * LANGS * jnp.sum(lang_onehot * per_lang[None, :], axis=1))
    weight = jnp.take(per_pair, pair)
    opposite = side[:, None] != side[None, :]
    partner = opposite & (pair[:, None] == pair[None, :])
    raw_scores = SCORE_SCALE * contract(every_unit, every_unit, 1, 1)
    pair_scores = jnp.where(partner, raw_scores - SCORE_SCALE * MARGIN_WIDTH, raw_scores)
    pair_scores = jnp.where(opposite, pair_scores, MASK_FLOOR)
    pair_peak = jnp.max(pair_scores, axis=1, keepdims=True)
    pair_exp = jnp.exp(pair_scores - pair_peak)
    pair_total = jnp.sum(pair_exp, axis=1, keepdims=True)
    log_total = pair_peak[:, 0] + jnp.log(pair_total[:, 0])
    picked = jnp.sum(jnp.where(partner, pair_scores, 0.0), axis=1)
    loss_value = jnp.sum(weight * (log_total - picked))
    coefficients = (weight[:, None] * (pair_exp / pair_total - partner.astype(wide))).astype(low)
    mine_rows = lax.dynamic_slice_in_dim(coefficients, me * sentences, sentences, 0)
    mine_columns = lax.dynamic_slice_in_dim(coefficients, me * sentences, sentences, 1)
    unit_grad = SCORE_SCALE * (
        contract(mine_rows, every_unit, 1, 0) + contract(mine_columns, every_unit, 0, 0)
    )
    along = jnp.sum(unit_vector * unit_grad, axis=-1, keepdims=True)
    summary_grad = (unit_grad - unit_vector * along) / magnitude

    residual_grad, grad_g2, grad_s2 = norm_back(
        summary_grad, first_rows(normed_two), first_rows(inverse_two), full_g2
    )
    down_grad = residual_grad.astype(low)
    act_grad = contract(down_grad, full_wdown, 1, 1)
    _, gelu_pull = jax.vjp(partial(jax.nn.gelu, approximate=False), first_rows(up_pre))
    up_grad = gelu_pull(act_grad)[0].astype(low)
    hidden_grad = contract(up_grad, full_wup, 1, 1) + residual_grad
    first_grad, grad_g1, grad_s1 = norm_back(
        hidden_grad, first_rows(normed_one), first_rows(inverse_one), full_g1
    )
    attend_grad = first_grad.astype(low)
    context_grad = contract(attend_grad, full_wo, 1, 1).astype(low)

    pairs = HEADS * PAD
    head_of = jnp.arange(pairs, dtype=jnp.int32) // PAD
    sent_of = jnp.arange(pairs, dtype=jnp.int32) % PAD
    in_head = head_of[:, None] == jnp.arange(width, dtype=jnp.int32)[None, :] // HEAD
    in_sent = sent_of[:, None] == jnp.arange(tokens, dtype=jnp.int32)[None, :] // length
    seen = in_sent & valid_mask.reshape(1, tokens)

    def spread(matrix):
        tiled = jnp.broadcast_to(padded(matrix)[None], (HEADS, PAD, width)).reshape(pairs, width)
        return jnp.where(in_head, tiled, jnp.zeros((), low))

    query_cls = first_rows(queries)
    cls_scores = contract(spread(query_cls), keys, 1, 1) * score_factor
    cls_scores = jnp.where(seen, cls_scores, MASK_FLOOR)
    cls_peak = jnp.max(cls_scores, axis=1, keepdims=True)
    cls_exp = jnp.where(seen, jnp.exp(cls_scores - cls_peak), 0.0)
    cls_total = jnp.sum(cls_exp, axis=1, keepdims=True)
    cls_probs = jnp.where(seen, cls_exp / cls_total, 0.0)
    probs_low = cls_probs.astype(low)
    prob_grad = contract(spread(context_grad), values, 1, 1)
    inner = jnp.sum(cls_probs * prob_grad, axis=1, keepdims=True)
    score_grad = (cls_probs * (prob_grad - inner)).astype(low)
    query_grad = jnp.where(in_head, contract(score_grad, keys, 1, 0), 0.0) * score_factor
    query_grad = jnp.sum(query_grad.reshape(HEADS, PAD, width), axis=0).astype(low)[:sentences]
    tall_key = contract(score_grad, embedded, 1, 0) * score_factor
    tall_value = contract(probs_low, embedded, 1, 0)
    seen_total = jnp.sum(probs_low.astype(wide), axis=1, keepdims=True)
    grad_bvalue = jnp.sum(
        jnp.where(in_head, seen_total, 0.0) * spread(context_grad).astype(wide), axis=0
    )
    grad_bquery = jnp.sum(query_grad.astype(wide), axis=0)

    own = jnp.concatenate(
        [
            padded(one)
            for one in (query_cls, down_grad, up_grad, attend_grad, context_grad, query_grad)
        ],
        axis=1,
    )
    left = jnp.concatenate(
        [
            padded(first_rows(one)).reshape(PAD, CHIPS, -1)
            for one in (hidden_low, context, embedded, activated)
        ],
        axis=2,
    )
    left = jnp.pad(left, ((0, 0), (0, 0), (0, 384 - left.shape[2]))).transpose(1, 0, 2)
    tall = jnp.concatenate(
        [one.astype(low).reshape(pairs, CHIPS, depth) for one in (tall_key, tall_value)], axis=2
    )
    tall = jnp.pad(tall, ((0, 0), (0, 0), (0, 128 - 2 * depth))).transpose(1, 0, 2)
    flat_ids = token_ids.reshape(tokens)
    owner_of = flat_ids // vocab_rows
    same = owner_of[:, None] == owner_of[None, :]
    before = jnp.arange(tokens)[None, :] < jnp.arange(tokens)[:, None]
    rank_of = jnp.sum((same & before).astype(jnp.int32), axis=1)
    slots = DEVICES * CAPACITY
    to_slot = (
        jnp.arange(slots, dtype=jnp.int32)[:, None] == (owner_of * CAPACITY + rank_of)[None, :]
    ).astype(low)
    fold_heads = (head_of[:, None] == jnp.arange(64, dtype=jnp.int32)[None, :]).astype(low)
    per_token = jnp.concatenate(
        [contract(score_grad, fold_heads, 0, 0), contract(probs_low, fold_heads, 0, 0)], axis=1
    ).astype(low)
    coefs = contract(to_slot, per_token, 1, 0).astype(low).reshape(DEVICES, CAPACITY, 128)

    every, lefts, talls, coefs = exchange(own, left, tall, coefs)

    every = unpadded(every)
    offsets = [0, width, 2 * width, 2 * width + hidden_width]
    offsets += [offsets[3] + width, offsets[3] + 2 * width, offsets[3] + 3 * width]
    all_query, all_down, all_up, all_attend, all_context, all_qgrad = (
        every[:, offsets[k] : offsets[k + 1]] for k in range(6)
    )
    lefts = unpadded(lefts)
    cut = [0, depth, 2 * depth, 3 * depth, 3 * depth + deep]
    left_hidden, left_context, left_embedded, left_activated = (
        lefts[:, cut[k] : cut[k + 1]] for k in range(4)
    )
    grad_wup = contract(left_hidden, all_up, 0, 0)
    grad_wout = contract(left_context, all_attend, 0, 0)
    grad_wquery = contract(left_embedded, all_qgrad, 0, 0)
    grad_wdown = contract(left_activated, all_down, 0, 0)
    talls = talls.reshape(DEVICES, HEADS, PAD, 128)[:, :, :sentences]
    by_head = (DEVICES, sentences, HEADS, HEAD)
    grad_wkey = jnp.einsum(
        "dhsk,dshe->khe",
        talls[..., :depth],
        all_query.reshape(by_head),
        preferred_element_type=wide,
    ).reshape(depth, width)
    grad_wvalue = jnp.einsum(
        "dhsk,dshe->khe",
        talls[..., depth : 2 * depth],
        all_context.reshape(by_head),
        preferred_element_type=wide,
    ).reshape(depth, width)

    all_ids = every_ids[:, : tokens // 128].reshape(DEVICES, tokens)
    asked = all_ids // vocab_rows == me
    ahead = (jnp.arange(tokens)[:, None] < jnp.arange(tokens)[None, :]).astype(low)
    ranks = jnp.dot(asked.astype(low), ahead, preferred_element_type=wide).astype(jnp.int32)
    ranks = jnp.where(asked, ranks, -1)
    at_slot = ranks[:, None, :] == jnp.arange(CAPACITY, dtype=jnp.int32)[None, :, None]
    local = all_ids % vocab_rows
    slot_row = jnp.sum(jnp.where(at_slot, local[:, None, :] + 1, 0), axis=2).reshape(slots) - 1
    sentence_of = (
        jnp.arange(DEVICES, dtype=jnp.int32)[:, None] * sentences
        + jnp.arange(tokens, dtype=jnp.int32)[None, :] // length
    )
    slot_sent = (
        jnp.sum(jnp.where(at_slot, sentence_of[:, None, :] + 1, 0), axis=2).reshape(slots) - 1
    )
    from_sent = (
        slot_sent[:, None] == jnp.arange(DEVICES * sentences, dtype=jnp.int32)[None, :]
    ).astype(low)
    coefs = coefs.reshape(slots, 128)
    widen = (
        jnp.arange(64, dtype=jnp.int32)[:, None]
        == jnp.arange(width, dtype=jnp.int32)[None, :] // HEAD
    ).astype(low)
    key_grad = (
        contract(coefs[:, :64], widen, 1, 0) * contract(from_sent, all_query, 1, 0) * score_factor
    ).astype(low)
    value_grad = (
        contract(coefs[:, 64:], widen, 1, 0) * contract(from_sent, all_context, 1, 0)
    ).astype(low)
    row_grads = contract(key_grad, full_wk, 1, 1) + contract(value_grad, full_wv, 1, 1)
    extra = contract(all_qgrad, full_wq, 1, 1) + all_attend.astype(wide)
    first_ids = all_ids.reshape(DEVICES * sentences, length)[:, 0]
    here = jnp.arange(vocab_rows, dtype=jnp.int32)[:, None] + me * vocab_rows
    rows_onehot = (jnp.arange(vocab_rows, dtype=jnp.int32)[:, None] == slot_row[None, :])
    table_grad = contract(rows_onehot.astype(low), row_grads.astype(low), 1, 0) + contract(
        (here == first_ids[None, :]).astype(low), extra.astype(low), 1, 0
    )

    sums = jnp.stack([grad_bquery, grad_bvalue, grad_g1, grad_s1, grad_g2, grad_s2])
    sums = lax.psum(sums, ("dp", "fsdp")).reshape(6, CHIPS, depth)
    sums = lax.dynamic_slice_in_dim(sums, chip, 1, 1)[:, 0]

    def owned_sum(matrix, size):
        full = jnp.sum(matrix.astype(wide), axis=0)
        return lax.dynamic_slice_in_dim(full, chip * size, size)

    return (
        layer_out,
        loss_value,
        table_grad,
        grad_wquery,
        sums[0],
        grad_wkey,
        grad_wvalue,
        sums[1],
        grad_wout,
        owned_sum(all_attend, depth),
        sums[2],
        sums[3],
        grad_wup,
        owned_sum(all_up, deep),
        grad_wdown,
        owned_sum(all_down, depth),
        sums[4],
        sums[5],
    )


def solution(mesh):
    in_specs = (
        P(("dp", "fsdp"), None),
        P(("dp", "fsdp"), None),
        P(("dp", "fsdp")),
        P(),
        P(),
        P("fsdp", None),
        P("fsdp"),
        P("fsdp", None),
        P("fsdp", None),
        P("fsdp"),
        P("fsdp", None),
        P("fsdp"),
        P("fsdp"),
        P("fsdp"),
        P("fsdp", None),
        P("fsdp"),
        P("fsdp", None),
        P("fsdp"),
        P("fsdp"),
        P("fsdp"),
    )
    out_specs = (
        P(("dp", "fsdp"), None, None),
        P(),
        P(("dp", "fsdp"), None),
        P("fsdp", None),
        P("fsdp"),
        P("fsdp", None),
        P("fsdp", None),
        P("fsdp"),
        P("fsdp", None),
        P("fsdp"),
        P("fsdp"),
        P("fsdp"),
        P("fsdp", None),
        P("fsdp"),
        P("fsdp", None),
        P("fsdp"),
        P("fsdp"),
        P("fsdp"),
    )
    sizes = dict(mesh.shape)
    body = general_body
    if sizes["dp"] == CORES and sizes["fsdp"] == CHIPS:
        body = block_body
    return jax.shard_map(body, mesh=mesh, in_specs=in_specs, out_specs=out_specs, check_vma=False)
```

```python
from functools import partial
from types import SimpleNamespace

import jax
import jax.numpy as jnp
from jax import lax
from jax.experimental import pallas as pl
from jax.experimental.pallas import tpu as pltpu
from jax.sharding import PartitionSpec as P

HEADS = 12
HEAD = 64
LANGS = 109


EPSILON = 1e-06
SCORE_SCALE = 50.0
MARGIN_WIDTH = 0.3
MASK_FLOOR = -1000000000.0


def contract(left_side, right_side, left_dim, right_dim):
    return lax.dot_general(
        left_side,
        right_side,
        (((left_dim,), (right_dim,)), ((), ())),
        preferred_element_type=jnp.float32,
    )


def norm_rows(inputs, ln_gain, ln_shift):
    row_mean = jnp.mean(inputs, axis=-1, keepdims=True)
    centered = inputs - row_mean
    variance = jnp.mean(centered * centered, axis=-1, keepdims=True)
    inverse = lax.rsqrt(variance + EPSILON)
    normed = centered * inverse
    return (normed * ln_gain + ln_shift, normed, inverse)


def norm_back(grad_output, normed, inverse, ln_gain):
    grad_normed = grad_output * ln_gain
    first_term = jnp.mean(grad_normed, axis=-1, keepdims=True)
    second_term = jnp.mean(grad_normed * normed, axis=-1, keepdims=True)
    grad_input = inverse * (grad_normed - first_term - normed * second_term)
    return (grad_input, jnp.sum(grad_output * normed, axis=0), jnp.sum(grad_output, axis=0))


def general_body(
    table,
    token_ids,
    sent_lengths,
    pair_slot,
    pair_lang,
    w_query,
    b_query,
    w_key,
    w_value,
    b_value,
    w_out,
    b_out,
    ln1_gain,
    ln1_bias,
    w_up,
    b_up,
    w_down,
    b_down,
    ln2_gain,
    ln2_bias,
):
    sentences, length = token_ids.shape
    tokens = sentences * length
    vocab_rows, model_width = table.shape
    owners = lax.axis_size(("dp", "fsdp"))
    dp_count = lax.axis_size("dp")
    fsdp_count = lax.axis_size("fsdp")
    capacity = max(2, 2 * tokens // owners)
    device = lax.axis_index(("dp", "fsdp"))
    score_factor = HEAD ** (-0.5)
    flat_ids = token_ids.reshape(tokens)
    owner_of = flat_ids // vocab_rows
    member = (owner_of[:, None] == jnp.arange(owners, dtype=jnp.int32)[None, :]).astype(jnp.int32)
    owner_rank = jnp.sum(jnp.cumsum(member, axis=0) * member, axis=1) - 1
    slot_of = owner_of * capacity + owner_rank
    requests = jnp.full((owners * capacity,), -1, jnp.int32).at[slot_of].set(flat_ids)
    received = lax.all_to_all(
        lax.all_to_all(
            requests.reshape(dp_count, fsdp_count, capacity),
            "dp",
            split_axis=0,
            concat_axis=0,
            tiled=True,
        ),
        "fsdp",
        split_axis=1,
        concat_axis=1,
        tiled=True,
    )
    present = received >= 0
    local_rows = jnp.where(present, received - device * vocab_rows, 0)
    found_rows = jnp.where(present[..., None], table[local_rows], jnp.zeros((), table.dtype))
    replies = lax.all_to_all(
        lax.all_to_all(found_rows, "dp", split_axis=0, concat_axis=0, tiled=True),
        "fsdp",
        split_axis=1,
        concat_axis=1,
        tiled=True,
    )
    embedded = replies.reshape(owners * capacity, model_width)[slot_of]
    gathered = (
        lax.all_gather(w_query, "fsdp", axis=0, tiled=True),
        lax.all_gather(b_query, "fsdp", axis=0, tiled=True),
        lax.all_gather(w_key, "fsdp", axis=0, tiled=True),
        lax.all_gather(w_value, "fsdp", axis=0, tiled=True),
        lax.all_gather(b_value, "fsdp", axis=0, tiled=True),
        lax.all_gather(w_out, "fsdp", axis=0, tiled=True),
        lax.all_gather(b_out, "fsdp", axis=0, tiled=True),
        lax.all_gather(ln1_gain, "fsdp", axis=0, tiled=True),
        lax.all_gather(ln1_bias, "fsdp", axis=0, tiled=True),
        lax.all_gather(w_up, "fsdp", axis=0, tiled=True),
        lax.all_gather(b_up, "fsdp", axis=0, tiled=True),
        lax.all_gather(w_down, "fsdp", axis=0, tiled=True),
        lax.all_gather(b_down, "fsdp", axis=0, tiled=True),
        lax.all_gather(ln2_gain, "fsdp", axis=0, tiled=True),
        lax.all_gather(ln2_bias, "fsdp", axis=0, tiled=True),
    )
    (
        full_wq,
        full_bq,
        full_wk,
        full_wv,
        full_bv,
        full_wo,
        full_bo,
        full_g1,
        full_s1,
        full_wup,
        full_bup,
        full_wdown,
        full_bdown,
        full_g2,
        full_s2,
    ) = gathered
    valid_mask = jnp.arange(length, dtype=jnp.int32)[None, :] < sent_lengths[:, None]
    head_shape = (sentences, length, HEADS, HEAD)
    queries = (jnp.dot(embedded, full_wq, preferred_element_type=jnp.float32) + full_bq).astype(
        jnp.bfloat16
    )
    key_heads = (
        jnp.dot(embedded, full_wk, preferred_element_type=jnp.float32)
        .astype(jnp.bfloat16)
        .reshape(head_shape)
    )
    value_heads = (
        (jnp.dot(embedded, full_wv, preferred_element_type=jnp.float32) + full_bv)
        .astype(jnp.bfloat16)
        .reshape(head_shape)
    )
    query_heads = queries.reshape(head_shape)
    scores = (
        jnp.einsum("bqhd,bkhd->bhqk", query_heads, key_heads, preferred_element_type=jnp.float32)
        * score_factor
    )
    scores = jnp.where(valid_mask[:, None, None, :], scores, MASK_FLOOR)
    row_peak = jnp.max(scores, axis=-1, keepdims=True)
    shifted = jnp.exp(scores - row_peak)
    totals = jnp.sum(shifted, axis=-1, keepdims=True)
    attn_probs = (shifted / totals).astype(jnp.bfloat16)
    context = jnp.einsum(
        "bhqk,bkhd->bqhd", attn_probs, value_heads, preferred_element_type=jnp.float32
    )
    context = context.reshape(tokens, model_width).astype(jnp.bfloat16)
    attended = jnp.dot(context, full_wo, preferred_element_type=jnp.float32) + full_bo
    hidden, normed_one, inverse_one = norm_rows(
        embedded.astype(jnp.float32) + attended, full_g1, full_s1
    )
    hidden_low = hidden.astype(jnp.bfloat16)
    up_pre = jnp.dot(hidden_low, full_wup, preferred_element_type=jnp.float32) + full_bup
    activated = jax.nn.gelu(up_pre, approximate=False).astype(jnp.bfloat16)
    down_pre = jnp.dot(activated, full_wdown, preferred_element_type=jnp.float32) + full_bdown
    normed_out, normed_two, inverse_two = norm_rows(hidden + down_pre, full_g2, full_s2)
    layer_out = jnp.where(valid_mask.reshape(tokens)[:, None], normed_out, 0.0).astype(jnp.bfloat16)
    layer_out = layer_out.reshape(sentences, length, model_width)

    def first_rows(matrix):
        return matrix.reshape(sentences, length, matrix.shape[-1])[:, 0]

    summary = first_rows(normed_out)
    magnitude = jnp.sqrt(jnp.sum(summary * summary, axis=-1, keepdims=True) + EPSILON)
    unit_vector = summary / magnitude
    unit_low = unit_vector.astype(jnp.bfloat16)
    every_unit = lax.all_gather(unit_low, ("dp", "fsdp"), axis=0, tiled=True)
    every_side = pair_slot % 2
    every_pair = pair_slot // 2
    my_slots = lax.dynamic_slice_in_dim(pair_slot, device * sentences, sentences)
    my_side = my_slots % 2
    my_pair = my_slots // 2
    lang_onehot = (pair_lang[:, None] == jnp.arange(LANGS, dtype=jnp.int32)[None, :]).astype(
        jnp.float32
    )
    per_lang = jnp.sum(lang_onehot, axis=0)
    per_pair = 1.0 / (2.0 * LANGS * jnp.sum(lang_onehot * per_lang[None, :], axis=1))
    my_weight = jnp.take(per_pair, my_pair)
    opposite = my_side[:, None] != every_side[None, :]
    partner = opposite & (my_pair[:, None] == every_pair[None, :])
    raw_scores = SCORE_SCALE * contract(unit_low, every_unit, 1, 1)
    pair_scores = jnp.where(partner, raw_scores - SCORE_SCALE * MARGIN_WIDTH, raw_scores)
    pair_scores = jnp.where(opposite, pair_scores, MASK_FLOOR)
    pair_peak = jnp.max(pair_scores, axis=1, keepdims=True)
    pair_exp = jnp.exp(pair_scores - pair_peak)
    pair_total = jnp.sum(pair_exp, axis=1, keepdims=True)
    log_total = pair_peak[:, 0] + jnp.log(pair_total[:, 0])
    picked = jnp.sum(jnp.where(partner, pair_scores, 0.0), axis=1)
    loss_value = lax.psum(jnp.sum(my_weight * (log_total - picked)), ("dp", "fsdp"))
    coefficients = (
        my_weight[:, None] * (pair_exp / pair_total - partner.astype(jnp.float32))
    ).astype(jnp.bfloat16)
    unit_grad = SCORE_SCALE * contract(coefficients, every_unit, 1, 0)
    column_terms = SCORE_SCALE * contract(coefficients, unit_low, 0, 0)
    unit_grad = unit_grad + lax.psum_scatter(
        column_terms, ("dp", "fsdp"), scatter_dimension=0, tiled=True
    )
    along = jnp.sum(unit_vector * unit_grad, axis=-1, keepdims=True)
    summary_grad = (unit_grad - unit_vector * along) / magnitude
    again_weights = (
        lax.all_gather(w_query, "fsdp", axis=0, tiled=True),
        lax.all_gather(w_key, "fsdp", axis=0, tiled=True),
        lax.all_gather(w_value, "fsdp", axis=0, tiled=True),
        lax.all_gather(w_out, "fsdp", axis=0, tiled=True),
        lax.all_gather(ln1_gain, "fsdp", axis=0, tiled=True),
        lax.all_gather(w_up, "fsdp", axis=0, tiled=True),
        lax.all_gather(w_down, "fsdp", axis=0, tiled=True),
        lax.all_gather(ln2_gain, "fsdp", axis=0, tiled=True),
    )
    again_wq, again_wk, again_wv, again_wo, again_g1, again_wup, again_wdown, again_g2 = (
        again_weights
    )
    residual_grad, grad_g2, grad_s2 = norm_back(
        summary_grad, first_rows(normed_two), first_rows(inverse_two), again_g2
    )
    down_grad = residual_grad.astype(jnp.bfloat16)
    activated_cls = first_rows(activated)
    act_grad = contract(down_grad, again_wdown, 1, 1)
    gelu_value, gelu_pull = jax.vjp(partial(jax.nn.gelu, approximate=False), first_rows(up_pre))
    up_grad = gelu_pull(act_grad)[0].astype(jnp.bfloat16)
    hidden_cls = first_rows(hidden_low)
    hidden_grad = contract(up_grad, again_wup, 1, 1) + residual_grad
    first_grad, grad_g1, grad_s1 = norm_back(
        hidden_grad, first_rows(normed_one), first_rows(inverse_one), again_g1
    )
    attend_grad = first_grad.astype(jnp.bfloat16)
    context_cls = first_rows(context)
    context_grad = (
        contract(attend_grad, again_wo, 1, 1).astype(jnp.bfloat16).reshape(sentences, HEADS, HEAD)
    )
    query_cls = query_heads[:, 0]
    cls_scores = (
        jnp.einsum("bhd,bkhd->bhk", query_cls, key_heads, preferred_element_type=jnp.float32)
        * score_factor
    )
    cls_scores = jnp.where(valid_mask[:, None, :], cls_scores, MASK_FLOOR)
    cls_probs = jnp.exp(cls_scores - row_peak[:, :, 0]) / totals[:, :, 0]
    prob_grad = jnp.einsum(
        "bhd,bkhd->bhk", context_grad, value_heads, preferred_element_type=jnp.float32
    )
    score_grad = (
        cls_probs * (prob_grad - jnp.sum(cls_probs * prob_grad, axis=-1, keepdims=True))
    ).astype(jnp.bfloat16)
    query_grad = (
        (
            jnp.einsum("bhk,bkhd->bhd", score_grad, key_heads, preferred_element_type=jnp.float32)
            * score_factor
        )
        .astype(jnp.bfloat16)
        .reshape(sentences, model_width)
    )
    key_grad = (
        (
            jnp.einsum("bhk,bhd->bkhd", score_grad, query_cls, preferred_element_type=jnp.float32)
            * score_factor
        )
        .astype(jnp.bfloat16)
        .reshape(tokens, model_width)
    )
    value_grad = (
        jnp.einsum(
            "bhk,bhd->bkhd",
            cls_probs.astype(jnp.bfloat16),
            context_grad,
            preferred_element_type=jnp.float32,
        )
        .astype(jnp.bfloat16)
        .reshape(tokens, model_width)
    )
    embedded_cls = first_rows(embedded)
    grad_wkey = contract(embedded, key_grad, 0, 0)
    grad_wvalue = contract(embedded, value_grad, 0, 0)
    grad_bvalue = jnp.sum(value_grad, axis=0, dtype=jnp.float32)
    row_grads = contract(key_grad, again_wk, 1, 1) + contract(value_grad, again_wv, 1, 1)
    summary_extra = contract(query_grad, again_wq, 1, 1) + first_grad
    row_grads = (
        row_grads.reshape(sentences, length, model_width)
        .at[:, 0]
        .add(summary_extra)
        .reshape(tokens, model_width)
    )
    outgoing = jnp.zeros((owners * capacity, model_width), jnp.float32).at[slot_of].set(row_grads)
    incoming = lax.all_to_all(
        lax.all_to_all(
            outgoing.reshape(dp_count, fsdp_count, capacity, model_width).astype(jnp.bfloat16),
            "dp",
            split_axis=0,
            concat_axis=0,
            tiled=True,
        ),
        "fsdp",
        split_axis=1,
        concat_axis=1,
        tiled=True,
    ).astype(jnp.float32)
    incoming = jnp.where(
        present.reshape(owners * capacity)[:, None],
        incoming.reshape(owners * capacity, model_width),
        0.0,
    )
    table_grad = (
        jnp.zeros((vocab_rows, model_width), jnp.float32)
        .at[local_rows.reshape(owners * capacity)]
        .add(incoming)
    )
    grad_wquery = contract(embedded_cls, query_grad, 0, 0)
    grad_bquery = jnp.sum(query_grad, axis=0, dtype=jnp.float32)
    grad_wout = contract(context_cls, attend_grad, 0, 0)
    grad_bout = jnp.sum(attend_grad, axis=0, dtype=jnp.float32)
    grad_wup = contract(hidden_cls, up_grad, 0, 0)
    grad_bup = jnp.sum(up_grad, axis=0, dtype=jnp.float32)
    grad_wdown = contract(activated_cls, down_grad, 0, 0)
    grad_bdown = jnp.sum(down_grad, axis=0, dtype=jnp.float32)
    owned_grads = (
        lax.psum_scatter(
            grad_wquery.astype(jnp.bfloat16), "fsdp", scatter_dimension=0, tiled=True
        ).astype(jnp.float32),
        lax.psum_scatter(
            grad_bquery.astype(jnp.bfloat16), "fsdp", scatter_dimension=0, tiled=True
        ).astype(jnp.float32),
        lax.psum_scatter(
            grad_wkey.astype(jnp.bfloat16), "fsdp", scatter_dimension=0, tiled=True
        ).astype(jnp.float32),
        lax.psum_scatter(
            grad_wvalue.astype(jnp.bfloat16), "fsdp", scatter_dimension=0, tiled=True
        ).astype(jnp.float32),
        lax.psum_scatter(
            grad_bvalue.astype(jnp.bfloat16), "fsdp", scatter_dimension=0, tiled=True
        ).astype(jnp.float32),
        lax.psum_scatter(
            grad_wout.astype(jnp.bfloat16), "fsdp", scatter_dimension=0, tiled=True
        ).astype(jnp.float32),
        lax.psum_scatter(
            grad_bout.astype(jnp.bfloat16), "fsdp", scatter_dimension=0, tiled=True
        ).astype(jnp.float32),
        lax.psum_scatter(
            grad_g1.astype(jnp.bfloat16), "fsdp", scatter_dimension=0, tiled=True
        ).astype(jnp.float32),
        lax.psum_scatter(
            grad_s1.astype(jnp.bfloat16), "fsdp", scatter_dimension=0, tiled=True
        ).astype(jnp.float32),
        lax.psum_scatter(
            grad_wup.astype(jnp.bfloat16), "fsdp", scatter_dimension=0, tiled=True
        ).astype(jnp.float32),
        lax.psum_scatter(
            grad_bup.astype(jnp.bfloat16), "fsdp", scatter_dimension=0, tiled=True
        ).astype(jnp.float32),
        lax.psum_scatter(
            grad_wdown.astype(jnp.bfloat16), "fsdp", scatter_dimension=0, tiled=True
        ).astype(jnp.float32),
        lax.psum_scatter(
            grad_bdown.astype(jnp.bfloat16), "fsdp", scatter_dimension=0, tiled=True
        ).astype(jnp.float32),
        lax.psum_scatter(
            grad_g2.astype(jnp.bfloat16), "fsdp", scatter_dimension=0, tiled=True
        ).astype(jnp.float32),
        lax.psum_scatter(
            grad_s2.astype(jnp.bfloat16), "fsdp", scatter_dimension=0, tiled=True
        ).astype(jnp.float32),
    )
    summed = (
        lax.psum(owned_grads[0].astype(jnp.bfloat16), "dp").astype(jnp.float32),
        lax.psum(owned_grads[1].astype(jnp.bfloat16), "dp").astype(jnp.float32),
        lax.psum(owned_grads[2].astype(jnp.bfloat16), "dp").astype(jnp.float32),
        lax.psum(owned_grads[3].astype(jnp.bfloat16), "dp").astype(jnp.float32),
        lax.psum(owned_grads[4].astype(jnp.bfloat16), "dp").astype(jnp.float32),
        lax.psum(owned_grads[5].astype(jnp.bfloat16), "dp").astype(jnp.float32),
        lax.psum(owned_grads[6].astype(jnp.bfloat16), "dp").astype(jnp.float32),
        lax.psum(owned_grads[7].astype(jnp.bfloat16), "dp").astype(jnp.float32),
        lax.psum(owned_grads[8].astype(jnp.bfloat16), "dp").astype(jnp.float32),
        lax.psum(owned_grads[9].astype(jnp.bfloat16), "dp").astype(jnp.float32),
        lax.psum(owned_grads[10].astype(jnp.bfloat16), "dp").astype(jnp.float32),
        lax.psum(owned_grads[11].astype(jnp.bfloat16), "dp").astype(jnp.float32),
        lax.psum(owned_grads[12].astype(jnp.bfloat16), "dp").astype(jnp.float32),
        lax.psum(owned_grads[13].astype(jnp.bfloat16), "dp").astype(jnp.float32),
        lax.psum(owned_grads[14].astype(jnp.bfloat16), "dp").astype(jnp.float32),
    )
    return (
        layer_out,
        loss_value,
        table_grad,
        summed[0],
        summed[1],
        summed[2],
        summed[3],
        summed[4],
        summed[5],
        summed[6],
        summed[7],
        summed[8],
        summed[9],
        summed[10],
        summed[11],
        summed[12],
        summed[13],
        summed[14],
    )


CORES = 2
PLANES = 4
LINES = 4
CHIPS = PLANES * LINES
DEVICES = CORES * CHIPS
CAPACITY = 48
GROUPS = 3
PAD = 16
TOKENS = 768
WIDTH = 768
WIDE = 3072
VOCAB_ROWS = 1024
PAIR_ROWS = HEADS * PAD
SLOT_ROWS = DEVICES * PAD
LONG = 64
BLOCK = 256
MESH = pl.DeviceIdType.MESH
LOW = jnp.bfloat16
FULL = jnp.float32
VMEM_LIMIT = 62 * 1024 * 1024

INPUTS = ["table", "token_ids", "lens", "slots", "langs"]
INPUTS += ["wq", "bq", "wk", "wv", "bv", "wo", "bo", "g1", "s1", "wup", "bup", "wdown", "bdown"]
INPUTS += ["g2", "s2"]
OUTPUTS = ["layer_out", "table_grad", "g_wq", "g_wk", "g_wv", "g_wo", "g_wup", "g_wdown"]
OUTPUTS += ["g_small", "loss"]


def place():
    core = lax.axis_index("dp")
    chip = lax.axis_index("fsdp")
    along_x = chip + 1 - 2 * (chip % 2)
    along_y = chip + 2 - 4 * ((chip // 2) % 2)
    first = along_x + core * (along_y - along_x)
    second = along_y + core * (along_x - along_y)
    return core, chip, first, second


def enter():
    core, chip, _, _ = place()
    me = core * CHIPS + chip
    barrier = pltpu.get_barrier_semaphore()

    def greet(step, carry):
        other = (me + step) % DEVICES
        pl.semaphore_signal(
            barrier, inc=1, device_id=(other // CHIPS, other % CHIPS), device_id_type=MESH
        )
        return carry

    lax.fori_loop(1, DEVICES, greet, 0)
    pl.semaphore_wait(barrier, DEVICES - 1)


def remote(source, target, send_sem, recv_sem, core, chip):
    return pltpu.make_async_remote_copy(
        src_ref=source,
        dst_ref=target,
        send_sem=send_sem,
        recv_sem=recv_sem,
        device_id=(core, chip),
        device_id_type=MESH,
    )


def every(start, stop, act):
    def step(index, carry):
        act(index)
        return carry

    lax.fori_loop(start, stop, step, 0)


def weight_steps(piece, send, recv):
    core, chip, first, second = place()
    plane, line = chip // LINES, chip % LINES
    line_first, line_second = first % LINES, second % LINES
    line_far = line_first + line_second - line
    is_low, is_high = plane > 0, plane < PLANES - 1

    def copy(send_index, recv_index, at, to_core, to_chip, carried=core):
        part = piece(at, carried)
        return remote(part, part, send.at[send_index], recv.at[recv_index], to_core, to_chip)

    def up(at_plane):
        return copy(at_plane, at_plane, at_plane * LINES + line, core, chip + LINES)

    def down(at_plane, index):
        return copy(index, at_plane, at_plane * LINES + line, core, chip - LINES)

    def side(at_plane, base, at_line, target):
        return copy(base + at_plane, base + at_plane, at_plane * LINES + at_line, core, target)

    def across(at_plane, base, at_line):
        return copy(base + at_plane, base + at_plane, at_plane * LINES + at_line, 1 - core, chip)

    def begin():
        pl.when(is_high)(lambda: up(plane).start())
        pl.when(is_low)(lambda: down(plane, PLANES).start())
        side(plane, 5, line, first).start()
        side(plane, 9, line, second).start()

    def at_distance(distance, act):
        if distance == 0:
            act(plane, None)
            return
        pl.when(plane >= distance)(lambda: act(plane - distance, True))
        pl.when(plane + distance < PLANES)(lambda: act(plane + distance, False))

    def chain(distance):
        def act(at_plane, from_low):
            if from_low:
                up(at_plane).wait_recv()
                pl.when(is_high)(lambda: up(at_plane).start())
            else:
                down(at_plane, at_plane).wait_recv()
                pl.when(is_low)(lambda: down(at_plane, at_plane).start())
            side(at_plane, 5, line, first).start()
            side(at_plane, 9, line, second).start()
            across(at_plane, 17, line).start()

        return partial(at_distance, distance, act)

    def near(distance):
        def act(at_plane, from_low):
            side(at_plane, 5, line_first, first).wait_recv()
            side(at_plane, 13, line_first, second).start()
            across(at_plane, 21, line_first).start()

        return partial(at_distance, distance, act)

    def far(distance):
        def act(at_plane, from_low):
            side(at_plane, 9, line_second, second).wait_recv()
            across(at_plane, 25, line_second).start()
            side(at_plane, 13, line_far, second).wait_recv()
            across(at_plane, 29, line_far).start()

        return partial(at_distance, distance, act)

    def finish():
        for step in range(1, PLANES):
            index = 17 + (plane + step) % PLANES
            copy(index, index, chip, 1 - core, chip, 1 - core).wait_recv()
        every(21, 33, lambda index: copy(index, index, chip, 1 - core, chip, 1 - core).wait_recv())

    def drain():
        def sent(index):
            copy(index, index, chip, 1 - core, chip).wait_send()

        for at_plane in range(PLANES):
            pl.when((plane >= at_plane) & is_high)(partial(sent, at_plane))
            pl.when((plane < at_plane) & is_low)(partial(sent, at_plane))
        pl.when(is_low)(partial(sent, PLANES))
        every(5, 17, sent)
        for step in range(1, PLANES):
            sent(17 + (plane + step) % PLANES)
        every(21, 33, sent)

    moves = [chain(1), near(0), chain(2), near(1), chain(3), far(0)]
    moves += [near(2), far(1), near(3), far(2), far(3)]
    return begin, moves, finish, drain


def gather_steps(buffer, send, recv):
    core, chip, first, second = place()
    plane, line = chip // LINES, chip % LINES
    line_first, line_second = first % LINES, second % LINES
    line_far = line_first + line_second - line
    half = buffer.shape[-1] // 2
    columns = pl.ds(pl.multiple_of(core * half, 128), half)
    others = pl.ds(pl.multiple_of((1 - core) * half, 128), half)

    def copy(index, part, to_core, to_chip):
        return remote(part, part, send.at[index], recv.at[index], to_core, to_chip)

    def own(at):
        return buffer.at[at, plane, line]

    def chip_part(at_plane, at_line, which):
        return buffer.at[:, at_plane, at_line, :, which]

    def line_part(at_line, which):
        return buffer.at[:, :, at_line, :, which]

    def start():
        copy(0, own(core), 1 - core, chip).start()

    def planes():
        copy(0, own(1 - core), 1 - core, chip).wait_recv()
        for step in range(1, PLANES):
            part = chip_part(plane, line, columns)
            copy(step, part, core, (chip + LINES * step) % CHIPS).start()

    def sides():
        for step in range(1, PLANES):
            part = chip_part((plane + PLANES - step) % PLANES, line, columns)
            copy(step, part, core, chip).wait_recv()
        copy(4, line_part(line, columns), core, first).start()
        copy(5, line_part(line, columns), core, second).start()
        for step in range(1, PLANES):
            part = chip_part((plane + PLANES - step) % PLANES, line, columns)
            copy(6 + step, part, 1 - core, chip).start()

    def corner():
        copy(4, line_part(line_first, columns), core, first).wait_recv()
        copy(6, line_part(line_first, columns), core, second).start()
        copy(10, line_part(line_first, columns), 1 - core, chip).start()
        copy(5, line_part(line_second, columns), core, second).wait_recv()
        copy(11, line_part(line_second, columns), 1 - core, chip).start()

    def last():
        copy(6, line_part(line_far, columns), core, second).wait_recv()
        copy(12, line_part(line_far, columns), 1 - core, chip).start()

    def finish():
        for step in range(1, PLANES):
            part = chip_part((plane + PLANES - step) % PLANES, line, others)
            copy(6 + step, part, 1 - core, chip).wait_recv()
        copy(10, line_part(line_second, others), 1 - core, chip).wait_recv()
        copy(11, line_part(line_first, others), 1 - core, chip).wait_recv()
        copy(12, line_part(line_far, others), 1 - core, chip).wait_recv()

    def drain():
        copy(0, own(core), 1 - core, chip).wait_send()
        for index in [1, 2, 3, 7, 8, 9]:
            copy(index, chip_part(plane, line, columns), 1 - core, chip).wait_send()
        for index in [4, 5, 6, 10, 11, 12]:
            copy(index, line_part(line, columns), 1 - core, chip).wait_send()

    return [start, planes, sides, corner, last, finish], drain


def iota(shape, axis):
    return lax.broadcasted_iota(jnp.int32, shape, axis)


def as_column(row):
    parts = []
    for start in range(0, row.shape[1], 128):
        tile = jnp.broadcast_to(row[:, start : start + 128], (128, 128))
        parts.append(jnp.transpose(tile)[:, 0:1])
    return jnp.concatenate(parts, axis=0)


def as_row(column):
    parts = []
    for start in range(0, column.shape[0], 128):
        tile = jnp.broadcast_to(column[start : start + 128, :], (128, 128))
        parts.append(jnp.transpose(tile)[0:1, :])
    return jnp.concatenate(parts, axis=1)


def dot(left_side, right_side):
    return contract(left_side, right_side, 1, 0)


def dot_turned(left_side, right_side):
    return contract(left_side, right_side, 1, 1)


def norm_parts(inputs):
    centered = inputs - jnp.mean(inputs, axis=-1, keepdims=True)
    inverse = lax.rsqrt(jnp.mean(centered * centered, axis=-1, keepdims=True) + EPSILON)
    return centered * inverse, inverse


def norm_back_parts(grad_output, normed, inverse, ln_gain):
    grad_normed = grad_output * ln_gain
    first_term = jnp.mean(grad_normed, axis=-1, keepdims=True)
    second_term = jnp.mean(grad_normed * normed, axis=-1, keepdims=True)
    return (
        inverse * (grad_normed - first_term - normed * second_term),
        jnp.sum(grad_output * normed, axis=0, keepdims=True),
        jnp.sum(grad_output, axis=0, keepdims=True),
    )


def gelu_parts(inputs):
    spread = 0.5 * (1.0 + lax.erf(inputs * (0.5**0.5)))
    density = jnp.exp(-0.5 * inputs * inputs) * ((2.0 * 3.141592653589793) ** -0.5)
    return inputs * spread, spread + inputs * density


def gelu(inputs):
    return inputs * (0.5 * (1.0 + lax.erf(inputs * (0.5**0.5))))


def layer_kernel(names, *refs):
    r = SimpleNamespace(**dict(zip(names, refs, strict=True)))
    core, chip, _, _ = place()
    me = core * CHIPS + chip
    here = (core, chip // LINES, chip % LINES)
    scale = HEAD ** (-0.5)
    depth, deep = WIDTH // CHIPS, WIDE // CHIPS
    sentences = TOKENS // LONG

    for j in range(TOKENS // 128):
        r.ids[j : j + 1, :] = jnp.concatenate(
            [r.token_ids[2 * j : 2 * j + 1, :], r.token_ids[2 * j + 1 : 2 * j + 2, :]], axis=1
        )
    r.ids[TOKENS // 128 : 8, :] = jnp.zeros((8 - TOKENS // 128, 128), jnp.int32)
    enter()

    def ids_copy(step):
        other = (me + step) % DEVICES
        return remote(
            r.ids,
            r.every_ids.at[me],
            r.ids_send.at[step],
            r.ids_recv.at[step],
            other // CHIPS,
            other % CHIPS,
        )

    every(1, DEVICES, lambda step: ids_copy(step).start())
    r.every_ids[me] = r.ids[...]

    mine = pl.ds(pl.multiple_of(chip * depth, 16), depth)
    for index, shard in enumerate([r.wq, r.wk, r.wv, r.wo]):
        r.wa[mine, index * WIDTH : (index + 1) * WIDTH] = shard[...]

    def block(ref, rows, columns):
        def piece(at, carried):
            return ref.at[
                pl.ds(pl.multiple_of(at * rows, 16), rows),
                pl.ds(pl.multiple_of(carried * columns, 128), columns),
            ]

        return piece

    begin_a, moves_a, finish_a, drain_a = weight_steps(
        block(r.wa, depth, 2 * WIDTH), r.weight_send.at[0], r.weight_recv.at[0]
    )
    begin_b, moves_b, finish_b, drain_b = weight_steps(
        block(r.wb, depth, WIDE // 2), r.weight_send.at[1], r.weight_recv.at[1]
    )
    begin_c, moves_c, finish_c, drain_c = weight_steps(
        block(r.wc, deep, WIDTH // 2), r.weight_send.at[2], r.weight_recv.at[2]
    )
    begin_a()
    r.wb[mine, :] = r.wup[...]
    begin_b()
    r.wc[pl.ds(pl.multiple_of(chip * deep, 16), deep), :] = r.wdown[...]

    small_here = pl.ds(pl.multiple_of(chip * 128, 128), 128)
    lines = [r.bq, r.bv, r.bo, r.g1, r.s1, r.bdown, r.g2, r.s2]
    lines = [line[...].reshape(1, depth).astype(FULL) for line in lines]
    up_line = r.bup[...].reshape(1, deep).astype(FULL)
    lines += [up_line[:, part * depth : (part + 1) * depth] for part in range(deep // depth)]
    lines.append(jnp.zeros((PAD - len(lines), depth), FULL))
    own_small = jnp.concatenate(lines, axis=0)
    own_small = jnp.concatenate([own_small, jnp.zeros((PAD, 128 - depth), FULL)], axis=1)
    r.smalls[:, small_here] = own_small.astype(LOW)

    def small_copy(step):
        part = r.smalls.at[:, small_here]
        return remote(
            part, part, r.small_send.at[step], r.small_recv.at[step], core, (chip + step) % CHIPS
        )

    every(1, CHIPS, lambda step: small_copy(step).start())

    own_row = jnp.concatenate([r.ids[j : j + 1, :] for j in range(TOKENS // 128)], axis=1)
    owner_row = (own_row // VOCAB_ROWS).astype(FULL)
    owner_col = as_column(owner_row)
    earlier = (owner_row == owner_col) & (iota((TOKENS, TOKENS), 1) < iota((TOKENS, TOKENS), 0))
    own_rank = jnp.sum(earlier.astype(FULL), axis=1, keepdims=True)
    own_group = jnp.floor(own_rank * (1.0 / PAD))
    own_slot = own_group * SLOT_ROWS + owner_col * PAD + (own_rank - own_group * PAD)
    r.slot_col[...] = own_slot
    r.slot_line[0:1, :] = as_row(own_slot)

    ahead = (iota((TOKENS, TOKENS), 0) < iota((TOKENS, TOKENS), 1)).astype(LOW)
    every(1, DEVICES, lambda step: ids_copy(step).wait_recv())
    all_ids = jnp.concatenate([r.every_ids[:, j, :] for j in range(TOKENS // 128)], axis=1)
    all_owner = all_ids // VOCAB_ROWS
    asked = all_owner == me
    ranks = dot(asked.astype(LOW), ahead)
    r.rank[...] = jnp.where(asked, ranks, -1.0)
    local_row = (all_ids - all_owner * VOCAB_ROWS + 1).astype(FULL)
    r.code[...] = local_row + (iota((DEVICES, TOKENS), 1) // LONG * 2048).astype(FULL)

    def rows_copy(step):
        other = (me + step) % DEVICES
        return remote(
            r.rows.at[:, pl.ds(pl.multiple_of(other * PAD, 16), PAD), :],
            r.replies.at[:, pl.ds(pl.multiple_of(me * PAD, 16), PAD), :],
            r.rows_send.at[step],
            r.rows_recv.at[step],
            other // CHIPS,
            other % CHIPS,
        )

    def pick(source):
        rank = r.rank[pl.ds(source, 1), :]
        code = r.code[pl.ds(source, 1), :]
        here_at = iota((CAPACITY, TOKENS), 0).astype(FULL) == rank
        found = jnp.sum(jnp.where(here_at, code, 0.0), axis=1, keepdims=True)
        sent = jnp.floor(found * (1.0 / 2048))
        row = found - sent * 2048.0 - 1.0
        chosen = (iota((CAPACITY, VOCAB_ROWS), 1).astype(FULL) == row).astype(LOW)
        at = pl.ds(pl.multiple_of(source * PAD, 16), PAD)
        source_sent = sent + (source * PAD).astype(FULL)
        for group in range(GROUPS):
            part = slice(group * PAD, (group + 1) * PAD)
            r.chosen[group, at, :] = chosen[part]
            r.found[group, at, 0:1] = row[part]
            r.found[group, at, 1:2] = source_sent[part]

    quarter_size = DEVICES // 4
    for quarter in range(4):
        now = (me // quarter_size + 1 + quarter) % 4
        every(0, quarter_size, lambda index: pick(now * quarter_size + index))
        span = pl.ds(pl.multiple_of(now * quarter_size * PAD, 128), quarter_size * PAD)
        picked = r.chosen[:, span, :].reshape(GROUPS * quarter_size * PAD, VOCAB_ROWS)
        found_rows = dot(picked, r.table[...]).astype(LOW)
        r.rows[:, span, :] = found_rows.reshape(GROUPS, quarter_size * PAD, WIDTH)

        def send(index):
            source = now * quarter_size + (me % quarter_size + index) % quarter_size
            rows_copy((source + DEVICES - me) % DEVICES).start()

        every(1 if quarter == 3 else 0, quarter_size, send)
        moves_a[quarter]()
    own_at = pl.ds(pl.multiple_of(me * PAD, 16), PAD)
    r.replies[:, own_at, :] = r.rows[:, own_at, :]
    moves_a[4]()
    moves_a[5]()
    begin_c()

    at_sent = iota((1, TOKENS), 1) // LONG
    lens = jnp.concatenate(
        [r.lens[...].reshape(1, sentences).astype(FULL), jnp.zeros((1, PAD - sentences), FULL)],
        axis=1,
    )
    spread_lens = dot(
        jnp.broadcast_to(lens, (8, PAD)).astype(LOW),
        (iota((PAD, TOKENS), 0) == iota((PAD, TOKENS), 1) // LONG).astype(LOW),
    )[0:1]
    valid_row = ((iota((1, TOKENS), 1) - at_sent * LONG).astype(FULL) < spread_lens).astype(FULL)
    r.valid_line[0:1, :] = valid_row
    r.valid_col[...] = as_column(valid_row)

    slots = r.slots[...].reshape(1, DEVICES * sentences)
    gap = jnp.full((1, PAD - sentences), -2, jnp.int32)
    slot_line = jnp.concatenate(
        [
            part
            for device in range(DEVICES)
            for part in (slots[:, device * sentences : (device + 1) * sentences], gap)
        ],
        axis=1,
    )
    side_line = slot_line - slot_line // 2 * 2 + jnp.where(slot_line < 0, 8, 0)
    pair_line = slot_line // 2
    pairs = r.langs.shape[0]
    lang_line = r.langs[...].reshape(1, pairs).astype(FULL)
    lang_line = jnp.concatenate([lang_line, jnp.full((1, -pairs % 128), -1.0, FULL)], axis=1)
    lang_col = as_column(lang_line)
    same_lang = jnp.sum(jnp.where(lang_col == lang_line, 1.0, 0.0), axis=1, keepdims=True)
    per_pair = 1.0 / (2.0 * LANGS * same_lang)
    at_pair = iota((lang_line.shape[1], SLOT_ROWS), 0) == pair_line
    weight_line = jnp.sum(jnp.where(at_pair, per_pair, 0.0), axis=0, keepdims=True)
    r.pairs[0:1, :] = weight_line
    r.pairs[1:2, :] = pair_line.astype(FULL)
    r.pairs[2:3, :] = side_line.astype(FULL)
    r.pairs_col[:, 0:1] = as_column(weight_line)
    r.pairs_col[:, 1:2] = as_column(pair_line.astype(FULL))
    r.pairs_col[:, 2:3] = as_column(side_line.astype(FULL))
    for move in moves_a[6:]:
        move()

    every(1, CHIPS, lambda step: small_copy(step).wait_recv())
    smalls = r.smalls[...].astype(FULL)
    r.vectors[:, 0:WIDTH] = jnp.concatenate(
        [smalls[:, at * 128 : at * 128 + depth] for at in range(CHIPS)], axis=1
    )
    r.up_bias[0:1, :] = jnp.concatenate(
        [
            smalls[8 + part : 9 + part, at * 128 : at * 128 + depth]
            for at in range(CHIPS)
            for part in range(deep // depth)
        ],
        axis=1,
    )

    def vector(index):
        return r.vectors[index : index + 1, :]

    r.qkv_bias[0:1, 0:WIDTH] = vector(0)
    r.qkv_bias[0:1, WIDTH : 2 * WIDTH] = jnp.zeros((1, WIDTH), FULL)
    r.qkv_bias[0:1, 2 * WIDTH : 3 * WIDTH] = vector(1)
    for move in moves_b[:6]:
        move()

    def first_row(source):
        code = jnp.where(r.rank[pl.ds(source, 1), :] >= 0.0, r.code[pl.ds(source, 1), :], 0.0)
        at_first = iota((PAD, TOKENS), 1) == iota((PAD, TOKENS), 0) * LONG
        found = jnp.sum(jnp.where(at_first, code, 0.0), axis=1, keepdims=True)
        row = found - jnp.floor(found * (1.0 / 2048)) * 2048.0 - 1.0
        r.found[GROUPS, pl.ds(pl.multiple_of(source * PAD, 16), PAD), 0:1] = row

    every(0, DEVICES, first_row)
    for group in range(GROUPS + 1):
        named = as_row(r.found[group, :, 0:1])
        by_row = iota((VOCAB_ROWS, SLOT_ROWS), 0).astype(FULL) == named
        r.by_row[:, group * SLOT_ROWS : (group + 1) * SLOT_ROWS] = by_row.astype(LOW)
    for move in moves_b[6:]:
        move()

    every(1, DEVICES, lambda step: rows_copy(step).wait_recv())

    def embed(tile):
        at = pl.ds(pl.multiple_of(tile * BLOCK, BLOCK), BLOCK)
        lanes = iota((BLOCK, GROUPS * SLOT_ROWS), 1).astype(FULL)
        order = (r.slot_col[at, :] == lanes).astype(LOW)
        replies = r.replies[...].reshape(GROUPS * SLOT_ROWS, WIDTH)
        r.embedded[at, :] = dot(order, replies).astype(LOW)

    every(0, TOKENS // BLOCK, embed)
    moves_c[0]()
    finish_a()
    moves_c[1]()

    def project(tile):
        at = pl.ds(pl.multiple_of(tile * BLOCK, BLOCK), BLOCK)
        r.qkv[:, at] = (dot(r.embedded[...], r.wa[:, at]) + r.qkv_bias[0:1, at]).astype(LOW)

    every(3, 6, project)
    moves_c[2]()
    every(6, 9, project)
    moves_c[3]()

    row_sent = iota((PAIR_ROWS, WIDTH), 0) % PAD
    row_head = iota((PAIR_ROWS, WIDTH), 0) // PAD
    lane_block = iota((PAIR_ROWS, WIDTH), 1) // HEAD
    in_head = row_head == lane_block
    seen = (row_sent == lane_block) & (r.valid_line[0:1, :] > 0.0)
    firsts = (iota((PAD, TOKENS), 1) == iota((PAD, TOKENS), 0) * LONG).astype(LOW)
    real_row = iota((PAD, 1), 0) < sentences

    def spread(rows):
        return jnp.where(in_head, jnp.concatenate([rows] * HEADS, axis=0), jnp.zeros((), LOW))

    def fold(tall):
        tall = jnp.where(in_head, tall, 0.0)
        return sum(tall[head * PAD : (head + 1) * PAD] for head in range(HEADS))

    keys, values = slice(WIDTH, 2 * WIDTH), slice(2 * WIDTH, 3 * WIDTH)
    embedded_cls = dot(firsts, r.embedded[...]).astype(LOW)
    query_cls = (dot(embedded_cls, r.wa[:, 0:WIDTH]) + vector(0)).astype(LOW)
    cls_scores = dot_turned(spread(query_cls), r.qkv[:, keys]) * scale
    cls_scores = jnp.where(seen, cls_scores, MASK_FLOOR)
    cls_peak = jnp.max(cls_scores, axis=1, keepdims=True)
    cls_exp = jnp.where(seen, jnp.exp(cls_scores - cls_peak), 0.0)
    cls_total = jnp.sum(cls_exp, axis=1, keepdims=True)
    cls_probs = cls_exp / jnp.where(cls_total > 0.0, cls_total, 1.0)
    probs_low = cls_probs.astype(LOW)
    r.probs[...] = cls_probs
    context_cls = fold(dot(probs_low, r.qkv[:, values])).astype(LOW)
    moves_c[4]()
    first_cls = (
        embedded_cls.astype(FULL)
        + dot(context_cls, r.wa[:, 3 * WIDTH : 4 * WIDTH])
        + vector(2)
    )
    normed_one, inverse_one = norm_parts(first_cls)
    r.normed_one[...] = normed_one
    hidden_cls = normed_one * vector(3) + vector(4)
    hidden_cls_low = hidden_cls.astype(LOW)
    early_here = r.early.at[here]
    early_here[:, 0:WIDTH] = hidden_cls_low
    early_here[:, WIDTH : 2 * WIDTH] = query_cls
    steps_u, drain_u = gather_steps(r.units, r.gather_send.at[0], r.gather_recv.at[0])
    steps_e, drain_e = gather_steps(r.early, r.gather_send.at[1], r.gather_recv.at[1])
    steps_d, drain_d = gather_steps(r.downs, r.gather_send.at[2], r.gather_recv.at[2])
    steps_a, drain_a2 = gather_steps(r.attends, r.gather_send.at[3], r.gather_recv.at[3])
    steps_q, drain_q = gather_steps(r.queries, r.gather_send.at[4], r.gather_recv.at[4])
    steps_e[0]()
    moves_c[5]()

    half_block = BLOCK // 2

    def attend(unit):
        rows = pl.ds(pl.multiple_of(unit // 3 * half_block, half_block), half_block)
        lane = unit % 3 * BLOCK

        def part(which):
            return r.qkv[rows, pl.ds(pl.multiple_of(which * WIDTH + lane, 128), BLOCK)]

        query, key, value = part(0), part(1), part(2)
        lane_head = iota((half_block, BLOCK), 1) // HEAD
        stacked = jnp.concatenate(
            [jnp.where(lane_head == head, query, jnp.zeros((), LOW)) for head in range(4)], axis=0
        )
        shape = (4 * half_block, half_block)
        same = iota(shape, 0) // LONG % 2 == iota(shape, 1) // LONG
        allowed = same & (r.valid_line[0:1, rows] > 0.0)
        scores = jnp.where(allowed, dot_turned(stacked, key) * scale, MASK_FLOOR)
        shifted = jnp.exp(scores - jnp.max(scores, axis=1, keepdims=True))
        probs = shifted * (1.0 / jnp.sum(shifted, axis=1, keepdims=True))
        mixed = dot(probs.astype(LOW), value)
        result = mixed[0:half_block]
        for head in range(1, 4):
            result = jnp.where(
                lane_head == head, mixed[head * half_block : (head + 1) * half_block], result
            )
        r.context[rows, pl.ds(pl.multiple_of(lane, 128), BLOCK)] = result.astype(LOW)

    def open_tile(tile):
        at = pl.ds(tile * BLOCK, BLOCK)
        attended = dot(r.context[at, :], r.wa[:, 3 * WIDTH : 4 * WIDTH]) + vector(2)
        normed, _ = norm_parts(r.embedded[at, :].astype(FULL) + attended)
        hidden = normed * vector(3) + vector(4)
        r.tile_low[...] = hidden.astype(LOW)
        r.tile_sum[...] = hidden + vector(5)

    def feed_tile(part):
        at = pl.ds(pl.multiple_of(part * BLOCK, BLOCK), BLOCK)
        up_pre = dot(r.tile_low[...], r.wb[:, at]) + r.up_bias[0:1, at]
        r.tile_sum[...] += dot(gelu(up_pre).astype(LOW), r.wc[at, :])

    def layer_copy(tile):
        at = pl.ds(tile * BLOCK, BLOCK)
        return pltpu.make_async_copy(r.context.at[at], r.layer_out.at[at], r.out_sem.at[tile])

    def close_tile(tile):
        at = pl.ds(tile * BLOCK, BLOCK)
        normed, _ = norm_parts(r.tile_sum[...])
        out = normed * vector(6) + vector(7)
        r.context[at, :] = (out * r.valid_col[at, :]).astype(LOW)
        layer_copy(tile).start()

    queue = [partial(every, 0, 3, project)]
    queue += [partial(every, unit, unit + 1, attend) for unit in range(18)]
    late = []
    for tile in range(TOKENS // BLOCK):
        late.append(partial(open_tile, tile))
        late += [partial(every, 2 * part, 2 * part + 2, feed_tile) for part in range(6)]
        late.append(partial(close_tile, tile))

    def fill(pieces, count):
        for _ in range(min(count, len(pieces))):
            pieces.pop(0)()

    finish_b()
    up_cls = dot(hidden_cls_low, r.wb[...]) + r.up_bias[0:1, :]
    activated_cls, slope_cls = gelu_parts(up_cls)
    activated_low = activated_cls.astype(LOW)
    steps_e[1]()
    for move in moves_c[6:]:
        fill(queue, 1)
        move()
    fill(queue, 1)

    def pack_tall(tall, target, first_row):
        for at in range(CHIPS):
            columns = tall[:, at * depth : (at + 1) * depth]
            for half in range(CORES):
                base = half * PAIR_ROWS // 2
                target[half * CHIPS + at, first_row : first_row + 48, :] = jnp.concatenate(
                    [
                        columns[base : base + 48],
                        columns[base + 48 : base + 96],
                        jnp.zeros((48, 128 - 2 * depth), FULL),
                    ],
                    axis=1,
                ).astype(LOW)

    def pack_coefs(coefs):
        total = None
        for group in range(GROUPS):
            folds = iota((PAIR_ROWS, 128), 0) // PAD + group * PAD == iota((PAIR_ROWS, 128), 1)
            lanes = contract(coefs, folds.astype(LOW), 0, 0).astype(LOW)
            part = dot(r.rows[group], lanes)
            total = part if total is None else total + part
        return total.astype(LOW).reshape(DEVICES, PAD, 128)

    finish_c()
    down_pre = dot(activated_low, r.wc[...]) + vector(5)
    normed_two, inverse_two = norm_parts(hidden_cls + down_pre)
    summary = normed_two * vector(6) + vector(7)
    magnitude = jnp.sqrt(jnp.sum(summary * summary, axis=-1, keepdims=True) + EPSILON)
    unit = jnp.where(real_row, summary / magnitude, 0.0)
    r.units[here] = unit.astype(LOW)

    steps_u[0]()
    every(1, DEVICES, lambda step: rows_copy(step).wait_send())
    for group in range(GROUPS):
        slot_at = iota((SLOT_ROWS, TOKENS), 0) + group * SLOT_ROWS
        r.rows[group] = (slot_at.astype(FULL) == r.slot_line[0:1, :]).astype(LOW)
    steps_u[1]()
    for at in range(CHIPS):
        cut = slice(at * depth, (at + 1) * depth)
        line = jnp.concatenate(
            [
                context_cls.astype(FULL)[:, cut],
                embedded_cls.astype(FULL)[:, cut],
                jnp.zeros((PAD, 128 - 2 * depth), FULL),
            ],
            axis=1,
        ).astype(LOW)
        for half in range(CORES):
            r.mail_one[half * CHIPS + at, 0:PAD, :] = line
    steps_u[2]()
    steps_e[2]()
    pack_tall(dot(probs_low, r.embedded[...]), r.mail_one, PAD)
    steps_u[3]()
    r.mail_one[:, 64:80, :] = pack_coefs(probs_low)

    def mail_copy(box, got, send, recv, step):
        other = (me + step) % DEVICES
        return remote(
            box.at[other], got.at[me], send.at[step], recv.at[step], other // CHIPS, other % CHIPS
        )

    one = partial(mail_copy, r.mail_one, r.got_one, r.one_send, r.one_recv)
    two = partial(mail_copy, r.mail_two, r.got_two, r.two_send, r.two_recv)
    three = partial(mail_copy, r.mail_three, r.got_three, r.three_send, r.three_recv)
    steps_u[4]()
    r.got_one[me] = r.mail_one[me]
    fill(queue, 2)
    steps_u[5]()
    every(1, DEVICES, lambda step: one(step).start())
    steps_e[3]()

    units = r.units[...].reshape(SLOT_ROWS, WIDTH)
    weight_row, pair_row, side_row = r.pairs[0:1, :], r.pairs[1:2, :], r.pairs[2:3, :]

    def pair_scores(rows, pair_col, side_col):
        opposite = side_col + side_row == 1.0
        partner = opposite & (pair_col == pair_row)
        raw = SCORE_SCALE * dot_turned(rows, units)
        shifted = jnp.where(partner, raw - SCORE_SCALE * MARGIN_WIDTH, raw)
        return jnp.where(opposite, shifted, MASK_FLOOR), partner

    every_score, every_partner = pair_scores(
        units, r.pairs_col[:, 1:2], r.pairs_col[:, 2:3]
    )
    peak_row = jnp.max(every_score, axis=0, keepdims=True)
    log_row = peak_row + jnp.log(
        jnp.sum(jnp.exp(every_score - peak_row), axis=0, keepdims=True)
    )
    picked_row = jnp.sum(jnp.where(every_partner, every_score, 0.0), axis=0, keepdims=True)
    r.loss[...] = jnp.sum(weight_row * (log_row - picked_row), axis=1, keepdims=True)

    rows_here = pl.ds(pl.multiple_of(me * PAD, 16), PAD)
    own_score, own_partner = pair_scores(
        r.units[here], r.pairs_col[rows_here, 1:2], r.pairs_col[rows_here, 2:3]
    )
    own_partner = own_partner.astype(FULL)
    own_peak = jnp.max(own_score, axis=1, keepdims=True)
    own_exp = jnp.exp(own_score - own_peak)
    own_share = own_exp / jnp.sum(own_exp, axis=1, keepdims=True)
    by_row = (r.pairs_col[rows_here, 0:1] * (own_share - own_partner)).astype(LOW)
    by_column = (weight_row * (jnp.exp(own_score - log_row) - own_partner)).astype(LOW)
    unit_grad = SCORE_SCALE * (dot(by_row, units) + dot(by_column, units))
    along = jnp.sum(unit * unit_grad, axis=-1, keepdims=True)
    summary_grad = (unit_grad - unit * along) / magnitude

    residual_grad, grad_g2, grad_s2 = norm_back_parts(
        summary_grad, normed_two, inverse_two, vector(6)
    )
    down_grad = residual_grad.astype(LOW)
    r.downs[here] = down_grad
    steps_d[0]()
    act_grad = dot_turned(down_grad, r.wc[...])
    up_grad = (act_grad * slope_cls).astype(LOW)
    steps_d[1]()
    hidden_grad = dot_turned(up_grad, r.wb[...]) + residual_grad
    first_grad, grad_g1, grad_s1 = norm_back_parts(
        hidden_grad, r.normed_one[...], inverse_one, vector(3)
    )
    attend_grad = first_grad.astype(LOW)
    steps_e[4]()
    context_grad = dot_turned(attend_grad, r.wa[:, 3 * WIDTH : 4 * WIDTH]).astype(LOW)
    attend_here = r.attends.at[here]
    attend_here[:, 0:WIDTH] = attend_grad
    attend_here[:, WIDTH : 2 * WIDTH] = context_grad
    steps_a[0]()
    steps_d[2]()
    context_tall = spread(context_grad)
    probs = r.probs[...]
    prob_grad = dot_turned(context_tall, r.qkv[:, values])
    inner = jnp.sum(probs * prob_grad, axis=1, keepdims=True)
    score_grad = (probs * (prob_grad - inner)).astype(LOW)
    steps_a[1]()
    r.mail_three[...] = pack_coefs(score_grad)
    every(1, DEVICES, lambda step: three(step).start())
    r.got_three[me] = r.mail_three[me]
    query_grad = (fold(dot(score_grad, r.qkv[:, keys])) * scale).astype(LOW)
    probs_total = jnp.sum(probs_low.astype(FULL), axis=1, keepdims=True)
    grad_bvalue = jnp.sum(probs_total * context_tall.astype(FULL), axis=0, keepdims=True)
    grad_bquery = jnp.sum(query_grad.astype(FULL), axis=0, keepdims=True)
    query_here = r.queries.at[here]
    query_here[:, 0:WIDTH] = query_grad
    query_here[:, WIDTH : 2 * WIDTH] = jnp.concatenate(
        [grad_bquery, grad_bvalue, grad_g1, grad_s1, grad_g2, grad_s2, jnp.zeros((10, WIDTH))],
        axis=0,
    ).astype(LOW)
    steps_q[0]()
    steps_a[2]()
    pack_tall(dot(score_grad, r.embedded[...]) * scale, r.mail_two, 0)
    steps_q[1]()
    every(1, DEVICES, lambda step: two(step).start())
    r.got_two[me] = r.mail_two[me]

    def all_rows(buffer, start):
        return buffer[:, :, :, :, start : start + WIDTH].reshape(SLOT_ROWS, WIDTH)

    def from_sent(group):
        lanes = iota((SLOT_ROWS, SLOT_ROWS), 1).astype(FULL)
        return (r.found[group, :, 1:2] == lanes).astype(LOW)

    def widened(coefs, group):
        lanes = iota((128, WIDTH), 0) == iota((128, WIDTH), 1) // HEAD + group * PAD
        return dot(coefs, lanes.astype(LOW))

    half_wide = WIDE // 2

    def slope_tile(part):
        at = pl.ds(pl.multiple_of(core * half_wide + part * BLOCK, BLOCK), BLOCK)
        up_pre = dot(all_rows(r.early, 0), r.wb[:, at]) + r.up_bias[0:1, at]
        _, slope = gelu_parts(up_pre)
        r.slopes[:, pl.ds(pl.multiple_of(part * BLOCK, BLOCK), BLOCK)] = slope.astype(LOW)

    def slot_queries(group):
        r.slot_query[group] = dot(from_sent(group), all_rows(r.early, WIDTH)).astype(LOW)

    def activate():
        at = pl.ds(pl.multiple_of(chip // 2 * 2 * deep, 128), 2 * deep)
        up_pre = dot(all_rows(r.early, 0), r.wb[:, at]) + r.up_bias[0:1, at]
        r.active_turned[...] = jnp.transpose(gelu(up_pre)).astype(LOW)
        r.hidden_turned[...] = jnp.transpose(all_rows(r.early, 0))

    steps_e[5]()
    between = [partial(slot_queries, group) for group in range(GROUPS)]
    between += [partial(every, part, part + 1, slope_tile) for part in range(6)]
    between.append(activate)

    steps_d[3]()
    fill(between, 1)
    steps_a[3]()
    fill(between, 1)
    steps_q[2]()
    steps_d[4]()
    fill(between, 1)
    steps_a[4]()
    fill(between, 1)
    steps_q[3]()
    fill(between, 1)
    steps_d[5]()
    steps_a[5]()
    steps_q[4]()
    fill(between, len(between))

    every(1, DEVICES, lambda step: one(step).wait_recv())
    got_probs = r.got_one[:, 64:80, :].reshape(SLOT_ROWS, 128)
    for group in range(GROUPS):
        slot_context = dot(from_sent(group), all_rows(r.attends, WIDTH))
        r.replies[group] = (widened(got_probs, group) * slot_context).astype(LOW)

    def head_products(got, first_row, right, start, target):
        for pair in range(HEADS // 4):
            lane = pl.ds(pl.multiple_of(start + (core * (HEADS // 4) + pair) * 128, 128), 128)
            pair_rows = right[:, :, :, :, lane].reshape(SLOT_ROWS, 128)
            parts = []
            for half in range(2):
                head = 2 * pair + half
                row = first_row + head % 3 * PAD
                block_rows = got[:, row : row + PAD, :].reshape(SLOT_ROWS, 128)
                product = contract(block_rows, pair_rows, 0, 0)
                column = head // 3 * depth
                parts.append(product[column : column + depth, :])
            low_lanes = iota((depth, 128), 1) < HEAD
            result = jnp.where(low_lanes, parts[0], parts[1])
            target[:, pl.ds(pl.multiple_of((core * (HEADS // 4) + pair) * 128, 128), 128)] = result

    def half_of(ref, at_core):
        half = ref.shape[1] // 2
        return ref.at[:, pl.ds(pl.multiple_of(at_core * half, 128), half)]

    def half_copy(index, ref, at_core):
        part = half_of(ref, at_core)
        return remote(part, part, r.half_send.at[index], r.half_recv.at[index], 1 - core, chip)

    head_products(r.got_one, PAD, r.attends, WIDTH, r.g_wv)
    half_copy(0, r.g_wv, core).start()

    downs = r.downs[...].reshape(SLOT_ROWS, WIDTH)
    attends = all_rows(r.attends, 0)

    def up_tile(part):
        at = pl.ds(pl.multiple_of(core * half_wide + part * BLOCK, BLOCK), BLOCK)
        slope = r.slopes[:, pl.ds(pl.multiple_of(part * BLOCK, BLOCK), BLOCK)].astype(FULL)
        up_all = (dot_turned(r.downs[...].reshape(SLOT_ROWS, WIDTH), r.wc[at, :]) * slope)
        up_all = up_all.astype(LOW)
        r.g_wup[0:depth, at] = dot(r.hidden_turned[mine, :], up_all)
        total = jnp.sum(up_all.astype(FULL), axis=0, keepdims=True)
        r.g_wup[depth : depth + 8, at] = jnp.broadcast_to(total, (8, BLOCK))

    every(0, half_wide // BLOCK, up_tile)
    half_copy(1, r.g_wup, core).start()
    r.down_both[...] = dot(r.active_turned[...], downs)
    r.g_wdown[...] = r.down_both[pl.ds(pl.multiple_of(chip % 2 * deep, 16), deep), :]
    r.left_turned[...] = jnp.transpose(r.got_one[:, 0:PAD, :].reshape(SLOT_ROWS, 128))
    r.g_wo[...] = dot(r.left_turned[0:depth, :], attends)
    own_lanes = (iota((WIDTH, 128), 0) == chip * depth + iota((WIDTH, 128), 1)).astype(LOW)

    def own_part(rows, select):
        total = None
        for _ in range(3):
            part = rows.astype(LOW)
            rows = rows - part.astype(FULL)
            picked = dot(part, select)
            total = picked if total is None else total + picked
        return total

    every(1, DEVICES, lambda step: three(step).wait_recv())
    got_scores = r.got_three[...].reshape(SLOT_ROWS, 128)
    for group in range(GROUPS):
        slot_query = r.slot_query[group].astype(FULL)
        key_grad = (widened(got_scores, group) * slot_query * scale).astype(LOW)
        row_grad = dot_turned(key_grad, r.wa[:, keys])
        row_grad = row_grad + dot_turned(r.replies[group], r.wa[:, values])
        r.rows[group] = row_grad.astype(LOW)
    steps_q[5]()
    query_grads = all_rows(r.queries, 0)
    extra = dot_turned(query_grads, r.wa[:, 0:WIDTH]) + attends.astype(FULL)
    r.extra[...] = extra.astype(LOW)
    r.g_wq[...] = dot(r.left_turned[depth : 2 * depth, :], query_grads)

    def table_copy(tile):
        at = pl.ds(pl.multiple_of(tile * BLOCK, BLOCK), BLOCK)
        return pltpu.make_async_copy(
            r.table_full.at[at], r.table_grad.at[at], r.table_sem.at[tile]
        )

    def table_tile(tile):
        at = pl.ds(pl.multiple_of(tile * BLOCK, BLOCK), BLOCK)
        slot_rows = r.rows[...].reshape(GROUPS * SLOT_ROWS, WIDTH)
        r.table_full[at, :] = dot(r.by_row[at, 0 : GROUPS * SLOT_ROWS], slot_rows) + dot(
            r.by_row[at, GROUPS * SLOT_ROWS :], r.extra[...]
        )
        table_copy(tile).start()

    every(0, VOCAB_ROWS // BLOCK, table_tile)
    every(1, DEVICES, lambda step: two(step).wait_recv())
    head_products(r.got_two, 0, r.early, WIDTH, r.g_wk)
    half_copy(2, r.g_wk, core).start()
    fill(queue, len(queue))
    fill(late, len(late))

    down_total = jnp.sum(downs.astype(FULL), axis=0, keepdims=True)
    attend_total = jnp.sum(attends.astype(FULL), axis=0, keepdims=True)
    device_sums = (iota((PAD, SLOT_ROWS), 1) % PAD == iota((PAD, SLOT_ROWS), 0)).astype(LOW)
    sums = dot(device_sums, all_rows(r.queries, WIDTH))
    stacked = jnp.concatenate(
        [sums[0:6], attend_total, down_total, jnp.zeros((8, WIDTH), FULL)], axis=0
    )
    r.g_small[0:16, 0:128] = own_part(stacked, own_lanes)
    r.g_small[0:16, 128:BLOCK] = jnp.zeros((PAD, BLOCK - 128), FULL)
    half_copy(1, r.g_wup, 1 - core).wait_recv()
    up_lanes = (iota((WIDE, BLOCK), 0) == chip * deep + iota((WIDE, BLOCK), 1)).astype(LOW)
    r.g_small[16:24, :] = own_part(r.g_wup[depth : depth + 8, :], up_lanes)

    half_copy(0, r.g_wv, 1 - core).wait_recv()
    half_copy(2, r.g_wk, 1 - core).wait_recv()
    for index, ref in enumerate([r.g_wv, r.g_wup, r.g_wk]):
        half_copy(index, ref, core).wait_send()

    def drain(step):
        ids_copy(step).wait_send()
        one(step).wait_send()
        two(step).wait_send()
        three(step).wait_send()

    every(1, DEVICES, drain)
    every(1, CHIPS, lambda step: small_copy(step).wait_send())
    for end in [drain_a, drain_b, drain_c, drain_u, drain_e, drain_d, drain_a2, drain_q]:
        end()
    for tile in range(TOKENS // BLOCK):
        layer_copy(tile).wait()
    every(0, VOCAB_ROWS // BLOCK, lambda tile: table_copy(tile).wait())


def layer(inputs):
    dma = pltpu.SemaphoreType.DMA
    vmem = pl.BlockSpec(memory_space=pltpu.VMEM)
    anywhere = pl.BlockSpec(memory_space=pl.ANY)
    depth, deep = WIDTH // CHIPS, WIDE // CHIPS

    def gathered(width):
        return pltpu.VMEM((CORES, PLANES, LINES, PAD, width), LOW)

    outputs = dict(
        layer_out=((TOKENS, WIDTH), LOW),
        table_grad=((VOCAB_ROWS, WIDTH), FULL),
        g_wq=((depth, WIDTH), FULL),
        g_wk=((depth, WIDTH), FULL),
        g_wv=((depth, WIDTH), FULL),
        g_wo=((depth, WIDTH), FULL),
        g_wup=((depth + 8, WIDE), FULL),
        g_wdown=((deep, WIDTH), FULL),
        g_small=((24, BLOCK), FULL),
        loss=((1, 1), FULL),
    )
    scratch = dict(
        ids=pltpu.VMEM((8, 128), jnp.int32),
        every_ids=pltpu.VMEM((DEVICES, 8, 128), jnp.int32),
        rank=pltpu.VMEM((DEVICES, TOKENS), FULL),
        code=pltpu.VMEM((DEVICES, TOKENS), FULL),
        found=pltpu.VMEM((GROUPS + 1, SLOT_ROWS, 2), FULL),
        slot_col=pltpu.VMEM((TOKENS, 1), FULL),
        slot_line=pltpu.VMEM((8, TOKENS), FULL),
        valid_col=pltpu.VMEM((TOKENS, 1), FULL),
        valid_line=pltpu.VMEM((8, TOKENS), FULL),
        pairs=pltpu.VMEM((8, SLOT_ROWS), FULL),
        pairs_col=pltpu.VMEM((SLOT_ROWS, 128), FULL),
        vectors=pltpu.VMEM((PAD, WIDTH), FULL),
        up_bias=pltpu.VMEM((8, WIDE), FULL),
        qkv_bias=pltpu.VMEM((8, 3 * WIDTH), FULL),
        smalls=pltpu.VMEM((PAD, CHIPS * 128), LOW),
        wa=pltpu.VMEM((WIDTH, 4 * WIDTH), LOW),
        wb=pltpu.VMEM((WIDTH, WIDE), LOW),
        wc=pltpu.VMEM((WIDE, WIDTH), LOW),
        chosen=pltpu.VMEM((GROUPS, SLOT_ROWS, VOCAB_ROWS), LOW),
        by_row=pltpu.VMEM((VOCAB_ROWS, (GROUPS + 1) * SLOT_ROWS), LOW),
        rows=pltpu.VMEM((GROUPS, SLOT_ROWS, WIDTH), LOW),
        replies=pltpu.VMEM((GROUPS, SLOT_ROWS, WIDTH), LOW),
        slot_query=pltpu.VMEM((GROUPS, SLOT_ROWS, WIDTH), LOW),
        extra=pltpu.VMEM((SLOT_ROWS, WIDTH), LOW),
        embedded=pltpu.VMEM((TOKENS, WIDTH), LOW),
        qkv=pltpu.VMEM((TOKENS, 3 * WIDTH), LOW),
        context=pltpu.VMEM((TOKENS, WIDTH), LOW),
        tile_low=pltpu.VMEM((BLOCK, WIDTH), LOW),
        tile_sum=pltpu.VMEM((BLOCK, WIDTH), FULL),
        table_full=pltpu.VMEM((VOCAB_ROWS, WIDTH), FULL),
        probs=pltpu.VMEM((PAIR_ROWS, TOKENS), FULL),
        normed_one=pltpu.VMEM((PAD, WIDTH), FULL),
        units=gathered(WIDTH),
        early=gathered(2 * WIDTH),
        downs=gathered(WIDTH),
        attends=gathered(2 * WIDTH),
        queries=gathered(2 * WIDTH),
        slopes=pltpu.VMEM((SLOT_ROWS, WIDE // 2), LOW),
        hidden_turned=pltpu.VMEM((WIDTH, SLOT_ROWS), LOW),
        active_turned=pltpu.VMEM((2 * deep, SLOT_ROWS), LOW),
        down_both=pltpu.VMEM((2 * deep, WIDTH), FULL),
        left_turned=pltpu.VMEM((128, SLOT_ROWS), LOW),
        mail_one=pltpu.VMEM((DEVICES, 80, 128), LOW),
        got_one=pltpu.VMEM((DEVICES, 80, 128), LOW),
        mail_two=pltpu.VMEM((DEVICES, 48, 128), LOW),
        got_two=pltpu.VMEM((DEVICES, 48, 128), LOW),
        mail_three=pltpu.VMEM((DEVICES, PAD, 128), LOW),
        got_three=pltpu.VMEM((DEVICES, PAD, 128), LOW),
        ids_send=dma((DEVICES,)),
        ids_recv=dma((DEVICES,)),
        rows_send=dma((DEVICES,)),
        rows_recv=dma((DEVICES,)),
        one_send=dma((DEVICES,)),
        one_recv=dma((DEVICES,)),
        two_send=dma((DEVICES,)),
        two_recv=dma((DEVICES,)),
        three_send=dma((DEVICES,)),
        three_recv=dma((DEVICES,)),
        small_send=dma((CHIPS,)),
        small_recv=dma((CHIPS,)),
        weight_send=dma((3, 33)),
        weight_recv=dma((3, 33)),
        gather_send=dma((5, 13)),
        gather_recv=dma((5, 13)),
        half_send=dma((3,)),
        half_recv=dma((3,)),
        out_sem=dma((TOKENS // BLOCK,)),
        table_sem=dma((VOCAB_ROWS // BLOCK,)),
    )
    names = INPUTS + OUTPUTS + list(scratch)
    return pl.pallas_call(
        partial(layer_kernel, names),
        out_shape=tuple(jax.ShapeDtypeStruct(*outputs[name]) for name in OUTPUTS),
        in_specs=[vmem] * len(INPUTS),
        out_specs=(anywhere, anywhere) + (vmem,) * (len(OUTPUTS) - 2),
        scratch_shapes=list(scratch.values()),
        compiler_params=pltpu.CompilerParams(
            collective_id=0, has_side_effects=True, vmem_limit_bytes=VMEM_LIMIT
        ),
        name="layer",
    )(*inputs)


def finish_kernel(count, *refs):
    large, (small, loss), outs = refs[:count], refs[count : count + 2], refs[count + 2 : -1]
    sems = refs[-1]
    copies = []
    for index, (source, target) in enumerate(zip(large, outs)):
        part = source if source.shape == target.shape else source.at[: target.shape[0]]
        copies.append(pltpu.make_async_copy(part, target, sems.at[index]))
        copies[-1].start()
    for row, target in zip([0, 1, 6, 2, 3, 16, 7, 4, 5], outs[count : count + 9]):
        size = target.shape[0]
        target[...] = small[row : row + 1, 0:size].reshape(size)
    outs[-1][...] = loss[...].reshape(1)
    for one in copies:
        one.wait()


def finish(results):
    vmem = pl.BlockSpec(memory_space=pltpu.VMEM)
    anywhere = pl.BlockSpec(memory_space=pl.ANY)
    depth, deep = WIDTH // CHIPS, WIDE // CHIPS
    count = len(results) - 2
    shapes = [(one.shape, one.dtype) for one in results[:count]]
    shapes[6] = ((depth, WIDE), FULL)
    shapes += [((depth,), FULL)] * 5 + [((deep,), FULL)] + [((depth,), FULL)] * 3
    shapes.append(((1,), FULL))
    return pl.pallas_call(
        partial(finish_kernel, count),
        out_shape=tuple(jax.ShapeDtypeStruct(*one) for one in shapes),
        in_specs=[anywhere] * count + [vmem] * 2,
        out_specs=(anywhere,) * count + (vmem,) * 10,
        scratch_shapes=[pltpu.SemaphoreType.DMA((count,))],
        name="finish",
    )(*results)


def block_body(
    table,
    token_ids,
    sent_lengths,
    pair_slot,
    pair_lang,
    *parameters,
):
    results = finish(layer((table, token_ids, sent_lengths, pair_slot, pair_lang) + parameters))
    layer_out, table_grad, g_wq, g_wk, g_wv, g_wo, g_wup, g_wdown = results[:8]
    g_bq, g_bv, g_bo, g_g1, g_s1, g_bup, g_bdown, g_g2, g_s2, loss = results[8:]
    return (
        layer_out.reshape(token_ids.shape + (WIDTH,)),
        loss.reshape(()),
        table_grad,
        g_wq,
        g_bq,
        g_wk,
        g_wv,
        g_bv,
        g_wo,
        g_bo,
        g_g1,
        g_s1,
        g_wup,
        g_bup,
        g_wdown,
        g_bdown,
        g_g2,
        g_s2,
    )


def solution(mesh):
    in_specs = (
        P(("dp", "fsdp"), None),
        P(("dp", "fsdp"), None),
        P(("dp", "fsdp")),
        P(),
        P(),
        P("fsdp", None),
        P("fsdp"),
        P("fsdp", None),
        P("fsdp", None),
        P("fsdp"),
        P("fsdp", None),
        P("fsdp"),
        P("fsdp"),
        P("fsdp"),
        P("fsdp", None),
        P("fsdp"),
        P("fsdp", None),
        P("fsdp"),
        P("fsdp"),
        P("fsdp"),
    )
    out_specs = (
        P(("dp", "fsdp"), None, None),
        P(),
        P(("dp", "fsdp"), None),
        P("fsdp", None),
        P("fsdp"),
        P("fsdp", None),
        P("fsdp", None),
        P("fsdp"),
        P("fsdp", None),
        P("fsdp"),
        P("fsdp"),
        P("fsdp"),
        P("fsdp", None),
        P("fsdp"),
        P("fsdp", None),
        P("fsdp"),
        P("fsdp"),
        P("fsdp"),
    )
    sizes = dict(mesh.shape)
    body = general_body
    if sizes["dp"] == CORES and sizes["fsdp"] == CHIPS:
        body = block_body
    return jax.shard_map(body, mesh=mesh, in_specs=in_specs, out_specs=out_specs, check_vma=False)
```

```python
from functools import partial
from types import SimpleNamespace

import jax
import jax.numpy as jnp
from jax import lax
from jax.experimental import pallas as pl
from jax.experimental.pallas import tpu as pltpu
from jax.sharding import PartitionSpec as P

HEADS = 12
HEAD = 64
LANGS = 109


EPSILON = 1e-06
SCORE_SCALE = 50.0
MARGIN_WIDTH = 0.3
MASK_FLOOR = -1000000000.0


def contract(left_side, right_side, left_dim, right_dim):
    return lax.dot_general(
        left_side,
        right_side,
        (((left_dim,), (right_dim,)), ((), ())),
        preferred_element_type=jnp.float32,
    )


def norm_rows(inputs, ln_gain, ln_shift):
    row_mean = jnp.mean(inputs, axis=-1, keepdims=True)
    centered = inputs - row_mean
    variance = jnp.mean(centered * centered, axis=-1, keepdims=True)
    inverse = lax.rsqrt(variance + EPSILON)
    normed = centered * inverse
    return (normed * ln_gain + ln_shift, normed, inverse)


def norm_back(grad_output, normed, inverse, ln_gain):
    grad_normed = grad_output * ln_gain
    first_term = jnp.mean(grad_normed, axis=-1, keepdims=True)
    second_term = jnp.mean(grad_normed * normed, axis=-1, keepdims=True)
    grad_input = inverse * (grad_normed - first_term - normed * second_term)
    return (grad_input, jnp.sum(grad_output * normed, axis=0), jnp.sum(grad_output, axis=0))


def general_body(
    table,
    token_ids,
    sent_lengths,
    pair_slot,
    pair_lang,
    w_query,
    b_query,
    w_key,
    w_value,
    b_value,
    w_out,
    b_out,
    ln1_gain,
    ln1_bias,
    w_up,
    b_up,
    w_down,
    b_down,
    ln2_gain,
    ln2_bias,
):
    sentences, length = token_ids.shape
    tokens = sentences * length
    vocab_rows, model_width = table.shape
    owners = lax.axis_size(("dp", "fsdp"))
    dp_count = lax.axis_size("dp")
    fsdp_count = lax.axis_size("fsdp")
    capacity = max(2, 2 * tokens // owners)
    device = lax.axis_index(("dp", "fsdp"))
    score_factor = HEAD ** (-0.5)
    flat_ids = token_ids.reshape(tokens)
    owner_of = flat_ids // vocab_rows
    member = (owner_of[:, None] == jnp.arange(owners, dtype=jnp.int32)[None, :]).astype(jnp.int32)
    owner_rank = jnp.sum(jnp.cumsum(member, axis=0) * member, axis=1) - 1
    slot_of = owner_of * capacity + owner_rank
    requests = jnp.full((owners * capacity,), -1, jnp.int32).at[slot_of].set(flat_ids)
    received = lax.all_to_all(
        lax.all_to_all(
            requests.reshape(dp_count, fsdp_count, capacity),
            "dp",
            split_axis=0,
            concat_axis=0,
            tiled=True,
        ),
        "fsdp",
        split_axis=1,
        concat_axis=1,
        tiled=True,
    )
    present = received >= 0
    local_rows = jnp.where(present, received - device * vocab_rows, 0)
    found_rows = jnp.where(present[..., None], table[local_rows], jnp.zeros((), table.dtype))
    replies = lax.all_to_all(
        lax.all_to_all(found_rows, "dp", split_axis=0, concat_axis=0, tiled=True),
        "fsdp",
        split_axis=1,
        concat_axis=1,
        tiled=True,
    )
    embedded = replies.reshape(owners * capacity, model_width)[slot_of]
    gathered = (
        lax.all_gather(w_query, "fsdp", axis=0, tiled=True),
        lax.all_gather(b_query, "fsdp", axis=0, tiled=True),
        lax.all_gather(w_key, "fsdp", axis=0, tiled=True),
        lax.all_gather(w_value, "fsdp", axis=0, tiled=True),
        lax.all_gather(b_value, "fsdp", axis=0, tiled=True),
        lax.all_gather(w_out, "fsdp", axis=0, tiled=True),
        lax.all_gather(b_out, "fsdp", axis=0, tiled=True),
        lax.all_gather(ln1_gain, "fsdp", axis=0, tiled=True),
        lax.all_gather(ln1_bias, "fsdp", axis=0, tiled=True),
        lax.all_gather(w_up, "fsdp", axis=0, tiled=True),
        lax.all_gather(b_up, "fsdp", axis=0, tiled=True),
        lax.all_gather(w_down, "fsdp", axis=0, tiled=True),
        lax.all_gather(b_down, "fsdp", axis=0, tiled=True),
        lax.all_gather(ln2_gain, "fsdp", axis=0, tiled=True),
        lax.all_gather(ln2_bias, "fsdp", axis=0, tiled=True),
    )
    (
        full_wq,
        full_bq,
        full_wk,
        full_wv,
        full_bv,
        full_wo,
        full_bo,
        full_g1,
        full_s1,
        full_wup,
        full_bup,
        full_wdown,
        full_bdown,
        full_g2,
        full_s2,
    ) = gathered
    valid_mask = jnp.arange(length, dtype=jnp.int32)[None, :] < sent_lengths[:, None]
    head_shape = (sentences, length, HEADS, HEAD)
    queries = (jnp.dot(embedded, full_wq, preferred_element_type=jnp.float32) + full_bq).astype(
        jnp.bfloat16
    )
    key_heads = (
        jnp.dot(embedded, full_wk, preferred_element_type=jnp.float32)
        .astype(jnp.bfloat16)
        .reshape(head_shape)
    )
    value_heads = (
        (jnp.dot(embedded, full_wv, preferred_element_type=jnp.float32) + full_bv)
        .astype(jnp.bfloat16)
        .reshape(head_shape)
    )
    query_heads = queries.reshape(head_shape)
    scores = (
        jnp.einsum("bqhd,bkhd->bhqk", query_heads, key_heads, preferred_element_type=jnp.float32)
        * score_factor
    )
    scores = jnp.where(valid_mask[:, None, None, :], scores, MASK_FLOOR)
    row_peak = jnp.max(scores, axis=-1, keepdims=True)
    shifted = jnp.exp(scores - row_peak)
    totals = jnp.sum(shifted, axis=-1, keepdims=True)
    attn_probs = (shifted / totals).astype(jnp.bfloat16)
    context = jnp.einsum(
        "bhqk,bkhd->bqhd", attn_probs, value_heads, preferred_element_type=jnp.float32
    )
    context = context.reshape(tokens, model_width).astype(jnp.bfloat16)
    attended = jnp.dot(context, full_wo, preferred_element_type=jnp.float32) + full_bo
    hidden, normed_one, inverse_one = norm_rows(
        embedded.astype(jnp.float32) + attended, full_g1, full_s1
    )
    hidden_low = hidden.astype(jnp.bfloat16)
    up_pre = jnp.dot(hidden_low, full_wup, preferred_element_type=jnp.float32) + full_bup
    activated = jax.nn.gelu(up_pre, approximate=False).astype(jnp.bfloat16)
    down_pre = jnp.dot(activated, full_wdown, preferred_element_type=jnp.float32) + full_bdown
    normed_out, normed_two, inverse_two = norm_rows(hidden + down_pre, full_g2, full_s2)
    layer_out = jnp.where(valid_mask.reshape(tokens)[:, None], normed_out, 0.0).astype(jnp.bfloat16)
    layer_out = layer_out.reshape(sentences, length, model_width)

    def first_rows(matrix):
        return matrix.reshape(sentences, length, matrix.shape[-1])[:, 0]

    summary = first_rows(normed_out)
    magnitude = jnp.sqrt(jnp.sum(summary * summary, axis=-1, keepdims=True) + EPSILON)
    unit_vector = summary / magnitude
    unit_low = unit_vector.astype(jnp.bfloat16)
    every_unit = lax.all_gather(unit_low, ("dp", "fsdp"), axis=0, tiled=True)
    every_side = pair_slot % 2
    every_pair = pair_slot // 2
    my_slots = lax.dynamic_slice_in_dim(pair_slot, device * sentences, sentences)
    my_side = my_slots % 2
    my_pair = my_slots // 2
    lang_onehot = (pair_lang[:, None] == jnp.arange(LANGS, dtype=jnp.int32)[None, :]).astype(
        jnp.float32
    )
    per_lang = jnp.sum(lang_onehot, axis=0)
    per_pair = 1.0 / (2.0 * LANGS * jnp.sum(lang_onehot * per_lang[None, :], axis=1))
    my_weight = jnp.take(per_pair, my_pair)
    opposite = my_side[:, None] != every_side[None, :]
    partner = opposite & (my_pair[:, None] == every_pair[None, :])
    raw_scores = SCORE_SCALE * contract(unit_low, every_unit, 1, 1)
    pair_scores = jnp.where(partner, raw_scores - SCORE_SCALE * MARGIN_WIDTH, raw_scores)
    pair_scores = jnp.where(opposite, pair_scores, MASK_FLOOR)
    pair_peak = jnp.max(pair_scores, axis=1, keepdims=True)
    pair_exp = jnp.exp(pair_scores - pair_peak)
    pair_total = jnp.sum(pair_exp, axis=1, keepdims=True)
    log_total = pair_peak[:, 0] + jnp.log(pair_total[:, 0])
    picked = jnp.sum(jnp.where(partner, pair_scores, 0.0), axis=1)
    loss_value = lax.psum(jnp.sum(my_weight * (log_total - picked)), ("dp", "fsdp"))
    coefficients = (
        my_weight[:, None] * (pair_exp / pair_total - partner.astype(jnp.float32))
    ).astype(jnp.bfloat16)
    unit_grad = SCORE_SCALE * contract(coefficients, every_unit, 1, 0)
    column_terms = SCORE_SCALE * contract(coefficients, unit_low, 0, 0)
    unit_grad = unit_grad + lax.psum_scatter(
        column_terms, ("dp", "fsdp"), scatter_dimension=0, tiled=True
    )
    along = jnp.sum(unit_vector * unit_grad, axis=-1, keepdims=True)
    summary_grad = (unit_grad - unit_vector * along) / magnitude
    again_weights = (
        lax.all_gather(w_query, "fsdp", axis=0, tiled=True),
        lax.all_gather(w_key, "fsdp", axis=0, tiled=True),
        lax.all_gather(w_value, "fsdp", axis=0, tiled=True),
        lax.all_gather(w_out, "fsdp", axis=0, tiled=True),
        lax.all_gather(ln1_gain, "fsdp", axis=0, tiled=True),
        lax.all_gather(w_up, "fsdp", axis=0, tiled=True),
        lax.all_gather(w_down, "fsdp", axis=0, tiled=True),
        lax.all_gather(ln2_gain, "fsdp", axis=0, tiled=True),
    )
    again_wq, again_wk, again_wv, again_wo, again_g1, again_wup, again_wdown, again_g2 = (
        again_weights
    )
    residual_grad, grad_g2, grad_s2 = norm_back(
        summary_grad, first_rows(normed_two), first_rows(inverse_two), again_g2
    )
    down_grad = residual_grad.astype(jnp.bfloat16)
    activated_cls = first_rows(activated)
    act_grad = contract(down_grad, again_wdown, 1, 1)
    gelu_value, gelu_pull = jax.vjp(partial(jax.nn.gelu, approximate=False), first_rows(up_pre))
    up_grad = gelu_pull(act_grad)[0].astype(jnp.bfloat16)
    hidden_cls = first_rows(hidden_low)
    hidden_grad = contract(up_grad, again_wup, 1, 1) + residual_grad
    first_grad, grad_g1, grad_s1 = norm_back(
        hidden_grad, first_rows(normed_one), first_rows(inverse_one), again_g1
    )
    attend_grad = first_grad.astype(jnp.bfloat16)
    context_cls = first_rows(context)
    context_grad = (
        contract(attend_grad, again_wo, 1, 1).astype(jnp.bfloat16).reshape(sentences, HEADS, HEAD)
    )
    query_cls = query_heads[:, 0]
    cls_scores = (
        jnp.einsum("bhd,bkhd->bhk", query_cls, key_heads, preferred_element_type=jnp.float32)
        * score_factor
    )
    cls_scores = jnp.where(valid_mask[:, None, :], cls_scores, MASK_FLOOR)
    cls_probs = jnp.exp(cls_scores - row_peak[:, :, 0]) / totals[:, :, 0]
    prob_grad = jnp.einsum(
        "bhd,bkhd->bhk", context_grad, value_heads, preferred_element_type=jnp.float32
    )
    score_grad = (
        cls_probs * (prob_grad - jnp.sum(cls_probs * prob_grad, axis=-1, keepdims=True))
    ).astype(jnp.bfloat16)
    query_grad = (
        (
            jnp.einsum("bhk,bkhd->bhd", score_grad, key_heads, preferred_element_type=jnp.float32)
            * score_factor
        )
        .astype(jnp.bfloat16)
        .reshape(sentences, model_width)
    )
    key_grad = (
        (
            jnp.einsum("bhk,bhd->bkhd", score_grad, query_cls, preferred_element_type=jnp.float32)
            * score_factor
        )
        .astype(jnp.bfloat16)
        .reshape(tokens, model_width)
    )
    value_grad = (
        jnp.einsum(
            "bhk,bhd->bkhd",
            cls_probs.astype(jnp.bfloat16),
            context_grad,
            preferred_element_type=jnp.float32,
        )
        .astype(jnp.bfloat16)
        .reshape(tokens, model_width)
    )
    embedded_cls = first_rows(embedded)
    grad_wkey = contract(embedded, key_grad, 0, 0)
    grad_wvalue = contract(embedded, value_grad, 0, 0)
    grad_bvalue = jnp.sum(value_grad, axis=0, dtype=jnp.float32)
    row_grads = contract(key_grad, again_wk, 1, 1) + contract(value_grad, again_wv, 1, 1)
    summary_extra = contract(query_grad, again_wq, 1, 1) + first_grad
    row_grads = (
        row_grads.reshape(sentences, length, model_width)
        .at[:, 0]
        .add(summary_extra)
        .reshape(tokens, model_width)
    )
    outgoing = jnp.zeros((owners * capacity, model_width), jnp.float32).at[slot_of].set(row_grads)
    incoming = lax.all_to_all(
        lax.all_to_all(
            outgoing.reshape(dp_count, fsdp_count, capacity, model_width).astype(jnp.bfloat16),
            "dp",
            split_axis=0,
            concat_axis=0,
            tiled=True,
        ),
        "fsdp",
        split_axis=1,
        concat_axis=1,
        tiled=True,
    ).astype(jnp.float32)
    incoming = jnp.where(
        present.reshape(owners * capacity)[:, None],
        incoming.reshape(owners * capacity, model_width),
        0.0,
    )
    table_grad = (
        jnp.zeros((vocab_rows, model_width), jnp.float32)
        .at[local_rows.reshape(owners * capacity)]
        .add(incoming)
    )
    grad_wquery = contract(embedded_cls, query_grad, 0, 0)
    grad_bquery = jnp.sum(query_grad, axis=0, dtype=jnp.float32)
    grad_wout = contract(context_cls, attend_grad, 0, 0)
    grad_bout = jnp.sum(attend_grad, axis=0, dtype=jnp.float32)
    grad_wup = contract(hidden_cls, up_grad, 0, 0)
    grad_bup = jnp.sum(up_grad, axis=0, dtype=jnp.float32)
    grad_wdown = contract(activated_cls, down_grad, 0, 0)
    grad_bdown = jnp.sum(down_grad, axis=0, dtype=jnp.float32)
    owned_grads = (
        lax.psum_scatter(
            grad_wquery.astype(jnp.bfloat16), "fsdp", scatter_dimension=0, tiled=True
        ).astype(jnp.float32),
        lax.psum_scatter(
            grad_bquery.astype(jnp.bfloat16), "fsdp", scatter_dimension=0, tiled=True
        ).astype(jnp.float32),
        lax.psum_scatter(
            grad_wkey.astype(jnp.bfloat16), "fsdp", scatter_dimension=0, tiled=True
        ).astype(jnp.float32),
        lax.psum_scatter(
            grad_wvalue.astype(jnp.bfloat16), "fsdp", scatter_dimension=0, tiled=True
        ).astype(jnp.float32),
        lax.psum_scatter(
            grad_bvalue.astype(jnp.bfloat16), "fsdp", scatter_dimension=0, tiled=True
        ).astype(jnp.float32),
        lax.psum_scatter(
            grad_wout.astype(jnp.bfloat16), "fsdp", scatter_dimension=0, tiled=True
        ).astype(jnp.float32),
        lax.psum_scatter(
            grad_bout.astype(jnp.bfloat16), "fsdp", scatter_dimension=0, tiled=True
        ).astype(jnp.float32),
        lax.psum_scatter(
            grad_g1.astype(jnp.bfloat16), "fsdp", scatter_dimension=0, tiled=True
        ).astype(jnp.float32),
        lax.psum_scatter(
            grad_s1.astype(jnp.bfloat16), "fsdp", scatter_dimension=0, tiled=True
        ).astype(jnp.float32),
        lax.psum_scatter(
            grad_wup.astype(jnp.bfloat16), "fsdp", scatter_dimension=0, tiled=True
        ).astype(jnp.float32),
        lax.psum_scatter(
            grad_bup.astype(jnp.bfloat16), "fsdp", scatter_dimension=0, tiled=True
        ).astype(jnp.float32),
        lax.psum_scatter(
            grad_wdown.astype(jnp.bfloat16), "fsdp", scatter_dimension=0, tiled=True
        ).astype(jnp.float32),
        lax.psum_scatter(
            grad_bdown.astype(jnp.bfloat16), "fsdp", scatter_dimension=0, tiled=True
        ).astype(jnp.float32),
        lax.psum_scatter(
            grad_g2.astype(jnp.bfloat16), "fsdp", scatter_dimension=0, tiled=True
        ).astype(jnp.float32),
        lax.psum_scatter(
            grad_s2.astype(jnp.bfloat16), "fsdp", scatter_dimension=0, tiled=True
        ).astype(jnp.float32),
    )
    summed = (
        lax.psum(owned_grads[0].astype(jnp.bfloat16), "dp").astype(jnp.float32),
        lax.psum(owned_grads[1].astype(jnp.bfloat16), "dp").astype(jnp.float32),
        lax.psum(owned_grads[2].astype(jnp.bfloat16), "dp").astype(jnp.float32),
        lax.psum(owned_grads[3].astype(jnp.bfloat16), "dp").astype(jnp.float32),
        lax.psum(owned_grads[4].astype(jnp.bfloat16), "dp").astype(jnp.float32),
        lax.psum(owned_grads[5].astype(jnp.bfloat16), "dp").astype(jnp.float32),
        lax.psum(owned_grads[6].astype(jnp.bfloat16), "dp").astype(jnp.float32),
        lax.psum(owned_grads[7].astype(jnp.bfloat16), "dp").astype(jnp.float32),
        lax.psum(owned_grads[8].astype(jnp.bfloat16), "dp").astype(jnp.float32),
        lax.psum(owned_grads[9].astype(jnp.bfloat16), "dp").astype(jnp.float32),
        lax.psum(owned_grads[10].astype(jnp.bfloat16), "dp").astype(jnp.float32),
        lax.psum(owned_grads[11].astype(jnp.bfloat16), "dp").astype(jnp.float32),
        lax.psum(owned_grads[12].astype(jnp.bfloat16), "dp").astype(jnp.float32),
        lax.psum(owned_grads[13].astype(jnp.bfloat16), "dp").astype(jnp.float32),
        lax.psum(owned_grads[14].astype(jnp.bfloat16), "dp").astype(jnp.float32),
    )
    return (
        layer_out,
        loss_value,
        table_grad,
        summed[0],
        summed[1],
        summed[2],
        summed[3],
        summed[4],
        summed[5],
        summed[6],
        summed[7],
        summed[8],
        summed[9],
        summed[10],
        summed[11],
        summed[12],
        summed[13],
        summed[14],
    )


CORES = 2
PLANES = 4
LINES = 4
CHIPS = PLANES * LINES
DEVICES = CORES * CHIPS
CAPACITY = 48
GROUPS = 3
PAD = 16
TOKENS = 768
WIDTH = 768
WIDE = 3072
VOCAB_ROWS = 1024
PAIR_ROWS = HEADS * PAD
SLOT_ROWS = DEVICES * PAD
LONG = 64
BLOCK = 256
MESH = pl.DeviceIdType.MESH
LOW = jnp.bfloat16
FULL = jnp.float32
VMEM_LIMIT = 62 * 1024 * 1024

INPUTS = ["table", "token_ids", "lens", "slots", "langs"]
INPUTS += ["wq", "bq", "wk", "wv", "bv", "wo", "bo", "g1", "s1", "wup", "bup", "wdown", "bdown"]
INPUTS += ["g2", "s2"]
OUTPUTS = ["layer_out", "table_grad", "g_wq", "g_wk", "g_wv", "g_wo", "g_wup", "g_wdown"]
OUTPUTS += ["g_small", "loss"]


def place():
    core = lax.axis_index("dp")
    chip = lax.axis_index("fsdp")
    along_x = chip + 1 - 2 * (chip % 2)
    along_y = chip + 2 - 4 * ((chip // 2) % 2)
    first = along_x + core * (along_y - along_x)
    second = along_y + core * (along_x - along_y)
    return core, chip, first, second


def enter():
    core, chip, _, _ = place()
    me = core * CHIPS + chip
    barrier = pltpu.get_barrier_semaphore()

    def greet(step, carry):
        other = (me + step) % DEVICES
        pl.semaphore_signal(
            barrier, inc=1, device_id=(other // CHIPS, other % CHIPS), device_id_type=MESH
        )
        return carry

    lax.fori_loop(1, DEVICES, greet, 0)
    pl.semaphore_wait(barrier, DEVICES - 1)


def remote(source, target, send_sem, recv_sem, core, chip):
    return pltpu.make_async_remote_copy(
        src_ref=source,
        dst_ref=target,
        send_sem=send_sem,
        recv_sem=recv_sem,
        device_id=(core, chip),
        device_id_type=MESH,
    )


def every(start, stop, act):
    def step(index, carry):
        act(index)
        return carry

    lax.fori_loop(start, stop, step, 0)


def weight_steps(piece, send, recv):
    core, chip, first, second = place()
    plane, line = chip // LINES, chip % LINES
    line_first, line_second = first % LINES, second % LINES
    line_far = line_first + line_second - line
    is_low, is_high = plane > 0, plane < PLANES - 1

    def copy(send_index, recv_index, at, to_core, to_chip, carried=core):
        part = piece(at, carried)
        return remote(part, part, send.at[send_index], recv.at[recv_index], to_core, to_chip)

    def up(at_plane):
        return copy(at_plane, at_plane, at_plane * LINES + line, core, chip + LINES)

    def down(at_plane, index):
        return copy(index, at_plane, at_plane * LINES + line, core, chip - LINES)

    def side(at_plane, base, at_line, target):
        return copy(base + at_plane, base + at_plane, at_plane * LINES + at_line, core, target)

    def across(at_plane, base, at_line):
        return copy(base + at_plane, base + at_plane, at_plane * LINES + at_line, 1 - core, chip)

    def begin():
        pl.when(is_high)(lambda: up(plane).start())
        pl.when(is_low)(lambda: down(plane, PLANES).start())
        side(plane, 5, line, first).start()
        side(plane, 9, line, second).start()

    def at_distance(distance, act):
        if distance == 0:
            act(plane, None)
            return
        pl.when(plane >= distance)(lambda: act(plane - distance, True))
        pl.when(plane + distance < PLANES)(lambda: act(plane + distance, False))

    def chain(distance):
        def act(at_plane, from_low):
            if from_low:
                up(at_plane).wait_recv()
                pl.when(is_high)(lambda: up(at_plane).start())
            else:
                down(at_plane, at_plane).wait_recv()
                pl.when(is_low)(lambda: down(at_plane, at_plane).start())
            side(at_plane, 5, line, first).start()
            side(at_plane, 9, line, second).start()
            across(at_plane, 17, line).start()

        return partial(at_distance, distance, act)

    def near(distance):
        def act(at_plane, from_low):
            side(at_plane, 5, line_first, first).wait_recv()
            side(at_plane, 13, line_first, second).start()
            across(at_plane, 21, line_first).start()

        return partial(at_distance, distance, act)

    def far(distance):
        def act(at_plane, from_low):
            side(at_plane, 9, line_second, second).wait_recv()
            across(at_plane, 25, line_second).start()
            side(at_plane, 13, line_far, second).wait_recv()
            across(at_plane, 29, line_far).start()

        return partial(at_distance, distance, act)

    def finish():
        for step in range(1, PLANES):
            index = 17 + (plane + step) % PLANES
            copy(index, index, chip, 1 - core, chip, 1 - core).wait_recv()
        every(21, 33, lambda index: copy(index, index, chip, 1 - core, chip, 1 - core).wait_recv())

    def drain():
        def sent(index):
            copy(index, index, chip, 1 - core, chip).wait_send()

        for at_plane in range(PLANES):
            pl.when((plane >= at_plane) & is_high)(partial(sent, at_plane))
            pl.when((plane < at_plane) & is_low)(partial(sent, at_plane))
        pl.when(is_low)(partial(sent, PLANES))
        every(5, 17, sent)
        for step in range(1, PLANES):
            sent(17 + (plane + step) % PLANES)
        every(21, 33, sent)

    moves = [chain(1), near(0), chain(2), near(1), chain(3), far(0)]
    moves += [near(2), far(1), near(3), far(2), far(3)]
    return begin, moves, finish, drain


def gather_steps(buffer, send, recv):
    core, chip, first, second = place()
    plane, line = chip // LINES, chip % LINES
    line_first, line_second = first % LINES, second % LINES
    line_far = line_first + line_second - line
    half = buffer.shape[-1] // 2
    columns = pl.ds(pl.multiple_of(core * half, 128), half)
    others = pl.ds(pl.multiple_of((1 - core) * half, 128), half)

    def copy(index, part, to_core, to_chip):
        return remote(part, part, send.at[index], recv.at[index], to_core, to_chip)

    def own(at):
        return buffer.at[at, plane, line]

    def chip_part(at_plane, at_line, which):
        return buffer.at[:, at_plane, at_line, :, which]

    def line_part(at_line, which):
        return buffer.at[:, :, at_line, :, which]

    def start():
        copy(0, own(core), 1 - core, chip).start()

    def planes():
        copy(0, own(1 - core), 1 - core, chip).wait_recv()
        for step in range(1, PLANES):
            part = chip_part(plane, line, columns)
            copy(step, part, core, (chip + LINES * step) % CHIPS).start()

    def sides():
        for step in range(1, PLANES):
            part = chip_part((plane + PLANES - step) % PLANES, line, columns)
            copy(step, part, core, chip).wait_recv()
        copy(4, line_part(line, columns), core, first).start()
        copy(5, line_part(line, columns), core, second).start()
        for step in range(1, PLANES):
            part = chip_part((plane + PLANES - step) % PLANES, line, columns)
            copy(6 + step, part, 1 - core, chip).start()

    def corner():
        copy(4, line_part(line_first, columns), core, first).wait_recv()
        copy(6, line_part(line_first, columns), core, second).start()
        copy(10, line_part(line_first, columns), 1 - core, chip).start()
        copy(5, line_part(line_second, columns), core, second).wait_recv()
        copy(11, line_part(line_second, columns), 1 - core, chip).start()

    def last():
        copy(6, line_part(line_far, columns), core, second).wait_recv()
        copy(12, line_part(line_far, columns), 1 - core, chip).start()

    def finish():
        for step in range(1, PLANES):
            part = chip_part((plane + PLANES - step) % PLANES, line, others)
            copy(6 + step, part, 1 - core, chip).wait_recv()
        copy(10, line_part(line_second, others), 1 - core, chip).wait_recv()
        copy(11, line_part(line_first, others), 1 - core, chip).wait_recv()
        copy(12, line_part(line_far, others), 1 - core, chip).wait_recv()

    def drain():
        copy(0, own(core), 1 - core, chip).wait_send()
        for index in [1, 2, 3, 7, 8, 9]:
            copy(index, chip_part(plane, line, columns), 1 - core, chip).wait_send()
        for index in [4, 5, 6, 10, 11, 12]:
            copy(index, line_part(line, columns), 1 - core, chip).wait_send()

    return [start, planes, sides, corner, last, finish], drain


def iota(shape, axis):
    return lax.broadcasted_iota(jnp.int32, shape, axis)


def as_column(row):
    parts = []
    for start in range(0, row.shape[1], 128):
        tile = jnp.broadcast_to(row[:, start : start + 128], (128, 128))
        parts.append(jnp.transpose(tile)[:, 0:1])
    return jnp.concatenate(parts, axis=0)


def as_row(column):
    parts = []
    for start in range(0, column.shape[0], 128):
        tile = jnp.broadcast_to(column[start : start + 128, :], (128, 128))
        parts.append(jnp.transpose(tile)[0:1, :])
    return jnp.concatenate(parts, axis=1)


def dot(left_side, right_side):
    return contract(left_side, right_side, 1, 0)


def dot_turned(left_side, right_side):
    return contract(left_side, right_side, 1, 1)


def norm_parts(inputs):
    centered = inputs - jnp.mean(inputs, axis=-1, keepdims=True)
    inverse = lax.rsqrt(jnp.mean(centered * centered, axis=-1, keepdims=True) + EPSILON)
    return centered * inverse, inverse


def norm_back_parts(grad_output, normed, inverse, ln_gain):
    grad_normed = grad_output * ln_gain
    first_term = jnp.mean(grad_normed, axis=-1, keepdims=True)
    second_term = jnp.mean(grad_normed * normed, axis=-1, keepdims=True)
    return (
        inverse * (grad_normed - first_term - normed * second_term),
        jnp.sum(grad_output * normed, axis=0, keepdims=True),
        jnp.sum(grad_output, axis=0, keepdims=True),
    )


def gelu_parts(inputs):
    spread = 0.5 * (1.0 + lax.erf(inputs * (0.5**0.5)))
    density = jnp.exp(-0.5 * inputs * inputs) * ((2.0 * 3.141592653589793) ** -0.5)
    return inputs * spread, spread + inputs * density


def gelu(inputs):
    return inputs * (0.5 * (1.0 + lax.erf(inputs * (0.5**0.5))))


def layer_kernel(names, *refs):
    r = SimpleNamespace(**dict(zip(names, refs, strict=True)))
    core, chip, _, _ = place()
    me = core * CHIPS + chip
    here = (core, chip // LINES, chip % LINES)
    scale = HEAD ** (-0.5)
    depth, deep = WIDTH // CHIPS, WIDE // CHIPS
    sentences = TOKENS // LONG

    for j in range(TOKENS // 128):
        r.ids[j : j + 1, :] = jnp.concatenate(
            [r.token_ids[2 * j : 2 * j + 1, :], r.token_ids[2 * j + 1 : 2 * j + 2, :]], axis=1
        )
    r.ids[TOKENS // 128 : 8, :] = jnp.zeros((8 - TOKENS // 128, 128), jnp.int32)
    enter()

    def ids_copy(step):
        other = (me + step) % DEVICES
        return remote(
            r.ids,
            r.every_ids.at[me],
            r.ids_send.at[step],
            r.ids_recv.at[step],
            other // CHIPS,
            other % CHIPS,
        )

    every(1, DEVICES, lambda step: ids_copy(step).start())
    r.every_ids[me] = r.ids[...]

    mine = pl.ds(pl.multiple_of(chip * depth, 16), depth)
    for index, shard in enumerate([r.wq, r.wk, r.wv, r.wo]):
        r.wa[mine, index * WIDTH : (index + 1) * WIDTH] = shard[...]

    def block(ref, rows, columns):
        def piece(at, carried):
            return ref.at[
                pl.ds(pl.multiple_of(at * rows, 16), rows),
                pl.ds(pl.multiple_of(carried * columns, 128), columns),
            ]

        return piece

    begin_a, moves_a, finish_a, drain_a = weight_steps(
        block(r.wa, depth, 2 * WIDTH), r.weight_send.at[0], r.weight_recv.at[0]
    )
    begin_b, moves_b, finish_b, drain_b = weight_steps(
        block(r.wb, depth, WIDE // 2), r.weight_send.at[1], r.weight_recv.at[1]
    )
    begin_c, moves_c, finish_c, drain_c = weight_steps(
        block(r.wc, deep, WIDTH // 2), r.weight_send.at[2], r.weight_recv.at[2]
    )
    begin_a()
    r.wb[mine, :] = r.wup[...]
    begin_b()
    r.wc[pl.ds(pl.multiple_of(chip * deep, 16), deep), :] = r.wdown[...]

    small_here = pl.ds(pl.multiple_of(chip * 128, 128), 128)
    lines = [r.bq, r.bv, r.bo, r.g1, r.s1, r.bdown, r.g2, r.s2]
    lines = [line[...].reshape(1, depth).astype(FULL) for line in lines]
    up_line = r.bup[...].reshape(1, deep).astype(FULL)
    lines += [up_line[:, part * depth : (part + 1) * depth] for part in range(deep // depth)]
    lines.append(jnp.zeros((PAD - len(lines), depth), FULL))
    own_small = jnp.concatenate(lines, axis=0)
    own_small = jnp.concatenate([own_small, jnp.zeros((PAD, 128 - depth), FULL)], axis=1)
    r.smalls[:, small_here] = own_small.astype(LOW)

    def small_copy(step):
        part = r.smalls.at[:, small_here]
        return remote(
            part, part, r.small_send.at[step], r.small_recv.at[step], core, (chip + step) % CHIPS
        )

    every(1, CHIPS, lambda step: small_copy(step).start())

    own_row = jnp.concatenate([r.ids[j : j + 1, :] for j in range(TOKENS // 128)], axis=1)
    owner_row = (own_row // VOCAB_ROWS).astype(FULL)
    owner_col = as_column(owner_row)
    earlier = (owner_row == owner_col) & (iota((TOKENS, TOKENS), 1) < iota((TOKENS, TOKENS), 0))
    own_rank = jnp.sum(earlier.astype(FULL), axis=1, keepdims=True)
    own_group = jnp.floor(own_rank * (1.0 / PAD))
    own_slot = own_group * SLOT_ROWS + owner_col * PAD + (own_rank - own_group * PAD)
    r.slot_col[...] = own_slot
    r.slot_line[0:1, :] = as_row(own_slot)

    ahead = (iota((TOKENS, TOKENS), 0) < iota((TOKENS, TOKENS), 1)).astype(LOW)
    moves_a[0]()
    moves_a[1]()
    every(1, DEVICES, lambda step: ids_copy(step).wait_recv())
    moves_a[2]()
    moves_a[3]()
    all_ids = jnp.concatenate([r.every_ids[:, j, :] for j in range(TOKENS // 128)], axis=1)
    all_owner = all_ids // VOCAB_ROWS
    asked = all_owner == me
    ranks = dot(asked.astype(LOW), ahead)
    r.rank[...] = jnp.where(asked, ranks, -1.0)
    local_row = (all_ids - all_owner * VOCAB_ROWS + 1).astype(FULL)
    r.code[...] = local_row + (iota((DEVICES, TOKENS), 1) // LONG * 2048).astype(FULL)

    def rows_copy(step):
        other = (me + step) % DEVICES
        return remote(
            r.rows.at[:, pl.ds(pl.multiple_of(other * PAD, 16), PAD), :],
            r.replies.at[:, pl.ds(pl.multiple_of(me * PAD, 16), PAD), :],
            r.rows_send.at[step],
            r.rows_recv.at[step],
            other // CHIPS,
            other % CHIPS,
        )

    def pick(source):
        rank = r.rank[pl.ds(source, 1), :]
        code = r.code[pl.ds(source, 1), :]
        here_at = iota((CAPACITY, TOKENS), 0).astype(FULL) == rank
        found = jnp.sum(jnp.where(here_at, code, 0.0), axis=1, keepdims=True)
        sent = jnp.floor(found * (1.0 / 2048))
        row = found - sent * 2048.0 - 1.0
        chosen = (iota((CAPACITY, VOCAB_ROWS), 1).astype(FULL) == row).astype(LOW)
        at = pl.ds(pl.multiple_of(source * PAD, 16), PAD)
        source_sent = sent + (source * PAD).astype(FULL)
        for group in range(GROUPS):
            part = slice(group * PAD, (group + 1) * PAD)
            r.chosen[group, at, :] = chosen[part]
            r.found[group, at, 0:1] = row[part]
            r.found[group, at, 1:2] = source_sent[part]

    quarter_size = DEVICES // 4
    for quarter in range(4):
        now = (me // quarter_size + 1 + quarter) % 4

        def pick_two(index):
            pick(now * quarter_size + 2 * index)
            pick(now * quarter_size + 2 * index + 1)

        every(0, quarter_size // 2, pick_two)
        span = pl.ds(pl.multiple_of(now * quarter_size * PAD, 128), quarter_size * PAD)
        picked = r.chosen[:, span, :].reshape(GROUPS * quarter_size * PAD, VOCAB_ROWS)
        found_rows = dot(picked, r.table[...]).astype(LOW)
        r.rows[:, span, :] = found_rows.reshape(GROUPS, quarter_size * PAD, WIDTH)

        def send(index):
            source = now * quarter_size + (me % quarter_size + index) % quarter_size
            rows_copy((source + DEVICES - me) % DEVICES).start()

        every(1 if quarter == 3 else 0, quarter_size, send)
        moves_a[4 + quarter]()
    own_at = pl.ds(pl.multiple_of(me * PAD, 16), PAD)
    r.replies[:, own_at, :] = r.rows[:, own_at, :]
    begin_c()

    at_sent = iota((1, TOKENS), 1) // LONG
    lens = jnp.concatenate(
        [r.lens[...].reshape(1, sentences).astype(FULL), jnp.zeros((1, PAD - sentences), FULL)],
        axis=1,
    )
    spread_lens = dot(
        jnp.broadcast_to(lens, (8, PAD)).astype(LOW),
        (iota((PAD, TOKENS), 0) == iota((PAD, TOKENS), 1) // LONG).astype(LOW),
    )[0:1]
    valid_row = ((iota((1, TOKENS), 1) - at_sent * LONG).astype(FULL) < spread_lens).astype(FULL)
    r.valid_line[0:1, :] = valid_row
    r.valid_col[...] = as_column(valid_row)

    slots = r.slots[...].reshape(1, DEVICES * sentences)
    gap = jnp.full((1, PAD - sentences), -2, jnp.int32)
    slot_line = jnp.concatenate(
        [
            part
            for device in range(DEVICES)
            for part in (slots[:, device * sentences : (device + 1) * sentences], gap)
        ],
        axis=1,
    )
    side_line = slot_line - slot_line // 2 * 2 + jnp.where(slot_line < 0, 8, 0)
    pair_line = slot_line // 2
    pairs = r.langs.shape[0]
    lang_line = r.langs[...].reshape(1, pairs).astype(FULL)
    lang_line = jnp.concatenate([lang_line, jnp.full((1, -pairs % 128), -1.0, FULL)], axis=1)
    lang_col = as_column(lang_line)
    same_lang = jnp.sum(jnp.where(lang_col == lang_line, 1.0, 0.0), axis=1, keepdims=True)
    per_pair = 1.0 / (2.0 * LANGS * same_lang)
    at_pair = iota((lang_line.shape[1], SLOT_ROWS), 0) == pair_line
    weight_line = jnp.sum(jnp.where(at_pair, per_pair, 0.0), axis=0, keepdims=True)
    r.pairs[0:1, :] = weight_line
    r.pairs[1:2, :] = pair_line.astype(FULL)
    r.pairs[2:3, :] = side_line.astype(FULL)
    r.pairs_col[:, 0:1] = as_column(weight_line)
    r.pairs_col[:, 1:2] = as_column(pair_line.astype(FULL))
    r.pairs_col[:, 2:3] = as_column(side_line.astype(FULL))
    for move in moves_a[8:] + moves_b[:2]:
        move()

    every(1, CHIPS, lambda step: small_copy(step).wait_recv())
    smalls = r.smalls[...].astype(FULL)
    r.vectors[:, 0:WIDTH] = jnp.concatenate(
        [smalls[:, at * 128 : at * 128 + depth] for at in range(CHIPS)], axis=1
    )
    r.up_bias[0:1, :] = jnp.concatenate(
        [
            smalls[8 + part : 9 + part, at * 128 : at * 128 + depth]
            for at in range(CHIPS)
            for part in range(deep // depth)
        ],
        axis=1,
    )

    def vector(index):
        return r.vectors[index : index + 1, :]

    r.qkv_bias[0:1, 0:WIDTH] = vector(0)
    r.qkv_bias[0:1, WIDTH : 2 * WIDTH] = jnp.zeros((1, WIDTH), FULL)
    r.qkv_bias[0:1, 2 * WIDTH : 3 * WIDTH] = vector(1)
    for move in moves_b[2:6]:
        move()

    def first_row(source):
        code = jnp.where(r.rank[pl.ds(source, 1), :] >= 0.0, r.code[pl.ds(source, 1), :], 0.0)
        at_first = iota((PAD, TOKENS), 1) == iota((PAD, TOKENS), 0) * LONG
        found = jnp.sum(jnp.where(at_first, code, 0.0), axis=1, keepdims=True)
        row = found - jnp.floor(found * (1.0 / 2048)) * 2048.0 - 1.0
        r.found[GROUPS, pl.ds(pl.multiple_of(source * PAD, 16), PAD), 0:1] = row

    every(0, DEVICES, first_row)
    for group in range(GROUPS + 1):
        named = as_row(r.found[group, :, 0:1])
        by_row = iota((VOCAB_ROWS, SLOT_ROWS), 0).astype(FULL) == named
        r.by_row[:, group * SLOT_ROWS : (group + 1) * SLOT_ROWS] = by_row.astype(LOW)
    for move in moves_b[6:]:
        move()

    every(1, DEVICES, lambda step: rows_copy(step).wait_recv())

    def embed(tile):
        at = pl.ds(pl.multiple_of(tile * BLOCK, BLOCK), BLOCK)
        lanes = iota((BLOCK, GROUPS * SLOT_ROWS), 1).astype(FULL)
        order = (r.slot_col[at, :] == lanes).astype(LOW)
        replies = r.replies[...].reshape(GROUPS * SLOT_ROWS, WIDTH)
        r.embedded[at, :] = dot(order, replies).astype(LOW)

    every(0, TOKENS // BLOCK, embed)
    moves_c[0]()
    finish_a()
    moves_c[1]()

    def project(tile):
        at = pl.ds(pl.multiple_of(tile * BLOCK, BLOCK), BLOCK)
        r.qkv[:, at] = (dot(r.embedded[...], r.wa[:, at]) + r.qkv_bias[0:1, at]).astype(LOW)

    every(3, 6, project)
    moves_c[2]()
    every(6, 9, project)
    moves_c[3]()

    row_sent = iota((PAIR_ROWS, WIDTH), 0) % PAD
    row_head = iota((PAIR_ROWS, WIDTH), 0) // PAD
    lane_block = iota((PAIR_ROWS, WIDTH), 1) // HEAD
    in_head = row_head == lane_block
    seen = (row_sent == lane_block) & (r.valid_line[0:1, :] > 0.0)
    firsts = (iota((PAD, TOKENS), 1) == iota((PAD, TOKENS), 0) * LONG).astype(LOW)
    real_row = iota((PAD, 1), 0) < sentences

    def spread(rows):
        return jnp.where(in_head, jnp.concatenate([rows] * HEADS, axis=0), jnp.zeros((), LOW))

    def fold(tall):
        tall = jnp.where(in_head, tall, 0.0)
        return sum(tall[head * PAD : (head + 1) * PAD] for head in range(HEADS))

    keys, values = slice(WIDTH, 2 * WIDTH), slice(2 * WIDTH, 3 * WIDTH)
    embedded_cls = dot(firsts, r.embedded[...]).astype(LOW)
    query_cls = (dot(embedded_cls, r.wa[:, 0:WIDTH]) + vector(0)).astype(LOW)
    cls_scores = dot_turned(spread(query_cls), r.qkv[:, keys]) * scale
    cls_scores = jnp.where(seen, cls_scores, MASK_FLOOR)
    cls_peak = jnp.max(cls_scores, axis=1, keepdims=True)
    cls_exp = jnp.where(seen, jnp.exp(cls_scores - cls_peak), 0.0)
    cls_total = jnp.sum(cls_exp, axis=1, keepdims=True)
    cls_probs = cls_exp / jnp.where(cls_total > 0.0, cls_total, 1.0)
    probs_low = cls_probs.astype(LOW)
    r.probs[...] = cls_probs
    context_cls = fold(dot(probs_low, r.qkv[:, values])).astype(LOW)
    moves_c[4]()
    first_cls = (
        embedded_cls.astype(FULL)
        + dot(context_cls, r.wa[:, 3 * WIDTH : 4 * WIDTH])
        + vector(2)
    )
    normed_one, inverse_one = norm_parts(first_cls)
    r.normed_one[...] = normed_one
    hidden_cls = normed_one * vector(3) + vector(4)
    hidden_cls_low = hidden_cls.astype(LOW)
    early_here = r.early.at[here]
    early_here[:, 0:WIDTH] = hidden_cls_low
    early_here[:, WIDTH : 2 * WIDTH] = query_cls
    steps_u, drain_u = gather_steps(r.units, r.gather_send.at[0], r.gather_recv.at[0])
    steps_e, drain_e = gather_steps(r.early, r.gather_send.at[1], r.gather_recv.at[1])
    steps_d, drain_d = gather_steps(r.downs, r.gather_send.at[2], r.gather_recv.at[2])
    steps_a, drain_a2 = gather_steps(r.attends, r.gather_send.at[3], r.gather_recv.at[3])
    steps_q, drain_q = gather_steps(r.queries, r.gather_send.at[4], r.gather_recv.at[4])
    steps_e[0]()
    moves_c[5]()

    half_block = BLOCK // 2

    def attend(unit):
        rows = pl.ds(pl.multiple_of(unit // 3 * half_block, half_block), half_block)
        lane = unit % 3 * BLOCK

        def part(which):
            return r.qkv[rows, pl.ds(pl.multiple_of(which * WIDTH + lane, 128), BLOCK)]

        query, key, value = part(0), part(1), part(2)
        lane_head = iota((half_block, BLOCK), 1) // HEAD
        stacked = jnp.concatenate(
            [jnp.where(lane_head == head, query, jnp.zeros((), LOW)) for head in range(4)], axis=0
        )
        shape = (4 * half_block, half_block)
        same = iota(shape, 0) // LONG % 2 == iota(shape, 1) // LONG
        allowed = same & (r.valid_line[0:1, rows] > 0.0)
        scores = jnp.where(allowed, dot_turned(stacked, key) * scale, MASK_FLOOR)
        shifted = jnp.exp(scores - jnp.max(scores, axis=1, keepdims=True))
        probs = shifted * (1.0 / jnp.sum(shifted, axis=1, keepdims=True))
        mixed = dot(probs.astype(LOW), value)
        result = mixed[0:half_block]
        for head in range(1, 4):
            result = jnp.where(
                lane_head == head, mixed[head * half_block : (head + 1) * half_block], result
            )
        r.context[rows, pl.ds(pl.multiple_of(lane, 128), BLOCK)] = result.astype(LOW)

    def open_tile(tile):
        at = pl.ds(tile * BLOCK, BLOCK)
        attended = dot(r.context[at, :], r.wa[:, 3 * WIDTH : 4 * WIDTH]) + vector(2)
        normed, _ = norm_parts(r.embedded[at, :].astype(FULL) + attended)
        hidden = normed * vector(3) + vector(4)
        r.tile_low[...] = hidden.astype(LOW)
        r.tile_sum[...] = hidden + vector(5)

    def feed_tile(part):
        halves = []
        for half in range(2):
            at = pl.ds(pl.multiple_of((2 * part + half) * BLOCK, BLOCK), BLOCK)
            up_pre = dot(r.tile_low[...], r.wb[:, at]) + r.up_bias[0:1, at]
            halves.append(gelu(up_pre).astype(LOW))
        at = pl.ds(pl.multiple_of(part * 2 * BLOCK, 2 * BLOCK), 2 * BLOCK)
        r.tile_sum[...] += dot(jnp.concatenate(halves, axis=1), r.wc[at, :])

    def layer_copy(tile):
        at = pl.ds(tile * BLOCK, BLOCK)
        return pltpu.make_async_copy(r.context.at[at], r.layer_out.at[at], r.out_sem.at[tile])

    def close_tile(tile):
        at = pl.ds(tile * BLOCK, BLOCK)
        normed, _ = norm_parts(r.tile_sum[...])
        out = normed * vector(6) + vector(7)
        r.context[at, :] = (out * r.valid_col[at, :]).astype(LOW)
        layer_copy(tile).start()

    queue = [partial(every, 0, 3, project)]
    queue += [partial(every, unit, unit + 1, attend) for unit in range(18)]
    late = []
    for tile in range(TOKENS // BLOCK):
        late.append(partial(open_tile, tile))
        late += [partial(every, part, part + 1, feed_tile) for part in range(6)]
        late.append(partial(close_tile, tile))

    def fill(pieces, count):
        for _ in range(min(count, len(pieces))):
            pieces.pop(0)()

    finish_b()
    up_cls = dot(hidden_cls_low, r.wb[...]) + r.up_bias[0:1, :]
    activated_cls, slope_cls = gelu_parts(up_cls)
    activated_low = activated_cls.astype(LOW)
    steps_e[1]()
    for move in moves_c[6:]:
        fill(queue, 4)
        move()

    def pack_tall(tall, target, first_row):
        for at in range(CHIPS):
            columns = tall[:, at * depth : (at + 1) * depth]
            for half in range(CORES):
                base = half * PAIR_ROWS // 2
                target[half * CHIPS + at, first_row : first_row + 48, :] = jnp.concatenate(
                    [
                        columns[base : base + 48],
                        columns[base + 48 : base + 96],
                        jnp.zeros((48, 128 - 2 * depth), FULL),
                    ],
                    axis=1,
                ).astype(LOW)

    def pack_coefs(coefs):
        total = None
        for group in range(GROUPS):
            folds = iota((PAIR_ROWS, 128), 0) // PAD + group * PAD == iota((PAIR_ROWS, 128), 1)
            lanes = contract(coefs, folds.astype(LOW), 0, 0).astype(LOW)
            part = dot(r.rows[group], lanes)
            total = part if total is None else total + part
        return total.astype(LOW).reshape(DEVICES, PAD, 128)

    finish_c()
    down_pre = dot(activated_low, r.wc[...]) + vector(5)
    normed_two, inverse_two = norm_parts(hidden_cls + down_pre)
    summary = normed_two * vector(6) + vector(7)
    magnitude = jnp.sqrt(jnp.sum(summary * summary, axis=-1, keepdims=True) + EPSILON)
    unit = jnp.where(real_row, summary / magnitude, 0.0)
    r.units[here] = unit.astype(LOW)

    steps_u[0]()
    every(1, DEVICES, lambda step: rows_copy(step).wait_send())
    for group in range(GROUPS):
        slot_at = iota((SLOT_ROWS, TOKENS), 0) + group * SLOT_ROWS
        r.rows[group] = (slot_at.astype(FULL) == r.slot_line[0:1, :]).astype(LOW)
    for at in range(CHIPS):
        cut = slice(at * depth, (at + 1) * depth)
        line = jnp.concatenate(
            [
                context_cls.astype(FULL)[:, cut],
                embedded_cls.astype(FULL)[:, cut],
                jnp.zeros((PAD, 128 - 2 * depth), FULL),
            ],
            axis=1,
        ).astype(LOW)
        for half in range(CORES):
            r.mail_one[half * CHIPS + at, 0:PAD, :] = line
    steps_u[1]()
    pack_tall(dot(probs_low, r.embedded[...]), r.mail_one, PAD)
    fill(late, 1)
    steps_u[2]()
    steps_e[2]()
    r.mail_one[:, 64:80, :] = pack_coefs(probs_low)
    fill(late, 1)
    steps_u[3]()
    fill(late, 2)

    def mail_copy(box, got, send, recv, step):
        other = (me + step) % DEVICES
        return remote(
            box.at[other], got.at[me], send.at[step], recv.at[step], other // CHIPS, other % CHIPS
        )

    one = partial(mail_copy, r.mail_one, r.got_one, r.one_send, r.one_recv)
    two = partial(mail_copy, r.mail_two, r.got_two, r.two_send, r.two_recv)
    three = partial(mail_copy, r.mail_three, r.got_three, r.three_send, r.three_recv)
    steps_u[4]()
    r.got_one[me] = r.mail_one[me]
    fill(late, 1)
    steps_u[5]()
    every(1, DEVICES, lambda step: one(step).start())
    steps_e[3]()

    units = r.units[...].reshape(SLOT_ROWS, WIDTH)
    weight_row, pair_row, side_row = r.pairs[0:1, :], r.pairs[1:2, :], r.pairs[2:3, :]

    def pair_scores(rows, pair_col, side_col):
        opposite = side_col + side_row == 1.0
        partner = opposite & (pair_col == pair_row)
        raw = SCORE_SCALE * dot_turned(rows, units)
        shifted = jnp.where(partner, raw - SCORE_SCALE * MARGIN_WIDTH, raw)
        return jnp.where(opposite, shifted, MASK_FLOOR), partner

    every_score, every_partner = pair_scores(
        units, r.pairs_col[:, 1:2], r.pairs_col[:, 2:3]
    )
    peak_row = jnp.max(every_score, axis=0, keepdims=True)
    log_row = peak_row + jnp.log(
        jnp.sum(jnp.exp(every_score - peak_row), axis=0, keepdims=True)
    )
    picked_row = jnp.sum(jnp.where(every_partner, every_score, 0.0), axis=0, keepdims=True)
    r.loss[...] = jnp.sum(weight_row * (log_row - picked_row), axis=1, keepdims=True)

    rows_here = pl.ds(pl.multiple_of(me * PAD, 16), PAD)
    own_score, own_partner = pair_scores(
        r.units[here], r.pairs_col[rows_here, 1:2], r.pairs_col[rows_here, 2:3]
    )
    own_partner = own_partner.astype(FULL)
    own_peak = jnp.max(own_score, axis=1, keepdims=True)
    own_exp = jnp.exp(own_score - own_peak)
    own_share = own_exp / jnp.sum(own_exp, axis=1, keepdims=True)
    by_row = (r.pairs_col[rows_here, 0:1] * (own_share - own_partner)).astype(LOW)
    by_column = (weight_row * (jnp.exp(own_score - log_row) - own_partner)).astype(LOW)
    unit_grad = SCORE_SCALE * (dot(by_row, units) + dot(by_column, units))
    along = jnp.sum(unit * unit_grad, axis=-1, keepdims=True)
    summary_grad = (unit_grad - unit * along) / magnitude

    residual_grad, grad_g2, grad_s2 = norm_back_parts(
        summary_grad, normed_two, inverse_two, vector(6)
    )
    down_grad = residual_grad.astype(LOW)
    r.downs[here] = down_grad
    steps_d[0]()
    act_grad = dot_turned(down_grad, r.wc[...])
    up_grad = (act_grad * slope_cls).astype(LOW)
    steps_d[1]()
    hidden_grad = dot_turned(up_grad, r.wb[...]) + residual_grad
    first_grad, grad_g1, grad_s1 = norm_back_parts(
        hidden_grad, r.normed_one[...], inverse_one, vector(3)
    )
    attend_grad = first_grad.astype(LOW)
    steps_e[4]()
    context_grad = dot_turned(attend_grad, r.wa[:, 3 * WIDTH : 4 * WIDTH]).astype(LOW)
    attend_here = r.attends.at[here]
    attend_here[:, 0:WIDTH] = attend_grad
    attend_here[:, WIDTH : 2 * WIDTH] = context_grad
    steps_a[0]()
    steps_d[2]()
    context_tall = spread(context_grad)
    probs = r.probs[...]
    prob_grad = dot_turned(context_tall, r.qkv[:, values])
    inner = jnp.sum(probs * prob_grad, axis=1, keepdims=True)
    score_grad = (probs * (prob_grad - inner)).astype(LOW)
    steps_a[1]()
    r.mail_three[...] = pack_coefs(score_grad)
    every(1, DEVICES, lambda step: three(step).start())
    r.got_three[me] = r.mail_three[me]
    query_grad = (fold(dot(score_grad, r.qkv[:, keys])) * scale).astype(LOW)
    probs_total = jnp.sum(probs_low.astype(FULL), axis=1, keepdims=True)
    grad_bvalue = jnp.sum(probs_total * context_tall.astype(FULL), axis=0, keepdims=True)
    grad_bquery = jnp.sum(query_grad.astype(FULL), axis=0, keepdims=True)
    query_here = r.queries.at[here]
    query_here[:, 0:WIDTH] = query_grad
    query_here[:, WIDTH : 2 * WIDTH] = jnp.concatenate(
        [grad_bquery, grad_bvalue, grad_g1, grad_s1, grad_g2, grad_s2, jnp.zeros((10, WIDTH))],
        axis=0,
    ).astype(LOW)
    steps_q[0]()
    steps_a[2]()
    pack_tall(dot(score_grad, r.embedded[...]) * scale, r.mail_two, 0)
    steps_q[1]()
    every(1, DEVICES, lambda step: two(step).start())
    r.got_two[me] = r.mail_two[me]

    def all_rows(buffer, start):
        return buffer[:, :, :, :, start : start + WIDTH].reshape(SLOT_ROWS, WIDTH)

    def from_sent(group):
        lanes = iota((SLOT_ROWS, SLOT_ROWS), 1).astype(FULL)
        return (r.found[group, :, 1:2] == lanes).astype(LOW)

    def widened(coefs, group):
        lanes = iota((128, WIDTH), 0) == iota((128, WIDTH), 1) // HEAD + group * PAD
        return dot(coefs, lanes.astype(LOW))

    half_wide = WIDE // 2

    def slope_tile(part):
        at = pl.ds(pl.multiple_of(core * half_wide + part * BLOCK, BLOCK), BLOCK)
        up_pre = dot(all_rows(r.early, 0), r.wb[:, at]) + r.up_bias[0:1, at]
        _, slope = gelu_parts(up_pre)
        r.slopes[:, pl.ds(pl.multiple_of(part * BLOCK, BLOCK), BLOCK)] = slope.astype(LOW)

    def slot_queries(group):
        r.slot_query[group] = dot(from_sent(group), all_rows(r.early, WIDTH)).astype(LOW)

    def activate():
        at = pl.ds(pl.multiple_of(chip // 2 * 2 * deep, 128), 2 * deep)
        up_pre = dot(all_rows(r.early, 0), r.wb[:, at]) + r.up_bias[0:1, at]
        r.active_turned[...] = jnp.transpose(gelu(up_pre)).astype(LOW)
        r.hidden_turned[...] = jnp.transpose(all_rows(r.early, 0))

    steps_e[5]()
    between = [partial(slot_queries, group) for group in range(GROUPS)]
    between += [partial(every, part, part + 1, slope_tile) for part in range(6)]
    between.append(activate)

    between += late
    late.clear()
    rest = [steps_d[3], steps_a[3], steps_q[2], steps_d[4], steps_a[4], steps_q[3]]
    rest += [steps_d[5], steps_a[5], steps_q[4]]
    for step in rest:
        step()
        fill(between, 2)
    fill(between, len(between))

    every(1, DEVICES, lambda step: one(step).wait_recv())
    got_probs = r.got_one[:, 64:80, :].reshape(SLOT_ROWS, 128)
    for group in range(GROUPS):
        slot_context = dot(from_sent(group), all_rows(r.attends, WIDTH))
        r.replies[group] = (widened(got_probs, group) * slot_context).astype(LOW)

    def head_products(got, first_row, right, start, target):
        for pair in range(HEADS // 4):
            lane = pl.ds(pl.multiple_of(start + (core * (HEADS // 4) + pair) * 128, 128), 128)
            pair_rows = right[:, :, :, :, lane].reshape(SLOT_ROWS, 128)
            parts = []
            for half in range(2):
                head = 2 * pair + half
                row = first_row + head % 3 * PAD
                block_rows = got[:, row : row + PAD, :].reshape(SLOT_ROWS, 128)
                product = contract(block_rows, pair_rows, 0, 0)
                column = head // 3 * depth
                parts.append(product[column : column + depth, :])
            low_lanes = iota((depth, 128), 1) < HEAD
            result = jnp.where(low_lanes, parts[0], parts[1])
            target[:, pl.ds(pl.multiple_of((core * (HEADS // 4) + pair) * 128, 128), 128)] = result

    def half_of(ref, at_core):
        half = ref.shape[1] // 2
        return ref.at[:, pl.ds(pl.multiple_of(at_core * half, 128), half)]

    def half_copy(index, ref, at_core):
        part = half_of(ref, at_core)
        return remote(part, part, r.half_send.at[index], r.half_recv.at[index], 1 - core, chip)

    head_products(r.got_one, PAD, r.attends, WIDTH, r.g_wv)
    half_copy(0, r.g_wv, core).start()

    downs = r.downs[...].reshape(SLOT_ROWS, WIDTH)
    attends = all_rows(r.attends, 0)

    def up_tile(part):
        at = pl.ds(pl.multiple_of(core * half_wide + part * BLOCK, BLOCK), BLOCK)
        slope = r.slopes[:, pl.ds(pl.multiple_of(part * BLOCK, BLOCK), BLOCK)].astype(FULL)
        up_all = (dot_turned(r.downs[...].reshape(SLOT_ROWS, WIDTH), r.wc[at, :]) * slope)
        up_all = up_all.astype(LOW)
        r.g_wup[0:depth, at] = dot(r.hidden_turned[mine, :], up_all)
        total = jnp.sum(up_all.astype(FULL), axis=0, keepdims=True)
        r.g_wup[depth : depth + 8, at] = jnp.broadcast_to(total, (8, BLOCK))

    every(0, half_wide // BLOCK, up_tile)
    half_copy(1, r.g_wup, core).start()
    r.down_both[...] = dot(r.active_turned[...], downs)
    r.g_wdown[...] = r.down_both[pl.ds(pl.multiple_of(chip % 2 * deep, 16), deep), :]
    r.left_turned[...] = jnp.transpose(r.got_one[:, 0:PAD, :].reshape(SLOT_ROWS, 128))
    r.g_wo[...] = dot(r.left_turned[0:depth, :], attends)
    own_lanes = (iota((WIDTH, 128), 0) == chip * depth + iota((WIDTH, 128), 1)).astype(LOW)

    def own_part(rows, select):
        total = None
        for _ in range(3):
            part = rows.astype(LOW)
            rows = rows - part.astype(FULL)
            picked = dot(part, select)
            total = picked if total is None else total + picked
        return total

    every(1, DEVICES, lambda step: three(step).wait_recv())
    got_scores = r.got_three[...].reshape(SLOT_ROWS, 128)
    for group in range(GROUPS):
        slot_query = r.slot_query[group].astype(FULL)
        key_grad = (widened(got_scores, group) * slot_query * scale).astype(LOW)
        row_grad = dot_turned(key_grad, r.wa[:, keys])
        row_grad = row_grad + dot_turned(r.replies[group], r.wa[:, values])
        r.rows[group] = row_grad.astype(LOW)
    steps_q[5]()
    query_grads = all_rows(r.queries, 0)
    extra = dot_turned(query_grads, r.wa[:, 0:WIDTH]) + attends.astype(FULL)
    r.extra[...] = extra.astype(LOW)
    r.g_wq[...] = dot(r.left_turned[depth : 2 * depth, :], query_grads)

    def table_copy(tile):
        at = pl.ds(pl.multiple_of(tile * BLOCK, BLOCK), BLOCK)
        return pltpu.make_async_copy(
            r.table_full.at[at], r.table_grad.at[at], r.table_sem.at[tile]
        )

    def table_tile(tile):
        at = pl.ds(pl.multiple_of(tile * BLOCK, BLOCK), BLOCK)
        slot_rows = r.rows[...].reshape(GROUPS * SLOT_ROWS, WIDTH)
        r.table_full[at, :] = dot(r.by_row[at, 0 : GROUPS * SLOT_ROWS], slot_rows) + dot(
            r.by_row[at, GROUPS * SLOT_ROWS :], r.extra[...]
        )
        table_copy(tile).start()

    every(0, VOCAB_ROWS // BLOCK, table_tile)
    every(1, DEVICES, lambda step: two(step).wait_recv())
    head_products(r.got_two, 0, r.early, WIDTH, r.g_wk)
    half_copy(2, r.g_wk, core).start()

    down_total = jnp.sum(downs.astype(FULL), axis=0, keepdims=True)
    attend_total = jnp.sum(attends.astype(FULL), axis=0, keepdims=True)
    device_sums = (iota((PAD, SLOT_ROWS), 1) % PAD == iota((PAD, SLOT_ROWS), 0)).astype(LOW)
    sums = dot(device_sums, all_rows(r.queries, WIDTH))
    stacked = jnp.concatenate(
        [sums[0:6], attend_total, down_total, jnp.zeros((8, WIDTH), FULL)], axis=0
    )
    r.g_small[0:16, 0:128] = own_part(stacked, own_lanes)
    r.g_small[0:16, 128:BLOCK] = jnp.zeros((PAD, BLOCK - 128), FULL)
    half_copy(1, r.g_wup, 1 - core).wait_recv()
    up_lanes = (iota((WIDE, BLOCK), 0) == chip * deep + iota((WIDE, BLOCK), 1)).astype(LOW)
    r.g_small[16:24, :] = own_part(r.g_wup[depth : depth + 8, :], up_lanes)

    half_copy(0, r.g_wv, 1 - core).wait_recv()
    half_copy(2, r.g_wk, 1 - core).wait_recv()
    for index, ref in enumerate([r.g_wv, r.g_wup, r.g_wk]):
        half_copy(index, ref, core).wait_send()

    def drain(step):
        ids_copy(step).wait_send()
        one(step).wait_send()
        two(step).wait_send()
        three(step).wait_send()

    every(1, DEVICES, drain)
    every(1, CHIPS, lambda step: small_copy(step).wait_send())
    for end in [drain_a, drain_b, drain_c, drain_u, drain_e, drain_d, drain_a2, drain_q]:
        end()
    for tile in range(TOKENS // BLOCK):
        layer_copy(tile).wait()
    every(0, VOCAB_ROWS // BLOCK, lambda tile: table_copy(tile).wait())


def layer(inputs):
    dma = pltpu.SemaphoreType.DMA
    vmem = pl.BlockSpec(memory_space=pltpu.VMEM)
    anywhere = pl.BlockSpec(memory_space=pl.ANY)
    depth, deep = WIDTH // CHIPS, WIDE // CHIPS

    def gathered(width):
        return pltpu.VMEM((CORES, PLANES, LINES, PAD, width), LOW)

    outputs = dict(
        layer_out=((TOKENS, WIDTH), LOW),
        table_grad=((VOCAB_ROWS, WIDTH), FULL),
        g_wq=((depth, WIDTH), FULL),
        g_wk=((depth, WIDTH), FULL),
        g_wv=((depth, WIDTH), FULL),
        g_wo=((depth, WIDTH), FULL),
        g_wup=((depth + 8, WIDE), FULL),
        g_wdown=((deep, WIDTH), FULL),
        g_small=((24, BLOCK), FULL),
        loss=((1, 1), FULL),
    )
    scratch = dict(
        ids=pltpu.VMEM((8, 128), jnp.int32),
        every_ids=pltpu.VMEM((DEVICES, 8, 128), jnp.int32),
        rank=pltpu.VMEM((DEVICES, TOKENS), FULL),
        code=pltpu.VMEM((DEVICES, TOKENS), FULL),
        found=pltpu.VMEM((GROUPS + 1, SLOT_ROWS, 2), FULL),
        slot_col=pltpu.VMEM((TOKENS, 1), FULL),
        slot_line=pltpu.VMEM((8, TOKENS), FULL),
        valid_col=pltpu.VMEM((TOKENS, 1), FULL),
        valid_line=pltpu.VMEM((8, TOKENS), FULL),
        pairs=pltpu.VMEM((8, SLOT_ROWS), FULL),
        pairs_col=pltpu.VMEM((SLOT_ROWS, 128), FULL),
        vectors=pltpu.VMEM((PAD, WIDTH), FULL),
        up_bias=pltpu.VMEM((8, WIDE), FULL),
        qkv_bias=pltpu.VMEM((8, 3 * WIDTH), FULL),
        smalls=pltpu.VMEM((PAD, CHIPS * 128), LOW),
        wa=pltpu.VMEM((WIDTH, 4 * WIDTH), LOW),
        wb=pltpu.VMEM((WIDTH, WIDE), LOW),
        wc=pltpu.VMEM((WIDE, WIDTH), LOW),
        chosen=pltpu.VMEM((GROUPS, SLOT_ROWS, VOCAB_ROWS), LOW),
        by_row=pltpu.VMEM((VOCAB_ROWS, (GROUPS + 1) * SLOT_ROWS), LOW),
        rows=pltpu.VMEM((GROUPS, SLOT_ROWS, WIDTH), LOW),
        replies=pltpu.VMEM((GROUPS, SLOT_ROWS, WIDTH), LOW),
        slot_query=pltpu.VMEM((GROUPS, SLOT_ROWS, WIDTH), LOW),
        extra=pltpu.VMEM((SLOT_ROWS, WIDTH), LOW),
        embedded=pltpu.VMEM((TOKENS, WIDTH), LOW),
        qkv=pltpu.VMEM((TOKENS, 3 * WIDTH), LOW),
        context=pltpu.VMEM((TOKENS, WIDTH), LOW),
        tile_low=pltpu.VMEM((BLOCK, WIDTH), LOW),
        tile_sum=pltpu.VMEM((BLOCK, WIDTH), FULL),
        table_full=pltpu.VMEM((VOCAB_ROWS, WIDTH), FULL),
        probs=pltpu.VMEM((PAIR_ROWS, TOKENS), FULL),
        normed_one=pltpu.VMEM((PAD, WIDTH), FULL),
        units=gathered(WIDTH),
        early=gathered(2 * WIDTH),
        downs=gathered(WIDTH),
        attends=gathered(2 * WIDTH),
        queries=gathered(2 * WIDTH),
        slopes=pltpu.VMEM((SLOT_ROWS, WIDE // 2), LOW),
        hidden_turned=pltpu.VMEM((WIDTH, SLOT_ROWS), LOW),
        active_turned=pltpu.VMEM((2 * deep, SLOT_ROWS), LOW),
        down_both=pltpu.VMEM((2 * deep, WIDTH), FULL),
        left_turned=pltpu.VMEM((128, SLOT_ROWS), LOW),
        mail_one=pltpu.VMEM((DEVICES, 80, 128), LOW),
        got_one=pltpu.VMEM((DEVICES, 80, 128), LOW),
        mail_two=pltpu.VMEM((DEVICES, 48, 128), LOW),
        got_two=pltpu.VMEM((DEVICES, 48, 128), LOW),
        mail_three=pltpu.VMEM((DEVICES, PAD, 128), LOW),
        got_three=pltpu.VMEM((DEVICES, PAD, 128), LOW),
        ids_send=dma((DEVICES,)),
        ids_recv=dma((DEVICES,)),
        rows_send=dma((DEVICES,)),
        rows_recv=dma((DEVICES,)),
        one_send=dma((DEVICES,)),
        one_recv=dma((DEVICES,)),
        two_send=dma((DEVICES,)),
        two_recv=dma((DEVICES,)),
        three_send=dma((DEVICES,)),
        three_recv=dma((DEVICES,)),
        small_send=dma((CHIPS,)),
        small_recv=dma((CHIPS,)),
        weight_send=dma((3, 33)),
        weight_recv=dma((3, 33)),
        gather_send=dma((5, 13)),
        gather_recv=dma((5, 13)),
        half_send=dma((3,)),
        half_recv=dma((3,)),
        out_sem=dma((TOKENS // BLOCK,)),
        table_sem=dma((VOCAB_ROWS // BLOCK,)),
    )
    names = INPUTS + OUTPUTS + list(scratch)
    return pl.pallas_call(
        partial(layer_kernel, names),
        out_shape=tuple(jax.ShapeDtypeStruct(*outputs[name]) for name in OUTPUTS),
        in_specs=[vmem] * len(INPUTS),
        out_specs=(anywhere, anywhere) + (vmem,) * (len(OUTPUTS) - 2),
        scratch_shapes=list(scratch.values()),
        compiler_params=pltpu.CompilerParams(
            collective_id=0, has_side_effects=True, vmem_limit_bytes=VMEM_LIMIT
        ),
        name="layer",
    )(*inputs)


def finish_kernel(count, *refs):
    large, (small, loss), outs = refs[:count], refs[count : count + 2], refs[count + 2 : -1]
    sems = refs[-1]
    copies = []
    for index, (source, target) in enumerate(zip(large, outs)):
        part = source if source.shape == target.shape else source.at[: target.shape[0]]
        copies.append(pltpu.make_async_copy(part, target, sems.at[index]))
        copies[-1].start()
    for row, target in zip([0, 1, 6, 2, 3, 16, 7, 4, 5], outs[count : count + 9]):
        size = target.shape[0]
        target[...] = small[row : row + 1, 0:size].reshape(size)
    outs[-1][...] = loss[...].reshape(1)
    for one in copies:
        one.wait()


def finish(results):
    vmem = pl.BlockSpec(memory_space=pltpu.VMEM)
    anywhere = pl.BlockSpec(memory_space=pl.ANY)
    depth, deep = WIDTH // CHIPS, WIDE // CHIPS
    count = len(results) - 2
    shapes = [(one.shape, one.dtype) for one in results[:count]]
    shapes[6] = ((depth, WIDE), FULL)
    shapes += [((depth,), FULL)] * 5 + [((deep,), FULL)] + [((depth,), FULL)] * 3
    shapes.append(((1,), FULL))
    return pl.pallas_call(
        partial(finish_kernel, count),
        out_shape=tuple(jax.ShapeDtypeStruct(*one) for one in shapes),
        in_specs=[vmem] * (count + 2),
        out_specs=(anywhere,) * count + (vmem,) * 10,
        scratch_shapes=[pltpu.SemaphoreType.DMA((count,))],
        name="finish",
    )(*results)


def block_body(
    table,
    token_ids,
    sent_lengths,
    pair_slot,
    pair_lang,
    *parameters,
):
    results = finish(layer((table, token_ids, sent_lengths, pair_slot, pair_lang) + parameters))
    layer_out, table_grad, g_wq, g_wk, g_wv, g_wo, g_wup, g_wdown = results[:8]
    g_bq, g_bv, g_bo, g_g1, g_s1, g_bup, g_bdown, g_g2, g_s2, loss = results[8:]
    return (
        layer_out.reshape(token_ids.shape + (WIDTH,)),
        loss.reshape(()),
        table_grad,
        g_wq,
        g_bq,
        g_wk,
        g_wv,
        g_bv,
        g_wo,
        g_bo,
        g_g1,
        g_s1,
        g_wup,
        g_bup,
        g_wdown,
        g_bdown,
        g_g2,
        g_s2,
    )


def solution(mesh):
    in_specs = (
        P(("dp", "fsdp"), None),
        P(("dp", "fsdp"), None),
        P(("dp", "fsdp")),
        P(),
        P(),
        P("fsdp", None),
        P("fsdp"),
        P("fsdp", None),
        P("fsdp", None),
        P("fsdp"),
        P("fsdp", None),
        P("fsdp"),
        P("fsdp"),
        P("fsdp"),
        P("fsdp", None),
        P("fsdp"),
        P("fsdp", None),
        P("fsdp"),
        P("fsdp"),
        P("fsdp"),
    )
    out_specs = (
        P(("dp", "fsdp"), None, None),
        P(),
        P(("dp", "fsdp"), None),
        P("fsdp", None),
        P("fsdp"),
        P("fsdp", None),
        P("fsdp", None),
        P("fsdp"),
        P("fsdp", None),
        P("fsdp"),
        P("fsdp"),
        P("fsdp"),
        P("fsdp", None),
        P("fsdp"),
        P("fsdp", None),
        P("fsdp"),
        P("fsdp"),
        P("fsdp"),
    )
    sizes = dict(mesh.shape)
    body = general_body
    if sizes["dp"] == CORES and sizes["fsdp"] == CHIPS:
        body = block_body
    return jax.shard_map(body, mesh=mesh, in_specs=in_specs, out_specs=out_specs, check_vma=False)
```

```python
from functools import partial
from types import SimpleNamespace

import jax
import jax.numpy as jnp
from jax import lax
from jax.experimental import pallas as pl
from jax.experimental.pallas import tpu as pltpu
from jax.sharding import PartitionSpec as P

HEADS = 12
HEAD = 64
LANGS = 109


EPSILON = 1e-06
SCORE_SCALE = 50.0
MARGIN_WIDTH = 0.3
MASK_FLOOR = -1000000000.0


def contract(left_side, right_side, left_dim, right_dim):
    return lax.dot_general(
        left_side,
        right_side,
        (((left_dim,), (right_dim,)), ((), ())),
        preferred_element_type=jnp.float32,
    )


def norm_rows(inputs, ln_gain, ln_shift):
    row_mean = jnp.mean(inputs, axis=-1, keepdims=True)
    centered = inputs - row_mean
    variance = jnp.mean(centered * centered, axis=-1, keepdims=True)
    inverse = lax.rsqrt(variance + EPSILON)
    normed = centered * inverse
    return (normed * ln_gain + ln_shift, normed, inverse)


def norm_back(grad_output, normed, inverse, ln_gain):
    grad_normed = grad_output * ln_gain
    first_term = jnp.mean(grad_normed, axis=-1, keepdims=True)
    second_term = jnp.mean(grad_normed * normed, axis=-1, keepdims=True)
    grad_input = inverse * (grad_normed - first_term - normed * second_term)
    return (grad_input, jnp.sum(grad_output * normed, axis=0), jnp.sum(grad_output, axis=0))


def general_body(
    table,
    token_ids,
    sent_lengths,
    pair_slot,
    pair_lang,
    w_query,
    b_query,
    w_key,
    w_value,
    b_value,
    w_out,
    b_out,
    ln1_gain,
    ln1_bias,
    w_up,
    b_up,
    w_down,
    b_down,
    ln2_gain,
    ln2_bias,
):
    sentences, length = token_ids.shape
    tokens = sentences * length
    vocab_rows, model_width = table.shape
    owners = lax.axis_size(("dp", "fsdp"))
    dp_count = lax.axis_size("dp")
    fsdp_count = lax.axis_size("fsdp")
    capacity = max(2, 2 * tokens // owners)
    device = lax.axis_index(("dp", "fsdp"))
    score_factor = HEAD ** (-0.5)
    flat_ids = token_ids.reshape(tokens)
    owner_of = flat_ids // vocab_rows
    member = (owner_of[:, None] == jnp.arange(owners, dtype=jnp.int32)[None, :]).astype(jnp.int32)
    owner_rank = jnp.sum(jnp.cumsum(member, axis=0) * member, axis=1) - 1
    slot_of = owner_of * capacity + owner_rank
    requests = jnp.full((owners * capacity,), -1, jnp.int32).at[slot_of].set(flat_ids)
    received = lax.all_to_all(
        lax.all_to_all(
            requests.reshape(dp_count, fsdp_count, capacity),
            "dp",
            split_axis=0,
            concat_axis=0,
            tiled=True,
        ),
        "fsdp",
        split_axis=1,
        concat_axis=1,
        tiled=True,
    )
    present = received >= 0
    local_rows = jnp.where(present, received - device * vocab_rows, 0)
    found_rows = jnp.where(present[..., None], table[local_rows], jnp.zeros((), table.dtype))
    replies = lax.all_to_all(
        lax.all_to_all(found_rows, "dp", split_axis=0, concat_axis=0, tiled=True),
        "fsdp",
        split_axis=1,
        concat_axis=1,
        tiled=True,
    )
    embedded = replies.reshape(owners * capacity, model_width)[slot_of]
    gathered = (
        lax.all_gather(w_query, "fsdp", axis=0, tiled=True),
        lax.all_gather(b_query, "fsdp", axis=0, tiled=True),
        lax.all_gather(w_key, "fsdp", axis=0, tiled=True),
        lax.all_gather(w_value, "fsdp", axis=0, tiled=True),
        lax.all_gather(b_value, "fsdp", axis=0, tiled=True),
        lax.all_gather(w_out, "fsdp", axis=0, tiled=True),
        lax.all_gather(b_out, "fsdp", axis=0, tiled=True),
        lax.all_gather(ln1_gain, "fsdp", axis=0, tiled=True),
        lax.all_gather(ln1_bias, "fsdp", axis=0, tiled=True),
        lax.all_gather(w_up, "fsdp", axis=0, tiled=True),
        lax.all_gather(b_up, "fsdp", axis=0, tiled=True),
        lax.all_gather(w_down, "fsdp", axis=0, tiled=True),
        lax.all_gather(b_down, "fsdp", axis=0, tiled=True),
        lax.all_gather(ln2_gain, "fsdp", axis=0, tiled=True),
        lax.all_gather(ln2_bias, "fsdp", axis=0, tiled=True),
    )
    (
        full_wq,
        full_bq,
        full_wk,
        full_wv,
        full_bv,
        full_wo,
        full_bo,
        full_g1,
        full_s1,
        full_wup,
        full_bup,
        full_wdown,
        full_bdown,
        full_g2,
        full_s2,
    ) = gathered
    valid_mask = jnp.arange(length, dtype=jnp.int32)[None, :] < sent_lengths[:, None]
    head_shape = (sentences, length, HEADS, HEAD)
    queries = (jnp.dot(embedded, full_wq, preferred_element_type=jnp.float32) + full_bq).astype(
        jnp.bfloat16
    )
    key_heads = (
        jnp.dot(embedded, full_wk, preferred_element_type=jnp.float32)
        .astype(jnp.bfloat16)
        .reshape(head_shape)
    )
    value_heads = (
        (jnp.dot(embedded, full_wv, preferred_element_type=jnp.float32) + full_bv)
        .astype(jnp.bfloat16)
        .reshape(head_shape)
    )
    query_heads = queries.reshape(head_shape)
    scores = (
        jnp.einsum("bqhd,bkhd->bhqk", query_heads, key_heads, preferred_element_type=jnp.float32)
        * score_factor
    )
    scores = jnp.where(valid_mask[:, None, None, :], scores, MASK_FLOOR)
    row_peak = jnp.max(scores, axis=-1, keepdims=True)
    shifted = jnp.exp(scores - row_peak)
    totals = jnp.sum(shifted, axis=-1, keepdims=True)
    attn_probs = (shifted / totals).astype(jnp.bfloat16)
    context = jnp.einsum(
        "bhqk,bkhd->bqhd", attn_probs, value_heads, preferred_element_type=jnp.float32
    )
    context = context.reshape(tokens, model_width).astype(jnp.bfloat16)
    attended = jnp.dot(context, full_wo, preferred_element_type=jnp.float32) + full_bo
    hidden, normed_one, inverse_one = norm_rows(
        embedded.astype(jnp.float32) + attended, full_g1, full_s1
    )
    hidden_low = hidden.astype(jnp.bfloat16)
    up_pre = jnp.dot(hidden_low, full_wup, preferred_element_type=jnp.float32) + full_bup
    activated = jax.nn.gelu(up_pre, approximate=False).astype(jnp.bfloat16)
    down_pre = jnp.dot(activated, full_wdown, preferred_element_type=jnp.float32) + full_bdown
    normed_out, normed_two, inverse_two = norm_rows(hidden + down_pre, full_g2, full_s2)
    layer_out = jnp.where(valid_mask.reshape(tokens)[:, None], normed_out, 0.0).astype(jnp.bfloat16)
    layer_out = layer_out.reshape(sentences, length, model_width)

    def first_rows(matrix):
        return matrix.reshape(sentences, length, matrix.shape[-1])[:, 0]

    summary = first_rows(normed_out)
    magnitude = jnp.sqrt(jnp.sum(summary * summary, axis=-1, keepdims=True) + EPSILON)
    unit_vector = summary / magnitude
    unit_low = unit_vector.astype(jnp.bfloat16)
    every_unit = lax.all_gather(unit_low, ("dp", "fsdp"), axis=0, tiled=True)
    every_side = pair_slot % 2
    every_pair = pair_slot // 2
    my_slots = lax.dynamic_slice_in_dim(pair_slot, device * sentences, sentences)
    my_side = my_slots % 2
    my_pair = my_slots // 2
    lang_onehot = (pair_lang[:, None] == jnp.arange(LANGS, dtype=jnp.int32)[None, :]).astype(
        jnp.float32
    )
    per_lang = jnp.sum(lang_onehot, axis=0)
    per_pair = 1.0 / (2.0 * LANGS * jnp.sum(lang_onehot * per_lang[None, :], axis=1))
    my_weight = jnp.take(per_pair, my_pair)
    opposite = my_side[:, None] != every_side[None, :]
    partner = opposite & (my_pair[:, None] == every_pair[None, :])
    raw_scores = SCORE_SCALE * contract(unit_low, every_unit, 1, 1)
    pair_scores = jnp.where(partner, raw_scores - SCORE_SCALE * MARGIN_WIDTH, raw_scores)
    pair_scores = jnp.where(opposite, pair_scores, MASK_FLOOR)
    pair_peak = jnp.max(pair_scores, axis=1, keepdims=True)
    pair_exp = jnp.exp(pair_scores - pair_peak)
    pair_total = jnp.sum(pair_exp, axis=1, keepdims=True)
    log_total = pair_peak[:, 0] + jnp.log(pair_total[:, 0])
    picked = jnp.sum(jnp.where(partner, pair_scores, 0.0), axis=1)
    loss_value = lax.psum(jnp.sum(my_weight * (log_total - picked)), ("dp", "fsdp"))
    coefficients = (
        my_weight[:, None] * (pair_exp / pair_total - partner.astype(jnp.float32))
    ).astype(jnp.bfloat16)
    unit_grad = SCORE_SCALE * contract(coefficients, every_unit, 1, 0)
    column_terms = SCORE_SCALE * contract(coefficients, unit_low, 0, 0)
    unit_grad = unit_grad + lax.psum_scatter(
        column_terms, ("dp", "fsdp"), scatter_dimension=0, tiled=True
    )
    along = jnp.sum(unit_vector * unit_grad, axis=-1, keepdims=True)
    summary_grad = (unit_grad - unit_vector * along) / magnitude
    again_weights = (
        lax.all_gather(w_query, "fsdp", axis=0, tiled=True),
        lax.all_gather(w_key, "fsdp", axis=0, tiled=True),
        lax.all_gather(w_value, "fsdp", axis=0, tiled=True),
        lax.all_gather(w_out, "fsdp", axis=0, tiled=True),
        lax.all_gather(ln1_gain, "fsdp", axis=0, tiled=True),
        lax.all_gather(w_up, "fsdp", axis=0, tiled=True),
        lax.all_gather(w_down, "fsdp", axis=0, tiled=True),
        lax.all_gather(ln2_gain, "fsdp", axis=0, tiled=True),
    )
    again_wq, again_wk, again_wv, again_wo, again_g1, again_wup, again_wdown, again_g2 = (
        again_weights
    )
    residual_grad, grad_g2, grad_s2 = norm_back(
        summary_grad, first_rows(normed_two), first_rows(inverse_two), again_g2
    )
    down_grad = residual_grad.astype(jnp.bfloat16)
    activated_cls = first_rows(activated)
    act_grad = contract(down_grad, again_wdown, 1, 1)
    gelu_value, gelu_pull = jax.vjp(partial(jax.nn.gelu, approximate=False), first_rows(up_pre))
    up_grad = gelu_pull(act_grad)[0].astype(jnp.bfloat16)
    hidden_cls = first_rows(hidden_low)
    hidden_grad = contract(up_grad, again_wup, 1, 1) + residual_grad
    first_grad, grad_g1, grad_s1 = norm_back(
        hidden_grad, first_rows(normed_one), first_rows(inverse_one), again_g1
    )
    attend_grad = first_grad.astype(jnp.bfloat16)
    context_cls = first_rows(context)
    context_grad = (
        contract(attend_grad, again_wo, 1, 1).astype(jnp.bfloat16).reshape(sentences, HEADS, HEAD)
    )
    query_cls = query_heads[:, 0]
    cls_scores = (
        jnp.einsum("bhd,bkhd->bhk", query_cls, key_heads, preferred_element_type=jnp.float32)
        * score_factor
    )
    cls_scores = jnp.where(valid_mask[:, None, :], cls_scores, MASK_FLOOR)
    cls_probs = jnp.exp(cls_scores - row_peak[:, :, 0]) / totals[:, :, 0]
    prob_grad = jnp.einsum(
        "bhd,bkhd->bhk", context_grad, value_heads, preferred_element_type=jnp.float32
    )
    score_grad = (
        cls_probs * (prob_grad - jnp.sum(cls_probs * prob_grad, axis=-1, keepdims=True))
    ).astype(jnp.bfloat16)
    query_grad = (
        (
            jnp.einsum("bhk,bkhd->bhd", score_grad, key_heads, preferred_element_type=jnp.float32)
            * score_factor
        )
        .astype(jnp.bfloat16)
        .reshape(sentences, model_width)
    )
    key_grad = (
        (
            jnp.einsum("bhk,bhd->bkhd", score_grad, query_cls, preferred_element_type=jnp.float32)
            * score_factor
        )
        .astype(jnp.bfloat16)
        .reshape(tokens, model_width)
    )
    value_grad = (
        jnp.einsum(
            "bhk,bhd->bkhd",
            cls_probs.astype(jnp.bfloat16),
            context_grad,
            preferred_element_type=jnp.float32,
        )
        .astype(jnp.bfloat16)
        .reshape(tokens, model_width)
    )
    embedded_cls = first_rows(embedded)
    grad_wkey = contract(embedded, key_grad, 0, 0)
    grad_wvalue = contract(embedded, value_grad, 0, 0)
    grad_bvalue = jnp.sum(value_grad, axis=0, dtype=jnp.float32)
    row_grads = contract(key_grad, again_wk, 1, 1) + contract(value_grad, again_wv, 1, 1)
    summary_extra = contract(query_grad, again_wq, 1, 1) + first_grad
    row_grads = (
        row_grads.reshape(sentences, length, model_width)
        .at[:, 0]
        .add(summary_extra)
        .reshape(tokens, model_width)
    )
    outgoing = jnp.zeros((owners * capacity, model_width), jnp.float32).at[slot_of].set(row_grads)
    incoming = lax.all_to_all(
        lax.all_to_all(
            outgoing.reshape(dp_count, fsdp_count, capacity, model_width).astype(jnp.bfloat16),
            "dp",
            split_axis=0,
            concat_axis=0,
            tiled=True,
        ),
        "fsdp",
        split_axis=1,
        concat_axis=1,
        tiled=True,
    ).astype(jnp.float32)
    incoming = jnp.where(
        present.reshape(owners * capacity)[:, None],
        incoming.reshape(owners * capacity, model_width),
        0.0,
    )
    table_grad = (
        jnp.zeros((vocab_rows, model_width), jnp.float32)
        .at[local_rows.reshape(owners * capacity)]
        .add(incoming)
    )
    grad_wquery = contract(embedded_cls, query_grad, 0, 0)
    grad_bquery = jnp.sum(query_grad, axis=0, dtype=jnp.float32)
    grad_wout = contract(context_cls, attend_grad, 0, 0)
    grad_bout = jnp.sum(attend_grad, axis=0, dtype=jnp.float32)
    grad_wup = contract(hidden_cls, up_grad, 0, 0)
    grad_bup = jnp.sum(up_grad, axis=0, dtype=jnp.float32)
    grad_wdown = contract(activated_cls, down_grad, 0, 0)
    grad_bdown = jnp.sum(down_grad, axis=0, dtype=jnp.float32)
    owned_grads = (
        lax.psum_scatter(
            grad_wquery.astype(jnp.bfloat16), "fsdp", scatter_dimension=0, tiled=True
        ).astype(jnp.float32),
        lax.psum_scatter(
            grad_bquery.astype(jnp.bfloat16), "fsdp", scatter_dimension=0, tiled=True
        ).astype(jnp.float32),
        lax.psum_scatter(
            grad_wkey.astype(jnp.bfloat16), "fsdp", scatter_dimension=0, tiled=True
        ).astype(jnp.float32),
        lax.psum_scatter(
            grad_wvalue.astype(jnp.bfloat16), "fsdp", scatter_dimension=0, tiled=True
        ).astype(jnp.float32),
        lax.psum_scatter(
            grad_bvalue.astype(jnp.bfloat16), "fsdp", scatter_dimension=0, tiled=True
        ).astype(jnp.float32),
        lax.psum_scatter(
            grad_wout.astype(jnp.bfloat16), "fsdp", scatter_dimension=0, tiled=True
        ).astype(jnp.float32),
        lax.psum_scatter(
            grad_bout.astype(jnp.bfloat16), "fsdp", scatter_dimension=0, tiled=True
        ).astype(jnp.float32),
        lax.psum_scatter(
            grad_g1.astype(jnp.bfloat16), "fsdp", scatter_dimension=0, tiled=True
        ).astype(jnp.float32),
        lax.psum_scatter(
            grad_s1.astype(jnp.bfloat16), "fsdp", scatter_dimension=0, tiled=True
        ).astype(jnp.float32),
        lax.psum_scatter(
            grad_wup.astype(jnp.bfloat16), "fsdp", scatter_dimension=0, tiled=True
        ).astype(jnp.float32),
        lax.psum_scatter(
            grad_bup.astype(jnp.bfloat16), "fsdp", scatter_dimension=0, tiled=True
        ).astype(jnp.float32),
        lax.psum_scatter(
            grad_wdown.astype(jnp.bfloat16), "fsdp", scatter_dimension=0, tiled=True
        ).astype(jnp.float32),
        lax.psum_scatter(
            grad_bdown.astype(jnp.bfloat16), "fsdp", scatter_dimension=0, tiled=True
        ).astype(jnp.float32),
        lax.psum_scatter(
            grad_g2.astype(jnp.bfloat16), "fsdp", scatter_dimension=0, tiled=True
        ).astype(jnp.float32),
        lax.psum_scatter(
            grad_s2.astype(jnp.bfloat16), "fsdp", scatter_dimension=0, tiled=True
        ).astype(jnp.float32),
    )
    summed = (
        lax.psum(owned_grads[0].astype(jnp.bfloat16), "dp").astype(jnp.float32),
        lax.psum(owned_grads[1].astype(jnp.bfloat16), "dp").astype(jnp.float32),
        lax.psum(owned_grads[2].astype(jnp.bfloat16), "dp").astype(jnp.float32),
        lax.psum(owned_grads[3].astype(jnp.bfloat16), "dp").astype(jnp.float32),
        lax.psum(owned_grads[4].astype(jnp.bfloat16), "dp").astype(jnp.float32),
        lax.psum(owned_grads[5].astype(jnp.bfloat16), "dp").astype(jnp.float32),
        lax.psum(owned_grads[6].astype(jnp.bfloat16), "dp").astype(jnp.float32),
        lax.psum(owned_grads[7].astype(jnp.bfloat16), "dp").astype(jnp.float32),
        lax.psum(owned_grads[8].astype(jnp.bfloat16), "dp").astype(jnp.float32),
        lax.psum(owned_grads[9].astype(jnp.bfloat16), "dp").astype(jnp.float32),
        lax.psum(owned_grads[10].astype(jnp.bfloat16), "dp").astype(jnp.float32),
        lax.psum(owned_grads[11].astype(jnp.bfloat16), "dp").astype(jnp.float32),
        lax.psum(owned_grads[12].astype(jnp.bfloat16), "dp").astype(jnp.float32),
        lax.psum(owned_grads[13].astype(jnp.bfloat16), "dp").astype(jnp.float32),
        lax.psum(owned_grads[14].astype(jnp.bfloat16), "dp").astype(jnp.float32),
    )
    return (
        layer_out,
        loss_value,
        table_grad,
        summed[0],
        summed[1],
        summed[2],
        summed[3],
        summed[4],
        summed[5],
        summed[6],
        summed[7],
        summed[8],
        summed[9],
        summed[10],
        summed[11],
        summed[12],
        summed[13],
        summed[14],
    )


CORES = 2
PLANES = 4
LINES = 4
CHIPS = PLANES * LINES
DEVICES = CORES * CHIPS
CAPACITY = 48
GROUPS = 3
PAD = 16
TOKENS = 768
WIDTH = 768
WIDE = 3072
VOCAB_ROWS = 1024
PAIR_ROWS = HEADS * PAD
SLOT_ROWS = DEVICES * PAD
LONG = 64
BLOCK = 256
MESH = pl.DeviceIdType.MESH
LOW = jnp.bfloat16
FULL = jnp.float32
VMEM_LIMIT = 62 * 1024 * 1024

INPUTS = ["table", "token_ids", "lens", "slots", "langs"]
INPUTS += ["wq", "bq", "wk", "wv", "bv", "wo", "bo", "g1", "s1", "wup", "bup", "wdown", "bdown"]
INPUTS += ["g2", "s2"]
OUTPUTS = ["layer_out", "table_grad", "g_wq", "g_wk", "g_wv", "g_wo", "g_wup", "g_wdown"]
OUTPUTS += ["g_small", "loss"]


def place():
    core = lax.axis_index("dp")
    chip = lax.axis_index("fsdp")
    along_x = chip + 1 - 2 * (chip % 2)
    along_y = chip + 2 - 4 * ((chip // 2) % 2)
    first = along_x + core * (along_y - along_x)
    second = along_y + core * (along_x - along_y)
    return core, chip, first, second


def greet():
    core, chip, _, _ = place()
    me = core * CHIPS + chip
    barrier = pltpu.get_barrier_semaphore()

    def signal(step):
        other = lax.rem(me + step, DEVICES)
        pl.semaphore_signal(
            barrier,
            inc=1,
            device_id=(lax.div(other, CHIPS), lax.rem(other, CHIPS)),
            device_id_type=MESH,
        )

    every(1, DEVICES, signal)


def enter():
    pl.semaphore_wait(pltpu.get_barrier_semaphore(), DEVICES - 1)


def remote(source, target, send_sem, recv_sem, core, chip):
    return pltpu.make_async_remote_copy(
        src_ref=source,
        dst_ref=target,
        send_sem=send_sem,
        recv_sem=recv_sem,
        device_id=(core, chip),
        device_id_type=MESH,
    )


def every(start, stop, act):
    def step(index, carry):
        act(index)
        return carry

    lax.fori_loop(start, stop, step, 0)


def weight_steps(piece, send, recv):
    core, chip, first, second = place()
    plane, line = chip // LINES, chip % LINES
    line_first, line_second = first % LINES, second % LINES
    line_far = line_first + line_second - line
    is_low, is_high = plane > 0, plane < PLANES - 1

    def copy(send_index, recv_index, at, to_core, to_chip, carried=core):
        part = piece(at, carried)
        return remote(part, part, send.at[send_index], recv.at[recv_index], to_core, to_chip)

    def up(at_plane):
        return copy(at_plane, at_plane, at_plane * LINES + line, core, chip + LINES)

    def down(at_plane, index):
        return copy(index, at_plane, at_plane * LINES + line, core, chip - LINES)

    def side(at_plane, base, at_line, target):
        return copy(base + at_plane, base + at_plane, at_plane * LINES + at_line, core, target)

    def across(at_plane, base, at_line):
        return copy(base + at_plane, base + at_plane, at_plane * LINES + at_line, 1 - core, chip)

    def begin():
        pl.when(is_high)(lambda: up(plane).start())
        pl.when(is_low)(lambda: down(plane, PLANES).start())
        side(plane, 5, line, first).start()
        side(plane, 9, line, second).start()

    def at_distance(distance, act):
        if distance == 0:
            act(plane, None)
            return
        pl.when(plane >= distance)(lambda: act(plane - distance, True))
        pl.when(plane + distance < PLANES)(lambda: act(plane + distance, False))

    def chain(distance):
        def act(at_plane, from_low):
            if from_low:
                up(at_plane).wait_recv()
                pl.when(is_high)(lambda: up(at_plane).start())
            else:
                down(at_plane, at_plane).wait_recv()
                pl.when(is_low)(lambda: down(at_plane, at_plane).start())
            side(at_plane, 5, line, first).start()
            side(at_plane, 9, line, second).start()
            across(at_plane, 17, line).start()

        return partial(at_distance, distance, act)

    def near(distance):
        def act(at_plane, from_low):
            side(at_plane, 5, line_first, first).wait_recv()
            side(at_plane, 13, line_first, second).start()
            across(at_plane, 21, line_first).start()

        return partial(at_distance, distance, act)

    def far(distance):
        def act(at_plane, from_low):
            side(at_plane, 9, line_second, second).wait_recv()
            across(at_plane, 25, line_second).start()
            side(at_plane, 13, line_far, second).wait_recv()
            across(at_plane, 29, line_far).start()

        return partial(at_distance, distance, act)

    def finish():
        for step in range(1, PLANES):
            index = 17 + (plane + step) % PLANES
            copy(index, index, chip, 1 - core, chip, 1 - core).wait_recv()
        every(21, 33, lambda index: copy(index, index, chip, 1 - core, chip, 1 - core).wait_recv())

    def drain():
        def sent(index):
            copy(index, index, chip, 1 - core, chip).wait_send()

        for at_plane in range(PLANES):
            pl.when((plane >= at_plane) & is_high)(partial(sent, at_plane))
            pl.when((plane < at_plane) & is_low)(partial(sent, at_plane))
        pl.when(is_low)(partial(sent, PLANES))
        every(5, 17, sent)
        for step in range(1, PLANES):
            sent(17 + (plane + step) % PLANES)
        every(21, 33, sent)

    moves = [chain(1), near(0), chain(2), near(1), chain(3), far(0)]
    moves += [near(2), far(1), near(3), far(2), far(3)]
    return begin, moves, finish, drain


def gather_steps(buffer, send, recv):
    core, chip, first, second = place()
    plane, line = chip // LINES, chip % LINES
    line_first, line_second = first % LINES, second % LINES
    line_far = line_first + line_second - line
    half = buffer.shape[-1] // 2
    columns = pl.ds(pl.multiple_of(core * half, 128), half)
    others = pl.ds(pl.multiple_of((1 - core) * half, 128), half)

    def copy(index, part, to_core, to_chip):
        return remote(part, part, send.at[index], recv.at[index], to_core, to_chip)

    def own(at):
        return buffer.at[at, plane, line]

    def chip_part(at_plane, at_line, which):
        return buffer.at[:, at_plane, at_line, :, which]

    def line_part(at_line, which):
        return buffer.at[:, :, at_line, :, which]

    def start():
        copy(0, own(core), 1 - core, chip).start()

    def planes():
        copy(0, own(1 - core), 1 - core, chip).wait_recv()
        for step in range(1, PLANES):
            part = chip_part(plane, line, columns)
            copy(step, part, core, (chip + LINES * step) % CHIPS).start()

    def sides():
        for step in range(1, PLANES):
            part = chip_part((plane + PLANES - step) % PLANES, line, columns)
            copy(step, part, core, chip).wait_recv()
        copy(4, line_part(line, columns), core, first).start()
        copy(5, line_part(line, columns), core, second).start()
        for step in range(1, PLANES):
            part = chip_part((plane + PLANES - step) % PLANES, line, columns)
            copy(6 + step, part, 1 - core, chip).start()

    def corner():
        copy(4, line_part(line_first, columns), core, first).wait_recv()
        copy(6, line_part(line_first, columns), core, second).start()
        copy(10, line_part(line_first, columns), 1 - core, chip).start()
        copy(5, line_part(line_second, columns), core, second).wait_recv()
        copy(11, line_part(line_second, columns), 1 - core, chip).start()

    def last():
        copy(6, line_part(line_far, columns), core, second).wait_recv()
        copy(12, line_part(line_far, columns), 1 - core, chip).start()

    def finish():
        for step in range(1, PLANES):
            part = chip_part((plane + PLANES - step) % PLANES, line, others)
            copy(6 + step, part, 1 - core, chip).wait_recv()
        copy(10, line_part(line_second, others), 1 - core, chip).wait_recv()
        copy(11, line_part(line_first, others), 1 - core, chip).wait_recv()
        copy(12, line_part(line_far, others), 1 - core, chip).wait_recv()

    def drain():
        copy(0, own(core), 1 - core, chip).wait_send()
        for index in [1, 2, 3, 7, 8, 9]:
            copy(index, chip_part(plane, line, columns), 1 - core, chip).wait_send()
        for index in [4, 5, 6, 10, 11, 12]:
            copy(index, line_part(line, columns), 1 - core, chip).wait_send()

    return [start, planes, sides, corner, last, finish], drain


def iota(shape, axis):
    return lax.broadcasted_iota(jnp.int32, shape, axis)


def as_column(row):
    parts = []
    for start in range(0, row.shape[1], 128):
        tile = jnp.broadcast_to(row[:, start : start + 128], (128, 128))
        parts.append(jnp.transpose(tile)[:, 0:1])
    return jnp.concatenate(parts, axis=0)


def as_row(column):
    parts = []
    for start in range(0, column.shape[0], 128):
        tile = jnp.broadcast_to(column[start : start + 128, :], (128, 128))
        parts.append(jnp.transpose(tile)[0:1, :])
    return jnp.concatenate(parts, axis=1)


def dot(left_side, right_side):
    return contract(left_side, right_side, 1, 0)


def dot_turned(left_side, right_side):
    return contract(left_side, right_side, 1, 1)


def norm_parts(inputs):
    centered = inputs - jnp.mean(inputs, axis=-1, keepdims=True)
    inverse = lax.rsqrt(jnp.mean(centered * centered, axis=-1, keepdims=True) + EPSILON)
    return centered * inverse, inverse


def norm_back_parts(grad_output, normed, inverse, ln_gain):
    grad_normed = grad_output * ln_gain
    first_term = jnp.mean(grad_normed, axis=-1, keepdims=True)
    second_term = jnp.mean(grad_normed * normed, axis=-1, keepdims=True)
    return (
        inverse * (grad_normed - first_term - normed * second_term),
        jnp.sum(grad_output * normed, axis=0, keepdims=True),
        jnp.sum(grad_output, axis=0, keepdims=True),
    )


def erf_parts(inputs):
    decay = jnp.exp(-0.5 * inputs * inputs)
    share = 1.0 / (1.0 + jnp.abs(inputs) * (0.3275911 * 0.5**0.5))
    terms = [1.061405429, -1.453152027, 1.421413741, -0.284496736, 0.254829592]
    series = 0.5 * terms[0]
    for term in terms[1:]:
        series = series * share + 0.5 * term
    tail = series * share * decay
    return jnp.where(inputs >= 0.0, 1.0 - tail, tail), decay


def gelu_parts(inputs):
    below, decay = erf_parts(inputs)
    return inputs * below, below + inputs * decay * ((2.0 * 3.141592653589793) ** -0.5)


def gelu(inputs):
    return inputs * erf_parts(inputs)[0]


def layer_kernel(names, *refs):
    r = SimpleNamespace(**dict(zip(names, refs, strict=True)))
    core, chip, _, _ = place()
    me = core * CHIPS + chip
    here = (core, chip // LINES, chip % LINES)
    scale = HEAD ** (-0.5)
    depth, deep = WIDTH // CHIPS, WIDE // CHIPS
    sentences = TOKENS // LONG

    for j in range(TOKENS // 128):
        r.ids[j : j + 1, :] = jnp.concatenate(
            [r.token_ids[2 * j : 2 * j + 1, :], r.token_ids[2 * j + 1 : 2 * j + 2, :]], axis=1
        )
    r.ids[TOKENS // 128 : 8, :] = jnp.zeros((8 - TOKENS // 128, 128), jnp.int32)
    greet()
    ahead = (iota((TOKENS, TOKENS), 0) < iota((TOKENS, TOKENS), 1)).astype(LOW)
    r.embedded[...] = ahead
    mine = pl.ds(pl.multiple_of(chip * depth, 16), depth)
    for index, shard in enumerate([r.wq, r.wk, r.wv, r.wo]):
        r.wa[mine, index * WIDTH : (index + 1) * WIDTH] = shard[...]
    r.every_ids[me] = r.ids[...]
    enter()

    def peer(step):
        other = lax.rem(me + step, DEVICES)
        return other, lax.div(other, CHIPS), lax.rem(other, CHIPS)

    def ids_copy(step):
        other, to_core, to_chip = peer(step)
        return remote(r.ids, r.every_ids.at[me], r.one_send.at[0], r.one_recv.at[0], to_core, to_chip)

    def all_but_one(ref, index):
        part = ref.at[0 : DEVICES - 1]
        return remote(part, part, r.one_send.at[index], r.one_recv.at[index], 1 - core, chip)

    every(1, DEVICES, lambda step: ids_copy(step).start())

    def block(ref, rows, columns):
        def piece(at, carried):
            return ref.at[
                pl.ds(pl.multiple_of(at * rows, 16), rows),
                pl.ds(pl.multiple_of(carried * columns, 128), columns),
            ]

        return piece

    begin_a, moves_a, finish_a, drain_a = weight_steps(
        block(r.wa, depth, 2 * WIDTH), r.weight_send.at[0], r.weight_recv.at[0]
    )
    begin_b, moves_b, finish_b, drain_b = weight_steps(
        block(r.wb, depth, WIDE // 2), r.weight_send.at[1], r.weight_recv.at[1]
    )
    begin_c, moves_c, finish_c, drain_c = weight_steps(
        block(r.wc, deep, WIDTH // 2), r.weight_send.at[2], r.weight_recv.at[2]
    )
    begin_a()

    all_but_one(r.every_ids, 0).wait_recv()
    all_ids = jnp.concatenate([r.every_ids[:, j, :] for j in range(TOKENS // 128)], axis=1)
    all_owner = all_ids // VOCAB_ROWS
    asked = all_owner == me
    ranks = dot(asked.astype(LOW), r.embedded[...])
    r.rank[...] = jnp.where(asked, ranks, -1.0)
    local_row = (all_ids - all_owner * VOCAB_ROWS + 1).astype(FULL)
    r.code[...] = local_row + (iota((DEVICES, TOKENS), 1) // LONG * 2048).astype(FULL)

    quarter_size = DEVICES // 4

    def rows_copy(other, quarter):
        return remote(
            r.rows.at[:, pl.ds(pl.multiple_of(other * PAD, 16), PAD), :],
            r.replies.at[:, pl.ds(pl.multiple_of(me * PAD, 16), PAD), :],
            r.rows_send.at[quarter],
            r.rows_recv.at[quarter],
            lax.div(other, CHIPS),
            lax.rem(other, CHIPS),
        )

    def rows_of(quarter):
        count = quarter_size - 1 if quarter == 3 else quarter_size
        part = r.replies.at[:, 0 : count * PAD, :]
        return remote(
            part, part, r.rows_send.at[quarter], r.rows_recv.at[quarter], 1 - core, chip
        )

    def pick(source):
        rank = r.rank[pl.ds(source, 1), :]
        code = r.code[pl.ds(source, 1), :]
        here_at = iota((CAPACITY, TOKENS), 0).astype(FULL) == rank
        found = jnp.sum(jnp.where(here_at, code, 0.0), axis=1, keepdims=True)
        sent = jnp.floor(found * (1.0 / 2048))
        row = found - sent * 2048.0 - 1.0
        chosen = (iota((CAPACITY, VOCAB_ROWS), 1).astype(FULL) == row).astype(LOW)
        at = pl.ds(pl.multiple_of(source * PAD, 16), PAD)
        source_sent = sent + (source * PAD).astype(FULL)
        for group in range(GROUPS):
            part = slice(group * PAD, (group + 1) * PAD)
            r.chosen[group, at, :] = chosen[part]
            r.found[group, at, 0:1] = row[part]
            r.found[group, at, 1:2] = source_sent[part]

    for quarter in range(4):
        now = lax.rem(lax.div(me, quarter_size) + 1 + quarter, 4)

        def pick_two(index):
            pick(now * quarter_size + 2 * index)
            pick(now * quarter_size + 2 * index + 1)

        every(0, quarter_size // 2, pick_two)
        span = pl.ds(pl.multiple_of(now * quarter_size * PAD, 128), quarter_size * PAD)
        picked = r.chosen[:, span, :].reshape(GROUPS * quarter_size * PAD, VOCAB_ROWS)
        found_rows = dot(picked, r.table[...]).astype(LOW)
        r.rows[:, span, :] = found_rows.reshape(GROUPS, quarter_size * PAD, WIDTH)

        def send(index):
            other = now * quarter_size + lax.rem(lax.rem(me, quarter_size) + index, quarter_size)
            rows_copy(other, quarter).start()

        every(1 if quarter == 3 else 0, quarter_size, send)
        moves_a[2 * quarter]()
        moves_a[2 * quarter + 1]()
    own_at = pl.ds(pl.multiple_of(me * PAD, 16), PAD)
    r.replies[:, own_at, :] = r.rows[:, own_at, :]

    small_here = pl.ds(pl.multiple_of(chip * 128, 128), 128)
    lines = [r.bq, r.bv, r.bo, r.g1, r.s1, r.bdown, r.g2, r.s2]
    lines = [line[...].reshape(1, depth).astype(FULL) for line in lines]
    up_line = r.bup[...].reshape(1, deep).astype(FULL)
    lines += [up_line[:, part * depth : (part + 1) * depth] for part in range(deep // depth)]
    lines.append(jnp.zeros((PAD - len(lines), depth), FULL))
    own_small = jnp.concatenate(lines, axis=0)
    own_small = jnp.concatenate([own_small, jnp.zeros((PAD, 128 - depth), FULL)], axis=1)
    r.smalls[:, small_here] = own_small.astype(LOW)

    def small_copy(step):
        part = r.smalls.at[:, small_here]
        to_chip = lax.rem(chip + step, CHIPS)
        return remote(part, part, r.small_send.at[0], r.small_recv.at[0], core, to_chip)

    def all_smalls():
        part = r.smalls.at[:, 0 : (CHIPS - 1) * 128]
        return remote(part, part, r.small_send.at[0], r.small_recv.at[0], 1 - core, chip)

    every(1, CHIPS, lambda step: small_copy(step).start())
    r.wb[mine, :] = r.wup[...]
    r.wc[pl.ds(pl.multiple_of(chip * deep, 16), deep), :] = r.wdown[...]

    own_row = jnp.concatenate([r.ids[j : j + 1, :] for j in range(TOKENS // 128)], axis=1)
    owner_row = (own_row // VOCAB_ROWS).astype(FULL)
    owner_col = as_column(owner_row)
    earlier = (owner_row == owner_col) & (iota((TOKENS, TOKENS), 1) < iota((TOKENS, TOKENS), 0))
    own_rank = jnp.sum(earlier.astype(FULL), axis=1, keepdims=True)
    own_group = jnp.floor(own_rank * (1.0 / PAD))
    own_slot = own_group * SLOT_ROWS + owner_col * PAD + (own_rank - own_group * PAD)
    r.slot_col[...] = own_slot
    r.slot_line[0:1, :] = as_row(own_slot)

    at_sent = iota((1, TOKENS), 1) // LONG
    lens = jnp.concatenate(
        [r.lens[...].reshape(1, sentences).astype(FULL), jnp.zeros((1, PAD - sentences), FULL)],
        axis=1,
    )
    spread_lens = dot(
        jnp.broadcast_to(lens, (8, PAD)).astype(LOW),
        (iota((PAD, TOKENS), 0) == iota((PAD, TOKENS), 1) // LONG).astype(LOW),
    )[0:1]
    valid_row = ((iota((1, TOKENS), 1) - at_sent * LONG).astype(FULL) < spread_lens).astype(FULL)
    r.valid_line[0:1, :] = valid_row
    r.valid_col[...] = as_column(valid_row)
    half_block = BLOCK // 2
    stacked_shape = (4 * half_block, half_block)
    same = iota(stacked_shape, 0) // LONG % 2 == iota(stacked_shape, 1) // LONG
    r.block_bias[...] = jnp.where(same, 0.0, MASK_FLOOR)
    r.valid_bias[0:1, :] = (1.0 - valid_row) * MASK_FLOOR

    slots = r.slots[...].reshape(1, DEVICES * sentences)
    gap = jnp.full((1, PAD - sentences), -2, jnp.int32)
    slot_line = jnp.concatenate(
        [
            part
            for device in range(DEVICES)
            for part in (slots[:, device * sentences : (device + 1) * sentences], gap)
        ],
        axis=1,
    )
    side_line = slot_line - slot_line // 2 * 2 + jnp.where(slot_line < 0, 8, 0)
    pair_line = slot_line // 2
    pairs = r.langs.shape[0]
    lang_line = r.langs[...].reshape(1, pairs).astype(FULL)
    lang_line = jnp.concatenate([lang_line, jnp.full((1, -pairs % 128), -1.0, FULL)], axis=1)
    lang_col = as_column(lang_line)
    same_lang = jnp.sum(jnp.where(lang_col == lang_line, 1.0, 0.0), axis=1, keepdims=True)
    per_pair = 1.0 / (2.0 * LANGS * same_lang)
    at_pair = iota((lang_line.shape[1], SLOT_ROWS), 0) == pair_line
    weight_line = jnp.sum(jnp.where(at_pair, per_pair, 0.0), axis=0, keepdims=True)
    r.pairs[0:1, :] = weight_line
    r.pairs[1:2, :] = pair_line.astype(FULL)
    r.pairs[2:3, :] = side_line.astype(FULL)
    r.pairs_col[:, 0:1] = as_column(weight_line)
    r.pairs_col[:, 1:2] = as_column(pair_line.astype(FULL))
    r.pairs_col[:, 2:3] = as_column(side_line.astype(FULL))
    for move in moves_a[8:]:
        move()

    all_smalls().wait_recv()
    smalls = r.smalls[...].astype(FULL)
    r.vectors[:, 0:WIDTH] = jnp.concatenate(
        [smalls[:, at * 128 : at * 128 + depth] for at in range(CHIPS)], axis=1
    )
    r.up_bias[0:1, :] = jnp.concatenate(
        [
            smalls[8 + part : 9 + part, at * 128 : at * 128 + depth]
            for at in range(CHIPS)
            for part in range(deep // depth)
        ],
        axis=1,
    )

    def vector(index):
        return r.vectors[index : index + 1, :]

    r.qkv_bias[0:1, 0:WIDTH] = vector(0)
    r.qkv_bias[0:1, WIDTH : 2 * WIDTH] = jnp.zeros((1, WIDTH), FULL)
    r.qkv_bias[0:1, 2 * WIDTH : 3 * WIDTH] = vector(1)

    def first_row(source):
        code = jnp.where(r.rank[pl.ds(source, 1), :] >= 0.0, r.code[pl.ds(source, 1), :], 0.0)
        at_first = iota((PAD, TOKENS), 1) == iota((PAD, TOKENS), 0) * LONG
        found = jnp.sum(jnp.where(at_first, code, 0.0), axis=1, keepdims=True)
        row = found - jnp.floor(found * (1.0 / 2048)) * 2048.0 - 1.0
        r.found[GROUPS, pl.ds(pl.multiple_of(source * PAD, 16), PAD), 0:1] = row

    every(0, DEVICES, first_row)
    for group in range(GROUPS + 1):
        named = as_row(r.found[group, :, 0:1])
        by_row = iota((VOCAB_ROWS, SLOT_ROWS), 0).astype(FULL) == named
        r.by_row[:, group * SLOT_ROWS : (group + 1) * SLOT_ROWS] = by_row.astype(LOW)

    def order(tile):
        at = pl.ds(pl.multiple_of(tile * BLOCK, BLOCK), BLOCK)
        lanes = iota((BLOCK, GROUPS * SLOT_ROWS), 1).astype(FULL)
        r.qkv[at, 0 : GROUPS * SLOT_ROWS] = (r.slot_col[at, :] == lanes).astype(LOW)

    every(0, TOKENS // BLOCK, order)
    rows_of(0).wait_recv()
    rows_of(1).wait_recv()
    begin_b()
    moves_b[0]()
    moves_b[1]()
    rows_of(2).wait_recv()
    moves_b[2]()
    moves_b[3]()
    rows_of(3).wait_recv()
    begin_c()

    def embed(tile):
        at = pl.ds(pl.multiple_of(tile * BLOCK, BLOCK), BLOCK)
        replies = r.replies[:, :, at].reshape(GROUPS * SLOT_ROWS, BLOCK)
        r.embedded[:, at] = dot(r.qkv[:, 0 : GROUPS * SLOT_ROWS], replies).astype(LOW)

    every(0, WIDTH // BLOCK, embed)
    finish_a()
    moves_b[4]()
    moves_b[5]()

    def project(tile):
        at = pl.ds(pl.multiple_of(tile * BLOCK, BLOCK), BLOCK)
        r.qkv[:, at] = (dot(r.embedded[...], r.wa[:, at]) + r.qkv_bias[0:1, at]).astype(LOW)

    every(3, 6, project)
    moves_b[6]()
    moves_b[7]()
    every(6, 9, project)
    moves_b[8]()
    moves_b[9]()
    moves_b[10]()

    row_sent = iota((PAIR_ROWS, WIDTH), 0) % PAD
    row_head = iota((PAIR_ROWS, WIDTH), 0) // PAD
    lane_block = iota((PAIR_ROWS, WIDTH), 1) // HEAD
    in_head = row_head == lane_block
    seen = (row_sent == lane_block) & (r.valid_line[0:1, :] > 0.0)
    firsts = (iota((PAD, TOKENS), 1) == iota((PAD, TOKENS), 0) * LONG).astype(LOW)
    real_row = iota((PAD, 1), 0) < sentences

    def spread(rows):
        return jnp.where(in_head, jnp.concatenate([rows] * HEADS, axis=0), jnp.zeros((), LOW))

    def fold(tall):
        tall = jnp.where(in_head, tall, 0.0)
        return sum(tall[head * PAD : (head + 1) * PAD] for head in range(HEADS))

    keys, values = slice(WIDTH, 2 * WIDTH), slice(2 * WIDTH, 3 * WIDTH)
    embedded_cls = dot(firsts, r.embedded[...]).astype(LOW)
    query_cls = (dot(embedded_cls, r.wa[:, 0:WIDTH]) + vector(0)).astype(LOW)
    cls_scores = dot_turned(spread(query_cls), r.qkv[:, keys]) * scale
    cls_scores = jnp.where(seen, cls_scores, MASK_FLOOR)
    cls_peak = jnp.max(cls_scores, axis=1, keepdims=True)
    cls_exp = jnp.where(seen, jnp.exp(cls_scores - cls_peak), 0.0)
    cls_total = jnp.sum(cls_exp, axis=1, keepdims=True)
    cls_probs = cls_exp / jnp.where(cls_total > 0.0, cls_total, 1.0)
    probs_low = cls_probs.astype(LOW)
    r.probs[...] = cls_probs
    context_cls = fold(dot(probs_low, r.qkv[:, values])).astype(LOW)
    moves_c[0]()
    moves_c[1]()
    first_cls = (
        embedded_cls.astype(FULL)
        + dot(context_cls, r.wa[:, 3 * WIDTH : 4 * WIDTH])
        + vector(2)
    )
    normed_one, inverse_one = norm_parts(first_cls)
    r.normed_one[...] = normed_one
    hidden_cls = normed_one * vector(3) + vector(4)
    hidden_cls_low = hidden_cls.astype(LOW)
    early_here = r.early.at[here]
    early_here[:, 0:WIDTH] = hidden_cls_low
    early_here[:, WIDTH : 2 * WIDTH] = query_cls
    steps_u, drain_u = gather_steps(r.units, r.gather_send.at[0], r.gather_recv.at[0])
    steps_e, drain_e = gather_steps(r.early, r.gather_send.at[1], r.gather_recv.at[1])
    steps_d, drain_d = gather_steps(r.downs, r.gather_send.at[2], r.gather_recv.at[2])
    steps_a, drain_a2 = gather_steps(r.attends, r.gather_send.at[3], r.gather_recv.at[3])
    steps_q, drain_q = gather_steps(r.queries, r.gather_send.at[4], r.gather_recv.at[4])
    steps_e[0]()
    moves_c[2]()

    def attend(unit):
        rows = pl.ds(pl.multiple_of(unit * half_block, half_block), half_block)
        lane_head = iota((half_block, BLOCK), 1) // HEAD
        bias = r.block_bias[...] + r.valid_bias[0:1, rows]

        def part(which, lane):
            return r.qkv[rows, which * WIDTH + lane : which * WIDTH + lane + BLOCK]

        for lane in range(0, WIDTH, BLOCK):
            query = part(0, lane) * jnp.asarray(scale, LOW)
            key, value = part(1, lane), part(2, lane)
            stacked = jnp.concatenate(
                [jnp.where(lane_head == head, query, jnp.zeros((), LOW)) for head in range(4)],
                axis=0,
            )
            scores = dot_turned(stacked, key) + bias
            shifted = jnp.exp(scores - jnp.max(scores, axis=1, keepdims=True))
            probs = shifted * (1.0 / jnp.sum(shifted, axis=1, keepdims=True))
            mixed = dot(probs.astype(LOW), value)
            result = mixed[0:half_block]
            for head in range(1, 4):
                result = jnp.where(
                    lane_head == head, mixed[head * half_block : (head + 1) * half_block], result
                )
            r.context[rows, lane : lane + BLOCK] = result.astype(LOW)

    def open_tile(tile):
        at = pl.ds(tile * BLOCK, BLOCK)
        attended = dot(r.context[at, :], r.wa[:, 3 * WIDTH : 4 * WIDTH]) + vector(2)
        normed, _ = norm_parts(r.embedded[at, :].astype(FULL) + attended)
        hidden = normed * vector(3) + vector(4)
        r.tile_low[...] = hidden.astype(LOW)
        r.tile_sum[...] = hidden + vector(5)

    def feed_tile(part):
        halves = []
        for half in range(2):
            at = pl.ds(pl.multiple_of((2 * part + half) * BLOCK, BLOCK), BLOCK)
            up_pre = dot(r.tile_low[...], r.wb[:, at]) + r.up_bias[0:1, at]
            halves.append(gelu(up_pre).astype(LOW))
        at = pl.ds(pl.multiple_of(part * 2 * BLOCK, 2 * BLOCK), 2 * BLOCK)
        r.tile_sum[...] += dot(jnp.concatenate(halves, axis=1), r.wc[at, :])

    def layer_copy(tile):
        at = pl.ds(tile * BLOCK, BLOCK)
        return pltpu.make_async_copy(r.context.at[at], r.layer_out.at[at], r.out_sem.at[tile])

    def close_tile(tile):
        at = pl.ds(tile * BLOCK, BLOCK)
        normed, _ = norm_parts(r.tile_sum[...])
        out = normed * vector(6) + vector(7)
        r.context[at, :] = (out * r.valid_col[at, :]).astype(LOW)
        layer_copy(tile).start()

    queue = [partial(every, 0, 3, project)]
    queue += [partial(every, unit, unit + 1, attend) for unit in range(6)]
    late = []
    for tile in range(TOKENS // BLOCK):
        late.append(partial(open_tile, tile))
        late += [partial(every, part, part + 1, feed_tile) for part in range(6)]
        late.append(partial(close_tile, tile))

    def fill(pieces, count):
        for _ in range(min(count, len(pieces))):
            pieces.pop(0)()

    fill(queue, 1)
    moves_c[3]()
    finish_b()
    up_cls = dot(hidden_cls_low, r.wb[...]) + r.up_bias[0:1, :]
    activated_cls, slope_cls = gelu_parts(up_cls)
    activated_low = activated_cls.astype(LOW)
    steps_e[1]()
    for move in moves_c[4:]:
        fill(queue, 1)
        move()

    def pack_tall(tall, target, first_row):
        for at in range(CHIPS):
            columns = tall[:, at * depth : (at + 1) * depth]
            for half in range(CORES):
                base = half * PAIR_ROWS // 2
                target[half * CHIPS + at, first_row : first_row + 48, :] = jnp.concatenate(
                    [
                        columns[base : base + 48],
                        columns[base + 48 : base + 96],
                        jnp.zeros((48, 128 - 2 * depth), FULL),
                    ],
                    axis=1,
                ).astype(LOW)

    def pack_coefs(coefs):
        total = None
        for group in range(GROUPS):
            folds = iota((PAIR_ROWS, 128), 0) // PAD + group * PAD == iota((PAIR_ROWS, 128), 1)
            lanes = contract(coefs, folds.astype(LOW), 0, 0).astype(LOW)
            part = dot(r.rows[group], lanes)
            total = part if total is None else total + part
        return total.astype(LOW).reshape(DEVICES, PAD, 128)

    finish_c()
    down_pre = dot(activated_low, r.wc[...]) + vector(5)
    normed_two, inverse_two = norm_parts(hidden_cls + down_pre)
    summary = normed_two * vector(6) + vector(7)
    magnitude = jnp.sqrt(jnp.sum(summary * summary, axis=-1, keepdims=True) + EPSILON)
    unit = jnp.where(real_row, summary / magnitude, 0.0)
    r.units[here] = unit.astype(LOW)

    steps_u[0]()
    for quarter in range(4):
        rows_of(quarter).wait_send()
    for group in range(GROUPS):
        slot_at = iota((SLOT_ROWS, TOKENS), 0) + group * SLOT_ROWS
        r.rows[group] = (slot_at.astype(FULL) == r.slot_line[0:1, :]).astype(LOW)
    for at in range(CHIPS):
        cut = slice(at * depth, (at + 1) * depth)
        line = jnp.concatenate(
            [
                context_cls.astype(FULL)[:, cut],
                embedded_cls.astype(FULL)[:, cut],
                jnp.zeros((PAD, 128 - 2 * depth), FULL),
            ],
            axis=1,
        ).astype(LOW)
        for half in range(CORES):
            r.mail_one[half * CHIPS + at, 0:PAD, :] = line
    steps_u[1]()
    pack_tall(dot(probs_low, r.embedded[...]), r.mail_one, PAD)
    fill(late, 1)
    steps_u[2]()
    steps_e[2]()
    r.mail_one[:, 64:80, :] = pack_coefs(probs_low)
    fill(late, 1)
    steps_u[3]()
    fill(late, 2)

    def post(box, got, index):
        def send(step):
            other, to_core, to_chip = peer(step)
            remote(
                box.at[other], got.at[me], r.one_send.at[index], r.one_recv.at[index], to_core, to_chip
            ).start()

        every(1, DEVICES, send)
        got[me] = box[me]

    steps_u[4]()
    fill(late, 1)
    steps_u[5]()
    post(r.mail_one, r.got_one, 1)
    steps_e[3]()

    units = r.units[...].reshape(SLOT_ROWS, WIDTH)
    weight_row, pair_row, side_row = r.pairs[0:1, :], r.pairs[1:2, :], r.pairs[2:3, :]

    def pair_scores(rows, pair_col, side_col):
        opposite = side_col + side_row == 1.0
        partner = opposite & (pair_col == pair_row)
        raw = SCORE_SCALE * dot_turned(rows, units)
        shifted = jnp.where(partner, raw - SCORE_SCALE * MARGIN_WIDTH, raw)
        return jnp.where(opposite, shifted, MASK_FLOOR), partner

    every_score, every_partner = pair_scores(
        units, r.pairs_col[:, 1:2], r.pairs_col[:, 2:3]
    )
    peak_row = jnp.max(every_score, axis=0, keepdims=True)
    log_row = peak_row + jnp.log(
        jnp.sum(jnp.exp(every_score - peak_row), axis=0, keepdims=True)
    )
    picked_row = jnp.sum(jnp.where(every_partner, every_score, 0.0), axis=0, keepdims=True)
    r.loss[...] = jnp.sum(weight_row * (log_row - picked_row), axis=1, keepdims=True)

    rows_here = pl.ds(pl.multiple_of(me * PAD, 16), PAD)
    own_score, own_partner = pair_scores(
        r.units[here], r.pairs_col[rows_here, 1:2], r.pairs_col[rows_here, 2:3]
    )
    own_partner = own_partner.astype(FULL)
    own_peak = jnp.max(own_score, axis=1, keepdims=True)
    own_exp = jnp.exp(own_score - own_peak)
    own_share = own_exp / jnp.sum(own_exp, axis=1, keepdims=True)
    by_row = (r.pairs_col[rows_here, 0:1] * (own_share - own_partner)).astype(LOW)
    by_column = (weight_row * (jnp.exp(own_score - log_row) - own_partner)).astype(LOW)
    unit_grad = SCORE_SCALE * (dot(by_row, units) + dot(by_column, units))
    along = jnp.sum(unit * unit_grad, axis=-1, keepdims=True)
    summary_grad = (unit_grad - unit * along) / magnitude

    residual_grad, grad_g2, grad_s2 = norm_back_parts(
        summary_grad, normed_two, inverse_two, vector(6)
    )
    down_grad = residual_grad.astype(LOW)
    r.downs[here] = down_grad
    steps_d[0]()
    act_grad = dot_turned(down_grad, r.wc[...])
    up_grad = (act_grad * slope_cls).astype(LOW)
    steps_d[1]()
    hidden_grad = dot_turned(up_grad, r.wb[...]) + residual_grad
    first_grad, grad_g1, grad_s1 = norm_back_parts(
        hidden_grad, r.normed_one[...], inverse_one, vector(3)
    )
    attend_grad = first_grad.astype(LOW)
    steps_e[4]()
    context_grad = dot_turned(attend_grad, r.wa[:, 3 * WIDTH : 4 * WIDTH]).astype(LOW)
    attend_here = r.attends.at[here]
    attend_here[:, 0:WIDTH] = attend_grad
    attend_here[:, WIDTH : 2 * WIDTH] = context_grad
    steps_a[0]()
    steps_d[2]()
    context_tall = spread(context_grad)
    probs = r.probs[...]
    prob_grad = dot_turned(context_tall, r.qkv[:, values])
    inner = jnp.sum(probs * prob_grad, axis=1, keepdims=True)
    score_grad = (probs * (prob_grad - inner)).astype(LOW)
    steps_a[1]()
    r.mail_three[...] = pack_coefs(score_grad)
    post(r.mail_three, r.got_three, 3)
    query_grad = (fold(dot(score_grad, r.qkv[:, keys])) * scale).astype(LOW)
    probs_total = jnp.sum(probs_low.astype(FULL), axis=1, keepdims=True)
    grad_bvalue = jnp.sum(probs_total * context_tall.astype(FULL), axis=0, keepdims=True)
    grad_bquery = jnp.sum(query_grad.astype(FULL), axis=0, keepdims=True)
    query_here = r.queries.at[here]
    query_here[:, 0:WIDTH] = query_grad
    query_here[:, WIDTH : 2 * WIDTH] = jnp.concatenate(
        [grad_bquery, grad_bvalue, grad_g1, grad_s1, grad_g2, grad_s2, jnp.zeros((10, WIDTH))],
        axis=0,
    ).astype(LOW)
    steps_q[0]()
    steps_a[2]()
    pack_tall(dot(score_grad, r.embedded[...]) * scale, r.mail_two, 0)
    steps_q[1]()
    post(r.mail_two, r.got_two, 2)

    def all_rows(buffer, start):
        return buffer[:, :, :, :, start : start + WIDTH].reshape(SLOT_ROWS, WIDTH)

    def from_sent(group):
        lanes = iota((SLOT_ROWS, SLOT_ROWS), 1).astype(FULL)
        return (r.found[group, :, 1:2] == lanes).astype(LOW)

    def widened(coefs, group):
        lanes = iota((128, WIDTH), 0) == iota((128, WIDTH), 1) // HEAD + group * PAD
        return dot(coefs, lanes.astype(LOW))

    half_wide = WIDE // 2

    def slope_tile(part):
        at = pl.ds(pl.multiple_of(core * half_wide + part * BLOCK, BLOCK), BLOCK)
        up_pre = dot(all_rows(r.early, 0), r.wb[:, at]) + r.up_bias[0:1, at]
        _, slope = gelu_parts(up_pre)
        r.slopes[:, pl.ds(pl.multiple_of(part * BLOCK, BLOCK), BLOCK)] = slope.astype(LOW)

    def slot_queries(group):
        r.slot_query[group] = dot(from_sent(group), all_rows(r.early, WIDTH)).astype(LOW)

    def activate():
        at = pl.ds(pl.multiple_of(chip // 2 * 2 * deep, 128), 2 * deep)
        up_pre = dot(all_rows(r.early, 0), r.wb[:, at]) + r.up_bias[0:1, at]
        r.active_turned[...] = jnp.transpose(gelu(up_pre)).astype(LOW)
        r.hidden_turned[...] = jnp.transpose(all_rows(r.early, 0))

    steps_e[5]()
    between = [partial(slot_queries, group) for group in range(GROUPS)]
    between += [partial(every, part, part + 1, slope_tile) for part in range(6)]
    between.append(activate)

    between += late
    late.clear()
    rest = [steps_d[3], steps_a[3], steps_q[2], steps_d[4], steps_a[4], steps_q[3]]
    rest += [steps_d[5], steps_a[5], steps_q[4]]
    for step in rest:
        step()
        fill(between, 2)
    fill(between, len(between))

    all_but_one(r.got_one, 1).wait_recv()
    got_probs = r.got_one[:, 64:80, :].reshape(SLOT_ROWS, 128)
    for group in range(GROUPS):
        slot_context = dot(from_sent(group), all_rows(r.attends, WIDTH))
        r.replies[group] = (widened(got_probs, group) * slot_context).astype(LOW)

    def head_products(got, first_row, right, start, target):
        for pair in range(HEADS // 4):
            lane = pl.ds(pl.multiple_of(start + (core * (HEADS // 4) + pair) * 128, 128), 128)
            pair_rows = right[:, :, :, :, lane].reshape(SLOT_ROWS, 128)
            parts = []
            for half in range(2):
                head = 2 * pair + half
                row = first_row + head % 3 * PAD
                block_rows = got[:, row : row + PAD, :].reshape(SLOT_ROWS, 128)
                product = contract(block_rows, pair_rows, 0, 0)
                column = head // 3 * depth
                parts.append(product[column : column + depth, :])
            low_lanes = iota((depth, 128), 1) < HEAD
            result = jnp.where(low_lanes, parts[0], parts[1])
            target[:, pl.ds(pl.multiple_of((core * (HEADS // 4) + pair) * 128, 128), 128)] = result

    def half_of(ref, at_core):
        half = ref.shape[1] // 2
        return ref.at[:, pl.ds(pl.multiple_of(at_core * half, 128), half)]

    def half_copy(index, ref, at_core):
        part = half_of(ref, at_core)
        return remote(part, part, r.half_send.at[index], r.half_recv.at[index], 1 - core, chip)

    head_products(r.got_one, PAD, r.attends, WIDTH, r.g_wv)
    half_copy(0, r.g_wv, core).start()

    downs = r.downs[...].reshape(SLOT_ROWS, WIDTH)
    attends = all_rows(r.attends, 0)

    def up_tile(part):
        at = pl.ds(pl.multiple_of(core * half_wide + part * BLOCK, BLOCK), BLOCK)
        slope = r.slopes[:, pl.ds(pl.multiple_of(part * BLOCK, BLOCK), BLOCK)].astype(FULL)
        up_all = (dot_turned(r.downs[...].reshape(SLOT_ROWS, WIDTH), r.wc[at, :]) * slope)
        up_all = up_all.astype(LOW)
        r.g_wup[0:depth, at] = dot(r.hidden_turned[mine, :], up_all)
        total = jnp.sum(up_all.astype(FULL), axis=0, keepdims=True)
        r.g_wup[depth : depth + 8, at] = jnp.broadcast_to(total, (8, BLOCK))

    every(0, half_wide // BLOCK, up_tile)
    half_copy(1, r.g_wup, core).start()
    r.g_wdown[...] = dot(r.active_turned[pl.ds(pl.multiple_of(chip % 2 * deep, 16), deep), :], downs)
    r.left_turned[...] = jnp.transpose(r.got_one[:, 0:PAD, :].reshape(SLOT_ROWS, 128))
    r.g_wo[...] = dot(r.left_turned[0:depth, :], attends)
    own_lanes = (iota((WIDTH, 128), 0) == chip * depth + iota((WIDTH, 128), 1)).astype(LOW)

    def own_part(rows, select):
        total = None
        for _ in range(3):
            part = rows.astype(LOW)
            rows = rows - part.astype(FULL)
            picked = dot(part, select)
            total = picked if total is None else total + picked
        return total

    all_but_one(r.got_three, 3).wait_recv()
    got_scores = r.got_three[...].reshape(SLOT_ROWS, 128)
    for group in range(GROUPS):
        slot_query = r.slot_query[group].astype(FULL)
        key_grad = (widened(got_scores, group) * slot_query * scale).astype(LOW)
        row_grad = dot_turned(key_grad, r.wa[:, keys])
        row_grad = row_grad + dot_turned(r.replies[group], r.wa[:, values])
        r.rows[group] = row_grad.astype(LOW)
    steps_q[5]()
    query_grads = all_rows(r.queries, 0)
    extra = dot_turned(query_grads, r.wa[:, 0:WIDTH]) + attends.astype(FULL)
    r.extra[...] = extra.astype(LOW)
    r.g_wq[...] = dot(r.left_turned[depth : 2 * depth, :], query_grads)

    half_rows = VOCAB_ROWS // 2

    def table_copy(tile):
        at = pl.ds(pl.multiple_of(tile * half_rows, BLOCK), half_rows)
        return pltpu.make_async_copy(
            r.table_full.at[at], r.table_grad.at[at], r.table_sem.at[tile]
        )

    def table_tile(tile):
        at = pl.ds(pl.multiple_of(tile * half_rows, BLOCK), half_rows)
        for start in range(0, WIDTH, BLOCK):
            lanes = slice(start, start + BLOCK)
            slot_rows = r.rows[:, :, lanes].reshape(GROUPS * SLOT_ROWS, BLOCK)
            r.table_full[at, lanes] = dot(r.by_row[at, 0 : GROUPS * SLOT_ROWS], slot_rows) + dot(
                r.by_row[at, GROUPS * SLOT_ROWS :], r.extra[:, lanes]
            )
        table_copy(tile).start()

    every(0, 2, table_tile)
    all_but_one(r.got_two, 2).wait_recv()
    head_products(r.got_two, 0, r.early, WIDTH, r.g_wk)
    half_copy(2, r.g_wk, core).start()

    down_total = jnp.sum(downs.astype(FULL), axis=0, keepdims=True)
    attend_total = jnp.sum(attends.astype(FULL), axis=0, keepdims=True)
    device_sums = (iota((PAD, SLOT_ROWS), 1) % PAD == iota((PAD, SLOT_ROWS), 0)).astype(LOW)
    sums = dot(device_sums, all_rows(r.queries, WIDTH))
    stacked = jnp.concatenate(
        [sums[0:6], attend_total, down_total, jnp.zeros((8, WIDTH), FULL)], axis=0
    )
    r.g_small[0:16, 0:128] = own_part(stacked, own_lanes)
    r.g_small[0:16, 128:BLOCK] = jnp.zeros((PAD, BLOCK - 128), FULL)
    half_copy(1, r.g_wup, 1 - core).wait_recv()
    up_lanes = (iota((WIDE, BLOCK), 0) == chip * deep + iota((WIDE, BLOCK), 1)).astype(LOW)
    r.g_small[16:24, :] = own_part(r.g_wup[depth : depth + 8, :], up_lanes)

    half_copy(0, r.g_wv, 1 - core).wait_recv()
    half_copy(2, r.g_wk, 1 - core).wait_recv()
    for index, ref in enumerate([r.g_wv, r.g_wup, r.g_wk]):
        half_copy(index, ref, core).wait_send()

    for index, ref in enumerate([r.every_ids, r.got_one, r.got_two, r.got_three]):
        all_but_one(ref, index).wait_send()
    all_smalls().wait_send()
    for end in [drain_a, drain_b, drain_c, drain_u, drain_e, drain_d, drain_a2, drain_q]:
        end()
    for tile in range(TOKENS // BLOCK):
        layer_copy(tile).wait()
    every(0, 2, lambda tile: table_copy(tile).wait())


def layer(inputs):
    dma = pltpu.SemaphoreType.DMA
    vmem = pl.BlockSpec(memory_space=pltpu.VMEM)
    anywhere = pl.BlockSpec(memory_space=pl.ANY)
    depth, deep = WIDTH // CHIPS, WIDE // CHIPS

    def gathered(width):
        return pltpu.VMEM((CORES, PLANES, LINES, PAD, width), LOW)

    outputs = dict(
        layer_out=((TOKENS, WIDTH), LOW),
        table_grad=((VOCAB_ROWS, WIDTH), FULL),
        g_wq=((depth, WIDTH), FULL),
        g_wk=((depth, WIDTH), FULL),
        g_wv=((depth, WIDTH), FULL),
        g_wo=((depth, WIDTH), FULL),
        g_wup=((depth + 8, WIDE), FULL),
        g_wdown=((deep, WIDTH), FULL),
        g_small=((24, BLOCK), FULL),
        loss=((1, 1), FULL),
    )
    scratch = dict(
        ids=pltpu.VMEM((8, 128), jnp.int32),
        every_ids=pltpu.VMEM((DEVICES, 8, 128), jnp.int32),
        rank=pltpu.VMEM((DEVICES, TOKENS), FULL),
        code=pltpu.VMEM((DEVICES, TOKENS), FULL),
        found=pltpu.VMEM((GROUPS + 1, SLOT_ROWS, 2), FULL),
        block_bias=pltpu.VMEM((2 * BLOCK, BLOCK // 2), FULL),
        valid_bias=pltpu.VMEM((8, TOKENS), FULL),
        slot_col=pltpu.VMEM((TOKENS, 1), FULL),
        slot_line=pltpu.VMEM((8, TOKENS), FULL),
        valid_col=pltpu.VMEM((TOKENS, 1), FULL),
        valid_line=pltpu.VMEM((8, TOKENS), FULL),
        pairs=pltpu.VMEM((8, SLOT_ROWS), FULL),
        pairs_col=pltpu.VMEM((SLOT_ROWS, 128), FULL),
        vectors=pltpu.VMEM((PAD, WIDTH), FULL),
        up_bias=pltpu.VMEM((8, WIDE), FULL),
        qkv_bias=pltpu.VMEM((8, 3 * WIDTH), FULL),
        smalls=pltpu.VMEM((PAD, CHIPS * 128), LOW),
        wa=pltpu.VMEM((WIDTH, 4 * WIDTH), LOW),
        wb=pltpu.VMEM((WIDTH, WIDE), LOW),
        wc=pltpu.VMEM((WIDE, WIDTH), LOW),
        chosen=pltpu.VMEM((GROUPS, SLOT_ROWS, VOCAB_ROWS), LOW),
        by_row=pltpu.VMEM((VOCAB_ROWS, (GROUPS + 1) * SLOT_ROWS), LOW),
        rows=pltpu.VMEM((GROUPS, SLOT_ROWS, WIDTH), LOW),
        replies=pltpu.VMEM((GROUPS, SLOT_ROWS, WIDTH), LOW),
        slot_query=pltpu.VMEM((GROUPS, SLOT_ROWS, WIDTH), LOW),
        extra=pltpu.VMEM((SLOT_ROWS, WIDTH), LOW),
        embedded=pltpu.VMEM((TOKENS, WIDTH), LOW),
        qkv=pltpu.VMEM((TOKENS, 3 * WIDTH), LOW),
        context=pltpu.VMEM((TOKENS, WIDTH), LOW),
        tile_low=pltpu.VMEM((BLOCK, WIDTH), LOW),
        tile_sum=pltpu.VMEM((BLOCK, WIDTH), FULL),
        table_full=pltpu.VMEM((VOCAB_ROWS, WIDTH), FULL),
        probs=pltpu.VMEM((PAIR_ROWS, TOKENS), FULL),
        normed_one=pltpu.VMEM((PAD, WIDTH), FULL),
        units=gathered(WIDTH),
        early=gathered(2 * WIDTH),
        downs=gathered(WIDTH),
        attends=gathered(2 * WIDTH),
        queries=gathered(2 * WIDTH),
        slopes=pltpu.VMEM((SLOT_ROWS, WIDE // 2), LOW),
        hidden_turned=pltpu.VMEM((WIDTH, SLOT_ROWS), LOW),
        active_turned=pltpu.VMEM((2 * deep, SLOT_ROWS), LOW),
        left_turned=pltpu.VMEM((128, SLOT_ROWS), LOW),
        mail_one=pltpu.VMEM((DEVICES, 80, 128), LOW),
        got_one=pltpu.VMEM((DEVICES, 80, 128), LOW),
        mail_two=pltpu.VMEM((DEVICES, 48, 128), LOW),
        got_two=pltpu.VMEM((DEVICES, 48, 128), LOW),
        mail_three=pltpu.VMEM((DEVICES, PAD, 128), LOW),
        got_three=pltpu.VMEM((DEVICES, PAD, 128), LOW),
        rows_send=dma((4,)),
        rows_recv=dma((4,)),
        one_send=dma((4,)),
        one_recv=dma((4,)),
        small_send=dma((1,)),
        small_recv=dma((1,)),
        weight_send=dma((3, 33)),
        weight_recv=dma((3, 33)),
        gather_send=dma((5, 13)),
        gather_recv=dma((5, 13)),
        half_send=dma((3,)),
        half_recv=dma((3,)),
        out_sem=dma((TOKENS // BLOCK,)),
        table_sem=dma((2,)),
    )
    names = INPUTS + OUTPUTS + list(scratch)
    return pl.pallas_call(
        partial(layer_kernel, names),
        out_shape=tuple(jax.ShapeDtypeStruct(*outputs[name]) for name in OUTPUTS),
        in_specs=[vmem] * len(INPUTS),
        out_specs=(anywhere, anywhere) + (vmem,) * (len(OUTPUTS) - 2),
        scratch_shapes=list(scratch.values()),
        compiler_params=pltpu.CompilerParams(
            collective_id=0, has_side_effects=True, vmem_limit_bytes=VMEM_LIMIT
        ),
        name="layer",
    )(*inputs)


def finish_kernel(count, *refs):
    large, (small, loss), outs = refs[:count], refs[count : count + 2], refs[count + 2 : 2 * count + 12]
    held, load_sems, store_sems = refs[2 * count + 12 : -2], refs[-2], refs[-1]
    pieces = []
    for index, (source, target) in enumerate(zip(large, outs)):
        rows = target.shape[0]
        step = BLOCK if rows > BLOCK else rows
        for start in range(0, rows, step):
            at = pl.ds(start, step)
            slot = len(pieces)
            pieces.append(
                (
                    pltpu.make_async_copy(source.at[at], held[index].at[at], load_sems.at[slot]),
                    pltpu.make_async_copy(held[index].at[at], target.at[at], store_sems.at[slot]),
                )
            )
    for load, _ in pieces:
        load.start()
    for row, target in zip([0, 1, 6, 2, 3, 16, 7, 4, 5], outs[count : count + 9]):
        size = target.shape[0]
        target[...] = small[row : row + 1, 0:size].reshape(size)
    outs[-1][...] = loss[...].reshape(1)
    for load, store in pieces:
        load.wait()
        store.start()
    for _, store in pieces:
        store.wait()


def finish(results):
    vmem = pl.BlockSpec(memory_space=pltpu.VMEM)
    anywhere = pl.BlockSpec(memory_space=pl.ANY)
    depth, deep = WIDTH // CHIPS, WIDE // CHIPS
    count = len(results) - 2
    shapes = [(one.shape, one.dtype) for one in results[:count]]
    shapes[6] = ((depth, WIDE), FULL)
    held = [pltpu.VMEM(*one) for one in shapes]
    shapes += [((depth,), FULL)] * 5 + [((deep,), FULL)] + [((depth,), FULL)] * 3
    shapes.append(((1,), FULL))
    dma = pltpu.SemaphoreType.DMA((16,))
    return pl.pallas_call(
        partial(finish_kernel, count),
        out_shape=tuple(jax.ShapeDtypeStruct(*one) for one in shapes),
        in_specs=[anywhere] * count + [vmem] * 2,
        out_specs=(anywhere,) * count + (vmem,) * 10,
        scratch_shapes=held + [dma, dma],
        compiler_params=pltpu.CompilerParams(vmem_limit_bytes=16 * 1024 * 1024),
        name="finish",
    )(*results)


def block_body(
    table,
    token_ids,
    sent_lengths,
    pair_slot,
    pair_lang,
    *parameters,
):
    results = finish(layer((table, token_ids, sent_lengths, pair_slot, pair_lang) + parameters))
    layer_out, table_grad, g_wq, g_wk, g_wv, g_wo, g_wup, g_wdown = results[:8]
    g_bq, g_bv, g_bo, g_g1, g_s1, g_bup, g_bdown, g_g2, g_s2, loss = results[8:]
    return (
        layer_out.reshape(token_ids.shape + (WIDTH,)),
        loss.reshape(()),
        table_grad,
        g_wq,
        g_bq,
        g_wk,
        g_wv,
        g_bv,
        g_wo,
        g_bo,
        g_g1,
        g_s1,
        g_wup,
        g_bup,
        g_wdown,
        g_bdown,
        g_g2,
        g_s2,
    )


def solution(mesh):
    in_specs = (
        P(("dp", "fsdp"), None),
        P(("dp", "fsdp"), None),
        P(("dp", "fsdp")),
        P(),
        P(),
        P("fsdp", None),
        P("fsdp"),
        P("fsdp", None),
        P("fsdp", None),
        P("fsdp"),
        P("fsdp", None),
        P("fsdp"),
        P("fsdp"),
        P("fsdp"),
        P("fsdp", None),
        P("fsdp"),
        P("fsdp", None),
        P("fsdp"),
        P("fsdp"),
        P("fsdp"),
    )
    out_specs = (
        P(("dp", "fsdp"), None, None),
        P(),
        P(("dp", "fsdp"), None),
        P("fsdp", None),
        P("fsdp"),
        P("fsdp", None),
        P("fsdp", None),
        P("fsdp"),
        P("fsdp", None),
        P("fsdp"),
        P("fsdp"),
        P("fsdp"),
        P("fsdp", None),
        P("fsdp"),
        P("fsdp", None),
        P("fsdp"),
        P("fsdp"),
        P("fsdp"),
    )
    sizes = dict(mesh.shape)
    body = general_body
    if sizes["dp"] == CORES and sizes["fsdp"] == CHIPS:
        body = block_body
    return jax.shard_map(body, mesh=mesh, in_specs=in_specs, out_specs=out_specs, check_vma=False)
```

```python
from functools import partial
from types import SimpleNamespace

import jax
import jax.numpy as jnp
from jax import lax
from jax.experimental import pallas as pl
from jax.experimental.pallas import tpu as pltpu
from jax.sharding import PartitionSpec as P

HEADS = 12
HEAD = 64
LANGS = 109


EPSILON = 1e-06
SCORE_SCALE = 50.0
MARGIN_WIDTH = 0.3
MASK_FLOOR = -1000000000.0


def contract(left_side, right_side, left_dim, right_dim):
    return lax.dot_general(
        left_side,
        right_side,
        (((left_dim,), (right_dim,)), ((), ())),
        preferred_element_type=jnp.float32,
    )


def norm_rows(inputs, ln_gain, ln_shift):
    row_mean = jnp.mean(inputs, axis=-1, keepdims=True)
    centered = inputs - row_mean
    variance = jnp.mean(centered * centered, axis=-1, keepdims=True)
    inverse = lax.rsqrt(variance + EPSILON)
    normed = centered * inverse
    return (normed * ln_gain + ln_shift, normed, inverse)


def norm_back(grad_output, normed, inverse, ln_gain):
    grad_normed = grad_output * ln_gain
    first_term = jnp.mean(grad_normed, axis=-1, keepdims=True)
    second_term = jnp.mean(grad_normed * normed, axis=-1, keepdims=True)
    grad_input = inverse * (grad_normed - first_term - normed * second_term)
    return (grad_input, jnp.sum(grad_output * normed, axis=0), jnp.sum(grad_output, axis=0))


def general_body(
    table,
    token_ids,
    sent_lengths,
    pair_slot,
    pair_lang,
    w_query,
    b_query,
    w_key,
    w_value,
    b_value,
    w_out,
    b_out,
    ln1_gain,
    ln1_bias,
    w_up,
    b_up,
    w_down,
    b_down,
    ln2_gain,
    ln2_bias,
):
    sentences, length = token_ids.shape
    tokens = sentences * length
    vocab_rows, model_width = table.shape
    owners = lax.axis_size(("dp", "fsdp"))
    dp_count = lax.axis_size("dp")
    fsdp_count = lax.axis_size("fsdp")
    capacity = max(2, 2 * tokens // owners)
    device = lax.axis_index(("dp", "fsdp"))
    score_factor = HEAD ** (-0.5)
    flat_ids = token_ids.reshape(tokens)
    owner_of = flat_ids // vocab_rows
    member = (owner_of[:, None] == jnp.arange(owners, dtype=jnp.int32)[None, :]).astype(jnp.int32)
    owner_rank = jnp.sum(jnp.cumsum(member, axis=0) * member, axis=1) - 1
    slot_of = owner_of * capacity + owner_rank
    requests = jnp.full((owners * capacity,), -1, jnp.int32).at[slot_of].set(flat_ids)
    received = lax.all_to_all(
        lax.all_to_all(
            requests.reshape(dp_count, fsdp_count, capacity),
            "dp",
            split_axis=0,
            concat_axis=0,
            tiled=True,
        ),
        "fsdp",
        split_axis=1,
        concat_axis=1,
        tiled=True,
    )
    present = received >= 0
    local_rows = jnp.where(present, received - device * vocab_rows, 0)
    found_rows = jnp.where(present[..., None], table[local_rows], jnp.zeros((), table.dtype))
    replies = lax.all_to_all(
        lax.all_to_all(found_rows, "dp", split_axis=0, concat_axis=0, tiled=True),
        "fsdp",
        split_axis=1,
        concat_axis=1,
        tiled=True,
    )
    embedded = replies.reshape(owners * capacity, model_width)[slot_of]
    gathered = (
        lax.all_gather(w_query, "fsdp", axis=0, tiled=True),
        lax.all_gather(b_query, "fsdp", axis=0, tiled=True),
        lax.all_gather(w_key, "fsdp", axis=0, tiled=True),
        lax.all_gather(w_value, "fsdp", axis=0, tiled=True),
        lax.all_gather(b_value, "fsdp", axis=0, tiled=True),
        lax.all_gather(w_out, "fsdp", axis=0, tiled=True),
        lax.all_gather(b_out, "fsdp", axis=0, tiled=True),
        lax.all_gather(ln1_gain, "fsdp", axis=0, tiled=True),
        lax.all_gather(ln1_bias, "fsdp", axis=0, tiled=True),
        lax.all_gather(w_up, "fsdp", axis=0, tiled=True),
        lax.all_gather(b_up, "fsdp", axis=0, tiled=True),
        lax.all_gather(w_down, "fsdp", axis=0, tiled=True),
        lax.all_gather(b_down, "fsdp", axis=0, tiled=True),
        lax.all_gather(ln2_gain, "fsdp", axis=0, tiled=True),
        lax.all_gather(ln2_bias, "fsdp", axis=0, tiled=True),
    )
    (
        full_wq,
        full_bq,
        full_wk,
        full_wv,
        full_bv,
        full_wo,
        full_bo,
        full_g1,
        full_s1,
        full_wup,
        full_bup,
        full_wdown,
        full_bdown,
        full_g2,
        full_s2,
    ) = gathered
    valid_mask = jnp.arange(length, dtype=jnp.int32)[None, :] < sent_lengths[:, None]
    head_shape = (sentences, length, HEADS, HEAD)
    queries = (jnp.dot(embedded, full_wq, preferred_element_type=jnp.float32) + full_bq).astype(
        jnp.bfloat16
    )
    key_heads = (
        jnp.dot(embedded, full_wk, preferred_element_type=jnp.float32)
        .astype(jnp.bfloat16)
        .reshape(head_shape)
    )
    value_heads = (
        (jnp.dot(embedded, full_wv, preferred_element_type=jnp.float32) + full_bv)
        .astype(jnp.bfloat16)
        .reshape(head_shape)
    )
    query_heads = queries.reshape(head_shape)
    scores = (
        jnp.einsum("bqhd,bkhd->bhqk", query_heads, key_heads, preferred_element_type=jnp.float32)
        * score_factor
    )
    scores = jnp.where(valid_mask[:, None, None, :], scores, MASK_FLOOR)
    row_peak = jnp.max(scores, axis=-1, keepdims=True)
    shifted = jnp.exp(scores - row_peak)
    totals = jnp.sum(shifted, axis=-1, keepdims=True)
    attn_probs = (shifted / totals).astype(jnp.bfloat16)
    context = jnp.einsum(
        "bhqk,bkhd->bqhd", attn_probs, value_heads, preferred_element_type=jnp.float32
    )
    context = context.reshape(tokens, model_width).astype(jnp.bfloat16)
    attended = jnp.dot(context, full_wo, preferred_element_type=jnp.float32) + full_bo
    hidden, normed_one, inverse_one = norm_rows(
        embedded.astype(jnp.float32) + attended, full_g1, full_s1
    )
    hidden_low = hidden.astype(jnp.bfloat16)
    up_pre = jnp.dot(hidden_low, full_wup, preferred_element_type=jnp.float32) + full_bup
    activated = jax.nn.gelu(up_pre, approximate=False).astype(jnp.bfloat16)
    down_pre = jnp.dot(activated, full_wdown, preferred_element_type=jnp.float32) + full_bdown
    normed_out, normed_two, inverse_two = norm_rows(hidden + down_pre, full_g2, full_s2)
    layer_out = jnp.where(valid_mask.reshape(tokens)[:, None], normed_out, 0.0).astype(jnp.bfloat16)
    layer_out = layer_out.reshape(sentences, length, model_width)

    def first_rows(matrix):
        return matrix.reshape(sentences, length, matrix.shape[-1])[:, 0]

    summary = first_rows(normed_out)
    magnitude = jnp.sqrt(jnp.sum(summary * summary, axis=-1, keepdims=True) + EPSILON)
    unit_vector = summary / magnitude
    unit_low = unit_vector.astype(jnp.bfloat16)
    every_unit = lax.all_gather(unit_low, ("dp", "fsdp"), axis=0, tiled=True)
    every_side = pair_slot % 2
    every_pair = pair_slot // 2
    my_slots = lax.dynamic_slice_in_dim(pair_slot, device * sentences, sentences)
    my_side = my_slots % 2
    my_pair = my_slots // 2
    lang_onehot = (pair_lang[:, None] == jnp.arange(LANGS, dtype=jnp.int32)[None, :]).astype(
        jnp.float32
    )
    per_lang = jnp.sum(lang_onehot, axis=0)
    per_pair = 1.0 / (2.0 * LANGS * jnp.sum(lang_onehot * per_lang[None, :], axis=1))
    my_weight = jnp.take(per_pair, my_pair)
    opposite = my_side[:, None] != every_side[None, :]
    partner = opposite & (my_pair[:, None] == every_pair[None, :])
    raw_scores = SCORE_SCALE * contract(unit_low, every_unit, 1, 1)
    pair_scores = jnp.where(partner, raw_scores - SCORE_SCALE * MARGIN_WIDTH, raw_scores)
    pair_scores = jnp.where(opposite, pair_scores, MASK_FLOOR)
    pair_peak = jnp.max(pair_scores, axis=1, keepdims=True)
    pair_exp = jnp.exp(pair_scores - pair_peak)
    pair_total = jnp.sum(pair_exp, axis=1, keepdims=True)
    log_total = pair_peak[:, 0] + jnp.log(pair_total[:, 0])
    picked = jnp.sum(jnp.where(partner, pair_scores, 0.0), axis=1)
    loss_value = lax.psum(jnp.sum(my_weight * (log_total - picked)), ("dp", "fsdp"))
    coefficients = (
        my_weight[:, None] * (pair_exp / pair_total - partner.astype(jnp.float32))
    ).astype(jnp.bfloat16)
    unit_grad = SCORE_SCALE * contract(coefficients, every_unit, 1, 0)
    column_terms = SCORE_SCALE * contract(coefficients, unit_low, 0, 0)
    unit_grad = unit_grad + lax.psum_scatter(
        column_terms, ("dp", "fsdp"), scatter_dimension=0, tiled=True
    )
    along = jnp.sum(unit_vector * unit_grad, axis=-1, keepdims=True)
    summary_grad = (unit_grad - unit_vector * along) / magnitude
    again_weights = (
        lax.all_gather(w_query, "fsdp", axis=0, tiled=True),
        lax.all_gather(w_key, "fsdp", axis=0, tiled=True),
        lax.all_gather(w_value, "fsdp", axis=0, tiled=True),
        lax.all_gather(w_out, "fsdp", axis=0, tiled=True),
        lax.all_gather(ln1_gain, "fsdp", axis=0, tiled=True),
        lax.all_gather(w_up, "fsdp", axis=0, tiled=True),
        lax.all_gather(w_down, "fsdp", axis=0, tiled=True),
        lax.all_gather(ln2_gain, "fsdp", axis=0, tiled=True),
    )
    again_wq, again_wk, again_wv, again_wo, again_g1, again_wup, again_wdown, again_g2 = (
        again_weights
    )
    residual_grad, grad_g2, grad_s2 = norm_back(
        summary_grad, first_rows(normed_two), first_rows(inverse_two), again_g2
    )
    down_grad = residual_grad.astype(jnp.bfloat16)
    activated_cls = first_rows(activated)
    act_grad = contract(down_grad, again_wdown, 1, 1)
    gelu_value, gelu_pull = jax.vjp(partial(jax.nn.gelu, approximate=False), first_rows(up_pre))
    up_grad = gelu_pull(act_grad)[0].astype(jnp.bfloat16)
    hidden_cls = first_rows(hidden_low)
    hidden_grad = contract(up_grad, again_wup, 1, 1) + residual_grad
    first_grad, grad_g1, grad_s1 = norm_back(
        hidden_grad, first_rows(normed_one), first_rows(inverse_one), again_g1
    )
    attend_grad = first_grad.astype(jnp.bfloat16)
    context_cls = first_rows(context)
    context_grad = (
        contract(attend_grad, again_wo, 1, 1).astype(jnp.bfloat16).reshape(sentences, HEADS, HEAD)
    )
    query_cls = query_heads[:, 0]
    cls_scores = (
        jnp.einsum("bhd,bkhd->bhk", query_cls, key_heads, preferred_element_type=jnp.float32)
        * score_factor
    )
    cls_scores = jnp.where(valid_mask[:, None, :], cls_scores, MASK_FLOOR)
    cls_probs = jnp.exp(cls_scores - row_peak[:, :, 0]) / totals[:, :, 0]
    prob_grad = jnp.einsum(
        "bhd,bkhd->bhk", context_grad, value_heads, preferred_element_type=jnp.float32
    )
    score_grad = (
        cls_probs * (prob_grad - jnp.sum(cls_probs * prob_grad, axis=-1, keepdims=True))
    ).astype(jnp.bfloat16)
    query_grad = (
        (
            jnp.einsum("bhk,bkhd->bhd", score_grad, key_heads, preferred_element_type=jnp.float32)
            * score_factor
        )
        .astype(jnp.bfloat16)
        .reshape(sentences, model_width)
    )
    key_grad = (
        (
            jnp.einsum("bhk,bhd->bkhd", score_grad, query_cls, preferred_element_type=jnp.float32)
            * score_factor
        )
        .astype(jnp.bfloat16)
        .reshape(tokens, model_width)
    )
    value_grad = (
        jnp.einsum(
            "bhk,bhd->bkhd",
            cls_probs.astype(jnp.bfloat16),
            context_grad,
            preferred_element_type=jnp.float32,
        )
        .astype(jnp.bfloat16)
        .reshape(tokens, model_width)
    )
    embedded_cls = first_rows(embedded)
    grad_wkey = contract(embedded, key_grad, 0, 0)
    grad_wvalue = contract(embedded, value_grad, 0, 0)
    grad_bvalue = jnp.sum(value_grad, axis=0, dtype=jnp.float32)
    row_grads = contract(key_grad, again_wk, 1, 1) + contract(value_grad, again_wv, 1, 1)
    summary_extra = contract(query_grad, again_wq, 1, 1) + first_grad
    row_grads = (
        row_grads.reshape(sentences, length, model_width)
        .at[:, 0]
        .add(summary_extra)
        .reshape(tokens, model_width)
    )
    outgoing = jnp.zeros((owners * capacity, model_width), jnp.float32).at[slot_of].set(row_grads)
    incoming = lax.all_to_all(
        lax.all_to_all(
            outgoing.reshape(dp_count, fsdp_count, capacity, model_width).astype(jnp.bfloat16),
            "dp",
            split_axis=0,
            concat_axis=0,
            tiled=True,
        ),
        "fsdp",
        split_axis=1,
        concat_axis=1,
        tiled=True,
    ).astype(jnp.float32)
    incoming = jnp.where(
        present.reshape(owners * capacity)[:, None],
        incoming.reshape(owners * capacity, model_width),
        0.0,
    )
    table_grad = (
        jnp.zeros((vocab_rows, model_width), jnp.float32)
        .at[local_rows.reshape(owners * capacity)]
        .add(incoming)
    )
    grad_wquery = contract(embedded_cls, query_grad, 0, 0)
    grad_bquery = jnp.sum(query_grad, axis=0, dtype=jnp.float32)
    grad_wout = contract(context_cls, attend_grad, 0, 0)
    grad_bout = jnp.sum(attend_grad, axis=0, dtype=jnp.float32)
    grad_wup = contract(hidden_cls, up_grad, 0, 0)
    grad_bup = jnp.sum(up_grad, axis=0, dtype=jnp.float32)
    grad_wdown = contract(activated_cls, down_grad, 0, 0)
    grad_bdown = jnp.sum(down_grad, axis=0, dtype=jnp.float32)
    owned_grads = (
        lax.psum_scatter(
            grad_wquery.astype(jnp.bfloat16), "fsdp", scatter_dimension=0, tiled=True
        ).astype(jnp.float32),
        lax.psum_scatter(
            grad_bquery.astype(jnp.bfloat16), "fsdp", scatter_dimension=0, tiled=True
        ).astype(jnp.float32),
        lax.psum_scatter(
            grad_wkey.astype(jnp.bfloat16), "fsdp", scatter_dimension=0, tiled=True
        ).astype(jnp.float32),
        lax.psum_scatter(
            grad_wvalue.astype(jnp.bfloat16), "fsdp", scatter_dimension=0, tiled=True
        ).astype(jnp.float32),
        lax.psum_scatter(
            grad_bvalue.astype(jnp.bfloat16), "fsdp", scatter_dimension=0, tiled=True
        ).astype(jnp.float32),
        lax.psum_scatter(
            grad_wout.astype(jnp.bfloat16), "fsdp", scatter_dimension=0, tiled=True
        ).astype(jnp.float32),
        lax.psum_scatter(
            grad_bout.astype(jnp.bfloat16), "fsdp", scatter_dimension=0, tiled=True
        ).astype(jnp.float32),
        lax.psum_scatter(
            grad_g1.astype(jnp.bfloat16), "fsdp", scatter_dimension=0, tiled=True
        ).astype(jnp.float32),
        lax.psum_scatter(
            grad_s1.astype(jnp.bfloat16), "fsdp", scatter_dimension=0, tiled=True
        ).astype(jnp.float32),
        lax.psum_scatter(
            grad_wup.astype(jnp.bfloat16), "fsdp", scatter_dimension=0, tiled=True
        ).astype(jnp.float32),
        lax.psum_scatter(
            grad_bup.astype(jnp.bfloat16), "fsdp", scatter_dimension=0, tiled=True
        ).astype(jnp.float32),
        lax.psum_scatter(
            grad_wdown.astype(jnp.bfloat16), "fsdp", scatter_dimension=0, tiled=True
        ).astype(jnp.float32),
        lax.psum_scatter(
            grad_bdown.astype(jnp.bfloat16), "fsdp", scatter_dimension=0, tiled=True
        ).astype(jnp.float32),
        lax.psum_scatter(
            grad_g2.astype(jnp.bfloat16), "fsdp", scatter_dimension=0, tiled=True
        ).astype(jnp.float32),
        lax.psum_scatter(
            grad_s2.astype(jnp.bfloat16), "fsdp", scatter_dimension=0, tiled=True
        ).astype(jnp.float32),
    )
    summed = (
        lax.psum(owned_grads[0].astype(jnp.bfloat16), "dp").astype(jnp.float32),
        lax.psum(owned_grads[1].astype(jnp.bfloat16), "dp").astype(jnp.float32),
        lax.psum(owned_grads[2].astype(jnp.bfloat16), "dp").astype(jnp.float32),
        lax.psum(owned_grads[3].astype(jnp.bfloat16), "dp").astype(jnp.float32),
        lax.psum(owned_grads[4].astype(jnp.bfloat16), "dp").astype(jnp.float32),
        lax.psum(owned_grads[5].astype(jnp.bfloat16), "dp").astype(jnp.float32),
        lax.psum(owned_grads[6].astype(jnp.bfloat16), "dp").astype(jnp.float32),
        lax.psum(owned_grads[7].astype(jnp.bfloat16), "dp").astype(jnp.float32),
        lax.psum(owned_grads[8].astype(jnp.bfloat16), "dp").astype(jnp.float32),
        lax.psum(owned_grads[9].astype(jnp.bfloat16), "dp").astype(jnp.float32),
        lax.psum(owned_grads[10].astype(jnp.bfloat16), "dp").astype(jnp.float32),
        lax.psum(owned_grads[11].astype(jnp.bfloat16), "dp").astype(jnp.float32),
        lax.psum(owned_grads[12].astype(jnp.bfloat16), "dp").astype(jnp.float32),
        lax.psum(owned_grads[13].astype(jnp.bfloat16), "dp").astype(jnp.float32),
        lax.psum(owned_grads[14].astype(jnp.bfloat16), "dp").astype(jnp.float32),
    )
    return (
        layer_out,
        loss_value,
        table_grad,
        summed[0],
        summed[1],
        summed[2],
        summed[3],
        summed[4],
        summed[5],
        summed[6],
        summed[7],
        summed[8],
        summed[9],
        summed[10],
        summed[11],
        summed[12],
        summed[13],
        summed[14],
    )


CORES = 2
PLANES = 4
LINES = 4
CHIPS = PLANES * LINES
DEVICES = CORES * CHIPS
CAPACITY = 48
GROUPS = 3
PAD = 16
TOKENS = 768
WIDTH = 768
WIDE = 3072
VOCAB_ROWS = 1024
PAIR_ROWS = HEADS * PAD
SLOT_ROWS = DEVICES * PAD
LONG = 64
BLOCK = 256
MESH = pl.DeviceIdType.MESH
LOW = jnp.bfloat16
FULL = jnp.float32
VMEM_LIMIT = 62 * 1024 * 1024

INPUTS = ["table", "token_ids", "lens", "slots", "langs"]
INPUTS += ["wq", "bq", "wk", "wv", "bv", "wo", "bo", "g1", "s1", "wup", "bup", "wdown", "bdown"]
INPUTS += ["g2", "s2"]
OUTPUTS = ["layer_out", "table_grad", "g_wq", "g_wk", "g_wv", "g_wo", "g_wup", "g_wdown"]
OUTPUTS += ["g_small", "loss"]


def place():
    core = lax.axis_index("dp")
    chip = lax.axis_index("fsdp")
    along_x = chip + 1 - 2 * (chip % 2)
    along_y = chip + 2 - 4 * ((chip // 2) % 2)
    first = along_x + core * (along_y - along_x)
    second = along_y + core * (along_x - along_y)
    return core, chip, first, second


def greet():
    core, chip, _, _ = place()
    me = core * CHIPS + chip
    barrier = pltpu.get_barrier_semaphore()

    def signal(step):
        other = lax.rem(me + step, DEVICES)
        pl.semaphore_signal(
            barrier,
            inc=1,
            device_id=(lax.div(other, CHIPS), lax.rem(other, CHIPS)),
            device_id_type=MESH,
        )

    every(1, DEVICES, signal)


def enter():
    pl.semaphore_wait(pltpu.get_barrier_semaphore(), DEVICES - 1)


def remote(source, target, send_sem, recv_sem, core, chip):
    return pltpu.make_async_remote_copy(
        src_ref=source,
        dst_ref=target,
        send_sem=send_sem,
        recv_sem=recv_sem,
        device_id=(core, chip),
        device_id_type=MESH,
    )


def every(start, stop, act):
    def step(index, carry):
        act(index)
        return carry

    lax.fori_loop(start, stop, step, 0)


def weight_steps(piece, send, recv):
    core, chip, first, second = place()
    plane, line = chip // LINES, chip % LINES
    line_first, line_second = first % LINES, second % LINES
    line_far = line_first + line_second - line
    is_low, is_high = plane > 0, plane < PLANES - 1

    def copy(send_index, recv_index, at, to_core, to_chip, carried=core):
        part = piece(at, carried)
        return remote(part, part, send.at[send_index], recv.at[recv_index], to_core, to_chip)

    def up(at_plane):
        return copy(at_plane, at_plane, at_plane * LINES + line, core, chip + LINES)

    def down(at_plane, index):
        return copy(index, at_plane, at_plane * LINES + line, core, chip - LINES)

    def side(at_plane, base, at_line, target):
        return copy(base + at_plane, base + at_plane, at_plane * LINES + at_line, core, target)

    def across(at_plane, base, at_line):
        return copy(base + at_plane, base + at_plane, at_plane * LINES + at_line, 1 - core, chip)

    def begin():
        pl.when(is_high)(lambda: up(plane).start())
        pl.when(is_low)(lambda: down(plane, PLANES).start())
        side(plane, 5, line, first).start()
        side(plane, 9, line, second).start()

    def at_distance(distance, act):
        if distance == 0:
            act(plane, None)
            return
        pl.when(plane >= distance)(lambda: act(plane - distance, True))
        pl.when(plane + distance < PLANES)(lambda: act(plane + distance, False))

    def chain(distance):
        def act(at_plane, from_low):
            if from_low:
                up(at_plane).wait_recv()
                pl.when(is_high)(lambda: up(at_plane).start())
            else:
                down(at_plane, at_plane).wait_recv()
                pl.when(is_low)(lambda: down(at_plane, at_plane).start())
            side(at_plane, 5, line, first).start()
            side(at_plane, 9, line, second).start()
            across(at_plane, 17, line).start()

        return partial(at_distance, distance, act)

    def near(distance):
        def act(at_plane, from_low):
            side(at_plane, 5, line_first, first).wait_recv()
            side(at_plane, 13, line_first, second).start()
            across(at_plane, 21, line_first).start()

        return partial(at_distance, distance, act)

    def far(distance):
        def act(at_plane, from_low):
            side(at_plane, 9, line_second, second).wait_recv()
            across(at_plane, 25, line_second).start()
            side(at_plane, 13, line_far, second).wait_recv()
            across(at_plane, 29, line_far).start()

        return partial(at_distance, distance, act)

    def finish():
        for step in range(1, PLANES):
            index = 17 + (plane + step) % PLANES
            copy(index, index, chip, 1 - core, chip, 1 - core).wait_recv()
        every(21, 33, lambda index: copy(index, index, chip, 1 - core, chip, 1 - core).wait_recv())

    def drain():
        def sent(index):
            copy(index, index, chip, 1 - core, chip).wait_send()

        for at_plane in range(PLANES):
            pl.when((plane >= at_plane) & is_high)(partial(sent, at_plane))
            pl.when((plane < at_plane) & is_low)(partial(sent, at_plane))
        pl.when(is_low)(partial(sent, PLANES))
        every(5, 17, sent)
        for step in range(1, PLANES):
            sent(17 + (plane + step) % PLANES)
        every(21, 33, sent)

    moves = [chain(1), near(0), chain(2), near(1), chain(3), far(0)]
    moves += [near(2), far(1), near(3), far(2), far(3)]
    return begin, moves, finish, drain


def gather_steps(buffer, send, recv):
    core, chip, first, second = place()
    plane, line = chip // LINES, chip % LINES
    line_first, line_second = first % LINES, second % LINES
    line_far = line_first + line_second - line
    half = buffer.shape[-1] // 2
    columns = pl.ds(pl.multiple_of(core * half, 128), half)
    others = pl.ds(pl.multiple_of((1 - core) * half, 128), half)

    def copy(index, part, to_core, to_chip):
        return remote(part, part, send.at[index], recv.at[index], to_core, to_chip)

    def own(at):
        return buffer.at[at, plane, line]

    def chip_part(at_plane, at_line, which):
        return buffer.at[:, at_plane, at_line, :, which]

    def line_part(at_line, which):
        return buffer.at[:, :, at_line, :, which]

    def start():
        copy(0, own(core), 1 - core, chip).start()

    def planes():
        copy(0, own(1 - core), 1 - core, chip).wait_recv()
        for step in range(1, PLANES):
            part = chip_part(plane, line, columns)
            copy(step, part, core, (chip + LINES * step) % CHIPS).start()

    def sides():
        for step in range(1, PLANES):
            part = chip_part((plane + PLANES - step) % PLANES, line, columns)
            copy(step, part, core, chip).wait_recv()
        copy(4, line_part(line, columns), core, first).start()
        copy(5, line_part(line, columns), core, second).start()
        for step in range(1, PLANES):
            part = chip_part((plane + PLANES - step) % PLANES, line, columns)
            copy(6 + step, part, 1 - core, chip).start()

    def corner():
        copy(4, line_part(line_first, columns), core, first).wait_recv()
        copy(6, line_part(line_first, columns), core, second).start()
        copy(10, line_part(line_first, columns), 1 - core, chip).start()
        copy(5, line_part(line_second, columns), core, second).wait_recv()
        copy(11, line_part(line_second, columns), 1 - core, chip).start()

    def last():
        copy(6, line_part(line_far, columns), core, second).wait_recv()
        copy(12, line_part(line_far, columns), 1 - core, chip).start()

    def finish():
        for step in range(1, PLANES):
            part = chip_part((plane + PLANES - step) % PLANES, line, others)
            copy(6 + step, part, 1 - core, chip).wait_recv()
        copy(10, line_part(line_second, others), 1 - core, chip).wait_recv()
        copy(11, line_part(line_first, others), 1 - core, chip).wait_recv()
        copy(12, line_part(line_far, others), 1 - core, chip).wait_recv()

    def drain():
        copy(0, own(core), 1 - core, chip).wait_send()
        for index in [1, 2, 3, 7, 8, 9]:
            copy(index, chip_part(plane, line, columns), 1 - core, chip).wait_send()
        for index in [4, 5, 6, 10, 11, 12]:
            copy(index, line_part(line, columns), 1 - core, chip).wait_send()

    return [start, planes, sides, corner, last, finish], drain


def iota(shape, axis):
    return lax.broadcasted_iota(jnp.int32, shape, axis)


def as_column(row):
    parts = []
    for start in range(0, row.shape[1], 128):
        tile = jnp.broadcast_to(row[:, start : start + 128], (128, 128))
        parts.append(jnp.transpose(tile)[:, 0:1])
    return jnp.concatenate(parts, axis=0)


def as_row(column):
    parts = []
    for start in range(0, column.shape[0], 128):
        tile = jnp.broadcast_to(column[start : start + 128, :], (128, 128))
        parts.append(jnp.transpose(tile)[0:1, :])
    return jnp.concatenate(parts, axis=1)


def dot(left_side, right_side):
    return contract(left_side, right_side, 1, 0)


def dot_turned(left_side, right_side):
    return contract(left_side, right_side, 1, 1)


def norm_parts(inputs):
    centered = inputs - jnp.mean(inputs, axis=-1, keepdims=True)
    inverse = lax.rsqrt(jnp.mean(centered * centered, axis=-1, keepdims=True) + EPSILON)
    return centered * inverse, inverse


def norm_back_parts(grad_output, normed, inverse, ln_gain):
    grad_normed = grad_output * ln_gain
    first_term = jnp.mean(grad_normed, axis=-1, keepdims=True)
    second_term = jnp.mean(grad_normed * normed, axis=-1, keepdims=True)
    return (
        inverse * (grad_normed - first_term - normed * second_term),
        jnp.sum(grad_output * normed, axis=0, keepdims=True),
        jnp.sum(grad_output, axis=0, keepdims=True),
    )


def erf_parts(inputs):
    decay = jnp.exp(-0.5 * inputs * inputs)
    share = 1.0 / (1.0 + jnp.abs(inputs) * (0.3275911 * 0.5**0.5))
    terms = [1.061405429, -1.453152027, 1.421413741, -0.284496736, 0.254829592]
    series = 0.5 * terms[0]
    for term in terms[1:]:
        series = series * share + 0.5 * term
    tail = series * share * decay
    return jnp.where(inputs >= 0.0, 1.0 - tail, tail), decay


def gelu_parts(inputs):
    below, decay = erf_parts(inputs)
    return inputs * below, below + inputs * decay * ((2.0 * 3.141592653589793) ** -0.5)


def gelu(inputs):
    return inputs * erf_parts(inputs)[0]


def layer_kernel(names, *refs):
    r = SimpleNamespace(**dict(zip(names, refs, strict=True)))
    core, chip, _, _ = place()
    me = core * CHIPS + chip
    here = (core, chip // LINES, chip % LINES)
    scale = HEAD ** (-0.5)
    depth, deep = WIDTH // CHIPS, WIDE // CHIPS
    sentences = TOKENS // LONG

    for j in range(TOKENS // 128):
        r.ids[j : j + 1, :] = jnp.concatenate(
            [r.token_ids[2 * j : 2 * j + 1, :], r.token_ids[2 * j + 1 : 2 * j + 2, :]], axis=1
        )
    r.ids[TOKENS // 128 : 8, :] = jnp.zeros((8 - TOKENS // 128, 128), jnp.int32)
    greet()
    ahead = (iota((TOKENS, TOKENS), 0) < iota((TOKENS, TOKENS), 1)).astype(LOW)
    r.embedded[...] = ahead
    mine = pl.ds(pl.multiple_of(chip * depth, 16), depth)
    for index, shard in enumerate([r.wq, r.wk, r.wv, r.wo]):
        r.wa[mine, index * WIDTH : (index + 1) * WIDTH] = shard[...]
    r.every_ids[me] = r.ids[...]
    enter()

    def peer(step):
        other = lax.rem(me + step, DEVICES)
        return other, lax.div(other, CHIPS), lax.rem(other, CHIPS)

    def ids_copy(step):
        other, to_core, to_chip = peer(step)
        return remote(r.ids, r.every_ids.at[me], r.one_send.at[0], r.one_recv.at[0], to_core, to_chip)

    def all_but_one(ref, index):
        part = ref.at[0 : DEVICES - 1]
        return remote(part, part, r.one_send.at[index], r.one_recv.at[index], 1 - core, chip)

    every(1, DEVICES, lambda step: ids_copy(step).start())

    def block(ref, rows, columns):
        def piece(at, carried):
            return ref.at[
                pl.ds(pl.multiple_of(at * rows, 16), rows),
                pl.ds(pl.multiple_of(carried * columns, 128), columns),
            ]

        return piece

    begin_a, moves_a, finish_a, drain_a = weight_steps(
        block(r.wa, depth, 2 * WIDTH), r.weight_send.at[0], r.weight_recv.at[0]
    )
    begin_b, moves_b, finish_b, drain_b = weight_steps(
        block(r.wb, depth, WIDE // 2), r.weight_send.at[1], r.weight_recv.at[1]
    )
    begin_c, moves_c, finish_c, drain_c = weight_steps(
        block(r.wc, deep, WIDTH // 2), r.weight_send.at[2], r.weight_recv.at[2]
    )
    begin_a()
    r.wb[mine, :] = r.wup[...]
    begin_b()
    r.wc[pl.ds(pl.multiple_of(chip * deep, 16), deep), :] = r.wdown[...]
    moves_a[0]()
    moves_a[1]()

    all_but_one(r.every_ids, 0).wait_recv()
    all_ids = jnp.concatenate([r.every_ids[:, j, :] for j in range(TOKENS // 128)], axis=1)
    all_owner = all_ids // VOCAB_ROWS
    asked = all_owner == me
    ranks = dot(asked.astype(LOW), r.embedded[...])
    r.rank[...] = jnp.where(asked, ranks, -1.0)
    local_row = (all_ids - all_owner * VOCAB_ROWS + 1).astype(FULL)
    r.code[...] = local_row + (iota((DEVICES, TOKENS), 1) // LONG * 2048).astype(FULL)

    quarter_size = DEVICES // 4

    def rows_copy(other, quarter):
        return remote(
            r.rows.at[:, pl.ds(pl.multiple_of(other * PAD, 16), PAD), :],
            r.replies.at[:, pl.ds(pl.multiple_of(me * PAD, 16), PAD), :],
            r.rows_send.at[quarter],
            r.rows_recv.at[quarter],
            lax.div(other, CHIPS),
            lax.rem(other, CHIPS),
        )

    def rows_of(quarter):
        count = quarter_size - 1 if quarter == 3 else quarter_size
        part = r.replies.at[:, 0 : count * PAD, :]
        return remote(
            part, part, r.rows_send.at[quarter], r.rows_recv.at[quarter], 1 - core, chip
        )

    def pick(source):
        rank = r.rank[pl.ds(source, 1), :]
        code = r.code[pl.ds(source, 1), :]
        here_at = iota((CAPACITY, TOKENS), 0).astype(FULL) == rank
        found = jnp.sum(jnp.where(here_at, code, 0.0), axis=1, keepdims=True)
        sent = jnp.floor(found * (1.0 / 2048))
        row = found - sent * 2048.0 - 1.0
        chosen = (iota((CAPACITY, VOCAB_ROWS), 1).astype(FULL) == row).astype(LOW)
        at = pl.ds(pl.multiple_of(source * PAD, 16), PAD)
        source_sent = sent + (source * PAD).astype(FULL)
        for group in range(GROUPS):
            part = slice(group * PAD, (group + 1) * PAD)
            r.chosen[group, at, :] = chosen[part]
            r.found[group, at, 0:1] = row[part]
            r.found[group, at, 1:2] = source_sent[part]

    for quarter in range(4):
        now = lax.rem(lax.div(me, quarter_size) + 1 + quarter, 4)

        def pick_two(index):
            pick(now * quarter_size + 2 * index)
            pick(now * quarter_size + 2 * index + 1)

        every(0, quarter_size // 2, pick_two)
        span = pl.ds(pl.multiple_of(now * quarter_size * PAD, 128), quarter_size * PAD)
        picked = r.chosen[:, span, :].reshape(GROUPS * quarter_size * PAD, VOCAB_ROWS)
        found_rows = dot(picked, r.table[...]).astype(LOW)
        r.rows[:, span, :] = found_rows.reshape(GROUPS, quarter_size * PAD, WIDTH)

        def send(index):
            other = now * quarter_size + lax.rem(lax.rem(me, quarter_size) + index, quarter_size)
            rows_copy(other, quarter).start()

        every(1 if quarter == 3 else 0, quarter_size, send)
        moves_a[2 + quarter]()
    begin_c()
    own_at = pl.ds(pl.multiple_of(me * PAD, 16), PAD)
    r.replies[:, own_at, :] = r.rows[:, own_at, :]

    small_here = pl.ds(pl.multiple_of(chip * 128, 128), 128)
    lines = [r.bq, r.bv, r.bo, r.g1, r.s1, r.bdown, r.g2, r.s2]
    lines = [line[...].reshape(1, depth).astype(FULL) for line in lines]
    up_line = r.bup[...].reshape(1, deep).astype(FULL)
    lines += [up_line[:, part * depth : (part + 1) * depth] for part in range(deep // depth)]
    lines.append(jnp.zeros((PAD - len(lines), depth), FULL))
    own_small = jnp.concatenate(lines, axis=0)
    own_small = jnp.concatenate([own_small, jnp.zeros((PAD, 128 - depth), FULL)], axis=1)
    r.smalls[:, small_here] = own_small.astype(LOW)

    def small_copy(step):
        part = r.smalls.at[:, small_here]
        to_chip = lax.rem(chip + step, CHIPS)
        return remote(part, part, r.small_send.at[0], r.small_recv.at[0], core, to_chip)

    def all_smalls():
        part = r.smalls.at[:, 0 : (CHIPS - 1) * 128]
        return remote(part, part, r.small_send.at[0], r.small_recv.at[0], 1 - core, chip)

    every(1, CHIPS, lambda step: small_copy(step).start())

    own_row = jnp.concatenate([r.ids[j : j + 1, :] for j in range(TOKENS // 128)], axis=1)
    owner_row = (own_row // VOCAB_ROWS).astype(FULL)
    owner_col = as_column(owner_row)
    earlier = (owner_row == owner_col) & (iota((TOKENS, TOKENS), 1) < iota((TOKENS, TOKENS), 0))
    own_rank = jnp.sum(earlier.astype(FULL), axis=1, keepdims=True)
    own_group = jnp.floor(own_rank * (1.0 / PAD))
    own_slot = own_group * SLOT_ROWS + owner_col * PAD + (own_rank - own_group * PAD)
    r.slot_col[...] = own_slot
    r.slot_line[0:1, :] = as_row(own_slot)

    at_sent = iota((1, TOKENS), 1) // LONG
    lens = jnp.concatenate(
        [r.lens[...].reshape(1, sentences).astype(FULL), jnp.zeros((1, PAD - sentences), FULL)],
        axis=1,
    )
    spread_lens = dot(
        jnp.broadcast_to(lens, (8, PAD)).astype(LOW),
        (iota((PAD, TOKENS), 0) == iota((PAD, TOKENS), 1) // LONG).astype(LOW),
    )[0:1]
    valid_row = ((iota((1, TOKENS), 1) - at_sent * LONG).astype(FULL) < spread_lens).astype(FULL)
    r.valid_line[0:1, :] = valid_row
    r.valid_col[...] = as_column(valid_row)
    half_block = BLOCK // 2
    stacked_shape = (4 * half_block, half_block)
    same = iota(stacked_shape, 0) // LONG % 2 == iota(stacked_shape, 1) // LONG
    r.block_bias[...] = jnp.where(same, 0.0, MASK_FLOOR)
    r.valid_bias[0:1, :] = (1.0 - valid_row) * MASK_FLOOR

    slots = r.slots[...].reshape(1, DEVICES * sentences)
    gap = jnp.full((1, PAD - sentences), -2, jnp.int32)
    slot_line = jnp.concatenate(
        [
            part
            for device in range(DEVICES)
            for part in (slots[:, device * sentences : (device + 1) * sentences], gap)
        ],
        axis=1,
    )
    side_line = slot_line - slot_line // 2 * 2 + jnp.where(slot_line < 0, 8, 0)
    pair_line = slot_line // 2
    pairs = r.langs.shape[0]
    lang_line = r.langs[...].reshape(1, pairs).astype(FULL)
    lang_line = jnp.concatenate([lang_line, jnp.full((1, -pairs % 128), -1.0, FULL)], axis=1)
    lang_col = as_column(lang_line)
    same_lang = jnp.sum(jnp.where(lang_col == lang_line, 1.0, 0.0), axis=1, keepdims=True)
    per_pair = 1.0 / (2.0 * LANGS * same_lang)
    at_pair = iota((lang_line.shape[1], SLOT_ROWS), 0) == pair_line
    weight_line = jnp.sum(jnp.where(at_pair, per_pair, 0.0), axis=0, keepdims=True)
    r.pairs[0:1, :] = weight_line
    r.pairs[1:2, :] = pair_line.astype(FULL)
    r.pairs[2:3, :] = side_line.astype(FULL)
    r.pairs_col[:, 0:1] = as_column(weight_line)
    r.pairs_col[:, 1:2] = as_column(pair_line.astype(FULL))
    r.pairs_col[:, 2:3] = as_column(side_line.astype(FULL))
    for move in moves_a[6:] + moves_b[:2]:
        move()

    all_smalls().wait_recv()
    smalls = r.smalls[...].astype(FULL)
    r.vectors[:, 0:WIDTH] = jnp.concatenate(
        [smalls[:, at * 128 : at * 128 + depth] for at in range(CHIPS)], axis=1
    )
    r.up_bias[0:1, :] = jnp.concatenate(
        [
            smalls[8 + part : 9 + part, at * 128 : at * 128 + depth]
            for at in range(CHIPS)
            for part in range(deep // depth)
        ],
        axis=1,
    )

    def vector(index):
        return r.vectors[index : index + 1, :]

    r.qkv_bias[0:1, 0:WIDTH] = vector(0)
    r.qkv_bias[0:1, WIDTH : 2 * WIDTH] = jnp.zeros((1, WIDTH), FULL)
    r.qkv_bias[0:1, 2 * WIDTH : 3 * WIDTH] = vector(1)
    for move in moves_b[2:6]:
        move()

    def first_row(source):
        code = jnp.where(r.rank[pl.ds(source, 1), :] >= 0.0, r.code[pl.ds(source, 1), :], 0.0)
        at_first = iota((PAD, TOKENS), 1) == iota((PAD, TOKENS), 0) * LONG
        found = jnp.sum(jnp.where(at_first, code, 0.0), axis=1, keepdims=True)
        row = found - jnp.floor(found * (1.0 / 2048)) * 2048.0 - 1.0
        r.found[GROUPS, pl.ds(pl.multiple_of(source * PAD, 16), PAD), 0:1] = row

    every(0, DEVICES, first_row)
    for group in range(GROUPS + 1):
        named = as_row(r.found[group, :, 0:1])
        by_row = iota((VOCAB_ROWS, SLOT_ROWS), 0).astype(FULL) == named
        r.by_row[:, group * SLOT_ROWS : (group + 1) * SLOT_ROWS] = by_row.astype(LOW)

    def order(tile):
        at = pl.ds(pl.multiple_of(tile * BLOCK, BLOCK), BLOCK)
        lanes = iota((BLOCK, GROUPS * SLOT_ROWS), 1).astype(FULL)
        r.qkv[at, 0 : GROUPS * SLOT_ROWS] = (r.slot_col[at, :] == lanes).astype(LOW)

    every(0, TOKENS // BLOCK, order)
    for group in range(GROUPS):
        slot_at = iota((SLOT_ROWS, TOKENS), 0) + group * SLOT_ROWS
        named = (slot_at.astype(FULL) == r.slot_line[0:1, :]).astype(LOW)
        r.chosen[group, :, 0:TOKENS] = named
    for move in moves_b[6:]:
        move()
    for quarter in range(4):
        rows_of(quarter).wait_recv()

    def embed(tile):
        at = pl.ds(pl.multiple_of(tile * BLOCK, BLOCK), BLOCK)
        replies = r.replies[:, :, at].reshape(GROUPS * SLOT_ROWS, BLOCK)
        r.embedded[:, at] = dot(r.qkv[:, 0 : GROUPS * SLOT_ROWS], replies).astype(LOW)

    every(0, WIDTH // BLOCK, embed)
    moves_c[0]()
    finish_a()
    moves_c[1]()

    def project(tile):
        at = pl.ds(pl.multiple_of(tile * BLOCK, BLOCK), BLOCK)
        r.qkv[:, at] = (dot(r.embedded[...], r.wa[:, at]) + r.qkv_bias[0:1, at]).astype(LOW)

    every(3, 6, project)
    moves_c[2]()
    every(6, 9, project)
    moves_c[3]()

    row_sent = iota((PAIR_ROWS, WIDTH), 0) % PAD
    row_head = iota((PAIR_ROWS, WIDTH), 0) // PAD
    lane_block = iota((PAIR_ROWS, WIDTH), 1) // HEAD
    in_head = row_head == lane_block
    seen = (row_sent == lane_block) & (r.valid_line[0:1, :] > 0.0)
    firsts = (iota((PAD, TOKENS), 1) == iota((PAD, TOKENS), 0) * LONG).astype(LOW)
    real_row = iota((PAD, 1), 0) < sentences

    def spread(rows):
        return jnp.where(in_head, jnp.concatenate([rows] * HEADS, axis=0), jnp.zeros((), LOW))

    def fold(tall):
        tall = jnp.where(in_head, tall, 0.0)
        return sum(tall[head * PAD : (head + 1) * PAD] for head in range(HEADS))

    keys, values = slice(WIDTH, 2 * WIDTH), slice(2 * WIDTH, 3 * WIDTH)
    embedded_cls = dot(firsts, r.embedded[...]).astype(LOW)
    query_cls = (dot(embedded_cls, r.wa[:, 0:WIDTH]) + vector(0)).astype(LOW)
    cls_scores = dot_turned(spread(query_cls), r.qkv[:, keys]) * scale
    cls_scores = jnp.where(seen, cls_scores, MASK_FLOOR)
    cls_peak = jnp.max(cls_scores, axis=1, keepdims=True)
    cls_exp = jnp.where(seen, jnp.exp(cls_scores - cls_peak), 0.0)
    cls_total = jnp.sum(cls_exp, axis=1, keepdims=True)
    cls_probs = cls_exp / jnp.where(cls_total > 0.0, cls_total, 1.0)
    probs_low = cls_probs.astype(LOW)
    r.probs[...] = cls_probs
    context_cls = fold(dot(probs_low, r.qkv[:, values])).astype(LOW)
    moves_c[4]()
    first_cls = (
        embedded_cls.astype(FULL)
        + dot(context_cls, r.wa[:, 3 * WIDTH : 4 * WIDTH])
        + vector(2)
    )
    normed_one, inverse_one = norm_parts(first_cls)
    r.normed_one[...] = normed_one
    hidden_cls = normed_one * vector(3) + vector(4)
    hidden_cls_low = hidden_cls.astype(LOW)
    early_here = r.early.at[here]
    early_here[:, 0:WIDTH] = hidden_cls_low
    early_here[:, WIDTH : 2 * WIDTH] = query_cls
    steps_u, drain_u = gather_steps(r.units, r.gather_send.at[0], r.gather_recv.at[0])
    steps_e, drain_e = gather_steps(r.early, r.gather_send.at[1], r.gather_recv.at[1])
    steps_d, drain_d = gather_steps(r.downs, r.gather_send.at[2], r.gather_recv.at[2])
    steps_a, drain_a2 = gather_steps(r.attends, r.gather_send.at[3], r.gather_recv.at[3])
    steps_q, drain_q = gather_steps(r.queries, r.gather_send.at[4], r.gather_recv.at[4])
    steps_e[0]()
    moves_c[5]()

    def attend(unit):
        rows = pl.ds(pl.multiple_of(unit * half_block, half_block), half_block)
        lane_head = iota((half_block, BLOCK), 1) // HEAD
        bias = r.block_bias[...] + r.valid_bias[0:1, rows]

        def part(which, lane):
            return r.qkv[rows, which * WIDTH + lane : which * WIDTH + lane + BLOCK]

        for lane in range(0, WIDTH, BLOCK):
            query = part(0, lane) * jnp.asarray(scale, LOW)
            key, value = part(1, lane), part(2, lane)
            stacked = jnp.concatenate(
                [jnp.where(lane_head == head, query, jnp.zeros((), LOW)) for head in range(4)],
                axis=0,
            )
            scores = dot_turned(stacked, key) + bias
            shifted = jnp.exp(scores - jnp.max(scores, axis=1, keepdims=True))
            probs = shifted * (1.0 / jnp.sum(shifted, axis=1, keepdims=True))
            mixed = dot(probs.astype(LOW), value)
            result = mixed[0:half_block]
            for head in range(1, 4):
                result = jnp.where(
                    lane_head == head, mixed[head * half_block : (head + 1) * half_block], result
                )
            r.context[rows, lane : lane + BLOCK] = result.astype(LOW)

    def open_tile(tile):
        at = pl.ds(tile * BLOCK, BLOCK)
        attended = dot(r.context[at, :], r.wa[:, 3 * WIDTH : 4 * WIDTH]) + vector(2)
        normed, _ = norm_parts(r.embedded[at, :].astype(FULL) + attended)
        hidden = normed * vector(3) + vector(4)
        r.tile_low[...] = hidden.astype(LOW)
        r.tile_sum[...] = hidden + vector(5)

    feed = 2 * BLOCK
    feeds = WIDE // feed

    def feed_at(part):
        return pl.ds(pl.multiple_of(part * feed, feed), feed)

    def feed_up(part):
        r.tile_up[...] = dot(r.tile_low[...], r.wb[:, feed_at(part)]) + r.up_bias[0:1, feed_at(part)]

    def feed_gelu():
        r.tile_active[...] = gelu(r.tile_up[...]).astype(LOW)

    def feed_down(part):
        r.tile_sum[...] += dot(r.tile_active[...], r.wc[feed_at(part), :])

    def feed_tile(part):
        down = dot(r.tile_active[...], r.wc[feed_at(part), :])
        active = gelu(r.tile_up[...]).astype(LOW)
        up = dot(r.tile_low[...], r.wb[:, feed_at(part + 2)]) + r.up_bias[0:1, feed_at(part + 2)]
        r.tile_sum[...] += down
        r.tile_active[...] = active
        r.tile_up[...] = up

    def feed_open():
        feed_up(0)
        feed_gelu()
        feed_up(1)

    def feed_close():
        feed_down(feeds - 2)
        feed_gelu()
        feed_down(feeds - 1)

    def layer_copy(tile):
        at = pl.ds(tile * BLOCK, BLOCK)
        return pltpu.make_async_copy(r.context.at[at], r.layer_out.at[at], r.out_sem.at[tile])

    def close_tile(tile):
        at = pl.ds(tile * BLOCK, BLOCK)
        normed, _ = norm_parts(r.tile_sum[...])
        out = normed * vector(6) + vector(7)
        r.context[at, :] = (out * r.valid_col[at, :]).astype(LOW)
        layer_copy(tile).start()

    queue = [partial(every, 0, 3, project)]
    queue += [partial(every, unit, unit + 1, attend) for unit in range(6)]
    late = []
    for tile in range(TOKENS // BLOCK):
        late += [partial(open_tile, tile), feed_open]
        late += [partial(every, part, part + 1, feed_tile) for part in range(feeds - 2)]
        late += [feed_close, partial(close_tile, tile)]

    def fill(pieces, count):
        for _ in range(min(count, len(pieces))):
            pieces.pop(0)()

    finish_b()
    up_cls = dot(hidden_cls_low, r.wb[...]) + r.up_bias[0:1, :]
    activated_cls, slope_cls = gelu_parts(up_cls)
    activated_low = activated_cls.astype(LOW)
    steps_e[1]()
    fill(queue, 1)
    for move in moves_c[6:]:
        fill(queue, 1)
        move()
    fill(queue, len(queue))

    def pack_tall(tall, target, first_row):
        for at in range(CHIPS):
            columns = tall[:, at * depth : (at + 1) * depth]
            for half in range(CORES):
                base = half * PAIR_ROWS // 2
                target[half * CHIPS + at, first_row : first_row + 48, :] = jnp.concatenate(
                    [
                        columns[base : base + 48],
                        columns[base + 48 : base + 96],
                        jnp.zeros((48, 128 - 2 * depth), FULL),
                    ],
                    axis=1,
                ).astype(LOW)

    def pack_coefs(coefs):
        shape = (PAIR_ROWS, GROUPS * 128)
        folds = iota(shape, 0) // PAD + iota(shape, 1) // 128 * PAD == iota(shape, 1) % 128
        lanes = contract(coefs, folds.astype(LOW), 0, 0).astype(LOW)
        total = None
        for group in range(GROUPS):
            part = dot(r.chosen[group, :, 0:TOKENS], lanes[:, group * 128 : (group + 1) * 128])
            total = part if total is None else total + part
        return total.astype(LOW).reshape(DEVICES, PAD, 128)

    finish_c()
    down_pre = dot(activated_low, r.wc[...]) + vector(5)
    normed_two, inverse_two = norm_parts(hidden_cls + down_pre)
    summary = normed_two * vector(6) + vector(7)
    magnitude = jnp.sqrt(jnp.sum(summary * summary, axis=-1, keepdims=True) + EPSILON)
    unit = jnp.where(real_row, summary / magnitude, 0.0)
    r.units[here] = unit.astype(LOW)

    steps_u[0]()
    for at in range(CHIPS):
        cut = slice(at * depth, (at + 1) * depth)
        line = jnp.concatenate(
            [
                context_cls.astype(FULL)[:, cut],
                embedded_cls.astype(FULL)[:, cut],
                jnp.zeros((PAD, 128 - 2 * depth), FULL),
            ],
            axis=1,
        ).astype(LOW)
        for half in range(CORES):
            r.mail_one[half * CHIPS + at, 0:PAD, :] = line
    steps_u[1]()
    pack_tall(dot(probs_low, r.embedded[...]), r.mail_one, PAD)
    fill(late, 1)
    steps_u[2]()
    steps_e[2]()
    r.mail_one[:, 64:80, :] = pack_coefs(probs_low)
    fill(late, 1)
    steps_u[3]()
    fill(late, 2)

    def post(box, got, index):
        def send(step):
            other, to_core, to_chip = peer(step)
            remote(
                box.at[other], got.at[me], r.one_send.at[index], r.one_recv.at[index], to_core, to_chip
            ).start()

        every(1, DEVICES, send)
        got[me] = box[me]

    steps_u[4]()
    fill(late, 1)
    steps_u[5]()
    post(r.mail_one, r.got_one, 1)
    steps_e[3]()

    units = r.units[...].reshape(SLOT_ROWS, WIDTH)
    weight_row, pair_row, side_row = r.pairs[0:1, :], r.pairs[1:2, :], r.pairs[2:3, :]

    def pair_scores(rows, pair_col, side_col):
        opposite = side_col + side_row == 1.0
        partner = opposite & (pair_col == pair_row)
        raw = SCORE_SCALE * dot_turned(rows, units)
        shifted = jnp.where(partner, raw - SCORE_SCALE * MARGIN_WIDTH, raw)
        return jnp.where(opposite, shifted, MASK_FLOOR), partner

    every_score, every_partner = pair_scores(
        units, r.pairs_col[:, 1:2], r.pairs_col[:, 2:3]
    )
    peak_row = jnp.max(every_score, axis=0, keepdims=True)
    log_row = peak_row + jnp.log(
        jnp.sum(jnp.exp(every_score - peak_row), axis=0, keepdims=True)
    )
    picked_row = jnp.sum(jnp.where(every_partner, every_score, 0.0), axis=0, keepdims=True)
    r.loss[...] = jnp.sum(weight_row * (log_row - picked_row), axis=1, keepdims=True)

    rows_here = pl.ds(pl.multiple_of(me * PAD, 16), PAD)
    own_score, own_partner = pair_scores(
        r.units[here], r.pairs_col[rows_here, 1:2], r.pairs_col[rows_here, 2:3]
    )
    own_partner = own_partner.astype(FULL)
    own_peak = jnp.max(own_score, axis=1, keepdims=True)
    own_exp = jnp.exp(own_score - own_peak)
    own_share = own_exp / jnp.sum(own_exp, axis=1, keepdims=True)
    by_row = (r.pairs_col[rows_here, 0:1] * (own_share - own_partner)).astype(LOW)
    by_column = (weight_row * (jnp.exp(own_score - log_row) - own_partner)).astype(LOW)
    unit_grad = SCORE_SCALE * (dot(by_row, units) + dot(by_column, units))
    along = jnp.sum(unit * unit_grad, axis=-1, keepdims=True)
    summary_grad = (unit_grad - unit * along) / magnitude

    residual_grad, grad_g2, grad_s2 = norm_back_parts(
        summary_grad, normed_two, inverse_two, vector(6)
    )
    down_grad = residual_grad.astype(LOW)
    r.downs[here] = down_grad
    steps_d[0]()
    act_grad = dot_turned(down_grad, r.wc[...])
    up_grad = (act_grad * slope_cls).astype(LOW)
    steps_d[1]()
    hidden_grad = dot_turned(up_grad, r.wb[...]) + residual_grad
    first_grad, grad_g1, grad_s1 = norm_back_parts(
        hidden_grad, r.normed_one[...], inverse_one, vector(3)
    )
    attend_grad = first_grad.astype(LOW)
    steps_e[4]()
    context_grad = dot_turned(attend_grad, r.wa[:, 3 * WIDTH : 4 * WIDTH]).astype(LOW)
    attend_here = r.attends.at[here]
    attend_here[:, 0:WIDTH] = attend_grad
    attend_here[:, WIDTH : 2 * WIDTH] = context_grad
    steps_a[0]()
    steps_d[2]()
    context_tall = spread(context_grad)
    probs = r.probs[...]
    prob_grad = dot_turned(context_tall, r.qkv[:, values])
    inner = jnp.sum(probs * prob_grad, axis=1, keepdims=True)
    score_grad = (probs * (prob_grad - inner)).astype(LOW)
    steps_a[1]()
    r.mail_three[...] = pack_coefs(score_grad)
    post(r.mail_three, r.got_three, 3)
    query_grad = (fold(dot(score_grad, r.qkv[:, keys])) * scale).astype(LOW)
    probs_total = jnp.sum(probs_low.astype(FULL), axis=1, keepdims=True)
    grad_bvalue = jnp.sum(probs_total * context_tall.astype(FULL), axis=0, keepdims=True)
    grad_bquery = jnp.sum(query_grad.astype(FULL), axis=0, keepdims=True)
    query_here = r.queries.at[here]
    query_here[:, 0:WIDTH] = query_grad
    query_here[:, WIDTH : 2 * WIDTH] = jnp.concatenate(
        [grad_bquery, grad_bvalue, grad_g1, grad_s1, grad_g2, grad_s2, jnp.zeros((10, WIDTH))],
        axis=0,
    ).astype(LOW)
    steps_q[0]()
    steps_a[2]()
    pack_tall(dot(score_grad, r.embedded[...]) * scale, r.mail_two, 0)
    steps_q[1]()
    post(r.mail_two, r.got_two, 2)

    def all_rows(buffer, start):
        return buffer[:, :, :, :, start : start + WIDTH].reshape(SLOT_ROWS, WIDTH)

    def from_sent(group):
        lanes = iota((SLOT_ROWS, SLOT_ROWS), 1).astype(FULL)
        return (r.found[group, :, 1:2] == lanes).astype(LOW)

    def widened(coefs, group):
        lanes = iota((128, WIDTH), 0) == iota((128, WIDTH), 1) // HEAD + group * PAD
        return dot(coefs, lanes.astype(LOW))

    half_wide = WIDE // 2

    def slope_tile(part):
        at = pl.ds(pl.multiple_of(core * half_wide + part * BLOCK, BLOCK), BLOCK)
        up_pre = dot(all_rows(r.early, 0), r.wb[:, at]) + r.up_bias[0:1, at]
        _, slope = gelu_parts(up_pre)
        r.slopes[:, pl.ds(pl.multiple_of(part * BLOCK, BLOCK), BLOCK)] = slope.astype(LOW)

    def slot_queries(group):
        r.slot_query[group] = dot(from_sent(group), all_rows(r.early, WIDTH)).astype(LOW)

    def activate():
        at = pl.ds(pl.multiple_of(chip // 2 * 2 * deep, 128), 2 * deep)
        up_pre = dot(all_rows(r.early, 0), r.wb[:, at]) + r.up_bias[0:1, at]
        r.active_turned[...] = jnp.transpose(gelu(up_pre)).astype(LOW)
        r.hidden_turned[...] = jnp.transpose(all_rows(r.early, 0))

    steps_e[5]()
    between = [partial(slot_queries, group) for group in range(GROUPS)]
    between += [partial(every, part, part + 1, slope_tile) for part in range(6)]
    between.append(activate)

    between += late
    late.clear()
    rest = [steps_d[3], steps_a[3], steps_q[2], steps_d[4], steps_a[4], steps_q[3]]
    rest += [steps_d[5], steps_a[5], steps_q[4]]
    for step in rest:
        step()
        fill(between, 2)
    fill(between, len(between))

    all_but_one(r.got_one, 1).wait_recv()
    got_probs = r.got_one[:, 64:80, :].reshape(SLOT_ROWS, 128)
    for group in range(GROUPS):
        slot_context = dot(from_sent(group), all_rows(r.attends, WIDTH))
        r.replies[group] = (widened(got_probs, group) * slot_context).astype(LOW)

    def head_products(got, first_row, right, start, target):
        for pair in range(HEADS // 4):
            lane = pl.ds(pl.multiple_of(start + (core * (HEADS // 4) + pair) * 128, 128), 128)
            pair_rows = right[:, :, :, :, lane].reshape(SLOT_ROWS, 128)
            parts = []
            for half in range(2):
                head = 2 * pair + half
                row = first_row + head % 3 * PAD
                block_rows = got[:, row : row + PAD, :].reshape(SLOT_ROWS, 128)
                product = contract(block_rows, pair_rows, 0, 0)
                column = head // 3 * depth
                parts.append(product[column : column + depth, :])
            low_lanes = iota((depth, 128), 1) < HEAD
            result = jnp.where(low_lanes, parts[0], parts[1])
            target[:, pl.ds(pl.multiple_of((core * (HEADS // 4) + pair) * 128, 128), 128)] = result

    def half_of(ref, at_core):
        half = ref.shape[1] // 2
        return ref.at[:, pl.ds(pl.multiple_of(at_core * half, 128), half)]

    def half_copy(index, ref, at_core):
        part = half_of(ref, at_core)
        return remote(part, part, r.half_send.at[index], r.half_recv.at[index], 1 - core, chip)

    head_products(r.got_one, PAD, r.attends, WIDTH, r.g_wv)
    half_copy(0, r.g_wv, core).start()

    downs = r.downs[...].reshape(SLOT_ROWS, WIDTH)
    attends = all_rows(r.attends, 0)

    def up_tile(part):
        at = pl.ds(pl.multiple_of(core * half_wide + part * BLOCK, BLOCK), BLOCK)
        slope = r.slopes[:, pl.ds(pl.multiple_of(part * BLOCK, BLOCK), BLOCK)].astype(FULL)
        up_all = (dot_turned(r.downs[...].reshape(SLOT_ROWS, WIDTH), r.wc[at, :]) * slope)
        up_all = up_all.astype(LOW)
        r.g_wup[0:depth, at] = dot(r.hidden_turned[mine, :], up_all)
        total = jnp.sum(up_all.astype(FULL), axis=0, keepdims=True)
        r.g_wup[depth : depth + 8, at] = jnp.broadcast_to(total, (8, BLOCK))

    every(0, half_wide // BLOCK, up_tile)
    half_copy(1, r.g_wup, core).start()
    r.g_wdown[...] = dot(r.active_turned[pl.ds(pl.multiple_of(chip % 2 * deep, 16), deep), :], downs)
    r.left_turned[...] = jnp.transpose(r.got_one[:, 0:PAD, :].reshape(SLOT_ROWS, 128))
    r.g_wo[...] = dot(r.left_turned[0:depth, :], attends)
    own_lanes = (iota((WIDTH, 128), 0) == chip * depth + iota((WIDTH, 128), 1)).astype(LOW)

    def own_part(rows, select):
        total = None
        for _ in range(3):
            part = rows.astype(LOW)
            rows = rows - part.astype(FULL)
            picked = dot(part, select)
            total = picked if total is None else total + picked
        return total

    for quarter in range(4):
        rows_of(quarter).wait_send()
    all_but_one(r.got_three, 3).wait_recv()
    got_scores = r.got_three[...].reshape(SLOT_ROWS, 128)
    for group in range(GROUPS):
        slot_query = r.slot_query[group].astype(FULL)
        key_grad = (widened(got_scores, group) * slot_query * scale).astype(LOW)
        row_grad = dot_turned(key_grad, r.wa[:, keys])
        row_grad = row_grad + dot_turned(r.replies[group], r.wa[:, values])
        r.rows[group] = row_grad.astype(LOW)
    steps_q[5]()
    query_grads = all_rows(r.queries, 0)
    extra = dot_turned(query_grads, r.wa[:, 0:WIDTH]) + attends.astype(FULL)
    r.extra[...] = extra.astype(LOW)
    r.g_wq[...] = dot(r.left_turned[depth : 2 * depth, :], query_grads)

    half_rows = VOCAB_ROWS // 2

    def table_copy(tile):
        at = pl.ds(pl.multiple_of(tile * half_rows, BLOCK), half_rows)
        return pltpu.make_async_copy(
            r.table_full.at[at], r.table_grad.at[at], r.table_sem.at[tile]
        )

    def table_tile(tile):
        at = pl.ds(pl.multiple_of(tile * half_rows, BLOCK), half_rows)
        for start in range(0, WIDTH, BLOCK):
            lanes = slice(start, start + BLOCK)
            slot_rows = r.rows[:, :, lanes].reshape(GROUPS * SLOT_ROWS, BLOCK)
            r.table_full[at, lanes] = dot(r.by_row[at, 0 : GROUPS * SLOT_ROWS], slot_rows) + dot(
                r.by_row[at, GROUPS * SLOT_ROWS :], r.extra[:, lanes]
            )
        table_copy(tile).start()

    every(0, 2, table_tile)
    all_but_one(r.got_two, 2).wait_recv()
    head_products(r.got_two, 0, r.early, WIDTH, r.g_wk)
    half_copy(2, r.g_wk, core).start()

    down_total = jnp.sum(downs.astype(FULL), axis=0, keepdims=True)
    attend_total = jnp.sum(attends.astype(FULL), axis=0, keepdims=True)
    device_sums = (iota((PAD, SLOT_ROWS), 1) % PAD == iota((PAD, SLOT_ROWS), 0)).astype(LOW)
    sums = dot(device_sums, all_rows(r.queries, WIDTH))
    stacked = jnp.concatenate(
        [sums[0:6], attend_total, down_total, jnp.zeros((8, WIDTH), FULL)], axis=0
    )
    r.g_small[0:16, 0:128] = own_part(stacked, own_lanes)
    r.g_small[0:16, 128:BLOCK] = jnp.zeros((PAD, BLOCK - 128), FULL)
    half_copy(1, r.g_wup, 1 - core).wait_recv()
    up_lanes = (iota((WIDE, BLOCK), 0) == chip * deep + iota((WIDE, BLOCK), 1)).astype(LOW)
    r.g_small[16:24, :] = own_part(r.g_wup[depth : depth + 8, :], up_lanes)

    half_copy(0, r.g_wv, 1 - core).wait_recv()
    half_copy(2, r.g_wk, 1 - core).wait_recv()
    for index, ref in enumerate([r.g_wv, r.g_wup, r.g_wk]):
        half_copy(index, ref, core).wait_send()

    for index, ref in enumerate([r.every_ids, r.got_one, r.got_two, r.got_three]):
        all_but_one(ref, index).wait_send()
    all_smalls().wait_send()
    for end in [drain_a, drain_b, drain_c, drain_u, drain_e, drain_d, drain_a2, drain_q]:
        end()
    for tile in range(TOKENS // BLOCK):
        layer_copy(tile).wait()
    every(0, 2, lambda tile: table_copy(tile).wait())


def layer(inputs):
    dma = pltpu.SemaphoreType.DMA
    vmem = pl.BlockSpec(memory_space=pltpu.VMEM)
    anywhere = pl.BlockSpec(memory_space=pl.ANY)
    depth, deep = WIDTH // CHIPS, WIDE // CHIPS

    def gathered(width):
        return pltpu.VMEM((CORES, PLANES, LINES, PAD, width), LOW)

    outputs = dict(
        layer_out=((TOKENS, WIDTH), LOW),
        table_grad=((VOCAB_ROWS, WIDTH), FULL),
        g_wq=((depth, WIDTH), FULL),
        g_wk=((depth, WIDTH), FULL),
        g_wv=((depth, WIDTH), FULL),
        g_wo=((depth, WIDTH), FULL),
        g_wup=((depth + 8, WIDE), FULL),
        g_wdown=((deep, WIDTH), FULL),
        g_small=((24, BLOCK), FULL),
        loss=((1, 1), FULL),
    )
    scratch = dict(
        ids=pltpu.VMEM((8, 128), jnp.int32),
        every_ids=pltpu.VMEM((DEVICES, 8, 128), jnp.int32),
        rank=pltpu.VMEM((DEVICES, TOKENS), FULL),
        code=pltpu.VMEM((DEVICES, TOKENS), FULL),
        found=pltpu.VMEM((GROUPS + 1, SLOT_ROWS, 2), FULL),
        block_bias=pltpu.VMEM((2 * BLOCK, BLOCK // 2), FULL),
        valid_bias=pltpu.VMEM((8, TOKENS), FULL),
        slot_col=pltpu.VMEM((TOKENS, 1), FULL),
        slot_line=pltpu.VMEM((8, TOKENS), FULL),
        valid_col=pltpu.VMEM((TOKENS, 1), FULL),
        valid_line=pltpu.VMEM((8, TOKENS), FULL),
        pairs=pltpu.VMEM((8, SLOT_ROWS), FULL),
        pairs_col=pltpu.VMEM((SLOT_ROWS, 128), FULL),
        vectors=pltpu.VMEM((PAD, WIDTH), FULL),
        up_bias=pltpu.VMEM((8, WIDE), FULL),
        qkv_bias=pltpu.VMEM((8, 3 * WIDTH), FULL),
        smalls=pltpu.VMEM((PAD, CHIPS * 128), LOW),
        wa=pltpu.VMEM((WIDTH, 4 * WIDTH), LOW),
        wb=pltpu.VMEM((WIDTH, WIDE), LOW),
        wc=pltpu.VMEM((WIDE, WIDTH), LOW),
        chosen=pltpu.VMEM((GROUPS, SLOT_ROWS, VOCAB_ROWS), LOW),
        by_row=pltpu.VMEM((VOCAB_ROWS, (GROUPS + 1) * SLOT_ROWS), LOW),
        rows=pltpu.VMEM((GROUPS, SLOT_ROWS, WIDTH), LOW),
        replies=pltpu.VMEM((GROUPS, SLOT_ROWS, WIDTH), LOW),
        slot_query=pltpu.VMEM((GROUPS, SLOT_ROWS, WIDTH), LOW),
        extra=pltpu.VMEM((SLOT_ROWS, WIDTH), LOW),
        embedded=pltpu.VMEM((TOKENS, WIDTH), LOW),
        qkv=pltpu.VMEM((TOKENS, 3 * WIDTH), LOW),
        context=pltpu.VMEM((TOKENS, WIDTH), LOW),
        tile_low=pltpu.VMEM((BLOCK, WIDTH), LOW),
        tile_up=pltpu.VMEM((BLOCK, 2 * BLOCK), FULL),
        tile_active=pltpu.VMEM((BLOCK, 2 * BLOCK), LOW),
        tile_sum=pltpu.VMEM((BLOCK, WIDTH), FULL),
        table_full=pltpu.VMEM((VOCAB_ROWS, WIDTH), FULL),
        probs=pltpu.VMEM((PAIR_ROWS, TOKENS), FULL),
        normed_one=pltpu.VMEM((PAD, WIDTH), FULL),
        units=gathered(WIDTH),
        early=gathered(2 * WIDTH),
        downs=gathered(WIDTH),
        attends=gathered(2 * WIDTH),
        queries=gathered(2 * WIDTH),
        slopes=pltpu.VMEM((SLOT_ROWS, WIDE // 2), LOW),
        hidden_turned=pltpu.VMEM((WIDTH, SLOT_ROWS), LOW),
        active_turned=pltpu.VMEM((2 * deep, SLOT_ROWS), LOW),
        left_turned=pltpu.VMEM((128, SLOT_ROWS), LOW),
        mail_one=pltpu.VMEM((DEVICES, 80, 128), LOW),
        got_one=pltpu.VMEM((DEVICES, 80, 128), LOW),
        mail_two=pltpu.VMEM((DEVICES, 48, 128), LOW),
        got_two=pltpu.VMEM((DEVICES, 48, 128), LOW),
        mail_three=pltpu.VMEM((DEVICES, PAD, 128), LOW),
        got_three=pltpu.VMEM((DEVICES, PAD, 128), LOW),
        rows_send=dma((4,)),
        rows_recv=dma((4,)),
        one_send=dma((4,)),
        one_recv=dma((4,)),
        small_send=dma((1,)),
        small_recv=dma((1,)),
        weight_send=dma((3, 33)),
        weight_recv=dma((3, 33)),
        gather_send=dma((5, 13)),
        gather_recv=dma((5, 13)),
        half_send=dma((3,)),
        half_recv=dma((3,)),
        out_sem=dma((TOKENS // BLOCK,)),
        table_sem=dma((2,)),
    )
    names = INPUTS + OUTPUTS + list(scratch)
    return pl.pallas_call(
        partial(layer_kernel, names),
        out_shape=tuple(jax.ShapeDtypeStruct(*outputs[name]) for name in OUTPUTS),
        in_specs=[vmem] * len(INPUTS),
        out_specs=(anywhere, anywhere) + (vmem,) * (len(OUTPUTS) - 2),
        scratch_shapes=list(scratch.values()),
        compiler_params=pltpu.CompilerParams(
            collective_id=0, has_side_effects=True, vmem_limit_bytes=VMEM_LIMIT
        ),
        name="layer",
    )(*inputs)


def finish_kernel(count, *refs):
    large, (small, loss), outs = refs[:count], refs[count : count + 2], refs[count + 2 : 2 * count + 12]
    held, load_sems, store_sems = refs[2 * count + 12 : -2], refs[-2], refs[-1]
    pieces = []
    for index, (source, target) in enumerate(zip(large, outs)):
        rows = target.shape[0]
        step = BLOCK if rows > BLOCK else rows
        for start in range(0, rows, step):
            at = pl.ds(start, step)
            slot = len(pieces)
            pieces.append(
                (
                    pltpu.make_async_copy(source.at[at], held[index].at[at], load_sems.at[slot]),
                    pltpu.make_async_copy(held[index].at[at], target.at[at], store_sems.at[slot]),
                )
            )
    for load, _ in pieces:
        load.start()
    for row, target in zip([0, 1, 6, 2, 3, 16, 7, 4, 5], outs[count : count + 9]):
        size = target.shape[0]
        target[...] = small[row : row + 1, 0:size].reshape(size)
    outs[-1][...] = loss[...].reshape(1)
    for load, store in pieces:
        load.wait()
        store.start()
    for _, store in pieces:
        store.wait()


def finish(results):
    vmem = pl.BlockSpec(memory_space=pltpu.VMEM)
    anywhere = pl.BlockSpec(memory_space=pl.ANY)
    depth, deep = WIDTH // CHIPS, WIDE // CHIPS
    count = len(results) - 2
    shapes = [(one.shape, one.dtype) for one in results[:count]]
    shapes[6] = ((depth, WIDE), FULL)
    held = [pltpu.VMEM(*one) for one in shapes]
    shapes += [((depth,), FULL)] * 5 + [((deep,), FULL)] + [((depth,), FULL)] * 3
    shapes.append(((1,), FULL))
    dma = pltpu.SemaphoreType.DMA((16,))
    return pl.pallas_call(
        partial(finish_kernel, count),
        out_shape=tuple(jax.ShapeDtypeStruct(*one) for one in shapes),
        in_specs=[anywhere] * count + [vmem] * 2,
        out_specs=(anywhere,) * count + (vmem,) * 10,
        scratch_shapes=held + [dma, dma],
        compiler_params=pltpu.CompilerParams(vmem_limit_bytes=VMEM_LIMIT),
        name="finish",
    )(*results)


def block_body(
    table,
    token_ids,
    sent_lengths,
    pair_slot,
    pair_lang,
    *parameters,
):
    results = finish(layer((table, token_ids, sent_lengths, pair_slot, pair_lang) + parameters))
    layer_out, table_grad, g_wq, g_wk, g_wv, g_wo, g_wup, g_wdown = results[:8]
    g_bq, g_bv, g_bo, g_g1, g_s1, g_bup, g_bdown, g_g2, g_s2, loss = results[8:]
    return (
        layer_out.reshape(token_ids.shape + (WIDTH,)),
        loss.reshape(()),
        table_grad,
        g_wq,
        g_bq,
        g_wk,
        g_wv,
        g_bv,
        g_wo,
        g_bo,
        g_g1,
        g_s1,
        g_wup,
        g_bup,
        g_wdown,
        g_bdown,
        g_g2,
        g_s2,
    )


def solution(mesh):
    in_specs = (
        P(("dp", "fsdp"), None),
        P(("dp", "fsdp"), None),
        P(("dp", "fsdp")),
        P(),
        P(),
        P("fsdp", None),
        P("fsdp"),
        P("fsdp", None),
        P("fsdp", None),
        P("fsdp"),
        P("fsdp", None),
        P("fsdp"),
        P("fsdp"),
        P("fsdp"),
        P("fsdp", None),
        P("fsdp"),
        P("fsdp", None),
        P("fsdp"),
        P("fsdp"),
        P("fsdp"),
    )
    out_specs = (
        P(("dp", "fsdp"), None, None),
        P(),
        P(("dp", "fsdp"), None),
        P("fsdp", None),
        P("fsdp"),
        P("fsdp", None),
        P("fsdp", None),
        P("fsdp"),
        P("fsdp", None),
        P("fsdp"),
        P("fsdp"),
        P("fsdp"),
        P("fsdp", None),
        P("fsdp"),
        P("fsdp", None),
        P("fsdp"),
        P("fsdp"),
        P("fsdp"),
    )
    sizes = dict(mesh.shape)
    body = general_body
    if sizes["dp"] == CORES and sizes["fsdp"] == CHIPS:
        body = block_body
    return jax.shard_map(body, mesh=mesh, in_specs=in_specs, out_specs=out_specs, check_vma=False)
```

```python
from functools import partial
from types import SimpleNamespace

import jax
import jax.numpy as jnp
from jax import lax
from jax.experimental import pallas as pl
from jax.experimental.pallas import tpu as pltpu
from jax.sharding import PartitionSpec as P

HEADS = 12
HEAD = 64
LANGS = 109


EPSILON = 1e-06
SCORE_SCALE = 50.0
MARGIN_WIDTH = 0.3
MASK_FLOOR = -1000000000.0


def contract(left_side, right_side, left_dim, right_dim):
    return lax.dot_general(
        left_side,
        right_side,
        (((left_dim,), (right_dim,)), ((), ())),
        preferred_element_type=jnp.float32,
    )


def norm_rows(inputs, ln_gain, ln_shift):
    row_mean = jnp.mean(inputs, axis=-1, keepdims=True)
    centered = inputs - row_mean
    variance = jnp.mean(centered * centered, axis=-1, keepdims=True)
    inverse = lax.rsqrt(variance + EPSILON)
    normed = centered * inverse
    return (normed * ln_gain + ln_shift, normed, inverse)


def norm_back(grad_output, normed, inverse, ln_gain):
    grad_normed = grad_output * ln_gain
    first_term = jnp.mean(grad_normed, axis=-1, keepdims=True)
    second_term = jnp.mean(grad_normed * normed, axis=-1, keepdims=True)
    grad_input = inverse * (grad_normed - first_term - normed * second_term)
    return (grad_input, jnp.sum(grad_output * normed, axis=0), jnp.sum(grad_output, axis=0))


def general_body(
    table,
    token_ids,
    sent_lengths,
    pair_slot,
    pair_lang,
    w_query,
    b_query,
    w_key,
    w_value,
    b_value,
    w_out,
    b_out,
    ln1_gain,
    ln1_bias,
    w_up,
    b_up,
    w_down,
    b_down,
    ln2_gain,
    ln2_bias,
):
    sentences, length = token_ids.shape
    tokens = sentences * length
    vocab_rows, model_width = table.shape
    owners = lax.axis_size(("dp", "fsdp"))
    dp_count = lax.axis_size("dp")
    fsdp_count = lax.axis_size("fsdp")
    capacity = max(2, 2 * tokens // owners)
    device = lax.axis_index(("dp", "fsdp"))
    score_factor = HEAD ** (-0.5)
    flat_ids = token_ids.reshape(tokens)
    owner_of = flat_ids // vocab_rows
    member = (owner_of[:, None] == jnp.arange(owners, dtype=jnp.int32)[None, :]).astype(jnp.int32)
    owner_rank = jnp.sum(jnp.cumsum(member, axis=0) * member, axis=1) - 1
    slot_of = owner_of * capacity + owner_rank
    requests = jnp.full((owners * capacity,), -1, jnp.int32).at[slot_of].set(flat_ids)
    received = lax.all_to_all(
        lax.all_to_all(
            requests.reshape(dp_count, fsdp_count, capacity),
            "dp",
            split_axis=0,
            concat_axis=0,
            tiled=True,
        ),
        "fsdp",
        split_axis=1,
        concat_axis=1,
        tiled=True,
    )
    present = received >= 0
    local_rows = jnp.where(present, received - device * vocab_rows, 0)
    found_rows = jnp.where(present[..., None], table[local_rows], jnp.zeros((), table.dtype))
    replies = lax.all_to_all(
        lax.all_to_all(found_rows, "dp", split_axis=0, concat_axis=0, tiled=True),
        "fsdp",
        split_axis=1,
        concat_axis=1,
        tiled=True,
    )
    embedded = replies.reshape(owners * capacity, model_width)[slot_of]
    gathered = (
        lax.all_gather(w_query, "fsdp", axis=0, tiled=True),
        lax.all_gather(b_query, "fsdp", axis=0, tiled=True),
        lax.all_gather(w_key, "fsdp", axis=0, tiled=True),
        lax.all_gather(w_value, "fsdp", axis=0, tiled=True),
        lax.all_gather(b_value, "fsdp", axis=0, tiled=True),
        lax.all_gather(w_out, "fsdp", axis=0, tiled=True),
        lax.all_gather(b_out, "fsdp", axis=0, tiled=True),
        lax.all_gather(ln1_gain, "fsdp", axis=0, tiled=True),
        lax.all_gather(ln1_bias, "fsdp", axis=0, tiled=True),
        lax.all_gather(w_up, "fsdp", axis=0, tiled=True),
        lax.all_gather(b_up, "fsdp", axis=0, tiled=True),
        lax.all_gather(w_down, "fsdp", axis=0, tiled=True),
        lax.all_gather(b_down, "fsdp", axis=0, tiled=True),
        lax.all_gather(ln2_gain, "fsdp", axis=0, tiled=True),
        lax.all_gather(ln2_bias, "fsdp", axis=0, tiled=True),
    )
    (
        full_wq,
        full_bq,
        full_wk,
        full_wv,
        full_bv,
        full_wo,
        full_bo,
        full_g1,
        full_s1,
        full_wup,
        full_bup,
        full_wdown,
        full_bdown,
        full_g2,
        full_s2,
    ) = gathered
    valid_mask = jnp.arange(length, dtype=jnp.int32)[None, :] < sent_lengths[:, None]
    head_shape = (sentences, length, HEADS, HEAD)
    queries = (jnp.dot(embedded, full_wq, preferred_element_type=jnp.float32) + full_bq).astype(
        jnp.bfloat16
    )
    key_heads = (
        jnp.dot(embedded, full_wk, preferred_element_type=jnp.float32)
        .astype(jnp.bfloat16)
        .reshape(head_shape)
    )
    value_heads = (
        (jnp.dot(embedded, full_wv, preferred_element_type=jnp.float32) + full_bv)
        .astype(jnp.bfloat16)
        .reshape(head_shape)
    )
    query_heads = queries.reshape(head_shape)
    scores = (
        jnp.einsum("bqhd,bkhd->bhqk", query_heads, key_heads, preferred_element_type=jnp.float32)
        * score_factor
    )
    scores = jnp.where(valid_mask[:, None, None, :], scores, MASK_FLOOR)
    row_peak = jnp.max(scores, axis=-1, keepdims=True)
    shifted = jnp.exp(scores - row_peak)
    totals = jnp.sum(shifted, axis=-1, keepdims=True)
    attn_probs = (shifted / totals).astype(jnp.bfloat16)
    context = jnp.einsum(
        "bhqk,bkhd->bqhd", attn_probs, value_heads, preferred_element_type=jnp.float32
    )
    context = context.reshape(tokens, model_width).astype(jnp.bfloat16)
    attended = jnp.dot(context, full_wo, preferred_element_type=jnp.float32) + full_bo
    hidden, normed_one, inverse_one = norm_rows(
        embedded.astype(jnp.float32) + attended, full_g1, full_s1
    )
    hidden_low = hidden.astype(jnp.bfloat16)
    up_pre = jnp.dot(hidden_low, full_wup, preferred_element_type=jnp.float32) + full_bup
    activated = jax.nn.gelu(up_pre, approximate=False).astype(jnp.bfloat16)
    down_pre = jnp.dot(activated, full_wdown, preferred_element_type=jnp.float32) + full_bdown
    normed_out, normed_two, inverse_two = norm_rows(hidden + down_pre, full_g2, full_s2)
    layer_out = jnp.where(valid_mask.reshape(tokens)[:, None], normed_out, 0.0).astype(jnp.bfloat16)
    layer_out = layer_out.reshape(sentences, length, model_width)

    def first_rows(matrix):
        return matrix.reshape(sentences, length, matrix.shape[-1])[:, 0]

    summary = first_rows(normed_out)
    magnitude = jnp.sqrt(jnp.sum(summary * summary, axis=-1, keepdims=True) + EPSILON)
    unit_vector = summary / magnitude
    unit_low = unit_vector.astype(jnp.bfloat16)
    every_unit = lax.all_gather(unit_low, ("dp", "fsdp"), axis=0, tiled=True)
    every_side = pair_slot % 2
    every_pair = pair_slot // 2
    my_slots = lax.dynamic_slice_in_dim(pair_slot, device * sentences, sentences)
    my_side = my_slots % 2
    my_pair = my_slots // 2
    lang_onehot = (pair_lang[:, None] == jnp.arange(LANGS, dtype=jnp.int32)[None, :]).astype(
        jnp.float32
    )
    per_lang = jnp.sum(lang_onehot, axis=0)
    per_pair = 1.0 / (2.0 * LANGS * jnp.sum(lang_onehot * per_lang[None, :], axis=1))
    my_weight = jnp.take(per_pair, my_pair)
    opposite = my_side[:, None] != every_side[None, :]
    partner = opposite & (my_pair[:, None] == every_pair[None, :])
    raw_scores = SCORE_SCALE * contract(unit_low, every_unit, 1, 1)
    pair_scores = jnp.where(partner, raw_scores - SCORE_SCALE * MARGIN_WIDTH, raw_scores)
    pair_scores = jnp.where(opposite, pair_scores, MASK_FLOOR)
    pair_peak = jnp.max(pair_scores, axis=1, keepdims=True)
    pair_exp = jnp.exp(pair_scores - pair_peak)
    pair_total = jnp.sum(pair_exp, axis=1, keepdims=True)
    log_total = pair_peak[:, 0] + jnp.log(pair_total[:, 0])
    picked = jnp.sum(jnp.where(partner, pair_scores, 0.0), axis=1)
    loss_value = lax.psum(jnp.sum(my_weight * (log_total - picked)), ("dp", "fsdp"))
    coefficients = (
        my_weight[:, None] * (pair_exp / pair_total - partner.astype(jnp.float32))
    ).astype(jnp.bfloat16)
    unit_grad = SCORE_SCALE * contract(coefficients, every_unit, 1, 0)
    column_terms = SCORE_SCALE * contract(coefficients, unit_low, 0, 0)
    unit_grad = unit_grad + lax.psum_scatter(
        column_terms, ("dp", "fsdp"), scatter_dimension=0, tiled=True
    )
    along = jnp.sum(unit_vector * unit_grad, axis=-1, keepdims=True)
    summary_grad = (unit_grad - unit_vector * along) / magnitude
    again_weights = (
        lax.all_gather(w_query, "fsdp", axis=0, tiled=True),
        lax.all_gather(w_key, "fsdp", axis=0, tiled=True),
        lax.all_gather(w_value, "fsdp", axis=0, tiled=True),
        lax.all_gather(w_out, "fsdp", axis=0, tiled=True),
        lax.all_gather(ln1_gain, "fsdp", axis=0, tiled=True),
        lax.all_gather(w_up, "fsdp", axis=0, tiled=True),
        lax.all_gather(w_down, "fsdp", axis=0, tiled=True),
        lax.all_gather(ln2_gain, "fsdp", axis=0, tiled=True),
    )
    again_wq, again_wk, again_wv, again_wo, again_g1, again_wup, again_wdown, again_g2 = (
        again_weights
    )
    residual_grad, grad_g2, grad_s2 = norm_back(
        summary_grad, first_rows(normed_two), first_rows(inverse_two), again_g2
    )
    down_grad = residual_grad.astype(jnp.bfloat16)
    activated_cls = first_rows(activated)
    act_grad = contract(down_grad, again_wdown, 1, 1)
    gelu_value, gelu_pull = jax.vjp(partial(jax.nn.gelu, approximate=False), first_rows(up_pre))
    up_grad = gelu_pull(act_grad)[0].astype(jnp.bfloat16)
    hidden_cls = first_rows(hidden_low)
    hidden_grad = contract(up_grad, again_wup, 1, 1) + residual_grad
    first_grad, grad_g1, grad_s1 = norm_back(
        hidden_grad, first_rows(normed_one), first_rows(inverse_one), again_g1
    )
    attend_grad = first_grad.astype(jnp.bfloat16)
    context_cls = first_rows(context)
    context_grad = (
        contract(attend_grad, again_wo, 1, 1).astype(jnp.bfloat16).reshape(sentences, HEADS, HEAD)
    )
    query_cls = query_heads[:, 0]
    cls_scores = (
        jnp.einsum("bhd,bkhd->bhk", query_cls, key_heads, preferred_element_type=jnp.float32)
        * score_factor
    )
    cls_scores = jnp.where(valid_mask[:, None, :], cls_scores, MASK_FLOOR)
    cls_probs = jnp.exp(cls_scores - row_peak[:, :, 0]) / totals[:, :, 0]
    prob_grad = jnp.einsum(
        "bhd,bkhd->bhk", context_grad, value_heads, preferred_element_type=jnp.float32
    )
    score_grad = (
        cls_probs * (prob_grad - jnp.sum(cls_probs * prob_grad, axis=-1, keepdims=True))
    ).astype(jnp.bfloat16)
    query_grad = (
        (
            jnp.einsum("bhk,bkhd->bhd", score_grad, key_heads, preferred_element_type=jnp.float32)
            * score_factor
        )
        .astype(jnp.bfloat16)
        .reshape(sentences, model_width)
    )
    key_grad = (
        (
            jnp.einsum("bhk,bhd->bkhd", score_grad, query_cls, preferred_element_type=jnp.float32)
            * score_factor
        )
        .astype(jnp.bfloat16)
        .reshape(tokens, model_width)
    )
    value_grad = (
        jnp.einsum(
            "bhk,bhd->bkhd",
            cls_probs.astype(jnp.bfloat16),
            context_grad,
            preferred_element_type=jnp.float32,
        )
        .astype(jnp.bfloat16)
        .reshape(tokens, model_width)
    )
    embedded_cls = first_rows(embedded)
    grad_wkey = contract(embedded, key_grad, 0, 0)
    grad_wvalue = contract(embedded, value_grad, 0, 0)
    grad_bvalue = jnp.sum(value_grad, axis=0, dtype=jnp.float32)
    row_grads = contract(key_grad, again_wk, 1, 1) + contract(value_grad, again_wv, 1, 1)
    summary_extra = contract(query_grad, again_wq, 1, 1) + first_grad
    row_grads = (
        row_grads.reshape(sentences, length, model_width)
        .at[:, 0]
        .add(summary_extra)
        .reshape(tokens, model_width)
    )
    outgoing = jnp.zeros((owners * capacity, model_width), jnp.float32).at[slot_of].set(row_grads)
    incoming = lax.all_to_all(
        lax.all_to_all(
            outgoing.reshape(dp_count, fsdp_count, capacity, model_width).astype(jnp.bfloat16),
            "dp",
            split_axis=0,
            concat_axis=0,
            tiled=True,
        ),
        "fsdp",
        split_axis=1,
        concat_axis=1,
        tiled=True,
    ).astype(jnp.float32)
    incoming = jnp.where(
        present.reshape(owners * capacity)[:, None],
        incoming.reshape(owners * capacity, model_width),
        0.0,
    )
    table_grad = (
        jnp.zeros((vocab_rows, model_width), jnp.float32)
        .at[local_rows.reshape(owners * capacity)]
        .add(incoming)
    )
    grad_wquery = contract(embedded_cls, query_grad, 0, 0)
    grad_bquery = jnp.sum(query_grad, axis=0, dtype=jnp.float32)
    grad_wout = contract(context_cls, attend_grad, 0, 0)
    grad_bout = jnp.sum(attend_grad, axis=0, dtype=jnp.float32)
    grad_wup = contract(hidden_cls, up_grad, 0, 0)
    grad_bup = jnp.sum(up_grad, axis=0, dtype=jnp.float32)
    grad_wdown = contract(activated_cls, down_grad, 0, 0)
    grad_bdown = jnp.sum(down_grad, axis=0, dtype=jnp.float32)
    owned_grads = (
        lax.psum_scatter(
            grad_wquery.astype(jnp.bfloat16), "fsdp", scatter_dimension=0, tiled=True
        ).astype(jnp.float32),
        lax.psum_scatter(
            grad_bquery.astype(jnp.bfloat16), "fsdp", scatter_dimension=0, tiled=True
        ).astype(jnp.float32),
        lax.psum_scatter(
            grad_wkey.astype(jnp.bfloat16), "fsdp", scatter_dimension=0, tiled=True
        ).astype(jnp.float32),
        lax.psum_scatter(
            grad_wvalue.astype(jnp.bfloat16), "fsdp", scatter_dimension=0, tiled=True
        ).astype(jnp.float32),
        lax.psum_scatter(
            grad_bvalue.astype(jnp.bfloat16), "fsdp", scatter_dimension=0, tiled=True
        ).astype(jnp.float32),
        lax.psum_scatter(
            grad_wout.astype(jnp.bfloat16), "fsdp", scatter_dimension=0, tiled=True
        ).astype(jnp.float32),
        lax.psum_scatter(
            grad_bout.astype(jnp.bfloat16), "fsdp", scatter_dimension=0, tiled=True
        ).astype(jnp.float32),
        lax.psum_scatter(
            grad_g1.astype(jnp.bfloat16), "fsdp", scatter_dimension=0, tiled=True
        ).astype(jnp.float32),
        lax.psum_scatter(
            grad_s1.astype(jnp.bfloat16), "fsdp", scatter_dimension=0, tiled=True
        ).astype(jnp.float32),
        lax.psum_scatter(
            grad_wup.astype(jnp.bfloat16), "fsdp", scatter_dimension=0, tiled=True
        ).astype(jnp.float32),
        lax.psum_scatter(
            grad_bup.astype(jnp.bfloat16), "fsdp", scatter_dimension=0, tiled=True
        ).astype(jnp.float32),
        lax.psum_scatter(
            grad_wdown.astype(jnp.bfloat16), "fsdp", scatter_dimension=0, tiled=True
        ).astype(jnp.float32),
        lax.psum_scatter(
            grad_bdown.astype(jnp.bfloat16), "fsdp", scatter_dimension=0, tiled=True
        ).astype(jnp.float32),
        lax.psum_scatter(
            grad_g2.astype(jnp.bfloat16), "fsdp", scatter_dimension=0, tiled=True
        ).astype(jnp.float32),
        lax.psum_scatter(
            grad_s2.astype(jnp.bfloat16), "fsdp", scatter_dimension=0, tiled=True
        ).astype(jnp.float32),
    )
    summed = (
        lax.psum(owned_grads[0].astype(jnp.bfloat16), "dp").astype(jnp.float32),
        lax.psum(owned_grads[1].astype(jnp.bfloat16), "dp").astype(jnp.float32),
        lax.psum(owned_grads[2].astype(jnp.bfloat16), "dp").astype(jnp.float32),
        lax.psum(owned_grads[3].astype(jnp.bfloat16), "dp").astype(jnp.float32),
        lax.psum(owned_grads[4].astype(jnp.bfloat16), "dp").astype(jnp.float32),
        lax.psum(owned_grads[5].astype(jnp.bfloat16), "dp").astype(jnp.float32),
        lax.psum(owned_grads[6].astype(jnp.bfloat16), "dp").astype(jnp.float32),
        lax.psum(owned_grads[7].astype(jnp.bfloat16), "dp").astype(jnp.float32),
        lax.psum(owned_grads[8].astype(jnp.bfloat16), "dp").astype(jnp.float32),
        lax.psum(owned_grads[9].astype(jnp.bfloat16), "dp").astype(jnp.float32),
        lax.psum(owned_grads[10].astype(jnp.bfloat16), "dp").astype(jnp.float32),
        lax.psum(owned_grads[11].astype(jnp.bfloat16), "dp").astype(jnp.float32),
        lax.psum(owned_grads[12].astype(jnp.bfloat16), "dp").astype(jnp.float32),
        lax.psum(owned_grads[13].astype(jnp.bfloat16), "dp").astype(jnp.float32),
        lax.psum(owned_grads[14].astype(jnp.bfloat16), "dp").astype(jnp.float32),
    )
    return (
        layer_out,
        loss_value,
        table_grad,
        summed[0],
        summed[1],
        summed[2],
        summed[3],
        summed[4],
        summed[5],
        summed[6],
        summed[7],
        summed[8],
        summed[9],
        summed[10],
        summed[11],
        summed[12],
        summed[13],
        summed[14],
    )


CORES = 2
PLANES = 4
LINES = 4
CHIPS = PLANES * LINES
DEVICES = CORES * CHIPS
CAPACITY = 48
GROUPS = 3
PAD = 16
TOKENS = 768
WIDTH = 768
WIDE = 3072
VOCAB_ROWS = 1024
PAIR_ROWS = HEADS * PAD
SLOT_ROWS = DEVICES * PAD
LONG = 64
BLOCK = 256
MESH = pl.DeviceIdType.MESH
LOW = jnp.bfloat16
FULL = jnp.float32
VMEM_LIMIT = 62 * 1024 * 1024

INPUTS = ["table", "token_ids", "lens", "slots", "langs"]
INPUTS += ["wq", "bq", "wk", "wv", "bv", "wo", "bo", "g1", "s1", "wup", "bup", "wdown", "bdown"]
INPUTS += ["g2", "s2"]
OUTPUTS = ["layer_out", "table_grad", "g_wq", "g_wk", "g_wv", "g_wo", "g_wup", "g_wdown"]
OUTPUTS += ["g_small", "loss"]


def place():
    core = lax.axis_index("dp")
    chip = lax.axis_index("fsdp")
    along_x = chip + 1 - 2 * (chip % 2)
    along_y = chip + 2 - 4 * ((chip // 2) % 2)
    first = along_x + core * (along_y - along_x)
    second = along_y + core * (along_x - along_y)
    return core, chip, first, second


def greet():
    core, chip, _, _ = place()
    me = core * CHIPS + chip
    barrier = pltpu.get_barrier_semaphore()

    def signal(step):
        other = lax.rem(me + step, DEVICES)
        pl.semaphore_signal(
            barrier,
            inc=1,
            device_id=(lax.div(other, CHIPS), lax.rem(other, CHIPS)),
            device_id_type=MESH,
        )

    every(1, DEVICES, signal)


def enter():
    pl.semaphore_wait(pltpu.get_barrier_semaphore(), DEVICES - 1)


def remote(source, target, send_sem, recv_sem, core, chip):
    return pltpu.make_async_remote_copy(
        src_ref=source,
        dst_ref=target,
        send_sem=send_sem,
        recv_sem=recv_sem,
        device_id=(core, chip),
        device_id_type=MESH,
    )


def every(start, stop, act):
    def step(index, carry):
        act(index)
        return carry

    lax.fori_loop(start, stop, step, 0)


def weight_steps(piece, send, recv):
    core, chip, first, second = place()
    plane, line = chip // LINES, chip % LINES
    line_first, line_second = first % LINES, second % LINES
    line_far = line_first + line_second - line
    is_low, is_high = plane > 0, plane < PLANES - 1

    def copy(send_index, recv_index, at, to_core, to_chip, carried=core):
        part = piece(at, carried)
        return remote(part, part, send.at[send_index], recv.at[recv_index], to_core, to_chip)

    def up(at_plane):
        return copy(at_plane, at_plane, at_plane * LINES + line, core, chip + LINES)

    def down(at_plane, index):
        return copy(index, at_plane, at_plane * LINES + line, core, chip - LINES)

    def side(at_plane, base, at_line, target):
        return copy(base + at_plane, base + at_plane, at_plane * LINES + at_line, core, target)

    def across(at_plane, base, at_line):
        return copy(base + at_plane, base + at_plane, at_plane * LINES + at_line, 1 - core, chip)

    def begin():
        pl.when(is_high)(lambda: up(plane).start())
        pl.when(is_low)(lambda: down(plane, PLANES).start())
        side(plane, 5, line, first).start()
        side(plane, 9, line, second).start()

    def at_distance(distance, act):
        if distance == 0:
            act(plane, None)
            return
        pl.when(plane >= distance)(lambda: act(plane - distance, True))
        pl.when(plane + distance < PLANES)(lambda: act(plane + distance, False))

    def chain(distance):
        def act(at_plane, from_low):
            if from_low:
                up(at_plane).wait_recv()
                pl.when(is_high)(lambda: up(at_plane).start())
            else:
                down(at_plane, at_plane).wait_recv()
                pl.when(is_low)(lambda: down(at_plane, at_plane).start())
            side(at_plane, 5, line, first).start()
            side(at_plane, 9, line, second).start()
            across(at_plane, 17, line).start()

        return partial(at_distance, distance, act)

    def near(distance):
        def act(at_plane, from_low):
            side(at_plane, 5, line_first, first).wait_recv()
            side(at_plane, 13, line_first, second).start()
            across(at_plane, 21, line_first).start()

        return partial(at_distance, distance, act)

    def far(distance):
        def act(at_plane, from_low):
            side(at_plane, 9, line_second, second).wait_recv()
            across(at_plane, 25, line_second).start()
            side(at_plane, 13, line_far, second).wait_recv()
            across(at_plane, 29, line_far).start()

        return partial(at_distance, distance, act)

    def finish():
        for step in range(1, PLANES):
            index = 17 + (plane + step) % PLANES
            copy(index, index, chip, 1 - core, chip, 1 - core).wait_recv()
        every(21, 33, lambda index: copy(index, index, chip, 1 - core, chip, 1 - core).wait_recv())

    def drain():
        def sent(index):
            copy(index, index, chip, 1 - core, chip).wait_send()

        for at_plane in range(PLANES):
            pl.when((plane >= at_plane) & is_high)(partial(sent, at_plane))
            pl.when((plane < at_plane) & is_low)(partial(sent, at_plane))
        pl.when(is_low)(partial(sent, PLANES))
        every(5, 17, sent)
        for step in range(1, PLANES):
            sent(17 + (plane + step) % PLANES)
        every(21, 33, sent)

    moves = [chain(1), near(0), chain(2), near(1), chain(3), far(0)]
    moves += [near(2), far(1), near(3), far(2), far(3)]
    return begin, moves, finish, drain


def gather_steps(buffer, send, recv):
    core, chip, first, second = place()
    plane, line = chip // LINES, chip % LINES
    line_first, line_second = first % LINES, second % LINES
    line_far = line_first + line_second - line
    half = buffer.shape[-1] // 2
    columns = pl.ds(pl.multiple_of(core * half, 128), half)
    others = pl.ds(pl.multiple_of((1 - core) * half, 128), half)

    def copy(index, part, to_core, to_chip):
        return remote(part, part, send.at[index], recv.at[index], to_core, to_chip)

    def own(at):
        return buffer.at[at, plane, line]

    def chip_part(at_plane, at_line, which):
        return buffer.at[:, at_plane, at_line, :, which]

    def line_part(at_line, which):
        return buffer.at[:, :, at_line, :, which]

    def start():
        copy(0, own(core), 1 - core, chip).start()

    def planes():
        copy(0, own(1 - core), 1 - core, chip).wait_recv()
        for step in range(1, PLANES):
            part = chip_part(plane, line, columns)
            copy(step, part, core, (chip + LINES * step) % CHIPS).start()

    def sides():
        for step in range(1, PLANES):
            part = chip_part((plane + PLANES - step) % PLANES, line, columns)
            copy(step, part, core, chip).wait_recv()
        copy(4, line_part(line, columns), core, first).start()
        copy(5, line_part(line, columns), core, second).start()
        for step in range(1, PLANES):
            part = chip_part((plane + PLANES - step) % PLANES, line, columns)
            copy(6 + step, part, 1 - core, chip).start()

    def corner():
        copy(4, line_part(line_first, columns), core, first).wait_recv()
        copy(6, line_part(line_first, columns), core, second).start()
        copy(10, line_part(line_first, columns), 1 - core, chip).start()
        copy(5, line_part(line_second, columns), core, second).wait_recv()
        copy(11, line_part(line_second, columns), 1 - core, chip).start()

    def last():
        copy(6, line_part(line_far, columns), core, second).wait_recv()
        copy(12, line_part(line_far, columns), 1 - core, chip).start()

    def finish():
        for step in range(1, PLANES):
            part = chip_part((plane + PLANES - step) % PLANES, line, others)
            copy(6 + step, part, 1 - core, chip).wait_recv()
        copy(10, line_part(line_second, others), 1 - core, chip).wait_recv()
        copy(11, line_part(line_first, others), 1 - core, chip).wait_recv()
        copy(12, line_part(line_far, others), 1 - core, chip).wait_recv()

    def drain():
        copy(0, own(core), 1 - core, chip).wait_send()
        for index in [1, 2, 3, 7, 8, 9]:
            copy(index, chip_part(plane, line, columns), 1 - core, chip).wait_send()
        for index in [4, 5, 6, 10, 11, 12]:
            copy(index, line_part(line, columns), 1 - core, chip).wait_send()

    return [start, planes, sides, corner, last, finish], drain


def iota(shape, axis):
    return lax.broadcasted_iota(jnp.int32, shape, axis)


def as_column(row):
    parts = []
    for start in range(0, row.shape[1], 128):
        tile = jnp.broadcast_to(row[:, start : start + 128], (128, 128))
        parts.append(jnp.transpose(tile)[:, 0:1])
    return jnp.concatenate(parts, axis=0)


def as_row(column):
    parts = []
    for start in range(0, column.shape[0], 128):
        tile = jnp.broadcast_to(column[start : start + 128, :], (128, 128))
        parts.append(jnp.transpose(tile)[0:1, :])
    return jnp.concatenate(parts, axis=1)


def dot(left_side, right_side):
    return contract(left_side, right_side, 1, 0)


def dot_turned(left_side, right_side):
    return contract(left_side, right_side, 1, 1)


def norm_parts(inputs):
    centered = inputs - jnp.mean(inputs, axis=-1, keepdims=True)
    inverse = lax.rsqrt(jnp.mean(centered * centered, axis=-1, keepdims=True) + EPSILON)
    return centered * inverse, inverse


def norm_back_parts(grad_output, normed, inverse, ln_gain):
    grad_normed = grad_output * ln_gain
    first_term = jnp.mean(grad_normed, axis=-1, keepdims=True)
    second_term = jnp.mean(grad_normed * normed, axis=-1, keepdims=True)
    return (
        inverse * (grad_normed - first_term - normed * second_term),
        jnp.sum(grad_output * normed, axis=0, keepdims=True),
        jnp.sum(grad_output, axis=0, keepdims=True),
    )


def erf_parts(inputs):
    decay = jnp.exp(-0.5 * inputs * inputs)
    share = 1.0 / (1.0 + jnp.abs(inputs) * (0.3275911 * 0.5**0.5))
    terms = [1.061405429, -1.453152027, 1.421413741, -0.284496736, 0.254829592]
    series = 0.5 * terms[0]
    for term in terms[1:]:
        series = series * share + 0.5 * term
    tail = series * share * decay
    return jnp.where(inputs >= 0.0, 1.0 - tail, tail), decay


def gelu_parts(inputs):
    below, decay = erf_parts(inputs)
    return inputs * below, below + inputs * decay * ((2.0 * 3.141592653589793) ** -0.5)


def gelu(inputs):
    return inputs * erf_parts(inputs)[0]


def layer_kernel(names, *refs):
    r = SimpleNamespace(**dict(zip(names, refs, strict=True)))
    core, chip, _, _ = place()
    me = core * CHIPS + chip
    here = (core, chip // LINES, chip % LINES)
    scale = HEAD ** (-0.5)
    depth, deep = WIDTH // CHIPS, WIDE // CHIPS
    sentences = TOKENS // LONG

    for j in range(TOKENS // 128):
        r.ids[j : j + 1, :] = jnp.concatenate(
            [r.token_ids[2 * j : 2 * j + 1, :], r.token_ids[2 * j + 1 : 2 * j + 2, :]], axis=1
        )
    r.ids[TOKENS // 128 : 8, :] = jnp.zeros((8 - TOKENS // 128, 128), jnp.int32)
    greet()
    ahead = (iota((TOKENS, TOKENS), 0) < iota((TOKENS, TOKENS), 1)).astype(LOW)
    r.embedded[...] = ahead
    mine = pl.ds(pl.multiple_of(chip * depth, 16), depth)
    for index, shard in enumerate([r.wq, r.wk, r.wv, r.wo]):
        r.wa[mine, index * WIDTH : (index + 1) * WIDTH] = shard[...]
    r.every_ids[me] = r.ids[...]
    enter()

    def peer(step):
        other = lax.rem(me + step, DEVICES)
        return other, lax.div(other, CHIPS), lax.rem(other, CHIPS)

    def ids_copy(step):
        other, to_core, to_chip = peer(step)
        return remote(r.ids, r.every_ids.at[me], r.one_send.at[0], r.one_recv.at[0], to_core, to_chip)

    def all_but_one(ref, index):
        part = ref.at[0 : DEVICES - 1]
        return remote(part, part, r.one_send.at[index], r.one_recv.at[index], 1 - core, chip)

    every(1, DEVICES, lambda step: ids_copy(step).start())

    def block(ref, rows, columns):
        def piece(at, carried):
            return ref.at[
                pl.ds(pl.multiple_of(at * rows, 16), rows),
                pl.ds(pl.multiple_of(carried * columns, 128), columns),
            ]

        return piece

    begin_a, moves_a, finish_a, drain_a = weight_steps(
        block(r.wa, depth, 2 * WIDTH), r.weight_send.at[0], r.weight_recv.at[0]
    )
    begin_b, moves_b, finish_b, drain_b = weight_steps(
        block(r.wb, depth, WIDE // 2), r.weight_send.at[1], r.weight_recv.at[1]
    )
    begin_c, moves_c, finish_c, drain_c = weight_steps(
        block(r.wc, deep, WIDTH // 2), r.weight_send.at[2], r.weight_recv.at[2]
    )
    begin_a()

    all_but_one(r.every_ids, 0).wait_recv()
    all_ids = jnp.concatenate([r.every_ids[:, j, :] for j in range(TOKENS // 128)], axis=1)
    all_owner = all_ids // VOCAB_ROWS
    asked = all_owner == me
    ranks = dot(asked.astype(LOW), r.embedded[...])
    r.rank[...] = jnp.where(asked, ranks, -1.0)
    local_row = (all_ids - all_owner * VOCAB_ROWS + 1).astype(FULL)
    r.code[...] = local_row + (iota((DEVICES, TOKENS), 1) // LONG * 2048).astype(FULL)

    quarter_size = DEVICES // 4

    def rows_copy(other, quarter):
        return remote(
            r.rows.at[:, pl.ds(pl.multiple_of(other * PAD, 16), PAD), :],
            r.replies.at[:, pl.ds(pl.multiple_of(me * PAD, 16), PAD), :],
            r.rows_send.at[quarter],
            r.rows_recv.at[quarter],
            lax.div(other, CHIPS),
            lax.rem(other, CHIPS),
        )

    def rows_of(quarter):
        count = quarter_size - 1 if quarter == 3 else quarter_size
        part = r.replies.at[:, 0 : count * PAD, :]
        return remote(
            part, part, r.rows_send.at[quarter], r.rows_recv.at[quarter], 1 - core, chip
        )

    def pick(source):
        rank = r.rank[pl.ds(source, 1), :]
        code = r.code[pl.ds(source, 1), :]
        here_at = iota((CAPACITY, TOKENS), 0).astype(FULL) == rank
        found = jnp.sum(jnp.where(here_at, code, 0.0), axis=1, keepdims=True)
        sent = jnp.floor(found * (1.0 / 2048))
        row = found - sent * 2048.0 - 1.0
        chosen = (iota((CAPACITY, VOCAB_ROWS), 1).astype(FULL) == row).astype(LOW)
        at = pl.ds(pl.multiple_of(source * PAD, 16), PAD)
        source_sent = sent + (source * PAD).astype(FULL)
        for group in range(GROUPS):
            part = slice(group * PAD, (group + 1) * PAD)
            r.chosen[group, at, :] = chosen[part]
            r.found[group, at, 0:1] = row[part]
            r.found[group, at, 1:2] = source_sent[part]

    for quarter in range(4):
        now = lax.rem(lax.div(me, quarter_size) + 1 + quarter, 4)

        def pick_two(index):
            pick(now * quarter_size + 2 * index)
            pick(now * quarter_size + 2 * index + 1)

        every(0, quarter_size // 2, pick_two)
        span = pl.ds(pl.multiple_of(now * quarter_size * PAD, 128), quarter_size * PAD)
        picked = r.chosen[:, span, :].reshape(GROUPS * quarter_size * PAD, VOCAB_ROWS)
        found_rows = dot(picked, r.table[...]).astype(LOW)
        r.rows[:, span, :] = found_rows.reshape(GROUPS, quarter_size * PAD, WIDTH)

        def send(index):
            other = now * quarter_size + lax.rem(lax.rem(me, quarter_size) + index, quarter_size)
            rows_copy(other, quarter).start()

        every(1 if quarter == 3 else 0, quarter_size, send)
        moves_a[2 * quarter]()
        moves_a[2 * quarter + 1]()
    own_at = pl.ds(pl.multiple_of(me * PAD, 16), PAD)
    r.replies[:, own_at, :] = r.rows[:, own_at, :]

    small_here = pl.ds(pl.multiple_of(chip * 128, 128), 128)
    lines = [r.bq, r.bv, r.bo, r.g1, r.s1, r.bdown, r.g2, r.s2]
    lines = [line[...].reshape(1, depth).astype(FULL) for line in lines]
    up_line = r.bup[...].reshape(1, deep).astype(FULL)
    lines += [up_line[:, part * depth : (part + 1) * depth] for part in range(deep // depth)]
    lines.append(jnp.zeros((PAD - len(lines), depth), FULL))
    own_small = jnp.concatenate(lines, axis=0)
    own_small = jnp.concatenate([own_small, jnp.zeros((PAD, 128 - depth), FULL)], axis=1)
    r.smalls[:, small_here] = own_small.astype(LOW)

    def small_copy(step):
        part = r.smalls.at[:, small_here]
        to_chip = lax.rem(chip + step, CHIPS)
        return remote(part, part, r.small_send.at[0], r.small_recv.at[0], core, to_chip)

    def all_smalls():
        part = r.smalls.at[:, 0 : (CHIPS - 1) * 128]
        return remote(part, part, r.small_send.at[0], r.small_recv.at[0], 1 - core, chip)

    every(1, CHIPS, lambda step: small_copy(step).start())
    r.wb[mine, :] = r.wup[...]
    r.wc[pl.ds(pl.multiple_of(chip * deep, 16), deep), :] = r.wdown[...]

    own_row = jnp.concatenate([r.ids[j : j + 1, :] for j in range(TOKENS // 128)], axis=1)
    owner_row = (own_row // VOCAB_ROWS).astype(FULL)
    owner_col = as_column(owner_row)
    earlier = (owner_row == owner_col) & (iota((TOKENS, TOKENS), 1) < iota((TOKENS, TOKENS), 0))
    own_rank = jnp.sum(earlier.astype(FULL), axis=1, keepdims=True)
    own_group = jnp.floor(own_rank * (1.0 / PAD))
    own_slot = own_group * SLOT_ROWS + owner_col * PAD + (own_rank - own_group * PAD)
    r.slot_col[...] = own_slot
    r.slot_line[0:1, :] = as_row(own_slot)

    at_sent = iota((1, TOKENS), 1) // LONG
    lens = jnp.concatenate(
        [r.lens[...].reshape(1, sentences).astype(FULL), jnp.zeros((1, PAD - sentences), FULL)],
        axis=1,
    )
    spread_lens = dot(
        jnp.broadcast_to(lens, (8, PAD)).astype(LOW),
        (iota((PAD, TOKENS), 0) == iota((PAD, TOKENS), 1) // LONG).astype(LOW),
    )[0:1]
    valid_row = ((iota((1, TOKENS), 1) - at_sent * LONG).astype(FULL) < spread_lens).astype(FULL)
    r.valid_line[0:1, :] = valid_row
    r.valid_col[...] = as_column(valid_row)
    half_block = BLOCK // 2
    stacked_shape = (4 * half_block, half_block)
    same = iota(stacked_shape, 0) // LONG % 2 == iota(stacked_shape, 1) // LONG
    r.block_bias[...] = jnp.where(same, 0.0, MASK_FLOOR)
    r.valid_bias[0:1, :] = (1.0 - valid_row) * MASK_FLOOR

    slots = r.slots[...].reshape(1, DEVICES * sentences)
    gap = jnp.full((1, PAD - sentences), -2, jnp.int32)
    slot_line = jnp.concatenate(
        [
            part
            for device in range(DEVICES)
            for part in (slots[:, device * sentences : (device + 1) * sentences], gap)
        ],
        axis=1,
    )
    side_line = slot_line - slot_line // 2 * 2 + jnp.where(slot_line < 0, 8, 0)
    pair_line = slot_line // 2
    pairs = r.langs.shape[0]
    lang_line = r.langs[...].reshape(1, pairs).astype(FULL)
    lang_line = jnp.concatenate([lang_line, jnp.full((1, -pairs % 128), -1.0, FULL)], axis=1)
    lang_col = as_column(lang_line)
    same_lang = jnp.sum(jnp.where(lang_col == lang_line, 1.0, 0.0), axis=1, keepdims=True)
    per_pair = 1.0 / (2.0 * LANGS * same_lang)
    at_pair = iota((lang_line.shape[1], SLOT_ROWS), 0) == pair_line
    weight_line = jnp.sum(jnp.where(at_pair, per_pair, 0.0), axis=0, keepdims=True)
    r.pairs[0:1, :] = weight_line
    r.pairs[1:2, :] = pair_line.astype(FULL)
    r.pairs[2:3, :] = side_line.astype(FULL)
    r.pairs_col[:, 0:1] = as_column(weight_line)
    r.pairs_col[:, 1:2] = as_column(pair_line.astype(FULL))
    r.pairs_col[:, 2:3] = as_column(side_line.astype(FULL))
    for move in moves_a[8:]:
        move()

    all_smalls().wait_recv()
    smalls = r.smalls[...].astype(FULL)
    r.vectors[:, 0:WIDTH] = jnp.concatenate(
        [smalls[:, at * 128 : at * 128 + depth] for at in range(CHIPS)], axis=1
    )
    r.up_bias[0:1, :] = jnp.concatenate(
        [
            smalls[8 + part : 9 + part, at * 128 : at * 128 + depth]
            for at in range(CHIPS)
            for part in range(deep // depth)
        ],
        axis=1,
    )

    def vector(index):
        return r.vectors[index : index + 1, :]

    r.qkv_bias[0:1, 0:WIDTH] = vector(0)
    r.qkv_bias[0:1, WIDTH : 2 * WIDTH] = jnp.zeros((1, WIDTH), FULL)
    r.qkv_bias[0:1, 2 * WIDTH : 3 * WIDTH] = vector(1)

    def first_row(source):
        code = jnp.where(r.rank[pl.ds(source, 1), :] >= 0.0, r.code[pl.ds(source, 1), :], 0.0)
        at_first = iota((PAD, TOKENS), 1) == iota((PAD, TOKENS), 0) * LONG
        found = jnp.sum(jnp.where(at_first, code, 0.0), axis=1, keepdims=True)
        row = found - jnp.floor(found * (1.0 / 2048)) * 2048.0 - 1.0
        r.found[GROUPS, pl.ds(pl.multiple_of(source * PAD, 16), PAD), 0:1] = row

    every(0, DEVICES, first_row)
    for group in range(GROUPS + 1):
        named = as_row(r.found[group, :, 0:1])
        by_row = iota((VOCAB_ROWS, SLOT_ROWS), 0).astype(FULL) == named
        r.by_row[:, group * SLOT_ROWS : (group + 1) * SLOT_ROWS] = by_row.astype(LOW)

    def order(tile):
        at = pl.ds(pl.multiple_of(tile * BLOCK, BLOCK), BLOCK)
        lanes = iota((BLOCK, GROUPS * SLOT_ROWS), 1).astype(FULL)
        r.qkv[at, 0 : GROUPS * SLOT_ROWS] = (r.slot_col[at, :] == lanes).astype(LOW)

    every(0, TOKENS // BLOCK, order)
    rows_of(0).wait_recv()
    rows_of(1).wait_recv()
    begin_b()
    moves_b[0]()
    moves_b[1]()
    rows_of(2).wait_recv()
    moves_b[2]()
    moves_b[3]()
    rows_of(3).wait_recv()
    begin_c()

    def embed(tile):
        at = pl.ds(pl.multiple_of(tile * BLOCK, BLOCK), BLOCK)
        replies = r.replies[:, :, at].reshape(GROUPS * SLOT_ROWS, BLOCK)
        r.embedded[:, at] = dot(r.qkv[:, 0 : GROUPS * SLOT_ROWS], replies).astype(LOW)

    every(0, WIDTH // BLOCK, embed)
    finish_a()
    moves_b[4]()
    moves_b[5]()

    def project(tile):
        at = pl.ds(pl.multiple_of(tile * BLOCK, BLOCK), BLOCK)
        r.qkv[:, at] = (dot(r.embedded[...], r.wa[:, at]) + r.qkv_bias[0:1, at]).astype(LOW)

    every(3, 6, project)
    moves_b[6]()
    moves_b[7]()
    every(6, 9, project)
    moves_b[8]()
    moves_b[9]()
    moves_b[10]()

    row_sent = iota((PAIR_ROWS, WIDTH), 0) % PAD
    row_head = iota((PAIR_ROWS, WIDTH), 0) // PAD
    lane_block = iota((PAIR_ROWS, WIDTH), 1) // HEAD
    in_head = row_head == lane_block
    seen = (row_sent == lane_block) & (r.valid_line[0:1, :] > 0.0)
    firsts = (iota((PAD, TOKENS), 1) == iota((PAD, TOKENS), 0) * LONG).astype(LOW)
    real_row = iota((PAD, 1), 0) < sentences

    def spread(rows):
        return jnp.where(in_head, jnp.concatenate([rows] * HEADS, axis=0), jnp.zeros((), LOW))

    def fold(tall):
        tall = jnp.where(in_head, tall, 0.0)
        return sum(tall[head * PAD : (head + 1) * PAD] for head in range(HEADS))

    keys, values = slice(WIDTH, 2 * WIDTH), slice(2 * WIDTH, 3 * WIDTH)
    embedded_cls = dot(firsts, r.embedded[...]).astype(LOW)
    query_cls = (dot(embedded_cls, r.wa[:, 0:WIDTH]) + vector(0)).astype(LOW)
    cls_scores = dot_turned(spread(query_cls), r.qkv[:, keys]) * scale
    cls_scores = jnp.where(seen, cls_scores, MASK_FLOOR)
    cls_peak = jnp.max(cls_scores, axis=1, keepdims=True)
    cls_exp = jnp.where(seen, jnp.exp(cls_scores - cls_peak), 0.0)
    cls_total = jnp.sum(cls_exp, axis=1, keepdims=True)
    cls_probs = cls_exp / jnp.where(cls_total > 0.0, cls_total, 1.0)
    probs_low = cls_probs.astype(LOW)
    r.probs[...] = cls_probs
    context_cls = fold(dot(probs_low, r.qkv[:, values])).astype(LOW)
    moves_c[0]()
    moves_c[1]()
    first_cls = (
        embedded_cls.astype(FULL)
        + dot(context_cls, r.wa[:, 3 * WIDTH : 4 * WIDTH])
        + vector(2)
    )
    normed_one, inverse_one = norm_parts(first_cls)
    r.normed_one[...] = normed_one
    hidden_cls = normed_one * vector(3) + vector(4)
    hidden_cls_low = hidden_cls.astype(LOW)
    early_here = r.early.at[here]
    early_here[:, 0:WIDTH] = hidden_cls_low
    early_here[:, WIDTH : 2 * WIDTH] = query_cls
    steps_u, drain_u = gather_steps(r.units, r.gather_send.at[0], r.gather_recv.at[0])
    steps_e, drain_e = gather_steps(r.early, r.gather_send.at[1], r.gather_recv.at[1])
    steps_d, drain_d = gather_steps(r.downs, r.gather_send.at[2], r.gather_recv.at[2])
    steps_a, drain_a2 = gather_steps(r.attends, r.gather_send.at[3], r.gather_recv.at[3])
    steps_q, drain_q = gather_steps(r.queries, r.gather_send.at[4], r.gather_recv.at[4])
    steps_e[0]()
    moves_c[2]()
    moves_c[3]()
    steps_e[1]()

    def attend(unit):
        rows = pl.ds(pl.multiple_of(unit * half_block, half_block), half_block)
        lane_head = iota((half_block, BLOCK), 1) // HEAD
        bias = r.block_bias[...] + r.valid_bias[0:1, rows]

        def part(which, lane):
            return r.qkv[rows, which * WIDTH + lane : which * WIDTH + lane + BLOCK]

        for lane in range(0, WIDTH, BLOCK):
            query = part(0, lane) * jnp.asarray(scale, LOW)
            key, value = part(1, lane), part(2, lane)
            stacked = jnp.concatenate(
                [jnp.where(lane_head == head, query, jnp.zeros((), LOW)) for head in range(4)],
                axis=0,
            )
            scores = dot_turned(stacked, key) + bias
            shifted = jnp.exp(scores - jnp.max(scores, axis=1, keepdims=True))
            probs = shifted * (1.0 / jnp.sum(shifted, axis=1, keepdims=True))
            mixed = dot(probs.astype(LOW), value)
            result = mixed[0:half_block]
            for head in range(1, 4):
                result = jnp.where(
                    lane_head == head, mixed[head * half_block : (head + 1) * half_block], result
                )
            r.context[rows, lane : lane + BLOCK] = result.astype(LOW)

    def open_tile(tile):
        at = pl.ds(pl.multiple_of(tile * BLOCK, BLOCK), BLOCK)
        attended = dot(r.context[at, :], r.wa[:, 3 * WIDTH : 4 * WIDTH]) + vector(2)
        normed, _ = norm_parts(r.embedded[at, :].astype(FULL) + attended)
        hidden = normed * vector(3) + vector(4)
        r.context[at, :] = hidden.astype(LOW)
        r.table_full[at, :] = hidden + vector(5)

    most = SLOT_ROWS
    rest_at = pl.ds(most, TOKENS - most)

    def feed_up(part):
        for quarter in range(4):
            column = part * 4 * BLOCK + quarter * BLOCK
            at = slice(column, column + BLOCK)
            up_pre = dot(r.context[...], r.wb[:, at]) + r.up_bias[0:1, at]
            active = gelu(up_pre).astype(LOW)
            r.chosen[part, :, quarter * BLOCK : (quarter + 1) * BLOCK] = active[:most]
            block, lane = column // WIDTH, column % WIDTH
            target = pl.ds(block % 2 * BLOCK, BLOCK)
            r.slot_query[block // 2, target, lane : lane + BLOCK] = active[most:]

    def feed_down(part):
        lanes = pl.ds(pl.multiple_of(part * BLOCK, BLOCK), BLOCK)
        total = r.table_full[0:most, lanes]
        for group in range(GROUPS):
            rows = slice(group * VOCAB_ROWS, (group + 1) * VOCAB_ROWS)
            total = total + dot(r.chosen[group], r.wc[rows, lanes])
        r.table_full[0:most, lanes] = total

    def feed_rest(part):
        lanes = pl.ds(pl.multiple_of(part * BLOCK, BLOCK), BLOCK)
        total = r.table_full[rest_at, lanes]
        for block in range(WIDE // WIDTH):
            active = r.slot_query[block // 2, block % 2 * BLOCK : (block % 2 + 1) * BLOCK, :]
            total = total + dot(active, r.wc[block * WIDTH : (block + 1) * WIDTH, lanes])
        r.table_full[rest_at, lanes] = total

    def layer_copy(tile):
        at = pl.ds(tile * BLOCK, BLOCK)
        return pltpu.make_async_copy(r.context.at[at], r.layer_out.at[at], r.out_sem.at[tile])

    def close_tile(tile):
        at = pl.ds(tile * BLOCK, BLOCK)
        normed, _ = norm_parts(r.table_full[at, :])
        out = normed * vector(6) + vector(7)
        r.context[at, :] = (out * r.valid_col[at, :]).astype(LOW)
        layer_copy(tile).start()

    queue = [partial(every, 0, 3, project)]
    queue += [partial(every, unit, unit + 1, attend) for unit in range(6)]
    queue.append(partial(every, 0, TOKENS // BLOCK, open_tile))
    queue += [partial(feed_up, part) for part in range(GROUPS)]
    late = [partial(every, part, part + 1, feed_rest) for part in range(WIDTH // BLOCK)]
    late += [partial(every, part, part + 1, feed_down) for part in range(WIDTH // BLOCK)]
    late += [partial(close_tile, tile) for tile in range(TOKENS // BLOCK)]

    def fill(pieces, count):
        for _ in range(min(count, len(pieces))):
            pieces.pop(0)()

    fill(queue, 1)
    finish_b()
    up_cls = dot(hidden_cls_low, r.wb[...]) + r.up_bias[0:1, :]
    activated_cls, slope_cls = gelu_parts(up_cls)
    activated_low = activated_cls.astype(LOW)
    fill(queue, 1)
    for move, step in zip(moves_c[4:], [None] + steps_e[2:] + [None, None]):
        fill(queue, 1)
        move()
        if step is not None:
            step()
    fill(queue, len(queue))

    def pack_tall(tall, target, first_row, spare=None):
        for at in range(CHIPS):
            last = jnp.zeros((48, 128 - 2 * depth), FULL)
            if spare is not None:
                last = spare[at * depth : (at + 1) * depth]
            columns = tall[:, at * depth : (at + 1) * depth]
            for half in range(CORES):
                base = half * PAIR_ROWS // 2
                target[half * CHIPS + at, first_row : first_row + 48, :] = jnp.concatenate(
                    [
                        columns[base : base + 48],
                        columns[base + 48 : base + 96],
                        last,
                    ],
                    axis=1,
                ).astype(LOW)

    def pack_coefs(coefs):
        shape = (PAIR_ROWS, GROUPS * 128)
        folds = iota(shape, 0) // PAD + iota(shape, 1) // 128 * PAD == iota(shape, 1) % 128
        lanes = contract(coefs, folds.astype(LOW), 0, 0).astype(LOW)
        total = None
        for group in range(GROUPS):
            part = dot(r.rows[group], lanes[:, group * 128 : (group + 1) * 128])
            total = part if total is None else total + part
        return total.astype(LOW).reshape(DEVICES, PAD, 128)

    for quarter in range(4):
        rows_of(quarter).wait_send()
    for group in range(GROUPS):
        slot_at = iota((SLOT_ROWS, TOKENS), 0) + group * SLOT_ROWS
        r.rows[group] = (slot_at.astype(FULL) == r.slot_line[0:1, :]).astype(LOW)
    finish_c()
    down_pre = dot(activated_low, r.wc[...]) + vector(5)
    normed_two, inverse_two = norm_parts(hidden_cls + down_pre)
    summary = normed_two * vector(6) + vector(7)
    magnitude = jnp.sqrt(jnp.sum(summary * summary, axis=-1, keepdims=True) + EPSILON)
    unit = jnp.where(real_row, summary / magnitude, 0.0)
    r.units[here] = unit.astype(LOW)

    steps_u[0]()
    for at in range(CHIPS):
        cut = slice(at * depth, (at + 1) * depth)
        line = jnp.concatenate(
            [
                context_cls.astype(FULL)[:, cut],
                embedded_cls.astype(FULL)[:, cut],
                jnp.zeros((PAD, 128 - 2 * depth), FULL),
            ],
            axis=1,
        ).astype(LOW)
        for half in range(CORES):
            r.mail_one[half * CHIPS + at, 0:PAD, :] = line
    steps_u[1]()
    pack_tall(dot(probs_low, r.embedded[...]), r.mail_one, PAD)
    fill(late, 1)
    steps_u[2]()
    r.mail_one[:, 64:80, :] = pack_coefs(probs_low)
    fill(late, 1)
    steps_u[3]()
    fill(late, 2)

    def post(box, got, index):
        def send(step):
            other, to_core, to_chip = peer(step)
            remote(
                box.at[other], got.at[me], r.one_send.at[index], r.one_recv.at[index], to_core, to_chip
            ).start()

        every(1, DEVICES, send)
        got[me] = box[me]

    steps_u[4]()
    fill(late, 2)
    steps_u[5]()
    post(r.mail_one, r.got_one, 1)

    units = r.units[...].reshape(SLOT_ROWS, WIDTH)
    weight_row, pair_row, side_row = r.pairs[0:1, :], r.pairs[1:2, :], r.pairs[2:3, :]

    def pair_scores(rows, pair_col, side_col):
        opposite = side_col + side_row == 1.0
        partner = opposite & (pair_col == pair_row)
        raw = SCORE_SCALE * dot_turned(rows, units)
        shifted = jnp.where(partner, raw - SCORE_SCALE * MARGIN_WIDTH, raw)
        return jnp.where(opposite, shifted, MASK_FLOOR), partner

    every_score, every_partner = pair_scores(
        units, r.pairs_col[:, 1:2], r.pairs_col[:, 2:3]
    )
    peak_row = jnp.max(every_score, axis=0, keepdims=True)
    log_row = peak_row + jnp.log(
        jnp.sum(jnp.exp(every_score - peak_row), axis=0, keepdims=True)
    )
    picked_row = jnp.sum(jnp.where(every_partner, every_score, 0.0), axis=0, keepdims=True)
    r.loss[...] = jnp.sum(weight_row * (log_row - picked_row), axis=1, keepdims=True)

    rows_here = pl.ds(pl.multiple_of(me * PAD, 16), PAD)
    own_score, own_partner = pair_scores(
        r.units[here], r.pairs_col[rows_here, 1:2], r.pairs_col[rows_here, 2:3]
    )
    own_partner = own_partner.astype(FULL)
    own_peak = jnp.max(own_score, axis=1, keepdims=True)
    own_exp = jnp.exp(own_score - own_peak)
    own_share = own_exp / jnp.sum(own_exp, axis=1, keepdims=True)
    by_row = (r.pairs_col[rows_here, 0:1] * (own_share - own_partner)).astype(LOW)
    by_column = (weight_row * (jnp.exp(own_score - log_row) - own_partner)).astype(LOW)
    unit_grad = SCORE_SCALE * (dot(by_row, units) + dot(by_column, units))
    along = jnp.sum(unit * unit_grad, axis=-1, keepdims=True)
    summary_grad = (unit_grad - unit * along) / magnitude

    residual_grad, grad_g2, grad_s2 = norm_back_parts(
        summary_grad, normed_two, inverse_two, vector(6)
    )
    down_grad = residual_grad.astype(LOW)
    r.downs[here] = down_grad
    steps_d[0]()
    act_grad = dot_turned(down_grad, r.wc[...])
    up_grad = (act_grad * slope_cls).astype(LOW)
    steps_d[1]()
    hidden_grad = dot_turned(up_grad, r.wb[...]) + residual_grad
    first_grad, grad_g1, grad_s1 = norm_back_parts(
        hidden_grad, r.normed_one[...], inverse_one, vector(3)
    )
    attend_grad = first_grad.astype(LOW)
    context_grad = dot_turned(attend_grad, r.wa[:, 3 * WIDTH : 4 * WIDTH]).astype(LOW)
    attend_here = r.attends.at[here]
    attend_here[:, 0:WIDTH] = attend_grad
    attend_here[:, WIDTH : 2 * WIDTH] = context_grad
    steps_a[0]()
    steps_d[2]()
    context_tall = spread(context_grad)
    probs = r.probs[...]
    prob_grad = dot_turned(context_tall, r.qkv[:, values])
    inner = jnp.sum(probs * prob_grad, axis=1, keepdims=True)
    score_grad = (probs * (prob_grad - inner)).astype(LOW)
    steps_a[1]()
    r.mail_three[...] = pack_coefs(score_grad)
    post(r.mail_three, r.got_three, 3)
    query_grad = (fold(dot(score_grad, r.qkv[:, keys])) * scale).astype(LOW)
    probs_total = jnp.sum(probs_low.astype(FULL), axis=1, keepdims=True)
    grad_bvalue = jnp.sum(probs_total * context_tall.astype(FULL), axis=0, keepdims=True)
    grad_bquery = jnp.sum(query_grad.astype(FULL), axis=0, keepdims=True)
    r.queries[here] = query_grad
    own_sums = jnp.concatenate(
        [grad_bquery, grad_bvalue, grad_g1, grad_s1, grad_g2, grad_s2]
        + [jnp.zeros((128 - 6, WIDTH), FULL)],
        axis=0,
    )
    own_sums = jnp.transpose(own_sums)[:, 0 : 128 - 2 * depth]
    steps_q[0]()
    steps_a[2]()
    pack_tall(dot(score_grad, r.embedded[...]) * scale, r.mail_two, 0, own_sums)
    steps_q[1]()
    post(r.mail_two, r.got_two, 2)

    def all_rows(buffer, start):
        return buffer[:, :, :, :, start : start + WIDTH].reshape(SLOT_ROWS, WIDTH)

    def from_sent(group):
        lanes = iota((SLOT_ROWS, SLOT_ROWS), 1).astype(FULL)
        return (r.found[group, :, 1:2] == lanes).astype(LOW)

    def widened(coefs, group):
        lanes = iota((128, WIDTH), 0) == iota((128, WIDTH), 1) // HEAD + group * PAD
        return dot(coefs, lanes.astype(LOW))

    half_wide = WIDE // 2

    def slope_tile(part):
        at = pl.ds(pl.multiple_of(core * half_wide + part * BLOCK, BLOCK), BLOCK)
        up_pre = dot(all_rows(r.early, 0), r.wb[:, at]) + r.up_bias[0:1, at]
        _, slope = gelu_parts(up_pre)
        r.slopes[:, pl.ds(pl.multiple_of(part * BLOCK, BLOCK), BLOCK)] = slope.astype(LOW)

    def slot_queries(group):
        r.slot_query[group] = dot(from_sent(group), all_rows(r.early, WIDTH)).astype(LOW)

    def activate():
        at = pl.ds(pl.multiple_of(chip // 2 * 2 * deep, 128), 2 * deep)
        up_pre = dot(all_rows(r.early, 0), r.wb[:, at]) + r.up_bias[0:1, at]
        r.active_turned[...] = jnp.transpose(gelu(up_pre)).astype(LOW)
        r.hidden_turned[...] = jnp.transpose(all_rows(r.early, 0))

    between = [partial(slot_queries, group) for group in range(GROUPS)]
    between += [partial(every, part, part + 1, slope_tile) for part in range(6)]
    between.append(activate)

    between += late
    late.clear()
    rest = [steps_d[3], steps_a[3], steps_q[2], steps_d[4], steps_a[4], steps_q[3]]
    rest += [steps_d[5], steps_a[5], steps_q[4]]
    for step in rest:
        step()
        fill(between, 2)
    fill(between, len(between))

    all_but_one(r.got_one, 1).wait_recv()
    got_probs = r.got_one[:, 64:80, :].reshape(SLOT_ROWS, 128)
    for group in range(GROUPS):
        slot_context = dot(from_sent(group), all_rows(r.attends, WIDTH))
        r.replies[group] = (widened(got_probs, group) * slot_context).astype(LOW)

    def head_products(got, first_row, right, start, target):
        for pair in range(HEADS // 4):
            lane = pl.ds(pl.multiple_of(start + (core * (HEADS // 4) + pair) * 128, 128), 128)
            pair_rows = right[:, :, :, :, lane].reshape(SLOT_ROWS, 128)
            parts = []
            for half in range(2):
                head = 2 * pair + half
                row = first_row + head % 3 * PAD
                block_rows = got[:, row : row + PAD, :].reshape(SLOT_ROWS, 128)
                product = contract(block_rows, pair_rows, 0, 0)
                column = head // 3 * depth
                parts.append(product[column : column + depth, :])
            low_lanes = iota((depth, 128), 1) < HEAD
            result = jnp.where(low_lanes, parts[0], parts[1])
            target[:, pl.ds(pl.multiple_of((core * (HEADS // 4) + pair) * 128, 128), 128)] = result

    def half_of(ref, at_core):
        half = ref.shape[1] // 2
        return ref.at[:, pl.ds(pl.multiple_of(at_core * half, 128), half)]

    def half_copy(index, ref, at_core):
        part = half_of(ref, at_core)
        return remote(part, part, r.half_send.at[index], r.half_recv.at[index], 1 - core, chip)

    head_products(r.got_one, PAD, r.attends, WIDTH, r.g_wv)
    half_copy(0, r.g_wv, core).start()

    downs = r.downs[...].reshape(SLOT_ROWS, WIDTH)
    attends = all_rows(r.attends, 0)

    def up_tile(part):
        at = pl.ds(pl.multiple_of(core * half_wide + part * BLOCK, BLOCK), BLOCK)
        slope = r.slopes[:, pl.ds(pl.multiple_of(part * BLOCK, BLOCK), BLOCK)].astype(FULL)
        up_all = (dot_turned(r.downs[...].reshape(SLOT_ROWS, WIDTH), r.wc[at, :]) * slope)
        up_all = up_all.astype(LOW)
        r.g_wup[0:depth, at] = dot(r.hidden_turned[mine, :], up_all)
        total = jnp.sum(up_all.astype(FULL), axis=0, keepdims=True)
        r.g_wup[depth : depth + 8, at] = jnp.broadcast_to(total, (8, BLOCK))

    every(0, half_wide // BLOCK, up_tile)
    half_copy(1, r.g_wup, core).start()
    r.g_wdown[...] = dot(r.active_turned[pl.ds(pl.multiple_of(chip % 2 * deep, 16), deep), :], downs)
    r.left_turned[...] = jnp.transpose(r.got_one[:, 0:PAD, :].reshape(SLOT_ROWS, 128))
    r.g_wo[...] = dot(r.left_turned[0:depth, :], attends)
    own_lanes = (iota((WIDTH, 128), 0) == chip * depth + iota((WIDTH, 128), 1)).astype(LOW)

    def own_part(rows, select):
        total = None
        for _ in range(3):
            part = rows.astype(LOW)
            rows = rows - part.astype(FULL)
            picked = dot(part, select)
            total = picked if total is None else total + picked
        return total

    all_but_one(r.got_three, 3).wait_recv()
    got_scores = r.got_three[...].reshape(SLOT_ROWS, 128)
    for group in range(GROUPS):
        slot_query = r.slot_query[group].astype(FULL)
        key_grad = (widened(got_scores, group) * slot_query * scale).astype(LOW)
        row_grad = dot_turned(key_grad, r.wa[:, keys])
        row_grad = row_grad + dot_turned(r.replies[group], r.wa[:, values])
        r.rows[group] = row_grad.astype(LOW)
    steps_q[5]()
    query_grads = all_rows(r.queries, 0)
    extra = dot_turned(query_grads, r.wa[:, 0:WIDTH]) + attends.astype(FULL)
    r.extra[...] = extra.astype(LOW)
    r.g_wq[...] = dot(r.left_turned[depth : 2 * depth, :], query_grads)

    half_rows = VOCAB_ROWS // 2

    def table_copy(tile):
        at = pl.ds(pl.multiple_of(tile * half_rows, BLOCK), half_rows)
        return pltpu.make_async_copy(
            r.table_full.at[at], r.table_grad.at[at], r.table_sem.at[tile]
        )

    def table_tile(tile):
        at = pl.ds(pl.multiple_of(tile * half_rows, BLOCK), half_rows)
        for start in range(0, WIDTH, BLOCK):
            lanes = slice(start, start + BLOCK)
            slot_rows = r.rows[:, :, lanes].reshape(GROUPS * SLOT_ROWS, BLOCK)
            r.table_full[at, lanes] = dot(r.by_row[at, 0 : GROUPS * SLOT_ROWS], slot_rows) + dot(
                r.by_row[at, GROUPS * SLOT_ROWS :], r.extra[:, lanes]
            )
        table_copy(tile).start()

    every(0, 2, table_tile)
    all_but_one(r.got_two, 2).wait_recv()
    head_products(r.got_two, 0, r.early, WIDTH, r.g_wk)
    half_copy(2, r.g_wk, core).start()

    down_total = jnp.sum(downs.astype(FULL), axis=0, keepdims=True)
    attend_total = jnp.sum(attends.astype(FULL), axis=0, keepdims=True)
    sums = jnp.sum(r.got_two[...].astype(FULL), axis=0)
    sums = jnp.concatenate([sums, jnp.zeros((128 - 48, 128), FULL)], axis=0)
    stacked = jnp.concatenate([attend_total, down_total, jnp.zeros((6, WIDTH), FULL)], axis=0)
    r.g_small[8:16, 0:128] = own_part(stacked, own_lanes)
    r.g_small[0:8, 0:128] = jnp.transpose(sums)[2 * depth : 2 * depth + 8, :]
    r.g_small[0:16, 128:BLOCK] = jnp.zeros((PAD, BLOCK - 128), FULL)
    half_copy(1, r.g_wup, 1 - core).wait_recv()
    up_lanes = (iota((WIDE, BLOCK), 0) == chip * deep + iota((WIDE, BLOCK), 1)).astype(LOW)
    r.g_small[16:24, :] = own_part(r.g_wup[depth : depth + 8, :], up_lanes)

    half_copy(0, r.g_wv, 1 - core).wait_recv()
    half_copy(2, r.g_wk, 1 - core).wait_recv()
    for index, ref in enumerate([r.g_wv, r.g_wup, r.g_wk]):
        half_copy(index, ref, core).wait_send()

    for index, ref in enumerate([r.every_ids, r.got_one, r.got_two, r.got_three]):
        all_but_one(ref, index).wait_send()
    all_smalls().wait_send()
    for end in [drain_a, drain_b, drain_c, drain_u, drain_e, drain_d, drain_a2, drain_q]:
        end()
    for tile in range(TOKENS // BLOCK):
        layer_copy(tile).wait()
    every(0, 2, lambda tile: table_copy(tile).wait())


def layer(inputs):
    dma = pltpu.SemaphoreType.DMA
    vmem = pl.BlockSpec(memory_space=pltpu.VMEM)
    anywhere = pl.BlockSpec(memory_space=pl.ANY)
    depth, deep = WIDTH // CHIPS, WIDE // CHIPS

    def gathered(width):
        return pltpu.VMEM((CORES, PLANES, LINES, PAD, width), LOW)

    outputs = dict(
        layer_out=((TOKENS, WIDTH), LOW),
        table_grad=((VOCAB_ROWS, WIDTH), FULL),
        g_wq=((depth, WIDTH), FULL),
        g_wk=((depth, WIDTH), FULL),
        g_wv=((depth, WIDTH), FULL),
        g_wo=((depth, WIDTH), FULL),
        g_wup=((depth + 8, WIDE), FULL),
        g_wdown=((deep, WIDTH), FULL),
        g_small=((24, BLOCK), FULL),
        loss=((1, 1), FULL),
    )
    scratch = dict(
        ids=pltpu.VMEM((8, 128), jnp.int32),
        every_ids=pltpu.VMEM((DEVICES, 8, 128), jnp.int32),
        rank=pltpu.VMEM((DEVICES, TOKENS), FULL),
        code=pltpu.VMEM((DEVICES, TOKENS), FULL),
        found=pltpu.VMEM((GROUPS + 1, SLOT_ROWS, 2), FULL),
        block_bias=pltpu.VMEM((2 * BLOCK, BLOCK // 2), FULL),
        valid_bias=pltpu.VMEM((8, TOKENS), FULL),
        slot_col=pltpu.VMEM((TOKENS, 1), FULL),
        slot_line=pltpu.VMEM((8, TOKENS), FULL),
        valid_col=pltpu.VMEM((TOKENS, 1), FULL),
        valid_line=pltpu.VMEM((8, TOKENS), FULL),
        pairs=pltpu.VMEM((8, SLOT_ROWS), FULL),
        pairs_col=pltpu.VMEM((SLOT_ROWS, 128), FULL),
        vectors=pltpu.VMEM((PAD, WIDTH), FULL),
        up_bias=pltpu.VMEM((8, WIDE), FULL),
        qkv_bias=pltpu.VMEM((8, 3 * WIDTH), FULL),
        smalls=pltpu.VMEM((PAD, CHIPS * 128), LOW),
        wa=pltpu.VMEM((WIDTH, 4 * WIDTH), LOW),
        wb=pltpu.VMEM((WIDTH, WIDE), LOW),
        wc=pltpu.VMEM((WIDE, WIDTH), LOW),
        chosen=pltpu.VMEM((GROUPS, SLOT_ROWS, VOCAB_ROWS), LOW),
        by_row=pltpu.VMEM((VOCAB_ROWS, (GROUPS + 1) * SLOT_ROWS), LOW),
        rows=pltpu.VMEM((GROUPS, SLOT_ROWS, WIDTH), LOW),
        replies=pltpu.VMEM((GROUPS, SLOT_ROWS, WIDTH), LOW),
        slot_query=pltpu.VMEM((GROUPS, SLOT_ROWS, WIDTH), LOW),
        extra=pltpu.VMEM((SLOT_ROWS, WIDTH), LOW),
        embedded=pltpu.VMEM((TOKENS, WIDTH), LOW),
        qkv=pltpu.VMEM((TOKENS, 3 * WIDTH), LOW),
        context=pltpu.VMEM((TOKENS, WIDTH), LOW),
        table_full=pltpu.VMEM((VOCAB_ROWS, WIDTH), FULL),
        probs=pltpu.VMEM((PAIR_ROWS, TOKENS), FULL),
        normed_one=pltpu.VMEM((PAD, WIDTH), FULL),
        units=gathered(WIDTH),
        early=gathered(2 * WIDTH),
        downs=gathered(WIDTH),
        attends=gathered(2 * WIDTH),
        queries=gathered(WIDTH),
        slopes=pltpu.VMEM((SLOT_ROWS, WIDE // 2), LOW),
        hidden_turned=pltpu.VMEM((WIDTH, SLOT_ROWS), LOW),
        active_turned=pltpu.VMEM((2 * deep, SLOT_ROWS), LOW),
        left_turned=pltpu.VMEM((128, SLOT_ROWS), LOW),
        mail_one=pltpu.VMEM((DEVICES, 80, 128), LOW),
        got_one=pltpu.VMEM((DEVICES, 80, 128), LOW),
        mail_two=pltpu.VMEM((DEVICES, 48, 128), LOW),
        got_two=pltpu.VMEM((DEVICES, 48, 128), LOW),
        mail_three=pltpu.VMEM((DEVICES, PAD, 128), LOW),
        got_three=pltpu.VMEM((DEVICES, PAD, 128), LOW),
        rows_send=dma((4,)),
        rows_recv=dma((4,)),
        one_send=dma((4,)),
        one_recv=dma((4,)),
        small_send=dma((1,)),
        small_recv=dma((1,)),
        weight_send=dma((3, 33)),
        weight_recv=dma((3, 33)),
        gather_send=dma((5, 13)),
        gather_recv=dma((5, 13)),
        half_send=dma((3,)),
        half_recv=dma((3,)),
        out_sem=dma((TOKENS // BLOCK,)),
        table_sem=dma((2,)),
    )
    names = INPUTS + OUTPUTS + list(scratch)
    return pl.pallas_call(
        partial(layer_kernel, names),
        out_shape=tuple(jax.ShapeDtypeStruct(*outputs[name]) for name in OUTPUTS),
        in_specs=[vmem] * len(INPUTS),
        out_specs=(anywhere, anywhere) + (vmem,) * (len(OUTPUTS) - 2),
        scratch_shapes=list(scratch.values()),
        compiler_params=pltpu.CompilerParams(
            collective_id=0, has_side_effects=True, vmem_limit_bytes=VMEM_LIMIT
        ),
        name="layer",
    )(*inputs)


def finish_kernel(count, *refs):
    large, (small, loss), outs = refs[:count], refs[count : count + 2], refs[count + 2 : -1]
    sems = refs[-1]
    copies = []
    for index, (source, target) in enumerate(zip(large, outs)):
        part = source if source.shape == target.shape else source.at[: target.shape[0]]
        copies.append(pltpu.make_async_copy(part, target, sems.at[index]))
        copies[-1].start()
    for row, target in zip([0, 1, 8, 2, 3, 16, 9, 4, 5], outs[count : count + 9]):
        size = target.shape[0]
        target[...] = small[row : row + 1, 0:size].reshape(size)
    outs[-1][...] = loss[...].reshape(1)
    for one in copies:
        one.wait()


def finish(results):
    vmem = pl.BlockSpec(memory_space=pltpu.VMEM)
    anywhere = pl.BlockSpec(memory_space=pl.ANY)
    depth, deep = WIDTH // CHIPS, WIDE // CHIPS
    count = len(results) - 2
    shapes = [(one.shape, one.dtype) for one in results[:count]]
    shapes[6] = ((depth, WIDE), FULL)
    shapes += [((depth,), FULL)] * 5 + [((deep,), FULL)] + [((depth,), FULL)] * 3
    shapes.append(((1,), FULL))
    return pl.pallas_call(
        partial(finish_kernel, count),
        out_shape=tuple(jax.ShapeDtypeStruct(*one) for one in shapes),
        in_specs=[vmem] * (count + 2),
        out_specs=(anywhere,) * count + (vmem,) * 10,
        scratch_shapes=[pltpu.SemaphoreType.DMA((count,))],
        name="finish",
    )(*results)


def block_body(
    table,
    token_ids,
    sent_lengths,
    pair_slot,
    pair_lang,
    *parameters,
):
    results = finish(layer((table, token_ids, sent_lengths, pair_slot, pair_lang) + parameters))
    layer_out, table_grad, g_wq, g_wk, g_wv, g_wo, g_wup, g_wdown = results[:8]
    g_bq, g_bv, g_bo, g_g1, g_s1, g_bup, g_bdown, g_g2, g_s2, loss = results[8:]
    return (
        layer_out.reshape(token_ids.shape + (WIDTH,)),
        loss.reshape(()),
        table_grad,
        g_wq,
        g_bq,
        g_wk,
        g_wv,
        g_bv,
        g_wo,
        g_bo,
        g_g1,
        g_s1,
        g_wup,
        g_bup,
        g_wdown,
        g_bdown,
        g_g2,
        g_s2,
    )


def solution(mesh):
    in_specs = (
        P(("dp", "fsdp"), None),
        P(("dp", "fsdp"), None),
        P(("dp", "fsdp")),
        P(),
        P(),
        P("fsdp", None),
        P("fsdp"),
        P("fsdp", None),
        P("fsdp", None),
        P("fsdp"),
        P("fsdp", None),
        P("fsdp"),
        P("fsdp"),
        P("fsdp"),
        P("fsdp", None),
        P("fsdp"),
        P("fsdp", None),
        P("fsdp"),
        P("fsdp"),
        P("fsdp"),
    )
    out_specs = (
        P(("dp", "fsdp"), None, None),
        P(),
        P(("dp", "fsdp"), None),
        P("fsdp", None),
        P("fsdp"),
        P("fsdp", None),
        P("fsdp", None),
        P("fsdp"),
        P("fsdp", None),
        P("fsdp"),
        P("fsdp"),
        P("fsdp"),
        P("fsdp", None),
        P("fsdp"),
        P("fsdp", None),
        P("fsdp"),
        P("fsdp"),
        P("fsdp"),
    )
    sizes = dict(mesh.shape)
    body = general_body
    if sizes["dp"] == CORES and sizes["fsdp"] == CHIPS:
        body = block_body
    return jax.shard_map(body, mesh=mesh, in_specs=in_specs, out_specs=out_specs, check_vma=False)
```

```python
from functools import partial
from types import SimpleNamespace

import jax
import jax.numpy as jnp
from jax import lax
from jax.experimental import pallas as pl
from jax.experimental.pallas import tpu as pltpu
from jax.sharding import PartitionSpec as P

HEADS = 12
HEAD = 64
LANGS = 109


EPSILON = 1e-06
SCORE_SCALE = 50.0
MARGIN_WIDTH = 0.3
MASK_FLOOR = -1000000000.0


def contract(left_side, right_side, left_dim, right_dim):
    return lax.dot_general(
        left_side,
        right_side,
        (((left_dim,), (right_dim,)), ((), ())),
        preferred_element_type=jnp.float32,
    )


def norm_rows(inputs, ln_gain, ln_shift):
    row_mean = jnp.mean(inputs, axis=-1, keepdims=True)
    centered = inputs - row_mean
    variance = jnp.mean(centered * centered, axis=-1, keepdims=True)
    inverse = lax.rsqrt(variance + EPSILON)
    normed = centered * inverse
    return (normed * ln_gain + ln_shift, normed, inverse)


def norm_back(grad_output, normed, inverse, ln_gain):
    grad_normed = grad_output * ln_gain
    first_term = jnp.mean(grad_normed, axis=-1, keepdims=True)
    second_term = jnp.mean(grad_normed * normed, axis=-1, keepdims=True)
    grad_input = inverse * (grad_normed - first_term - normed * second_term)
    return (grad_input, jnp.sum(grad_output * normed, axis=0), jnp.sum(grad_output, axis=0))


def general_body(
    table,
    token_ids,
    sent_lengths,
    pair_slot,
    pair_lang,
    w_query,
    b_query,
    w_key,
    w_value,
    b_value,
    w_out,
    b_out,
    ln1_gain,
    ln1_bias,
    w_up,
    b_up,
    w_down,
    b_down,
    ln2_gain,
    ln2_bias,
):
    sentences, length = token_ids.shape
    tokens = sentences * length
    vocab_rows, model_width = table.shape
    owners = lax.axis_size(("dp", "fsdp"))
    dp_count = lax.axis_size("dp")
    fsdp_count = lax.axis_size("fsdp")
    capacity = max(2, 2 * tokens // owners)
    device = lax.axis_index(("dp", "fsdp"))
    score_factor = HEAD ** (-0.5)
    flat_ids = token_ids.reshape(tokens)
    owner_of = flat_ids // vocab_rows
    member = (owner_of[:, None] == jnp.arange(owners, dtype=jnp.int32)[None, :]).astype(jnp.int32)
    owner_rank = jnp.sum(jnp.cumsum(member, axis=0) * member, axis=1) - 1
    slot_of = owner_of * capacity + owner_rank
    requests = jnp.full((owners * capacity,), -1, jnp.int32).at[slot_of].set(flat_ids)
    received = lax.all_to_all(
        lax.all_to_all(
            requests.reshape(dp_count, fsdp_count, capacity),
            "dp",
            split_axis=0,
            concat_axis=0,
            tiled=True,
        ),
        "fsdp",
        split_axis=1,
        concat_axis=1,
        tiled=True,
    )
    present = received >= 0
    local_rows = jnp.where(present, received - device * vocab_rows, 0)
    found_rows = jnp.where(present[..., None], table[local_rows], jnp.zeros((), table.dtype))
    replies = lax.all_to_all(
        lax.all_to_all(found_rows, "dp", split_axis=0, concat_axis=0, tiled=True),
        "fsdp",
        split_axis=1,
        concat_axis=1,
        tiled=True,
    )
    embedded = replies.reshape(owners * capacity, model_width)[slot_of]
    gathered = (
        lax.all_gather(w_query, "fsdp", axis=0, tiled=True),
        lax.all_gather(b_query, "fsdp", axis=0, tiled=True),
        lax.all_gather(w_key, "fsdp", axis=0, tiled=True),
        lax.all_gather(w_value, "fsdp", axis=0, tiled=True),
        lax.all_gather(b_value, "fsdp", axis=0, tiled=True),
        lax.all_gather(w_out, "fsdp", axis=0, tiled=True),
        lax.all_gather(b_out, "fsdp", axis=0, tiled=True),
        lax.all_gather(ln1_gain, "fsdp", axis=0, tiled=True),
        lax.all_gather(ln1_bias, "fsdp", axis=0, tiled=True),
        lax.all_gather(w_up, "fsdp", axis=0, tiled=True),
        lax.all_gather(b_up, "fsdp", axis=0, tiled=True),
        lax.all_gather(w_down, "fsdp", axis=0, tiled=True),
        lax.all_gather(b_down, "fsdp", axis=0, tiled=True),
        lax.all_gather(ln2_gain, "fsdp", axis=0, tiled=True),
        lax.all_gather(ln2_bias, "fsdp", axis=0, tiled=True),
    )
    (
        full_wq,
        full_bq,
        full_wk,
        full_wv,
        full_bv,
        full_wo,
        full_bo,
        full_g1,
        full_s1,
        full_wup,
        full_bup,
        full_wdown,
        full_bdown,
        full_g2,
        full_s2,
    ) = gathered
    valid_mask = jnp.arange(length, dtype=jnp.int32)[None, :] < sent_lengths[:, None]
    head_shape = (sentences, length, HEADS, HEAD)
    queries = (jnp.dot(embedded, full_wq, preferred_element_type=jnp.float32) + full_bq).astype(
        jnp.bfloat16
    )
    key_heads = (
        jnp.dot(embedded, full_wk, preferred_element_type=jnp.float32)
        .astype(jnp.bfloat16)
        .reshape(head_shape)
    )
    value_heads = (
        (jnp.dot(embedded, full_wv, preferred_element_type=jnp.float32) + full_bv)
        .astype(jnp.bfloat16)
        .reshape(head_shape)
    )
    query_heads = queries.reshape(head_shape)
    scores = (
        jnp.einsum("bqhd,bkhd->bhqk", query_heads, key_heads, preferred_element_type=jnp.float32)
        * score_factor
    )
    scores = jnp.where(valid_mask[:, None, None, :], scores, MASK_FLOOR)
    row_peak = jnp.max(scores, axis=-1, keepdims=True)
    shifted = jnp.exp(scores - row_peak)
    totals = jnp.sum(shifted, axis=-1, keepdims=True)
    attn_probs = (shifted / totals).astype(jnp.bfloat16)
    context = jnp.einsum(
        "bhqk,bkhd->bqhd", attn_probs, value_heads, preferred_element_type=jnp.float32
    )
    context = context.reshape(tokens, model_width).astype(jnp.bfloat16)
    attended = jnp.dot(context, full_wo, preferred_element_type=jnp.float32) + full_bo
    hidden, normed_one, inverse_one = norm_rows(
        embedded.astype(jnp.float32) + attended, full_g1, full_s1
    )
    hidden_low = hidden.astype(jnp.bfloat16)
    up_pre = jnp.dot(hidden_low, full_wup, preferred_element_type=jnp.float32) + full_bup
    activated = jax.nn.gelu(up_pre, approximate=False).astype(jnp.bfloat16)
    down_pre = jnp.dot(activated, full_wdown, preferred_element_type=jnp.float32) + full_bdown
    normed_out, normed_two, inverse_two = norm_rows(hidden + down_pre, full_g2, full_s2)
    layer_out = jnp.where(valid_mask.reshape(tokens)[:, None], normed_out, 0.0).astype(jnp.bfloat16)
    layer_out = layer_out.reshape(sentences, length, model_width)

    def first_rows(matrix):
        return matrix.reshape(sentences, length, matrix.shape[-1])[:, 0]

    summary = first_rows(normed_out)
    magnitude = jnp.sqrt(jnp.sum(summary * summary, axis=-1, keepdims=True) + EPSILON)
    unit_vector = summary / magnitude
    unit_low = unit_vector.astype(jnp.bfloat16)
    every_unit = lax.all_gather(unit_low, ("dp", "fsdp"), axis=0, tiled=True)
    every_side = pair_slot % 2
    every_pair = pair_slot // 2
    my_slots = lax.dynamic_slice_in_dim(pair_slot, device * sentences, sentences)
    my_side = my_slots % 2
    my_pair = my_slots // 2
    lang_onehot = (pair_lang[:, None] == jnp.arange(LANGS, dtype=jnp.int32)[None, :]).astype(
        jnp.float32
    )
    per_lang = jnp.sum(lang_onehot, axis=0)
    per_pair = 1.0 / (2.0 * LANGS * jnp.sum(lang_onehot * per_lang[None, :], axis=1))
    my_weight = jnp.take(per_pair, my_pair)
    opposite = my_side[:, None] != every_side[None, :]
    partner = opposite & (my_pair[:, None] == every_pair[None, :])
    raw_scores = SCORE_SCALE * contract(unit_low, every_unit, 1, 1)
    pair_scores = jnp.where(partner, raw_scores - SCORE_SCALE * MARGIN_WIDTH, raw_scores)
    pair_scores = jnp.where(opposite, pair_scores, MASK_FLOOR)
    pair_peak = jnp.max(pair_scores, axis=1, keepdims=True)
    pair_exp = jnp.exp(pair_scores - pair_peak)
    pair_total = jnp.sum(pair_exp, axis=1, keepdims=True)
    log_total = pair_peak[:, 0] + jnp.log(pair_total[:, 0])
    picked = jnp.sum(jnp.where(partner, pair_scores, 0.0), axis=1)
    loss_value = lax.psum(jnp.sum(my_weight * (log_total - picked)), ("dp", "fsdp"))
    coefficients = (
        my_weight[:, None] * (pair_exp / pair_total - partner.astype(jnp.float32))
    ).astype(jnp.bfloat16)
    unit_grad = SCORE_SCALE * contract(coefficients, every_unit, 1, 0)
    column_terms = SCORE_SCALE * contract(coefficients, unit_low, 0, 0)
    unit_grad = unit_grad + lax.psum_scatter(
        column_terms, ("dp", "fsdp"), scatter_dimension=0, tiled=True
    )
    along = jnp.sum(unit_vector * unit_grad, axis=-1, keepdims=True)
    summary_grad = (unit_grad - unit_vector * along) / magnitude
    again_weights = (
        lax.all_gather(w_query, "fsdp", axis=0, tiled=True),
        lax.all_gather(w_key, "fsdp", axis=0, tiled=True),
        lax.all_gather(w_value, "fsdp", axis=0, tiled=True),
        lax.all_gather(w_out, "fsdp", axis=0, tiled=True),
        lax.all_gather(ln1_gain, "fsdp", axis=0, tiled=True),
        lax.all_gather(w_up, "fsdp", axis=0, tiled=True),
        lax.all_gather(w_down, "fsdp", axis=0, tiled=True),
        lax.all_gather(ln2_gain, "fsdp", axis=0, tiled=True),
    )
    again_wq, again_wk, again_wv, again_wo, again_g1, again_wup, again_wdown, again_g2 = (
        again_weights
    )
    residual_grad, grad_g2, grad_s2 = norm_back(
        summary_grad, first_rows(normed_two), first_rows(inverse_two), again_g2
    )
    down_grad = residual_grad.astype(jnp.bfloat16)
    activated_cls = first_rows(activated)
    act_grad = contract(down_grad, again_wdown, 1, 1)
    gelu_value, gelu_pull = jax.vjp(partial(jax.nn.gelu, approximate=False), first_rows(up_pre))
    up_grad = gelu_pull(act_grad)[0].astype(jnp.bfloat16)
    hidden_cls = first_rows(hidden_low)
    hidden_grad = contract(up_grad, again_wup, 1, 1) + residual_grad
    first_grad, grad_g1, grad_s1 = norm_back(
        hidden_grad, first_rows(normed_one), first_rows(inverse_one), again_g1
    )
    attend_grad = first_grad.astype(jnp.bfloat16)
    context_cls = first_rows(context)
    context_grad = (
        contract(attend_grad, again_wo, 1, 1).astype(jnp.bfloat16).reshape(sentences, HEADS, HEAD)
    )
    query_cls = query_heads[:, 0]
    cls_scores = (
        jnp.einsum("bhd,bkhd->bhk", query_cls, key_heads, preferred_element_type=jnp.float32)
        * score_factor
    )
    cls_scores = jnp.where(valid_mask[:, None, :], cls_scores, MASK_FLOOR)
    cls_probs = jnp.exp(cls_scores - row_peak[:, :, 0]) / totals[:, :, 0]
    prob_grad = jnp.einsum(
        "bhd,bkhd->bhk", context_grad, value_heads, preferred_element_type=jnp.float32
    )
    score_grad = (
        cls_probs * (prob_grad - jnp.sum(cls_probs * prob_grad, axis=-1, keepdims=True))
    ).astype(jnp.bfloat16)
    query_grad = (
        (
            jnp.einsum("bhk,bkhd->bhd", score_grad, key_heads, preferred_element_type=jnp.float32)
            * score_factor
        )
        .astype(jnp.bfloat16)
        .reshape(sentences, model_width)
    )
    key_grad = (
        (
            jnp.einsum("bhk,bhd->bkhd", score_grad, query_cls, preferred_element_type=jnp.float32)
            * score_factor
        )
        .astype(jnp.bfloat16)
        .reshape(tokens, model_width)
    )
    value_grad = (
        jnp.einsum(
            "bhk,bhd->bkhd",
            cls_probs.astype(jnp.bfloat16),
            context_grad,
            preferred_element_type=jnp.float32,
        )
        .astype(jnp.bfloat16)
        .reshape(tokens, model_width)
    )
    embedded_cls = first_rows(embedded)
    grad_wkey = contract(embedded, key_grad, 0, 0)
    grad_wvalue = contract(embedded, value_grad, 0, 0)
    grad_bvalue = jnp.sum(value_grad, axis=0, dtype=jnp.float32)
    row_grads = contract(key_grad, again_wk, 1, 1) + contract(value_grad, again_wv, 1, 1)
    summary_extra = contract(query_grad, again_wq, 1, 1) + first_grad
    row_grads = (
        row_grads.reshape(sentences, length, model_width)
        .at[:, 0]
        .add(summary_extra)
        .reshape(tokens, model_width)
    )
    outgoing = jnp.zeros((owners * capacity, model_width), jnp.float32).at[slot_of].set(row_grads)
    incoming = lax.all_to_all(
        lax.all_to_all(
            outgoing.reshape(dp_count, fsdp_count, capacity, model_width).astype(jnp.bfloat16),
            "dp",
            split_axis=0,
            concat_axis=0,
            tiled=True,
        ),
        "fsdp",
        split_axis=1,
        concat_axis=1,
        tiled=True,
    ).astype(jnp.float32)
    incoming = jnp.where(
        present.reshape(owners * capacity)[:, None],
        incoming.reshape(owners * capacity, model_width),
        0.0,
    )
    table_grad = (
        jnp.zeros((vocab_rows, model_width), jnp.float32)
        .at[local_rows.reshape(owners * capacity)]
        .add(incoming)
    )
    grad_wquery = contract(embedded_cls, query_grad, 0, 0)
    grad_bquery = jnp.sum(query_grad, axis=0, dtype=jnp.float32)
    grad_wout = contract(context_cls, attend_grad, 0, 0)
    grad_bout = jnp.sum(attend_grad, axis=0, dtype=jnp.float32)
    grad_wup = contract(hidden_cls, up_grad, 0, 0)
    grad_bup = jnp.sum(up_grad, axis=0, dtype=jnp.float32)
    grad_wdown = contract(activated_cls, down_grad, 0, 0)
    grad_bdown = jnp.sum(down_grad, axis=0, dtype=jnp.float32)
    owned_grads = (
        lax.psum_scatter(
            grad_wquery.astype(jnp.bfloat16), "fsdp", scatter_dimension=0, tiled=True
        ).astype(jnp.float32),
        lax.psum_scatter(
            grad_bquery.astype(jnp.bfloat16), "fsdp", scatter_dimension=0, tiled=True
        ).astype(jnp.float32),
        lax.psum_scatter(
            grad_wkey.astype(jnp.bfloat16), "fsdp", scatter_dimension=0, tiled=True
        ).astype(jnp.float32),
        lax.psum_scatter(
            grad_wvalue.astype(jnp.bfloat16), "fsdp", scatter_dimension=0, tiled=True
        ).astype(jnp.float32),
        lax.psum_scatter(
            grad_bvalue.astype(jnp.bfloat16), "fsdp", scatter_dimension=0, tiled=True
        ).astype(jnp.float32),
        lax.psum_scatter(
            grad_wout.astype(jnp.bfloat16), "fsdp", scatter_dimension=0, tiled=True
        ).astype(jnp.float32),
        lax.psum_scatter(
            grad_bout.astype(jnp.bfloat16), "fsdp", scatter_dimension=0, tiled=True
        ).astype(jnp.float32),
        lax.psum_scatter(
            grad_g1.astype(jnp.bfloat16), "fsdp", scatter_dimension=0, tiled=True
        ).astype(jnp.float32),
        lax.psum_scatter(
            grad_s1.astype(jnp.bfloat16), "fsdp", scatter_dimension=0, tiled=True
        ).astype(jnp.float32),
        lax.psum_scatter(
            grad_wup.astype(jnp.bfloat16), "fsdp", scatter_dimension=0, tiled=True
        ).astype(jnp.float32),
        lax.psum_scatter(
            grad_bup.astype(jnp.bfloat16), "fsdp", scatter_dimension=0, tiled=True
        ).astype(jnp.float32),
        lax.psum_scatter(
            grad_wdown.astype(jnp.bfloat16), "fsdp", scatter_dimension=0, tiled=True
        ).astype(jnp.float32),
        lax.psum_scatter(
            grad_bdown.astype(jnp.bfloat16), "fsdp", scatter_dimension=0, tiled=True
        ).astype(jnp.float32),
        lax.psum_scatter(
            grad_g2.astype(jnp.bfloat16), "fsdp", scatter_dimension=0, tiled=True
        ).astype(jnp.float32),
        lax.psum_scatter(
            grad_s2.astype(jnp.bfloat16), "fsdp", scatter_dimension=0, tiled=True
        ).astype(jnp.float32),
    )
    summed = (
        lax.psum(owned_grads[0].astype(jnp.bfloat16), "dp").astype(jnp.float32),
        lax.psum(owned_grads[1].astype(jnp.bfloat16), "dp").astype(jnp.float32),
        lax.psum(owned_grads[2].astype(jnp.bfloat16), "dp").astype(jnp.float32),
        lax.psum(owned_grads[3].astype(jnp.bfloat16), "dp").astype(jnp.float32),
        lax.psum(owned_grads[4].astype(jnp.bfloat16), "dp").astype(jnp.float32),
        lax.psum(owned_grads[5].astype(jnp.bfloat16), "dp").astype(jnp.float32),
        lax.psum(owned_grads[6].astype(jnp.bfloat16), "dp").astype(jnp.float32),
        lax.psum(owned_grads[7].astype(jnp.bfloat16), "dp").astype(jnp.float32),
        lax.psum(owned_grads[8].astype(jnp.bfloat16), "dp").astype(jnp.float32),
        lax.psum(owned_grads[9].astype(jnp.bfloat16), "dp").astype(jnp.float32),
        lax.psum(owned_grads[10].astype(jnp.bfloat16), "dp").astype(jnp.float32),
        lax.psum(owned_grads[11].astype(jnp.bfloat16), "dp").astype(jnp.float32),
        lax.psum(owned_grads[12].astype(jnp.bfloat16), "dp").astype(jnp.float32),
        lax.psum(owned_grads[13].astype(jnp.bfloat16), "dp").astype(jnp.float32),
        lax.psum(owned_grads[14].astype(jnp.bfloat16), "dp").astype(jnp.float32),
    )
    return (
        layer_out,
        loss_value,
        table_grad,
        summed[0],
        summed[1],
        summed[2],
        summed[3],
        summed[4],
        summed[5],
        summed[6],
        summed[7],
        summed[8],
        summed[9],
        summed[10],
        summed[11],
        summed[12],
        summed[13],
        summed[14],
    )


CORES = 2
PLANES = 4
LINES = 4
CHIPS = PLANES * LINES
DEVICES = CORES * CHIPS
CAPACITY = 48
GROUPS = 3
PAD = 16
TOKENS = 768
WIDTH = 768
WIDE = 3072
VOCAB_ROWS = 1024
PAIR_ROWS = HEADS * PAD
SLOT_ROWS = DEVICES * PAD
LONG = 64
BLOCK = 256
MESH = pl.DeviceIdType.MESH
LOW = jnp.bfloat16
FULL = jnp.float32
VMEM_LIMIT = 62 * 1024 * 1024

INPUTS = ["table", "token_ids", "lens", "slots", "langs"]
INPUTS += ["wq", "bq", "wk", "wv", "bv", "wo", "bo", "g1", "s1", "wup", "bup", "wdown", "bdown"]
INPUTS += ["g2", "s2"]
OUTPUTS = ["layer_out", "table_grad", "g_wq", "g_wk", "g_wv", "g_wo", "g_wup", "g_wdown"]
OUTPUTS += ["g_small", "loss"]


def place():
    core = lax.axis_index("dp")
    chip = lax.axis_index("fsdp")
    along_x = chip + 1 - 2 * (chip % 2)
    along_y = chip + 2 - 4 * ((chip // 2) % 2)
    first = along_x + core * (along_y - along_x)
    second = along_y + core * (along_x - along_y)
    return core, chip, first, second


def greet():
    core, chip, _, _ = place()
    me = core * CHIPS + chip
    barrier = pltpu.get_barrier_semaphore()

    def signal(step):
        other = lax.rem(me + step, DEVICES)
        pl.semaphore_signal(
            barrier,
            inc=1,
            device_id=(lax.div(other, CHIPS), lax.rem(other, CHIPS)),
            device_id_type=MESH,
        )

    every(1, DEVICES, signal)


def enter():
    pl.semaphore_wait(pltpu.get_barrier_semaphore(), DEVICES - 1)


def remote(source, target, send_sem, recv_sem, core, chip):
    return pltpu.make_async_remote_copy(
        src_ref=source,
        dst_ref=target,
        send_sem=send_sem,
        recv_sem=recv_sem,
        device_id=(core, chip),
        device_id_type=MESH,
    )


def every(start, stop, act):
    def step(index, carry):
        act(index)
        return carry

    lax.fori_loop(start, stop, step, 0)


def weight_steps(buffer, depth, send, recv):
    core, chip, first, second = place()
    plane, line = chip // LINES, chip % LINES
    line_first, line_second = first % LINES, second % LINES
    line_far = line_first + line_second - line
    is_low, is_high = plane > 0, plane < PLANES - 1
    half = buffer.shape[1] // 2
    by_place = buffer.reshape(PLANES, LINES, depth, buffer.shape[1])
    columns = pl.ds(pl.multiple_of(core * half, 128), half)
    others = pl.ds(pl.multiple_of((1 - core) * half, 128), half)

    def copy(send_index, recv_index, part, to_core, to_chip):
        return remote(part, part, send.at[send_index], recv.at[recv_index], to_core, to_chip)

    def piece(at_plane, which):
        return by_place.at[at_plane, line, :, which]

    def lines(at_line, which):
        return by_place.at[:, at_line, :, which]

    def up(at_plane):
        return copy(at_plane, at_plane, piece(at_plane, columns), core, chip + LINES)

    def down(at_plane, index):
        return copy(index, at_plane, piece(at_plane, columns), core, chip - LINES)

    def begin():
        pl.when(is_high)(lambda: up(plane).start())
        pl.when(is_low)(lambda: down(plane, PLANES).start())

    def chain(distance):
        def from_low():
            up(plane - distance).wait_recv()
            pl.when(is_high)(lambda: up(plane - distance).start())

        def from_high():
            at = plane + distance
            down(at, at).wait_recv()
            pl.when(is_low)(lambda: down(at, at).start())

        pl.when(plane >= distance)(from_low)
        pl.when(plane + distance < PLANES)(from_high)

    def across(step, which):
        at = (plane + step) % PLANES
        return copy(7 + step, 7 + step, piece(at, which), 1 - core, chip)

    def sides():
        copy(5, 5, lines(line, columns), core, first).start()
        copy(6, 6, lines(line, columns), core, second).start()
        for step in range(1, PLANES):
            across(step, columns).start()

    def corner():
        copy(5, 5, lines(line_first, columns), core, first).wait_recv()
        copy(7, 7, lines(line_first, columns), core, second).start()
        copy(11, 11, lines(line_first, columns), 1 - core, chip).start()
        copy(6, 6, lines(line_second, columns), core, second).wait_recv()
        copy(12, 12, lines(line_second, columns), 1 - core, chip).start()

    def last():
        copy(7, 7, lines(line_far, columns), core, second).wait_recv()
        copy(13, 13, lines(line_far, columns), 1 - core, chip).start()

    def finish():
        for step in range(1, PLANES):
            across(step, others).wait_recv()
        copy(11, 11, lines(line_second, others), 1 - core, chip).wait_recv()
        copy(12, 12, lines(line_first, others), 1 - core, chip).wait_recv()
        copy(13, 13, lines(line_far, others), 1 - core, chip).wait_recv()

    def drain():
        def sent(index):
            copy(index, index, piece(plane, columns), 1 - core, chip).wait_send()

        for at_plane in range(PLANES):
            pl.when((plane >= at_plane) & is_high)(partial(sent, at_plane))
            pl.when((plane < at_plane) & is_low)(partial(sent, at_plane))
        pl.when(is_low)(partial(sent, PLANES))
        every(8, 11, sent)
        for index in [5, 6, 7, 11, 12, 13]:
            copy(index, index, lines(line, columns), 1 - core, chip).wait_send()

    steps = SimpleNamespace(
        begin=begin, chain=chain, sides=sides, corner=corner, last=last, finish=finish
    )
    return steps, drain


def gather_steps(buffer, send, recv):
    core, chip, first, second = place()
    plane, line = chip // LINES, chip % LINES
    line_first, line_second = first % LINES, second % LINES
    line_far = line_first + line_second - line
    half = buffer.shape[-1] // 2
    columns = pl.ds(pl.multiple_of(core * half, 128), half)
    others = pl.ds(pl.multiple_of((1 - core) * half, 128), half)

    def copy(index, part, to_core, to_chip):
        return remote(part, part, send.at[index], recv.at[index], to_core, to_chip)

    def own(at):
        return buffer.at[at, plane, line]

    def chip_part(at_plane, at_line, which):
        return buffer.at[:, at_plane, at_line, :, which]

    def line_part(at_line, which):
        return buffer.at[:, :, at_line, :, which]

    def start():
        copy(0, own(core), 1 - core, chip).start()

    def planes():
        copy(0, own(1 - core), 1 - core, chip).wait_recv()
        for step in range(1, PLANES):
            part = chip_part(plane, line, columns)
            copy(step, part, core, (chip + LINES * step) % CHIPS).start()

    def sides():
        for step in range(1, PLANES):
            part = chip_part((plane + PLANES - step) % PLANES, line, columns)
            copy(step, part, core, chip).wait_recv()
        copy(4, line_part(line, columns), core, first).start()
        copy(5, line_part(line, columns), core, second).start()
        for step in range(1, PLANES):
            part = chip_part((plane + PLANES - step) % PLANES, line, columns)
            copy(6 + step, part, 1 - core, chip).start()

    def corner():
        copy(4, line_part(line_first, columns), core, first).wait_recv()
        copy(6, line_part(line_first, columns), core, second).start()
        copy(10, line_part(line_first, columns), 1 - core, chip).start()
        copy(5, line_part(line_second, columns), core, second).wait_recv()
        copy(11, line_part(line_second, columns), 1 - core, chip).start()

    def last():
        copy(6, line_part(line_far, columns), core, second).wait_recv()
        copy(12, line_part(line_far, columns), 1 - core, chip).start()

    def finish():
        for step in range(1, PLANES):
            part = chip_part((plane + PLANES - step) % PLANES, line, others)
            copy(6 + step, part, 1 - core, chip).wait_recv()
        copy(10, line_part(line_second, others), 1 - core, chip).wait_recv()
        copy(11, line_part(line_first, others), 1 - core, chip).wait_recv()
        copy(12, line_part(line_far, others), 1 - core, chip).wait_recv()

    def drain():
        copy(0, own(core), 1 - core, chip).wait_send()
        for index in [1, 2, 3, 7, 8, 9]:
            copy(index, chip_part(plane, line, columns), 1 - core, chip).wait_send()
        for index in [4, 5, 6, 10, 11, 12]:
            copy(index, line_part(line, columns), 1 - core, chip).wait_send()

    return [start, planes, sides, corner, last, finish], drain


def iota(shape, axis):
    return lax.broadcasted_iota(jnp.int32, shape, axis)


def as_column(row):
    parts = []
    for start in range(0, row.shape[1], 128):
        tile = jnp.broadcast_to(row[:, start : start + 128], (128, 128))
        parts.append(jnp.transpose(tile)[:, 0:1])
    return jnp.concatenate(parts, axis=0)


def as_row(column):
    parts = []
    for start in range(0, column.shape[0], 128):
        tile = jnp.broadcast_to(column[start : start + 128, :], (128, 128))
        parts.append(jnp.transpose(tile)[0:1, :])
    return jnp.concatenate(parts, axis=1)


def dot(left_side, right_side):
    return contract(left_side, right_side, 1, 0)


def dot_turned(left_side, right_side):
    return contract(left_side, right_side, 1, 1)


def norm_parts(inputs):
    centered = inputs - jnp.mean(inputs, axis=-1, keepdims=True)
    inverse = lax.rsqrt(jnp.mean(centered * centered, axis=-1, keepdims=True) + EPSILON)
    return centered * inverse, inverse


def norm_back_parts(grad_output, normed, inverse, ln_gain):
    grad_normed = grad_output * ln_gain
    first_term = jnp.mean(grad_normed, axis=-1, keepdims=True)
    second_term = jnp.mean(grad_normed * normed, axis=-1, keepdims=True)
    return (
        inverse * (grad_normed - first_term - normed * second_term),
        jnp.sum(grad_output * normed, axis=0, keepdims=True),
        jnp.sum(grad_output, axis=0, keepdims=True),
    )


def erf_parts(inputs):
    decay = jnp.exp(-0.5 * inputs * inputs)
    share = 1.0 / (1.0 + jnp.abs(inputs) * (0.3275911 * 0.5**0.5))
    terms = [1.061405429, -1.453152027, 1.421413741, -0.284496736, 0.254829592]
    series = 0.5 * terms[0]
    for term in terms[1:]:
        series = series * share + 0.5 * term
    tail = series * share * decay
    return jnp.where(inputs >= 0.0, 1.0 - tail, tail), decay


def gelu_parts(inputs):
    below, decay = erf_parts(inputs)
    return inputs * below, below + inputs * decay * ((2.0 * 3.141592653589793) ** -0.5)


def gelu(inputs):
    return inputs * erf_parts(inputs)[0]


def layer_kernel(names, *refs):
    r = SimpleNamespace(**dict(zip(names, refs, strict=True)))
    core, chip, _, _ = place()
    me = core * CHIPS + chip
    here = (core, chip // LINES, chip % LINES)
    scale = HEAD ** (-0.5)
    depth, deep = WIDTH // CHIPS, WIDE // CHIPS
    sentences = TOKENS // LONG

    for j in range(TOKENS // 128):
        r.ids[j : j + 1, :] = jnp.concatenate(
            [r.token_ids[2 * j : 2 * j + 1, :], r.token_ids[2 * j + 1 : 2 * j + 2, :]], axis=1
        )
    r.ids[TOKENS // 128 : 8, :] = jnp.zeros((8 - TOKENS // 128, 128), jnp.int32)
    greet()
    ahead = (iota((TOKENS, TOKENS), 0) < iota((TOKENS, TOKENS), 1)).astype(LOW)
    r.embedded[...] = ahead
    mine = pl.ds(pl.multiple_of(chip * depth, 16), depth)
    for index, shard in enumerate([r.wq, r.wk, r.wv, r.wo]):
        r.wa[mine, index * WIDTH : (index + 1) * WIDTH] = shard[...]
    r.wb[mine, :] = r.wup[...]
    r.wc[pl.ds(pl.multiple_of(chip * deep, 16), deep), :] = r.wdown[...]
    r.every_ids[me] = r.ids[...]
    enter()

    def peer(step):
        other = lax.rem(me + step, DEVICES)
        return other, lax.div(other, CHIPS), lax.rem(other, CHIPS)

    def ids_copy(step):
        other, to_core, to_chip = peer(step)
        return remote(r.ids, r.every_ids.at[me], r.one_send.at[0], r.one_recv.at[0], to_core, to_chip)

    def all_but_one(ref, index):
        part = ref.at[0 : DEVICES - 1]
        return remote(part, part, r.one_send.at[index], r.one_recv.at[index], 1 - core, chip)

    every(1, DEVICES, lambda step: ids_copy(step).start())

    a_steps, drain_a = weight_steps(r.wa, depth, r.weight_send.at[0], r.weight_recv.at[0])
    b_steps, drain_b = weight_steps(r.wb, depth, r.weight_send.at[1], r.weight_recv.at[1])
    c_steps, drain_c = weight_steps(r.wc, deep, r.weight_send.at[2], r.weight_recv.at[2])
    a_steps.begin()
    b_steps.begin()
    c_steps.begin()

    all_but_one(r.every_ids, 0).wait_recv()
    all_ids = jnp.concatenate([r.every_ids[:, j, :] for j in range(TOKENS // 128)], axis=1)
    all_owner = all_ids // VOCAB_ROWS
    asked = all_owner == me
    ranks = dot(asked.astype(LOW), r.embedded[...])
    r.rank[...] = jnp.where(asked, ranks, -1.0)
    local_row = (all_ids - all_owner * VOCAB_ROWS + 1).astype(FULL)
    r.code[...] = local_row + (iota((DEVICES, TOKENS), 1) // LONG * 2048).astype(FULL)

    quarter_size = DEVICES // 4

    def rows_copy(other, quarter):
        return remote(
            r.rows.at[:, pl.ds(pl.multiple_of(other * PAD, 16), PAD), :],
            r.replies.at[:, pl.ds(pl.multiple_of(me * PAD, 16), PAD), :],
            r.rows_send.at[quarter],
            r.rows_recv.at[quarter],
            lax.div(other, CHIPS),
            lax.rem(other, CHIPS),
        )

    def rows_of(quarter):
        count = quarter_size - 1 if quarter == 3 else quarter_size
        part = r.replies.at[:, 0 : count * PAD, :]
        return remote(
            part, part, r.rows_send.at[quarter], r.rows_recv.at[quarter], 1 - core, chip
        )

    def pick(source):
        rank = r.rank[pl.ds(source, 1), :]
        code = r.code[pl.ds(source, 1), :]
        here_at = iota((CAPACITY, TOKENS), 0).astype(FULL) == rank
        found = jnp.sum(jnp.where(here_at, code, 0.0), axis=1, keepdims=True)
        sent = jnp.floor(found * (1.0 / 2048))
        row = found - sent * 2048.0 - 1.0
        chosen = (iota((CAPACITY, VOCAB_ROWS), 1).astype(FULL) == row).astype(LOW)
        at = pl.ds(pl.multiple_of(source * PAD, 16), PAD)
        source_sent = sent + (source * PAD).astype(FULL)
        for group in range(GROUPS):
            part = slice(group * PAD, (group + 1) * PAD)
            r.chosen[group, at, :] = chosen[part]
            r.found[group, at, 0:1] = row[part]
            r.found[group, at, 1:2] = source_sent[part]

    for quarter in range(4):
        now = lax.rem(lax.div(me, quarter_size) + 1 + quarter, 4)

        def pick_two(index):
            pick(now * quarter_size + 2 * index)
            pick(now * quarter_size + 2 * index + 1)

        every(0, quarter_size // 2, pick_two)
        span = pl.ds(pl.multiple_of(now * quarter_size * PAD, 128), quarter_size * PAD)
        picked = r.chosen[:, span, :].reshape(GROUPS * quarter_size * PAD, VOCAB_ROWS)
        found_rows = dot(picked, r.table[...]).astype(LOW)
        r.rows[:, span, :] = found_rows.reshape(GROUPS, quarter_size * PAD, WIDTH)

        def send(index):
            other = now * quarter_size + lax.rem(lax.rem(me, quarter_size) + index, quarter_size)
            rows_copy(other, quarter).start()

        every(1 if quarter == 3 else 0, quarter_size, send)
        [
            lambda: a_steps.chain(1),
            lambda: b_steps.chain(1),
            lambda: (c_steps.chain(1), a_steps.chain(2)),
            lambda: (b_steps.chain(2), c_steps.chain(2)),
        ][quarter]()
    a_steps.chain(3)
    a_steps.sides()
    own_at = pl.ds(pl.multiple_of(me * PAD, 16), PAD)
    r.replies[:, own_at, :] = r.rows[:, own_at, :]

    small_here = pl.ds(pl.multiple_of(chip * 128, 128), 128)
    lines = [r.bq, r.bv, r.bo, r.g1, r.s1, r.bdown, r.g2, r.s2]
    lines = [line[...].reshape(1, depth).astype(FULL) for line in lines]
    up_line = r.bup[...].reshape(1, deep).astype(FULL)
    lines += [up_line[:, part * depth : (part + 1) * depth] for part in range(deep // depth)]
    lines.append(jnp.zeros((PAD - len(lines), depth), FULL))
    own_small = jnp.concatenate(lines, axis=0)
    own_small = jnp.concatenate([own_small, jnp.zeros((PAD, 128 - depth), FULL)], axis=1)
    r.smalls[:, small_here] = own_small.astype(LOW)

    def small_copy(step):
        part = r.smalls.at[:, small_here]
        to_chip = lax.rem(chip + step, CHIPS)
        return remote(part, part, r.small_send.at[0], r.small_recv.at[0], core, to_chip)

    def all_smalls():
        part = r.smalls.at[:, 0 : (CHIPS - 1) * 128]
        return remote(part, part, r.small_send.at[0], r.small_recv.at[0], 1 - core, chip)

    every(1, CHIPS, lambda step: small_copy(step).start())
    b_steps.chain(3)
    b_steps.sides()

    own_row = jnp.concatenate([r.ids[j : j + 1, :] for j in range(TOKENS // 128)], axis=1)
    owner_row = (own_row // VOCAB_ROWS).astype(FULL)
    owner_col = as_column(owner_row)
    earlier = (owner_row == owner_col) & (iota((TOKENS, TOKENS), 1) < iota((TOKENS, TOKENS), 0))
    own_rank = jnp.sum(earlier.astype(FULL), axis=1, keepdims=True)
    own_group = jnp.floor(own_rank * (1.0 / PAD))
    own_slot = own_group * SLOT_ROWS + owner_col * PAD + (own_rank - own_group * PAD)
    r.slot_col[...] = own_slot
    r.slot_line[0:1, :] = as_row(own_slot)
    c_steps.chain(3)
    c_steps.sides()
    a_steps.corner()

    at_sent = iota((1, TOKENS), 1) // LONG
    lens = jnp.concatenate(
        [r.lens[...].reshape(1, sentences).astype(FULL), jnp.zeros((1, PAD - sentences), FULL)],
        axis=1,
    )
    spread_lens = dot(
        jnp.broadcast_to(lens, (8, PAD)).astype(LOW),
        (iota((PAD, TOKENS), 0) == iota((PAD, TOKENS), 1) // LONG).astype(LOW),
    )[0:1]
    valid_row = ((iota((1, TOKENS), 1) - at_sent * LONG).astype(FULL) < spread_lens).astype(FULL)
    r.valid_line[0:1, :] = valid_row
    r.valid_col[...] = as_column(valid_row)
    half_block = BLOCK // 2
    stacked_shape = (4 * half_block, half_block)
    same = iota(stacked_shape, 0) // LONG % 2 == iota(stacked_shape, 1) // LONG
    r.block_bias[...] = jnp.where(same, 0.0, MASK_FLOOR)
    r.valid_bias[0:1, :] = (1.0 - valid_row) * MASK_FLOOR

    slots = r.slots[...].reshape(1, DEVICES * sentences)
    gap = jnp.full((1, PAD - sentences), -2, jnp.int32)
    slot_line = jnp.concatenate(
        [
            part
            for device in range(DEVICES)
            for part in (slots[:, device * sentences : (device + 1) * sentences], gap)
        ],
        axis=1,
    )
    side_line = slot_line - slot_line // 2 * 2 + jnp.where(slot_line < 0, 8, 0)
    pair_line = slot_line // 2
    pairs = r.langs.shape[0]
    lang_line = r.langs[...].reshape(1, pairs).astype(FULL)
    lang_line = jnp.concatenate([lang_line, jnp.full((1, -pairs % 128), -1.0, FULL)], axis=1)
    lang_col = as_column(lang_line)
    same_lang = jnp.sum(jnp.where(lang_col == lang_line, 1.0, 0.0), axis=1, keepdims=True)
    per_pair = 1.0 / (2.0 * LANGS * same_lang)
    at_pair = iota((lang_line.shape[1], SLOT_ROWS), 0) == pair_line
    weight_line = jnp.sum(jnp.where(at_pair, per_pair, 0.0), axis=0, keepdims=True)
    r.pairs[0:1, :] = weight_line
    r.pairs[1:2, :] = pair_line.astype(FULL)
    r.pairs[2:3, :] = side_line.astype(FULL)
    r.pairs_col[:, 0:1] = as_column(weight_line)
    r.pairs_col[:, 1:2] = as_column(pair_line.astype(FULL))
    r.pairs_col[:, 2:3] = as_column(side_line.astype(FULL))
    b_steps.corner()
    a_steps.last()

    all_smalls().wait_recv()
    smalls = r.smalls[...].astype(FULL)
    r.vectors[:, 0:WIDTH] = jnp.concatenate(
        [smalls[:, at * 128 : at * 128 + depth] for at in range(CHIPS)], axis=1
    )
    r.up_bias[0:1, :] = jnp.concatenate(
        [
            smalls[8 + part : 9 + part, at * 128 : at * 128 + depth]
            for at in range(CHIPS)
            for part in range(deep // depth)
        ],
        axis=1,
    )

    def vector(index):
        return r.vectors[index : index + 1, :]

    r.qkv_bias[0:1, 0:WIDTH] = vector(0)
    r.qkv_bias[0:1, WIDTH : 2 * WIDTH] = jnp.zeros((1, WIDTH), FULL)
    r.qkv_bias[0:1, 2 * WIDTH : 3 * WIDTH] = vector(1)

    c_steps.corner()
    b_steps.last()

    def first_row(source):
        code = jnp.where(r.rank[pl.ds(source, 1), :] >= 0.0, r.code[pl.ds(source, 1), :], 0.0)
        at_first = iota((PAD, TOKENS), 1) == iota((PAD, TOKENS), 0) * LONG
        found = jnp.sum(jnp.where(at_first, code, 0.0), axis=1, keepdims=True)
        row = found - jnp.floor(found * (1.0 / 2048)) * 2048.0 - 1.0
        r.found[GROUPS, pl.ds(pl.multiple_of(source * PAD, 16), PAD), 0:1] = row

    every(0, DEVICES, first_row)
    for group in range(GROUPS + 1):
        named = as_row(r.found[group, :, 0:1])
        by_row = iota((VOCAB_ROWS, SLOT_ROWS), 0).astype(FULL) == named
        r.by_row[:, group * SLOT_ROWS : (group + 1) * SLOT_ROWS] = by_row.astype(LOW)

    def order(tile):
        at = pl.ds(pl.multiple_of(tile * BLOCK, BLOCK), BLOCK)
        lanes = iota((BLOCK, GROUPS * SLOT_ROWS), 1).astype(FULL)
        r.qkv[at, 0 : GROUPS * SLOT_ROWS] = (r.slot_col[at, :] == lanes).astype(LOW)

    every(0, TOKENS // BLOCK, order)
    for group in range(GROUPS):
        slot_at = iota((SLOT_ROWS, TOKENS), 0) + group * SLOT_ROWS
        r.slot_hot[group] = (slot_at.astype(FULL) == r.slot_line[0:1, :]).astype(LOW)
    c_steps.last()
    a_steps.finish()
    for quarter in range(4):
        rows_of(quarter).wait_recv()

    def embed(tile):
        at = pl.ds(pl.multiple_of(tile * BLOCK, BLOCK), BLOCK)
        replies = r.replies[:, :, at].reshape(GROUPS * SLOT_ROWS, BLOCK)
        r.embedded[:, at] = dot(r.qkv[:, 0 : GROUPS * SLOT_ROWS], replies).astype(LOW)

    every(0, WIDTH // BLOCK, embed)

    def project(tile):
        at = pl.ds(pl.multiple_of(tile * BLOCK, BLOCK), BLOCK)
        r.qkv[:, at] = (dot(r.embedded[...], r.wa[:, at]) + r.qkv_bias[0:1, at]).astype(LOW)

    every(3, 6, project)
    every(6, 9, project)

    row_sent = iota((PAIR_ROWS, WIDTH), 0) % PAD
    row_head = iota((PAIR_ROWS, WIDTH), 0) // PAD
    lane_block = iota((PAIR_ROWS, WIDTH), 1) // HEAD
    in_head = row_head == lane_block
    seen = (row_sent == lane_block) & (r.valid_line[0:1, :] > 0.0)
    firsts = (iota((PAD, TOKENS), 1) == iota((PAD, TOKENS), 0) * LONG).astype(LOW)
    real_row = iota((PAD, 1), 0) < sentences

    def spread(rows):
        return jnp.where(in_head, jnp.concatenate([rows] * HEADS, axis=0), jnp.zeros((), LOW))

    def fold(tall):
        tall = jnp.where(in_head, tall, 0.0)
        return sum(tall[head * PAD : (head + 1) * PAD] for head in range(HEADS))

    keys, values = slice(WIDTH, 2 * WIDTH), slice(2 * WIDTH, 3 * WIDTH)
    embedded_cls = dot(firsts, r.embedded[...]).astype(LOW)
    query_cls = (dot(embedded_cls, r.wa[:, 0:WIDTH]) + vector(0)).astype(LOW)
    cls_scores = dot_turned(spread(query_cls), r.qkv[:, keys]) * scale
    cls_scores = jnp.where(seen, cls_scores, MASK_FLOOR)
    cls_peak = jnp.max(cls_scores, axis=1, keepdims=True)
    cls_exp = jnp.where(seen, jnp.exp(cls_scores - cls_peak), 0.0)
    cls_total = jnp.sum(cls_exp, axis=1, keepdims=True)
    cls_probs = cls_exp / jnp.where(cls_total > 0.0, cls_total, 1.0)
    probs_low = cls_probs.astype(LOW)
    r.probs[...] = cls_probs
    context_cls = fold(dot(probs_low, r.qkv[:, values])).astype(LOW)
    first_cls = (
        embedded_cls.astype(FULL)
        + dot(context_cls, r.wa[:, 3 * WIDTH : 4 * WIDTH])
        + vector(2)
    )
    normed_one, inverse_one = norm_parts(first_cls)
    r.normed_one[...] = normed_one
    hidden_cls = normed_one * vector(3) + vector(4)
    hidden_cls_low = hidden_cls.astype(LOW)
    early_here = r.early.at[here]
    early_here[:, 0:WIDTH] = hidden_cls_low
    early_here[:, WIDTH : 2 * WIDTH] = query_cls
    steps_u, drain_u = gather_steps(r.units, r.gather_send.at[0], r.gather_recv.at[0])
    steps_e, drain_e = gather_steps(r.early, r.gather_send.at[1], r.gather_recv.at[1])
    steps_d, drain_d = gather_steps(r.downs, r.gather_send.at[2], r.gather_recv.at[2])
    steps_a, drain_a2 = gather_steps(r.attends, r.gather_send.at[3], r.gather_recv.at[3])
    steps_q, drain_q = gather_steps(r.queries, r.gather_send.at[4], r.gather_recv.at[4])
    steps_e[0]()

    def attend(unit):
        rows = pl.ds(pl.multiple_of(unit * half_block, half_block), half_block)
        lane_head = iota((half_block, BLOCK), 1) // HEAD
        bias = r.block_bias[...] + r.valid_bias[0:1, rows]

        def part(which, lane):
            return r.qkv[rows, which * WIDTH + lane : which * WIDTH + lane + BLOCK]

        for lane in range(0, WIDTH, BLOCK):
            query = part(0, lane) * jnp.asarray(scale, LOW)
            key, value = part(1, lane), part(2, lane)
            stacked = jnp.concatenate(
                [jnp.where(lane_head == head, query, jnp.zeros((), LOW)) for head in range(4)],
                axis=0,
            )
            scores = dot_turned(stacked, key) + bias
            shifted = jnp.exp(scores - jnp.max(scores, axis=1, keepdims=True))
            probs = shifted * (1.0 / jnp.sum(shifted, axis=1, keepdims=True))
            mixed = dot(probs.astype(LOW), value)
            result = mixed[0:half_block]
            for head in range(1, 4):
                result = jnp.where(
                    lane_head == head, mixed[head * half_block : (head + 1) * half_block], result
                )
            r.context[rows, lane : lane + BLOCK] = result.astype(LOW)

    def open_tile(tile):
        at = pl.ds(pl.multiple_of(tile * BLOCK, BLOCK), BLOCK)
        attended = dot(r.context[at, :], r.wa[:, 3 * WIDTH : 4 * WIDTH]) + vector(2)
        normed, _ = norm_parts(r.embedded[at, :].astype(FULL) + attended)
        hidden = normed * vector(3) + vector(4)
        r.context[at, :] = hidden.astype(LOW)
        r.table_full[at, :] = hidden + vector(5)

    most = SLOT_ROWS
    rest_at = pl.ds(most, TOKENS - most)

    def feed_up(part):
        at = slice(part * BLOCK, (part + 1) * BLOCK)
        up_pre = dot(r.context[...], r.wb[:, at]) + r.up_bias[0:1, at]
        active = gelu(up_pre).astype(LOW)
        lane = part % 4 * BLOCK
        r.chosen[part // 4, :, lane : lane + BLOCK] = active[:most]
        r.tile_rest[:, at] = active[most:]

    def feed_down(part):
        lanes = pl.ds(pl.multiple_of(part * BLOCK, BLOCK), BLOCK)
        total = r.table_full[0:most, lanes]
        for group in range(GROUPS):
            rows = slice(group * VOCAB_ROWS, (group + 1) * VOCAB_ROWS)
            total = total + dot(r.chosen[group], r.wc[rows, lanes])
        r.table_full[0:most, lanes] = total

    def feed_rest(part):
        lanes = pl.ds(pl.multiple_of(part * BLOCK, BLOCK), BLOCK)
        r.table_full[rest_at, lanes] += dot(r.tile_rest[...], r.wc[:, lanes])

    def layer_copy(tile):
        at = pl.ds(tile * BLOCK, BLOCK)
        return pltpu.make_async_copy(r.context.at[at], r.layer_out.at[at], r.out_sem.at[tile])

    def close_tile(tile):
        at = pl.ds(tile * BLOCK, BLOCK)
        normed, _ = norm_parts(r.table_full[at, :])
        out = normed * vector(6) + vector(7)
        r.context[at, :] = (out * r.valid_col[at, :]).astype(LOW)
        layer_copy(tile).start()

    pieces = [partial(every, 0, 3, project)]
    pieces += [partial(every, unit, unit + 1, attend) for unit in range(6)]
    pieces += [partial(every, tile, tile + 1, open_tile) for tile in range(TOKENS // BLOCK)]
    pieces += [partial(feed_up, part) for part in range(WIDE // BLOCK)]
    pieces += [partial(every, part, part + 1, feed_rest) for part in range(WIDTH // BLOCK)]
    pieces += [partial(every, part, part + 1, feed_down) for part in range(WIDTH // BLOCK)]
    pieces += [partial(close_tile, tile) for tile in range(TOKENS // BLOCK)]

    def fill(count):
        for _ in range(min(count, len(pieces))):
            pieces.pop(0)()

    b_steps.finish()
    up_cls = dot(hidden_cls_low, r.wb[...]) + r.up_bias[0:1, :]
    activated_cls, slope_cls = gelu_parts(up_cls)
    activated_low = activated_cls.astype(LOW)
    steps_e[1]()
    c_steps.finish()

    def pack_tall(tall, target, first_row, spare=None):
        for at in range(CHIPS):
            last = jnp.zeros((48, 128 - 2 * depth), FULL)
            if spare is not None:
                last = spare[at * depth : (at + 1) * depth]
            columns = tall[:, at * depth : (at + 1) * depth]
            for half in range(CORES):
                base = half * PAIR_ROWS // 2
                target[half * CHIPS + at, first_row : first_row + 48, :] = jnp.concatenate(
                    [
                        columns[base : base + 48],
                        columns[base + 48 : base + 96],
                        last,
                    ],
                    axis=1,
                ).astype(LOW)

    def pack_coefs(coefs):
        shape = (PAIR_ROWS, GROUPS * 128)
        folds = iota(shape, 0) // PAD + iota(shape, 1) // 128 * PAD == iota(shape, 1) % 128
        lanes = contract(coefs, folds.astype(LOW), 0, 0).astype(LOW)
        total = None
        for group in range(GROUPS):
            part = dot(r.slot_hot[group], lanes[:, group * 128 : (group + 1) * 128])
            total = part if total is None else total + part
        return total.astype(LOW).reshape(DEVICES, PAD, 128)

    down_pre = dot(activated_low, r.wc[...]) + vector(5)
    normed_two, inverse_two = norm_parts(hidden_cls + down_pre)
    summary = normed_two * vector(6) + vector(7)
    magnitude = jnp.sqrt(jnp.sum(summary * summary, axis=-1, keepdims=True) + EPSILON)
    unit = jnp.where(real_row, summary / magnitude, 0.0)
    r.units[here] = unit.astype(LOW)

    steps_u[0]()
    for at in range(CHIPS):
        cut = slice(at * depth, (at + 1) * depth)
        line = jnp.concatenate(
            [
                context_cls.astype(FULL)[:, cut],
                embedded_cls.astype(FULL)[:, cut],
                jnp.zeros((PAD, 128 - 2 * depth), FULL),
            ],
            axis=1,
        ).astype(LOW)
        for half in range(CORES):
            r.mail_one[half * CHIPS + at, 0:PAD, :] = line
    steps_u[1]()
    pack_tall(dot(probs_low, r.embedded[...]), r.mail_one, PAD)
    steps_u[2]()
    steps_e[2]()
    r.mail_one[:, 64:80, :] = pack_coefs(probs_low)
    fill(1)
    steps_u[3]()
    steps_e[3]()
    fill(2)

    def post(box, got, index):
        def send(step):
            other, to_core, to_chip = peer(step)
            remote(
                box.at[other], got.at[me], r.one_send.at[index], r.one_recv.at[index], to_core, to_chip
            ).start()

        every(1, DEVICES, send)
        got[me] = box[me]

    steps_u[4]()
    steps_e[4]()
    fill(1)
    steps_u[5]()
    steps_e[5]()
    post(r.mail_one, r.got_one, 1)

    units = r.units[...].reshape(SLOT_ROWS, WIDTH)
    weight_row, pair_row, side_row = r.pairs[0:1, :], r.pairs[1:2, :], r.pairs[2:3, :]

    def pair_scores(rows, pair_col, side_col):
        opposite = side_col + side_row == 1.0
        partner = opposite & (pair_col == pair_row)
        raw = SCORE_SCALE * dot_turned(rows, units)
        shifted = jnp.where(partner, raw - SCORE_SCALE * MARGIN_WIDTH, raw)
        return jnp.where(opposite, shifted, MASK_FLOOR), partner

    every_score, every_partner = pair_scores(
        units, r.pairs_col[:, 1:2], r.pairs_col[:, 2:3]
    )
    peak_row = jnp.max(every_score, axis=0, keepdims=True)
    log_row = peak_row + jnp.log(
        jnp.sum(jnp.exp(every_score - peak_row), axis=0, keepdims=True)
    )
    picked_row = jnp.sum(jnp.where(every_partner, every_score, 0.0), axis=0, keepdims=True)
    r.loss[...] = jnp.sum(weight_row * (log_row - picked_row), axis=1, keepdims=True)

    rows_here = pl.ds(pl.multiple_of(me * PAD, 16), PAD)
    own_score, own_partner = pair_scores(
        r.units[here], r.pairs_col[rows_here, 1:2], r.pairs_col[rows_here, 2:3]
    )
    own_partner = own_partner.astype(FULL)
    own_peak = jnp.max(own_score, axis=1, keepdims=True)
    own_exp = jnp.exp(own_score - own_peak)
    own_share = own_exp / jnp.sum(own_exp, axis=1, keepdims=True)
    by_row = (r.pairs_col[rows_here, 0:1] * (own_share - own_partner)).astype(LOW)
    by_column = (weight_row * (jnp.exp(own_score - log_row) - own_partner)).astype(LOW)
    unit_grad = SCORE_SCALE * (dot(by_row, units) + dot(by_column, units))
    along = jnp.sum(unit * unit_grad, axis=-1, keepdims=True)
    summary_grad = (unit_grad - unit * along) / magnitude

    residual_grad, grad_g2, grad_s2 = norm_back_parts(
        summary_grad, normed_two, inverse_two, vector(6)
    )
    down_grad = residual_grad.astype(LOW)
    r.downs[here] = down_grad
    steps_d[0]()
    act_grad = dot_turned(down_grad, r.wc[...])
    up_grad = (act_grad * slope_cls).astype(LOW)
    steps_d[1]()
    hidden_grad = dot_turned(up_grad, r.wb[...]) + residual_grad
    first_grad, grad_g1, grad_s1 = norm_back_parts(
        hidden_grad, r.normed_one[...], inverse_one, vector(3)
    )
    attend_grad = first_grad.astype(LOW)
    context_grad = dot_turned(attend_grad, r.wa[:, 3 * WIDTH : 4 * WIDTH]).astype(LOW)
    attend_here = r.attends.at[here]
    attend_here[:, 0:WIDTH] = attend_grad
    attend_here[:, WIDTH : 2 * WIDTH] = context_grad
    steps_a[0]()
    steps_d[2]()
    context_tall = spread(context_grad)
    probs = r.probs[...]
    prob_grad = dot_turned(context_tall, r.qkv[:, values])
    inner = jnp.sum(probs * prob_grad, axis=1, keepdims=True)
    score_grad = (probs * (prob_grad - inner)).astype(LOW)
    steps_a[1]()
    r.mail_three[...] = pack_coefs(score_grad)
    post(r.mail_three, r.got_three, 3)
    query_grad = (fold(dot(score_grad, r.qkv[:, keys])) * scale).astype(LOW)
    probs_total = jnp.sum(probs_low.astype(FULL), axis=1, keepdims=True)
    grad_bvalue = jnp.sum(probs_total * context_tall.astype(FULL), axis=0, keepdims=True)
    grad_bquery = jnp.sum(query_grad.astype(FULL), axis=0, keepdims=True)
    r.queries[here] = query_grad
    own_sums = jnp.concatenate(
        [grad_bquery, grad_bvalue, grad_g1, grad_s1, grad_g2, grad_s2]
        + [jnp.zeros((128 - 6, WIDTH), FULL)],
        axis=0,
    )
    own_sums = jnp.transpose(own_sums)[:, 0 : 128 - 2 * depth]
    steps_q[0]()
    steps_a[2]()
    pack_tall(dot(score_grad, r.embedded[...]) * scale, r.mail_two, 0, own_sums)
    steps_q[1]()
    post(r.mail_two, r.got_two, 2)

    def all_rows(buffer, start):
        return buffer[:, :, :, :, start : start + WIDTH].reshape(SLOT_ROWS, WIDTH)

    def from_sent(group):
        lanes = iota((SLOT_ROWS, SLOT_ROWS), 1).astype(FULL)
        return (r.found[group, :, 1:2] == lanes).astype(LOW)

    def widened(coefs, group):
        lanes = iota((128, WIDTH), 0) == iota((128, WIDTH), 1) // HEAD + group * PAD
        return dot(coefs, lanes.astype(LOW))

    half_wide = WIDE // 2

    def slope_tile(part):
        at = pl.ds(pl.multiple_of(core * half_wide + part * BLOCK, BLOCK), BLOCK)
        up_pre = dot(all_rows(r.early, 0), r.wb[:, at]) + r.up_bias[0:1, at]
        _, slope = gelu_parts(up_pre)
        r.slopes[:, pl.ds(pl.multiple_of(part * BLOCK, BLOCK), BLOCK)] = slope.astype(LOW)

    def slot_queries(group):
        r.slot_query[group] = dot(from_sent(group), all_rows(r.early, WIDTH)).astype(LOW)

    def activate():
        at = pl.ds(pl.multiple_of(chip // 2 * 2 * deep, 128), 2 * deep)
        up_pre = dot(all_rows(r.early, 0), r.wb[:, at]) + r.up_bias[0:1, at]
        r.active_turned[...] = jnp.transpose(gelu(up_pre)).astype(LOW)
        r.hidden_turned[...] = jnp.transpose(all_rows(r.early, 0))

    pieces += [partial(slot_queries, group) for group in range(GROUPS)]
    pieces += [partial(every, part, part + 1, slope_tile) for part in range(6)]
    pieces.append(activate)
    rest = [steps_d[3], steps_a[3], steps_q[2], steps_d[4], steps_a[4], steps_q[3]]
    rest += [steps_d[5], steps_a[5], steps_q[4]]
    for step in rest:
        step()
        fill(2)
    fill(len(pieces))

    all_but_one(r.got_one, 1).wait_recv()
    got_probs = r.got_one[:, 64:80, :].reshape(SLOT_ROWS, 128)
    for group in range(GROUPS):
        slot_context = dot(from_sent(group), all_rows(r.attends, WIDTH))
        r.replies[group] = (widened(got_probs, group) * slot_context).astype(LOW)

    def head_products(got, first_row, right, start, target):
        for pair in range(HEADS // 4):
            lane = pl.ds(pl.multiple_of(start + (core * (HEADS // 4) + pair) * 128, 128), 128)
            pair_rows = right[:, :, :, :, lane].reshape(SLOT_ROWS, 128)
            parts = []
            for half in range(2):
                head = 2 * pair + half
                row = first_row + head % 3 * PAD
                block_rows = got[:, row : row + PAD, :].reshape(SLOT_ROWS, 128)
                product = contract(block_rows, pair_rows, 0, 0)
                column = head // 3 * depth
                parts.append(product[column : column + depth, :])
            low_lanes = iota((depth, 128), 1) < HEAD
            result = jnp.where(low_lanes, parts[0], parts[1])
            target[:, pl.ds(pl.multiple_of((core * (HEADS // 4) + pair) * 128, 128), 128)] = result

    def half_of(ref, at_core):
        half = ref.shape[1] // 2
        return ref.at[:, pl.ds(pl.multiple_of(at_core * half, 128), half)]

    def half_copy(index, ref, at_core):
        part = half_of(ref, at_core)
        return remote(part, part, r.half_send.at[index], r.half_recv.at[index], 1 - core, chip)

    head_products(r.got_one, PAD, r.attends, WIDTH, r.g_wv)
    half_copy(0, r.g_wv, core).start()

    downs = r.downs[...].reshape(SLOT_ROWS, WIDTH)
    attends = all_rows(r.attends, 0)

    def up_tile(part):
        at = pl.ds(pl.multiple_of(core * half_wide + part * BLOCK, BLOCK), BLOCK)
        slope = r.slopes[:, pl.ds(pl.multiple_of(part * BLOCK, BLOCK), BLOCK)].astype(FULL)
        up_all = (dot_turned(r.downs[...].reshape(SLOT_ROWS, WIDTH), r.wc[at, :]) * slope)
        up_all = up_all.astype(LOW)
        r.g_wup[0:depth, at] = dot(r.hidden_turned[mine, :], up_all)
        total = jnp.sum(up_all.astype(FULL), axis=0, keepdims=True)
        r.g_wup[depth : depth + 8, at] = jnp.broadcast_to(total, (8, BLOCK))

    every(0, half_wide // BLOCK, up_tile)
    half_copy(1, r.g_wup, core).start()
    r.g_wdown[...] = dot(r.active_turned[pl.ds(pl.multiple_of(chip % 2 * deep, 16), deep), :], downs)
    r.left_turned[...] = jnp.transpose(r.got_one[:, 0:PAD, :].reshape(SLOT_ROWS, 128))
    r.g_wo[...] = dot(r.left_turned[0:depth, :], attends)
    own_lanes = (iota((WIDTH, 128), 0) == chip * depth + iota((WIDTH, 128), 1)).astype(LOW)

    def own_part(rows, select):
        total = None
        for _ in range(3):
            part = rows.astype(LOW)
            rows = rows - part.astype(FULL)
            picked = dot(part, select)
            total = picked if total is None else total + picked
        return total

    for quarter in range(4):
        rows_of(quarter).wait_send()
    all_but_one(r.got_three, 3).wait_recv()
    got_scores = r.got_three[...].reshape(SLOT_ROWS, 128)
    for group in range(GROUPS):
        slot_query = r.slot_query[group].astype(FULL)
        key_grad = (widened(got_scores, group) * slot_query * scale).astype(LOW)
        row_grad = dot_turned(key_grad, r.wa[:, keys])
        row_grad = row_grad + dot_turned(r.replies[group], r.wa[:, values])
        r.rows[group] = row_grad.astype(LOW)
    steps_q[5]()
    query_grads = all_rows(r.queries, 0)
    extra = dot_turned(query_grads, r.wa[:, 0:WIDTH]) + attends.astype(FULL)
    r.extra[...] = extra.astype(LOW)
    r.g_wq[...] = dot(r.left_turned[depth : 2 * depth, :], query_grads)

    half_rows = VOCAB_ROWS // 2

    def table_copy(tile):
        at = pl.ds(pl.multiple_of(tile * half_rows, BLOCK), half_rows)
        return pltpu.make_async_copy(
            r.table_full.at[at], r.table_grad.at[at], r.table_sem.at[tile]
        )

    def table_tile(tile):
        at = pl.ds(pl.multiple_of(tile * half_rows, BLOCK), half_rows)
        for start in range(0, WIDTH, BLOCK):
            lanes = slice(start, start + BLOCK)
            slot_rows = r.rows[:, :, lanes].reshape(GROUPS * SLOT_ROWS, BLOCK)
            r.table_full[at, lanes] = dot(r.by_row[at, 0 : GROUPS * SLOT_ROWS], slot_rows) + dot(
                r.by_row[at, GROUPS * SLOT_ROWS :], r.extra[:, lanes]
            )
        table_copy(tile).start()

    every(0, 2, table_tile)
    all_but_one(r.got_two, 2).wait_recv()
    head_products(r.got_two, 0, r.early, WIDTH, r.g_wk)
    half_copy(2, r.g_wk, core).start()

    down_total = jnp.sum(downs.astype(FULL), axis=0, keepdims=True)
    attend_total = jnp.sum(attends.astype(FULL), axis=0, keepdims=True)
    sums = jnp.sum(r.got_two[...].astype(FULL), axis=0)
    sums = jnp.concatenate([sums, jnp.zeros((128 - 48, 128), FULL)], axis=0)
    stacked = jnp.concatenate([attend_total, down_total, jnp.zeros((6, WIDTH), FULL)], axis=0)
    r.g_small[8:16, 0:128] = own_part(stacked, own_lanes)
    r.g_small[0:8, 0:128] = jnp.transpose(sums)[2 * depth : 2 * depth + 8, :]
    r.g_small[0:16, 128:BLOCK] = jnp.zeros((PAD, BLOCK - 128), FULL)
    half_copy(1, r.g_wup, 1 - core).wait_recv()
    up_lanes = (iota((WIDE, BLOCK), 0) == chip * deep + iota((WIDE, BLOCK), 1)).astype(LOW)
    r.g_small[16:24, :] = own_part(r.g_wup[depth : depth + 8, :], up_lanes)

    half_copy(0, r.g_wv, 1 - core).wait_recv()
    half_copy(2, r.g_wk, 1 - core).wait_recv()
    for index, ref in enumerate([r.g_wv, r.g_wup, r.g_wk]):
        half_copy(index, ref, core).wait_send()

    for index, ref in enumerate([r.every_ids, r.got_one, r.got_two, r.got_three]):
        all_but_one(ref, index).wait_send()
    all_smalls().wait_send()
    for end in [drain_a, drain_b, drain_c, drain_u, drain_e, drain_d, drain_a2, drain_q]:
        end()
    for tile in range(TOKENS // BLOCK):
        layer_copy(tile).wait()
    every(0, 2, lambda tile: table_copy(tile).wait())


def layer(inputs):
    dma = pltpu.SemaphoreType.DMA
    vmem = pl.BlockSpec(memory_space=pltpu.VMEM)
    anywhere = pl.BlockSpec(memory_space=pl.ANY)
    depth, deep = WIDTH // CHIPS, WIDE // CHIPS

    def gathered(width):
        return pltpu.VMEM((CORES, PLANES, LINES, PAD, width), LOW)

    outputs = dict(
        layer_out=((TOKENS, WIDTH), LOW),
        table_grad=((VOCAB_ROWS, WIDTH), FULL),
        g_wq=((depth, WIDTH), FULL),
        g_wk=((depth, WIDTH), FULL),
        g_wv=((depth, WIDTH), FULL),
        g_wo=((depth, WIDTH), FULL),
        g_wup=((depth + 8, WIDE), FULL),
        g_wdown=((deep, WIDTH), FULL),
        g_small=((24, BLOCK), FULL),
        loss=((1, 1), FULL),
    )
    scratch = dict(
        ids=pltpu.VMEM((8, 128), jnp.int32),
        every_ids=pltpu.VMEM((DEVICES, 8, 128), jnp.int32),
        rank=pltpu.VMEM((DEVICES, TOKENS), FULL),
        code=pltpu.VMEM((DEVICES, TOKENS), FULL),
        found=pltpu.VMEM((GROUPS + 1, SLOT_ROWS, 2), FULL),
        block_bias=pltpu.VMEM((2 * BLOCK, BLOCK // 2), FULL),
        valid_bias=pltpu.VMEM((8, TOKENS), FULL),
        slot_col=pltpu.VMEM((TOKENS, 1), FULL),
        slot_line=pltpu.VMEM((8, TOKENS), FULL),
        valid_col=pltpu.VMEM((TOKENS, 1), FULL),
        valid_line=pltpu.VMEM((8, TOKENS), FULL),
        pairs=pltpu.VMEM((8, SLOT_ROWS), FULL),
        pairs_col=pltpu.VMEM((SLOT_ROWS, 128), FULL),
        vectors=pltpu.VMEM((PAD, WIDTH), FULL),
        up_bias=pltpu.VMEM((8, WIDE), FULL),
        qkv_bias=pltpu.VMEM((8, 3 * WIDTH), FULL),
        smalls=pltpu.VMEM((PAD, CHIPS * 128), LOW),
        wa=pltpu.VMEM((WIDTH, 4 * WIDTH), LOW),
        wb=pltpu.VMEM((WIDTH, WIDE), LOW),
        wc=pltpu.VMEM((WIDE, WIDTH), LOW),
        chosen=pltpu.VMEM((GROUPS, SLOT_ROWS, VOCAB_ROWS), LOW),
        by_row=pltpu.VMEM((VOCAB_ROWS, (GROUPS + 1) * SLOT_ROWS), LOW),
        rows=pltpu.VMEM((GROUPS, SLOT_ROWS, WIDTH), LOW),
        replies=pltpu.VMEM((GROUPS, SLOT_ROWS, WIDTH), LOW),
        slot_query=pltpu.VMEM((GROUPS, SLOT_ROWS, WIDTH), LOW),
        extra=pltpu.VMEM((SLOT_ROWS, WIDTH), LOW),
        slot_hot=pltpu.VMEM((GROUPS, SLOT_ROWS, TOKENS), LOW),
        tile_rest=pltpu.VMEM((TOKENS - SLOT_ROWS, WIDE), LOW),
        embedded=pltpu.VMEM((TOKENS, WIDTH), LOW),
        qkv=pltpu.VMEM((TOKENS, 3 * WIDTH), LOW),
        context=pltpu.VMEM((TOKENS, WIDTH), LOW),
        table_full=pltpu.VMEM((VOCAB_ROWS, WIDTH), FULL),
        probs=pltpu.VMEM((PAIR_ROWS, TOKENS), FULL),
        normed_one=pltpu.VMEM((PAD, WIDTH), FULL),
        units=gathered(WIDTH),
        early=gathered(2 * WIDTH),
        downs=gathered(WIDTH),
        attends=gathered(2 * WIDTH),
        queries=gathered(WIDTH),
        slopes=pltpu.VMEM((SLOT_ROWS, WIDE // 2), LOW),
        hidden_turned=pltpu.VMEM((WIDTH, SLOT_ROWS), LOW),
        active_turned=pltpu.VMEM((2 * deep, SLOT_ROWS), LOW),
        left_turned=pltpu.VMEM((128, SLOT_ROWS), LOW),
        mail_one=pltpu.VMEM((DEVICES, 80, 128), LOW),
        got_one=pltpu.VMEM((DEVICES, 80, 128), LOW),
        mail_two=pltpu.VMEM((DEVICES, 48, 128), LOW),
        got_two=pltpu.VMEM((DEVICES, 48, 128), LOW),
        mail_three=pltpu.VMEM((DEVICES, PAD, 128), LOW),
        got_three=pltpu.VMEM((DEVICES, PAD, 128), LOW),
        rows_send=dma((4,)),
        rows_recv=dma((4,)),
        one_send=dma((4,)),
        one_recv=dma((4,)),
        small_send=dma((1,)),
        small_recv=dma((1,)),
        weight_send=dma((3, 14)),
        weight_recv=dma((3, 14)),
        gather_send=dma((5, 13)),
        gather_recv=dma((5, 13)),
        half_send=dma((3,)),
        half_recv=dma((3,)),
        out_sem=dma((TOKENS // BLOCK,)),
        table_sem=dma((2,)),
    )
    names = INPUTS + OUTPUTS + list(scratch)
    return pl.pallas_call(
        partial(layer_kernel, names),
        out_shape=tuple(jax.ShapeDtypeStruct(*outputs[name]) for name in OUTPUTS),
        in_specs=[vmem] * len(INPUTS),
        out_specs=(anywhere, anywhere) + (vmem,) * (len(OUTPUTS) - 2),
        scratch_shapes=list(scratch.values()),
        compiler_params=pltpu.CompilerParams(
            collective_id=0, has_side_effects=True, vmem_limit_bytes=VMEM_LIMIT
        ),
        name="layer",
    )(*inputs)


def finish_kernel(count, *refs):
    large, (small, loss), outs = refs[:count], refs[count : count + 2], refs[count + 2 : -1]
    sems = refs[-1]
    copies = []
    for index, (source, target) in enumerate(zip(large, outs)):
        part = source if source.shape == target.shape else source.at[: target.shape[0]]
        copies.append(pltpu.make_async_copy(part, target, sems.at[index]))
        copies[-1].start()
    for row, target in zip([0, 1, 8, 2, 3, 16, 9, 4, 5], outs[count : count + 9]):
        size = target.shape[0]
        target[...] = small[row : row + 1, 0:size].reshape(size)
    outs[-1][...] = loss[...].reshape(1)
    for one in copies:
        one.wait()


def finish(results):
    vmem = pl.BlockSpec(memory_space=pltpu.VMEM)
    anywhere = pl.BlockSpec(memory_space=pl.ANY)
    depth, deep = WIDTH // CHIPS, WIDE // CHIPS
    count = len(results) - 2
    shapes = [(one.shape, one.dtype) for one in results[:count]]
    shapes[6] = ((depth, WIDE), FULL)
    shapes += [((depth,), FULL)] * 5 + [((deep,), FULL)] + [((depth,), FULL)] * 3
    shapes.append(((1,), FULL))
    return pl.pallas_call(
        partial(finish_kernel, count),
        out_shape=tuple(jax.ShapeDtypeStruct(*one) for one in shapes),
        in_specs=[vmem] * (count + 2),
        out_specs=(anywhere,) * count + (vmem,) * 10,
        scratch_shapes=[pltpu.SemaphoreType.DMA((count,))],
        name="finish",
    )(*results)


def block_body(
    table,
    token_ids,
    sent_lengths,
    pair_slot,
    pair_lang,
    *parameters,
):
    results = finish(layer((table, token_ids, sent_lengths, pair_slot, pair_lang) + parameters))
    layer_out, table_grad, g_wq, g_wk, g_wv, g_wo, g_wup, g_wdown = results[:8]
    g_bq, g_bv, g_bo, g_g1, g_s1, g_bup, g_bdown, g_g2, g_s2, loss = results[8:]
    return (
        layer_out.reshape(token_ids.shape + (WIDTH,)),
        loss.reshape(()),
        table_grad,
        g_wq,
        g_bq,
        g_wk,
        g_wv,
        g_bv,
        g_wo,
        g_bo,
        g_g1,
        g_s1,
        g_wup,
        g_bup,
        g_wdown,
        g_bdown,
        g_g2,
        g_s2,
    )


def solution(mesh):
    in_specs = (
        P(("dp", "fsdp"), None),
        P(("dp", "fsdp"), None),
        P(("dp", "fsdp")),
        P(),
        P(),
        P("fsdp", None),
        P("fsdp"),
        P("fsdp", None),
        P("fsdp", None),
        P("fsdp"),
        P("fsdp", None),
        P("fsdp"),
        P("fsdp"),
        P("fsdp"),
        P("fsdp", None),
        P("fsdp"),
        P("fsdp", None),
        P("fsdp"),
        P("fsdp"),
        P("fsdp"),
    )
    out_specs = (
        P(("dp", "fsdp"), None, None),
        P(),
        P(("dp", "fsdp"), None),
        P("fsdp", None),
        P("fsdp"),
        P("fsdp", None),
        P("fsdp", None),
        P("fsdp"),
        P("fsdp", None),
        P("fsdp"),
        P("fsdp"),
        P("fsdp"),
        P("fsdp", None),
        P("fsdp"),
        P("fsdp", None),
        P("fsdp"),
        P("fsdp"),
        P("fsdp"),
    )
    sizes = dict(mesh.shape)
    body = general_body
    if sizes["dp"] == CORES and sizes["fsdp"] == CHIPS:
        body = block_body
    return jax.shard_map(body, mesh=mesh, in_specs=in_specs, out_specs=out_specs, check_vma=False)
```

```python
from functools import partial
from types import SimpleNamespace

import jax
import jax.numpy as jnp
from jax import lax
from jax.experimental import pallas as pl
from jax.experimental.pallas import tpu as pltpu
from jax.sharding import PartitionSpec as P

HEADS = 12
HEAD = 64
LANGS = 109


EPSILON = 1e-06
SCORE_SCALE = 50.0
MARGIN_WIDTH = 0.3
MASK_FLOOR = -1000000000.0


def contract(left_side, right_side, left_dim, right_dim):
    return lax.dot_general(
        left_side,
        right_side,
        (((left_dim,), (right_dim,)), ((), ())),
        preferred_element_type=jnp.float32,
    )


def norm_rows(inputs, ln_gain, ln_shift):
    row_mean = jnp.mean(inputs, axis=-1, keepdims=True)
    centered = inputs - row_mean
    variance = jnp.mean(centered * centered, axis=-1, keepdims=True)
    inverse = lax.rsqrt(variance + EPSILON)
    normed = centered * inverse
    return (normed * ln_gain + ln_shift, normed, inverse)


def norm_back(grad_output, normed, inverse, ln_gain):
    grad_normed = grad_output * ln_gain
    first_term = jnp.mean(grad_normed, axis=-1, keepdims=True)
    second_term = jnp.mean(grad_normed * normed, axis=-1, keepdims=True)
    grad_input = inverse * (grad_normed - first_term - normed * second_term)
    return (grad_input, jnp.sum(grad_output * normed, axis=0), jnp.sum(grad_output, axis=0))


def general_body(
    table,
    token_ids,
    sent_lengths,
    pair_slot,
    pair_lang,
    w_query,
    b_query,
    w_key,
    w_value,
    b_value,
    w_out,
    b_out,
    ln1_gain,
    ln1_bias,
    w_up,
    b_up,
    w_down,
    b_down,
    ln2_gain,
    ln2_bias,
):
    sentences, length = token_ids.shape
    tokens = sentences * length
    vocab_rows, model_width = table.shape
    owners = lax.axis_size(("dp", "fsdp"))
    dp_count = lax.axis_size("dp")
    fsdp_count = lax.axis_size("fsdp")
    capacity = max(2, 2 * tokens // owners)
    device = lax.axis_index(("dp", "fsdp"))
    score_factor = HEAD ** (-0.5)
    flat_ids = token_ids.reshape(tokens)
    owner_of = flat_ids // vocab_rows
    member = (owner_of[:, None] == jnp.arange(owners, dtype=jnp.int32)[None, :]).astype(jnp.int32)
    owner_rank = jnp.sum(jnp.cumsum(member, axis=0) * member, axis=1) - 1
    slot_of = owner_of * capacity + owner_rank
    requests = jnp.full((owners * capacity,), -1, jnp.int32).at[slot_of].set(flat_ids)
    received = lax.all_to_all(
        lax.all_to_all(
            requests.reshape(dp_count, fsdp_count, capacity),
            "dp",
            split_axis=0,
            concat_axis=0,
            tiled=True,
        ),
        "fsdp",
        split_axis=1,
        concat_axis=1,
        tiled=True,
    )
    present = received >= 0
    local_rows = jnp.where(present, received - device * vocab_rows, 0)
    found_rows = jnp.where(present[..., None], table[local_rows], jnp.zeros((), table.dtype))
    replies = lax.all_to_all(
        lax.all_to_all(found_rows, "dp", split_axis=0, concat_axis=0, tiled=True),
        "fsdp",
        split_axis=1,
        concat_axis=1,
        tiled=True,
    )
    embedded = replies.reshape(owners * capacity, model_width)[slot_of]
    gathered = (
        lax.all_gather(w_query, "fsdp", axis=0, tiled=True),
        lax.all_gather(b_query, "fsdp", axis=0, tiled=True),
        lax.all_gather(w_key, "fsdp", axis=0, tiled=True),
        lax.all_gather(w_value, "fsdp", axis=0, tiled=True),
        lax.all_gather(b_value, "fsdp", axis=0, tiled=True),
        lax.all_gather(w_out, "fsdp", axis=0, tiled=True),
        lax.all_gather(b_out, "fsdp", axis=0, tiled=True),
        lax.all_gather(ln1_gain, "fsdp", axis=0, tiled=True),
        lax.all_gather(ln1_bias, "fsdp", axis=0, tiled=True),
        lax.all_gather(w_up, "fsdp", axis=0, tiled=True),
        lax.all_gather(b_up, "fsdp", axis=0, tiled=True),
        lax.all_gather(w_down, "fsdp", axis=0, tiled=True),
        lax.all_gather(b_down, "fsdp", axis=0, tiled=True),
        lax.all_gather(ln2_gain, "fsdp", axis=0, tiled=True),
        lax.all_gather(ln2_bias, "fsdp", axis=0, tiled=True),
    )
    (
        full_wq,
        full_bq,
        full_wk,
        full_wv,
        full_bv,
        full_wo,
        full_bo,
        full_g1,
        full_s1,
        full_wup,
        full_bup,
        full_wdown,
        full_bdown,
        full_g2,
        full_s2,
    ) = gathered
    valid_mask = jnp.arange(length, dtype=jnp.int32)[None, :] < sent_lengths[:, None]
    head_shape = (sentences, length, HEADS, HEAD)
    queries = (jnp.dot(embedded, full_wq, preferred_element_type=jnp.float32) + full_bq).astype(
        jnp.bfloat16
    )
    key_heads = (
        jnp.dot(embedded, full_wk, preferred_element_type=jnp.float32)
        .astype(jnp.bfloat16)
        .reshape(head_shape)
    )
    value_heads = (
        (jnp.dot(embedded, full_wv, preferred_element_type=jnp.float32) + full_bv)
        .astype(jnp.bfloat16)
        .reshape(head_shape)
    )
    query_heads = queries.reshape(head_shape)
    scores = (
        jnp.einsum("bqhd,bkhd->bhqk", query_heads, key_heads, preferred_element_type=jnp.float32)
        * score_factor
    )
    scores = jnp.where(valid_mask[:, None, None, :], scores, MASK_FLOOR)
    row_peak = jnp.max(scores, axis=-1, keepdims=True)
    shifted = jnp.exp(scores - row_peak)
    totals = jnp.sum(shifted, axis=-1, keepdims=True)
    attn_probs = (shifted / totals).astype(jnp.bfloat16)
    context = jnp.einsum(
        "bhqk,bkhd->bqhd", attn_probs, value_heads, preferred_element_type=jnp.float32
    )
    context = context.reshape(tokens, model_width).astype(jnp.bfloat16)
    attended = jnp.dot(context, full_wo, preferred_element_type=jnp.float32) + full_bo
    hidden, normed_one, inverse_one = norm_rows(
        embedded.astype(jnp.float32) + attended, full_g1, full_s1
    )
    hidden_low = hidden.astype(jnp.bfloat16)
    up_pre = jnp.dot(hidden_low, full_wup, preferred_element_type=jnp.float32) + full_bup
    activated = jax.nn.gelu(up_pre, approximate=False).astype(jnp.bfloat16)
    down_pre = jnp.dot(activated, full_wdown, preferred_element_type=jnp.float32) + full_bdown
    normed_out, normed_two, inverse_two = norm_rows(hidden + down_pre, full_g2, full_s2)
    layer_out = jnp.where(valid_mask.reshape(tokens)[:, None], normed_out, 0.0).astype(jnp.bfloat16)
    layer_out = layer_out.reshape(sentences, length, model_width)

    def first_rows(matrix):
        return matrix.reshape(sentences, length, matrix.shape[-1])[:, 0]

    summary = first_rows(normed_out)
    magnitude = jnp.sqrt(jnp.sum(summary * summary, axis=-1, keepdims=True) + EPSILON)
    unit_vector = summary / magnitude
    unit_low = unit_vector.astype(jnp.bfloat16)
    every_unit = lax.all_gather(unit_low, ("dp", "fsdp"), axis=0, tiled=True)
    every_side = pair_slot % 2
    every_pair = pair_slot // 2
    my_slots = lax.dynamic_slice_in_dim(pair_slot, device * sentences, sentences)
    my_side = my_slots % 2
    my_pair = my_slots // 2
    lang_onehot = (pair_lang[:, None] == jnp.arange(LANGS, dtype=jnp.int32)[None, :]).astype(
        jnp.float32
    )
    per_lang = jnp.sum(lang_onehot, axis=0)
    per_pair = 1.0 / (2.0 * LANGS * jnp.sum(lang_onehot * per_lang[None, :], axis=1))
    my_weight = jnp.take(per_pair, my_pair)
    opposite = my_side[:, None] != every_side[None, :]
    partner = opposite & (my_pair[:, None] == every_pair[None, :])
    raw_scores = SCORE_SCALE * contract(unit_low, every_unit, 1, 1)
    pair_scores = jnp.where(partner, raw_scores - SCORE_SCALE * MARGIN_WIDTH, raw_scores)
    pair_scores = jnp.where(opposite, pair_scores, MASK_FLOOR)
    pair_peak = jnp.max(pair_scores, axis=1, keepdims=True)
    pair_exp = jnp.exp(pair_scores - pair_peak)
    pair_total = jnp.sum(pair_exp, axis=1, keepdims=True)
    log_total = pair_peak[:, 0] + jnp.log(pair_total[:, 0])
    picked = jnp.sum(jnp.where(partner, pair_scores, 0.0), axis=1)
    loss_value = lax.psum(jnp.sum(my_weight * (log_total - picked)), ("dp", "fsdp"))
    coefficients = (
        my_weight[:, None] * (pair_exp / pair_total - partner.astype(jnp.float32))
    ).astype(jnp.bfloat16)
    unit_grad = SCORE_SCALE * contract(coefficients, every_unit, 1, 0)
    column_terms = SCORE_SCALE * contract(coefficients, unit_low, 0, 0)
    unit_grad = unit_grad + lax.psum_scatter(
        column_terms, ("dp", "fsdp"), scatter_dimension=0, tiled=True
    )
    along = jnp.sum(unit_vector * unit_grad, axis=-1, keepdims=True)
    summary_grad = (unit_grad - unit_vector * along) / magnitude
    again_weights = (
        lax.all_gather(w_query, "fsdp", axis=0, tiled=True),
        lax.all_gather(w_key, "fsdp", axis=0, tiled=True),
        lax.all_gather(w_value, "fsdp", axis=0, tiled=True),
        lax.all_gather(w_out, "fsdp", axis=0, tiled=True),
        lax.all_gather(ln1_gain, "fsdp", axis=0, tiled=True),
        lax.all_gather(w_up, "fsdp", axis=0, tiled=True),
        lax.all_gather(w_down, "fsdp", axis=0, tiled=True),
        lax.all_gather(ln2_gain, "fsdp", axis=0, tiled=True),
    )
    again_wq, again_wk, again_wv, again_wo, again_g1, again_wup, again_wdown, again_g2 = (
        again_weights
    )
    residual_grad, grad_g2, grad_s2 = norm_back(
        summary_grad, first_rows(normed_two), first_rows(inverse_two), again_g2
    )
    down_grad = residual_grad.astype(jnp.bfloat16)
    activated_cls = first_rows(activated)
    act_grad = contract(down_grad, again_wdown, 1, 1)
    gelu_value, gelu_pull = jax.vjp(partial(jax.nn.gelu, approximate=False), first_rows(up_pre))
    up_grad = gelu_pull(act_grad)[0].astype(jnp.bfloat16)
    hidden_cls = first_rows(hidden_low)
    hidden_grad = contract(up_grad, again_wup, 1, 1) + residual_grad
    first_grad, grad_g1, grad_s1 = norm_back(
        hidden_grad, first_rows(normed_one), first_rows(inverse_one), again_g1
    )
    attend_grad = first_grad.astype(jnp.bfloat16)
    context_cls = first_rows(context)
    context_grad = (
        contract(attend_grad, again_wo, 1, 1).astype(jnp.bfloat16).reshape(sentences, HEADS, HEAD)
    )
    query_cls = query_heads[:, 0]
    cls_scores = (
        jnp.einsum("bhd,bkhd->bhk", query_cls, key_heads, preferred_element_type=jnp.float32)
        * score_factor
    )
    cls_scores = jnp.where(valid_mask[:, None, :], cls_scores, MASK_FLOOR)
    cls_probs = jnp.exp(cls_scores - row_peak[:, :, 0]) / totals[:, :, 0]
    prob_grad = jnp.einsum(
        "bhd,bkhd->bhk", context_grad, value_heads, preferred_element_type=jnp.float32
    )
    score_grad = (
        cls_probs * (prob_grad - jnp.sum(cls_probs * prob_grad, axis=-1, keepdims=True))
    ).astype(jnp.bfloat16)
    query_grad = (
        (
            jnp.einsum("bhk,bkhd->bhd", score_grad, key_heads, preferred_element_type=jnp.float32)
            * score_factor
        )
        .astype(jnp.bfloat16)
        .reshape(sentences, model_width)
    )
    key_grad = (
        (
            jnp.einsum("bhk,bhd->bkhd", score_grad, query_cls, preferred_element_type=jnp.float32)
            * score_factor
        )
        .astype(jnp.bfloat16)
        .reshape(tokens, model_width)
    )
    value_grad = (
        jnp.einsum(
            "bhk,bhd->bkhd",
            cls_probs.astype(jnp.bfloat16),
            context_grad,
            preferred_element_type=jnp.float32,
        )
        .astype(jnp.bfloat16)
        .reshape(tokens, model_width)
    )
    embedded_cls = first_rows(embedded)
    grad_wkey = contract(embedded, key_grad, 0, 0)
    grad_wvalue = contract(embedded, value_grad, 0, 0)
    grad_bvalue = jnp.sum(value_grad, axis=0, dtype=jnp.float32)
    row_grads = contract(key_grad, again_wk, 1, 1) + contract(value_grad, again_wv, 1, 1)
    summary_extra = contract(query_grad, again_wq, 1, 1) + first_grad
    row_grads = (
        row_grads.reshape(sentences, length, model_width)
        .at[:, 0]
        .add(summary_extra)
        .reshape(tokens, model_width)
    )
    outgoing = jnp.zeros((owners * capacity, model_width), jnp.float32).at[slot_of].set(row_grads)
    incoming = lax.all_to_all(
        lax.all_to_all(
            outgoing.reshape(dp_count, fsdp_count, capacity, model_width).astype(jnp.bfloat16),
            "dp",
            split_axis=0,
            concat_axis=0,
            tiled=True,
        ),
        "fsdp",
        split_axis=1,
        concat_axis=1,
        tiled=True,
    ).astype(jnp.float32)
    incoming = jnp.where(
        present.reshape(owners * capacity)[:, None],
        incoming.reshape(owners * capacity, model_width),
        0.0,
    )
    table_grad = (
        jnp.zeros((vocab_rows, model_width), jnp.float32)
        .at[local_rows.reshape(owners * capacity)]
        .add(incoming)
    )
    grad_wquery = contract(embedded_cls, query_grad, 0, 0)
    grad_bquery = jnp.sum(query_grad, axis=0, dtype=jnp.float32)
    grad_wout = contract(context_cls, attend_grad, 0, 0)
    grad_bout = jnp.sum(attend_grad, axis=0, dtype=jnp.float32)
    grad_wup = contract(hidden_cls, up_grad, 0, 0)
    grad_bup = jnp.sum(up_grad, axis=0, dtype=jnp.float32)
    grad_wdown = contract(activated_cls, down_grad, 0, 0)
    grad_bdown = jnp.sum(down_grad, axis=0, dtype=jnp.float32)
    owned_grads = (
        lax.psum_scatter(
            grad_wquery.astype(jnp.bfloat16), "fsdp", scatter_dimension=0, tiled=True
        ).astype(jnp.float32),
        lax.psum_scatter(
            grad_bquery.astype(jnp.bfloat16), "fsdp", scatter_dimension=0, tiled=True
        ).astype(jnp.float32),
        lax.psum_scatter(
            grad_wkey.astype(jnp.bfloat16), "fsdp", scatter_dimension=0, tiled=True
        ).astype(jnp.float32),
        lax.psum_scatter(
            grad_wvalue.astype(jnp.bfloat16), "fsdp", scatter_dimension=0, tiled=True
        ).astype(jnp.float32),
        lax.psum_scatter(
            grad_bvalue.astype(jnp.bfloat16), "fsdp", scatter_dimension=0, tiled=True
        ).astype(jnp.float32),
        lax.psum_scatter(
            grad_wout.astype(jnp.bfloat16), "fsdp", scatter_dimension=0, tiled=True
        ).astype(jnp.float32),
        lax.psum_scatter(
            grad_bout.astype(jnp.bfloat16), "fsdp", scatter_dimension=0, tiled=True
        ).astype(jnp.float32),
        lax.psum_scatter(
            grad_g1.astype(jnp.bfloat16), "fsdp", scatter_dimension=0, tiled=True
        ).astype(jnp.float32),
        lax.psum_scatter(
            grad_s1.astype(jnp.bfloat16), "fsdp", scatter_dimension=0, tiled=True
        ).astype(jnp.float32),
        lax.psum_scatter(
            grad_wup.astype(jnp.bfloat16), "fsdp", scatter_dimension=0, tiled=True
        ).astype(jnp.float32),
        lax.psum_scatter(
            grad_bup.astype(jnp.bfloat16), "fsdp", scatter_dimension=0, tiled=True
        ).astype(jnp.float32),
        lax.psum_scatter(
            grad_wdown.astype(jnp.bfloat16), "fsdp", scatter_dimension=0, tiled=True
        ).astype(jnp.float32),
        lax.psum_scatter(
            grad_bdown.astype(jnp.bfloat16), "fsdp", scatter_dimension=0, tiled=True
        ).astype(jnp.float32),
        lax.psum_scatter(
            grad_g2.astype(jnp.bfloat16), "fsdp", scatter_dimension=0, tiled=True
        ).astype(jnp.float32),
        lax.psum_scatter(
            grad_s2.astype(jnp.bfloat16), "fsdp", scatter_dimension=0, tiled=True
        ).astype(jnp.float32),
    )
    summed = (
        lax.psum(owned_grads[0].astype(jnp.bfloat16), "dp").astype(jnp.float32),
        lax.psum(owned_grads[1].astype(jnp.bfloat16), "dp").astype(jnp.float32),
        lax.psum(owned_grads[2].astype(jnp.bfloat16), "dp").astype(jnp.float32),
        lax.psum(owned_grads[3].astype(jnp.bfloat16), "dp").astype(jnp.float32),
        lax.psum(owned_grads[4].astype(jnp.bfloat16), "dp").astype(jnp.float32),
        lax.psum(owned_grads[5].astype(jnp.bfloat16), "dp").astype(jnp.float32),
        lax.psum(owned_grads[6].astype(jnp.bfloat16), "dp").astype(jnp.float32),
        lax.psum(owned_grads[7].astype(jnp.bfloat16), "dp").astype(jnp.float32),
        lax.psum(owned_grads[8].astype(jnp.bfloat16), "dp").astype(jnp.float32),
        lax.psum(owned_grads[9].astype(jnp.bfloat16), "dp").astype(jnp.float32),
        lax.psum(owned_grads[10].astype(jnp.bfloat16), "dp").astype(jnp.float32),
        lax.psum(owned_grads[11].astype(jnp.bfloat16), "dp").astype(jnp.float32),
        lax.psum(owned_grads[12].astype(jnp.bfloat16), "dp").astype(jnp.float32),
        lax.psum(owned_grads[13].astype(jnp.bfloat16), "dp").astype(jnp.float32),
        lax.psum(owned_grads[14].astype(jnp.bfloat16), "dp").astype(jnp.float32),
    )
    return (
        layer_out,
        loss_value,
        table_grad,
        summed[0],
        summed[1],
        summed[2],
        summed[3],
        summed[4],
        summed[5],
        summed[6],
        summed[7],
        summed[8],
        summed[9],
        summed[10],
        summed[11],
        summed[12],
        summed[13],
        summed[14],
    )


CORES = 2
PLANES = 4
LINES = 4
CHIPS = PLANES * LINES
DEVICES = CORES * CHIPS
CAPACITY = 48
GROUPS = 3
PAD = 16
TOKENS = 768
WIDTH = 768
WIDE = 3072
VOCAB_ROWS = 1024
PAIR_ROWS = HEADS * PAD
SLOT_ROWS = DEVICES * PAD
LONG = 64
BLOCK = 256
MESH = pl.DeviceIdType.MESH
LOW = jnp.bfloat16
FULL = jnp.float32
VMEM_LIMIT = 62 * 1024 * 1024

INPUTS = ["table", "token_ids", "lens", "slots", "langs"]
INPUTS += ["wq", "bq", "wk", "wv", "bv", "wo", "bo", "g1", "s1", "wup", "bup", "wdown", "bdown"]
INPUTS += ["g2", "s2"]
OUTPUTS = ["layer_out", "table_grad", "g_wq", "g_wk", "g_wv", "g_wo", "g_wup", "g_wdown"]
OUTPUTS += ["g_small", "loss"]


def place():
    core = lax.axis_index("dp")
    chip = lax.axis_index("fsdp")
    along_x = chip + 1 - 2 * (chip % 2)
    along_y = chip + 2 - 4 * ((chip // 2) % 2)
    first = along_x + core * (along_y - along_x)
    second = along_y + core * (along_x - along_y)
    return core, chip, first, second


def greet():
    core, chip, _, _ = place()
    me = core * CHIPS + chip
    barrier = pltpu.get_barrier_semaphore()

    def signal(step):
        other = lax.rem(me + step, DEVICES)
        pl.semaphore_signal(
            barrier,
            inc=1,
            device_id=(lax.div(other, CHIPS), lax.rem(other, CHIPS)),
            device_id_type=MESH,
        )

    every(1, DEVICES, signal)


def enter():
    pl.semaphore_wait(pltpu.get_barrier_semaphore(), DEVICES - 1)


def remote(source, target, send_sem, recv_sem, core, chip):
    return pltpu.make_async_remote_copy(
        src_ref=source,
        dst_ref=target,
        send_sem=send_sem,
        recv_sem=recv_sem,
        device_id=(core, chip),
        device_id_type=MESH,
    )


def every(start, stop, act):
    def step(index, carry):
        act(index)
        return carry

    lax.fori_loop(start, stop, step, 0)


def weight_steps(buffer, depth, send, recv):
    core, chip, first, second = place()
    plane, line = chip // LINES, chip % LINES
    line_first, line_second = first % LINES, second % LINES
    line_far = line_first + line_second - line
    is_low, is_high = plane > 0, plane < PLANES - 1
    half = buffer.shape[1] // 2
    by_place = buffer.reshape(PLANES, LINES, depth, buffer.shape[1])
    columns = pl.ds(pl.multiple_of(core * half, 128), half)
    others = pl.ds(pl.multiple_of((1 - core) * half, 128), half)

    def copy(send_index, recv_index, part, to_core, to_chip):
        return remote(part, part, send.at[send_index], recv.at[recv_index], to_core, to_chip)

    def piece(at_plane, which):
        return by_place.at[at_plane, line, :, which]

    def lines(at_line, which):
        return by_place.at[:, at_line, :, which]

    def up(at_plane):
        return copy(at_plane, at_plane, piece(at_plane, columns), core, chip + LINES)

    def down(at_plane, index):
        return copy(index, at_plane, piece(at_plane, columns), core, chip - LINES)

    def begin():
        pl.when(is_high)(lambda: up(plane).start())
        pl.when(is_low)(lambda: down(plane, PLANES).start())

    def chain(distance):
        def from_low():
            up(plane - distance).wait_recv()
            pl.when(is_high)(lambda: up(plane - distance).start())

        def from_high():
            at = plane + distance
            down(at, at).wait_recv()
            pl.when(is_low)(lambda: down(at, at).start())

        pl.when(plane >= distance)(from_low)
        pl.when(plane + distance < PLANES)(from_high)

    def across(step, which):
        at = (plane + step) % PLANES
        return copy(7 + step, 7 + step, piece(at, which), 1 - core, chip)

    def sides():
        copy(5, 5, lines(line, columns), core, first).start()
        copy(6, 6, lines(line, columns), core, second).start()
        for step in range(1, PLANES):
            across(step, columns).start()

    def corner():
        copy(5, 5, lines(line_first, columns), core, first).wait_recv()
        copy(7, 7, lines(line_first, columns), core, second).start()
        copy(11, 11, lines(line_first, columns), 1 - core, chip).start()
        copy(6, 6, lines(line_second, columns), core, second).wait_recv()
        copy(12, 12, lines(line_second, columns), 1 - core, chip).start()

    def last():
        copy(7, 7, lines(line_far, columns), core, second).wait_recv()
        copy(13, 13, lines(line_far, columns), 1 - core, chip).start()

    def finish():
        for step in range(1, PLANES):
            across(step, others).wait_recv()
        copy(11, 11, lines(line_second, others), 1 - core, chip).wait_recv()
        copy(12, 12, lines(line_first, others), 1 - core, chip).wait_recv()
        copy(13, 13, lines(line_far, others), 1 - core, chip).wait_recv()

    def drain():
        def sent(index):
            copy(index, index, piece(plane, columns), 1 - core, chip).wait_send()

        for at_plane in range(PLANES):
            pl.when((plane >= at_plane) & is_high)(partial(sent, at_plane))
            pl.when((plane < at_plane) & is_low)(partial(sent, at_plane))
        pl.when(is_low)(partial(sent, PLANES))
        every(8, 11, sent)
        for index in [5, 6, 7, 11, 12, 13]:
            copy(index, index, lines(line, columns), 1 - core, chip).wait_send()

    steps = SimpleNamespace(
        begin=begin, chain=chain, sides=sides, corner=corner, last=last, finish=finish
    )
    return steps, drain


def gather_steps(buffer, send, recv):
    core, chip, first, second = place()
    plane, line = chip // LINES, chip % LINES
    line_first, line_second = first % LINES, second % LINES
    line_far = line_first + line_second - line
    half = buffer.shape[-1] // 2
    columns = pl.ds(pl.multiple_of(core * half, 128), half)
    others = pl.ds(pl.multiple_of((1 - core) * half, 128), half)

    def copy(index, part, to_core, to_chip):
        return remote(part, part, send.at[index], recv.at[index], to_core, to_chip)

    def own(at):
        return buffer.at[at, plane, line]

    def chip_part(at_plane, at_line, which):
        return buffer.at[:, at_plane, at_line, :, which]

    def line_part(at_line, which):
        return buffer.at[:, :, at_line, :, which]

    def start():
        copy(0, own(core), 1 - core, chip).start()

    def planes():
        copy(0, own(1 - core), 1 - core, chip).wait_recv()
        for step in range(1, PLANES):
            part = chip_part(plane, line, columns)
            copy(step, part, core, (chip + LINES * step) % CHIPS).start()

    def sides():
        for step in range(1, PLANES):
            part = chip_part((plane + PLANES - step) % PLANES, line, columns)
            copy(step, part, core, chip).wait_recv()
        copy(4, line_part(line, columns), core, first).start()
        copy(5, line_part(line, columns), core, second).start()
        for step in range(1, PLANES):
            part = chip_part((plane + PLANES - step) % PLANES, line, columns)
            copy(6 + step, part, 1 - core, chip).start()

    def corner():
        copy(4, line_part(line_first, columns), core, first).wait_recv()
        copy(6, line_part(line_first, columns), core, second).start()
        copy(10, line_part(line_first, columns), 1 - core, chip).start()
        copy(5, line_part(line_second, columns), core, second).wait_recv()
        copy(11, line_part(line_second, columns), 1 - core, chip).start()

    def last():
        copy(6, line_part(line_far, columns), core, second).wait_recv()
        copy(12, line_part(line_far, columns), 1 - core, chip).start()

    def finish():
        for step in range(1, PLANES):
            part = chip_part((plane + PLANES - step) % PLANES, line, others)
            copy(6 + step, part, 1 - core, chip).wait_recv()
        copy(10, line_part(line_second, others), 1 - core, chip).wait_recv()
        copy(11, line_part(line_first, others), 1 - core, chip).wait_recv()
        copy(12, line_part(line_far, others), 1 - core, chip).wait_recv()

    def drain():
        copy(0, own(core), 1 - core, chip).wait_send()
        for index in [1, 2, 3, 7, 8, 9]:
            copy(index, chip_part(plane, line, columns), 1 - core, chip).wait_send()
        for index in [4, 5, 6, 10, 11, 12]:
            copy(index, line_part(line, columns), 1 - core, chip).wait_send()

    return [start, planes, sides, corner, last, finish], drain


def iota(shape, axis):
    return lax.broadcasted_iota(jnp.int32, shape, axis)


def as_column(row):
    parts = []
    for start in range(0, row.shape[1], 128):
        tile = jnp.broadcast_to(row[:, start : start + 128], (128, 128))
        parts.append(jnp.transpose(tile)[:, 0:1])
    return jnp.concatenate(parts, axis=0)


def as_row(column):
    parts = []
    for start in range(0, column.shape[0], 128):
        tile = jnp.broadcast_to(column[start : start + 128, :], (128, 128))
        parts.append(jnp.transpose(tile)[0:1, :])
    return jnp.concatenate(parts, axis=1)


def dot(left_side, right_side):
    return contract(left_side, right_side, 1, 0)


def dot_turned(left_side, right_side):
    return contract(left_side, right_side, 1, 1)


def norm_parts(inputs):
    centered = inputs - jnp.mean(inputs, axis=-1, keepdims=True)
    inverse = lax.rsqrt(jnp.mean(centered * centered, axis=-1, keepdims=True) + EPSILON)
    return centered * inverse, inverse


def norm_back_parts(grad_output, normed, inverse, ln_gain):
    grad_normed = grad_output * ln_gain
    first_term = jnp.mean(grad_normed, axis=-1, keepdims=True)
    second_term = jnp.mean(grad_normed * normed, axis=-1, keepdims=True)
    return (
        inverse * (grad_normed - first_term - normed * second_term),
        jnp.sum(grad_output * normed, axis=0, keepdims=True),
        jnp.sum(grad_output, axis=0, keepdims=True),
    )


def erf_parts(inputs):
    decay = jnp.exp(-0.5 * inputs * inputs)
    share = 1.0 / (1.0 + jnp.abs(inputs) * (0.3275911 * 0.5**0.5))
    terms = [1.061405429, -1.453152027, 1.421413741, -0.284496736, 0.254829592]
    series = 0.5 * terms[0]
    for term in terms[1:]:
        series = series * share + 0.5 * term
    tail = series * share * decay
    return jnp.where(inputs >= 0.0, 1.0 - tail, tail), decay


def gelu_parts(inputs):
    below, decay = erf_parts(inputs)
    return inputs * below, below + inputs * decay * ((2.0 * 3.141592653589793) ** -0.5)


def gelu(inputs):
    return inputs * erf_parts(inputs)[0]


def layer_kernel(names, *refs):
    r = SimpleNamespace(**dict(zip(names, refs, strict=True)))
    core, chip, _, _ = place()
    me = core * CHIPS + chip
    here = (core, chip // LINES, chip % LINES)
    scale = HEAD ** (-0.5)
    depth, deep = WIDTH // CHIPS, WIDE // CHIPS
    sentences = TOKENS // LONG

    for j in range(TOKENS // 128):
        r.ids[j : j + 1, :] = jnp.concatenate(
            [r.token_ids[2 * j : 2 * j + 1, :], r.token_ids[2 * j + 1 : 2 * j + 2, :]], axis=1
        )
    r.ids[TOKENS // 128 : 8, :] = jnp.zeros((8 - TOKENS // 128, 128), jnp.int32)
    greet()
    ahead = (iota((TOKENS, TOKENS), 0) < iota((TOKENS, TOKENS), 1)).astype(LOW)
    r.embedded[...] = ahead
    mine = pl.ds(pl.multiple_of(chip * depth, 16), depth)
    for index, shard in enumerate([r.wq, r.wk, r.wv, r.wo]):
        r.wa[mine, index * WIDTH : (index + 1) * WIDTH] = shard[...]
    r.wb[mine, :] = r.wup[...]
    r.wc[pl.ds(pl.multiple_of(chip * deep, 16), deep), :] = r.wdown[...]
    r.every_ids[me] = r.ids[...]
    enter()

    def peer(step):
        other = lax.rem(me + step, DEVICES)
        return other, lax.div(other, CHIPS), lax.rem(other, CHIPS)

    def ids_copy(step):
        other, to_core, to_chip = peer(step)
        return remote(r.ids, r.every_ids.at[me], r.one_send.at[0], r.one_recv.at[0], to_core, to_chip)

    def all_but_one(ref, index):
        part = ref.at[0 : DEVICES - 1]
        return remote(part, part, r.one_send.at[index], r.one_recv.at[index], 1 - core, chip)

    every(1, DEVICES, lambda step: ids_copy(step).start())

    a_steps, drain_a = weight_steps(r.wa, depth, r.weight_send.at[0], r.weight_recv.at[0])
    b_steps, drain_b = weight_steps(r.wb, depth, r.weight_send.at[1], r.weight_recv.at[1])
    c_steps, drain_c = weight_steps(r.wc, deep, r.weight_send.at[2], r.weight_recv.at[2])
    a_steps.begin()
    b_steps.begin()
    c_steps.begin()

    all_but_one(r.every_ids, 0).wait_recv()
    all_ids = jnp.concatenate([r.every_ids[:, j, :] for j in range(TOKENS // 128)], axis=1)
    all_owner = all_ids // VOCAB_ROWS
    asked = all_owner == me
    ranks = dot(asked.astype(LOW), r.embedded[...])
    r.rank[...] = jnp.where(asked, ranks, -1.0)
    local_row = (all_ids - all_owner * VOCAB_ROWS + 1).astype(FULL)
    r.code[...] = local_row + (iota((DEVICES, TOKENS), 1) // LONG * 2048).astype(FULL)

    quarter_size = DEVICES // 4

    def rows_copy(other, quarter):
        return remote(
            r.rows.at[:, pl.ds(pl.multiple_of(other * PAD, 16), PAD), :],
            r.replies.at[:, pl.ds(pl.multiple_of(me * PAD, 16), PAD), :],
            r.rows_send.at[quarter],
            r.rows_recv.at[quarter],
            lax.div(other, CHIPS),
            lax.rem(other, CHIPS),
        )

    def rows_of(quarter):
        count = quarter_size - 1 if quarter == 3 else quarter_size
        part = r.replies.at[:, 0 : count * PAD, :]
        return remote(
            part, part, r.rows_send.at[quarter], r.rows_recv.at[quarter], 1 - core, chip
        )

    def pick(source):
        rank = r.rank[pl.ds(source, 1), :]
        code = r.code[pl.ds(source, 1), :]
        here_at = iota((CAPACITY, TOKENS), 0).astype(FULL) == rank
        found = jnp.sum(jnp.where(here_at, code, 0.0), axis=1, keepdims=True)
        sent = jnp.floor(found * (1.0 / 2048))
        row = found - sent * 2048.0 - 1.0
        chosen = (iota((CAPACITY, VOCAB_ROWS), 1).astype(FULL) == row).astype(LOW)
        at = pl.ds(pl.multiple_of(source * PAD, 16), PAD)
        source_sent = sent + (source * PAD).astype(FULL)
        for group in range(GROUPS):
            part = slice(group * PAD, (group + 1) * PAD)
            r.chosen[group, at, :] = chosen[part]
            r.found[group, at, 0:1] = row[part]
            r.found[group, at, 1:2] = source_sent[part]

    def quarter_rows(quarter):
        now = lax.rem(lax.div(me, quarter_size) + 1 + quarter, 4)

        def pick_two(index):
            pick(now * quarter_size + 2 * index)
            pick(now * quarter_size + 2 * index + 1)

        every(0, quarter_size // 2, pick_two)
        span = pl.ds(pl.multiple_of(now * quarter_size * PAD, 128), quarter_size * PAD)
        for start in range(0, WIDTH, BLOCK):
            lanes = slice(start, start + BLOCK)
            picked = r.chosen[:, span, :].reshape(GROUPS * quarter_size * PAD, VOCAB_ROWS)
            found_rows = dot(picked, r.table[:, lanes]).astype(LOW)
            r.rows[:, span, lanes] = found_rows.reshape(GROUPS, quarter_size * PAD, BLOCK)

        def send(index):
            other = now * quarter_size + lax.rem(lax.rem(me, quarter_size) + index, quarter_size)
            rows_copy(other, quarter).start()

        every(lax.div(quarter, 3), quarter_size, send)
        pl.when(quarter == 0)(lambda: a_steps.chain(1))
        pl.when(quarter == 1)(lambda: b_steps.chain(1))

    every(0, 4, quarter_rows)
    c_steps.chain(1)
    a_steps.chain(2)
    b_steps.chain(2)
    c_steps.chain(2)
    a_steps.chain(3)
    a_steps.sides()
    own_at = pl.ds(pl.multiple_of(me * PAD, 16), PAD)
    r.replies[:, own_at, :] = r.rows[:, own_at, :]

    small_here = pl.ds(pl.multiple_of(chip * 128, 128), 128)
    lines = [r.bq, r.bv, r.bo, r.g1, r.s1, r.bdown, r.g2, r.s2]
    lines = [line[...].reshape(1, depth).astype(FULL) for line in lines]
    up_line = r.bup[...].reshape(1, deep).astype(FULL)
    lines += [up_line[:, part * depth : (part + 1) * depth] for part in range(deep // depth)]
    lines.append(jnp.zeros((PAD - len(lines), depth), FULL))
    own_small = jnp.concatenate(lines, axis=0)
    own_small = jnp.concatenate([own_small, jnp.zeros((PAD, 128 - depth), FULL)], axis=1)
    r.smalls[:, small_here] = own_small.astype(LOW)

    def small_copy(step):
        part = r.smalls.at[:, small_here]
        to_chip = lax.rem(chip + step, CHIPS)
        return remote(part, part, r.small_send.at[0], r.small_recv.at[0], core, to_chip)

    def all_smalls():
        part = r.smalls.at[:, 0 : (CHIPS - 1) * 128]
        return remote(part, part, r.small_send.at[0], r.small_recv.at[0], 1 - core, chip)

    every(1, CHIPS, lambda step: small_copy(step).start())
    b_steps.chain(3)
    b_steps.sides()

    own_row = jnp.concatenate([r.ids[j : j + 1, :] for j in range(TOKENS // 128)], axis=1)
    owner_row = (own_row // VOCAB_ROWS).astype(FULL)
    owner_col = as_column(owner_row)
    earlier = (owner_row == owner_col) & (iota((TOKENS, TOKENS), 1) < iota((TOKENS, TOKENS), 0))
    own_rank = jnp.sum(earlier.astype(FULL), axis=1, keepdims=True)
    own_group = jnp.floor(own_rank * (1.0 / PAD))
    own_slot = own_group * SLOT_ROWS + owner_col * PAD + (own_rank - own_group * PAD)
    r.slot_col[...] = own_slot
    r.slot_line[0:1, :] = as_row(own_slot)
    c_steps.chain(3)
    c_steps.sides()
    a_steps.corner()

    at_sent = iota((1, TOKENS), 1) // LONG
    lens = jnp.concatenate(
        [r.lens[...].reshape(1, sentences).astype(FULL), jnp.zeros((1, PAD - sentences), FULL)],
        axis=1,
    )
    spread_lens = dot(
        jnp.broadcast_to(lens, (8, PAD)).astype(LOW),
        (iota((PAD, TOKENS), 0) == iota((PAD, TOKENS), 1) // LONG).astype(LOW),
    )[0:1]
    valid_row = ((iota((1, TOKENS), 1) - at_sent * LONG).astype(FULL) < spread_lens).astype(FULL)
    r.valid_line[0:1, :] = valid_row
    r.valid_col[...] = as_column(valid_row)
    half_block = BLOCK // 2
    stacked_shape = (4 * half_block, half_block)
    same = iota(stacked_shape, 0) // LONG % 2 == iota(stacked_shape, 1) // LONG
    r.block_bias[...] = jnp.where(same, 0.0, MASK_FLOOR)
    r.valid_bias[0:1, :] = (1.0 - valid_row) * MASK_FLOOR

    slots = r.slots[...].reshape(1, DEVICES * sentences)
    gap = jnp.full((1, PAD - sentences), -2, jnp.int32)
    slot_line = jnp.concatenate(
        [
            part
            for device in range(DEVICES)
            for part in (slots[:, device * sentences : (device + 1) * sentences], gap)
        ],
        axis=1,
    )
    side_line = slot_line - slot_line // 2 * 2 + jnp.where(slot_line < 0, 8, 0)
    pair_line = slot_line // 2
    pairs = r.langs.shape[0]
    lang_line = r.langs[...].reshape(1, pairs).astype(FULL)
    lang_line = jnp.concatenate([lang_line, jnp.full((1, -pairs % 128), -1.0, FULL)], axis=1)
    lang_col = as_column(lang_line)
    same_lang = jnp.sum(jnp.where(lang_col == lang_line, 1.0, 0.0), axis=1, keepdims=True)
    per_pair = 1.0 / (2.0 * LANGS * same_lang)
    at_pair = iota((lang_line.shape[1], SLOT_ROWS), 0) == pair_line
    weight_line = jnp.sum(jnp.where(at_pair, per_pair, 0.0), axis=0, keepdims=True)
    r.pairs[0:1, :] = weight_line
    r.pairs[1:2, :] = pair_line.astype(FULL)
    r.pairs[2:3, :] = side_line.astype(FULL)
    r.pairs_col[:, 0:1] = as_column(weight_line)
    r.pairs_col[:, 1:2] = as_column(pair_line.astype(FULL))
    r.pairs_col[:, 2:3] = as_column(side_line.astype(FULL))
    b_steps.corner()
    a_steps.last()

    all_smalls().wait_recv()
    smalls = r.smalls[...].astype(FULL)
    r.vectors[:, 0:WIDTH] = jnp.concatenate(
        [smalls[:, at * 128 : at * 128 + depth] for at in range(CHIPS)], axis=1
    )
    r.up_bias[0:1, :] = jnp.concatenate(
        [
            smalls[8 + part : 9 + part, at * 128 : at * 128 + depth]
            for at in range(CHIPS)
            for part in range(deep // depth)
        ],
        axis=1,
    )

    def vector(index):
        return r.vectors[index : index + 1, :]

    r.qkv_bias[0:1, 0:WIDTH] = vector(0)
    r.qkv_bias[0:1, WIDTH : 2 * WIDTH] = jnp.zeros((1, WIDTH), FULL)
    r.qkv_bias[0:1, 2 * WIDTH : 3 * WIDTH] = vector(1)

    c_steps.corner()
    b_steps.last()

    def first_row(source):
        code = jnp.where(r.rank[pl.ds(source, 1), :] >= 0.0, r.code[pl.ds(source, 1), :], 0.0)
        at_first = iota((PAD, TOKENS), 1) == iota((PAD, TOKENS), 0) * LONG
        found = jnp.sum(jnp.where(at_first, code, 0.0), axis=1, keepdims=True)
        row = found - jnp.floor(found * (1.0 / 2048)) * 2048.0 - 1.0
        r.found[GROUPS, pl.ds(pl.multiple_of(source * PAD, 16), PAD), 0:1] = row

    every(0, DEVICES, first_row)
    for group in range(GROUPS + 1):
        named = as_row(r.found[group, :, 0:1])
        by_row = iota((VOCAB_ROWS, SLOT_ROWS), 0).astype(FULL) == named
        r.by_row[:, group * SLOT_ROWS : (group + 1) * SLOT_ROWS] = by_row.astype(LOW)

    def order(tile):
        at = pl.ds(pl.multiple_of(tile * BLOCK, BLOCK), BLOCK)
        lanes = iota((BLOCK, GROUPS * SLOT_ROWS), 1).astype(FULL)
        r.qkv[at, 0 : GROUPS * SLOT_ROWS] = (r.slot_col[at, :] == lanes).astype(LOW)

    every(0, TOKENS // BLOCK, order)
    for group in range(GROUPS):
        slot_at = iota((SLOT_ROWS, TOKENS), 0) + group * SLOT_ROWS
        named = (slot_at.astype(FULL) == r.slot_line[0:1, :]).astype(LOW)
        r.chosen[group, :, 0:TOKENS] = named
    c_steps.last()
    a_steps.finish()
    for quarter in range(4):
        rows_of(quarter).wait_recv()

    def embed(tile):
        at = pl.ds(pl.multiple_of(tile * BLOCK, BLOCK), BLOCK)
        replies = r.replies[:, :, at].reshape(GROUPS * SLOT_ROWS, BLOCK)
        r.embedded[:, at] = dot(r.qkv[:, 0 : GROUPS * SLOT_ROWS], replies).astype(LOW)

    every(0, WIDTH // BLOCK, embed)

    def project(tile):
        at = pl.ds(pl.multiple_of(tile * BLOCK, BLOCK), BLOCK)
        r.qkv[:, at] = (dot(r.embedded[...], r.wa[:, at]) + r.qkv_bias[0:1, at]).astype(LOW)

    every(0, 9, project)

    row_sent = iota((PAIR_ROWS, WIDTH), 0) % PAD
    row_head = iota((PAIR_ROWS, WIDTH), 0) // PAD
    lane_block = iota((PAIR_ROWS, WIDTH), 1) // HEAD
    in_head = row_head == lane_block
    seen = (row_sent == lane_block) & (r.valid_line[0:1, :] > 0.0)
    firsts = (iota((PAD, TOKENS), 1) == iota((PAD, TOKENS), 0) * LONG).astype(LOW)
    real_row = iota((PAD, 1), 0) < sentences

    def spread(rows):
        return jnp.where(in_head, jnp.concatenate([rows] * HEADS, axis=0), jnp.zeros((), LOW))

    def fold(tall):
        tall = jnp.where(in_head, tall, 0.0)
        return sum(tall[head * PAD : (head + 1) * PAD] for head in range(HEADS))

    keys, values = slice(WIDTH, 2 * WIDTH), slice(2 * WIDTH, 3 * WIDTH)
    embedded_cls = dot(firsts, r.embedded[...]).astype(LOW)
    query_cls = (dot(embedded_cls, r.wa[:, 0:WIDTH]) + vector(0)).astype(LOW)
    cls_scores = dot_turned(spread(query_cls), r.qkv[:, keys]) * scale
    cls_scores = jnp.where(seen, cls_scores, MASK_FLOOR)
    cls_peak = jnp.max(cls_scores, axis=1, keepdims=True)
    cls_exp = jnp.where(seen, jnp.exp(cls_scores - cls_peak), 0.0)
    cls_total = jnp.sum(cls_exp, axis=1, keepdims=True)
    cls_probs = cls_exp / jnp.where(cls_total > 0.0, cls_total, 1.0)
    probs_low = cls_probs.astype(LOW)
    r.probs[...] = cls_probs
    context_cls = fold(dot(probs_low, r.qkv[:, values])).astype(LOW)
    first_cls = (
        embedded_cls.astype(FULL)
        + dot(context_cls, r.wa[:, 3 * WIDTH : 4 * WIDTH])
        + vector(2)
    )
    normed_one, inverse_one = norm_parts(first_cls)
    r.normed_one[...] = normed_one
    hidden_cls = normed_one * vector(3) + vector(4)
    hidden_cls_low = hidden_cls.astype(LOW)
    early_here = r.early.at[here]
    early_here[:, 0:WIDTH] = hidden_cls_low
    early_here[:, WIDTH : 2 * WIDTH] = query_cls
    steps_u, drain_u = gather_steps(r.units, r.gather_send.at[0], r.gather_recv.at[0])
    steps_e, drain_e = gather_steps(r.early, r.gather_send.at[1], r.gather_recv.at[1])
    steps_d, drain_d = gather_steps(r.downs, r.gather_send.at[2], r.gather_recv.at[2])
    steps_a, drain_a2 = gather_steps(r.attends, r.gather_send.at[3], r.gather_recv.at[3])
    steps_q, drain_q = gather_steps(r.queries, r.gather_send.at[4], r.gather_recv.at[4])
    steps_e[0]()

    def attend(unit):
        rows = pl.ds(pl.multiple_of(unit * half_block, half_block), half_block)
        lane_head = iota((half_block, BLOCK), 1) // HEAD
        bias = r.block_bias[...] + r.valid_bias[0:1, rows]

        def part(which, lane):
            return r.qkv[rows, which * WIDTH + lane : which * WIDTH + lane + BLOCK]

        for lane in range(0, WIDTH, BLOCK):
            query = part(0, lane) * jnp.asarray(scale, LOW)
            key, value = part(1, lane), part(2, lane)
            stacked = jnp.concatenate(
                [jnp.where(lane_head == head, query, jnp.zeros((), LOW)) for head in range(4)],
                axis=0,
            )
            scores = dot_turned(stacked, key) + bias
            shifted = jnp.exp(scores - jnp.max(scores, axis=1, keepdims=True))
            probs = shifted * (1.0 / jnp.sum(shifted, axis=1, keepdims=True))
            mixed = dot(probs.astype(LOW), value)
            result = mixed[0:half_block]
            for head in range(1, 4):
                result = jnp.where(
                    lane_head == head, mixed[head * half_block : (head + 1) * half_block], result
                )
            r.context[rows, lane : lane + BLOCK] = result.astype(LOW)

    def open_tile(tile):
        at = pl.ds(pl.multiple_of(tile * BLOCK, BLOCK), BLOCK)
        attended = dot(r.context[at, :], r.wa[:, 3 * WIDTH : 4 * WIDTH]) + vector(2)
        normed, _ = norm_parts(r.embedded[at, :].astype(FULL) + attended)
        hidden = normed * vector(3) + vector(4)
        r.context[at, :] = hidden.astype(LOW)
        r.table_full[at, :] = hidden + vector(5)

    most = SLOT_ROWS
    rest_at = pl.ds(most, TOKENS - most)

    def feed_up(part):
        at = pl.ds(pl.multiple_of(part * BLOCK, BLOCK), BLOCK)
        up_pre = dot(r.context[...], r.wb[:, at]) + r.up_bias[0:1, at]
        active = gelu(up_pre).astype(LOW)
        lanes = pl.ds(pl.multiple_of(lax.rem(part, 4) * BLOCK, BLOCK), BLOCK)
        r.chosen[lax.div(part, 4), :, lanes] = active[:most]
        rest = pl.ds(pl.multiple_of(lax.div(part, 6) * BLOCK, BLOCK), BLOCK)
        lanes = pl.ds(pl.multiple_of(lax.rem(part, 6) * BLOCK, BLOCK), BLOCK)
        r.slopes[rest, lanes] = active[most:]

    def feed_down(part):
        lanes = pl.ds(pl.multiple_of(part * BLOCK, BLOCK), BLOCK)
        total = r.table_full[0:most, lanes]
        for group in range(GROUPS):
            rows = slice(group * VOCAB_ROWS, (group + 1) * VOCAB_ROWS)
            total = total + dot(r.chosen[group], r.wc[rows, lanes])
        r.table_full[0:most, lanes] = total

    def feed_rest(part):
        lanes = pl.ds(pl.multiple_of(part * BLOCK, BLOCK), BLOCK)
        low_part = dot(r.slopes[0:BLOCK, :], r.wc[0 : WIDE // 2, lanes])
        high_part = dot(r.slopes[BLOCK : 2 * BLOCK, :], r.wc[WIDE // 2 :, lanes])
        r.table_full[rest_at, lanes] += low_part + high_part

    def layer_copy(tile):
        at = pl.ds(pl.multiple_of(tile * BLOCK, BLOCK), BLOCK)
        return pltpu.make_async_copy(r.context.at[at], r.layer_out.at[at], r.out_sem.at[tile])

    def close_tile(tile):
        at = pl.ds(pl.multiple_of(tile * BLOCK, BLOCK), BLOCK)
        normed, _ = norm_parts(r.table_full[at, :])
        out = normed * vector(6) + vector(7)
        r.context[at, :] = (out * r.valid_col[at, :]).astype(LOW)
        layer_copy(tile).start()

    b_steps.finish()
    r.hidden_cls[...] = hidden_cls_low

    def up_part(part):
        at = pl.ds(pl.multiple_of(part * BLOCK, BLOCK), BLOCK)
        active, slope = gelu_parts(dot(r.hidden_cls[...], r.wb[:, at]) + r.up_bias[0:1, at])
        r.active_cls[:, at] = active.astype(LOW)
        r.slope_cls[:, at] = slope

    every(0, WIDE // BLOCK, up_part)
    steps_e[1]()
    c_steps.finish()

    def pack_tall(target, first_row, act):
        def run(part):
            shape = (WIDTH, 2 * 128)
            lane = iota(shape, 1)
            chip_lane = lane % 128
            column = (2 * part + lane // 128) * depth + chip_lane
            low_part = ((iota(shape, 0) == column) & (chip_lane < depth)).astype(LOW)
            high_part = ((iota(shape, 0) == column - depth) & (chip_lane < 2 * depth)).astype(LOW)
            high_part = jnp.where(chip_lane >= depth, high_part, jnp.zeros((), LOW))
            low_rows = dot(r.tall[...], low_part)
            high_rows = dot(r.tall[...], high_part)
            for half in range(CORES):
                base = half * PAIR_ROWS // 2
                both = low_rows[base : base + 48] + high_rows[base + 48 : base + 96]
                for one in range(2):
                    at = half * CHIPS + 2 * part + one
                    target[at, first_row : first_row + 48, :] = (
                        act(2 * part + one, both[:, one * 128 : (one + 1) * 128])
                    ).astype(LOW)
            left = low_rows[PAIR_ROWS : PAIR_ROWS + PAD] + high_rows[PAIR_ROWS + PAD :]
            if first_row:
                for half in range(CORES):
                    for one in range(2):
                        at = half * CHIPS + 2 * part + one
                        target[at, 0:PAD, :] = left[:, one * 128 : (one + 1) * 128].astype(LOW)

        return run

    def pack_coefs(coefs):
        shape = (PAIR_ROWS, GROUPS * 128)
        folds = iota(shape, 0) // PAD + iota(shape, 1) // 128 * PAD == iota(shape, 1) % 128
        lanes = contract(coefs, folds.astype(LOW), 0, 0).astype(LOW)
        total = None
        for group in range(GROUPS):
            part = dot(r.chosen[group, :, 0:TOKENS], lanes[:, group * 128 : (group + 1) * 128])
            total = part if total is None else total + part
        return total.astype(LOW).reshape(DEVICES, PAD, 128)


    def down_part(part):
        at = pl.ds(pl.multiple_of(part * BLOCK, BLOCK), BLOCK)
        r.wide_cls[:, at] = dot(r.active_cls[...], r.wc[:, at])

    every(0, WIDTH // BLOCK, down_part)
    down_pre = r.wide_cls[:, 0:WIDTH] + vector(5)
    normed_two, inverse_two = norm_parts(hidden_cls + down_pre)
    summary = normed_two * vector(6) + vector(7)
    magnitude = jnp.sqrt(jnp.sum(summary * summary, axis=-1, keepdims=True) + EPSILON)
    unit = jnp.where(real_row, summary / magnitude, 0.0)
    r.units[here] = unit.astype(LOW)

    steps_u[0]()
    r.tall[0:PAIR_ROWS, :] = dot(probs_low, r.embedded[...]).astype(LOW)
    r.tall[PAIR_ROWS : PAIR_ROWS + PAD, :] = context_cls
    r.tall[PAIR_ROWS + PAD :, :] = embedded_cls
    pack_one = pack_tall(r.mail_one, PAD, lambda at, both: both)

    def pack_one_step(part):
        pack_one(part)
        pl.when(part == 0)(steps_u[1])
        pl.when(part == 4)(steps_u[2])

    every(0, CHIPS // 2, pack_one_step)
    steps_e[2]()
    r.mail_one[:, 64:80, :] = pack_coefs(probs_low)
    steps_u[3]()

    def post(box, got, index):
        def send(step):
            other, to_core, to_chip = peer(step)
            remote(
                box.at[other], got.at[me], r.one_send.at[index], r.one_recv.at[index], to_core, to_chip
            ).start()

        every(1, DEVICES, send)
        got[me] = box[me]


    def attend_step(unit):
        attend(unit)
        pl.when(unit == 0)(steps_e[3])
        pl.when(unit == 1)(steps_u[4])
        pl.when(unit == 3)(steps_u[5])

    every(0, 6, attend_step)
    post(r.mail_one, r.got_one, 1)
    steps_e[4]()

    units = r.units[...].reshape(SLOT_ROWS, WIDTH)
    weight_row, pair_row, side_row = r.pairs[0:1, :], r.pairs[1:2, :], r.pairs[2:3, :]

    def pair_scores(rows, pair_col, side_col):
        opposite = side_col + side_row == 1.0
        partner = opposite & (pair_col == pair_row)
        raw = SCORE_SCALE * dot_turned(rows, units)
        shifted = jnp.where(partner, raw - SCORE_SCALE * MARGIN_WIDTH, raw)
        return jnp.where(opposite, shifted, MASK_FLOOR), partner

    every_score, every_partner = pair_scores(
        units, r.pairs_col[:, 1:2], r.pairs_col[:, 2:3]
    )
    peak_row = jnp.max(every_score, axis=0, keepdims=True)
    log_row = peak_row + jnp.log(
        jnp.sum(jnp.exp(every_score - peak_row), axis=0, keepdims=True)
    )
    picked_row = jnp.sum(jnp.where(every_partner, every_score, 0.0), axis=0, keepdims=True)
    r.loss[...] = jnp.sum(weight_row * (log_row - picked_row), axis=1, keepdims=True)

    rows_here = pl.ds(pl.multiple_of(me * PAD, 16), PAD)
    own_score, own_partner = pair_scores(
        r.units[here], r.pairs_col[rows_here, 1:2], r.pairs_col[rows_here, 2:3]
    )
    own_partner = own_partner.astype(FULL)
    own_peak = jnp.max(own_score, axis=1, keepdims=True)
    own_exp = jnp.exp(own_score - own_peak)
    own_share = own_exp / jnp.sum(own_exp, axis=1, keepdims=True)
    by_row = (r.pairs_col[rows_here, 0:1] * (own_share - own_partner)).astype(LOW)
    by_column = (weight_row * (jnp.exp(own_score - log_row) - own_partner)).astype(LOW)
    unit_grad = SCORE_SCALE * (dot(by_row, units) + dot(by_column, units))
    along = jnp.sum(unit * unit_grad, axis=-1, keepdims=True)
    summary_grad = (unit_grad - unit * along) / magnitude

    residual_grad, grad_g2, grad_s2 = norm_back_parts(
        summary_grad, normed_two, inverse_two, vector(6)
    )
    down_grad = residual_grad.astype(LOW)
    r.downs[here] = down_grad
    steps_d[0]()
    r.hidden_cls[...] = down_grad

    def up_back(part):
        at = pl.ds(pl.multiple_of(part * BLOCK, BLOCK), BLOCK)
        act_grad = dot_turned(r.hidden_cls[...], r.wc[at, :])
        r.active_cls[:, at] = (act_grad * r.slope_cls[:, at]).astype(LOW)

    every(0, WIDE // BLOCK, up_back)
    steps_d[1]()

    def hidden_back(part):
        at = pl.ds(pl.multiple_of(part * BLOCK, BLOCK), BLOCK)
        r.wide_cls[:, at] = dot_turned(r.active_cls[...], r.wb[at, :])

    every(0, WIDTH // BLOCK, hidden_back)
    hidden_grad = r.wide_cls[:, 0:WIDTH] + residual_grad
    first_grad, grad_g1, grad_s1 = norm_back_parts(
        hidden_grad, r.normed_one[...], inverse_one, vector(3)
    )
    attend_grad = first_grad.astype(LOW)
    context_grad = dot_turned(attend_grad, r.wa[:, 3 * WIDTH : 4 * WIDTH]).astype(LOW)
    attend_here = r.attends.at[here]
    attend_here[:, 0:WIDTH] = attend_grad
    attend_here[:, WIDTH : 2 * WIDTH] = context_grad
    steps_a[0]()
    steps_d[2]()
    context_tall = spread(context_grad)
    probs = r.probs[...]
    prob_grad = dot_turned(context_tall, r.qkv[:, values])
    inner = jnp.sum(probs * prob_grad, axis=1, keepdims=True)
    score_grad = (probs * (prob_grad - inner)).astype(LOW)
    steps_a[1]()
    r.mail_three[...] = pack_coefs(score_grad)
    post(r.mail_three, r.got_three, 3)
    query_grad = (fold(dot(score_grad, r.qkv[:, keys])) * scale).astype(LOW)
    probs_total = jnp.sum(probs_low.astype(FULL), axis=1, keepdims=True)
    grad_bvalue = jnp.sum(probs_total * context_tall.astype(FULL), axis=0, keepdims=True)
    grad_bquery = jnp.sum(query_grad.astype(FULL), axis=0, keepdims=True)
    r.queries[here] = query_grad
    own_sums = jnp.concatenate(
        [jnp.zeros((2 * depth, WIDTH), FULL)]
        + [grad_bquery, grad_bvalue, grad_g1, grad_s1, grad_g2, grad_s2]
        + [jnp.zeros((128 - 2 * depth - 6, WIDTH), FULL)],
        axis=0,
    )
    r.own_sums[...] = jnp.transpose(own_sums)
    steps_q[0]()
    steps_a[2]()
    r.tall[0:PAIR_ROWS, :] = (dot(score_grad, r.embedded[...]) * scale).astype(LOW)

    def with_sums(at, both):
        return both + r.own_sums[pl.ds(pl.multiple_of(at * depth, 16), depth), :]

    every(0, CHIPS // 2, pack_tall(r.mail_two, 0, with_sums))
    steps_q[1]()
    post(r.mail_two, r.got_two, 2)

    def all_rows(buffer, start, width=WIDTH):
        return buffer[:, :, :, :, start : start + width].reshape(SLOT_ROWS, width)

    def from_sent(group):
        lanes = iota((SLOT_ROWS, SLOT_ROWS), 1).astype(FULL)
        return (r.found[group, :, 1:2] == lanes).astype(LOW)

    def widened(coefs, group, start):
        lanes = iota((128, BLOCK), 0) == (iota((128, BLOCK), 1) + start) // HEAD + group * PAD
        return dot(coefs, lanes.astype(LOW))

    half_wide = WIDE // 2

    def slope_tile(part):
        at = pl.ds(pl.multiple_of(core * half_wide + part * BLOCK, BLOCK), BLOCK)
        up_pre = dot(all_rows(r.early, 0), r.wb[:, at]) + r.up_bias[0:1, at]
        _, slope = gelu_parts(up_pre)
        r.slopes[:, pl.ds(pl.multiple_of(part * BLOCK, BLOCK), BLOCK)] = slope.astype(LOW)

    def slot_queries(group):
        sents = from_sent(group)
        for start in range(0, WIDTH, BLOCK):
            rows = dot(sents, all_rows(r.early, WIDTH + start, BLOCK))
            r.slot_query[group, :, start : start + BLOCK] = rows.astype(LOW)

    def activate():
        at = pl.ds(pl.multiple_of(chip // 2 * 2 * deep, 128), 2 * deep)
        up_pre = dot(all_rows(r.early, 0), r.wb[:, at]) + r.up_bias[0:1, at]
        r.active_turned[...] = jnp.transpose(gelu(up_pre)).astype(LOW)
        r.hidden_turned[...] = jnp.transpose(all_rows(r.early, 0))

    steps_e[5]()

    def open_step(tile):
        open_tile(tile)
        pl.when(tile == 0)(steps_d[3])
        pl.when(tile == 2)(steps_a[3])

    def feed_step(part):
        feed_up(part)
        for index, step in enumerate([steps_q[2], steps_d[4], steps_a[4], steps_q[3], steps_d[5]]):
            pl.when(part == index)(step)
        pl.when(part == 6)(steps_a[5])
        pl.when(part == 7)(steps_q[4])

    every(0, TOKENS // BLOCK, open_step)
    every(0, WIDE // BLOCK, feed_step)
    every(0, WIDTH // BLOCK, feed_rest)
    every(0, WIDTH // BLOCK, feed_down)
    every(0, TOKENS // BLOCK, close_tile)
    every(0, GROUPS, slot_queries)
    every(0, 6, slope_tile)
    activate()

    all_but_one(r.got_one, 1).wait_recv()
    def slot_values(group):
        sents = from_sent(group)
        got_probs = r.got_one[:, 64:80, :].reshape(SLOT_ROWS, 128)
        for start in range(0, WIDTH, BLOCK):
            rows = dot(sents, all_rows(r.attends, WIDTH + start, BLOCK))
            rows = widened(got_probs, group, start) * rows
            r.replies[group, :, start : start + BLOCK] = rows.astype(LOW)

    every(0, GROUPS, slot_values)

    def head_products(got, first_row, right, start, target):
        def one_head(head):
            lane = core * (WIDTH // 2) + lax.div(head, 2) * 128
            pair_rows = right[:, :, :, :, pl.ds(pl.multiple_of(start + lane, 128), 128)]
            row = pl.ds(pl.multiple_of(first_row + lax.rem(head, 3) * PAD, 16), PAD)
            block_rows = got[:, row, :].reshape(SLOT_ROWS, 128)
            r.product[...] = contract(block_rows, pair_rows.reshape(SLOT_ROWS, 128), 0, 0)
            part = r.product[pl.ds(pl.multiple_of(lax.div(head, 3) * depth, 16), depth), :]
            at = pl.ds(pl.multiple_of(lane, 128), 128)
            own_lanes = lax.div(iota((depth, 128), 1), HEAD) == lax.rem(head, 2)
            target[:, at] = jnp.where(own_lanes, part, target[:, at])

        every(0, HEADS // 2, one_head)

    def half_of(ref, at_core):
        half = ref.shape[1] // 2
        return ref.at[:, pl.ds(pl.multiple_of(at_core * half, 128), half)]

    def half_copy(index, ref, at_core):
        part = half_of(ref, at_core)
        return remote(part, part, r.half_send.at[index], r.half_recv.at[index], 1 - core, chip)

    own_half = pl.ds(pl.multiple_of(core * (WIDTH // 2), 128), WIDTH // 2)
    r.g_wv[:, own_half] = jnp.zeros((depth, WIDTH // 2), FULL)
    r.g_wk[:, own_half] = jnp.zeros((depth, WIDTH // 2), FULL)
    head_products(r.got_one, PAD, r.attends, WIDTH, r.g_wv)
    half_copy(0, r.g_wv, core).start()

    downs = r.downs[...].reshape(SLOT_ROWS, WIDTH)
    attends = all_rows(r.attends, 0)

    def up_tile(part):
        at = pl.ds(pl.multiple_of(core * half_wide + part * BLOCK, BLOCK), BLOCK)
        slope = r.slopes[:, pl.ds(pl.multiple_of(part * BLOCK, BLOCK), BLOCK)].astype(FULL)
        up_all = (dot_turned(r.downs[...].reshape(SLOT_ROWS, WIDTH), r.wc[at, :]) * slope)
        up_all = up_all.astype(LOW)
        r.g_wup[0:depth, at] = dot(r.hidden_turned[mine, :], up_all)
        total = jnp.sum(up_all.astype(FULL), axis=0, keepdims=True)
        r.g_wup[depth : depth + 8, at] = jnp.broadcast_to(total, (8, BLOCK))

    every(0, half_wide // BLOCK, up_tile)
    half_copy(1, r.g_wup, core).start()
    r.g_wdown[...] = dot(r.active_turned[pl.ds(pl.multiple_of(chip % 2 * deep, 16), deep), :], downs)
    r.left_turned[...] = jnp.transpose(r.got_one[:, 0:PAD, :].reshape(SLOT_ROWS, 128))
    r.g_wo[...] = dot(r.left_turned[0:depth, :], attends)
    own_lanes = (iota((WIDTH, 128), 0) == chip * depth + iota((WIDTH, 128), 1)).astype(LOW)

    def own_part(rows, select):
        total = None
        for _ in range(3):
            part = rows.astype(LOW)
            rows = rows - part.astype(FULL)
            picked = dot(part, select)
            total = picked if total is None else total + picked
        return total

    for quarter in range(4):
        rows_of(quarter).wait_send()
    all_but_one(r.got_three, 3).wait_recv()

    def slot_grads(group):
        got_scores = r.got_three[...].reshape(SLOT_ROWS, 128)
        for start in range(0, WIDTH, BLOCK):
            lanes = slice(start, start + BLOCK)
            rows = r.slot_query[group, :, lanes].astype(FULL)
            rows = widened(got_scores, group, start) * rows * scale
            r.slot_query[group, :, lanes] = rows.astype(LOW)
        for start in range(0, WIDTH, BLOCK):
            row_grad = dot_turned(r.slot_query[group], r.wa[start : start + BLOCK, keys])
            row_grad = row_grad + dot_turned(r.replies[group], r.wa[start : start + BLOCK, values])
            r.rows[group, :, start : start + BLOCK] = row_grad.astype(LOW)

    every(0, GROUPS, slot_grads)
    steps_q[5]()
    query_grads = all_rows(r.queries, 0)
    extra = dot_turned(query_grads, r.wa[:, 0:WIDTH]) + attends.astype(FULL)
    r.extra[...] = extra.astype(LOW)
    r.g_wq[...] = dot(r.left_turned[depth : 2 * depth, :], query_grads)

    half_rows = VOCAB_ROWS // 2

    def table_copy(tile):
        at = pl.ds(pl.multiple_of(tile * half_rows, BLOCK), half_rows)
        return pltpu.make_async_copy(
            r.table_full.at[at], r.table_grad.at[at], r.table_sem.at[tile]
        )

    def table_tile(tile):
        at = pl.ds(pl.multiple_of(tile * half_rows, BLOCK), half_rows)
        for start in range(0, WIDTH, BLOCK):
            lanes = slice(start, start + BLOCK)
            slot_rows = r.rows[:, :, lanes].reshape(GROUPS * SLOT_ROWS, BLOCK)
            r.table_full[at, lanes] = dot(r.by_row[at, 0 : GROUPS * SLOT_ROWS], slot_rows) + dot(
                r.by_row[at, GROUPS * SLOT_ROWS :], r.extra[:, lanes]
            )
        table_copy(tile).start()

    every(0, 2, table_tile)
    all_but_one(r.got_two, 2).wait_recv()
    head_products(r.got_two, 0, r.early, WIDTH, r.g_wk)
    half_copy(2, r.g_wk, core).start()

    down_total = jnp.sum(downs.astype(FULL), axis=0, keepdims=True)
    attend_total = jnp.sum(attends.astype(FULL), axis=0, keepdims=True)
    sums = jnp.sum(r.got_two[...].astype(FULL), axis=0)
    sums = jnp.concatenate([sums, jnp.zeros((128 - 48, 128), FULL)], axis=0)
    stacked = jnp.concatenate([attend_total, down_total, jnp.zeros((6, WIDTH), FULL)], axis=0)
    r.g_small[8:16, 0:128] = own_part(stacked, own_lanes)
    r.g_small[0:8, 0:128] = jnp.transpose(sums)[2 * depth : 2 * depth + 8, :]
    r.g_small[0:16, 128:BLOCK] = jnp.zeros((PAD, BLOCK - 128), FULL)
    half_copy(1, r.g_wup, 1 - core).wait_recv()
    up_lanes = (iota((WIDE, BLOCK), 0) == chip * deep + iota((WIDE, BLOCK), 1)).astype(LOW)
    r.g_small[16:24, :] = own_part(r.g_wup[depth : depth + 8, :], up_lanes)

    half_copy(0, r.g_wv, 1 - core).wait_recv()
    half_copy(2, r.g_wk, 1 - core).wait_recv()
    for index, ref in enumerate([r.g_wv, r.g_wup, r.g_wk]):
        half_copy(index, ref, core).wait_send()

    for index, ref in enumerate([r.every_ids, r.got_one, r.got_two, r.got_three]):
        all_but_one(ref, index).wait_send()
    all_smalls().wait_send()
    for end in [drain_a, drain_b, drain_c, drain_u, drain_e, drain_d, drain_a2, drain_q]:
        end()
    every(0, TOKENS // BLOCK, lambda tile: layer_copy(tile).wait())
    every(0, 2, lambda tile: table_copy(tile).wait())


def layer(inputs):
    dma = pltpu.SemaphoreType.DMA
    vmem = pl.BlockSpec(memory_space=pltpu.VMEM)
    anywhere = pl.BlockSpec(memory_space=pl.ANY)
    depth, deep = WIDTH // CHIPS, WIDE // CHIPS

    def gathered(width):
        return pltpu.VMEM((CORES, PLANES, LINES, PAD, width), LOW)

    outputs = dict(
        layer_out=((TOKENS, WIDTH), LOW),
        table_grad=((VOCAB_ROWS, WIDTH), FULL),
        g_wq=((depth, WIDTH), FULL),
        g_wk=((depth, WIDTH), FULL),
        g_wv=((depth, WIDTH), FULL),
        g_wo=((depth, WIDTH), FULL),
        g_wup=((depth + 8, WIDE), FULL),
        g_wdown=((deep, WIDTH), FULL),
        g_small=((24, BLOCK), FULL),
        loss=((1, 1), FULL),
    )
    scratch = dict(
        ids=pltpu.VMEM((8, 128), jnp.int32),
        every_ids=pltpu.VMEM((DEVICES, 8, 128), jnp.int32),
        rank=pltpu.VMEM((DEVICES, TOKENS), FULL),
        code=pltpu.VMEM((DEVICES, TOKENS), FULL),
        found=pltpu.VMEM((GROUPS + 1, SLOT_ROWS, 2), FULL),
        block_bias=pltpu.VMEM((2 * BLOCK, BLOCK // 2), FULL),
        valid_bias=pltpu.VMEM((8, TOKENS), FULL),
        slot_col=pltpu.VMEM((TOKENS, 1), FULL),
        slot_line=pltpu.VMEM((8, TOKENS), FULL),
        valid_col=pltpu.VMEM((TOKENS, 1), FULL),
        valid_line=pltpu.VMEM((8, TOKENS), FULL),
        pairs=pltpu.VMEM((8, SLOT_ROWS), FULL),
        pairs_col=pltpu.VMEM((SLOT_ROWS, 128), FULL),
        vectors=pltpu.VMEM((PAD, WIDTH), FULL),
        up_bias=pltpu.VMEM((8, WIDE), FULL),
        qkv_bias=pltpu.VMEM((8, 3 * WIDTH), FULL),
        smalls=pltpu.VMEM((PAD, CHIPS * 128), LOW),
        wa=pltpu.VMEM((WIDTH, 4 * WIDTH), LOW),
        wb=pltpu.VMEM((WIDTH, WIDE), LOW),
        wc=pltpu.VMEM((WIDE, WIDTH), LOW),
        chosen=pltpu.VMEM((GROUPS, SLOT_ROWS, VOCAB_ROWS), LOW),
        by_row=pltpu.VMEM((VOCAB_ROWS, (GROUPS + 1) * SLOT_ROWS), LOW),
        rows=pltpu.VMEM((GROUPS, SLOT_ROWS, WIDTH), LOW),
        replies=pltpu.VMEM((GROUPS, SLOT_ROWS, WIDTH), LOW),
        slot_query=pltpu.VMEM((GROUPS, SLOT_ROWS, WIDTH), LOW),
        extra=pltpu.VMEM((SLOT_ROWS, WIDTH), LOW),
        hidden_cls=pltpu.VMEM((PAD, WIDTH), LOW),
        active_cls=pltpu.VMEM((PAD, WIDE), LOW),
        slope_cls=pltpu.VMEM((PAD, WIDE), FULL),
        wide_cls=pltpu.VMEM((PAD, WIDTH), FULL),
        tall=pltpu.VMEM((PAIR_ROWS + 2 * PAD, WIDTH), LOW),
        own_sums=pltpu.VMEM((WIDTH, 128), FULL),
        product=pltpu.VMEM((128, 128), FULL),
        embedded=pltpu.VMEM((TOKENS, WIDTH), LOW),
        qkv=pltpu.VMEM((TOKENS, 3 * WIDTH), LOW),
        context=pltpu.VMEM((TOKENS, WIDTH), LOW),
        table_full=pltpu.VMEM((VOCAB_ROWS, WIDTH), FULL),
        probs=pltpu.VMEM((PAIR_ROWS, TOKENS), FULL),
        normed_one=pltpu.VMEM((PAD, WIDTH), FULL),
        units=gathered(WIDTH),
        early=gathered(2 * WIDTH),
        downs=gathered(WIDTH),
        attends=gathered(2 * WIDTH),
        queries=gathered(WIDTH),
        slopes=pltpu.VMEM((SLOT_ROWS, WIDE // 2), LOW),
        hidden_turned=pltpu.VMEM((WIDTH, SLOT_ROWS), LOW),
        active_turned=pltpu.VMEM((2 * deep, SLOT_ROWS), LOW),
        left_turned=pltpu.VMEM((128, SLOT_ROWS), LOW),
        mail_one=pltpu.VMEM((DEVICES, 80, 128), LOW),
        got_one=pltpu.VMEM((DEVICES, 80, 128), LOW),
        mail_two=pltpu.VMEM((DEVICES, 48, 128), LOW),
        got_two=pltpu.VMEM((DEVICES, 48, 128), LOW),
        mail_three=pltpu.VMEM((DEVICES, PAD, 128), LOW),
        got_three=pltpu.VMEM((DEVICES, PAD, 128), LOW),
        rows_send=dma((4,)),
        rows_recv=dma((4,)),
        one_send=dma((4,)),
        one_recv=dma((4,)),
        small_send=dma((1,)),
        small_recv=dma((1,)),
        weight_send=dma((3, 14)),
        weight_recv=dma((3, 14)),
        gather_send=dma((5, 13)),
        gather_recv=dma((5, 13)),
        half_send=dma((3,)),
        half_recv=dma((3,)),
        out_sem=dma((TOKENS // BLOCK,)),
        table_sem=dma((2,)),
    )
    names = INPUTS + OUTPUTS + list(scratch)
    return pl.pallas_call(
        partial(layer_kernel, names),
        out_shape=tuple(jax.ShapeDtypeStruct(*outputs[name]) for name in OUTPUTS),
        in_specs=[vmem] * len(INPUTS),
        out_specs=(anywhere, anywhere) + (vmem,) * (len(OUTPUTS) - 2),
        scratch_shapes=list(scratch.values()),
        compiler_params=pltpu.CompilerParams(
            collective_id=0, has_side_effects=True, vmem_limit_bytes=VMEM_LIMIT
        ),
        name="layer",
    )(*inputs)


def finish_kernel(count, *refs):
    large, (small, loss), outs = refs[:count], refs[count : count + 2], refs[count + 2 : -1]
    sems = refs[-1]
    copies = []
    for index, (source, target) in enumerate(zip(large, outs)):
        part = source if source.shape == target.shape else source.at[: target.shape[0]]
        copies.append(pltpu.make_async_copy(part, target, sems.at[index]))
        copies[-1].start()
    for row, target in zip([0, 1, 8, 2, 3, 16, 9, 4, 5], outs[count : count + 9]):
        size = target.shape[0]
        target[...] = small[row : row + 1, 0:size].reshape(size)
    outs[-1][...] = loss[...].reshape(1)
    for one in copies:
        one.wait()


def finish(results):
    vmem = pl.BlockSpec(memory_space=pltpu.VMEM)
    anywhere = pl.BlockSpec(memory_space=pl.ANY)
    depth, deep = WIDTH // CHIPS, WIDE // CHIPS
    count = len(results) - 2
    shapes = [(one.shape, one.dtype) for one in results[:count]]
    shapes[6] = ((depth, WIDE), FULL)
    shapes += [((depth,), FULL)] * 5 + [((deep,), FULL)] + [((depth,), FULL)] * 3
    shapes.append(((1,), FULL))
    return pl.pallas_call(
        partial(finish_kernel, count),
        out_shape=tuple(jax.ShapeDtypeStruct(*one) for one in shapes),
        in_specs=[vmem] * (count + 2),
        out_specs=(anywhere,) * count + (vmem,) * 10,
        scratch_shapes=[pltpu.SemaphoreType.DMA((count,))],
        name="finish",
    )(*results)


def block_body(
    table,
    token_ids,
    sent_lengths,
    pair_slot,
    pair_lang,
    *parameters,
):
    results = finish(layer((table, token_ids, sent_lengths, pair_slot, pair_lang) + parameters))
    layer_out, table_grad, g_wq, g_wk, g_wv, g_wo, g_wup, g_wdown = results[:8]
    g_bq, g_bv, g_bo, g_g1, g_s1, g_bup, g_bdown, g_g2, g_s2, loss = results[8:]
    return (
        layer_out.reshape(token_ids.shape + (WIDTH,)),
        loss.reshape(()),
        table_grad,
        g_wq,
        g_bq,
        g_wk,
        g_wv,
        g_bv,
        g_wo,
        g_bo,
        g_g1,
        g_s1,
        g_wup,
        g_bup,
        g_wdown,
        g_bdown,
        g_g2,
        g_s2,
    )


def solution(mesh):
    in_specs = (
        P(("dp", "fsdp"), None),
        P(("dp", "fsdp"), None),
        P(("dp", "fsdp")),
        P(),
        P(),
        P("fsdp", None),
        P("fsdp"),
        P("fsdp", None),
        P("fsdp", None),
        P("fsdp"),
        P("fsdp", None),
        P("fsdp"),
        P("fsdp"),
        P("fsdp"),
        P("fsdp", None),
        P("fsdp"),
        P("fsdp", None),
        P("fsdp"),
        P("fsdp"),
        P("fsdp"),
    )
    out_specs = (
        P(("dp", "fsdp"), None, None),
        P(),
        P(("dp", "fsdp"), None),
        P("fsdp", None),
        P("fsdp"),
        P("fsdp", None),
        P("fsdp", None),
        P("fsdp"),
        P("fsdp", None),
        P("fsdp"),
        P("fsdp"),
        P("fsdp"),
        P("fsdp", None),
        P("fsdp"),
        P("fsdp", None),
        P("fsdp"),
        P("fsdp"),
        P("fsdp"),
    )
    sizes = dict(mesh.shape)
    body = general_body
    if sizes["dp"] == CORES and sizes["fsdp"] == CHIPS:
        body = block_body
    return jax.shard_map(body, mesh=mesh, in_specs=in_specs, out_specs=out_specs, check_vma=False)
```

```python
from functools import partial
from types import SimpleNamespace

import jax
import jax.numpy as jnp
from jax import lax
from jax.experimental import pallas as pl
from jax.experimental.pallas import tpu as pltpu
from jax.sharding import PartitionSpec as P

HEADS = 12
HEAD = 64
LANGS = 109


EPSILON = 1e-06
SCORE_SCALE = 50.0
MARGIN_WIDTH = 0.3
MASK_FLOOR = -1000000000.0


def contract(left_side, right_side, left_dim, right_dim):
    return lax.dot_general(
        left_side,
        right_side,
        (((left_dim,), (right_dim,)), ((), ())),
        preferred_element_type=jnp.float32,
    )


def norm_rows(inputs, ln_gain, ln_shift):
    row_mean = jnp.mean(inputs, axis=-1, keepdims=True)
    centered = inputs - row_mean
    variance = jnp.mean(centered * centered, axis=-1, keepdims=True)
    inverse = lax.rsqrt(variance + EPSILON)
    normed = centered * inverse
    return (normed * ln_gain + ln_shift, normed, inverse)


def norm_back(grad_output, normed, inverse, ln_gain):
    grad_normed = grad_output * ln_gain
    first_term = jnp.mean(grad_normed, axis=-1, keepdims=True)
    second_term = jnp.mean(grad_normed * normed, axis=-1, keepdims=True)
    grad_input = inverse * (grad_normed - first_term - normed * second_term)
    return (grad_input, jnp.sum(grad_output * normed, axis=0), jnp.sum(grad_output, axis=0))


def general_body(
    table,
    token_ids,
    sent_lengths,
    pair_slot,
    pair_lang,
    w_query,
    b_query,
    w_key,
    w_value,
    b_value,
    w_out,
    b_out,
    ln1_gain,
    ln1_bias,
    w_up,
    b_up,
    w_down,
    b_down,
    ln2_gain,
    ln2_bias,
):
    sentences, length = token_ids.shape
    tokens = sentences * length
    vocab_rows, model_width = table.shape
    owners = lax.axis_size(("dp", "fsdp"))
    dp_count = lax.axis_size("dp")
    fsdp_count = lax.axis_size("fsdp")
    capacity = max(2, 2 * tokens // owners)
    device = lax.axis_index(("dp", "fsdp"))
    score_factor = HEAD ** (-0.5)
    flat_ids = token_ids.reshape(tokens)
    owner_of = flat_ids // vocab_rows
    member = (owner_of[:, None] == jnp.arange(owners, dtype=jnp.int32)[None, :]).astype(jnp.int32)
    owner_rank = jnp.sum(jnp.cumsum(member, axis=0) * member, axis=1) - 1
    slot_of = owner_of * capacity + owner_rank
    requests = jnp.full((owners * capacity,), -1, jnp.int32).at[slot_of].set(flat_ids)
    received = lax.all_to_all(
        lax.all_to_all(
            requests.reshape(dp_count, fsdp_count, capacity),
            "dp",
            split_axis=0,
            concat_axis=0,
            tiled=True,
        ),
        "fsdp",
        split_axis=1,
        concat_axis=1,
        tiled=True,
    )
    present = received >= 0
    local_rows = jnp.where(present, received - device * vocab_rows, 0)
    found_rows = jnp.where(present[..., None], table[local_rows], jnp.zeros((), table.dtype))
    replies = lax.all_to_all(
        lax.all_to_all(found_rows, "dp", split_axis=0, concat_axis=0, tiled=True),
        "fsdp",
        split_axis=1,
        concat_axis=1,
        tiled=True,
    )
    embedded = replies.reshape(owners * capacity, model_width)[slot_of]
    gathered = (
        lax.all_gather(w_query, "fsdp", axis=0, tiled=True),
        lax.all_gather(b_query, "fsdp", axis=0, tiled=True),
        lax.all_gather(w_key, "fsdp", axis=0, tiled=True),
        lax.all_gather(w_value, "fsdp", axis=0, tiled=True),
        lax.all_gather(b_value, "fsdp", axis=0, tiled=True),
        lax.all_gather(w_out, "fsdp", axis=0, tiled=True),
        lax.all_gather(b_out, "fsdp", axis=0, tiled=True),
        lax.all_gather(ln1_gain, "fsdp", axis=0, tiled=True),
        lax.all_gather(ln1_bias, "fsdp", axis=0, tiled=True),
        lax.all_gather(w_up, "fsdp", axis=0, tiled=True),
        lax.all_gather(b_up, "fsdp", axis=0, tiled=True),
        lax.all_gather(w_down, "fsdp", axis=0, tiled=True),
        lax.all_gather(b_down, "fsdp", axis=0, tiled=True),
        lax.all_gather(ln2_gain, "fsdp", axis=0, tiled=True),
        lax.all_gather(ln2_bias, "fsdp", axis=0, tiled=True),
    )
    (
        full_wq,
        full_bq,
        full_wk,
        full_wv,
        full_bv,
        full_wo,
        full_bo,
        full_g1,
        full_s1,
        full_wup,
        full_bup,
        full_wdown,
        full_bdown,
        full_g2,
        full_s2,
    ) = gathered
    valid_mask = jnp.arange(length, dtype=jnp.int32)[None, :] < sent_lengths[:, None]
    head_shape = (sentences, length, HEADS, HEAD)
    queries = (jnp.dot(embedded, full_wq, preferred_element_type=jnp.float32) + full_bq).astype(
        jnp.bfloat16
    )
    key_heads = (
        jnp.dot(embedded, full_wk, preferred_element_type=jnp.float32)
        .astype(jnp.bfloat16)
        .reshape(head_shape)
    )
    value_heads = (
        (jnp.dot(embedded, full_wv, preferred_element_type=jnp.float32) + full_bv)
        .astype(jnp.bfloat16)
        .reshape(head_shape)
    )
    query_heads = queries.reshape(head_shape)
    scores = (
        jnp.einsum("bqhd,bkhd->bhqk", query_heads, key_heads, preferred_element_type=jnp.float32)
        * score_factor
    )
    scores = jnp.where(valid_mask[:, None, None, :], scores, MASK_FLOOR)
    row_peak = jnp.max(scores, axis=-1, keepdims=True)
    shifted = jnp.exp(scores - row_peak)
    totals = jnp.sum(shifted, axis=-1, keepdims=True)
    attn_probs = (shifted / totals).astype(jnp.bfloat16)
    context = jnp.einsum(
        "bhqk,bkhd->bqhd", attn_probs, value_heads, preferred_element_type=jnp.float32
    )
    context = context.reshape(tokens, model_width).astype(jnp.bfloat16)
    attended = jnp.dot(context, full_wo, preferred_element_type=jnp.float32) + full_bo
    hidden, normed_one, inverse_one = norm_rows(
        embedded.astype(jnp.float32) + attended, full_g1, full_s1
    )
    hidden_low = hidden.astype(jnp.bfloat16)
    up_pre = jnp.dot(hidden_low, full_wup, preferred_element_type=jnp.float32) + full_bup
    activated = jax.nn.gelu(up_pre, approximate=False).astype(jnp.bfloat16)
    down_pre = jnp.dot(activated, full_wdown, preferred_element_type=jnp.float32) + full_bdown
    normed_out, normed_two, inverse_two = norm_rows(hidden + down_pre, full_g2, full_s2)
    layer_out = jnp.where(valid_mask.reshape(tokens)[:, None], normed_out, 0.0).astype(jnp.bfloat16)
    layer_out = layer_out.reshape(sentences, length, model_width)

    def first_rows(matrix):
        return matrix.reshape(sentences, length, matrix.shape[-1])[:, 0]

    summary = first_rows(normed_out)
    magnitude = jnp.sqrt(jnp.sum(summary * summary, axis=-1, keepdims=True) + EPSILON)
    unit_vector = summary / magnitude
    unit_low = unit_vector.astype(jnp.bfloat16)
    every_unit = lax.all_gather(unit_low, ("dp", "fsdp"), axis=0, tiled=True)
    every_side = pair_slot % 2
    every_pair = pair_slot // 2
    my_slots = lax.dynamic_slice_in_dim(pair_slot, device * sentences, sentences)
    my_side = my_slots % 2
    my_pair = my_slots // 2
    lang_onehot = (pair_lang[:, None] == jnp.arange(LANGS, dtype=jnp.int32)[None, :]).astype(
        jnp.float32
    )
    per_lang = jnp.sum(lang_onehot, axis=0)
    per_pair = 1.0 / (2.0 * LANGS * jnp.sum(lang_onehot * per_lang[None, :], axis=1))
    my_weight = jnp.take(per_pair, my_pair)
    opposite = my_side[:, None] != every_side[None, :]
    partner = opposite & (my_pair[:, None] == every_pair[None, :])
    raw_scores = SCORE_SCALE * contract(unit_low, every_unit, 1, 1)
    pair_scores = jnp.where(partner, raw_scores - SCORE_SCALE * MARGIN_WIDTH, raw_scores)
    pair_scores = jnp.where(opposite, pair_scores, MASK_FLOOR)
    pair_peak = jnp.max(pair_scores, axis=1, keepdims=True)
    pair_exp = jnp.exp(pair_scores - pair_peak)
    pair_total = jnp.sum(pair_exp, axis=1, keepdims=True)
    log_total = pair_peak[:, 0] + jnp.log(pair_total[:, 0])
    picked = jnp.sum(jnp.where(partner, pair_scores, 0.0), axis=1)
    loss_value = lax.psum(jnp.sum(my_weight * (log_total - picked)), ("dp", "fsdp"))
    coefficients = (
        my_weight[:, None] * (pair_exp / pair_total - partner.astype(jnp.float32))
    ).astype(jnp.bfloat16)
    unit_grad = SCORE_SCALE * contract(coefficients, every_unit, 1, 0)
    column_terms = SCORE_SCALE * contract(coefficients, unit_low, 0, 0)
    unit_grad = unit_grad + lax.psum_scatter(
        column_terms, ("dp", "fsdp"), scatter_dimension=0, tiled=True
    )
    along = jnp.sum(unit_vector * unit_grad, axis=-1, keepdims=True)
    summary_grad = (unit_grad - unit_vector * along) / magnitude
    again_weights = (
        lax.all_gather(w_query, "fsdp", axis=0, tiled=True),
        lax.all_gather(w_key, "fsdp", axis=0, tiled=True),
        lax.all_gather(w_value, "fsdp", axis=0, tiled=True),
        lax.all_gather(w_out, "fsdp", axis=0, tiled=True),
        lax.all_gather(ln1_gain, "fsdp", axis=0, tiled=True),
        lax.all_gather(w_up, "fsdp", axis=0, tiled=True),
        lax.all_gather(w_down, "fsdp", axis=0, tiled=True),
        lax.all_gather(ln2_gain, "fsdp", axis=0, tiled=True),
    )
    again_wq, again_wk, again_wv, again_wo, again_g1, again_wup, again_wdown, again_g2 = (
        again_weights
    )
    residual_grad, grad_g2, grad_s2 = norm_back(
        summary_grad, first_rows(normed_two), first_rows(inverse_two), again_g2
    )
    down_grad = residual_grad.astype(jnp.bfloat16)
    activated_cls = first_rows(activated)
    act_grad = contract(down_grad, again_wdown, 1, 1)
    gelu_value, gelu_pull = jax.vjp(partial(jax.nn.gelu, approximate=False), first_rows(up_pre))
    up_grad = gelu_pull(act_grad)[0].astype(jnp.bfloat16)
    hidden_cls = first_rows(hidden_low)
    hidden_grad = contract(up_grad, again_wup, 1, 1) + residual_grad
    first_grad, grad_g1, grad_s1 = norm_back(
        hidden_grad, first_rows(normed_one), first_rows(inverse_one), again_g1
    )
    attend_grad = first_grad.astype(jnp.bfloat16)
    context_cls = first_rows(context)
    context_grad = (
        contract(attend_grad, again_wo, 1, 1).astype(jnp.bfloat16).reshape(sentences, HEADS, HEAD)
    )
    query_cls = query_heads[:, 0]
    cls_scores = (
        jnp.einsum("bhd,bkhd->bhk", query_cls, key_heads, preferred_element_type=jnp.float32)
        * score_factor
    )
    cls_scores = jnp.where(valid_mask[:, None, :], cls_scores, MASK_FLOOR)
    cls_probs = jnp.exp(cls_scores - row_peak[:, :, 0]) / totals[:, :, 0]
    prob_grad = jnp.einsum(
        "bhd,bkhd->bhk", context_grad, value_heads, preferred_element_type=jnp.float32
    )
    score_grad = (
        cls_probs * (prob_grad - jnp.sum(cls_probs * prob_grad, axis=-1, keepdims=True))
    ).astype(jnp.bfloat16)
    query_grad = (
        (
            jnp.einsum("bhk,bkhd->bhd", score_grad, key_heads, preferred_element_type=jnp.float32)
            * score_factor
        )
        .astype(jnp.bfloat16)
        .reshape(sentences, model_width)
    )
    key_grad = (
        (
            jnp.einsum("bhk,bhd->bkhd", score_grad, query_cls, preferred_element_type=jnp.float32)
            * score_factor
        )
        .astype(jnp.bfloat16)
        .reshape(tokens, model_width)
    )
    value_grad = (
        jnp.einsum(
            "bhk,bhd->bkhd",
            cls_probs.astype(jnp.bfloat16),
            context_grad,
            preferred_element_type=jnp.float32,
        )
        .astype(jnp.bfloat16)
        .reshape(tokens, model_width)
    )
    embedded_cls = first_rows(embedded)
    grad_wkey = contract(embedded, key_grad, 0, 0)
    grad_wvalue = contract(embedded, value_grad, 0, 0)
    grad_bvalue = jnp.sum(value_grad, axis=0, dtype=jnp.float32)
    row_grads = contract(key_grad, again_wk, 1, 1) + contract(value_grad, again_wv, 1, 1)
    summary_extra = contract(query_grad, again_wq, 1, 1) + first_grad
    row_grads = (
        row_grads.reshape(sentences, length, model_width)
        .at[:, 0]
        .add(summary_extra)
        .reshape(tokens, model_width)
    )
    outgoing = jnp.zeros((owners * capacity, model_width), jnp.float32).at[slot_of].set(row_grads)
    incoming = lax.all_to_all(
        lax.all_to_all(
            outgoing.reshape(dp_count, fsdp_count, capacity, model_width).astype(jnp.bfloat16),
            "dp",
            split_axis=0,
            concat_axis=0,
            tiled=True,
        ),
        "fsdp",
        split_axis=1,
        concat_axis=1,
        tiled=True,
    ).astype(jnp.float32)
    incoming = jnp.where(
        present.reshape(owners * capacity)[:, None],
        incoming.reshape(owners * capacity, model_width),
        0.0,
    )
    table_grad = (
        jnp.zeros((vocab_rows, model_width), jnp.float32)
        .at[local_rows.reshape(owners * capacity)]
        .add(incoming)
    )
    grad_wquery = contract(embedded_cls, query_grad, 0, 0)
    grad_bquery = jnp.sum(query_grad, axis=0, dtype=jnp.float32)
    grad_wout = contract(context_cls, attend_grad, 0, 0)
    grad_bout = jnp.sum(attend_grad, axis=0, dtype=jnp.float32)
    grad_wup = contract(hidden_cls, up_grad, 0, 0)
    grad_bup = jnp.sum(up_grad, axis=0, dtype=jnp.float32)
    grad_wdown = contract(activated_cls, down_grad, 0, 0)
    grad_bdown = jnp.sum(down_grad, axis=0, dtype=jnp.float32)
    owned_grads = (
        lax.psum_scatter(
            grad_wquery.astype(jnp.bfloat16), "fsdp", scatter_dimension=0, tiled=True
        ).astype(jnp.float32),
        lax.psum_scatter(
            grad_bquery.astype(jnp.bfloat16), "fsdp", scatter_dimension=0, tiled=True
        ).astype(jnp.float32),
        lax.psum_scatter(
            grad_wkey.astype(jnp.bfloat16), "fsdp", scatter_dimension=0, tiled=True
        ).astype(jnp.float32),
        lax.psum_scatter(
            grad_wvalue.astype(jnp.bfloat16), "fsdp", scatter_dimension=0, tiled=True
        ).astype(jnp.float32),
        lax.psum_scatter(
            grad_bvalue.astype(jnp.bfloat16), "fsdp", scatter_dimension=0, tiled=True
        ).astype(jnp.float32),
        lax.psum_scatter(
            grad_wout.astype(jnp.bfloat16), "fsdp", scatter_dimension=0, tiled=True
        ).astype(jnp.float32),
        lax.psum_scatter(
            grad_bout.astype(jnp.bfloat16), "fsdp", scatter_dimension=0, tiled=True
        ).astype(jnp.float32),
        lax.psum_scatter(
            grad_g1.astype(jnp.bfloat16), "fsdp", scatter_dimension=0, tiled=True
        ).astype(jnp.float32),
        lax.psum_scatter(
            grad_s1.astype(jnp.bfloat16), "fsdp", scatter_dimension=0, tiled=True
        ).astype(jnp.float32),
        lax.psum_scatter(
            grad_wup.astype(jnp.bfloat16), "fsdp", scatter_dimension=0, tiled=True
        ).astype(jnp.float32),
        lax.psum_scatter(
            grad_bup.astype(jnp.bfloat16), "fsdp", scatter_dimension=0, tiled=True
        ).astype(jnp.float32),
        lax.psum_scatter(
            grad_wdown.astype(jnp.bfloat16), "fsdp", scatter_dimension=0, tiled=True
        ).astype(jnp.float32),
        lax.psum_scatter(
            grad_bdown.astype(jnp.bfloat16), "fsdp", scatter_dimension=0, tiled=True
        ).astype(jnp.float32),
        lax.psum_scatter(
            grad_g2.astype(jnp.bfloat16), "fsdp", scatter_dimension=0, tiled=True
        ).astype(jnp.float32),
        lax.psum_scatter(
            grad_s2.astype(jnp.bfloat16), "fsdp", scatter_dimension=0, tiled=True
        ).astype(jnp.float32),
    )
    summed = (
        lax.psum(owned_grads[0].astype(jnp.bfloat16), "dp").astype(jnp.float32),
        lax.psum(owned_grads[1].astype(jnp.bfloat16), "dp").astype(jnp.float32),
        lax.psum(owned_grads[2].astype(jnp.bfloat16), "dp").astype(jnp.float32),
        lax.psum(owned_grads[3].astype(jnp.bfloat16), "dp").astype(jnp.float32),
        lax.psum(owned_grads[4].astype(jnp.bfloat16), "dp").astype(jnp.float32),
        lax.psum(owned_grads[5].astype(jnp.bfloat16), "dp").astype(jnp.float32),
        lax.psum(owned_grads[6].astype(jnp.bfloat16), "dp").astype(jnp.float32),
        lax.psum(owned_grads[7].astype(jnp.bfloat16), "dp").astype(jnp.float32),
        lax.psum(owned_grads[8].astype(jnp.bfloat16), "dp").astype(jnp.float32),
        lax.psum(owned_grads[9].astype(jnp.bfloat16), "dp").astype(jnp.float32),
        lax.psum(owned_grads[10].astype(jnp.bfloat16), "dp").astype(jnp.float32),
        lax.psum(owned_grads[11].astype(jnp.bfloat16), "dp").astype(jnp.float32),
        lax.psum(owned_grads[12].astype(jnp.bfloat16), "dp").astype(jnp.float32),
        lax.psum(owned_grads[13].astype(jnp.bfloat16), "dp").astype(jnp.float32),
        lax.psum(owned_grads[14].astype(jnp.bfloat16), "dp").astype(jnp.float32),
    )
    return (
        layer_out,
        loss_value,
        table_grad,
        summed[0],
        summed[1],
        summed[2],
        summed[3],
        summed[4],
        summed[5],
        summed[6],
        summed[7],
        summed[8],
        summed[9],
        summed[10],
        summed[11],
        summed[12],
        summed[13],
        summed[14],
    )


CORES = 2
PLANES = 4
LINES = 4
CHIPS = PLANES * LINES
DEVICES = CORES * CHIPS
CAPACITY = 48
GROUPS = 3
PAD = 16
TOKENS = 768
WIDTH = 768
WIDE = 3072
VOCAB_ROWS = 1024
PAIR_ROWS = HEADS * PAD
SLOT_ROWS = DEVICES * PAD
LONG = 64
BLOCK = 256
MESH = pl.DeviceIdType.MESH
LOW = jnp.bfloat16
FULL = jnp.float32
VMEM_LIMIT = 62 * 1024 * 1024

INPUTS = ["table", "token_ids", "lens", "slots", "langs"]
INPUTS += ["wq", "bq", "wk", "wv", "bv", "wo", "bo", "g1", "s1", "wup", "bup", "wdown", "bdown"]
INPUTS += ["g2", "s2"]
OUTPUTS = ["layer_out", "table_grad", "g_wq", "g_wk", "g_wv", "g_wo", "g_wup", "g_wdown"]
OUTPUTS += ["g_small", "loss"]


def place():
    core = lax.axis_index("dp")
    chip = lax.axis_index("fsdp")
    along_x = chip + 1 - 2 * (chip % 2)
    along_y = chip + 2 - 4 * ((chip // 2) % 2)
    first = along_x + core * (along_y - along_x)
    second = along_y + core * (along_x - along_y)
    return core, chip, first, second


def greet():
    core, chip, _, _ = place()
    me = core * CHIPS + chip
    barrier = pltpu.get_barrier_semaphore()

    def signal(step):
        other = lax.rem(me + step, DEVICES)
        pl.semaphore_signal(
            barrier,
            inc=1,
            device_id=(lax.div(other, CHIPS), lax.rem(other, CHIPS)),
            device_id_type=MESH,
        )

    every(1, DEVICES, signal)


def enter():
    pl.semaphore_wait(pltpu.get_barrier_semaphore(), DEVICES - 1)


def remote(source, target, send_sem, recv_sem, core, chip):
    return pltpu.make_async_remote_copy(
        src_ref=source,
        dst_ref=target,
        send_sem=send_sem,
        recv_sem=recv_sem,
        device_id=(core, chip),
        device_id_type=MESH,
    )


def every(start, stop, act):
    def step(index, carry):
        act(index)
        return carry

    lax.fori_loop(start, stop, step, 0)


def weight_steps(piece, send, recv):
    core, chip, first, second = place()
    plane, line = chip // LINES, chip % LINES
    line_first, line_second = first % LINES, second % LINES
    line_far = line_first + line_second - line
    is_low, is_high = plane > 0, plane < PLANES - 1

    def copy(send_index, recv_index, at, to_core, to_chip, carried=core):
        part = piece(at, carried)
        return remote(part, part, send.at[send_index], recv.at[recv_index], to_core, to_chip)

    def up(at_plane):
        return copy(at_plane, at_plane, at_plane * LINES + line, core, chip + LINES)

    def down(at_plane, index):
        return copy(index, at_plane, at_plane * LINES + line, core, chip - LINES)

    def side(at_plane, base, at_line, target):
        return copy(base + at_plane, base + at_plane, at_plane * LINES + at_line, core, target)

    def across(at_plane, base, at_line):
        return copy(base + at_plane, base + at_plane, at_plane * LINES + at_line, 1 - core, chip)

    def begin():
        pl.when(is_high)(lambda: up(plane).start())
        pl.when(is_low)(lambda: down(plane, PLANES).start())
        side(plane, 5, line, first).start()
        side(plane, 9, line, second).start()

    def at_distance(distance, act):
        if distance == 0:
            act(plane, None)
            return
        pl.when(plane >= distance)(lambda: act(plane - distance, True))
        pl.when(plane + distance < PLANES)(lambda: act(plane + distance, False))

    def chain(distance):
        def act(at_plane, from_low):
            if from_low:
                up(at_plane).wait_recv()
                pl.when(is_high)(lambda: up(at_plane).start())
            else:
                down(at_plane, at_plane).wait_recv()
                pl.when(is_low)(lambda: down(at_plane, at_plane).start())
            side(at_plane, 5, line, first).start()
            side(at_plane, 9, line, second).start()
            across(at_plane, 17, line).start()

        return partial(at_distance, distance, act)

    def near(distance):
        def act(at_plane, from_low):
            side(at_plane, 5, line_first, first).wait_recv()
            side(at_plane, 13, line_first, second).start()
            across(at_plane, 21, line_first).start()

        return partial(at_distance, distance, act)

    def far(distance):
        def act(at_plane, from_low):
            side(at_plane, 9, line_second, second).wait_recv()
            across(at_plane, 25, line_second).start()
            side(at_plane, 13, line_far, second).wait_recv()
            across(at_plane, 29, line_far).start()

        return partial(at_distance, distance, act)

    def finish():
        for step in range(1, PLANES):
            index = 17 + (plane + step) % PLANES
            copy(index, index, chip, 1 - core, chip, 1 - core).wait_recv()
        every(21, 33, lambda index: copy(index, index, chip, 1 - core, chip, 1 - core).wait_recv())

    def drain():
        def sent(index):
            copy(index, index, chip, 1 - core, chip).wait_send()

        for at_plane in range(PLANES):
            pl.when((plane >= at_plane) & is_high)(partial(sent, at_plane))
            pl.when((plane < at_plane) & is_low)(partial(sent, at_plane))
        pl.when(is_low)(partial(sent, PLANES))
        every(5, 17, sent)
        for step in range(1, PLANES):
            sent(17 + (plane + step) % PLANES)
        every(21, 33, sent)

    moves = [chain(1), near(0), chain(2), near(1), chain(3), far(0)]
    moves += [near(2), far(1), near(3), far(2), far(3)]
    return begin, moves, finish, drain


def gather_steps(buffer, send, recv):
    core, chip, first, second = place()
    plane, line = chip // LINES, chip % LINES
    line_first, line_second = first % LINES, second % LINES
    line_far = line_first + line_second - line
    half = buffer.shape[-1] // 2
    columns = pl.ds(pl.multiple_of(core * half, 128), half)
    others = pl.ds(pl.multiple_of((1 - core) * half, 128), half)

    def copy(index, part, to_core, to_chip):
        return remote(part, part, send.at[index], recv.at[index], to_core, to_chip)

    def own(at):
        return buffer.at[at, plane, line]

    def chip_part(at_plane, at_line, which):
        return buffer.at[:, at_plane, at_line, :, which]

    def line_part(at_line, which):
        return buffer.at[:, :, at_line, :, which]

    def start():
        copy(0, own(core), 1 - core, chip).start()

    def planes():
        copy(0, own(1 - core), 1 - core, chip).wait_recv()
        for step in range(1, PLANES):
            part = chip_part(plane, line, columns)
            copy(step, part, core, (chip + LINES * step) % CHIPS).start()

    def sides():
        for step in range(1, PLANES):
            part = chip_part((plane + PLANES - step) % PLANES, line, columns)
            copy(step, part, core, chip).wait_recv()
        copy(4, line_part(line, columns), core, first).start()
        copy(5, line_part(line, columns), core, second).start()
        for step in range(1, PLANES):
            part = chip_part((plane + PLANES - step) % PLANES, line, columns)
            copy(6 + step, part, 1 - core, chip).start()

    def corner():
        copy(4, line_part(line_first, columns), core, first).wait_recv()
        copy(6, line_part(line_first, columns), core, second).start()
        copy(10, line_part(line_first, columns), 1 - core, chip).start()
        copy(5, line_part(line_second, columns), core, second).wait_recv()
        copy(11, line_part(line_second, columns), 1 - core, chip).start()

    def last():
        copy(6, line_part(line_far, columns), core, second).wait_recv()
        copy(12, line_part(line_far, columns), 1 - core, chip).start()

    def finish():
        for step in range(1, PLANES):
            part = chip_part((plane + PLANES - step) % PLANES, line, others)
            copy(6 + step, part, 1 - core, chip).wait_recv()
        copy(10, line_part(line_second, others), 1 - core, chip).wait_recv()
        copy(11, line_part(line_first, others), 1 - core, chip).wait_recv()
        copy(12, line_part(line_far, others), 1 - core, chip).wait_recv()

    def drain():
        copy(0, own(core), 1 - core, chip).wait_send()
        for index in [1, 2, 3, 7, 8, 9]:
            copy(index, chip_part(plane, line, columns), 1 - core, chip).wait_send()
        for index in [4, 5, 6, 10, 11, 12]:
            copy(index, line_part(line, columns), 1 - core, chip).wait_send()

    return [start, planes, sides, corner, last, finish], drain


def iota(shape, axis):
    return lax.broadcasted_iota(jnp.int32, shape, axis)


def over(numbers, power):
    return lax.shift_right_arithmetic(numbers, jnp.full_like(numbers, power.bit_length() - 1))


def within(numbers, power):
    return numbers & (power - 1)


def as_column(row):
    parts = []
    for start in range(0, row.shape[1], 128):
        tile = jnp.broadcast_to(row[:, start : start + 128], (128, 128))
        parts.append(jnp.transpose(tile)[:, 0:1])
    return jnp.concatenate(parts, axis=0)


def as_row(column):
    parts = []
    for start in range(0, column.shape[0], 128):
        tile = jnp.broadcast_to(column[start : start + 128, :], (128, 128))
        parts.append(jnp.transpose(tile)[0:1, :])
    return jnp.concatenate(parts, axis=1)


def dot(left_side, right_side):
    return contract(left_side, right_side, 1, 0)


def dot_turned(left_side, right_side):
    return contract(left_side, right_side, 1, 1)


def norm_parts(inputs):
    centered = inputs - jnp.mean(inputs, axis=-1, keepdims=True)
    inverse = lax.rsqrt(jnp.mean(centered * centered, axis=-1, keepdims=True) + EPSILON)
    return centered * inverse, inverse


def norm_back_parts(grad_output, normed, inverse, ln_gain):
    grad_normed = grad_output * ln_gain
    first_term = jnp.mean(grad_normed, axis=-1, keepdims=True)
    second_term = jnp.mean(grad_normed * normed, axis=-1, keepdims=True)
    return (
        inverse * (grad_normed - first_term - normed * second_term),
        jnp.sum(grad_output * normed, axis=0, keepdims=True),
        jnp.sum(grad_output, axis=0, keepdims=True),
    )


def erf_parts(inputs):
    decay = jnp.exp(-0.5 * inputs * inputs)
    share = 1.0 / (1.0 + jnp.abs(inputs) * (0.3275911 * 0.5**0.5))
    terms = [1.061405429, -1.453152027, 1.421413741, -0.284496736, 0.254829592]
    series = 0.5 * terms[0]
    for term in terms[1:]:
        series = series * share + 0.5 * term
    tail = series * share * decay
    return jnp.where(inputs >= 0.0, 1.0 - tail, tail), decay


def gelu_parts(inputs):
    below, decay = erf_parts(inputs)
    return inputs * below, below + inputs * decay * ((2.0 * 3.141592653589793) ** -0.5)


def gelu(inputs):
    return inputs * erf_parts(inputs)[0]


def layer_kernel(names, *refs):
    r = SimpleNamespace(**dict(zip(names, refs, strict=True)))
    core, chip, _, _ = place()
    me = core * CHIPS + chip
    here = (core, chip // LINES, chip % LINES)
    scale = HEAD ** (-0.5)
    depth, deep = WIDTH // CHIPS, WIDE // CHIPS
    sentences = TOKENS // LONG

    for j in range(TOKENS // 128):
        r.ids[j : j + 1, :] = jnp.concatenate(
            [r.token_ids[2 * j : 2 * j + 1, :], r.token_ids[2 * j + 1 : 2 * j + 2, :]], axis=1
        )
    r.ids[TOKENS // 128 : 8, :] = jnp.zeros((8 - TOKENS // 128, 128), jnp.int32)
    greet()
    ahead = (iota((TOKENS, TOKENS), 0) < iota((TOKENS, TOKENS), 1)).astype(LOW)
    r.embedded[...] = ahead
    mine = pl.ds(pl.multiple_of(chip * depth, 16), depth)
    for index, shard in enumerate([r.wq, r.wk, r.wv, r.wo]):
        r.wa[mine, index * WIDTH : (index + 1) * WIDTH] = shard[...]
    r.wb[mine, :] = r.wup[...]
    r.wc[pl.ds(pl.multiple_of(chip * deep, 16), deep), :] = r.wdown[...]
    r.every_ids[me] = r.ids[...]
    enter()

    def peer(step):
        other = lax.rem(me + step, DEVICES)
        return other, lax.div(other, CHIPS), lax.rem(other, CHIPS)

    def ids_copy(step):
        other, to_core, to_chip = peer(step)
        return remote(r.ids, r.every_ids.at[me], r.one_send.at[0], r.one_recv.at[0], to_core, to_chip)

    def all_but_one(ref, index):
        part = ref.at[0 : DEVICES - 1]
        return remote(part, part, r.one_send.at[index], r.one_recv.at[index], 1 - core, chip)

    every(1, DEVICES, lambda step: ids_copy(step).start())

    def block(ref, rows, columns):
        def piece(at, carried):
            return ref.at[
                pl.ds(pl.multiple_of(at * rows, 16), rows),
                pl.ds(pl.multiple_of(carried * columns, 128), columns),
            ]

        return piece

    begin_a, moves_a, finish_a, drain_a = weight_steps(
        block(r.wa, depth, 2 * WIDTH), r.weight_send.at[0], r.weight_recv.at[0]
    )
    begin_b, moves_b, finish_b, drain_b = weight_steps(
        block(r.wb, depth, WIDE // 2), r.weight_send.at[1], r.weight_recv.at[1]
    )
    begin_c, moves_c, finish_c, drain_c = weight_steps(
        block(r.wc, deep, WIDTH // 2), r.weight_send.at[2], r.weight_recv.at[2]
    )
    begin_a()
    begin_b()
    begin_c()

    def move(*steps):
        for moves, first_step in steps:
            moves[first_step]()
            moves[first_step + 1]()

    all_but_one(r.every_ids, 0).wait_recv()
    all_ids = jnp.concatenate([r.every_ids[:, j, :] for j in range(TOKENS // 128)], axis=1)
    all_owner = over(all_ids, VOCAB_ROWS)
    asked = all_owner == me
    ranks = dot(asked.astype(LOW), r.embedded[...])
    r.rank[...] = jnp.where(asked, ranks, -1.0)
    local_row = (all_ids - all_owner * VOCAB_ROWS + 1).astype(FULL)
    r.code[...] = local_row + (over(iota((DEVICES, TOKENS), 1), LONG) * 2048).astype(FULL)

    quarter_size = DEVICES // 4

    def rows_copy(other, quarter):
        return remote(
            r.rows.at[:, pl.ds(pl.multiple_of(other * PAD, 16), PAD), :],
            r.replies.at[:, pl.ds(pl.multiple_of(me * PAD, 16), PAD), :],
            r.rows_send.at[quarter],
            r.rows_recv.at[quarter],
            lax.div(other, CHIPS),
            lax.rem(other, CHIPS),
        )

    def rows_of(quarter):
        count = quarter_size - 1 if quarter == 3 else quarter_size
        part = r.replies.at[:, 0 : count * PAD, :]
        return remote(
            part, part, r.rows_send.at[quarter], r.rows_recv.at[quarter], 1 - core, chip
        )

    def pick(source):
        rank = r.rank[pl.ds(source, 1), :]
        code = r.code[pl.ds(source, 1), :]
        here_at = iota((CAPACITY, TOKENS), 0).astype(FULL) == rank
        found = jnp.sum(jnp.where(here_at, code, 0.0), axis=1, keepdims=True)
        sent = jnp.floor(found * (1.0 / 2048))
        row = found - sent * 2048.0 - 1.0
        chosen = (iota((CAPACITY, VOCAB_ROWS), 1).astype(FULL) == row).astype(LOW)
        at = pl.ds(pl.multiple_of(source * PAD, 16), PAD)
        source_sent = sent + (source * PAD).astype(FULL)
        for group in range(GROUPS):
            part = slice(group * PAD, (group + 1) * PAD)
            r.chosen[group, at, :] = chosen[part]
            r.found[group, at, 0:1] = row[part]
            r.found[group, at, 1:2] = source_sent[part]

    def quarter_rows(quarter):
        now = lax.rem(lax.div(me, quarter_size) + 1 + quarter, 4)

        def pick_two(index):
            pick(now * quarter_size + 2 * index)
            pick(now * quarter_size + 2 * index + 1)

        every(0, quarter_size // 2, pick_two)
        span = pl.ds(pl.multiple_of(now * quarter_size * PAD, 128), quarter_size * PAD)
        for start in range(0, WIDTH, BLOCK):
            lanes = slice(start, start + BLOCK)
            picked = r.chosen[:, span, :].reshape(GROUPS * quarter_size * PAD, VOCAB_ROWS)
            found_rows = dot(picked, r.table[:, lanes]).astype(LOW)
            r.rows[:, span, lanes] = found_rows.reshape(GROUPS, quarter_size * PAD, BLOCK)

        def send(index):
            other = now * quarter_size + lax.rem(lax.rem(me, quarter_size) + index, quarter_size)
            rows_copy(other, quarter).start()

        every(lax.div(quarter, 3), quarter_size, send)
        pl.when(quarter == 0)(partial(move, (moves_a, 0)))
        pl.when(quarter == 1)(partial(move, (moves_b, 0)))
        pl.when(quarter == 2)(partial(move, (moves_c, 0)))
        pl.when(quarter == 3)(partial(move, (moves_a, 2)))

    every(0, 4, quarter_rows)
    own_at = pl.ds(pl.multiple_of(me * PAD, 16), PAD)
    r.replies[:, own_at, :] = r.rows[:, own_at, :]

    move((moves_b, 2), (moves_c, 2))

    small_here = pl.ds(pl.multiple_of(chip * 128, 128), 128)
    lines = [r.bq, r.bv, r.bo, r.g1, r.s1, r.bdown, r.g2, r.s2]
    lines = [line[...].reshape(1, depth).astype(FULL) for line in lines]
    up_line = r.bup[...].reshape(1, deep).astype(FULL)
    lines += [up_line[:, part * depth : (part + 1) * depth] for part in range(deep // depth)]
    lines.append(jnp.zeros((PAD - len(lines), depth), FULL))
    own_small = jnp.concatenate(lines, axis=0)
    own_small = jnp.concatenate([own_small, jnp.zeros((PAD, 128 - depth), FULL)], axis=1)
    r.smalls[:, small_here] = own_small.astype(LOW)

    def small_copy(step):
        part = r.smalls.at[:, small_here]
        to_chip = lax.rem(chip + step, CHIPS)
        return remote(part, part, r.small_send.at[0], r.small_recv.at[0], core, to_chip)

    def all_smalls():
        part = r.smalls.at[:, 0 : (CHIPS - 1) * 128]
        return remote(part, part, r.small_send.at[0], r.small_recv.at[0], 1 - core, chip)

    every(1, CHIPS, lambda step: small_copy(step).start())
    move((moves_a, 4))

    own_row = jnp.concatenate([r.ids[j : j + 1, :] for j in range(TOKENS // 128)], axis=1)
    owner_row = over(own_row, VOCAB_ROWS).astype(FULL)
    owner_col = as_column(owner_row)
    earlier = (owner_row == owner_col) & (iota((TOKENS, TOKENS), 1) < iota((TOKENS, TOKENS), 0))
    own_rank = jnp.sum(earlier.astype(FULL), axis=1, keepdims=True)
    own_group = jnp.floor(own_rank * (1.0 / PAD))
    own_slot = own_group * SLOT_ROWS + owner_col * PAD + (own_rank - own_group * PAD)
    r.slot_col[...] = own_slot
    r.slot_line[0:1, :] = as_row(own_slot)
    move((moves_b, 4), (moves_c, 4))

    at_sent = over(iota((1, TOKENS), 1), LONG)
    lens = jnp.concatenate(
        [r.lens[...].reshape(1, sentences).astype(FULL), jnp.zeros((1, PAD - sentences), FULL)],
        axis=1,
    )
    spread_lens = dot(
        jnp.broadcast_to(lens, (8, PAD)).astype(LOW),
        (iota((PAD, TOKENS), 0) == over(iota((PAD, TOKENS), 1), LONG)).astype(LOW),
    )[0:1]
    valid_row = ((iota((1, TOKENS), 1) - at_sent * LONG).astype(FULL) < spread_lens).astype(FULL)
    r.valid_line[0:1, :] = valid_row
    r.valid_col[...] = as_column(valid_row)
    half_block = BLOCK // 2
    stacked_shape = (4 * half_block, half_block)
    same = within(over(iota(stacked_shape, 0), LONG), 2) == over(iota(stacked_shape, 1), LONG)
    r.block_bias[...] = jnp.where(same, 0.0, MASK_FLOOR)
    r.valid_bias[0:1, :] = (1.0 - valid_row) * MASK_FLOOR

    slots = r.slots[...].reshape(1, DEVICES * sentences)
    gap = jnp.full((1, PAD - sentences), -2, jnp.int32)
    slot_line = jnp.concatenate(
        [
            part
            for device in range(DEVICES)
            for part in (slots[:, device * sentences : (device + 1) * sentences], gap)
        ],
        axis=1,
    )
    side_line = within(slot_line, 2) + jnp.where(slot_line < 0, 8, 0)
    pair_line = over(slot_line, 2)
    pairs = r.langs.shape[0]
    lang_line = r.langs[...].reshape(1, pairs).astype(FULL)
    lang_line = jnp.concatenate([lang_line, jnp.full((1, -pairs % 128), -1.0, FULL)], axis=1)
    lang_col = as_column(lang_line)
    same_lang = jnp.sum(jnp.where(lang_col == lang_line, 1.0, 0.0), axis=1, keepdims=True)
    per_pair = 1.0 / (2.0 * LANGS * same_lang)
    at_pair = iota((lang_line.shape[1], SLOT_ROWS), 0) == pair_line
    weight_line = jnp.sum(jnp.where(at_pair, per_pair, 0.0), axis=0, keepdims=True)
    r.pairs[0:1, :] = weight_line
    r.pairs[1:2, :] = pair_line.astype(FULL)
    r.pairs[2:3, :] = side_line.astype(FULL)
    r.pairs_col[:, 0:1] = as_column(weight_line)
    r.pairs_col[:, 1:2] = as_column(pair_line.astype(FULL))
    r.pairs_col[:, 2:3] = as_column(side_line.astype(FULL))
    move((moves_a, 6))

    all_smalls().wait_recv()
    smalls = r.smalls[...].astype(FULL)
    r.vectors[:, 0:WIDTH] = jnp.concatenate(
        [smalls[:, at * 128 : at * 128 + depth] for at in range(CHIPS)], axis=1
    )
    r.up_bias[0:1, :] = jnp.concatenate(
        [
            smalls[8 + part : 9 + part, at * 128 : at * 128 + depth]
            for at in range(CHIPS)
            for part in range(deep // depth)
        ],
        axis=1,
    )

    def vector(index):
        return r.vectors[index : index + 1, :]

    r.qkv_bias[0:1, 0:WIDTH] = vector(0)
    r.qkv_bias[0:1, WIDTH : 2 * WIDTH] = jnp.zeros((1, WIDTH), FULL)
    r.qkv_bias[0:1, 2 * WIDTH : 3 * WIDTH] = vector(1)

    move((moves_b, 6), (moves_c, 6))

    def first_row(source):
        code = jnp.where(r.rank[pl.ds(source, 1), :] >= 0.0, r.code[pl.ds(source, 1), :], 0.0)
        at_first = iota((PAD, TOKENS), 1) == iota((PAD, TOKENS), 0) * LONG
        found = jnp.sum(jnp.where(at_first, code, 0.0), axis=1, keepdims=True)
        row = found - jnp.floor(found * (1.0 / 2048)) * 2048.0 - 1.0
        r.found[GROUPS, pl.ds(pl.multiple_of(source * PAD, 16), PAD), 0:1] = row

    every(0, DEVICES, first_row)
    for group in range(GROUPS + 1):
        named = as_row(r.found[group, :, 0:1])
        by_row = iota((VOCAB_ROWS, SLOT_ROWS), 0).astype(FULL) == named
        r.by_row[:, group * SLOT_ROWS : (group + 1) * SLOT_ROWS] = by_row.astype(LOW)

    def order(tile):
        at = pl.ds(pl.multiple_of(tile * BLOCK, BLOCK), BLOCK)
        lanes = iota((BLOCK, GROUPS * SLOT_ROWS), 1).astype(FULL)
        r.qkv[at, 0 : GROUPS * SLOT_ROWS] = (r.slot_col[at, :] == lanes).astype(LOW)

    every(0, TOKENS // BLOCK, order)
    for group in range(GROUPS):
        slot_at = iota((SLOT_ROWS, TOKENS), 0) + group * SLOT_ROWS
        named = (slot_at.astype(FULL) == r.slot_line[0:1, :]).astype(LOW)
        r.chosen[group, :, 0:TOKENS] = named
    move((moves_a, 8), (moves_b, 8), (moves_c, 8))
    for moves in (moves_a, moves_b, moves_c):
        moves[10]()
    finish_a()
    for quarter in range(4):
        rows_of(quarter).wait_recv()

    def embed(tile):
        at = pl.ds(pl.multiple_of(tile * BLOCK, BLOCK), BLOCK)
        replies = r.replies[:, :, at].reshape(GROUPS * SLOT_ROWS, BLOCK)
        r.embedded[:, at] = dot(r.qkv[:, 0 : GROUPS * SLOT_ROWS], replies).astype(LOW)

    every(0, WIDTH // BLOCK, embed)

    def project(tile):
        at = pl.ds(pl.multiple_of(tile * BLOCK, BLOCK), BLOCK)
        r.qkv[:, at] = (dot(r.embedded[...], r.wa[:, at]) + r.qkv_bias[0:1, at]).astype(LOW)

    every(0, 9, project)

    row_sent = within(iota((PAIR_ROWS, WIDTH), 0), PAD)
    row_head = over(iota((PAIR_ROWS, WIDTH), 0), PAD)
    lane_block = over(iota((PAIR_ROWS, WIDTH), 1), HEAD)
    in_head = row_head == lane_block
    seen = (row_sent == lane_block) & (r.valid_line[0:1, :] > 0.0)
    firsts = (iota((PAD, TOKENS), 1) == iota((PAD, TOKENS), 0) * LONG).astype(LOW)
    real_row = iota((PAD, 1), 0) < sentences

    def spread(rows):
        return jnp.where(in_head, jnp.concatenate([rows] * HEADS, axis=0), jnp.zeros((), LOW))

    def fold(tall):
        tall = jnp.where(in_head, tall, 0.0)
        return sum(tall[head * PAD : (head + 1) * PAD] for head in range(HEADS))

    keys, values = slice(WIDTH, 2 * WIDTH), slice(2 * WIDTH, 3 * WIDTH)
    embedded_cls = dot(firsts, r.embedded[...]).astype(LOW)
    query_cls = (dot(embedded_cls, r.wa[:, 0:WIDTH]) + vector(0)).astype(LOW)
    cls_scores = dot_turned(spread(query_cls), r.qkv[:, keys]) * scale
    cls_scores = jnp.where(seen, cls_scores, MASK_FLOOR)
    cls_peak = jnp.max(cls_scores, axis=1, keepdims=True)
    cls_exp = jnp.where(seen, jnp.exp(cls_scores - cls_peak), 0.0)
    cls_total = jnp.sum(cls_exp, axis=1, keepdims=True)
    cls_probs = cls_exp / jnp.where(cls_total > 0.0, cls_total, 1.0)
    probs_low = cls_probs.astype(LOW)
    r.probs[...] = cls_probs
    context_cls = fold(dot(probs_low, r.qkv[:, values])).astype(LOW)
    first_cls = (
        embedded_cls.astype(FULL)
        + dot(context_cls, r.wa[:, 3 * WIDTH : 4 * WIDTH])
        + vector(2)
    )
    normed_one, inverse_one = norm_parts(first_cls)
    r.normed_one[...] = normed_one
    hidden_cls = normed_one * vector(3) + vector(4)
    hidden_cls_low = hidden_cls.astype(LOW)
    early_here = r.early.at[here]
    early_here[:, 0:WIDTH] = hidden_cls_low
    early_here[:, WIDTH : 2 * WIDTH] = query_cls
    steps_u, drain_u = gather_steps(r.units, r.gather_send.at[0], r.gather_recv.at[0])
    steps_e, drain_e = gather_steps(r.early, r.gather_send.at[1], r.gather_recv.at[1])
    steps_d, drain_d = gather_steps(r.downs, r.gather_send.at[2], r.gather_recv.at[2])
    steps_a, drain_a2 = gather_steps(r.attends, r.gather_send.at[3], r.gather_recv.at[3])
    steps_q, drain_q = gather_steps(r.queries, r.gather_send.at[4], r.gather_recv.at[4])
    steps_e[0]()

    def attend(unit):
        rows = pl.ds(pl.multiple_of(unit * half_block, half_block), half_block)
        lane_head = over(iota((half_block, BLOCK), 1), HEAD)
        bias = r.block_bias[...] + r.valid_bias[0:1, rows]

        def part(which, lane):
            return r.qkv[rows, which * WIDTH + lane : which * WIDTH + lane + BLOCK]

        for lane in range(0, WIDTH, BLOCK):
            query = part(0, lane) * jnp.asarray(scale, LOW)
            key, value = part(1, lane), part(2, lane)
            stacked = jnp.concatenate(
                [jnp.where(lane_head == head, query, jnp.zeros((), LOW)) for head in range(4)],
                axis=0,
            )
            scores = dot_turned(stacked, key) + bias
            shifted = jnp.exp(scores - jnp.max(scores, axis=1, keepdims=True))
            probs = shifted * (1.0 / jnp.sum(shifted, axis=1, keepdims=True))
            mixed = dot(probs.astype(LOW), value)
            result = mixed[0:half_block]
            for head in range(1, 4):
                result = jnp.where(
                    lane_head == head, mixed[head * half_block : (head + 1) * half_block], result
                )
            r.context[rows, lane : lane + BLOCK] = result.astype(LOW)

    def open_tile(tile):
        at = pl.ds(pl.multiple_of(tile * BLOCK, BLOCK), BLOCK)
        attended = dot(r.context[at, :], r.wa[:, 3 * WIDTH : 4 * WIDTH]) + vector(2)
        normed, _ = norm_parts(r.embedded[at, :].astype(FULL) + attended)
        hidden = normed * vector(3) + vector(4)
        r.context[at, :] = hidden.astype(LOW)
        r.table_full[at, :] = hidden + vector(5)

    most = SLOT_ROWS
    rest_at = pl.ds(most, TOKENS - most)

    def feed_up(part):
        at = pl.ds(pl.multiple_of(part * BLOCK, BLOCK), BLOCK)
        up_pre = dot(r.context[...], r.wb[:, at]) + r.up_bias[0:1, at]
        active = gelu(up_pre).astype(LOW)
        lanes = pl.ds(pl.multiple_of(lax.rem(part, 4) * BLOCK, BLOCK), BLOCK)
        r.chosen[lax.div(part, 4), :, lanes] = active[:most]
        rest = pl.ds(pl.multiple_of(lax.div(part, 6) * BLOCK, BLOCK), BLOCK)
        lanes = pl.ds(pl.multiple_of(lax.rem(part, 6) * BLOCK, BLOCK), BLOCK)
        r.slopes[rest, lanes] = active[most:]

    def feed_down(part):
        lanes = pl.ds(pl.multiple_of(part * BLOCK, BLOCK), BLOCK)
        total = r.table_full[0:most, lanes]
        for group in range(GROUPS):
            rows = slice(group * VOCAB_ROWS, (group + 1) * VOCAB_ROWS)
            total = total + dot(r.chosen[group], r.wc[rows, lanes])
        r.table_full[0:most, lanes] = total

    def feed_rest(part):
        lanes = pl.ds(pl.multiple_of(part * BLOCK, BLOCK), BLOCK)
        low_part = dot(r.slopes[0:BLOCK, :], r.wc[0 : WIDE // 2, lanes])
        high_part = dot(r.slopes[BLOCK : 2 * BLOCK, :], r.wc[WIDE // 2 :, lanes])
        r.table_full[rest_at, lanes] += low_part + high_part

    def layer_copy(tile):
        at = pl.ds(pl.multiple_of(tile * BLOCK, BLOCK), BLOCK)
        return pltpu.make_async_copy(r.context.at[at], r.layer_out.at[at], r.out_sem.at[tile])

    def close_tile(tile):
        at = pl.ds(pl.multiple_of(tile * BLOCK, BLOCK), BLOCK)
        normed, _ = norm_parts(r.table_full[at, :])
        out = normed * vector(6) + vector(7)
        r.context[at, :] = (out * r.valid_col[at, :]).astype(LOW)
        layer_copy(tile).start()

    finish_b()
    r.hidden_cls[...] = hidden_cls_low

    def up_part(part):
        at = pl.ds(pl.multiple_of(part * BLOCK, BLOCK), BLOCK)
        active, slope = gelu_parts(dot(r.hidden_cls[...], r.wb[:, at]) + r.up_bias[0:1, at])
        r.active_cls[:, at] = active.astype(LOW)
        r.slope_cls[:, at] = slope

    every(0, WIDE // BLOCK, up_part)
    steps_e[1]()
    finish_c()

    def pack_tall(target, first_row, act):
        def run(part):
            window = jnp.minimum(lax.div(part * 2 * depth, 128) * 128, WIDTH - BLOCK)
            shape = (BLOCK, BLOCK)
            lane = within(iota(shape, 1), 128)
            column = over(iota(shape, 1), 128) * depth + lane + (part * 2 * depth - window)
            select = ((iota(shape, 0) == column) & (lane < depth)).astype(LOW)
            taken = dot(r.tall[:, pl.ds(pl.multiple_of(window, 128), BLOCK)], select)

            def beside(low, high):
                return [
                    low[:, one * 128 : (one + 1) * 128]
                    + pltpu.roll(high[:, one * 128 : (one + 1) * 128], depth, 1)
                    for one in range(2)
                ]

            for half in range(CORES):
                base = half * PAIR_ROWS // 2
                both = beside(taken[base : base + 48], taken[base + 48 : base + 96])
                for one in range(2):
                    at = half * CHIPS + 2 * part + one
                    target[at, first_row : first_row + 48, :] = act(
                        2 * part + one, both[one]
                    ).astype(LOW)
            if first_row:
                left = beside(taken[PAIR_ROWS : PAIR_ROWS + PAD], taken[PAIR_ROWS + PAD :])
                for half in range(CORES):
                    for one in range(2):
                        target[half * CHIPS + 2 * part + one, 0:PAD, :] = left[one].astype(LOW)

        return run

    def pack_coefs(coefs):
        shape = (PAIR_ROWS, GROUPS * 128)
        folds = over(iota(shape, 0), PAD) + over(iota(shape, 1), 128) * PAD == within(
            iota(shape, 1), 128
        )
        lanes = contract(coefs, folds.astype(LOW), 0, 0).astype(LOW)
        total = None
        for group in range(GROUPS):
            part = dot(r.chosen[group, :, 0:TOKENS], lanes[:, group * 128 : (group + 1) * 128])
            total = part if total is None else total + part
        return total.astype(LOW).reshape(DEVICES, PAD, 128)


    def down_part(part):
        at = pl.ds(pl.multiple_of(part * BLOCK, BLOCK), BLOCK)
        r.wide_cls[:, at] = dot(r.active_cls[...], r.wc[:, at])

    every(0, WIDTH // BLOCK, down_part)
    down_pre = r.wide_cls[:, 0:WIDTH] + vector(5)
    normed_two, inverse_two = norm_parts(hidden_cls + down_pre)
    summary = normed_two * vector(6) + vector(7)
    magnitude = jnp.sqrt(jnp.sum(summary * summary, axis=-1, keepdims=True) + EPSILON)
    unit = jnp.where(real_row, summary / magnitude, 0.0)
    r.units[here] = unit.astype(LOW)

    steps_u[0]()
    r.tall[0:PAIR_ROWS, :] = dot(probs_low, r.embedded[...]).astype(LOW)
    r.tall[PAIR_ROWS : PAIR_ROWS + PAD, :] = context_cls
    r.tall[PAIR_ROWS + PAD :, :] = embedded_cls
    pack_one = pack_tall(r.mail_one, PAD, lambda at, both: both)

    def pack_one_step(part):
        pack_one(part)
        pl.when(part == 0)(steps_u[1])
        pl.when(part == 4)(steps_u[2])

    every(0, CHIPS // 2, pack_one_step)
    steps_e[2]()
    r.mail_one[:, 64:80, :] = pack_coefs(probs_low)
    steps_u[3]()

    def post(box, got, index):
        def send(step):
            other, to_core, to_chip = peer(step)
            remote(
                box.at[other], got.at[me], r.one_send.at[index], r.one_recv.at[index], to_core, to_chip
            ).start()

        every(1, DEVICES, send)
        got[me] = box[me]


    def attend_step(unit):
        attend(unit)
        pl.when(unit == 0)(steps_e[3])
        pl.when(unit == 1)(steps_u[4])
        pl.when(unit == 3)(steps_u[5])

    every(0, 6, attend_step)
    post(r.mail_one, r.got_one, 1)
    steps_e[4]()

    units = r.units[...].reshape(SLOT_ROWS, WIDTH)
    weight_row, pair_row, side_row = r.pairs[0:1, :], r.pairs[1:2, :], r.pairs[2:3, :]

    def pair_scores(rows, pair_col, side_col):
        opposite = side_col + side_row == 1.0
        partner = opposite & (pair_col == pair_row)
        raw = SCORE_SCALE * dot_turned(rows, units)
        shifted = jnp.where(partner, raw - SCORE_SCALE * MARGIN_WIDTH, raw)
        return jnp.where(opposite, shifted, MASK_FLOOR), partner

    every_score, every_partner = pair_scores(
        units, r.pairs_col[:, 1:2], r.pairs_col[:, 2:3]
    )
    peak_row = jnp.max(every_score, axis=0, keepdims=True)
    log_row = peak_row + jnp.log(
        jnp.sum(jnp.exp(every_score - peak_row), axis=0, keepdims=True)
    )
    picked_row = jnp.sum(jnp.where(every_partner, every_score, 0.0), axis=0, keepdims=True)
    r.loss[...] = jnp.sum(weight_row * (log_row - picked_row), axis=1, keepdims=True)

    rows_here = pl.ds(pl.multiple_of(me * PAD, 16), PAD)
    own_score, own_partner = pair_scores(
        r.units[here], r.pairs_col[rows_here, 1:2], r.pairs_col[rows_here, 2:3]
    )
    own_partner = own_partner.astype(FULL)
    own_peak = jnp.max(own_score, axis=1, keepdims=True)
    own_exp = jnp.exp(own_score - own_peak)
    own_share = own_exp / jnp.sum(own_exp, axis=1, keepdims=True)
    by_row = (r.pairs_col[rows_here, 0:1] * (own_share - own_partner)).astype(LOW)
    by_column = (weight_row * (jnp.exp(own_score - log_row) - own_partner)).astype(LOW)
    unit_grad = SCORE_SCALE * (dot(by_row, units) + dot(by_column, units))
    along = jnp.sum(unit * unit_grad, axis=-1, keepdims=True)
    summary_grad = (unit_grad - unit * along) / magnitude

    residual_grad, grad_g2, grad_s2 = norm_back_parts(
        summary_grad, normed_two, inverse_two, vector(6)
    )
    down_grad = residual_grad.astype(LOW)
    r.downs[here] = down_grad
    steps_d[0]()
    r.hidden_cls[...] = down_grad

    def up_back(part):
        at = pl.ds(pl.multiple_of(part * BLOCK, BLOCK), BLOCK)
        act_grad = dot_turned(r.hidden_cls[...], r.wc[at, :])
        r.active_cls[:, at] = (act_grad * r.slope_cls[:, at]).astype(LOW)

    every(0, WIDE // BLOCK, up_back)
    steps_d[1]()

    def hidden_back(part):
        at = pl.ds(pl.multiple_of(part * BLOCK, BLOCK), BLOCK)
        r.wide_cls[:, at] = dot_turned(r.active_cls[...], r.wb[at, :])

    every(0, WIDTH // BLOCK, hidden_back)
    hidden_grad = r.wide_cls[:, 0:WIDTH] + residual_grad
    first_grad, grad_g1, grad_s1 = norm_back_parts(
        hidden_grad, r.normed_one[...], inverse_one, vector(3)
    )
    attend_grad = first_grad.astype(LOW)
    context_grad = dot_turned(attend_grad, r.wa[:, 3 * WIDTH : 4 * WIDTH]).astype(LOW)
    attend_here = r.attends.at[here]
    attend_here[:, 0:WIDTH] = attend_grad
    attend_here[:, WIDTH : 2 * WIDTH] = context_grad
    steps_a[0]()
    steps_d[2]()
    context_tall = spread(context_grad)
    probs = r.probs[...]
    prob_grad = dot_turned(context_tall, r.qkv[:, values])
    inner = jnp.sum(probs * prob_grad, axis=1, keepdims=True)
    score_grad = (probs * (prob_grad - inner)).astype(LOW)
    steps_a[1]()
    r.mail_three[...] = pack_coefs(score_grad)
    post(r.mail_three, r.got_three, 3)
    query_grad = (fold(dot(score_grad, r.qkv[:, keys])) * scale).astype(LOW)
    probs_total = jnp.sum(probs_low.astype(FULL), axis=1, keepdims=True)
    grad_bvalue = jnp.sum(probs_total * context_tall.astype(FULL), axis=0, keepdims=True)
    grad_bquery = jnp.sum(query_grad.astype(FULL), axis=0, keepdims=True)
    r.queries[here] = query_grad
    own_sums = jnp.concatenate(
        [jnp.zeros((2 * depth, WIDTH), FULL)]
        + [grad_bquery, grad_bvalue, grad_g1, grad_s1, grad_g2, grad_s2]
        + [jnp.zeros((128 - 2 * depth - 6, WIDTH), FULL)],
        axis=0,
    )
    r.own_sums[...] = jnp.transpose(own_sums)
    steps_q[0]()
    steps_a[2]()
    r.tall[0:PAIR_ROWS, :] = (dot(score_grad, r.embedded[...]) * scale).astype(LOW)

    def with_sums(at, both):
        return both + r.own_sums[pl.ds(pl.multiple_of(at * depth, 16), depth), :]

    every(0, CHIPS // 2, pack_tall(r.mail_two, 0, with_sums))
    steps_q[1]()
    post(r.mail_two, r.got_two, 2)

    def all_rows(buffer, start, width=WIDTH):
        return buffer[:, :, :, :, start : start + width].reshape(SLOT_ROWS, width)

    def from_sent(group):
        lanes = iota((SLOT_ROWS, SLOT_ROWS), 1).astype(FULL)
        return (r.found[group, :, 1:2] == lanes).astype(LOW)

    def widened(coefs, group, start):
        lanes = iota((128, BLOCK), 0) == over(iota((128, BLOCK), 1) + start, HEAD) + group * PAD
        return dot(coefs, lanes.astype(LOW))

    half_wide = WIDE // 2

    def slope_tile(part):
        at = pl.ds(pl.multiple_of(core * half_wide + part * BLOCK, BLOCK), BLOCK)
        up_pre = dot(all_rows(r.early, 0), r.wb[:, at]) + r.up_bias[0:1, at]
        _, slope = gelu_parts(up_pre)
        r.slopes[:, pl.ds(pl.multiple_of(part * BLOCK, BLOCK), BLOCK)] = slope.astype(LOW)

    def slot_queries(group):
        sents = from_sent(group)
        for start in range(0, WIDTH, BLOCK):
            rows = dot(sents, all_rows(r.early, WIDTH + start, BLOCK))
            r.slot_query[group, :, start : start + BLOCK] = rows.astype(LOW)

    def activate():
        at = pl.ds(pl.multiple_of(chip // 2 * 2 * deep, 128), 2 * deep)
        up_pre = dot(all_rows(r.early, 0), r.wb[:, at]) + r.up_bias[0:1, at]
        r.active_turned[...] = jnp.transpose(gelu(up_pre)).astype(LOW)
        r.hidden_turned[...] = jnp.transpose(all_rows(r.early, 0))

    steps_e[5]()

    def open_step(tile):
        open_tile(tile)
        pl.when(tile == 0)(steps_d[3])
        pl.when(tile == 2)(steps_a[3])

    def feed_step(part):
        feed_up(part)
        for index, step in enumerate([steps_q[2], steps_d[4], steps_a[4], steps_q[3], steps_d[5]]):
            pl.when(part == index)(step)
        pl.when(part == 6)(steps_a[5])
        pl.when(part == 7)(steps_q[4])

    every(0, TOKENS // BLOCK, open_step)
    every(0, WIDE // BLOCK, feed_step)
    every(0, WIDTH // BLOCK, feed_rest)
    every(0, WIDTH // BLOCK, feed_down)
    every(0, TOKENS // BLOCK, close_tile)
    every(0, GROUPS, slot_queries)
    every(0, 6, slope_tile)
    activate()

    all_but_one(r.got_one, 1).wait_recv()
    def slot_values(group):
        sents = from_sent(group)
        got_probs = r.got_one[:, 64:80, :].reshape(SLOT_ROWS, 128)
        for start in range(0, WIDTH, BLOCK):
            rows = dot(sents, all_rows(r.attends, WIDTH + start, BLOCK))
            rows = widened(got_probs, group, start) * rows
            r.replies[group, :, start : start + BLOCK] = rows.astype(LOW)

    every(0, GROUPS, slot_values)

    def head_products(got, first_row, right, start, target):
        def one_head(head):
            lane = core * (WIDTH // 2) + lax.div(head, 2) * 128
            pair_rows = right[:, :, :, :, pl.ds(pl.multiple_of(start + lane, 128), 128)]
            row = pl.ds(pl.multiple_of(first_row + lax.rem(head, 3) * PAD, 16), PAD)
            block_rows = got[:, row, :].reshape(SLOT_ROWS, 128)
            r.product[...] = contract(block_rows, pair_rows.reshape(SLOT_ROWS, 128), 0, 0)
            part = r.product[pl.ds(pl.multiple_of(lax.div(head, 3) * depth, 16), depth), :]
            at = pl.ds(pl.multiple_of(lane, 128), 128)
            own_lanes = over(iota((depth, 128), 1), HEAD) == lax.rem(head, 2)
            target[:, at] = jnp.where(own_lanes, part, target[:, at])

        every(0, HEADS // 2, one_head)

    def half_of(ref, at_core):
        half = ref.shape[1] // 2
        return ref.at[:, pl.ds(pl.multiple_of(at_core * half, 128), half)]

    def half_copy(index, ref, at_core):
        part = half_of(ref, at_core)
        return remote(part, part, r.half_send.at[index], r.half_recv.at[index], 1 - core, chip)

    own_half = pl.ds(pl.multiple_of(core * (WIDTH // 2), 128), WIDTH // 2)
    r.g_wv[:, own_half] = jnp.zeros((depth, WIDTH // 2), FULL)
    r.g_wk[:, own_half] = jnp.zeros((depth, WIDTH // 2), FULL)
    head_products(r.got_one, PAD, r.attends, WIDTH, r.g_wv)
    half_copy(0, r.g_wv, core).start()

    downs = r.downs[...].reshape(SLOT_ROWS, WIDTH)
    attends = all_rows(r.attends, 0)

    def up_tile(part):
        at = pl.ds(pl.multiple_of(core * half_wide + part * BLOCK, BLOCK), BLOCK)
        slope = r.slopes[:, pl.ds(pl.multiple_of(part * BLOCK, BLOCK), BLOCK)].astype(FULL)
        up_all = (dot_turned(r.downs[...].reshape(SLOT_ROWS, WIDTH), r.wc[at, :]) * slope)
        up_all = up_all.astype(LOW)
        r.g_wup[0:depth, at] = dot(r.hidden_turned[mine, :], up_all)
        total = jnp.sum(up_all.astype(FULL), axis=0, keepdims=True)
        r.g_wup[depth : depth + 8, at] = jnp.broadcast_to(total, (8, BLOCK))

    every(0, half_wide // BLOCK, up_tile)
    half_copy(1, r.g_wup, core).start()
    r.g_wdown[...] = dot(r.active_turned[pl.ds(pl.multiple_of(chip % 2 * deep, 16), deep), :], downs)
    r.left_turned[...] = jnp.transpose(r.got_one[:, 0:PAD, :].reshape(SLOT_ROWS, 128))
    r.g_wo[...] = dot(r.left_turned[0:depth, :], attends)
    own_lanes = (iota((WIDTH, 128), 0) == chip * depth + iota((WIDTH, 128), 1)).astype(LOW)

    def own_part(rows, select):
        total = None
        for _ in range(3):
            part = rows.astype(LOW)
            rows = rows - part.astype(FULL)
            picked = dot(part, select)
            total = picked if total is None else total + picked
        return total

    for quarter in range(4):
        rows_of(quarter).wait_send()
    all_but_one(r.got_three, 3).wait_recv()

    def slot_grads(group):
        got_scores = r.got_three[...].reshape(SLOT_ROWS, 128)
        for start in range(0, WIDTH, BLOCK):
            lanes = slice(start, start + BLOCK)
            rows = r.slot_query[group, :, lanes].astype(FULL)
            rows = widened(got_scores, group, start) * rows * scale
            r.slot_query[group, :, lanes] = rows.astype(LOW)
        for start in range(0, WIDTH, BLOCK):
            row_grad = dot_turned(r.slot_query[group], r.wa[start : start + BLOCK, keys])
            row_grad = row_grad + dot_turned(r.replies[group], r.wa[start : start + BLOCK, values])
            r.rows[group, :, start : start + BLOCK] = row_grad.astype(LOW)

    every(0, GROUPS, slot_grads)
    steps_q[5]()
    query_grads = all_rows(r.queries, 0)
    extra = dot_turned(query_grads, r.wa[:, 0:WIDTH]) + attends.astype(FULL)
    r.extra[...] = extra.astype(LOW)
    r.g_wq[...] = dot(r.left_turned[depth : 2 * depth, :], query_grads)

    half_rows = VOCAB_ROWS // 2

    def table_copy(tile):
        at = pl.ds(pl.multiple_of(tile * half_rows, BLOCK), half_rows)
        return pltpu.make_async_copy(
            r.table_full.at[at], r.table_grad.at[at], r.table_sem.at[tile]
        )

    def table_tile(tile):
        at = pl.ds(pl.multiple_of(tile * half_rows, BLOCK), half_rows)
        for start in range(0, WIDTH, BLOCK):
            lanes = slice(start, start + BLOCK)
            slot_rows = r.rows[:, :, lanes].reshape(GROUPS * SLOT_ROWS, BLOCK)
            r.table_full[at, lanes] = dot(r.by_row[at, 0 : GROUPS * SLOT_ROWS], slot_rows) + dot(
                r.by_row[at, GROUPS * SLOT_ROWS :], r.extra[:, lanes]
            )
        table_copy(tile).start()

    every(0, 2, table_tile)
    all_but_one(r.got_two, 2).wait_recv()
    head_products(r.got_two, 0, r.early, WIDTH, r.g_wk)
    half_copy(2, r.g_wk, core).start()

    down_total = jnp.sum(downs.astype(FULL), axis=0, keepdims=True)
    attend_total = jnp.sum(attends.astype(FULL), axis=0, keepdims=True)
    sums = jnp.sum(r.got_two[...].astype(FULL), axis=0)
    sums = jnp.concatenate([sums, jnp.zeros((128 - 48, 128), FULL)], axis=0)
    stacked = jnp.concatenate([attend_total, down_total, jnp.zeros((6, WIDTH), FULL)], axis=0)
    r.g_small[8:16, 0:128] = own_part(stacked, own_lanes)
    r.g_small[0:8, 0:128] = jnp.transpose(sums)[2 * depth : 2 * depth + 8, :]
    r.g_small[0:16, 128:BLOCK] = jnp.zeros((PAD, BLOCK - 128), FULL)
    half_copy(1, r.g_wup, 1 - core).wait_recv()
    up_lanes = (iota((WIDE, BLOCK), 0) == chip * deep + iota((WIDE, BLOCK), 1)).astype(LOW)
    r.g_small[16:24, :] = own_part(r.g_wup[depth : depth + 8, :], up_lanes)

    half_copy(0, r.g_wv, 1 - core).wait_recv()
    half_copy(2, r.g_wk, 1 - core).wait_recv()
    for index, ref in enumerate([r.g_wv, r.g_wup, r.g_wk]):
        half_copy(index, ref, core).wait_send()

    for index, ref in enumerate([r.every_ids, r.got_one, r.got_two, r.got_three]):
        all_but_one(ref, index).wait_send()
    all_smalls().wait_send()
    for end in [drain_a, drain_b, drain_c, drain_u, drain_e, drain_d, drain_a2, drain_q]:
        end()
    every(0, TOKENS // BLOCK, lambda tile: layer_copy(tile).wait())
    every(0, 2, lambda tile: table_copy(tile).wait())


def layer(inputs):
    dma = pltpu.SemaphoreType.DMA
    vmem = pl.BlockSpec(memory_space=pltpu.VMEM)
    anywhere = pl.BlockSpec(memory_space=pl.ANY)
    depth, deep = WIDTH // CHIPS, WIDE // CHIPS

    def gathered(width):
        return pltpu.VMEM((CORES, PLANES, LINES, PAD, width), LOW)

    outputs = dict(
        layer_out=((TOKENS, WIDTH), LOW),
        table_grad=((VOCAB_ROWS, WIDTH), FULL),
        g_wq=((depth, WIDTH), FULL),
        g_wk=((depth, WIDTH), FULL),
        g_wv=((depth, WIDTH), FULL),
        g_wo=((depth, WIDTH), FULL),
        g_wup=((depth + 8, WIDE), FULL),
        g_wdown=((deep, WIDTH), FULL),
        g_small=((24, BLOCK), FULL),
        loss=((1, 1), FULL),
    )
    scratch = dict(
        ids=pltpu.VMEM((8, 128), jnp.int32),
        every_ids=pltpu.VMEM((DEVICES, 8, 128), jnp.int32),
        rank=pltpu.VMEM((DEVICES, TOKENS), FULL),
        code=pltpu.VMEM((DEVICES, TOKENS), FULL),
        found=pltpu.VMEM((GROUPS + 1, SLOT_ROWS, 2), FULL),
        block_bias=pltpu.VMEM((2 * BLOCK, BLOCK // 2), FULL),
        valid_bias=pltpu.VMEM((8, TOKENS), FULL),
        slot_col=pltpu.VMEM((TOKENS, 1), FULL),
        slot_line=pltpu.VMEM((8, TOKENS), FULL),
        valid_col=pltpu.VMEM((TOKENS, 1), FULL),
        valid_line=pltpu.VMEM((8, TOKENS), FULL),
        pairs=pltpu.VMEM((8, SLOT_ROWS), FULL),
        pairs_col=pltpu.VMEM((SLOT_ROWS, 128), FULL),
        vectors=pltpu.VMEM((PAD, WIDTH), FULL),
        up_bias=pltpu.VMEM((8, WIDE), FULL),
        qkv_bias=pltpu.VMEM((8, 3 * WIDTH), FULL),
        smalls=pltpu.VMEM((PAD, CHIPS * 128), LOW),
        wa=pltpu.VMEM((WIDTH, 4 * WIDTH), LOW),
        wb=pltpu.VMEM((WIDTH, WIDE), LOW),
        wc=pltpu.VMEM((WIDE, WIDTH), LOW),
        chosen=pltpu.VMEM((GROUPS, SLOT_ROWS, VOCAB_ROWS), LOW),
        by_row=pltpu.VMEM((VOCAB_ROWS, (GROUPS + 1) * SLOT_ROWS), LOW),
        rows=pltpu.VMEM((GROUPS, SLOT_ROWS, WIDTH), LOW),
        replies=pltpu.VMEM((GROUPS, SLOT_ROWS, WIDTH), LOW),
        slot_query=pltpu.VMEM((GROUPS, SLOT_ROWS, WIDTH), LOW),
        extra=pltpu.VMEM((SLOT_ROWS, WIDTH), LOW),
        hidden_cls=pltpu.VMEM((PAD, WIDTH), LOW),
        active_cls=pltpu.VMEM((PAD, WIDE), LOW),
        slope_cls=pltpu.VMEM((PAD, WIDE), FULL),
        wide_cls=pltpu.VMEM((PAD, WIDTH), FULL),
        tall=pltpu.VMEM((PAIR_ROWS + 2 * PAD, WIDTH), LOW),
        own_sums=pltpu.VMEM((WIDTH, 128), FULL),
        product=pltpu.VMEM((128, 128), FULL),
        embedded=pltpu.VMEM((TOKENS, WIDTH), LOW),
        qkv=pltpu.VMEM((TOKENS, 3 * WIDTH), LOW),
        context=pltpu.VMEM((TOKENS, WIDTH), LOW),
        table_full=pltpu.VMEM((VOCAB_ROWS, WIDTH), FULL),
        probs=pltpu.VMEM((PAIR_ROWS, TOKENS), FULL),
        normed_one=pltpu.VMEM((PAD, WIDTH), FULL),
        units=gathered(WIDTH),
        early=gathered(2 * WIDTH),
        downs=gathered(WIDTH),
        attends=gathered(2 * WIDTH),
        queries=gathered(WIDTH),
        slopes=pltpu.VMEM((SLOT_ROWS, WIDE // 2), LOW),
        hidden_turned=pltpu.VMEM((WIDTH, SLOT_ROWS), LOW),
        active_turned=pltpu.VMEM((2 * deep, SLOT_ROWS), LOW),
        left_turned=pltpu.VMEM((128, SLOT_ROWS), LOW),
        mail_one=pltpu.VMEM((DEVICES, 80, 128), LOW),
        got_one=pltpu.VMEM((DEVICES, 80, 128), LOW),
        mail_two=pltpu.VMEM((DEVICES, 48, 128), LOW),
        got_two=pltpu.VMEM((DEVICES, 48, 128), LOW),
        mail_three=pltpu.VMEM((DEVICES, PAD, 128), LOW),
        got_three=pltpu.VMEM((DEVICES, PAD, 128), LOW),
        rows_send=dma((4,)),
        rows_recv=dma((4,)),
        one_send=dma((4,)),
        one_recv=dma((4,)),
        small_send=dma((1,)),
        small_recv=dma((1,)),
        weight_send=dma((3, 33)),
        weight_recv=dma((3, 33)),
        gather_send=dma((5, 13)),
        gather_recv=dma((5, 13)),
        half_send=dma((3,)),
        half_recv=dma((3,)),
        out_sem=dma((TOKENS // BLOCK,)),
        table_sem=dma((2,)),
    )
    names = INPUTS + OUTPUTS + list(scratch)
    return pl.pallas_call(
        partial(layer_kernel, names),
        out_shape=tuple(jax.ShapeDtypeStruct(*outputs[name]) for name in OUTPUTS),
        in_specs=[vmem] * len(INPUTS),
        out_specs=(anywhere, anywhere) + (vmem,) * (len(OUTPUTS) - 2),
        scratch_shapes=list(scratch.values()),
        compiler_params=pltpu.CompilerParams(
            collective_id=0, has_side_effects=True, vmem_limit_bytes=VMEM_LIMIT
        ),
        name="layer",
    )(*inputs)


def finish_kernel(count, *refs):
    large, (small, loss), outs = refs[:count], refs[count : count + 2], refs[count + 2 : -1]
    sems = refs[-1]
    copies = []
    for index, (source, target) in enumerate(zip(large, outs)):
        part = source if source.shape == target.shape else source.at[: target.shape[0]]
        copies.append(pltpu.make_async_copy(part, target, sems.at[index]))
        copies[-1].start()
    for row, target in zip([0, 1, 8, 2, 3, 16, 9, 4, 5], outs[count : count + 9]):
        size = target.shape[0]
        target[...] = small[row : row + 1, 0:size].reshape(size)
    outs[-1][...] = loss[...].reshape(1)
    for one in copies:
        one.wait()


def finish(results):
    vmem = pl.BlockSpec(memory_space=pltpu.VMEM)
    anywhere = pl.BlockSpec(memory_space=pl.ANY)
    depth, deep = WIDTH // CHIPS, WIDE // CHIPS
    count = len(results) - 2
    shapes = [(one.shape, one.dtype) for one in results[:count]]
    shapes[6] = ((depth, WIDE), FULL)
    shapes += [((depth,), FULL)] * 5 + [((deep,), FULL)] + [((depth,), FULL)] * 3
    shapes.append(((1,), FULL))
    return pl.pallas_call(
        partial(finish_kernel, count),
        out_shape=tuple(jax.ShapeDtypeStruct(*one) for one in shapes),
        in_specs=[vmem] * (count + 2),
        out_specs=(anywhere,) * count + (vmem,) * 10,
        scratch_shapes=[pltpu.SemaphoreType.DMA((count,))],
        name="finish",
    )(*results)


def block_body(
    table,
    token_ids,
    sent_lengths,
    pair_slot,
    pair_lang,
    *parameters,
):
    results = finish(layer((table, token_ids, sent_lengths, pair_slot, pair_lang) + parameters))
    layer_out, table_grad, g_wq, g_wk, g_wv, g_wo, g_wup, g_wdown = results[:8]
    g_bq, g_bv, g_bo, g_g1, g_s1, g_bup, g_bdown, g_g2, g_s2, loss = results[8:]
    return (
        layer_out.reshape(token_ids.shape + (WIDTH,)),
        loss.reshape(()),
        table_grad,
        g_wq,
        g_bq,
        g_wk,
        g_wv,
        g_bv,
        g_wo,
        g_bo,
        g_g1,
        g_s1,
        g_wup,
        g_bup,
        g_wdown,
        g_bdown,
        g_g2,
        g_s2,
    )


def solution(mesh):
    in_specs = (
        P(("dp", "fsdp"), None),
        P(("dp", "fsdp"), None),
        P(("dp", "fsdp")),
        P(),
        P(),
        P("fsdp", None),
        P("fsdp"),
        P("fsdp", None),
        P("fsdp", None),
        P("fsdp"),
        P("fsdp", None),
        P("fsdp"),
        P("fsdp"),
        P("fsdp"),
        P("fsdp", None),
        P("fsdp"),
        P("fsdp", None),
        P("fsdp"),
        P("fsdp"),
        P("fsdp"),
    )
    out_specs = (
        P(("dp", "fsdp"), None, None),
        P(),
        P(("dp", "fsdp"), None),
        P("fsdp", None),
        P("fsdp"),
        P("fsdp", None),
        P("fsdp", None),
        P("fsdp"),
        P("fsdp", None),
        P("fsdp"),
        P("fsdp"),
        P("fsdp"),
        P("fsdp", None),
        P("fsdp"),
        P("fsdp", None),
        P("fsdp"),
        P("fsdp"),
        P("fsdp"),
    )
    sizes = dict(mesh.shape)
    body = general_body
    if sizes["dp"] == CORES and sizes["fsdp"] == CHIPS:
        body = block_body
    return jax.shard_map(body, mesh=mesh, in_specs=in_specs, out_specs=out_specs, check_vma=False)
```

```python
from functools import partial
from types import SimpleNamespace

import jax
import jax.numpy as jnp
from jax import lax
from jax.experimental import pallas as pl
from jax.experimental.pallas import tpu as pltpu
from jax.sharding import PartitionSpec as P

HEADS = 12
HEAD = 64
LANGS = 109


EPSILON = 1e-06
SCORE_SCALE = 50.0
MARGIN_WIDTH = 0.3
MASK_FLOOR = -1000000000.0


def contract(left_side, right_side, left_dim, right_dim):
    return lax.dot_general(
        left_side,
        right_side,
        (((left_dim,), (right_dim,)), ((), ())),
        preferred_element_type=jnp.float32,
    )


def norm_rows(inputs, ln_gain, ln_shift):
    row_mean = jnp.mean(inputs, axis=-1, keepdims=True)
    centered = inputs - row_mean
    variance = jnp.mean(centered * centered, axis=-1, keepdims=True)
    inverse = lax.rsqrt(variance + EPSILON)
    normed = centered * inverse
    return (normed * ln_gain + ln_shift, normed, inverse)


def norm_back(grad_output, normed, inverse, ln_gain):
    grad_normed = grad_output * ln_gain
    first_term = jnp.mean(grad_normed, axis=-1, keepdims=True)
    second_term = jnp.mean(grad_normed * normed, axis=-1, keepdims=True)
    grad_input = inverse * (grad_normed - first_term - normed * second_term)
    return (grad_input, jnp.sum(grad_output * normed, axis=0), jnp.sum(grad_output, axis=0))


def general_body(
    table,
    token_ids,
    sent_lengths,
    pair_slot,
    pair_lang,
    w_query,
    b_query,
    w_key,
    w_value,
    b_value,
    w_out,
    b_out,
    ln1_gain,
    ln1_bias,
    w_up,
    b_up,
    w_down,
    b_down,
    ln2_gain,
    ln2_bias,
):
    sentences, length = token_ids.shape
    tokens = sentences * length
    vocab_rows, model_width = table.shape
    owners = lax.axis_size(("dp", "fsdp"))
    dp_count = lax.axis_size("dp")
    fsdp_count = lax.axis_size("fsdp")
    capacity = max(2, 2 * tokens // owners)
    device = lax.axis_index(("dp", "fsdp"))
    score_factor = HEAD ** (-0.5)
    flat_ids = token_ids.reshape(tokens)
    owner_of = flat_ids // vocab_rows
    member = (owner_of[:, None] == jnp.arange(owners, dtype=jnp.int32)[None, :]).astype(jnp.int32)
    owner_rank = jnp.sum(jnp.cumsum(member, axis=0) * member, axis=1) - 1
    slot_of = owner_of * capacity + owner_rank
    requests = jnp.full((owners * capacity,), -1, jnp.int32).at[slot_of].set(flat_ids)
    received = lax.all_to_all(
        lax.all_to_all(
            requests.reshape(dp_count, fsdp_count, capacity),
            "dp",
            split_axis=0,
            concat_axis=0,
            tiled=True,
        ),
        "fsdp",
        split_axis=1,
        concat_axis=1,
        tiled=True,
    )
    present = received >= 0
    local_rows = jnp.where(present, received - device * vocab_rows, 0)
    found_rows = jnp.where(present[..., None], table[local_rows], jnp.zeros((), table.dtype))
    replies = lax.all_to_all(
        lax.all_to_all(found_rows, "dp", split_axis=0, concat_axis=0, tiled=True),
        "fsdp",
        split_axis=1,
        concat_axis=1,
        tiled=True,
    )
    embedded = replies.reshape(owners * capacity, model_width)[slot_of]
    gathered = (
        lax.all_gather(w_query, "fsdp", axis=0, tiled=True),
        lax.all_gather(b_query, "fsdp", axis=0, tiled=True),
        lax.all_gather(w_key, "fsdp", axis=0, tiled=True),
        lax.all_gather(w_value, "fsdp", axis=0, tiled=True),
        lax.all_gather(b_value, "fsdp", axis=0, tiled=True),
        lax.all_gather(w_out, "fsdp", axis=0, tiled=True),
        lax.all_gather(b_out, "fsdp", axis=0, tiled=True),
        lax.all_gather(ln1_gain, "fsdp", axis=0, tiled=True),
        lax.all_gather(ln1_bias, "fsdp", axis=0, tiled=True),
        lax.all_gather(w_up, "fsdp", axis=0, tiled=True),
        lax.all_gather(b_up, "fsdp", axis=0, tiled=True),
        lax.all_gather(w_down, "fsdp", axis=0, tiled=True),
        lax.all_gather(b_down, "fsdp", axis=0, tiled=True),
        lax.all_gather(ln2_gain, "fsdp", axis=0, tiled=True),
        lax.all_gather(ln2_bias, "fsdp", axis=0, tiled=True),
    )
    (
        full_wq,
        full_bq,
        full_wk,
        full_wv,
        full_bv,
        full_wo,
        full_bo,
        full_g1,
        full_s1,
        full_wup,
        full_bup,
        full_wdown,
        full_bdown,
        full_g2,
        full_s2,
    ) = gathered
    valid_mask = jnp.arange(length, dtype=jnp.int32)[None, :] < sent_lengths[:, None]
    head_shape = (sentences, length, HEADS, HEAD)
    queries = (jnp.dot(embedded, full_wq, preferred_element_type=jnp.float32) + full_bq).astype(
        jnp.bfloat16
    )
    key_heads = (
        jnp.dot(embedded, full_wk, preferred_element_type=jnp.float32)
        .astype(jnp.bfloat16)
        .reshape(head_shape)
    )
    value_heads = (
        (jnp.dot(embedded, full_wv, preferred_element_type=jnp.float32) + full_bv)
        .astype(jnp.bfloat16)
        .reshape(head_shape)
    )
    query_heads = queries.reshape(head_shape)
    scores = (
        jnp.einsum("bqhd,bkhd->bhqk", query_heads, key_heads, preferred_element_type=jnp.float32)
        * score_factor
    )
    scores = jnp.where(valid_mask[:, None, None, :], scores, MASK_FLOOR)
    row_peak = jnp.max(scores, axis=-1, keepdims=True)
    shifted = jnp.exp(scores - row_peak)
    totals = jnp.sum(shifted, axis=-1, keepdims=True)
    attn_probs = (shifted / totals).astype(jnp.bfloat16)
    context = jnp.einsum(
        "bhqk,bkhd->bqhd", attn_probs, value_heads, preferred_element_type=jnp.float32
    )
    context = context.reshape(tokens, model_width).astype(jnp.bfloat16)
    attended = jnp.dot(context, full_wo, preferred_element_type=jnp.float32) + full_bo
    hidden, normed_one, inverse_one = norm_rows(
        embedded.astype(jnp.float32) + attended, full_g1, full_s1
    )
    hidden_low = hidden.astype(jnp.bfloat16)
    up_pre = jnp.dot(hidden_low, full_wup, preferred_element_type=jnp.float32) + full_bup
    activated = jax.nn.gelu(up_pre, approximate=False).astype(jnp.bfloat16)
    down_pre = jnp.dot(activated, full_wdown, preferred_element_type=jnp.float32) + full_bdown
    normed_out, normed_two, inverse_two = norm_rows(hidden + down_pre, full_g2, full_s2)
    layer_out = jnp.where(valid_mask.reshape(tokens)[:, None], normed_out, 0.0).astype(jnp.bfloat16)
    layer_out = layer_out.reshape(sentences, length, model_width)

    def first_rows(matrix):
        return matrix.reshape(sentences, length, matrix.shape[-1])[:, 0]

    summary = first_rows(normed_out)
    magnitude = jnp.sqrt(jnp.sum(summary * summary, axis=-1, keepdims=True) + EPSILON)
    unit_vector = summary / magnitude
    unit_low = unit_vector.astype(jnp.bfloat16)
    every_unit = lax.all_gather(unit_low, ("dp", "fsdp"), axis=0, tiled=True)
    every_side = pair_slot % 2
    every_pair = pair_slot // 2
    my_slots = lax.dynamic_slice_in_dim(pair_slot, device * sentences, sentences)
    my_side = my_slots % 2
    my_pair = my_slots // 2
    lang_onehot = (pair_lang[:, None] == jnp.arange(LANGS, dtype=jnp.int32)[None, :]).astype(
        jnp.float32
    )
    per_lang = jnp.sum(lang_onehot, axis=0)
    per_pair = 1.0 / (2.0 * LANGS * jnp.sum(lang_onehot * per_lang[None, :], axis=1))
    my_weight = jnp.take(per_pair, my_pair)
    opposite = my_side[:, None] != every_side[None, :]
    partner = opposite & (my_pair[:, None] == every_pair[None, :])
    raw_scores = SCORE_SCALE * contract(unit_low, every_unit, 1, 1)
    pair_scores = jnp.where(partner, raw_scores - SCORE_SCALE * MARGIN_WIDTH, raw_scores)
    pair_scores = jnp.where(opposite, pair_scores, MASK_FLOOR)
    pair_peak = jnp.max(pair_scores, axis=1, keepdims=True)
    pair_exp = jnp.exp(pair_scores - pair_peak)
    pair_total = jnp.sum(pair_exp, axis=1, keepdims=True)
    log_total = pair_peak[:, 0] + jnp.log(pair_total[:, 0])
    picked = jnp.sum(jnp.where(partner, pair_scores, 0.0), axis=1)
    loss_value = lax.psum(jnp.sum(my_weight * (log_total - picked)), ("dp", "fsdp"))
    coefficients = (
        my_weight[:, None] * (pair_exp / pair_total - partner.astype(jnp.float32))
    ).astype(jnp.bfloat16)
    unit_grad = SCORE_SCALE * contract(coefficients, every_unit, 1, 0)
    column_terms = SCORE_SCALE * contract(coefficients, unit_low, 0, 0)
    unit_grad = unit_grad + lax.psum_scatter(
        column_terms, ("dp", "fsdp"), scatter_dimension=0, tiled=True
    )
    along = jnp.sum(unit_vector * unit_grad, axis=-1, keepdims=True)
    summary_grad = (unit_grad - unit_vector * along) / magnitude
    again_weights = (
        lax.all_gather(w_query, "fsdp", axis=0, tiled=True),
        lax.all_gather(w_key, "fsdp", axis=0, tiled=True),
        lax.all_gather(w_value, "fsdp", axis=0, tiled=True),
        lax.all_gather(w_out, "fsdp", axis=0, tiled=True),
        lax.all_gather(ln1_gain, "fsdp", axis=0, tiled=True),
        lax.all_gather(w_up, "fsdp", axis=0, tiled=True),
        lax.all_gather(w_down, "fsdp", axis=0, tiled=True),
        lax.all_gather(ln2_gain, "fsdp", axis=0, tiled=True),
    )
    again_wq, again_wk, again_wv, again_wo, again_g1, again_wup, again_wdown, again_g2 = (
        again_weights
    )
    residual_grad, grad_g2, grad_s2 = norm_back(
        summary_grad, first_rows(normed_two), first_rows(inverse_two), again_g2
    )
    down_grad = residual_grad.astype(jnp.bfloat16)
    activated_cls = first_rows(activated)
    act_grad = contract(down_grad, again_wdown, 1, 1)
    gelu_value, gelu_pull = jax.vjp(partial(jax.nn.gelu, approximate=False), first_rows(up_pre))
    up_grad = gelu_pull(act_grad)[0].astype(jnp.bfloat16)
    hidden_cls = first_rows(hidden_low)
    hidden_grad = contract(up_grad, again_wup, 1, 1) + residual_grad
    first_grad, grad_g1, grad_s1 = norm_back(
        hidden_grad, first_rows(normed_one), first_rows(inverse_one), again_g1
    )
    attend_grad = first_grad.astype(jnp.bfloat16)
    context_cls = first_rows(context)
    context_grad = (
        contract(attend_grad, again_wo, 1, 1).astype(jnp.bfloat16).reshape(sentences, HEADS, HEAD)
    )
    query_cls = query_heads[:, 0]
    cls_scores = (
        jnp.einsum("bhd,bkhd->bhk", query_cls, key_heads, preferred_element_type=jnp.float32)
        * score_factor
    )
    cls_scores = jnp.where(valid_mask[:, None, :], cls_scores, MASK_FLOOR)
    cls_probs = jnp.exp(cls_scores - row_peak[:, :, 0]) / totals[:, :, 0]
    prob_grad = jnp.einsum(
        "bhd,bkhd->bhk", context_grad, value_heads, preferred_element_type=jnp.float32
    )
    score_grad = (
        cls_probs * (prob_grad - jnp.sum(cls_probs * prob_grad, axis=-1, keepdims=True))
    ).astype(jnp.bfloat16)
    query_grad = (
        (
            jnp.einsum("bhk,bkhd->bhd", score_grad, key_heads, preferred_element_type=jnp.float32)
            * score_factor
        )
        .astype(jnp.bfloat16)
        .reshape(sentences, model_width)
    )
    key_grad = (
        (
            jnp.einsum("bhk,bhd->bkhd", score_grad, query_cls, preferred_element_type=jnp.float32)
            * score_factor
        )
        .astype(jnp.bfloat16)
        .reshape(tokens, model_width)
    )
    value_grad = (
        jnp.einsum(
            "bhk,bhd->bkhd",
            cls_probs.astype(jnp.bfloat16),
            context_grad,
            preferred_element_type=jnp.float32,
        )
        .astype(jnp.bfloat16)
        .reshape(tokens, model_width)
    )
    embedded_cls = first_rows(embedded)
    grad_wkey = contract(embedded, key_grad, 0, 0)
    grad_wvalue = contract(embedded, value_grad, 0, 0)
    grad_bvalue = jnp.sum(value_grad, axis=0, dtype=jnp.float32)
    row_grads = contract(key_grad, again_wk, 1, 1) + contract(value_grad, again_wv, 1, 1)
    summary_extra = contract(query_grad, again_wq, 1, 1) + first_grad
    row_grads = (
        row_grads.reshape(sentences, length, model_width)
        .at[:, 0]
        .add(summary_extra)
        .reshape(tokens, model_width)
    )
    outgoing = jnp.zeros((owners * capacity, model_width), jnp.float32).at[slot_of].set(row_grads)
    incoming = lax.all_to_all(
        lax.all_to_all(
            outgoing.reshape(dp_count, fsdp_count, capacity, model_width).astype(jnp.bfloat16),
            "dp",
            split_axis=0,
            concat_axis=0,
            tiled=True,
        ),
        "fsdp",
        split_axis=1,
        concat_axis=1,
        tiled=True,
    ).astype(jnp.float32)
    incoming = jnp.where(
        present.reshape(owners * capacity)[:, None],
        incoming.reshape(owners * capacity, model_width),
        0.0,
    )
    table_grad = (
        jnp.zeros((vocab_rows, model_width), jnp.float32)
        .at[local_rows.reshape(owners * capacity)]
        .add(incoming)
    )
    grad_wquery = contract(embedded_cls, query_grad, 0, 0)
    grad_bquery = jnp.sum(query_grad, axis=0, dtype=jnp.float32)
    grad_wout = contract(context_cls, attend_grad, 0, 0)
    grad_bout = jnp.sum(attend_grad, axis=0, dtype=jnp.float32)
    grad_wup = contract(hidden_cls, up_grad, 0, 0)
    grad_bup = jnp.sum(up_grad, axis=0, dtype=jnp.float32)
    grad_wdown = contract(activated_cls, down_grad, 0, 0)
    grad_bdown = jnp.sum(down_grad, axis=0, dtype=jnp.float32)
    owned_grads = (
        lax.psum_scatter(
            grad_wquery.astype(jnp.bfloat16), "fsdp", scatter_dimension=0, tiled=True
        ).astype(jnp.float32),
        lax.psum_scatter(
            grad_bquery.astype(jnp.bfloat16), "fsdp", scatter_dimension=0, tiled=True
        ).astype(jnp.float32),
        lax.psum_scatter(
            grad_wkey.astype(jnp.bfloat16), "fsdp", scatter_dimension=0, tiled=True
        ).astype(jnp.float32),
        lax.psum_scatter(
            grad_wvalue.astype(jnp.bfloat16), "fsdp", scatter_dimension=0, tiled=True
        ).astype(jnp.float32),
        lax.psum_scatter(
            grad_bvalue.astype(jnp.bfloat16), "fsdp", scatter_dimension=0, tiled=True
        ).astype(jnp.float32),
        lax.psum_scatter(
            grad_wout.astype(jnp.bfloat16), "fsdp", scatter_dimension=0, tiled=True
        ).astype(jnp.float32),
        lax.psum_scatter(
            grad_bout.astype(jnp.bfloat16), "fsdp", scatter_dimension=0, tiled=True
        ).astype(jnp.float32),
        lax.psum_scatter(
            grad_g1.astype(jnp.bfloat16), "fsdp", scatter_dimension=0, tiled=True
        ).astype(jnp.float32),
        lax.psum_scatter(
            grad_s1.astype(jnp.bfloat16), "fsdp", scatter_dimension=0, tiled=True
        ).astype(jnp.float32),
        lax.psum_scatter(
            grad_wup.astype(jnp.bfloat16), "fsdp", scatter_dimension=0, tiled=True
        ).astype(jnp.float32),
        lax.psum_scatter(
            grad_bup.astype(jnp.bfloat16), "fsdp", scatter_dimension=0, tiled=True
        ).astype(jnp.float32),
        lax.psum_scatter(
            grad_wdown.astype(jnp.bfloat16), "fsdp", scatter_dimension=0, tiled=True
        ).astype(jnp.float32),
        lax.psum_scatter(
            grad_bdown.astype(jnp.bfloat16), "fsdp", scatter_dimension=0, tiled=True
        ).astype(jnp.float32),
        lax.psum_scatter(
            grad_g2.astype(jnp.bfloat16), "fsdp", scatter_dimension=0, tiled=True
        ).astype(jnp.float32),
        lax.psum_scatter(
            grad_s2.astype(jnp.bfloat16), "fsdp", scatter_dimension=0, tiled=True
        ).astype(jnp.float32),
    )
    summed = (
        lax.psum(owned_grads[0].astype(jnp.bfloat16), "dp").astype(jnp.float32),
        lax.psum(owned_grads[1].astype(jnp.bfloat16), "dp").astype(jnp.float32),
        lax.psum(owned_grads[2].astype(jnp.bfloat16), "dp").astype(jnp.float32),
        lax.psum(owned_grads[3].astype(jnp.bfloat16), "dp").astype(jnp.float32),
        lax.psum(owned_grads[4].astype(jnp.bfloat16), "dp").astype(jnp.float32),
        lax.psum(owned_grads[5].astype(jnp.bfloat16), "dp").astype(jnp.float32),
        lax.psum(owned_grads[6].astype(jnp.bfloat16), "dp").astype(jnp.float32),
        lax.psum(owned_grads[7].astype(jnp.bfloat16), "dp").astype(jnp.float32),
        lax.psum(owned_grads[8].astype(jnp.bfloat16), "dp").astype(jnp.float32),
        lax.psum(owned_grads[9].astype(jnp.bfloat16), "dp").astype(jnp.float32),
        lax.psum(owned_grads[10].astype(jnp.bfloat16), "dp").astype(jnp.float32),
        lax.psum(owned_grads[11].astype(jnp.bfloat16), "dp").astype(jnp.float32),
        lax.psum(owned_grads[12].astype(jnp.bfloat16), "dp").astype(jnp.float32),
        lax.psum(owned_grads[13].astype(jnp.bfloat16), "dp").astype(jnp.float32),
        lax.psum(owned_grads[14].astype(jnp.bfloat16), "dp").astype(jnp.float32),
    )
    return (
        layer_out,
        loss_value,
        table_grad,
        summed[0],
        summed[1],
        summed[2],
        summed[3],
        summed[4],
        summed[5],
        summed[6],
        summed[7],
        summed[8],
        summed[9],
        summed[10],
        summed[11],
        summed[12],
        summed[13],
        summed[14],
    )


CORES = 2
PLANES = 4
LINES = 4
CHIPS = PLANES * LINES
DEVICES = CORES * CHIPS
CAPACITY = 48
GROUPS = 3
PAD = 16
TOKENS = 768
WIDTH = 768
WIDE = 3072
VOCAB_ROWS = 1024
PAIR_ROWS = HEADS * PAD
SLOT_ROWS = DEVICES * PAD
LONG = 64
BLOCK = 256
MESH = pl.DeviceIdType.MESH
LOW = jnp.bfloat16
FULL = jnp.float32
VMEM_LIMIT = 62 * 1024 * 1024

INPUTS = ["table", "token_ids", "lens", "slots", "langs"]
INPUTS += ["wq", "bq", "wk", "wv", "bv", "wo", "bo", "g1", "s1", "wup", "bup", "wdown", "bdown"]
INPUTS += ["g2", "s2"]
OUTPUTS = ["layer_out", "table_grad", "g_wq", "g_wk", "g_wv", "g_wo", "g_wup", "g_wdown"]
OUTPUTS += ["g_small", "loss"]


def place():
    core = lax.axis_index("dp")
    chip = lax.axis_index("fsdp")
    along_x = chip + 1 - 2 * (chip % 2)
    along_y = chip + 2 - 4 * ((chip // 2) % 2)
    first = along_x + core * (along_y - along_x)
    second = along_y + core * (along_x - along_y)
    return core, chip, first, second


def greet():
    core, chip, _, _ = place()
    me = core * CHIPS + chip
    barrier = pltpu.get_barrier_semaphore()

    def signal(step):
        other = lax.rem(me + step, DEVICES)
        pl.semaphore_signal(
            barrier,
            inc=1,
            device_id=(lax.div(other, CHIPS), lax.rem(other, CHIPS)),
            device_id_type=MESH,
        )

    every(1, DEVICES, signal)


def enter():
    pl.semaphore_wait(pltpu.get_barrier_semaphore(), DEVICES - 1)


def remote(source, target, send_sem, recv_sem, core, chip):
    return pltpu.make_async_remote_copy(
        src_ref=source,
        dst_ref=target,
        send_sem=send_sem,
        recv_sem=recv_sem,
        device_id=(core, chip),
        device_id_type=MESH,
    )


def every(start, stop, act):
    def step(index, carry):
        act(index)
        return carry

    lax.fori_loop(start, stop, step, 0)


def weight_steps(piece, many, send, recv):
    core, chip, first, second = place()
    plane, line = chip // LINES, chip % LINES
    line_first, line_second = first % LINES, second % LINES
    line_far = line_first + line_second - line
    is_low, is_high = plane > 0, plane < PLANES - 1

    def copy(send_index, recv_index, at, to_core, to_chip, carried=core):
        part = piece(at, carried)
        return remote(part, part, send.at[send_index], recv.at[recv_index], to_core, to_chip)

    def up(at_plane):
        return copy(at_plane, at_plane, at_plane * LINES + line, core, chip + LINES)

    def down(at_plane, index):
        return copy(index, at_plane, at_plane * LINES + line, core, chip - LINES)

    def side(at_plane, base, at_line, target):
        return copy(5, base + at_plane, at_plane * LINES + at_line, core, target)

    def across(at_plane, at_line):
        return copy(6, 17, at_plane * LINES + at_line, 1 - core, chip)

    def all_of(count, send_index, recv_index):
        part = many(count)
        return remote(part, part, send.at[send_index], recv.at[recv_index], 1 - core, chip)

    def begin():
        pl.when(is_high)(lambda: up(plane).start())
        pl.when(is_low)(lambda: down(plane, PLANES).start())
        side(plane, 5, line, first).start()
        side(plane, 9, line, second).start()

    def at_distance(distance, act):
        if distance == 0:
            act(plane, None)
            return
        pl.when(plane >= distance)(lambda: act(plane - distance, True))
        pl.when(plane + distance < PLANES)(lambda: act(plane + distance, False))

    def chain(distance):
        def act(at_plane, from_low):
            if from_low:
                up(at_plane).wait_recv()
                pl.when(is_high)(lambda: up(at_plane).start())
            else:
                down(at_plane, at_plane).wait_recv()
                pl.when(is_low)(lambda: down(at_plane, at_plane).start())
            side(at_plane, 5, line, first).start()
            side(at_plane, 9, line, second).start()
            across(at_plane, line).start()

        return partial(at_distance, distance, act)

    def near(distance):
        def act(at_plane, from_low):
            side(at_plane, 5, line_first, first).wait_recv()
            side(at_plane, 13, line_first, second).start()
            across(at_plane, line_first).start()

        return partial(at_distance, distance, act)

    def far(distance):
        def act(at_plane, from_low):
            side(at_plane, 9, line_second, second).wait_recv()
            across(at_plane, line_second).start()
            side(at_plane, 13, line_far, second).wait_recv()
            across(at_plane, line_far).start()

        return partial(at_distance, distance, act)

    def finish():
        all_of(15, 6, 17).wait_recv()

    def drain():
        def sent(index):
            copy(index, index, chip, 1 - core, chip).wait_send()

        for at_plane in range(PLANES):
            pl.when((plane >= at_plane) & is_high)(partial(sent, at_plane))
            pl.when((plane < at_plane) & is_low)(partial(sent, at_plane))
        pl.when(is_low)(partial(sent, PLANES))
        all_of(12, 5, 17).wait_send()
        all_of(15, 6, 17).wait_send()

    moves = [chain(1), near(0), chain(2), near(1), chain(3), far(0)]
    moves += [near(2), far(1), near(3), far(2), far(3)]
    return begin, moves, finish, drain


def gather_steps(buffer, send, recv):
    core, chip, first, second = place()
    plane, line = chip // LINES, chip % LINES
    line_first, line_second = first % LINES, second % LINES
    line_far = line_first + line_second - line
    half = buffer.shape[-1] // 2
    columns = pl.ds(pl.multiple_of(core * half, 128), half)
    others = pl.ds(pl.multiple_of((1 - core) * half, 128), half)

    def copy(index, part, to_core, to_chip):
        return remote(part, part, send.at[index], recv.at[index], to_core, to_chip)

    def own(at):
        return buffer.at[at, plane, line]

    def chip_part(at_plane, at_line, which):
        return buffer.at[:, at_plane, at_line, :, which]

    def line_part(at_line, which):
        return buffer.at[:, :, at_line, :, which]

    def start():
        copy(0, own(core), 1 - core, chip).start()

    def planes():
        copy(0, own(1 - core), 1 - core, chip).wait_recv()
        for step in range(1, PLANES):
            part = chip_part(plane, line, columns)
            copy(step, part, core, (chip + LINES * step) % CHIPS).start()

    def sides():
        for step in range(1, PLANES):
            part = chip_part((plane + PLANES - step) % PLANES, line, columns)
            copy(step, part, core, chip).wait_recv()
        copy(4, line_part(line, columns), core, first).start()
        copy(5, line_part(line, columns), core, second).start()
        for step in range(1, PLANES):
            part = chip_part((plane + PLANES - step) % PLANES, line, columns)
            copy(6 + step, part, 1 - core, chip).start()

    def corner():
        copy(4, line_part(line_first, columns), core, first).wait_recv()
        copy(6, line_part(line_first, columns), core, second).start()
        copy(10, line_part(line_first, columns), 1 - core, chip).start()
        copy(5, line_part(line_second, columns), core, second).wait_recv()
        copy(11, line_part(line_second, columns), 1 - core, chip).start()

    def last():
        copy(6, line_part(line_far, columns), core, second).wait_recv()
        copy(12, line_part(line_far, columns), 1 - core, chip).start()

    def finish():
        for step in range(1, PLANES):
            part = chip_part((plane + PLANES - step) % PLANES, line, others)
            copy(6 + step, part, 1 - core, chip).wait_recv()
        copy(10, line_part(line_second, others), 1 - core, chip).wait_recv()
        copy(11, line_part(line_first, others), 1 - core, chip).wait_recv()
        copy(12, line_part(line_far, others), 1 - core, chip).wait_recv()

    def drain():
        copy(0, own(core), 1 - core, chip).wait_send()
        for index in [1, 2, 3, 7, 8, 9]:
            copy(index, chip_part(plane, line, columns), 1 - core, chip).wait_send()
        for index in [4, 5, 6, 10, 11, 12]:
            copy(index, line_part(line, columns), 1 - core, chip).wait_send()

    return [start, planes, sides, corner, last, finish], drain


def iota(shape, axis):
    return lax.broadcasted_iota(jnp.int32, shape, axis)


def over(numbers, power):
    return lax.shift_right_arithmetic(numbers, jnp.full_like(numbers, power.bit_length() - 1))


def within(numbers, power):
    return numbers & (power - 1)


def as_column(row):
    parts = []
    for start in range(0, row.shape[1], 128):
        tile = jnp.broadcast_to(row[:, start : start + 128], (128, 128))
        parts.append(jnp.transpose(tile)[:, 0:1])
    return jnp.concatenate(parts, axis=0)


def as_row(column):
    parts = []
    for start in range(0, column.shape[0], 128):
        tile = jnp.broadcast_to(column[start : start + 128, :], (128, 128))
        parts.append(jnp.transpose(tile)[0:1, :])
    return jnp.concatenate(parts, axis=1)


def dot(left_side, right_side):
    return contract(left_side, right_side, 1, 0)


def dot_turned(left_side, right_side):
    return contract(left_side, right_side, 1, 1)


def norm_parts(inputs):
    centered = inputs - jnp.mean(inputs, axis=-1, keepdims=True)
    inverse = lax.rsqrt(jnp.mean(centered * centered, axis=-1, keepdims=True) + EPSILON)
    return centered * inverse, inverse


def norm_back_parts(grad_output, normed, inverse, ln_gain):
    grad_normed = grad_output * ln_gain
    first_term = jnp.mean(grad_normed, axis=-1, keepdims=True)
    second_term = jnp.mean(grad_normed * normed, axis=-1, keepdims=True)
    return (
        inverse * (grad_normed - first_term - normed * second_term),
        jnp.sum(grad_output * normed, axis=0, keepdims=True),
        jnp.sum(grad_output, axis=0, keepdims=True),
    )


def erf_parts(inputs):
    decay = jnp.exp(-0.5 * inputs * inputs)
    share = 1.0 / (1.0 + jnp.abs(inputs) * (0.3275911 * 0.5**0.5))
    terms = [1.061405429, -1.453152027, 1.421413741, -0.284496736, 0.254829592]
    series = 0.5 * terms[0]
    for term in terms[1:]:
        series = series * share + 0.5 * term
    tail = series * share * decay
    return jnp.where(inputs >= 0.0, 1.0 - tail, tail), decay


def gelu_parts(inputs):
    below, decay = erf_parts(inputs)
    return inputs * below, below + inputs * decay * ((2.0 * 3.141592653589793) ** -0.5)


def gelu(inputs):
    return inputs * erf_parts(inputs)[0]


def layer_kernel(names, *refs):
    r = SimpleNamespace(**dict(zip(names, refs, strict=True)))
    core, chip, _, _ = place()
    me = core * CHIPS + chip
    here = (core, chip // LINES, chip % LINES)
    scale = HEAD ** (-0.5)
    depth, deep = WIDTH // CHIPS, WIDE // CHIPS
    sentences = TOKENS // LONG

    for j in range(TOKENS // 128):
        r.ids[j : j + 1, :] = jnp.concatenate(
            [r.token_ids[2 * j : 2 * j + 1, :], r.token_ids[2 * j + 1 : 2 * j + 2, :]], axis=1
        )
    r.ids[TOKENS // 128 : 8, :] = jnp.zeros((8 - TOKENS // 128, 128), jnp.int32)
    greet()
    ahead = (iota((TOKENS, TOKENS), 0) < iota((TOKENS, TOKENS), 1)).astype(LOW)
    r.embedded[...] = ahead
    mine = pl.ds(pl.multiple_of(chip * depth, 16), depth)
    for index, shard in enumerate([r.wq, r.wk, r.wv, r.wo]):
        r.wa[mine, index * WIDTH : (index + 1) * WIDTH] = shard[...]
    r.wb[mine, :] = r.wup[...]
    r.wc[pl.ds(pl.multiple_of(chip * deep, 16), deep), :] = r.wdown[...]
    r.every_ids[me] = r.ids[...]
    enter()

    def peer(step):
        other = lax.rem(me + step, DEVICES)
        return other, lax.div(other, CHIPS), lax.rem(other, CHIPS)

    def ids_copy(step):
        other, to_core, to_chip = peer(step)
        return remote(r.ids, r.every_ids.at[me], r.one_send.at[0], r.one_recv.at[0], to_core, to_chip)

    def all_but_one(ref, index):
        part = ref.at[0 : DEVICES - 1]
        return remote(part, part, r.one_send.at[index], r.one_recv.at[index], 1 - core, chip)

    every(1, DEVICES, lambda step: ids_copy(step).start())

    def block(ref, rows, columns):
        def piece(at, carried):
            return ref.at[
                pl.ds(pl.multiple_of(at * rows, 16), rows),
                pl.ds(pl.multiple_of(carried * columns, 128), columns),
            ]

        def many(count):
            return ref.at[0 : count * rows, 0:columns]

        return piece, many

    begin_a, moves_a, finish_a, drain_a = weight_steps(
        *block(r.wa, depth, 2 * WIDTH), r.weight_send.at[0], r.weight_recv.at[0]
    )
    begin_b, moves_b, finish_b, drain_b = weight_steps(
        *block(r.wb, depth, WIDE // 2), r.weight_send.at[1], r.weight_recv.at[1]
    )
    begin_c, moves_c, finish_c, drain_c = weight_steps(
        *block(r.wc, deep, WIDTH // 2), r.weight_send.at[2], r.weight_recv.at[2]
    )
    begin_a()
    begin_b()

    def move(*steps):
        for moves, first_step in steps:
            moves[first_step]()
            moves[first_step + 1]()

    all_but_one(r.every_ids, 0).wait_recv()
    all_ids = jnp.concatenate([r.every_ids[:, j, :] for j in range(TOKENS // 128)], axis=1)
    all_owner = over(all_ids, VOCAB_ROWS)
    asked = all_owner == me
    ranks = dot(asked.astype(LOW), r.embedded[...])
    r.rank[...] = jnp.where(asked, ranks, -1.0)
    local_row = (all_ids - all_owner * VOCAB_ROWS + 1).astype(FULL)
    r.code[...] = local_row + (over(iota((DEVICES, TOKENS), 1), LONG) * 2048).astype(FULL)

    quarter_size = DEVICES // 4

    def rows_copy(other, quarter):
        return remote(
            r.rows.at[:, pl.ds(pl.multiple_of(other * PAD, 16), PAD), :],
            r.replies.at[:, pl.ds(pl.multiple_of(me * PAD, 16), PAD), :],
            r.rows_send.at[quarter],
            r.rows_recv.at[quarter],
            lax.div(other, CHIPS),
            lax.rem(other, CHIPS),
        )

    def rows_of(quarter):
        count = quarter_size - 1 if quarter == 3 else quarter_size
        part = r.replies.at[:, 0 : count * PAD, :]
        return remote(
            part, part, r.rows_send.at[quarter], r.rows_recv.at[quarter], 1 - core, chip
        )

    def pick(source):
        rank = r.rank[pl.ds(source, 1), :]
        code = r.code[pl.ds(source, 1), :]
        here_at = iota((CAPACITY, TOKENS), 0).astype(FULL) == rank
        found = jnp.sum(jnp.where(here_at, code, 0.0), axis=1, keepdims=True)
        sent = jnp.floor(found * (1.0 / 2048))
        row = found - sent * 2048.0 - 1.0
        chosen = (iota((CAPACITY, VOCAB_ROWS), 1).astype(FULL) == row).astype(LOW)
        at = pl.ds(pl.multiple_of(source * PAD, 16), PAD)
        source_sent = sent + (source * PAD).astype(FULL)
        for group in range(GROUPS):
            part = slice(group * PAD, (group + 1) * PAD)
            r.chosen[group, at, :] = chosen[part]
            r.found[group, at, 0:1] = row[part]
            r.found[group, at, 1:2] = source_sent[part]

    def quarter_rows(quarter):
        now = lax.rem(lax.div(me, quarter_size) + 1 + quarter, 4)

        def pick_two(index):
            pick(now * quarter_size + 2 * index)
            pick(now * quarter_size + 2 * index + 1)

        every(0, quarter_size // 2, pick_two)
        span = pl.ds(pl.multiple_of(now * quarter_size * PAD, 128), quarter_size * PAD)
        for start in range(0, WIDTH, BLOCK):
            lanes = slice(start, start + BLOCK)
            picked = r.chosen[:, span, :].reshape(GROUPS * quarter_size * PAD, VOCAB_ROWS)
            found_rows = dot(picked, r.table[:, lanes]).astype(LOW)
            r.rows[:, span, lanes] = found_rows.reshape(GROUPS, quarter_size * PAD, BLOCK)

        def send(index):
            other = now * quarter_size + lax.rem(lax.rem(me, quarter_size) + index, quarter_size)
            rows_copy(other, quarter).start()

        every(lax.div(quarter, 3), quarter_size, send)
        pl.when(quarter == 0)(partial(move, (moves_a, 0)))
        pl.when(quarter == 1)(partial(move, (moves_b, 0)))
        pl.when(quarter == 2)(partial(move, (moves_a, 2)))
        pl.when(quarter == 3)(partial(move, (moves_b, 2)))

    every(0, 4, quarter_rows)
    begin_c()
    own_at = pl.ds(pl.multiple_of(me * PAD, 16), PAD)
    r.replies[:, own_at, :] = r.rows[:, own_at, :]

    move((moves_a, 4))

    small_here = pl.ds(pl.multiple_of(chip * 128, 128), 128)
    lines = [r.bq, r.bv, r.bo, r.g1, r.s1, r.bdown, r.g2, r.s2]
    lines = [line[...].reshape(1, depth).astype(FULL) for line in lines]
    up_line = r.bup[...].reshape(1, deep).astype(FULL)
    lines += [up_line[:, part * depth : (part + 1) * depth] for part in range(deep // depth)]
    lines.append(jnp.zeros((PAD - len(lines), depth), FULL))
    own_small = jnp.concatenate(lines, axis=0)
    own_small = jnp.concatenate([own_small, jnp.zeros((PAD, 128 - depth), FULL)], axis=1)
    r.smalls[:, small_here] = own_small.astype(LOW)

    def small_copy(step):
        part = r.smalls.at[:, small_here]
        to_chip = lax.rem(chip + step, CHIPS)
        return remote(part, part, r.small_send.at[0], r.small_recv.at[0], core, to_chip)

    def all_smalls():
        part = r.smalls.at[:, 0 : (CHIPS - 1) * 128]
        return remote(part, part, r.small_send.at[0], r.small_recv.at[0], 1 - core, chip)

    every(1, CHIPS, lambda step: small_copy(step).start())
    move((moves_b, 4))

    own_row = jnp.concatenate([r.ids[j : j + 1, :] for j in range(TOKENS // 128)], axis=1)
    owner_row = over(own_row, VOCAB_ROWS).astype(FULL)
    owner_col = as_column(owner_row)
    earlier = (owner_row == owner_col) & (iota((TOKENS, TOKENS), 1) < iota((TOKENS, TOKENS), 0))
    own_rank = jnp.sum(earlier.astype(FULL), axis=1, keepdims=True)
    own_group = jnp.floor(own_rank * (1.0 / PAD))
    own_slot = own_group * SLOT_ROWS + owner_col * PAD + (own_rank - own_group * PAD)
    r.slot_col[...] = own_slot
    r.slot_line[0:1, :] = as_row(own_slot)
    move((moves_a, 6), (moves_c, 0))

    at_sent = over(iota((1, TOKENS), 1), LONG)
    lens = jnp.concatenate(
        [r.lens[...].reshape(1, sentences).astype(FULL), jnp.zeros((1, PAD - sentences), FULL)],
        axis=1,
    )
    spread_lens = dot(
        jnp.broadcast_to(lens, (8, PAD)).astype(LOW),
        (iota((PAD, TOKENS), 0) == over(iota((PAD, TOKENS), 1), LONG)).astype(LOW),
    )[0:1]
    valid_row = ((iota((1, TOKENS), 1) - at_sent * LONG).astype(FULL) < spread_lens).astype(FULL)
    r.valid_line[0:1, :] = valid_row
    r.valid_col[...] = as_column(valid_row)
    half_block = BLOCK // 2
    stacked_shape = (4 * half_block, half_block)
    same = within(over(iota(stacked_shape, 0), LONG), 2) == over(iota(stacked_shape, 1), LONG)
    r.block_bias[...] = jnp.where(same, 0.0, MASK_FLOOR)
    r.valid_bias[0:1, :] = (1.0 - valid_row) * MASK_FLOOR

    slots = r.slots[...].reshape(1, DEVICES * sentences)
    gap = jnp.full((1, PAD - sentences), -2, jnp.int32)
    slot_line = jnp.concatenate(
        [
            part
            for device in range(DEVICES)
            for part in (slots[:, device * sentences : (device + 1) * sentences], gap)
        ],
        axis=1,
    )
    side_line = within(slot_line, 2) + jnp.where(slot_line < 0, 8, 0)
    pair_line = over(slot_line, 2)
    pairs = r.langs.shape[0]
    lang_line = r.langs[...].reshape(1, pairs).astype(FULL)
    lang_line = jnp.concatenate([lang_line, jnp.full((1, -pairs % 128), -1.0, FULL)], axis=1)
    lang_col = as_column(lang_line)
    same_lang = jnp.sum(jnp.where(lang_col == lang_line, 1.0, 0.0), axis=1, keepdims=True)
    per_pair = 1.0 / (2.0 * LANGS * same_lang)
    at_pair = iota((lang_line.shape[1], SLOT_ROWS), 0) == pair_line
    weight_line = jnp.sum(jnp.where(at_pair, per_pair, 0.0), axis=0, keepdims=True)
    r.pairs[0:1, :] = weight_line
    r.pairs[1:2, :] = pair_line.astype(FULL)
    r.pairs[2:3, :] = side_line.astype(FULL)
    r.pairs_col[:, 0:1] = as_column(weight_line)
    r.pairs_col[:, 1:2] = as_column(pair_line.astype(FULL))
    r.pairs_col[:, 2:3] = as_column(side_line.astype(FULL))
    move((moves_b, 6), (moves_c, 2))

    all_smalls().wait_recv()
    smalls = r.smalls[...].astype(FULL)
    r.vectors[:, 0:WIDTH] = jnp.concatenate(
        [smalls[:, at * 128 : at * 128 + depth] for at in range(CHIPS)], axis=1
    )
    r.up_bias[0:1, :] = jnp.concatenate(
        [
            smalls[8 + part : 9 + part, at * 128 : at * 128 + depth]
            for at in range(CHIPS)
            for part in range(deep // depth)
        ],
        axis=1,
    )

    def vector(index):
        return r.vectors[index : index + 1, :]

    r.qkv_bias[0:1, 0:WIDTH] = vector(0)
    r.qkv_bias[0:1, WIDTH : 2 * WIDTH] = jnp.zeros((1, WIDTH), FULL)
    r.qkv_bias[0:1, 2 * WIDTH : 3 * WIDTH] = vector(1)

    move((moves_a, 8), (moves_b, 8), (moves_c, 4))

    def first_row(source):
        code = jnp.where(r.rank[pl.ds(source, 1), :] >= 0.0, r.code[pl.ds(source, 1), :], 0.0)
        at_first = iota((PAD, TOKENS), 1) == iota((PAD, TOKENS), 0) * LONG
        found = jnp.sum(jnp.where(at_first, code, 0.0), axis=1, keepdims=True)
        row = found - jnp.floor(found * (1.0 / 2048)) * 2048.0 - 1.0
        r.found[GROUPS, pl.ds(pl.multiple_of(source * PAD, 16), PAD), 0:1] = row

    every(0, DEVICES, first_row)
    for group in range(GROUPS + 1):
        named = as_row(r.found[group, :, 0:1])
        by_row = iota((VOCAB_ROWS, SLOT_ROWS), 0).astype(FULL) == named
        r.by_row[:, group * SLOT_ROWS : (group + 1) * SLOT_ROWS] = by_row.astype(LOW)

    def order(tile):
        at = pl.ds(pl.multiple_of(tile * BLOCK, BLOCK), BLOCK)
        lanes = iota((BLOCK, GROUPS * SLOT_ROWS), 1).astype(FULL)
        r.qkv[at, 0 : GROUPS * SLOT_ROWS] = (r.slot_col[at, :] == lanes).astype(LOW)

    every(0, TOKENS // BLOCK, order)
    for group in range(GROUPS):
        slot_at = iota((SLOT_ROWS, TOKENS), 0) + group * SLOT_ROWS
        named = (slot_at.astype(FULL) == r.slot_line[0:1, :]).astype(LOW)
        r.chosen[group, :, 0:TOKENS] = named
    moves_a[10]()
    moves_b[10]()
    finish_a()
    for index, which in enumerate([1, 2]):
        turned = jnp.transpose(r.wa[:, which * WIDTH : (which + 1) * WIDTH])
        r.turned[index * WIDTH : (index + 1) * WIDTH, :] = turned
    for quarter in range(4):
        rows_of(quarter).wait_recv()

    def embed(tile):
        at = pl.ds(pl.multiple_of(tile * BLOCK, BLOCK), BLOCK)
        replies = r.replies[:, :, at].reshape(GROUPS * SLOT_ROWS, BLOCK)
        r.embedded[:, at] = dot(r.qkv[:, 0 : GROUPS * SLOT_ROWS], replies).astype(LOW)

    every(0, WIDTH // BLOCK, embed)

    def project(tile):
        at = pl.ds(pl.multiple_of(tile * BLOCK, BLOCK), BLOCK)
        r.qkv[:, at] = (dot(r.embedded[...], r.wa[:, at]) + r.qkv_bias[0:1, at]).astype(LOW)

    move((moves_c, 6))
    every(0, 9, project)

    row_sent = within(iota((PAIR_ROWS, WIDTH), 0), PAD)
    row_head = over(iota((PAIR_ROWS, WIDTH), 0), PAD)
    lane_block = over(iota((PAIR_ROWS, WIDTH), 1), HEAD)
    in_head = row_head == lane_block
    seen = (row_sent == lane_block) & (r.valid_line[0:1, :] > 0.0)
    firsts = (iota((PAD, TOKENS), 1) == iota((PAD, TOKENS), 0) * LONG).astype(LOW)
    real_row = iota((PAD, 1), 0) < sentences

    def spread(rows):
        return jnp.where(in_head, jnp.concatenate([rows] * HEADS, axis=0), jnp.zeros((), LOW))

    def fold(tall):
        tall = jnp.where(in_head, tall, 0.0)
        return sum(tall[head * PAD : (head + 1) * PAD] for head in range(HEADS))

    keys, values = slice(WIDTH, 2 * WIDTH), slice(2 * WIDTH, 3 * WIDTH)
    embedded_cls = dot(firsts, r.embedded[...]).astype(LOW)
    query_cls = (dot(embedded_cls, r.wa[:, 0:WIDTH]) + vector(0)).astype(LOW)
    cls_scores = dot_turned(spread(query_cls), r.qkv[:, keys]) * scale
    cls_scores = jnp.where(seen, cls_scores, MASK_FLOOR)
    cls_peak = jnp.max(cls_scores, axis=1, keepdims=True)
    cls_exp = jnp.where(seen, jnp.exp(cls_scores - cls_peak), 0.0)
    cls_total = jnp.sum(cls_exp, axis=1, keepdims=True)
    cls_probs = cls_exp / jnp.where(cls_total > 0.0, cls_total, 1.0)
    probs_low = cls_probs.astype(LOW)
    r.probs[...] = cls_probs
    context_cls = fold(dot(probs_low, r.qkv[:, values])).astype(LOW)
    first_cls = (
        embedded_cls.astype(FULL)
        + dot(context_cls, r.wa[:, 3 * WIDTH : 4 * WIDTH])
        + vector(2)
    )
    normed_one, inverse_one = norm_parts(first_cls)
    r.normed_one[...] = normed_one
    hidden_cls = normed_one * vector(3) + vector(4)
    hidden_cls_low = hidden_cls.astype(LOW)
    early_here = r.early.at[here]
    early_here[:, 0:WIDTH] = hidden_cls_low
    early_here[:, WIDTH : 2 * WIDTH] = query_cls
    steps_u, drain_u = gather_steps(r.units, r.gather_send.at[0], r.gather_recv.at[0])
    steps_e, drain_e = gather_steps(r.early, r.gather_send.at[1], r.gather_recv.at[1])
    steps_d, drain_d = gather_steps(r.downs, r.gather_send.at[2], r.gather_recv.at[2])
    steps_a, drain_a2 = gather_steps(r.attends, r.gather_send.at[3], r.gather_recv.at[3])
    steps_q, drain_q = gather_steps(r.queries, r.gather_send.at[4], r.gather_recv.at[4])
    steps_e[0]()

    def attend(unit):
        rows = pl.ds(pl.multiple_of(unit * half_block, half_block), half_block)
        lane_head = over(iota((half_block, BLOCK), 1), HEAD)
        bias = r.block_bias[...] + r.valid_bias[0:1, rows]

        def part(which, lane):
            return r.qkv[rows, which * WIDTH + lane : which * WIDTH + lane + BLOCK]

        for lane in range(0, WIDTH, BLOCK):
            query = part(0, lane) * jnp.asarray(scale, LOW)
            key, value = part(1, lane), part(2, lane)
            stacked = jnp.concatenate(
                [jnp.where(lane_head == head, query, jnp.zeros((), LOW)) for head in range(4)],
                axis=0,
            )
            scores = dot_turned(stacked, key) + bias
            shifted = jnp.exp(scores - jnp.max(scores, axis=1, keepdims=True))
            probs = shifted * (1.0 / jnp.sum(shifted, axis=1, keepdims=True))
            mixed = dot(probs.astype(LOW), value)
            result = mixed[0:half_block]
            for head in range(1, 4):
                result = jnp.where(
                    lane_head == head, mixed[head * half_block : (head + 1) * half_block], result
                )
            r.context[rows, lane : lane + BLOCK] = result.astype(LOW)

    def open_tile(tile):
        at = pl.ds(pl.multiple_of(tile * BLOCK, BLOCK), BLOCK)
        attended = dot(r.context[at, :], r.wa[:, 3 * WIDTH : 4 * WIDTH]) + vector(2)
        normed, _ = norm_parts(r.embedded[at, :].astype(FULL) + attended)
        hidden = normed * vector(3) + vector(4)
        r.context[at, :] = hidden.astype(LOW)
        r.table_full[at, :] = hidden + vector(5)

    most = SLOT_ROWS
    rest_at = pl.ds(most, TOKENS - most)

    def up_product(part):
        at = pl.ds(pl.multiple_of(part * BLOCK, BLOCK), BLOCK)
        return dot(r.context[...], r.wb[:, at]) + r.up_bias[0:1, at]

    def feed_up(part, last=False):
        active = gelu(r.tile_up[...]).astype(LOW)
        if not last:
            r.tile_up[...] = up_product(part + 1)
        lanes = pl.ds(pl.multiple_of(lax.rem(part, 4) * BLOCK, BLOCK), BLOCK)
        r.chosen[lax.div(part, 4), :, lanes] = active[:most]
        rest = pl.ds(pl.multiple_of(lax.div(part, 6) * BLOCK, BLOCK), BLOCK)
        lanes = pl.ds(pl.multiple_of(lax.rem(part, 6) * BLOCK, BLOCK), BLOCK)
        r.slopes[rest, lanes] = active[most:]

    def feed_down(part):
        lanes = pl.ds(pl.multiple_of(part * BLOCK, BLOCK), BLOCK)
        total = r.table_full[0:most, lanes]
        for group in range(GROUPS):
            rows = slice(group * VOCAB_ROWS, (group + 1) * VOCAB_ROWS)
            total = total + dot(r.chosen[group], r.wc[rows, lanes])
        r.table_full[0:most, lanes] = total

    def feed_rest(part):
        lanes = pl.ds(pl.multiple_of(part * BLOCK, BLOCK), BLOCK)
        low_part = dot(r.slopes[0:BLOCK, :], r.wc[0 : WIDE // 2, lanes])
        high_part = dot(r.slopes[BLOCK : 2 * BLOCK, :], r.wc[WIDE // 2 :, lanes])
        r.table_full[rest_at, lanes] += low_part + high_part

    def layer_copy(tile):
        at = pl.ds(pl.multiple_of(tile * BLOCK, BLOCK), BLOCK)
        return pltpu.make_async_copy(r.context.at[at], r.layer_out.at[at], r.out_sem.at[tile])

    def close_tile(tile):
        at = pl.ds(pl.multiple_of(tile * BLOCK, BLOCK), BLOCK)
        normed, _ = norm_parts(r.table_full[at, :])
        out = normed * vector(6) + vector(7)
        r.context[at, :] = (out * r.valid_col[at, :]).astype(LOW)
        layer_copy(tile).start()

    finish_b()
    r.hidden_cls[...] = hidden_cls_low

    def up_part(part):
        at = pl.ds(pl.multiple_of(part * BLOCK, BLOCK), BLOCK)
        active, slope = gelu_parts(dot(r.hidden_cls[...], r.wb[:, at]) + r.up_bias[0:1, at])
        r.active_cls[:, at] = active.astype(LOW)
        r.slope_cls[:, at] = slope

    every(0, WIDE // BLOCK, up_part)
    steps_e[1]()

    def attend_step(unit):
        attend(unit)
        pl.when(unit == 1)(partial(move, (moves_c, 8)))
        pl.when(unit == 3)(moves_c[10])
        pl.when(unit == 4)(steps_e[2])

    every(0, 6, attend_step)
    finish_c()

    def pack_tall(target, first_row, act):
        def run(part):
            window = jnp.minimum(lax.div(part * 2 * depth, 128) * 128, WIDTH - BLOCK)
            shape = (BLOCK, BLOCK)
            lane = within(iota(shape, 1), 128)
            column = over(iota(shape, 1), 128) * depth + lane + (part * 2 * depth - window)
            select = ((iota(shape, 0) == column) & (lane < depth)).astype(LOW)
            taken = dot(r.tall[:, pl.ds(pl.multiple_of(window, 128), BLOCK)], select)

            def beside(low, high):
                return [
                    low[:, one * 128 : (one + 1) * 128]
                    + pltpu.roll(high[:, one * 128 : (one + 1) * 128], depth, 1)
                    for one in range(2)
                ]

            for half in range(CORES):
                base = half * PAIR_ROWS // 2
                both = beside(taken[base : base + 48], taken[base + 48 : base + 96])
                for one in range(2):
                    at = half * CHIPS + 2 * part + one
                    target[at, first_row : first_row + 48, :] = act(
                        2 * part + one, both[one]
                    ).astype(LOW)
            if first_row:
                left = beside(taken[PAIR_ROWS : PAIR_ROWS + PAD], taken[PAIR_ROWS + PAD :])
                for half in range(CORES):
                    for one in range(2):
                        target[half * CHIPS + 2 * part + one, 0:PAD, :] = left[one].astype(LOW)

        return run

    def pack_coefs(coefs):
        shape = (PAIR_ROWS, GROUPS * 128)
        folds = over(iota(shape, 0), PAD) + over(iota(shape, 1), 128) * PAD == within(
            iota(shape, 1), 128
        )
        lanes = contract(coefs, folds.astype(LOW), 0, 0).astype(LOW)
        total = None
        for group in range(GROUPS):
            part = dot(r.chosen[group, :, 0:TOKENS], lanes[:, group * 128 : (group + 1) * 128])
            total = part if total is None else total + part
        return total.astype(LOW).reshape(DEVICES, PAD, 128)


    def down_part(part):
        at = pl.ds(pl.multiple_of(part * BLOCK, BLOCK), BLOCK)
        r.wide_cls[:, at] = dot(r.active_cls[...], r.wc[:, at])

    every(0, WIDTH // BLOCK, down_part)
    down_pre = r.wide_cls[:, 0:WIDTH] + vector(5)
    normed_two, inverse_two = norm_parts(hidden_cls + down_pre)
    summary = normed_two * vector(6) + vector(7)
    magnitude = jnp.sqrt(jnp.sum(summary * summary, axis=-1, keepdims=True) + EPSILON)
    unit = jnp.where(real_row, summary / magnitude, 0.0)
    r.units[here] = unit.astype(LOW)

    steps_u[0]()
    r.tall[0:PAIR_ROWS, :] = dot(probs_low, r.embedded[...]).astype(LOW)
    r.tall[PAIR_ROWS : PAIR_ROWS + PAD, :] = context_cls
    r.tall[PAIR_ROWS + PAD :, :] = embedded_cls
    pack_one = pack_tall(r.mail_one, PAD, lambda at, both: both)

    def pack_one_step(part):
        pack_one(part)
        pl.when(part == 0)(steps_u[1])
        pl.when(part == 4)(steps_u[2])

    every(0, CHIPS // 2, pack_one_step)
    r.mail_one[:, 64:80, :] = pack_coefs(probs_low)
    steps_u[3]()

    def post(box, got, index):
        def send(step):
            other, to_core, to_chip = peer(step)
            remote(
                box.at[other], got.at[me], r.one_send.at[index], r.one_recv.at[index], to_core, to_chip
            ).start()

        every(1, DEVICES, send)
        got[me] = box[me]


    def open_step(tile):
        open_tile(tile)
        pl.when(tile == 0)(steps_e[3])
        pl.when(tile == 1)(steps_u[4])

    every(0, TOKENS // BLOCK, open_step)
    steps_u[5]()
    post(r.mail_one, r.got_one, 1)
    steps_e[4]()

    units = r.units[...].reshape(SLOT_ROWS, WIDTH)
    weight_row, pair_row, side_row = r.pairs[0:1, :], r.pairs[1:2, :], r.pairs[2:3, :]

    def pair_scores(rows, pair_col, side_col):
        opposite = side_col + side_row == 1.0
        partner = opposite & (pair_col == pair_row)
        raw = SCORE_SCALE * dot_turned(rows, units)
        shifted = jnp.where(partner, raw - SCORE_SCALE * MARGIN_WIDTH, raw)
        return jnp.where(opposite, shifted, MASK_FLOOR), partner

    every_score, every_partner = pair_scores(
        units, r.pairs_col[:, 1:2], r.pairs_col[:, 2:3]
    )
    peak_row = jnp.max(every_score, axis=0, keepdims=True)
    log_row = peak_row + jnp.log(
        jnp.sum(jnp.exp(every_score - peak_row), axis=0, keepdims=True)
    )
    picked_row = jnp.sum(jnp.where(every_partner, every_score, 0.0), axis=0, keepdims=True)
    r.loss[...] = jnp.sum(weight_row * (log_row - picked_row), axis=1, keepdims=True)

    rows_here = pl.ds(pl.multiple_of(me * PAD, 16), PAD)
    own_score, own_partner = pair_scores(
        r.units[here], r.pairs_col[rows_here, 1:2], r.pairs_col[rows_here, 2:3]
    )
    own_partner = own_partner.astype(FULL)
    own_peak = jnp.max(own_score, axis=1, keepdims=True)
    own_exp = jnp.exp(own_score - own_peak)
    own_share = own_exp / jnp.sum(own_exp, axis=1, keepdims=True)
    by_row = (r.pairs_col[rows_here, 0:1] * (own_share - own_partner)).astype(LOW)
    by_column = (weight_row * (jnp.exp(own_score - log_row) - own_partner)).astype(LOW)
    unit_grad = SCORE_SCALE * (dot(by_row, units) + dot(by_column, units))
    along = jnp.sum(unit * unit_grad, axis=-1, keepdims=True)
    summary_grad = (unit_grad - unit * along) / magnitude

    residual_grad, grad_g2, grad_s2 = norm_back_parts(
        summary_grad, normed_two, inverse_two, vector(6)
    )
    down_grad = residual_grad.astype(LOW)
    r.downs[here] = down_grad
    steps_d[0]()
    r.hidden_cls[...] = down_grad

    def up_back(part):
        at = pl.ds(pl.multiple_of(part * BLOCK, BLOCK), BLOCK)
        act_grad = dot_turned(r.hidden_cls[...], r.wc[at, :])
        r.active_cls[:, at] = (act_grad * r.slope_cls[:, at]).astype(LOW)

    every(0, WIDE // BLOCK, up_back)
    steps_d[1]()

    def hidden_back(part):
        at = pl.ds(pl.multiple_of(part * BLOCK, BLOCK), BLOCK)
        r.wide_cls[:, at] = dot_turned(r.active_cls[...], r.wb[at, :])

    every(0, WIDTH // BLOCK, hidden_back)
    hidden_grad = r.wide_cls[:, 0:WIDTH] + residual_grad
    first_grad, grad_g1, grad_s1 = norm_back_parts(
        hidden_grad, r.normed_one[...], inverse_one, vector(3)
    )
    attend_grad = first_grad.astype(LOW)
    context_grad = dot_turned(attend_grad, r.wa[:, 3 * WIDTH : 4 * WIDTH]).astype(LOW)
    attend_here = r.attends.at[here]
    attend_here[:, 0:WIDTH] = attend_grad
    attend_here[:, WIDTH : 2 * WIDTH] = context_grad
    steps_a[0]()
    steps_d[2]()
    context_tall = spread(context_grad)
    probs = r.probs[...]
    prob_grad = dot_turned(context_tall, r.qkv[:, values])
    inner = jnp.sum(probs * prob_grad, axis=1, keepdims=True)
    score_grad = (probs * (prob_grad - inner)).astype(LOW)
    steps_a[1]()
    r.mail_two[:, 48:64, :] = pack_coefs(score_grad)
    query_grad = (fold(dot(score_grad, r.qkv[:, keys])) * scale).astype(LOW)
    probs_total = jnp.sum(probs_low.astype(FULL), axis=1, keepdims=True)
    grad_bvalue = jnp.sum(probs_total * context_tall.astype(FULL), axis=0, keepdims=True)
    grad_bquery = jnp.sum(query_grad.astype(FULL), axis=0, keepdims=True)
    r.queries[here] = query_grad
    own_sums = jnp.concatenate(
        [jnp.zeros((2 * depth, WIDTH), FULL)]
        + [grad_bquery, grad_bvalue, grad_g1, grad_s1, grad_g2, grad_s2]
        + [jnp.zeros((128 - 2 * depth - 6, WIDTH), FULL)],
        axis=0,
    )
    r.own_sums[...] = jnp.transpose(own_sums)
    steps_q[0]()
    steps_a[2]()
    r.tall[0:PAIR_ROWS, :] = (dot(score_grad, r.embedded[...]) * scale).astype(LOW)

    def with_sums(at, both):
        return both + r.own_sums[pl.ds(pl.multiple_of(at * depth, 16), depth), :]

    every(0, CHIPS // 2, pack_tall(r.mail_two, 0, with_sums))
    steps_q[1]()
    post(r.mail_two, r.got_two, 2)

    def all_rows(buffer, start, width=WIDTH):
        return buffer[:, :, :, :, start : start + width].reshape(SLOT_ROWS, width)

    def from_sent(group):
        lanes = iota((SLOT_ROWS, SLOT_ROWS), 1).astype(FULL)
        return (r.found[group, :, 1:2] == lanes).astype(LOW)

    def widened(coefs, group, start):
        lanes = iota((128, BLOCK), 0) == over(iota((128, BLOCK), 1) + start, HEAD) + group * PAD
        return dot(coefs, lanes.astype(LOW))

    half_wide = WIDE // 2

    def slope_tile(part):
        at = pl.ds(pl.multiple_of(core * half_wide + part * BLOCK, BLOCK), BLOCK)
        up_pre = dot(all_rows(r.early, 0), r.wb[:, at]) + r.up_bias[0:1, at]
        _, slope = gelu_parts(up_pre)
        r.slopes[:, pl.ds(pl.multiple_of(part * BLOCK, BLOCK), BLOCK)] = slope.astype(LOW)

    def slot_queries(group):
        sents = from_sent(group)
        for start in range(0, WIDTH, BLOCK):
            rows = dot(sents, all_rows(r.early, WIDTH + start, BLOCK))
            r.slot_query[group, :, start : start + BLOCK] = rows.astype(LOW)

    def activate():
        at = pl.ds(pl.multiple_of(chip // 2 * 2 * deep, 128), 2 * deep)
        up_pre = dot(all_rows(r.early, 0), r.wb[:, at]) + r.up_bias[0:1, at]
        r.active_turned[...] = jnp.transpose(gelu(up_pre)).astype(LOW)
        r.hidden_turned[...] = jnp.transpose(all_rows(r.early, 0))

    steps_e[5]()

    def feed_step(part):
        feed_up(part)
        rest = [steps_d[3], steps_a[3], steps_q[2], steps_d[4], steps_a[4], steps_q[3]]
        rest += [steps_d[5], steps_a[5], steps_q[4]]
        for index, step in enumerate(rest):
            pl.when(part == index)(step)

    r.tile_up[...] = up_product(0)
    every(0, WIDE // BLOCK - 1, feed_step)
    feed_up(WIDE // BLOCK - 1, last=True)
    every(0, WIDTH // BLOCK, feed_rest)
    every(0, WIDTH // BLOCK, feed_down)
    every(0, TOKENS // BLOCK, close_tile)
    every(0, GROUPS, slot_queries)
    every(0, 6, slope_tile)
    activate()

    all_but_one(r.got_one, 1).wait_recv()
    def slot_values(group):
        sents = from_sent(group)
        got_probs = r.got_one[:, 64:80, :].reshape(SLOT_ROWS, 128)
        for start in range(0, WIDTH, BLOCK):
            rows = dot(sents, all_rows(r.attends, WIDTH + start, BLOCK))
            rows = widened(got_probs, group, start) * rows
            r.replies[group, :, start : start + BLOCK] = rows.astype(LOW)

    every(0, GROUPS, slot_values)

    def head_products(got, first_row, right, start, target):
        def one_head(head):
            lane = core * (WIDTH // 2) + lax.div(head, 2) * 128
            pair_rows = right[:, :, :, :, pl.ds(pl.multiple_of(start + lane, 128), 128)]
            row = pl.ds(pl.multiple_of(first_row + lax.rem(head, 3) * PAD, 16), PAD)
            block_rows = got[:, row, :].reshape(SLOT_ROWS, 128)
            r.product[...] = contract(block_rows, pair_rows.reshape(SLOT_ROWS, 128), 0, 0)
            part = r.product[pl.ds(pl.multiple_of(lax.div(head, 3) * depth, 16), depth), :]
            at = pl.ds(pl.multiple_of(lane, 128), 128)
            own_lanes = over(iota((depth, 128), 1), HEAD) == lax.rem(head, 2)
            target[:, at] = jnp.where(own_lanes, part, target[:, at])

        every(0, HEADS // 2, one_head)

    def half_of(ref, at_core):
        half = ref.shape[1] // 2
        return ref.at[:, pl.ds(pl.multiple_of(at_core * half, 128), half)]

    def half_copy(index, ref, at_core):
        part = half_of(ref, at_core)
        return remote(part, part, r.half_send.at[index], r.half_recv.at[index], 1 - core, chip)

    own_half = pl.ds(pl.multiple_of(core * (WIDTH // 2), 128), WIDTH // 2)
    r.g_wv[:, own_half] = jnp.zeros((depth, WIDTH // 2), FULL)
    r.g_wk[:, own_half] = jnp.zeros((depth, WIDTH // 2), FULL)
    head_products(r.got_one, PAD, r.attends, WIDTH, r.g_wv)
    half_copy(0, r.g_wv, core).start()

    downs = r.downs[...].reshape(SLOT_ROWS, WIDTH)
    attends = all_rows(r.attends, 0)

    def up_tile(part):
        at = pl.ds(pl.multiple_of(core * half_wide + part * BLOCK, BLOCK), BLOCK)
        slope = r.slopes[:, pl.ds(pl.multiple_of(part * BLOCK, BLOCK), BLOCK)].astype(FULL)
        up_all = (dot_turned(r.downs[...].reshape(SLOT_ROWS, WIDTH), r.wc[at, :]) * slope)
        up_all = up_all.astype(LOW)
        r.g_wup[0:depth, at] = dot(r.hidden_turned[mine, :], up_all)
        total = jnp.sum(up_all.astype(FULL), axis=0, keepdims=True)
        r.g_wup[depth : depth + 8, at] = jnp.broadcast_to(total, (8, BLOCK))

    every(0, half_wide // BLOCK, up_tile)
    half_copy(1, r.g_wup, core).start()
    r.g_wdown[...] = dot(r.active_turned[pl.ds(pl.multiple_of(chip % 2 * deep, 16), deep), :], downs)
    r.left_turned[...] = jnp.transpose(r.got_one[:, 0:PAD, :].reshape(SLOT_ROWS, 128))
    r.g_wo[...] = dot(r.left_turned[0:depth, :], attends)
    own_lanes = (iota((WIDTH, 128), 0) == chip * depth + iota((WIDTH, 128), 1)).astype(LOW)

    def own_part(rows, select):
        total = None
        for _ in range(3):
            part = rows.astype(LOW)
            rows = rows - part.astype(FULL)
            picked = dot(part, select)
            total = picked if total is None else total + picked
        return total

    for quarter in range(4):
        rows_of(quarter).wait_send()
    all_but_one(r.got_two, 2).wait_recv()

    def slot_grads(group):
        got_scores = r.got_two[:, 48:64, :].reshape(SLOT_ROWS, 128)
        for start in range(0, WIDTH, BLOCK):
            lanes = slice(start, start + BLOCK)
            rows = r.slot_query[group, :, lanes].astype(FULL)
            rows = widened(got_scores, group, start) * rows * scale
            r.slot_query[group, :, lanes] = rows.astype(LOW)
        for start in range(0, WIDTH, BLOCK):
            lanes = slice(start, start + BLOCK)
            row_grad = dot(r.slot_query[group], r.turned[0:WIDTH, lanes])
            row_grad = row_grad + dot(r.replies[group], r.turned[WIDTH : 2 * WIDTH, lanes])
            r.rows[group, :, lanes] = row_grad.astype(LOW)

    every(0, GROUPS, slot_grads)
    steps_q[5]()
    query_grads = all_rows(r.queries, 0)
    extra = dot_turned(query_grads, r.wa[:, 0:WIDTH]) + attends.astype(FULL)
    r.extra[...] = extra.astype(LOW)
    r.g_wq[...] = dot(r.left_turned[depth : 2 * depth, :], query_grads)

    half_rows = VOCAB_ROWS // 2

    def table_copy(tile):
        at = pl.ds(pl.multiple_of(tile * half_rows, BLOCK), half_rows)
        return pltpu.make_async_copy(
            r.table_full.at[at], r.table_grad.at[at], r.table_sem.at[tile]
        )

    def table_tile(tile):
        at = pl.ds(pl.multiple_of(tile * half_rows, BLOCK), half_rows)
        for start in range(0, WIDTH, BLOCK):
            lanes = slice(start, start + BLOCK)
            slot_rows = r.rows[:, :, lanes].reshape(GROUPS * SLOT_ROWS, BLOCK)
            r.table_full[at, lanes] = dot(r.by_row[at, 0 : GROUPS * SLOT_ROWS], slot_rows) + dot(
                r.by_row[at, GROUPS * SLOT_ROWS :], r.extra[:, lanes]
            )
        table_copy(tile).start()

    every(0, 2, table_tile)
    head_products(r.got_two, 0, r.early, WIDTH, r.g_wk)
    half_copy(2, r.g_wk, core).start()

    down_total = jnp.sum(downs.astype(FULL), axis=0, keepdims=True)
    attend_total = jnp.sum(attends.astype(FULL), axis=0, keepdims=True)
    sums = jnp.sum(r.got_two[:, 0:48, :].astype(FULL), axis=0)
    sums = jnp.concatenate([sums, jnp.zeros((128 - 48, 128), FULL)], axis=0)
    stacked = jnp.concatenate([attend_total, down_total, jnp.zeros((6, WIDTH), FULL)], axis=0)
    r.g_small[8:16, 0:128] = own_part(stacked, own_lanes)
    r.g_small[0:8, 0:128] = jnp.transpose(sums)[2 * depth : 2 * depth + 8, :]
    r.g_small[0:16, 128:BLOCK] = jnp.zeros((PAD, BLOCK - 128), FULL)
    half_copy(1, r.g_wup, 1 - core).wait_recv()
    up_lanes = (iota((WIDE, BLOCK), 0) == chip * deep + iota((WIDE, BLOCK), 1)).astype(LOW)
    r.g_small[16:24, :] = own_part(r.g_wup[depth : depth + 8, :], up_lanes)

    half_copy(0, r.g_wv, 1 - core).wait_recv()
    half_copy(2, r.g_wk, 1 - core).wait_recv()
    for index, ref in enumerate([r.g_wv, r.g_wup, r.g_wk]):
        half_copy(index, ref, core).wait_send()

    for index, ref in enumerate([r.every_ids, r.got_one, r.got_two]):
        all_but_one(ref, index).wait_send()
    all_smalls().wait_send()
    for end in [drain_a, drain_b, drain_c, drain_u, drain_e, drain_d, drain_a2, drain_q]:
        end()
    every(0, TOKENS // BLOCK, lambda tile: layer_copy(tile).wait())
    every(0, 2, lambda tile: table_copy(tile).wait())


def layer(inputs):
    dma = pltpu.SemaphoreType.DMA
    vmem = pl.BlockSpec(memory_space=pltpu.VMEM)
    anywhere = pl.BlockSpec(memory_space=pl.ANY)
    depth, deep = WIDTH // CHIPS, WIDE // CHIPS

    def gathered(width):
        return pltpu.VMEM((CORES, PLANES, LINES, PAD, width), LOW)

    outputs = dict(
        layer_out=((TOKENS, WIDTH), LOW),
        table_grad=((VOCAB_ROWS, WIDTH), FULL),
        g_wq=((depth, WIDTH), FULL),
        g_wk=((depth, WIDTH), FULL),
        g_wv=((depth, WIDTH), FULL),
        g_wo=((depth, WIDTH), FULL),
        g_wup=((depth + 8, WIDE), FULL),
        g_wdown=((deep, WIDTH), FULL),
        g_small=((24, BLOCK), FULL),
        loss=((1, 1), FULL),
    )
    scratch = dict(
        ids=pltpu.VMEM((8, 128), jnp.int32),
        every_ids=pltpu.VMEM((DEVICES, 8, 128), jnp.int32),
        rank=pltpu.VMEM((DEVICES, TOKENS), FULL),
        code=pltpu.VMEM((DEVICES, TOKENS), FULL),
        found=pltpu.VMEM((GROUPS + 1, SLOT_ROWS, 2), FULL),
        block_bias=pltpu.VMEM((2 * BLOCK, BLOCK // 2), FULL),
        valid_bias=pltpu.VMEM((8, TOKENS), FULL),
        slot_col=pltpu.VMEM((TOKENS, 1), FULL),
        slot_line=pltpu.VMEM((8, TOKENS), FULL),
        valid_col=pltpu.VMEM((TOKENS, 1), FULL),
        valid_line=pltpu.VMEM((8, TOKENS), FULL),
        pairs=pltpu.VMEM((8, SLOT_ROWS), FULL),
        pairs_col=pltpu.VMEM((SLOT_ROWS, 128), FULL),
        vectors=pltpu.VMEM((PAD, WIDTH), FULL),
        up_bias=pltpu.VMEM((8, WIDE), FULL),
        qkv_bias=pltpu.VMEM((8, 3 * WIDTH), FULL),
        smalls=pltpu.VMEM((PAD, CHIPS * 128), LOW),
        wa=pltpu.VMEM((WIDTH, 4 * WIDTH), LOW),
        wb=pltpu.VMEM((WIDTH, WIDE), LOW),
        wc=pltpu.VMEM((WIDE, WIDTH), LOW),
        chosen=pltpu.VMEM((GROUPS, SLOT_ROWS, VOCAB_ROWS), LOW),
        by_row=pltpu.VMEM((VOCAB_ROWS, (GROUPS + 1) * SLOT_ROWS), LOW),
        rows=pltpu.VMEM((GROUPS, SLOT_ROWS, WIDTH), LOW),
        replies=pltpu.VMEM((GROUPS, SLOT_ROWS, WIDTH), LOW),
        slot_query=pltpu.VMEM((GROUPS, SLOT_ROWS, WIDTH), LOW),
        extra=pltpu.VMEM((SLOT_ROWS, WIDTH), LOW),
        hidden_cls=pltpu.VMEM((PAD, WIDTH), LOW),
        active_cls=pltpu.VMEM((PAD, WIDE), LOW),
        slope_cls=pltpu.VMEM((PAD, WIDE), FULL),
        wide_cls=pltpu.VMEM((PAD, WIDTH), FULL),
        tall=pltpu.VMEM((PAIR_ROWS + 2 * PAD, WIDTH), LOW),
        own_sums=pltpu.VMEM((WIDTH, 128), FULL),
        product=pltpu.VMEM((128, 128), FULL),
        turned=pltpu.VMEM((2 * WIDTH, WIDTH), LOW),
        tile_up=pltpu.VMEM((TOKENS, BLOCK), FULL),
        embedded=pltpu.VMEM((TOKENS, WIDTH), LOW),
        qkv=pltpu.VMEM((TOKENS, 3 * WIDTH), LOW),
        context=pltpu.VMEM((TOKENS, WIDTH), LOW),
        table_full=pltpu.VMEM((VOCAB_ROWS, WIDTH), FULL),
        probs=pltpu.VMEM((PAIR_ROWS, TOKENS), FULL),
        normed_one=pltpu.VMEM((PAD, WIDTH), FULL),
        units=gathered(WIDTH),
        early=gathered(2 * WIDTH),
        downs=gathered(WIDTH),
        attends=gathered(2 * WIDTH),
        queries=gathered(WIDTH),
        slopes=pltpu.VMEM((SLOT_ROWS, WIDE // 2), LOW),
        hidden_turned=pltpu.VMEM((WIDTH, SLOT_ROWS), LOW),
        active_turned=pltpu.VMEM((2 * deep, SLOT_ROWS), LOW),
        left_turned=pltpu.VMEM((128, SLOT_ROWS), LOW),
        mail_one=pltpu.VMEM((DEVICES, 80, 128), LOW),
        got_one=pltpu.VMEM((DEVICES, 80, 128), LOW),
        mail_two=pltpu.VMEM((DEVICES, 64, 128), LOW),
        got_two=pltpu.VMEM((DEVICES, 64, 128), LOW),
        rows_send=dma((4,)),
        rows_recv=dma((4,)),
        one_send=dma((4,)),
        one_recv=dma((4,)),
        small_send=dma((1,)),
        small_recv=dma((1,)),
        weight_send=dma((3, 7)),
        weight_recv=dma((3, 18)),
        gather_send=dma((5, 13)),
        gather_recv=dma((5, 13)),
        half_send=dma((3,)),
        half_recv=dma((3,)),
        out_sem=dma((TOKENS // BLOCK,)),
        table_sem=dma((2,)),
    )
    names = INPUTS + OUTPUTS + list(scratch)
    return pl.pallas_call(
        partial(layer_kernel, names),
        out_shape=tuple(jax.ShapeDtypeStruct(*outputs[name]) for name in OUTPUTS),
        in_specs=[vmem] * len(INPUTS),
        out_specs=(anywhere, anywhere) + (vmem,) * (len(OUTPUTS) - 2),
        scratch_shapes=list(scratch.values()),
        compiler_params=pltpu.CompilerParams(
            collective_id=0, has_side_effects=True, vmem_limit_bytes=VMEM_LIMIT
        ),
        name="layer",
    )(*inputs)


def finish_kernel(count, *refs):
    large, (small, loss), outs = refs[:count], refs[count : count + 2], refs[count + 2 : -1]
    sems = refs[-1]
    copies = []
    for index, (source, target) in enumerate(zip(large, outs)):
        part = source if source.shape == target.shape else source.at[: target.shape[0]]
        copies.append(pltpu.make_async_copy(part, target, sems.at[index]))
        copies[-1].start()
    for row, target in zip([0, 1, 8, 2, 3, 16, 9, 4, 5], outs[count : count + 9]):
        size = target.shape[0]
        target[...] = small[row : row + 1, 0:size].reshape(size)
    outs[-1][...] = loss[...].reshape(1)
    for one in copies:
        one.wait()


def finish(results):
    vmem = pl.BlockSpec(memory_space=pltpu.VMEM)
    anywhere = pl.BlockSpec(memory_space=pl.ANY)
    depth, deep = WIDTH // CHIPS, WIDE // CHIPS
    count = len(results) - 2
    shapes = [(one.shape, one.dtype) for one in results[:count]]
    shapes[6] = ((depth, WIDE), FULL)
    shapes += [((depth,), FULL)] * 5 + [((deep,), FULL)] + [((depth,), FULL)] * 3
    shapes.append(((1,), FULL))
    return pl.pallas_call(
        partial(finish_kernel, count),
        out_shape=tuple(jax.ShapeDtypeStruct(*one) for one in shapes),
        in_specs=[vmem] * (count + 2),
        out_specs=(anywhere,) * count + (vmem,) * 10,
        scratch_shapes=[pltpu.SemaphoreType.DMA((count,))],
        name="finish",
    )(*results)


def block_body(
    table,
    token_ids,
    sent_lengths,
    pair_slot,
    pair_lang,
    *parameters,
):
    results = finish(layer((table, token_ids, sent_lengths, pair_slot, pair_lang) + parameters))
    layer_out, table_grad, g_wq, g_wk, g_wv, g_wo, g_wup, g_wdown = results[:8]
    g_bq, g_bv, g_bo, g_g1, g_s1, g_bup, g_bdown, g_g2, g_s2, loss = results[8:]
    return (
        layer_out.reshape(token_ids.shape + (WIDTH,)),
        loss.reshape(()),
        table_grad,
        g_wq,
        g_bq,
        g_wk,
        g_wv,
        g_bv,
        g_wo,
        g_bo,
        g_g1,
        g_s1,
        g_wup,
        g_bup,
        g_wdown,
        g_bdown,
        g_g2,
        g_s2,
    )


def solution(mesh):
    in_specs = (
        P(("dp", "fsdp"), None),
        P(("dp", "fsdp"), None),
        P(("dp", "fsdp")),
        P(),
        P(),
        P("fsdp", None),
        P("fsdp"),
        P("fsdp", None),
        P("fsdp", None),
        P("fsdp"),
        P("fsdp", None),
        P("fsdp"),
        P("fsdp"),
        P("fsdp"),
        P("fsdp", None),
        P("fsdp"),
        P("fsdp", None),
        P("fsdp"),
        P("fsdp"),
        P("fsdp"),
    )
    out_specs = (
        P(("dp", "fsdp"), None, None),
        P(),
        P(("dp", "fsdp"), None),
        P("fsdp", None),
        P("fsdp"),
        P("fsdp", None),
        P("fsdp", None),
        P("fsdp"),
        P("fsdp", None),
        P("fsdp"),
        P("fsdp"),
        P("fsdp"),
        P("fsdp", None),
        P("fsdp"),
        P("fsdp", None),
        P("fsdp"),
        P("fsdp"),
        P("fsdp"),
    )
    sizes = dict(mesh.shape)
    body = general_body
    if sizes["dp"] == CORES and sizes["fsdp"] == CHIPS:
        body = block_body
    return jax.shard_map(body, mesh=mesh, in_specs=in_specs, out_specs=out_specs, check_vma=False)
```

```python
from functools import partial
from types import SimpleNamespace

import jax
import jax.numpy as jnp
from jax import lax
from jax.experimental import pallas as pl
from jax.experimental.pallas import tpu as pltpu
from jax.sharding import PartitionSpec as P

HEADS = 12
HEAD = 64
LANGS = 109


EPSILON = 1e-06
SCORE_SCALE = 50.0
MARGIN_WIDTH = 0.3
MASK_FLOOR = -1000000000.0


def contract(left_side, right_side, left_dim, right_dim):
    return lax.dot_general(
        left_side,
        right_side,
        (((left_dim,), (right_dim,)), ((), ())),
        preferred_element_type=jnp.float32,
    )


def norm_rows(inputs, ln_gain, ln_shift):
    row_mean = jnp.mean(inputs, axis=-1, keepdims=True)
    centered = inputs - row_mean
    variance = jnp.mean(centered * centered, axis=-1, keepdims=True)
    inverse = lax.rsqrt(variance + EPSILON)
    normed = centered * inverse
    return (normed * ln_gain + ln_shift, normed, inverse)


def norm_back(grad_output, normed, inverse, ln_gain):
    grad_normed = grad_output * ln_gain
    first_term = jnp.mean(grad_normed, axis=-1, keepdims=True)
    second_term = jnp.mean(grad_normed * normed, axis=-1, keepdims=True)
    grad_input = inverse * (grad_normed - first_term - normed * second_term)
    return (grad_input, jnp.sum(grad_output * normed, axis=0), jnp.sum(grad_output, axis=0))


def general_body(
    table,
    token_ids,
    sent_lengths,
    pair_slot,
    pair_lang,
    w_query,
    b_query,
    w_key,
    w_value,
    b_value,
    w_out,
    b_out,
    ln1_gain,
    ln1_bias,
    w_up,
    b_up,
    w_down,
    b_down,
    ln2_gain,
    ln2_bias,
):
    sentences, length = token_ids.shape
    tokens = sentences * length
    vocab_rows, model_width = table.shape
    owners = lax.axis_size(("dp", "fsdp"))
    dp_count = lax.axis_size("dp")
    fsdp_count = lax.axis_size("fsdp")
    capacity = max(2, 2 * tokens // owners)
    device = lax.axis_index(("dp", "fsdp"))
    score_factor = HEAD ** (-0.5)
    flat_ids = token_ids.reshape(tokens)
    owner_of = flat_ids // vocab_rows
    member = (owner_of[:, None] == jnp.arange(owners, dtype=jnp.int32)[None, :]).astype(jnp.int32)
    owner_rank = jnp.sum(jnp.cumsum(member, axis=0) * member, axis=1) - 1
    slot_of = owner_of * capacity + owner_rank
    requests = jnp.full((owners * capacity,), -1, jnp.int32).at[slot_of].set(flat_ids)
    received = lax.all_to_all(
        lax.all_to_all(
            requests.reshape(dp_count, fsdp_count, capacity),
            "dp",
            split_axis=0,
            concat_axis=0,
            tiled=True,
        ),
        "fsdp",
        split_axis=1,
        concat_axis=1,
        tiled=True,
    )
    present = received >= 0
    local_rows = jnp.where(present, received - device * vocab_rows, 0)
    found_rows = jnp.where(present[..., None], table[local_rows], jnp.zeros((), table.dtype))
    replies = lax.all_to_all(
        lax.all_to_all(found_rows, "dp", split_axis=0, concat_axis=0, tiled=True),
        "fsdp",
        split_axis=1,
        concat_axis=1,
        tiled=True,
    )
    embedded = replies.reshape(owners * capacity, model_width)[slot_of]
    gathered = (
        lax.all_gather(w_query, "fsdp", axis=0, tiled=True),
        lax.all_gather(b_query, "fsdp", axis=0, tiled=True),
        lax.all_gather(w_key, "fsdp", axis=0, tiled=True),
        lax.all_gather(w_value, "fsdp", axis=0, tiled=True),
        lax.all_gather(b_value, "fsdp", axis=0, tiled=True),
        lax.all_gather(w_out, "fsdp", axis=0, tiled=True),
        lax.all_gather(b_out, "fsdp", axis=0, tiled=True),
        lax.all_gather(ln1_gain, "fsdp", axis=0, tiled=True),
        lax.all_gather(ln1_bias, "fsdp", axis=0, tiled=True),
        lax.all_gather(w_up, "fsdp", axis=0, tiled=True),
        lax.all_gather(b_up, "fsdp", axis=0, tiled=True),
        lax.all_gather(w_down, "fsdp", axis=0, tiled=True),
        lax.all_gather(b_down, "fsdp", axis=0, tiled=True),
        lax.all_gather(ln2_gain, "fsdp", axis=0, tiled=True),
        lax.all_gather(ln2_bias, "fsdp", axis=0, tiled=True),
    )
    (
        full_wq,
        full_bq,
        full_wk,
        full_wv,
        full_bv,
        full_wo,
        full_bo,
        full_g1,
        full_s1,
        full_wup,
        full_bup,
        full_wdown,
        full_bdown,
        full_g2,
        full_s2,
    ) = gathered
    valid_mask = jnp.arange(length, dtype=jnp.int32)[None, :] < sent_lengths[:, None]
    head_shape = (sentences, length, HEADS, HEAD)
    queries = (jnp.dot(embedded, full_wq, preferred_element_type=jnp.float32) + full_bq).astype(
        jnp.bfloat16
    )
    key_heads = (
        jnp.dot(embedded, full_wk, preferred_element_type=jnp.float32)
        .astype(jnp.bfloat16)
        .reshape(head_shape)
    )
    value_heads = (
        (jnp.dot(embedded, full_wv, preferred_element_type=jnp.float32) + full_bv)
        .astype(jnp.bfloat16)
        .reshape(head_shape)
    )
    query_heads = queries.reshape(head_shape)
    scores = (
        jnp.einsum("bqhd,bkhd->bhqk", query_heads, key_heads, preferred_element_type=jnp.float32)
        * score_factor
    )
    scores = jnp.where(valid_mask[:, None, None, :], scores, MASK_FLOOR)
    row_peak = jnp.max(scores, axis=-1, keepdims=True)
    shifted = jnp.exp(scores - row_peak)
    totals = jnp.sum(shifted, axis=-1, keepdims=True)
    attn_probs = (shifted / totals).astype(jnp.bfloat16)
    context = jnp.einsum(
        "bhqk,bkhd->bqhd", attn_probs, value_heads, preferred_element_type=jnp.float32
    )
    context = context.reshape(tokens, model_width).astype(jnp.bfloat16)
    attended = jnp.dot(context, full_wo, preferred_element_type=jnp.float32) + full_bo
    hidden, normed_one, inverse_one = norm_rows(
        embedded.astype(jnp.float32) + attended, full_g1, full_s1
    )
    hidden_low = hidden.astype(jnp.bfloat16)
    up_pre = jnp.dot(hidden_low, full_wup, preferred_element_type=jnp.float32) + full_bup
    activated = jax.nn.gelu(up_pre, approximate=False).astype(jnp.bfloat16)
    down_pre = jnp.dot(activated, full_wdown, preferred_element_type=jnp.float32) + full_bdown
    normed_out, normed_two, inverse_two = norm_rows(hidden + down_pre, full_g2, full_s2)
    layer_out = jnp.where(valid_mask.reshape(tokens)[:, None], normed_out, 0.0).astype(jnp.bfloat16)
    layer_out = layer_out.reshape(sentences, length, model_width)

    def first_rows(matrix):
        return matrix.reshape(sentences, length, matrix.shape[-1])[:, 0]

    summary = first_rows(normed_out)
    magnitude = jnp.sqrt(jnp.sum(summary * summary, axis=-1, keepdims=True) + EPSILON)
    unit_vector = summary / magnitude
    unit_low = unit_vector.astype(jnp.bfloat16)
    every_unit = lax.all_gather(unit_low, ("dp", "fsdp"), axis=0, tiled=True)
    every_side = pair_slot % 2
    every_pair = pair_slot // 2
    my_slots = lax.dynamic_slice_in_dim(pair_slot, device * sentences, sentences)
    my_side = my_slots % 2
    my_pair = my_slots // 2
    lang_onehot = (pair_lang[:, None] == jnp.arange(LANGS, dtype=jnp.int32)[None, :]).astype(
        jnp.float32
    )
    per_lang = jnp.sum(lang_onehot, axis=0)
    per_pair = 1.0 / (2.0 * LANGS * jnp.sum(lang_onehot * per_lang[None, :], axis=1))
    my_weight = jnp.take(per_pair, my_pair)
    opposite = my_side[:, None] != every_side[None, :]
    partner = opposite & (my_pair[:, None] == every_pair[None, :])
    raw_scores = SCORE_SCALE * contract(unit_low, every_unit, 1, 1)
    pair_scores = jnp.where(partner, raw_scores - SCORE_SCALE * MARGIN_WIDTH, raw_scores)
    pair_scores = jnp.where(opposite, pair_scores, MASK_FLOOR)
    pair_peak = jnp.max(pair_scores, axis=1, keepdims=True)
    pair_exp = jnp.exp(pair_scores - pair_peak)
    pair_total = jnp.sum(pair_exp, axis=1, keepdims=True)
    log_total = pair_peak[:, 0] + jnp.log(pair_total[:, 0])
    picked = jnp.sum(jnp.where(partner, pair_scores, 0.0), axis=1)
    loss_value = lax.psum(jnp.sum(my_weight * (log_total - picked)), ("dp", "fsdp"))
    coefficients = (
        my_weight[:, None] * (pair_exp / pair_total - partner.astype(jnp.float32))
    ).astype(jnp.bfloat16)
    unit_grad = SCORE_SCALE * contract(coefficients, every_unit, 1, 0)
    column_terms = SCORE_SCALE * contract(coefficients, unit_low, 0, 0)
    unit_grad = unit_grad + lax.psum_scatter(
        column_terms, ("dp", "fsdp"), scatter_dimension=0, tiled=True
    )
    along = jnp.sum(unit_vector * unit_grad, axis=-1, keepdims=True)
    summary_grad = (unit_grad - unit_vector * along) / magnitude
    again_weights = (
        lax.all_gather(w_query, "fsdp", axis=0, tiled=True),
        lax.all_gather(w_key, "fsdp", axis=0, tiled=True),
        lax.all_gather(w_value, "fsdp", axis=0, tiled=True),
        lax.all_gather(w_out, "fsdp", axis=0, tiled=True),
        lax.all_gather(ln1_gain, "fsdp", axis=0, tiled=True),
        lax.all_gather(w_up, "fsdp", axis=0, tiled=True),
        lax.all_gather(w_down, "fsdp", axis=0, tiled=True),
        lax.all_gather(ln2_gain, "fsdp", axis=0, tiled=True),
    )
    again_wq, again_wk, again_wv, again_wo, again_g1, again_wup, again_wdown, again_g2 = (
        again_weights
    )
    residual_grad, grad_g2, grad_s2 = norm_back(
        summary_grad, first_rows(normed_two), first_rows(inverse_two), again_g2
    )
    down_grad = residual_grad.astype(jnp.bfloat16)
    activated_cls = first_rows(activated)
    act_grad = contract(down_grad, again_wdown, 1, 1)
    gelu_value, gelu_pull = jax.vjp(partial(jax.nn.gelu, approximate=False), first_rows(up_pre))
    up_grad = gelu_pull(act_grad)[0].astype(jnp.bfloat16)
    hidden_cls = first_rows(hidden_low)
    hidden_grad = contract(up_grad, again_wup, 1, 1) + residual_grad
    first_grad, grad_g1, grad_s1 = norm_back(
        hidden_grad, first_rows(normed_one), first_rows(inverse_one), again_g1
    )
    attend_grad = first_grad.astype(jnp.bfloat16)
    context_cls = first_rows(context)
    context_grad = (
        contract(attend_grad, again_wo, 1, 1).astype(jnp.bfloat16).reshape(sentences, HEADS, HEAD)
    )
    query_cls = query_heads[:, 0]
    cls_scores = (
        jnp.einsum("bhd,bkhd->bhk", query_cls, key_heads, preferred_element_type=jnp.float32)
        * score_factor
    )
    cls_scores = jnp.where(valid_mask[:, None, :], cls_scores, MASK_FLOOR)
    cls_probs = jnp.exp(cls_scores - row_peak[:, :, 0]) / totals[:, :, 0]
    prob_grad = jnp.einsum(
        "bhd,bkhd->bhk", context_grad, value_heads, preferred_element_type=jnp.float32
    )
    score_grad = (
        cls_probs * (prob_grad - jnp.sum(cls_probs * prob_grad, axis=-1, keepdims=True))
    ).astype(jnp.bfloat16)
    query_grad = (
        (
            jnp.einsum("bhk,bkhd->bhd", score_grad, key_heads, preferred_element_type=jnp.float32)
            * score_factor
        )
        .astype(jnp.bfloat16)
        .reshape(sentences, model_width)
    )
    key_grad = (
        (
            jnp.einsum("bhk,bhd->bkhd", score_grad, query_cls, preferred_element_type=jnp.float32)
            * score_factor
        )
        .astype(jnp.bfloat16)
        .reshape(tokens, model_width)
    )
    value_grad = (
        jnp.einsum(
            "bhk,bhd->bkhd",
            cls_probs.astype(jnp.bfloat16),
            context_grad,
            preferred_element_type=jnp.float32,
        )
        .astype(jnp.bfloat16)
        .reshape(tokens, model_width)
    )
    embedded_cls = first_rows(embedded)
    grad_wkey = contract(embedded, key_grad, 0, 0)
    grad_wvalue = contract(embedded, value_grad, 0, 0)
    grad_bvalue = jnp.sum(value_grad, axis=0, dtype=jnp.float32)
    row_grads = contract(key_grad, again_wk, 1, 1) + contract(value_grad, again_wv, 1, 1)
    summary_extra = contract(query_grad, again_wq, 1, 1) + first_grad
    row_grads = (
        row_grads.reshape(sentences, length, model_width)
        .at[:, 0]
        .add(summary_extra)
        .reshape(tokens, model_width)
    )
    outgoing = jnp.zeros((owners * capacity, model_width), jnp.float32).at[slot_of].set(row_grads)
    incoming = lax.all_to_all(
        lax.all_to_all(
            outgoing.reshape(dp_count, fsdp_count, capacity, model_width).astype(jnp.bfloat16),
            "dp",
            split_axis=0,
            concat_axis=0,
            tiled=True,
        ),
        "fsdp",
        split_axis=1,
        concat_axis=1,
        tiled=True,
    ).astype(jnp.float32)
    incoming = jnp.where(
        present.reshape(owners * capacity)[:, None],
        incoming.reshape(owners * capacity, model_width),
        0.0,
    )
    table_grad = (
        jnp.zeros((vocab_rows, model_width), jnp.float32)
        .at[local_rows.reshape(owners * capacity)]
        .add(incoming)
    )
    grad_wquery = contract(embedded_cls, query_grad, 0, 0)
    grad_bquery = jnp.sum(query_grad, axis=0, dtype=jnp.float32)
    grad_wout = contract(context_cls, attend_grad, 0, 0)
    grad_bout = jnp.sum(attend_grad, axis=0, dtype=jnp.float32)
    grad_wup = contract(hidden_cls, up_grad, 0, 0)
    grad_bup = jnp.sum(up_grad, axis=0, dtype=jnp.float32)
    grad_wdown = contract(activated_cls, down_grad, 0, 0)
    grad_bdown = jnp.sum(down_grad, axis=0, dtype=jnp.float32)
    owned_grads = (
        lax.psum_scatter(
            grad_wquery.astype(jnp.bfloat16), "fsdp", scatter_dimension=0, tiled=True
        ).astype(jnp.float32),
        lax.psum_scatter(
            grad_bquery.astype(jnp.bfloat16), "fsdp", scatter_dimension=0, tiled=True
        ).astype(jnp.float32),
        lax.psum_scatter(
            grad_wkey.astype(jnp.bfloat16), "fsdp", scatter_dimension=0, tiled=True
        ).astype(jnp.float32),
        lax.psum_scatter(
            grad_wvalue.astype(jnp.bfloat16), "fsdp", scatter_dimension=0, tiled=True
        ).astype(jnp.float32),
        lax.psum_scatter(
            grad_bvalue.astype(jnp.bfloat16), "fsdp", scatter_dimension=0, tiled=True
        ).astype(jnp.float32),
        lax.psum_scatter(
            grad_wout.astype(jnp.bfloat16), "fsdp", scatter_dimension=0, tiled=True
        ).astype(jnp.float32),
        lax.psum_scatter(
            grad_bout.astype(jnp.bfloat16), "fsdp", scatter_dimension=0, tiled=True
        ).astype(jnp.float32),
        lax.psum_scatter(
            grad_g1.astype(jnp.bfloat16), "fsdp", scatter_dimension=0, tiled=True
        ).astype(jnp.float32),
        lax.psum_scatter(
            grad_s1.astype(jnp.bfloat16), "fsdp", scatter_dimension=0, tiled=True
        ).astype(jnp.float32),
        lax.psum_scatter(
            grad_wup.astype(jnp.bfloat16), "fsdp", scatter_dimension=0, tiled=True
        ).astype(jnp.float32),
        lax.psum_scatter(
            grad_bup.astype(jnp.bfloat16), "fsdp", scatter_dimension=0, tiled=True
        ).astype(jnp.float32),
        lax.psum_scatter(
            grad_wdown.astype(jnp.bfloat16), "fsdp", scatter_dimension=0, tiled=True
        ).astype(jnp.float32),
        lax.psum_scatter(
            grad_bdown.astype(jnp.bfloat16), "fsdp", scatter_dimension=0, tiled=True
        ).astype(jnp.float32),
        lax.psum_scatter(
            grad_g2.astype(jnp.bfloat16), "fsdp", scatter_dimension=0, tiled=True
        ).astype(jnp.float32),
        lax.psum_scatter(
            grad_s2.astype(jnp.bfloat16), "fsdp", scatter_dimension=0, tiled=True
        ).astype(jnp.float32),
    )
    summed = (
        lax.psum(owned_grads[0].astype(jnp.bfloat16), "dp").astype(jnp.float32),
        lax.psum(owned_grads[1].astype(jnp.bfloat16), "dp").astype(jnp.float32),
        lax.psum(owned_grads[2].astype(jnp.bfloat16), "dp").astype(jnp.float32),
        lax.psum(owned_grads[3].astype(jnp.bfloat16), "dp").astype(jnp.float32),
        lax.psum(owned_grads[4].astype(jnp.bfloat16), "dp").astype(jnp.float32),
        lax.psum(owned_grads[5].astype(jnp.bfloat16), "dp").astype(jnp.float32),
        lax.psum(owned_grads[6].astype(jnp.bfloat16), "dp").astype(jnp.float32),
        lax.psum(owned_grads[7].astype(jnp.bfloat16), "dp").astype(jnp.float32),
        lax.psum(owned_grads[8].astype(jnp.bfloat16), "dp").astype(jnp.float32),
        lax.psum(owned_grads[9].astype(jnp.bfloat16), "dp").astype(jnp.float32),
        lax.psum(owned_grads[10].astype(jnp.bfloat16), "dp").astype(jnp.float32),
        lax.psum(owned_grads[11].astype(jnp.bfloat16), "dp").astype(jnp.float32),
        lax.psum(owned_grads[12].astype(jnp.bfloat16), "dp").astype(jnp.float32),
        lax.psum(owned_grads[13].astype(jnp.bfloat16), "dp").astype(jnp.float32),
        lax.psum(owned_grads[14].astype(jnp.bfloat16), "dp").astype(jnp.float32),
    )
    return (
        layer_out,
        loss_value,
        table_grad,
        summed[0],
        summed[1],
        summed[2],
        summed[3],
        summed[4],
        summed[5],
        summed[6],
        summed[7],
        summed[8],
        summed[9],
        summed[10],
        summed[11],
        summed[12],
        summed[13],
        summed[14],
    )


CORES = 2
PLANES = 4
LINES = 4
CHIPS = PLANES * LINES
DEVICES = CORES * CHIPS
CAPACITY = 48
GROUPS = 3
PAD = 16
TOKENS = 768
WIDTH = 768
WIDE = 3072
VOCAB_ROWS = 1024
PAIR_ROWS = HEADS * PAD
SLOT_ROWS = DEVICES * PAD
LONG = 64
BLOCK = 256
MESH = pl.DeviceIdType.MESH
LOW = jnp.bfloat16
FULL = jnp.float32
VMEM_LIMIT = 62 * 1024 * 1024

INPUTS = ["table", "token_ids", "lens", "slots", "langs"]
INPUTS += ["wq", "bq", "wk", "wv", "bv", "wo", "bo", "g1", "s1", "wup", "bup", "wdown", "bdown"]
INPUTS += ["g2", "s2"]
OUTPUTS = ["layer_out", "table_grad", "g_wq", "g_wk", "g_wv", "g_wo", "g_wup", "g_wdown"]
OUTPUTS += ["g_small", "loss"]


def place():
    core = lax.axis_index("dp")
    chip = lax.axis_index("fsdp")
    along_x = chip + 1 - 2 * (chip % 2)
    along_y = chip + 2 - 4 * ((chip // 2) % 2)
    first = along_x + core * (along_y - along_x)
    second = along_y + core * (along_x - along_y)
    return core, chip, first, second


def greet():
    core, chip, _, _ = place()
    me = core * CHIPS + chip
    barrier = pltpu.get_barrier_semaphore()

    def signal(step):
        other = lax.rem(me + step, DEVICES)
        pl.semaphore_signal(
            barrier,
            inc=1,
            device_id=(lax.div(other, CHIPS), lax.rem(other, CHIPS)),
            device_id_type=MESH,
        )

    every(1, DEVICES, signal)


def enter():
    pl.semaphore_wait(pltpu.get_barrier_semaphore(), DEVICES - 1)


def remote(source, target, send_sem, recv_sem, core, chip):
    return pltpu.make_async_remote_copy(
        src_ref=source,
        dst_ref=target,
        send_sem=send_sem,
        recv_sem=recv_sem,
        device_id=(core, chip),
        device_id_type=MESH,
    )


def every(start, stop, act):
    def step(index, carry):
        act(index)
        return carry

    lax.fori_loop(start, stop, step, 0)


def weight_steps(piece, many, send, recv):
    core, chip, first, second = place()
    plane, line = chip // LINES, chip % LINES
    line_first, line_second = first % LINES, second % LINES
    line_far = line_first + line_second - line
    is_low, is_high = plane > 0, plane < PLANES - 1

    def copy(send_index, recv_index, at, to_core, to_chip, carried=core):
        part = piece(at, carried)
        return remote(part, part, send.at[send_index], recv.at[recv_index], to_core, to_chip)

    def up(at_plane):
        return copy(at_plane, at_plane, at_plane * LINES + line, core, chip + LINES)

    def down(at_plane, index):
        return copy(index, at_plane, at_plane * LINES + line, core, chip - LINES)

    def side(at_plane, base, at_line, target):
        return copy(5, base + at_plane, at_plane * LINES + at_line, core, target)

    def across(at_plane, at_line):
        return copy(6, 17, at_plane * LINES + at_line, 1 - core, chip)

    def all_of(count, send_index, recv_index):
        part = many(count)
        return remote(part, part, send.at[send_index], recv.at[recv_index], 1 - core, chip)

    def begin():
        pl.when(is_high)(lambda: up(plane).start())
        pl.when(is_low)(lambda: down(plane, PLANES).start())
        side(plane, 5, line, first).start()
        side(plane, 9, line, second).start()

    def at_distance(distance, act):
        if distance == 0:
            act(plane, None)
            return
        pl.when(plane >= distance)(lambda: act(plane - distance, True))
        pl.when(plane + distance < PLANES)(lambda: act(plane + distance, False))

    def chain(distance):
        def act(at_plane, from_low):
            if from_low:
                up(at_plane).wait_recv()
                pl.when(is_high)(lambda: up(at_plane).start())
            else:
                down(at_plane, at_plane).wait_recv()
                pl.when(is_low)(lambda: down(at_plane, at_plane).start())
            side(at_plane, 5, line, first).start()
            side(at_plane, 9, line, second).start()
            across(at_plane, line).start()

        return partial(at_distance, distance, act)

    def near(distance):
        def act(at_plane, from_low):
            side(at_plane, 5, line_first, first).wait_recv()
            side(at_plane, 13, line_first, second).start()
            across(at_plane, line_first).start()

        return partial(at_distance, distance, act)

    def far(distance):
        def act(at_plane, from_low):
            side(at_plane, 9, line_second, second).wait_recv()
            across(at_plane, line_second).start()
            side(at_plane, 13, line_far, second).wait_recv()
            across(at_plane, line_far).start()

        return partial(at_distance, distance, act)

    def finish():
        all_of(15, 6, 17).wait_recv()

    def drain():
        def sent(index):
            copy(index, index, chip, 1 - core, chip).wait_send()

        for at_plane in range(PLANES):
            pl.when((plane >= at_plane) & is_high)(partial(sent, at_plane))
            pl.when((plane < at_plane) & is_low)(partial(sent, at_plane))
        pl.when(is_low)(partial(sent, PLANES))
        all_of(12, 5, 17).wait_send()
        all_of(15, 6, 17).wait_send()

    moves = [chain(1), near(0), chain(2), near(1), chain(3), far(0)]
    moves += [near(2), far(1), near(3), far(2), far(3)]
    return begin, moves, finish, drain


def gather_steps(buffer, send, recv):
    core, chip, first, second = place()
    plane, line = chip // LINES, chip % LINES
    line_first, line_second = first % LINES, second % LINES
    line_far = line_first + line_second - line
    half = buffer.shape[-1] // 2
    columns = pl.ds(pl.multiple_of(core * half, 128), half)
    others = pl.ds(pl.multiple_of((1 - core) * half, 128), half)

    def copy(index, part, to_core, to_chip):
        return remote(part, part, send.at[index], recv.at[index], to_core, to_chip)

    def own(at):
        return buffer.at[at, plane, line]

    def chip_part(at_plane, at_line, which):
        return buffer.at[:, at_plane, at_line, :, which]

    def line_part(at_line, which):
        return buffer.at[:, :, at_line, :, which]

    def start():
        copy(0, own(core), 1 - core, chip).start()

    def planes():
        copy(0, own(1 - core), 1 - core, chip).wait_recv()
        for step in range(1, PLANES):
            part = chip_part(plane, line, columns)
            copy(step, part, core, (chip + LINES * step) % CHIPS).start()

    def sides():
        for step in range(1, PLANES):
            part = chip_part((plane + PLANES - step) % PLANES, line, columns)
            copy(step, part, core, chip).wait_recv()
        copy(4, line_part(line, columns), core, first).start()
        copy(5, line_part(line, columns), core, second).start()
        for step in range(1, PLANES):
            part = chip_part((plane + PLANES - step) % PLANES, line, columns)
            copy(6 + step, part, 1 - core, chip).start()

    def corner():
        copy(4, line_part(line_first, columns), core, first).wait_recv()
        copy(6, line_part(line_first, columns), core, second).start()
        copy(10, line_part(line_first, columns), 1 - core, chip).start()
        copy(5, line_part(line_second, columns), core, second).wait_recv()
        copy(11, line_part(line_second, columns), 1 - core, chip).start()

    def last():
        copy(6, line_part(line_far, columns), core, second).wait_recv()
        copy(12, line_part(line_far, columns), 1 - core, chip).start()

    def finish():
        for step in range(1, PLANES):
            part = chip_part((plane + PLANES - step) % PLANES, line, others)
            copy(6 + step, part, 1 - core, chip).wait_recv()
        copy(10, line_part(line_second, others), 1 - core, chip).wait_recv()
        copy(11, line_part(line_first, others), 1 - core, chip).wait_recv()
        copy(12, line_part(line_far, others), 1 - core, chip).wait_recv()

    def drain():
        copy(0, own(core), 1 - core, chip).wait_send()
        for index in [1, 2, 3, 7, 8, 9]:
            copy(index, chip_part(plane, line, columns), 1 - core, chip).wait_send()
        for index in [4, 5, 6, 10, 11, 12]:
            copy(index, line_part(line, columns), 1 - core, chip).wait_send()

    return [start, planes, sides, corner, last, finish], drain


def iota(shape, axis):
    return lax.broadcasted_iota(jnp.int32, shape, axis)


def over(numbers, power):
    return lax.shift_right_arithmetic(numbers, jnp.full_like(numbers, power.bit_length() - 1))


def within(numbers, power):
    return numbers & (power - 1)


def as_column(row):
    parts = []
    for start in range(0, row.shape[1], 128):
        tile = jnp.broadcast_to(row[:, start : start + 128], (128, 128))
        parts.append(jnp.transpose(tile)[:, 0:1])
    return jnp.concatenate(parts, axis=0)


def as_row(column):
    parts = []
    for start in range(0, column.shape[0], 128):
        tile = jnp.broadcast_to(column[start : start + 128, :], (128, 128))
        parts.append(jnp.transpose(tile)[0:1, :])
    return jnp.concatenate(parts, axis=1)


def dot(left_side, right_side):
    return contract(left_side, right_side, 1, 0)


def dot_turned(left_side, right_side):
    return contract(left_side, right_side, 1, 1)


def norm_parts(inputs):
    centered = inputs - jnp.mean(inputs, axis=-1, keepdims=True)
    inverse = lax.rsqrt(jnp.mean(centered * centered, axis=-1, keepdims=True) + EPSILON)
    return centered * inverse, inverse


def norm_back_parts(grad_output, normed, inverse, ln_gain):
    grad_normed = grad_output * ln_gain
    first_term = jnp.mean(grad_normed, axis=-1, keepdims=True)
    second_term = jnp.mean(grad_normed * normed, axis=-1, keepdims=True)
    return (
        inverse * (grad_normed - first_term - normed * second_term),
        jnp.sum(grad_output * normed, axis=0, keepdims=True),
        jnp.sum(grad_output, axis=0, keepdims=True),
    )


def erf_parts(inputs):
    decay = jnp.exp(-0.5 * inputs * inputs)
    share = 1.0 / (1.0 + jnp.abs(inputs) * (0.3275911 * 0.5**0.5))
    terms = [1.061405429, -1.453152027, 1.421413741, -0.284496736, 0.254829592]
    series = 0.5 * terms[0]
    for term in terms[1:]:
        series = series * share + 0.5 * term
    tail = series * share * decay
    return jnp.where(inputs >= 0.0, 1.0 - tail, tail), decay


def gelu_parts(inputs):
    below, decay = erf_parts(inputs)
    return inputs * below, below + inputs * decay * ((2.0 * 3.141592653589793) ** -0.5)


def gelu(inputs):
    return inputs * erf_parts(inputs)[0]


def layer_kernel(names, *refs):
    r = SimpleNamespace(**dict(zip(names, refs, strict=True)))
    core, chip, _, _ = place()
    me = core * CHIPS + chip
    here = (core, chip // LINES, chip % LINES)
    scale = HEAD ** (-0.5)
    depth, deep = WIDTH // CHIPS, WIDE // CHIPS
    sentences = TOKENS // LONG

    for j in range(TOKENS // 128):
        r.ids[j : j + 1, :] = jnp.concatenate(
            [r.token_ids[2 * j : 2 * j + 1, :], r.token_ids[2 * j + 1 : 2 * j + 2, :]], axis=1
        )
    r.ids[TOKENS // 128 : 8, :] = jnp.zeros((8 - TOKENS // 128, 128), jnp.int32)
    greet()
    ahead = (iota((TOKENS, TOKENS), 0) < iota((TOKENS, TOKENS), 1)).astype(LOW)
    r.embedded[...] = ahead
    mine = pl.ds(pl.multiple_of(chip * depth, 16), depth)
    for index, shard in enumerate([r.wq, r.wk, r.wv, r.wo]):
        r.wa[mine, index * WIDTH : (index + 1) * WIDTH] = shard[...]
    r.wb[mine, :] = r.wup[...]
    r.wc[pl.ds(pl.multiple_of(chip * deep, 16), deep), :] = r.wdown[...]
    r.every_ids[me] = r.ids[...]
    enter()

    def peer(step):
        other = lax.rem(me + step, DEVICES)
        return other, lax.div(other, CHIPS), lax.rem(other, CHIPS)

    def ids_copy(step):
        other, to_core, to_chip = peer(step)
        return remote(r.ids, r.every_ids.at[me], r.one_send.at[0], r.one_recv.at[0], to_core, to_chip)

    def all_but_one(ref, index):
        part = ref.at[0 : DEVICES - 1]
        return remote(part, part, r.one_send.at[index], r.one_recv.at[index], 1 - core, chip)

    every(1, DEVICES, lambda step: ids_copy(step).start())

    def block(ref, rows, columns):
        def piece(at, carried):
            return ref.at[
                pl.ds(pl.multiple_of(at * rows, 16), rows),
                pl.ds(pl.multiple_of(carried * columns, 128), columns),
            ]

        def many(count):
            return ref.at[0 : count * rows, 0:columns]

        return piece, many

    begin_a, moves_a, finish_a, drain_a = weight_steps(
        *block(r.wa, depth, 2 * WIDTH), r.weight_send.at[0], r.weight_recv.at[0]
    )
    begin_b, moves_b, finish_b, drain_b = weight_steps(
        *block(r.wb, depth, WIDE // 2), r.weight_send.at[1], r.weight_recv.at[1]
    )
    begin_c, moves_c, finish_c, drain_c = weight_steps(
        *block(r.wc, deep, WIDTH // 2), r.weight_send.at[2], r.weight_recv.at[2]
    )
    begin_a()
    begin_b()

    def move(*steps):
        for moves, first_step in steps:
            moves[first_step]()
            moves[first_step + 1]()

    all_but_one(r.every_ids, 0).wait_recv()
    all_ids = jnp.concatenate([r.every_ids[:, j, :] for j in range(TOKENS // 128)], axis=1)
    all_owner = over(all_ids, VOCAB_ROWS)
    asked = all_owner == me
    ranks = dot(asked.astype(LOW), r.embedded[...])
    r.rank[...] = jnp.where(asked, ranks, -1.0)
    local_row = (all_ids - all_owner * VOCAB_ROWS + 1).astype(FULL)
    r.code[...] = local_row + (over(iota((DEVICES, TOKENS), 1), LONG) * 2048).astype(FULL)

    quarter_size = DEVICES // 4

    def rows_copy(other, quarter):
        return remote(
            r.rows.at[:, pl.ds(pl.multiple_of(other * PAD, 16), PAD), :],
            r.replies.at[:, pl.ds(pl.multiple_of(me * PAD, 16), PAD), :],
            r.rows_send.at[quarter],
            r.rows_recv.at[quarter],
            lax.div(other, CHIPS),
            lax.rem(other, CHIPS),
        )

    def rows_of(quarter):
        count = quarter_size - 1 if quarter == 3 else quarter_size
        part = r.replies.at[:, 0 : count * PAD, :]
        return remote(
            part, part, r.rows_send.at[quarter], r.rows_recv.at[quarter], 1 - core, chip
        )

    def pick(source):
        rank = r.rank[pl.ds(source, 1), :]
        code = r.code[pl.ds(source, 1), :]
        here_at = iota((CAPACITY, TOKENS), 0).astype(FULL) == rank
        found = jnp.sum(jnp.where(here_at, code, 0.0), axis=1, keepdims=True)
        sent = jnp.floor(found * (1.0 / 2048))
        row = found - sent * 2048.0 - 1.0
        chosen = (iota((CAPACITY, VOCAB_ROWS), 1).astype(FULL) == row).astype(LOW)
        at = pl.ds(pl.multiple_of(source * PAD, 16), PAD)
        source_sent = sent + (source * PAD).astype(FULL)
        for group in range(GROUPS):
            part = slice(group * PAD, (group + 1) * PAD)
            r.chosen[group, at, :] = chosen[part]
            r.found[group, at, 0:1] = row[part]
            r.found[group, at, 1:2] = source_sent[part]

    def quarter_rows(quarter):
        now = lax.rem(lax.div(me, quarter_size) + 1 + quarter, 4)

        def pick_two(index):
            pick(now * quarter_size + 2 * index)
            pick(now * quarter_size + 2 * index + 1)

        every(0, quarter_size // 2, pick_two)
        span = pl.ds(pl.multiple_of(now * quarter_size * PAD, 128), quarter_size * PAD)
        for start in range(0, WIDTH, BLOCK):
            lanes = slice(start, start + BLOCK)
            picked = r.chosen[:, span, :].reshape(GROUPS * quarter_size * PAD, VOCAB_ROWS)
            found_rows = dot(picked, r.table[:, lanes]).astype(LOW)
            r.rows[:, span, lanes] = found_rows.reshape(GROUPS, quarter_size * PAD, BLOCK)

        def send(index):
            other = now * quarter_size + lax.rem(lax.rem(me, quarter_size) + index, quarter_size)
            rows_copy(other, quarter).start()

        every(lax.div(quarter, 3), quarter_size, send)
        pl.when(quarter == 0)(partial(move, (moves_a, 0)))
        pl.when(quarter == 1)(partial(move, (moves_b, 0)))
        pl.when(quarter == 2)(partial(move, (moves_a, 2)))
        pl.when(quarter == 3)(partial(move, (moves_b, 2)))

    every(0, 4, quarter_rows)
    begin_c()
    own_at = pl.ds(pl.multiple_of(me * PAD, 16), PAD)
    r.replies[:, own_at, :] = r.rows[:, own_at, :]

    move((moves_a, 4))

    small_here = pl.ds(pl.multiple_of(chip * 128, 128), 128)
    lines = [r.bq, r.bv, r.bo, r.g1, r.s1, r.bdown, r.g2, r.s2]
    lines = [line[...].reshape(1, depth).astype(FULL) for line in lines]
    up_line = r.bup[...].reshape(1, deep).astype(FULL)
    lines += [up_line[:, part * depth : (part + 1) * depth] for part in range(deep // depth)]
    lines.append(jnp.zeros((PAD - len(lines), depth), FULL))
    own_small = jnp.concatenate(lines, axis=0)
    own_small = jnp.concatenate([own_small, jnp.zeros((PAD, 128 - depth), FULL)], axis=1)
    r.smalls[:, small_here] = own_small.astype(LOW)

    def small_copy(step):
        part = r.smalls.at[:, small_here]
        to_chip = lax.rem(chip + step, CHIPS)
        return remote(part, part, r.small_send.at[0], r.small_recv.at[0], core, to_chip)

    def all_smalls():
        part = r.smalls.at[:, 0 : (CHIPS - 1) * 128]
        return remote(part, part, r.small_send.at[0], r.small_recv.at[0], 1 - core, chip)

    every(1, CHIPS, lambda step: small_copy(step).start())
    move((moves_b, 4))

    own_row = jnp.concatenate([r.ids[j : j + 1, :] for j in range(TOKENS // 128)], axis=1)
    owner_row = over(own_row, VOCAB_ROWS).astype(FULL)
    owner_col = as_column(owner_row)
    earlier = (owner_row == owner_col) & (iota((TOKENS, TOKENS), 1) < iota((TOKENS, TOKENS), 0))
    own_rank = jnp.sum(earlier.astype(FULL), axis=1, keepdims=True)
    own_group = jnp.floor(own_rank * (1.0 / PAD))
    own_slot = own_group * SLOT_ROWS + owner_col * PAD + (own_rank - own_group * PAD)
    r.slot_col[...] = own_slot
    r.slot_line[0:1, :] = as_row(own_slot)
    move((moves_a, 6), (moves_c, 0))

    at_sent = over(iota((1, TOKENS), 1), LONG)
    lens = jnp.concatenate(
        [r.lens[...].reshape(1, sentences).astype(FULL), jnp.zeros((1, PAD - sentences), FULL)],
        axis=1,
    )
    spread_lens = dot(
        jnp.broadcast_to(lens, (8, PAD)).astype(LOW),
        (iota((PAD, TOKENS), 0) == over(iota((PAD, TOKENS), 1), LONG)).astype(LOW),
    )[0:1]
    valid_row = ((iota((1, TOKENS), 1) - at_sent * LONG).astype(FULL) < spread_lens).astype(FULL)
    r.valid_line[0:1, :] = valid_row
    r.valid_col[...] = as_column(valid_row)
    half_block = BLOCK // 2
    stacked_shape = (4 * half_block, half_block)
    same = within(over(iota(stacked_shape, 0), LONG), 2) == over(iota(stacked_shape, 1), LONG)
    r.block_bias[...] = jnp.where(same, 0.0, MASK_FLOOR)
    r.valid_bias[0:1, :] = (1.0 - valid_row) * MASK_FLOOR

    slots = r.slots[...].reshape(1, DEVICES * sentences)
    gap = jnp.full((1, PAD - sentences), -2, jnp.int32)
    slot_line = jnp.concatenate(
        [
            part
            for device in range(DEVICES)
            for part in (slots[:, device * sentences : (device + 1) * sentences], gap)
        ],
        axis=1,
    )
    side_line = within(slot_line, 2) + jnp.where(slot_line < 0, 8, 0)
    pair_line = over(slot_line, 2)
    pairs = r.langs.shape[0]
    lang_line = r.langs[...].reshape(1, pairs).astype(FULL)
    lang_line = jnp.concatenate([lang_line, jnp.full((1, -pairs % 128), -1.0, FULL)], axis=1)
    lang_col = as_column(lang_line)
    same_lang = jnp.sum(jnp.where(lang_col == lang_line, 1.0, 0.0), axis=1, keepdims=True)
    per_pair = 1.0 / (2.0 * LANGS * same_lang)
    at_pair = iota((lang_line.shape[1], SLOT_ROWS), 0) == pair_line
    weight_line = jnp.sum(jnp.where(at_pair, per_pair, 0.0), axis=0, keepdims=True)
    r.pairs[0:1, :] = weight_line
    r.pairs[1:2, :] = pair_line.astype(FULL)
    r.pairs[2:3, :] = side_line.astype(FULL)
    r.pairs_col[:, 0:1] = as_column(weight_line)
    r.pairs_col[:, 1:2] = as_column(pair_line.astype(FULL))
    r.pairs_col[:, 2:3] = as_column(side_line.astype(FULL))
    move((moves_b, 6), (moves_c, 2))

    all_smalls().wait_recv()
    smalls = r.smalls[...].astype(FULL)
    r.vectors[:, 0:WIDTH] = jnp.concatenate(
        [smalls[:, at * 128 : at * 128 + depth] for at in range(CHIPS)], axis=1
    )
    r.up_bias[0:1, :] = jnp.concatenate(
        [
            smalls[8 + part : 9 + part, at * 128 : at * 128 + depth]
            for at in range(CHIPS)
            for part in range(deep // depth)
        ],
        axis=1,
    )

    def vector(index):
        return r.vectors[index : index + 1, :]

    r.qkv_bias[0:1, 0:WIDTH] = vector(0)
    r.qkv_bias[0:1, WIDTH : 2 * WIDTH] = jnp.zeros((1, WIDTH), FULL)
    r.qkv_bias[0:1, 2 * WIDTH : 3 * WIDTH] = vector(1)

    move((moves_a, 8), (moves_b, 8), (moves_c, 4))

    def first_row(source):
        code = jnp.where(r.rank[pl.ds(source, 1), :] >= 0.0, r.code[pl.ds(source, 1), :], 0.0)
        at_first = iota((PAD, TOKENS), 1) == iota((PAD, TOKENS), 0) * LONG
        found = jnp.sum(jnp.where(at_first, code, 0.0), axis=1, keepdims=True)
        row = found - jnp.floor(found * (1.0 / 2048)) * 2048.0 - 1.0
        r.found[GROUPS, pl.ds(pl.multiple_of(source * PAD, 16), PAD), 0:1] = row

    every(0, DEVICES, first_row)
    for group in range(GROUPS + 1):
        named = as_row(r.found[group, :, 0:1])
        by_row = iota((VOCAB_ROWS, SLOT_ROWS), 0).astype(FULL) == named
        r.by_row[:, group * SLOT_ROWS : (group + 1) * SLOT_ROWS] = by_row.astype(LOW)

    def order(tile):
        at = pl.ds(pl.multiple_of(tile * BLOCK, BLOCK), BLOCK)
        lanes = iota((BLOCK, GROUPS * SLOT_ROWS), 1).astype(FULL)
        r.qkv[at, 0 : GROUPS * SLOT_ROWS] = (r.slot_col[at, :] == lanes).astype(LOW)

    every(0, TOKENS // BLOCK, order)
    for group in range(GROUPS):
        slot_at = iota((SLOT_ROWS, TOKENS), 0) + group * SLOT_ROWS
        named = (slot_at.astype(FULL) == r.slot_line[0:1, :]).astype(LOW)
        r.slot_hot[group] = named
    moves_a[10]()
    moves_b[10]()
    finish_a()
    for quarter in range(4):
        rows_of(quarter).wait_recv()

    def embed(tile):
        at = pl.ds(pl.multiple_of(tile * BLOCK, BLOCK), BLOCK)
        replies = r.replies[:, :, at].reshape(GROUPS * SLOT_ROWS, BLOCK)
        r.embedded[:, at] = dot(r.qkv[:, 0 : GROUPS * SLOT_ROWS], replies).astype(LOW)

    every(0, WIDTH // BLOCK, embed)

    def project(tile):
        at = pl.ds(pl.multiple_of(tile * BLOCK, BLOCK), BLOCK)
        r.qkv[:, at] = (dot(r.embedded[...], r.wa[:, at]) + r.qkv_bias[0:1, at]).astype(LOW)

    move((moves_c, 6))
    every(0, 9, project)

    row_sent = within(iota((PAIR_ROWS, WIDTH), 0), PAD)
    row_head = over(iota((PAIR_ROWS, WIDTH), 0), PAD)
    lane_block = over(iota((PAIR_ROWS, WIDTH), 1), HEAD)
    in_head = row_head == lane_block
    seen = (row_sent == lane_block) & (r.valid_line[0:1, :] > 0.0)
    firsts = (iota((PAD, TOKENS), 1) == iota((PAD, TOKENS), 0) * LONG).astype(LOW)
    real_row = iota((PAD, 1), 0) < sentences

    def spread(rows):
        return jnp.where(in_head, jnp.concatenate([rows] * HEADS, axis=0), jnp.zeros((), LOW))

    def fold(tall):
        tall = jnp.where(in_head, tall, 0.0)
        return sum(tall[head * PAD : (head + 1) * PAD] for head in range(HEADS))

    keys, values = slice(WIDTH, 2 * WIDTH), slice(2 * WIDTH, 3 * WIDTH)
    embedded_cls = dot(firsts, r.embedded[...]).astype(LOW)
    query_cls = (dot(embedded_cls, r.wa[:, 0:WIDTH]) + vector(0)).astype(LOW)
    cls_scores = dot_turned(spread(query_cls), r.qkv[:, keys]) * scale
    cls_scores = jnp.where(seen, cls_scores, MASK_FLOOR)
    cls_peak = jnp.max(cls_scores, axis=1, keepdims=True)
    cls_exp = jnp.where(seen, jnp.exp(cls_scores - cls_peak), 0.0)
    cls_total = jnp.sum(cls_exp, axis=1, keepdims=True)
    cls_probs = cls_exp / jnp.where(cls_total > 0.0, cls_total, 1.0)
    probs_low = cls_probs.astype(LOW)
    r.probs[...] = cls_probs
    context_cls = fold(dot(probs_low, r.qkv[:, values])).astype(LOW)
    first_cls = (
        embedded_cls.astype(FULL)
        + dot(context_cls, r.wa[:, 3 * WIDTH : 4 * WIDTH])
        + vector(2)
    )
    normed_one, inverse_one = norm_parts(first_cls)
    r.normed_one[...] = normed_one
    hidden_cls = normed_one * vector(3) + vector(4)
    hidden_cls_low = hidden_cls.astype(LOW)
    early_here = r.early.at[here]
    early_here[:, 0:WIDTH] = hidden_cls_low
    early_here[:, WIDTH : 2 * WIDTH] = query_cls
    steps_u, drain_u = gather_steps(r.units, r.gather_send.at[0], r.gather_recv.at[0])
    steps_e, drain_e = gather_steps(r.early, r.gather_send.at[1], r.gather_recv.at[1])
    steps_d, drain_d = gather_steps(r.downs, r.gather_send.at[2], r.gather_recv.at[2])
    steps_a, drain_a2 = gather_steps(r.attends, r.gather_send.at[3], r.gather_recv.at[3])
    steps_q, drain_q = gather_steps(r.queries, r.gather_send.at[4], r.gather_recv.at[4])
    steps_e[0]()

    def attend(unit):
        rows = pl.ds(pl.multiple_of(unit * half_block, half_block), half_block)
        lane_head = over(iota((half_block, BLOCK), 1), HEAD)
        bias = r.block_bias[...] + r.valid_bias[0:1, rows]

        def part(which, lane):
            return r.qkv[rows, which * WIDTH + lane : which * WIDTH + lane + BLOCK]

        for lane in range(0, WIDTH, BLOCK):
            query = part(0, lane) * jnp.asarray(scale, LOW)
            key, value = part(1, lane), part(2, lane)
            stacked = jnp.concatenate(
                [jnp.where(lane_head == head, query, jnp.zeros((), LOW)) for head in range(4)],
                axis=0,
            )
            scores = dot_turned(stacked, key) + bias
            shifted = jnp.exp(scores - jnp.max(scores, axis=1, keepdims=True))
            probs = shifted * (1.0 / jnp.sum(shifted, axis=1, keepdims=True))
            mixed = dot(probs.astype(LOW), value)
            result = mixed[0:half_block]
            for head in range(1, 4):
                result = jnp.where(
                    lane_head == head, mixed[head * half_block : (head + 1) * half_block], result
                )
            r.context[rows, lane : lane + BLOCK] = result.astype(LOW)

    def open_tile(tile):
        at = pl.ds(pl.multiple_of(tile * BLOCK, BLOCK), BLOCK)
        attended = dot(r.context[at, :], r.wa[:, 3 * WIDTH : 4 * WIDTH]) + vector(2)
        normed, _ = norm_parts(r.embedded[at, :].astype(FULL) + attended)
        hidden = normed * vector(3) + vector(4)
        r.context[at, :] = hidden.astype(LOW)
        r.table_full[at, :] = hidden + vector(5)

    most = SLOT_ROWS
    rest_at = pl.ds(most, TOKENS - most)

    def up_product(part):
        at = pl.ds(pl.multiple_of(part * BLOCK, BLOCK), BLOCK)
        return dot(r.context[...], r.wb[:, at]) + r.up_bias[0:1, at]

    def feed_up(part, last=False):
        active = gelu(r.tile_up[...]).astype(LOW)
        if not last:
            r.tile_up[...] = up_product(part + 1)
        lanes = pl.ds(pl.multiple_of(lax.rem(part, 4) * BLOCK, BLOCK), BLOCK)
        r.chosen[lax.div(part, 4), :, lanes] = active[:most]
        rest = pl.ds(pl.multiple_of(lax.div(part, 6) * BLOCK, BLOCK), BLOCK)
        lanes = pl.ds(pl.multiple_of(lax.rem(part, 6) * BLOCK, BLOCK), BLOCK)
        r.slopes[rest, lanes] = active[most:]

    def feed_down(part):
        lanes = pl.ds(pl.multiple_of(part * BLOCK, BLOCK), BLOCK)
        total = r.table_full[0:most, lanes]
        for group in range(GROUPS):
            rows = slice(group * VOCAB_ROWS, (group + 1) * VOCAB_ROWS)
            total = total + dot(r.chosen[group], r.wc[rows, lanes])
        r.table_full[0:most, lanes] = total

    def feed_rest(part):
        lanes = pl.ds(pl.multiple_of(part * BLOCK, BLOCK), BLOCK)
        low_part = dot(r.slopes[0:BLOCK, :], r.wc[0 : WIDE // 2, lanes])
        high_part = dot(r.slopes[BLOCK : 2 * BLOCK, :], r.wc[WIDE // 2 :, lanes])
        r.table_full[rest_at, lanes] += low_part + high_part

    def layer_copy(tile):
        at = pl.ds(pl.multiple_of(tile * BLOCK, BLOCK), BLOCK)
        return pltpu.make_async_copy(r.context.at[at], r.layer_out.at[at], r.out_sem.at[tile])

    def close_tile(tile):
        at = pl.ds(pl.multiple_of(tile * BLOCK, BLOCK), BLOCK)
        normed, _ = norm_parts(r.table_full[at, :])
        out = normed * vector(6) + vector(7)
        r.context[at, :] = (out * r.valid_col[at, :]).astype(LOW)
        layer_copy(tile).start()

    finish_b()
    r.hidden_cls[...] = hidden_cls_low

    def up_part(part):
        at = pl.ds(pl.multiple_of(part * WIDTH, BLOCK), WIDTH)
        active, slope = gelu_parts(dot(r.hidden_cls[...], r.wb[:, at]) + r.up_bias[0:1, at])
        r.active_cls[:, at] = active.astype(LOW)
        r.slope_cls[:, at] = slope

    every(0, WIDE // WIDTH, up_part)
    steps_e[1]()

    def attend_step(unit):
        attend(unit)
        pl.when(unit == 1)(partial(move, (moves_c, 8)))
        pl.when(unit == 3)(moves_c[10])
        pl.when(unit == 4)(steps_e[2])

    every(0, 6, attend_step)
    finish_c()

    def pack_tall(target, first_row, act):
        def run(part):
            window = jnp.minimum(lax.div(part * 2 * depth, 128) * 128, WIDTH - BLOCK)
            shape = (BLOCK, BLOCK)
            lane = within(iota(shape, 1), 128)
            column = over(iota(shape, 1), 128) * depth + lane + (part * 2 * depth - window)
            select = ((iota(shape, 0) == column) & (lane < depth)).astype(LOW)
            taken = dot(r.tall[:, pl.ds(pl.multiple_of(window, 128), BLOCK)], select)

            def beside(low, high):
                return [
                    low[:, one * 128 : (one + 1) * 128]
                    + pltpu.roll(high[:, one * 128 : (one + 1) * 128], depth, 1)
                    for one in range(2)
                ]

            for half in range(CORES):
                base = half * PAIR_ROWS // 2
                both = beside(taken[base : base + 48], taken[base + 48 : base + 96])
                for one in range(2):
                    at = half * CHIPS + 2 * part + one
                    target[at, first_row : first_row + 48, :] = act(
                        2 * part + one, both[one]
                    ).astype(LOW)
            if first_row:
                left = beside(taken[PAIR_ROWS : PAIR_ROWS + PAD], taken[PAIR_ROWS + PAD :])
                for half in range(CORES):
                    for one in range(2):
                        target[half * CHIPS + 2 * part + one, 0:PAD, :] = left[one].astype(LOW)

        return run

    def pack_coefs(coefs):
        shape = (PAIR_ROWS, GROUPS * 128)
        folds = over(iota(shape, 0), PAD) + over(iota(shape, 1), 128) * PAD == within(
            iota(shape, 1), 128
        )
        lanes = contract(coefs, folds.astype(LOW), 0, 0).astype(LOW)
        total = None
        for group in range(GROUPS):
            part = dot(r.slot_hot[group], lanes[:, group * 128 : (group + 1) * 128])
            total = part if total is None else total + part
        return total.astype(LOW).reshape(DEVICES, PAD, 128)


    def down_part(part):
        at = pl.ds(pl.multiple_of(part * BLOCK, BLOCK), BLOCK)
        r.wide_cls[:, at] = dot(r.active_cls[...], r.wc[:, at])

    every(0, WIDTH // BLOCK, down_part)
    down_pre = r.wide_cls[:, 0:WIDTH] + vector(5)
    normed_two, inverse_two = norm_parts(hidden_cls + down_pre)
    summary = normed_two * vector(6) + vector(7)
    magnitude = jnp.sqrt(jnp.sum(summary * summary, axis=-1, keepdims=True) + EPSILON)
    unit = jnp.where(real_row, summary / magnitude, 0.0)
    r.units[here] = unit.astype(LOW)

    steps_u[0]()
    r.tall[0:PAIR_ROWS, :] = dot(probs_low, r.embedded[...]).astype(LOW)
    r.tall[PAIR_ROWS : PAIR_ROWS + PAD, :] = context_cls
    r.tall[PAIR_ROWS + PAD :, :] = embedded_cls
    pack_one = pack_tall(r.mail_one, PAD, lambda at, both: both)

    def pack_one_step(part):
        pack_one(part)
        pl.when(part == 0)(steps_u[1])
        pl.when(part == 4)(steps_u[2])

    every(0, CHIPS // 2, pack_one_step)
    r.mail_one[:, 64:80, :] = pack_coefs(probs_low)
    steps_u[3]()

    def post_one(box, got, index, step):
        other, to_core, to_chip = peer(step)
        remote(
            box.at[other], got.at[me], r.one_send.at[index], r.one_recv.at[index], to_core, to_chip
        ).start()

    def post(box, got, index):
        every(1, DEVICES, partial(post_one, box, got, index))
        got[me] = box[me]


    r.got_one[me] = r.mail_one[me]

    def open_step(tile):
        open_tile(tile)
        pl.when(tile == 0)(steps_e[3])
        pl.when(tile == 2)(steps_u[4])

    def feed_step(steps, part):
        feed_up(part)
        for index in range(3):
            step = 3 * part + index + 1
            pl.when(step < DEVICES)(partial(post_one, r.mail_one, r.got_one, 1, step))
        for index, step in steps:
            pl.when(part == index)(step)

    first_parts, parts = 6, WIDE // BLOCK
    every(0, TOKENS // BLOCK, open_step)
    r.tile_up[...] = up_product(0)
    every(0, first_parts, partial(feed_step, [(1, steps_u[5]), (2, steps_e[4]), (5, steps_e[5])]))

    units = r.units[...].reshape(SLOT_ROWS, WIDTH)
    weight_row, pair_row, side_row = r.pairs[0:1, :], r.pairs[1:2, :], r.pairs[2:3, :]

    def pair_scores(rows, pair_col, side_col):
        opposite = side_col + side_row == 1.0
        partner = opposite & (pair_col == pair_row)
        raw = SCORE_SCALE * dot_turned(rows, units)
        shifted = jnp.where(partner, raw - SCORE_SCALE * MARGIN_WIDTH, raw)
        return jnp.where(opposite, shifted, MASK_FLOOR), partner

    every_score, every_partner = pair_scores(
        units, r.pairs_col[:, 1:2], r.pairs_col[:, 2:3]
    )
    peak_row = jnp.max(every_score, axis=0, keepdims=True)
    log_row = peak_row + jnp.log(
        jnp.sum(jnp.exp(every_score - peak_row), axis=0, keepdims=True)
    )
    picked_row = jnp.sum(jnp.where(every_partner, every_score, 0.0), axis=0, keepdims=True)
    r.loss[...] = jnp.sum(weight_row * (log_row - picked_row), axis=1, keepdims=True)

    rows_here = pl.ds(pl.multiple_of(me * PAD, 16), PAD)
    own_score, own_partner = pair_scores(
        r.units[here], r.pairs_col[rows_here, 1:2], r.pairs_col[rows_here, 2:3]
    )
    own_partner = own_partner.astype(FULL)
    own_peak = jnp.max(own_score, axis=1, keepdims=True)
    own_exp = jnp.exp(own_score - own_peak)
    own_share = own_exp / jnp.sum(own_exp, axis=1, keepdims=True)
    by_row = (r.pairs_col[rows_here, 0:1] * (own_share - own_partner)).astype(LOW)
    by_column = (weight_row * (jnp.exp(own_score - log_row) - own_partner)).astype(LOW)
    unit_grad = SCORE_SCALE * (dot(by_row, units) + dot(by_column, units))
    along = jnp.sum(unit * unit_grad, axis=-1, keepdims=True)
    summary_grad = (unit_grad - unit * along) / magnitude

    residual_grad, grad_g2, grad_s2 = norm_back_parts(
        summary_grad, normed_two, inverse_two, vector(6)
    )
    down_grad = residual_grad.astype(LOW)
    r.downs[here] = down_grad
    steps_d[0]()
    r.hidden_cls[...] = down_grad

    def up_back(part):
        at = pl.ds(pl.multiple_of(part * WIDTH, BLOCK), WIDTH)
        act_grad = dot_turned(r.hidden_cls[...], r.wc[at, :])
        r.active_cls[:, at] = (act_grad * r.slope_cls[:, at]).astype(LOW)

    every(0, WIDE // WIDTH, up_back)
    steps_d[1]()

    def hidden_back(part):
        at = pl.ds(pl.multiple_of(part * BLOCK, BLOCK), BLOCK)
        r.wide_cls[:, at] = dot_turned(r.active_cls[...], r.wb[at, :])

    every(0, WIDTH // BLOCK, hidden_back)
    hidden_grad = r.wide_cls[:, 0:WIDTH] + residual_grad
    first_grad, grad_g1, grad_s1 = norm_back_parts(
        hidden_grad, r.normed_one[...], inverse_one, vector(3)
    )
    attend_grad = first_grad.astype(LOW)
    context_grad = dot_turned(attend_grad, r.wa[:, 3 * WIDTH : 4 * WIDTH]).astype(LOW)
    attend_here = r.attends.at[here]
    attend_here[:, 0:WIDTH] = attend_grad
    attend_here[:, WIDTH : 2 * WIDTH] = context_grad
    steps_a[0]()
    steps_d[2]()
    context_tall = spread(context_grad)
    probs = r.probs[...]
    prob_grad = dot_turned(context_tall, r.qkv[:, values])
    inner = jnp.sum(probs * prob_grad, axis=1, keepdims=True)
    score_grad = (probs * (prob_grad - inner)).astype(LOW)
    steps_a[1]()
    r.mail_two[:, 48:64, :] = pack_coefs(score_grad)
    query_grad = (fold(dot(score_grad, r.qkv[:, keys])) * scale).astype(LOW)
    probs_total = jnp.sum(probs_low.astype(FULL), axis=1, keepdims=True)
    grad_bvalue = jnp.sum(probs_total * context_tall.astype(FULL), axis=0, keepdims=True)
    grad_bquery = jnp.sum(query_grad.astype(FULL), axis=0, keepdims=True)
    r.queries[here] = query_grad
    own_sums = jnp.concatenate(
        [jnp.zeros((2 * depth, WIDTH), FULL)]
        + [grad_bquery, grad_bvalue, grad_g1, grad_s1, grad_g2, grad_s2]
        + [jnp.zeros((128 - 2 * depth - 6, WIDTH), FULL)],
        axis=0,
    )
    r.own_sums[...] = jnp.transpose(own_sums)
    steps_q[0]()
    steps_a[2]()
    r.tall[0:PAIR_ROWS, :] = (dot(score_grad, r.embedded[...]) * scale).astype(LOW)

    def with_sums(at, both):
        return both + r.own_sums[pl.ds(pl.multiple_of(at * depth, 16), depth), :]

    every(0, CHIPS // 2, pack_tall(r.mail_two, 0, with_sums))
    steps_q[1]()
    post(r.mail_two, r.got_two, 2)

    def all_rows(buffer, start, width=WIDTH):
        return buffer[:, :, :, :, start : start + width].reshape(SLOT_ROWS, width)

    quarter_rows_count = quarter_size * PAD

    def from_sent(quarter):
        span = pl.ds(pl.multiple_of(quarter * quarter_rows_count, 128), quarter_rows_count)
        shape = (GROUPS * quarter_rows_count, quarter_rows_count)
        lanes = (iota(shape, 1) + quarter * quarter_rows_count).astype(FULL)
        named = r.found[0:GROUPS, span, 1:2].reshape(GROUPS * quarter_rows_count, 1)
        return (named == lanes).astype(LOW), span

    def quarter_part(buffer, quarter, start):
        planes = pl.ds(lax.rem(quarter, 2) * 2, 2)
        part = buffer[lax.div(quarter, 2), planes, :, :, start : start + BLOCK]
        return part.reshape(quarter_rows_count, BLOCK)

    def widened(coefs, group, start):
        lanes = iota((128, BLOCK), 0) == over(iota((128, BLOCK), 1) + start, HEAD) + group * PAD
        return dot(coefs, lanes.astype(LOW))

    half_wide = WIDE // 2

    def slope_tile(part):
        at = pl.ds(pl.multiple_of(core * half_wide + part * BLOCK, BLOCK), BLOCK)
        up_pre = dot(all_rows(r.early, 0), r.wb[:, at]) + r.up_bias[0:1, at]
        _, slope = gelu_parts(up_pre)
        r.slopes[:, pl.ds(pl.multiple_of(part * BLOCK, BLOCK), BLOCK)] = slope.astype(LOW)

    def slot_queries(quarter):
        sents, span = from_sent(quarter)
        for start in range(0, WIDTH, BLOCK):
            rows = dot(sents, quarter_part(r.early, quarter, WIDTH + start)).astype(LOW)
            rows = rows.reshape(GROUPS, quarter_rows_count, BLOCK)
            r.slot_query[:, span, start : start + BLOCK] = rows

    def activate():
        at = pl.ds(pl.multiple_of(chip // 2 * 2 * deep, 128), 2 * deep)
        up_pre = dot(all_rows(r.early, 0), r.wb[:, at]) + r.up_bias[0:1, at]
        r.active_turned[...] = jnp.transpose(gelu(up_pre)).astype(LOW)
        r.hidden_turned[...] = jnp.transpose(all_rows(r.early, 0))

    rest = [steps_d[3], steps_a[3], steps_q[2], steps_d[4], steps_a[4]]
    rest = [(first_parts + index, step) for index, step in enumerate(rest)]
    every(first_parts, parts - 1, partial(feed_step, rest))
    feed_up(parts - 1, last=True)

    def rest_step(part):
        feed_rest(part)
        for index, step in enumerate([steps_q[3], steps_d[5], steps_a[5]]):
            pl.when(part == index)(step)

    every(0, WIDTH // BLOCK, rest_step)
    steps_q[4]()
    every(0, WIDTH // BLOCK, feed_down)
    every(0, TOKENS // BLOCK, close_tile)
    every(0, 4, slot_queries)
    every(0, 6, slope_tile)
    activate()

    all_but_one(r.got_one, 1).wait_recv()
    def slot_probs(group):
        got_probs = r.got_one[:, 64:80, :].reshape(SLOT_ROWS, 128)
        for start in range(0, WIDTH, BLOCK):
            r.replies[group, :, start : start + BLOCK] = widened(got_probs, group, start).astype(LOW)

    def slot_values(quarter):
        sents, span = from_sent(quarter)
        for start in range(0, WIDTH, BLOCK):
            lanes = slice(start, start + BLOCK)
            rows = dot(sents, quarter_part(r.attends, quarter, WIDTH + start))
            rows = rows.reshape(GROUPS, quarter_rows_count, BLOCK)
            rows = r.replies[:, span, lanes].astype(FULL) * rows
            r.replies[:, span, lanes] = rows.astype(LOW)

    every(0, GROUPS, slot_probs)
    every(0, 4, slot_values)

    def head_products(got, first_row, right, start, target):
        def one_head(head):
            lane = core * (WIDTH // 2) + lax.div(head, 2) * 128
            pair_rows = right[:, :, :, :, pl.ds(pl.multiple_of(start + lane, 128), 128)]
            row = pl.ds(pl.multiple_of(first_row + lax.rem(head, 3) * PAD, 16), PAD)
            block_rows = got[:, row, :].reshape(SLOT_ROWS, 128)
            r.product[...] = contract(block_rows, pair_rows.reshape(SLOT_ROWS, 128), 0, 0)
            part = r.product[pl.ds(pl.multiple_of(lax.div(head, 3) * depth, 16), depth), :]
            at = pl.ds(pl.multiple_of(lane, 128), 128)
            own_lanes = over(iota((depth, 128), 1), HEAD) == lax.rem(head, 2)
            target[:, at] = jnp.where(own_lanes, part, target[:, at])

        every(0, HEADS // 2, one_head)

    def half_of(ref, at_core):
        half = ref.shape[1] // 2
        return ref.at[:, pl.ds(pl.multiple_of(at_core * half, 128), half)]

    def half_copy(index, ref, at_core):
        part = half_of(ref, at_core)
        return remote(part, part, r.half_send.at[index], r.half_recv.at[index], 1 - core, chip)

    own_half = pl.ds(pl.multiple_of(core * (WIDTH // 2), 128), WIDTH // 2)
    r.g_wv[:, own_half] = jnp.zeros((depth, WIDTH // 2), FULL)
    r.g_wk[:, own_half] = jnp.zeros((depth, WIDTH // 2), FULL)
    head_products(r.got_one, PAD, r.attends, WIDTH, r.g_wv)
    half_copy(0, r.g_wv, core).start()

    downs = r.downs[...].reshape(SLOT_ROWS, WIDTH)
    attends = all_rows(r.attends, 0)

    def up_tile(part):
        at = pl.ds(pl.multiple_of(core * half_wide + part * BLOCK, BLOCK), BLOCK)
        slope = r.slopes[:, pl.ds(pl.multiple_of(part * BLOCK, BLOCK), BLOCK)].astype(FULL)
        up_all = (dot_turned(r.downs[...].reshape(SLOT_ROWS, WIDTH), r.wc[at, :]) * slope)
        up_all = up_all.astype(LOW)
        r.g_wup[0:depth, at] = dot(r.hidden_turned[mine, :], up_all)
        total = jnp.sum(up_all.astype(FULL), axis=0, keepdims=True)
        r.g_wup[depth : depth + 8, at] = jnp.broadcast_to(total, (8, BLOCK))

    every(0, half_wide // BLOCK, up_tile)
    half_copy(1, r.g_wup, core).start()
    r.g_wdown[...] = dot(r.active_turned[pl.ds(pl.multiple_of(chip % 2 * deep, 16), deep), :], downs)
    r.left_turned[...] = jnp.transpose(r.got_one[:, 0:PAD, :].reshape(SLOT_ROWS, 128))
    r.g_wo[...] = dot(r.left_turned[0:depth, :], attends)
    own_lanes = (iota((WIDTH, 128), 0) == chip * depth + iota((WIDTH, 128), 1)).astype(LOW)

    def own_part(rows, select):
        total = None
        for _ in range(3):
            part = rows.astype(LOW)
            rows = rows - part.astype(FULL)
            picked = dot(part, select)
            total = picked if total is None else total + picked
        return total

    for quarter in range(4):
        rows_of(quarter).wait_send()
    all_but_one(r.got_two, 2).wait_recv()

    def slot_grads(group):
        got_scores = r.got_two[:, 48:64, :].reshape(SLOT_ROWS, 128)
        for start in range(0, WIDTH, BLOCK):
            lanes = slice(start, start + BLOCK)
            rows = r.slot_query[group, :, lanes].astype(FULL)
            rows = widened(got_scores, group, start) * rows * scale
            r.slot_query[group, :, lanes] = rows.astype(LOW)
        for start in range(0, WIDTH, BLOCK):
            lanes = slice(start, start + BLOCK)
            row_grad = dot_turned(r.slot_query[group], r.wa[lanes, keys])
            row_grad = row_grad + dot_turned(r.replies[group], r.wa[lanes, values])
            r.rows[group, :, lanes] = row_grad.astype(LOW)

    every(0, GROUPS, slot_grads)
    steps_q[5]()
    query_grads = all_rows(r.queries, 0)
    extra = dot_turned(query_grads, r.wa[:, 0:WIDTH]) + attends.astype(FULL)
    r.extra[...] = extra.astype(LOW)
    r.g_wq[...] = dot(r.left_turned[depth : 2 * depth, :], query_grads)

    half_rows = VOCAB_ROWS // 2

    def table_copy(tile):
        at = pl.ds(pl.multiple_of(tile * half_rows, BLOCK), half_rows)
        return pltpu.make_async_copy(
            r.table_full.at[at], r.table_grad.at[at], r.table_sem.at[tile]
        )

    def table_tile(tile):
        at = pl.ds(pl.multiple_of(tile * half_rows, BLOCK), half_rows)
        for start in range(0, WIDTH, BLOCK):
            lanes = slice(start, start + BLOCK)
            slot_rows = r.rows[:, :, lanes].reshape(GROUPS * SLOT_ROWS, BLOCK)
            r.table_full[at, lanes] = dot(r.by_row[at, 0 : GROUPS * SLOT_ROWS], slot_rows) + dot(
                r.by_row[at, GROUPS * SLOT_ROWS :], r.extra[:, lanes]
            )
        table_copy(tile).start()

    every(0, 2, table_tile)
    head_products(r.got_two, 0, r.early, WIDTH, r.g_wk)
    half_copy(2, r.g_wk, core).start()

    down_total = jnp.sum(downs.astype(FULL), axis=0, keepdims=True)
    attend_total = jnp.sum(attends.astype(FULL), axis=0, keepdims=True)
    sums = jnp.sum(r.got_two[:, 0:48, :].astype(FULL), axis=0)
    sums = jnp.concatenate([sums, jnp.zeros((128 - 48, 128), FULL)], axis=0)
    stacked = jnp.concatenate([attend_total, down_total, jnp.zeros((6, WIDTH), FULL)], axis=0)
    r.g_small[8:16, 0:128] = own_part(stacked, own_lanes)
    r.g_small[0:8, 0:128] = jnp.transpose(sums)[2 * depth : 2 * depth + 8, :]
    r.g_small[0:16, 128:BLOCK] = jnp.zeros((PAD, BLOCK - 128), FULL)
    half_copy(1, r.g_wup, 1 - core).wait_recv()
    up_lanes = (iota((WIDE, BLOCK), 0) == chip * deep + iota((WIDE, BLOCK), 1)).astype(LOW)
    r.g_small[16:24, :] = own_part(r.g_wup[depth : depth + 8, :], up_lanes)

    half_copy(0, r.g_wv, 1 - core).wait_recv()
    half_copy(2, r.g_wk, 1 - core).wait_recv()
    for index, ref in enumerate([r.g_wv, r.g_wup, r.g_wk]):
        half_copy(index, ref, core).wait_send()

    for index, ref in enumerate([r.every_ids, r.got_one, r.got_two]):
        all_but_one(ref, index).wait_send()
    all_smalls().wait_send()
    for end in [drain_a, drain_b, drain_c, drain_u, drain_e, drain_d, drain_a2, drain_q]:
        end()
    every(0, TOKENS // BLOCK, lambda tile: layer_copy(tile).wait())
    every(0, 2, lambda tile: table_copy(tile).wait())


def layer(inputs):
    dma = pltpu.SemaphoreType.DMA
    vmem = pl.BlockSpec(memory_space=pltpu.VMEM)
    anywhere = pl.BlockSpec(memory_space=pl.ANY)
    depth, deep = WIDTH // CHIPS, WIDE // CHIPS

    def gathered(width):
        return pltpu.VMEM((CORES, PLANES, LINES, PAD, width), LOW)

    outputs = dict(
        layer_out=((TOKENS, WIDTH), LOW),
        table_grad=((VOCAB_ROWS, WIDTH), FULL),
        g_wq=((depth, WIDTH), FULL),
        g_wk=((depth, WIDTH), FULL),
        g_wv=((depth, WIDTH), FULL),
        g_wo=((depth, WIDTH), FULL),
        g_wup=((depth + 8, WIDE), FULL),
        g_wdown=((deep, WIDTH), FULL),
        g_small=((24, BLOCK), FULL),
        loss=((1, 1), FULL),
    )
    scratch = dict(
        ids=pltpu.VMEM((8, 128), jnp.int32),
        every_ids=pltpu.VMEM((DEVICES, 8, 128), jnp.int32),
        rank=pltpu.VMEM((DEVICES, TOKENS), FULL),
        code=pltpu.VMEM((DEVICES, TOKENS), FULL),
        found=pltpu.VMEM((GROUPS + 1, SLOT_ROWS, 2), FULL),
        block_bias=pltpu.VMEM((2 * BLOCK, BLOCK // 2), FULL),
        valid_bias=pltpu.VMEM((8, TOKENS), FULL),
        slot_col=pltpu.VMEM((TOKENS, 1), FULL),
        slot_line=pltpu.VMEM((8, TOKENS), FULL),
        valid_col=pltpu.VMEM((TOKENS, 1), FULL),
        valid_line=pltpu.VMEM((8, TOKENS), FULL),
        pairs=pltpu.VMEM((8, SLOT_ROWS), FULL),
        pairs_col=pltpu.VMEM((SLOT_ROWS, 128), FULL),
        vectors=pltpu.VMEM((PAD, WIDTH), FULL),
        up_bias=pltpu.VMEM((8, WIDE), FULL),
        qkv_bias=pltpu.VMEM((8, 3 * WIDTH), FULL),
        smalls=pltpu.VMEM((PAD, CHIPS * 128), LOW),
        wa=pltpu.VMEM((WIDTH, 4 * WIDTH), LOW),
        wb=pltpu.VMEM((WIDTH, WIDE), LOW),
        wc=pltpu.VMEM((WIDE, WIDTH), LOW),
        chosen=pltpu.VMEM((GROUPS, SLOT_ROWS, VOCAB_ROWS), LOW),
        by_row=pltpu.VMEM((VOCAB_ROWS, (GROUPS + 1) * SLOT_ROWS), LOW),
        rows=pltpu.VMEM((GROUPS, SLOT_ROWS, WIDTH), LOW),
        replies=pltpu.VMEM((GROUPS, SLOT_ROWS, WIDTH), LOW),
        slot_query=pltpu.VMEM((GROUPS, SLOT_ROWS, WIDTH), LOW),
        extra=pltpu.VMEM((SLOT_ROWS, WIDTH), LOW),
        hidden_cls=pltpu.VMEM((PAD, WIDTH), LOW),
        active_cls=pltpu.VMEM((PAD, WIDE), LOW),
        slope_cls=pltpu.VMEM((PAD, WIDE), FULL),
        wide_cls=pltpu.VMEM((PAD, WIDTH), FULL),
        tall=pltpu.VMEM((PAIR_ROWS + 2 * PAD, WIDTH), LOW),
        own_sums=pltpu.VMEM((WIDTH, 128), FULL),
        product=pltpu.VMEM((128, 128), FULL),
        slot_hot=pltpu.VMEM((GROUPS, SLOT_ROWS, TOKENS), LOW),
        tile_up=pltpu.VMEM((TOKENS, BLOCK), FULL),
        embedded=pltpu.VMEM((TOKENS, WIDTH), LOW),
        qkv=pltpu.VMEM((TOKENS, 3 * WIDTH), LOW),
        context=pltpu.VMEM((TOKENS, WIDTH), LOW),
        table_full=pltpu.VMEM((VOCAB_ROWS, WIDTH), FULL),
        probs=pltpu.VMEM((PAIR_ROWS, TOKENS), FULL),
        normed_one=pltpu.VMEM((PAD, WIDTH), FULL),
        units=gathered(WIDTH),
        early=gathered(2 * WIDTH),
        downs=gathered(WIDTH),
        attends=gathered(2 * WIDTH),
        queries=gathered(WIDTH),
        slopes=pltpu.VMEM((SLOT_ROWS, WIDE // 2), LOW),
        hidden_turned=pltpu.VMEM((WIDTH, SLOT_ROWS), LOW),
        active_turned=pltpu.VMEM((2 * deep, SLOT_ROWS), LOW),
        left_turned=pltpu.VMEM((128, SLOT_ROWS), LOW),
        mail_one=pltpu.VMEM((DEVICES, 80, 128), LOW),
        got_one=pltpu.VMEM((DEVICES, 80, 128), LOW),
        mail_two=pltpu.VMEM((DEVICES, 64, 128), LOW),
        got_two=pltpu.VMEM((DEVICES, 64, 128), LOW),
        rows_send=dma((4,)),
        rows_recv=dma((4,)),
        one_send=dma((4,)),
        one_recv=dma((4,)),
        small_send=dma((1,)),
        small_recv=dma((1,)),
        weight_send=dma((3, 7)),
        weight_recv=dma((3, 18)),
        gather_send=dma((5, 13)),
        gather_recv=dma((5, 13)),
        half_send=dma((3,)),
        half_recv=dma((3,)),
        out_sem=dma((TOKENS // BLOCK,)),
        table_sem=dma((2,)),
    )
    names = INPUTS + OUTPUTS + list(scratch)
    return pl.pallas_call(
        partial(layer_kernel, names),
        out_shape=tuple(jax.ShapeDtypeStruct(*outputs[name]) for name in OUTPUTS),
        in_specs=[vmem] * len(INPUTS),
        out_specs=(anywhere, anywhere) + (vmem,) * (len(OUTPUTS) - 2),
        scratch_shapes=list(scratch.values()),
        compiler_params=pltpu.CompilerParams(
            collective_id=0, has_side_effects=True, vmem_limit_bytes=VMEM_LIMIT
        ),
        name="layer",
    )(*inputs)


def finish_kernel(count, *refs):
    large, (small, loss), outs = refs[:count], refs[count : count + 2], refs[count + 2 : -1]
    sems = refs[-1]
    copies = []
    for index, (source, target) in enumerate(zip(large, outs)):
        part = source if source.shape == target.shape else source.at[: target.shape[0]]
        copies.append(pltpu.make_async_copy(part, target, sems.at[index]))
        copies[-1].start()
    for row, target in zip([0, 1, 8, 2, 3, 16, 9, 4, 5], outs[count : count + 9]):
        size = target.shape[0]
        target[...] = small[row : row + 1, 0:size].reshape(size)
    outs[-1][...] = loss[...].reshape(1)
    for one in copies:
        one.wait()


def finish(results):
    vmem = pl.BlockSpec(memory_space=pltpu.VMEM)
    anywhere = pl.BlockSpec(memory_space=pl.ANY)
    depth, deep = WIDTH // CHIPS, WIDE // CHIPS
    count = len(results) - 2
    shapes = [(one.shape, one.dtype) for one in results[:count]]
    shapes[6] = ((depth, WIDE), FULL)
    shapes += [((depth,), FULL)] * 5 + [((deep,), FULL)] + [((depth,), FULL)] * 3
    shapes.append(((1,), FULL))
    return pl.pallas_call(
        partial(finish_kernel, count),
        out_shape=tuple(jax.ShapeDtypeStruct(*one) for one in shapes),
        in_specs=[vmem] * (count + 2),
        out_specs=(anywhere,) * count + (vmem,) * 10,
        scratch_shapes=[pltpu.SemaphoreType.DMA((count,))],
        name="finish",
    )(*results)


def block_body(
    table,
    token_ids,
    sent_lengths,
    pair_slot,
    pair_lang,
    *parameters,
):
    results = finish(layer((table, token_ids, sent_lengths, pair_slot, pair_lang) + parameters))
    layer_out, table_grad, g_wq, g_wk, g_wv, g_wo, g_wup, g_wdown = results[:8]
    g_bq, g_bv, g_bo, g_g1, g_s1, g_bup, g_bdown, g_g2, g_s2, loss = results[8:]
    return (
        layer_out.reshape(token_ids.shape + (WIDTH,)),
        loss.reshape(()),
        table_grad,
        g_wq,
        g_bq,
        g_wk,
        g_wv,
        g_bv,
        g_wo,
        g_bo,
        g_g1,
        g_s1,
        g_wup,
        g_bup,
        g_wdown,
        g_bdown,
        g_g2,
        g_s2,
    )


def solution(mesh):
    in_specs = (
        P(("dp", "fsdp"), None),
        P(("dp", "fsdp"), None),
        P(("dp", "fsdp")),
        P(),
        P(),
        P("fsdp", None),
        P("fsdp"),
        P("fsdp", None),
        P("fsdp", None),
        P("fsdp"),
        P("fsdp", None),
        P("fsdp"),
        P("fsdp"),
        P("fsdp"),
        P("fsdp", None),
        P("fsdp"),
        P("fsdp", None),
        P("fsdp"),
        P("fsdp"),
        P("fsdp"),
    )
    out_specs = (
        P(("dp", "fsdp"), None, None),
        P(),
        P(("dp", "fsdp"), None),
        P("fsdp", None),
        P("fsdp"),
        P("fsdp", None),
        P("fsdp", None),
        P("fsdp"),
        P("fsdp", None),
        P("fsdp"),
        P("fsdp"),
        P("fsdp"),
        P("fsdp", None),
        P("fsdp"),
        P("fsdp", None),
        P("fsdp"),
        P("fsdp"),
        P("fsdp"),
    )
    sizes = dict(mesh.shape)
    body = general_body
    if sizes["dp"] == CORES and sizes["fsdp"] == CHIPS:
        body = block_body
    return jax.shard_map(body, mesh=mesh, in_specs=in_specs, out_specs=out_specs, check_vma=False)
```

```python
from functools import partial
from types import SimpleNamespace

import jax
import jax.numpy as jnp
from jax import lax
from jax.experimental import pallas as pl
from jax.experimental.pallas import tpu as pltpu
from jax.sharding import PartitionSpec as P

HEADS = 12
HEAD = 64
LANGS = 109


EPSILON = 1e-06
SCORE_SCALE = 50.0
MARGIN_WIDTH = 0.3
MASK_FLOOR = -1000000000.0


def contract(left_side, right_side, left_dim, right_dim):
    return lax.dot_general(
        left_side,
        right_side,
        (((left_dim,), (right_dim,)), ((), ())),
        preferred_element_type=jnp.float32,
    )


def norm_rows(inputs, ln_gain, ln_shift):
    row_mean = jnp.mean(inputs, axis=-1, keepdims=True)
    centered = inputs - row_mean
    variance = jnp.mean(centered * centered, axis=-1, keepdims=True)
    inverse = lax.rsqrt(variance + EPSILON)
    normed = centered * inverse
    return (normed * ln_gain + ln_shift, normed, inverse)


def norm_back(grad_output, normed, inverse, ln_gain):
    grad_normed = grad_output * ln_gain
    first_term = jnp.mean(grad_normed, axis=-1, keepdims=True)
    second_term = jnp.mean(grad_normed * normed, axis=-1, keepdims=True)
    grad_input = inverse * (grad_normed - first_term - normed * second_term)
    return (grad_input, jnp.sum(grad_output * normed, axis=0), jnp.sum(grad_output, axis=0))


def general_body(
    table,
    token_ids,
    sent_lengths,
    pair_slot,
    pair_lang,
    w_query,
    b_query,
    w_key,
    w_value,
    b_value,
    w_out,
    b_out,
    ln1_gain,
    ln1_bias,
    w_up,
    b_up,
    w_down,
    b_down,
    ln2_gain,
    ln2_bias,
):
    sentences, length = token_ids.shape
    tokens = sentences * length
    vocab_rows, model_width = table.shape
    owners = lax.axis_size(("dp", "fsdp"))
    dp_count = lax.axis_size("dp")
    fsdp_count = lax.axis_size("fsdp")
    capacity = max(2, 2 * tokens // owners)
    device = lax.axis_index(("dp", "fsdp"))
    score_factor = HEAD ** (-0.5)
    flat_ids = token_ids.reshape(tokens)
    owner_of = flat_ids // vocab_rows
    member = (owner_of[:, None] == jnp.arange(owners, dtype=jnp.int32)[None, :]).astype(jnp.int32)
    owner_rank = jnp.sum(jnp.cumsum(member, axis=0) * member, axis=1) - 1
    slot_of = owner_of * capacity + owner_rank
    requests = jnp.full((owners * capacity,), -1, jnp.int32).at[slot_of].set(flat_ids)
    received = lax.all_to_all(
        lax.all_to_all(
            requests.reshape(dp_count, fsdp_count, capacity),
            "dp",
            split_axis=0,
            concat_axis=0,
            tiled=True,
        ),
        "fsdp",
        split_axis=1,
        concat_axis=1,
        tiled=True,
    )
    present = received >= 0
    local_rows = jnp.where(present, received - device * vocab_rows, 0)
    found_rows = jnp.where(present[..., None], table[local_rows], jnp.zeros((), table.dtype))
    replies = lax.all_to_all(
        lax.all_to_all(found_rows, "dp", split_axis=0, concat_axis=0, tiled=True),
        "fsdp",
        split_axis=1,
        concat_axis=1,
        tiled=True,
    )
    embedded = replies.reshape(owners * capacity, model_width)[slot_of]
    gathered = (
        lax.all_gather(w_query, "fsdp", axis=0, tiled=True),
        lax.all_gather(b_query, "fsdp", axis=0, tiled=True),
        lax.all_gather(w_key, "fsdp", axis=0, tiled=True),
        lax.all_gather(w_value, "fsdp", axis=0, tiled=True),
        lax.all_gather(b_value, "fsdp", axis=0, tiled=True),
        lax.all_gather(w_out, "fsdp", axis=0, tiled=True),
        lax.all_gather(b_out, "fsdp", axis=0, tiled=True),
        lax.all_gather(ln1_gain, "fsdp", axis=0, tiled=True),
        lax.all_gather(ln1_bias, "fsdp", axis=0, tiled=True),
        lax.all_gather(w_up, "fsdp", axis=0, tiled=True),
        lax.all_gather(b_up, "fsdp", axis=0, tiled=True),
        lax.all_gather(w_down, "fsdp", axis=0, tiled=True),
        lax.all_gather(b_down, "fsdp", axis=0, tiled=True),
        lax.all_gather(ln2_gain, "fsdp", axis=0, tiled=True),
        lax.all_gather(ln2_bias, "fsdp", axis=0, tiled=True),
    )
    (
        full_wq,
        full_bq,
        full_wk,
        full_wv,
        full_bv,
        full_wo,
        full_bo,
        full_g1,
        full_s1,
        full_wup,
        full_bup,
        full_wdown,
        full_bdown,
        full_g2,
        full_s2,
    ) = gathered
    valid_mask = jnp.arange(length, dtype=jnp.int32)[None, :] < sent_lengths[:, None]
    head_shape = (sentences, length, HEADS, HEAD)
    queries = (jnp.dot(embedded, full_wq, preferred_element_type=jnp.float32) + full_bq).astype(
        jnp.bfloat16
    )
    key_heads = (
        jnp.dot(embedded, full_wk, preferred_element_type=jnp.float32)
        .astype(jnp.bfloat16)
        .reshape(head_shape)
    )
    value_heads = (
        (jnp.dot(embedded, full_wv, preferred_element_type=jnp.float32) + full_bv)
        .astype(jnp.bfloat16)
        .reshape(head_shape)
    )
    query_heads = queries.reshape(head_shape)
    scores = (
        jnp.einsum("bqhd,bkhd->bhqk", query_heads, key_heads, preferred_element_type=jnp.float32)
        * score_factor
    )
    scores = jnp.where(valid_mask[:, None, None, :], scores, MASK_FLOOR)
    row_peak = jnp.max(scores, axis=-1, keepdims=True)
    shifted = jnp.exp(scores - row_peak)
    totals = jnp.sum(shifted, axis=-1, keepdims=True)
    attn_probs = (shifted / totals).astype(jnp.bfloat16)
    context = jnp.einsum(
        "bhqk,bkhd->bqhd", attn_probs, value_heads, preferred_element_type=jnp.float32
    )
    context = context.reshape(tokens, model_width).astype(jnp.bfloat16)
    attended = jnp.dot(context, full_wo, preferred_element_type=jnp.float32) + full_bo
    hidden, normed_one, inverse_one = norm_rows(
        embedded.astype(jnp.float32) + attended, full_g1, full_s1
    )
    hidden_low = hidden.astype(jnp.bfloat16)
    up_pre = jnp.dot(hidden_low, full_wup, preferred_element_type=jnp.float32) + full_bup
    activated = jax.nn.gelu(up_pre, approximate=False).astype(jnp.bfloat16)
    down_pre = jnp.dot(activated, full_wdown, preferred_element_type=jnp.float32) + full_bdown
    normed_out, normed_two, inverse_two = norm_rows(hidden + down_pre, full_g2, full_s2)
    layer_out = jnp.where(valid_mask.reshape(tokens)[:, None], normed_out, 0.0).astype(jnp.bfloat16)
    layer_out = layer_out.reshape(sentences, length, model_width)

    def first_rows(matrix):
        return matrix.reshape(sentences, length, matrix.shape[-1])[:, 0]

    summary = first_rows(normed_out)
    magnitude = jnp.sqrt(jnp.sum(summary * summary, axis=-1, keepdims=True) + EPSILON)
    unit_vector = summary / magnitude
    unit_low = unit_vector.astype(jnp.bfloat16)
    every_unit = lax.all_gather(unit_low, ("dp", "fsdp"), axis=0, tiled=True)
    every_side = pair_slot % 2
    every_pair = pair_slot // 2
    my_slots = lax.dynamic_slice_in_dim(pair_slot, device * sentences, sentences)
    my_side = my_slots % 2
    my_pair = my_slots // 2
    lang_onehot = (pair_lang[:, None] == jnp.arange(LANGS, dtype=jnp.int32)[None, :]).astype(
        jnp.float32
    )
    per_lang = jnp.sum(lang_onehot, axis=0)
    per_pair = 1.0 / (2.0 * LANGS * jnp.sum(lang_onehot * per_lang[None, :], axis=1))
    my_weight = jnp.take(per_pair, my_pair)
    opposite = my_side[:, None] != every_side[None, :]
    partner = opposite & (my_pair[:, None] == every_pair[None, :])
    raw_scores = SCORE_SCALE * contract(unit_low, every_unit, 1, 1)
    pair_scores = jnp.where(partner, raw_scores - SCORE_SCALE * MARGIN_WIDTH, raw_scores)
    pair_scores = jnp.where(opposite, pair_scores, MASK_FLOOR)
    pair_peak = jnp.max(pair_scores, axis=1, keepdims=True)
    pair_exp = jnp.exp(pair_scores - pair_peak)
    pair_total = jnp.sum(pair_exp, axis=1, keepdims=True)
    log_total = pair_peak[:, 0] + jnp.log(pair_total[:, 0])
    picked = jnp.sum(jnp.where(partner, pair_scores, 0.0), axis=1)
    loss_value = lax.psum(jnp.sum(my_weight * (log_total - picked)), ("dp", "fsdp"))
    coefficients = (
        my_weight[:, None] * (pair_exp / pair_total - partner.astype(jnp.float32))
    ).astype(jnp.bfloat16)
    unit_grad = SCORE_SCALE * contract(coefficients, every_unit, 1, 0)
    column_terms = SCORE_SCALE * contract(coefficients, unit_low, 0, 0)
    unit_grad = unit_grad + lax.psum_scatter(
        column_terms, ("dp", "fsdp"), scatter_dimension=0, tiled=True
    )
    along = jnp.sum(unit_vector * unit_grad, axis=-1, keepdims=True)
    summary_grad = (unit_grad - unit_vector * along) / magnitude
    again_weights = (
        lax.all_gather(w_query, "fsdp", axis=0, tiled=True),
        lax.all_gather(w_key, "fsdp", axis=0, tiled=True),
        lax.all_gather(w_value, "fsdp", axis=0, tiled=True),
        lax.all_gather(w_out, "fsdp", axis=0, tiled=True),
        lax.all_gather(ln1_gain, "fsdp", axis=0, tiled=True),
        lax.all_gather(w_up, "fsdp", axis=0, tiled=True),
        lax.all_gather(w_down, "fsdp", axis=0, tiled=True),
        lax.all_gather(ln2_gain, "fsdp", axis=0, tiled=True),
    )
    again_wq, again_wk, again_wv, again_wo, again_g1, again_wup, again_wdown, again_g2 = (
        again_weights
    )
    residual_grad, grad_g2, grad_s2 = norm_back(
        summary_grad, first_rows(normed_two), first_rows(inverse_two), again_g2
    )
    down_grad = residual_grad.astype(jnp.bfloat16)
    activated_cls = first_rows(activated)
    act_grad = contract(down_grad, again_wdown, 1, 1)
    gelu_value, gelu_pull = jax.vjp(partial(jax.nn.gelu, approximate=False), first_rows(up_pre))
    up_grad = gelu_pull(act_grad)[0].astype(jnp.bfloat16)
    hidden_cls = first_rows(hidden_low)
    hidden_grad = contract(up_grad, again_wup, 1, 1) + residual_grad
    first_grad, grad_g1, grad_s1 = norm_back(
        hidden_grad, first_rows(normed_one), first_rows(inverse_one), again_g1
    )
    attend_grad = first_grad.astype(jnp.bfloat16)
    context_cls = first_rows(context)
    context_grad = (
        contract(attend_grad, again_wo, 1, 1).astype(jnp.bfloat16).reshape(sentences, HEADS, HEAD)
    )
    query_cls = query_heads[:, 0]
    cls_scores = (
        jnp.einsum("bhd,bkhd->bhk", query_cls, key_heads, preferred_element_type=jnp.float32)
        * score_factor
    )
    cls_scores = jnp.where(valid_mask[:, None, :], cls_scores, MASK_FLOOR)
    cls_probs = jnp.exp(cls_scores - row_peak[:, :, 0]) / totals[:, :, 0]
    prob_grad = jnp.einsum(
        "bhd,bkhd->bhk", context_grad, value_heads, preferred_element_type=jnp.float32
    )
    score_grad = (
        cls_probs * (prob_grad - jnp.sum(cls_probs * prob_grad, axis=-1, keepdims=True))
    ).astype(jnp.bfloat16)
    query_grad = (
        (
            jnp.einsum("bhk,bkhd->bhd", score_grad, key_heads, preferred_element_type=jnp.float32)
            * score_factor
        )
        .astype(jnp.bfloat16)
        .reshape(sentences, model_width)
    )
    key_grad = (
        (
            jnp.einsum("bhk,bhd->bkhd", score_grad, query_cls, preferred_element_type=jnp.float32)
            * score_factor
        )
        .astype(jnp.bfloat16)
        .reshape(tokens, model_width)
    )
    value_grad = (
        jnp.einsum(
            "bhk,bhd->bkhd",
            cls_probs.astype(jnp.bfloat16),
            context_grad,
            preferred_element_type=jnp.float32,
        )
        .astype(jnp.bfloat16)
        .reshape(tokens, model_width)
    )
    embedded_cls = first_rows(embedded)
    grad_wkey = contract(embedded, key_grad, 0, 0)
    grad_wvalue = contract(embedded, value_grad, 0, 0)
    grad_bvalue = jnp.sum(value_grad, axis=0, dtype=jnp.float32)
    row_grads = contract(key_grad, again_wk, 1, 1) + contract(value_grad, again_wv, 1, 1)
    summary_extra = contract(query_grad, again_wq, 1, 1) + first_grad
    row_grads = (
        row_grads.reshape(sentences, length, model_width)
        .at[:, 0]
        .add(summary_extra)
        .reshape(tokens, model_width)
    )
    outgoing = jnp.zeros((owners * capacity, model_width), jnp.float32).at[slot_of].set(row_grads)
    incoming = lax.all_to_all(
        lax.all_to_all(
            outgoing.reshape(dp_count, fsdp_count, capacity, model_width).astype(jnp.bfloat16),
            "dp",
            split_axis=0,
            concat_axis=0,
            tiled=True,
        ),
        "fsdp",
        split_axis=1,
        concat_axis=1,
        tiled=True,
    ).astype(jnp.float32)
    incoming = jnp.where(
        present.reshape(owners * capacity)[:, None],
        incoming.reshape(owners * capacity, model_width),
        0.0,
    )
    table_grad = (
        jnp.zeros((vocab_rows, model_width), jnp.float32)
        .at[local_rows.reshape(owners * capacity)]
        .add(incoming)
    )
    grad_wquery = contract(embedded_cls, query_grad, 0, 0)
    grad_bquery = jnp.sum(query_grad, axis=0, dtype=jnp.float32)
    grad_wout = contract(context_cls, attend_grad, 0, 0)
    grad_bout = jnp.sum(attend_grad, axis=0, dtype=jnp.float32)
    grad_wup = contract(hidden_cls, up_grad, 0, 0)
    grad_bup = jnp.sum(up_grad, axis=0, dtype=jnp.float32)
    grad_wdown = contract(activated_cls, down_grad, 0, 0)
    grad_bdown = jnp.sum(down_grad, axis=0, dtype=jnp.float32)
    owned_grads = (
        lax.psum_scatter(
            grad_wquery.astype(jnp.bfloat16), "fsdp", scatter_dimension=0, tiled=True
        ).astype(jnp.float32),
        lax.psum_scatter(
            grad_bquery.astype(jnp.bfloat16), "fsdp", scatter_dimension=0, tiled=True
        ).astype(jnp.float32),
        lax.psum_scatter(
            grad_wkey.astype(jnp.bfloat16), "fsdp", scatter_dimension=0, tiled=True
        ).astype(jnp.float32),
        lax.psum_scatter(
            grad_wvalue.astype(jnp.bfloat16), "fsdp", scatter_dimension=0, tiled=True
        ).astype(jnp.float32),
        lax.psum_scatter(
            grad_bvalue.astype(jnp.bfloat16), "fsdp", scatter_dimension=0, tiled=True
        ).astype(jnp.float32),
        lax.psum_scatter(
            grad_wout.astype(jnp.bfloat16), "fsdp", scatter_dimension=0, tiled=True
        ).astype(jnp.float32),
        lax.psum_scatter(
            grad_bout.astype(jnp.bfloat16), "fsdp", scatter_dimension=0, tiled=True
        ).astype(jnp.float32),
        lax.psum_scatter(
            grad_g1.astype(jnp.bfloat16), "fsdp", scatter_dimension=0, tiled=True
        ).astype(jnp.float32),
        lax.psum_scatter(
            grad_s1.astype(jnp.bfloat16), "fsdp", scatter_dimension=0, tiled=True
        ).astype(jnp.float32),
        lax.psum_scatter(
            grad_wup.astype(jnp.bfloat16), "fsdp", scatter_dimension=0, tiled=True
        ).astype(jnp.float32),
        lax.psum_scatter(
            grad_bup.astype(jnp.bfloat16), "fsdp", scatter_dimension=0, tiled=True
        ).astype(jnp.float32),
        lax.psum_scatter(
            grad_wdown.astype(jnp.bfloat16), "fsdp", scatter_dimension=0, tiled=True
        ).astype(jnp.float32),
        lax.psum_scatter(
            grad_bdown.astype(jnp.bfloat16), "fsdp", scatter_dimension=0, tiled=True
        ).astype(jnp.float32),
        lax.psum_scatter(
            grad_g2.astype(jnp.bfloat16), "fsdp", scatter_dimension=0, tiled=True
        ).astype(jnp.float32),
        lax.psum_scatter(
            grad_s2.astype(jnp.bfloat16), "fsdp", scatter_dimension=0, tiled=True
        ).astype(jnp.float32),
    )
    summed = (
        lax.psum(owned_grads[0].astype(jnp.bfloat16), "dp").astype(jnp.float32),
        lax.psum(owned_grads[1].astype(jnp.bfloat16), "dp").astype(jnp.float32),
        lax.psum(owned_grads[2].astype(jnp.bfloat16), "dp").astype(jnp.float32),
        lax.psum(owned_grads[3].astype(jnp.bfloat16), "dp").astype(jnp.float32),
        lax.psum(owned_grads[4].astype(jnp.bfloat16), "dp").astype(jnp.float32),
        lax.psum(owned_grads[5].astype(jnp.bfloat16), "dp").astype(jnp.float32),
        lax.psum(owned_grads[6].astype(jnp.bfloat16), "dp").astype(jnp.float32),
        lax.psum(owned_grads[7].astype(jnp.bfloat16), "dp").astype(jnp.float32),
        lax.psum(owned_grads[8].astype(jnp.bfloat16), "dp").astype(jnp.float32),
        lax.psum(owned_grads[9].astype(jnp.bfloat16), "dp").astype(jnp.float32),
        lax.psum(owned_grads[10].astype(jnp.bfloat16), "dp").astype(jnp.float32),
        lax.psum(owned_grads[11].astype(jnp.bfloat16), "dp").astype(jnp.float32),
        lax.psum(owned_grads[12].astype(jnp.bfloat16), "dp").astype(jnp.float32),
        lax.psum(owned_grads[13].astype(jnp.bfloat16), "dp").astype(jnp.float32),
        lax.psum(owned_grads[14].astype(jnp.bfloat16), "dp").astype(jnp.float32),
    )
    return (
        layer_out,
        loss_value,
        table_grad,
        summed[0],
        summed[1],
        summed[2],
        summed[3],
        summed[4],
        summed[5],
        summed[6],
        summed[7],
        summed[8],
        summed[9],
        summed[10],
        summed[11],
        summed[12],
        summed[13],
        summed[14],
    )


CORES = 2
PLANES = 4
LINES = 4
CHIPS = PLANES * LINES
DEVICES = CORES * CHIPS
CAPACITY = 48
GROUPS = 3
PAD = 16
TOKENS = 768
WIDTH = 768
WIDE = 3072
VOCAB_ROWS = 1024
PAIR_ROWS = HEADS * PAD
SLOT_ROWS = DEVICES * PAD
LONG = 64
BLOCK = 256
MESH = pl.DeviceIdType.MESH
LOW = jnp.bfloat16
FULL = jnp.float32
VMEM_LIMIT = 62 * 1024 * 1024

INPUTS = ["table", "token_ids", "lens", "slots", "langs"]
INPUTS += ["wq", "bq", "wk", "wv", "bv", "wo", "bo", "g1", "s1", "wup", "bup", "wdown", "bdown"]
INPUTS += ["g2", "s2"]
OUTPUTS = ["layer_out", "table_grad", "g_wq", "g_wk", "g_wv", "g_wo", "g_wup", "g_wdown"]
OUTPUTS += ["g_small", "loss"]


def place():
    core = lax.axis_index("dp")
    chip = lax.axis_index("fsdp")
    along_x = chip + 1 - 2 * (chip % 2)
    along_y = chip + 2 - 4 * ((chip // 2) % 2)
    first = along_x + core * (along_y - along_x)
    second = along_y + core * (along_x - along_y)
    return core, chip, first, second


def greet():
    core, chip, _, _ = place()
    me = core * CHIPS + chip
    barrier = pltpu.get_barrier_semaphore()

    def signal(step):
        other = lax.rem(me + step, DEVICES)
        pl.semaphore_signal(
            barrier,
            inc=1,
            device_id=(lax.div(other, CHIPS), lax.rem(other, CHIPS)),
            device_id_type=MESH,
        )

    every(1, DEVICES, signal)


def enter():
    pl.semaphore_wait(pltpu.get_barrier_semaphore(), DEVICES - 1)


def remote(source, target, send_sem, recv_sem, core, chip):
    return pltpu.make_async_remote_copy(
        src_ref=source,
        dst_ref=target,
        send_sem=send_sem,
        recv_sem=recv_sem,
        device_id=(core, chip),
        device_id_type=MESH,
    )


def every(start, stop, act):
    def step(index, carry):
        act(index)
        return carry

    lax.fori_loop(start, stop, step, 0)


def weight_steps(piece, many, send, recv):
    core, chip, first, second = place()
    plane, line = chip // LINES, chip % LINES
    line_first, line_second = first % LINES, second % LINES
    line_far = line_first + line_second - line
    is_low, is_high = plane > 0, plane < PLANES - 1

    def copy(send_index, recv_index, at, to_core, to_chip, carried=core):
        part = piece(at, carried)
        return remote(part, part, send.at[send_index], recv.at[recv_index], to_core, to_chip)

    def up(at_plane):
        return copy(at_plane, at_plane, at_plane * LINES + line, core, chip + LINES)

    def down(at_plane, index):
        return copy(index, at_plane, at_plane * LINES + line, core, chip - LINES)

    def side(at_plane, base, at_line, target):
        return copy(5, base + at_plane, at_plane * LINES + at_line, core, target)

    def across(at_plane, at_line):
        return copy(6, 17, at_plane * LINES + at_line, 1 - core, chip)

    def all_of(count, send_index, recv_index):
        part = many(count)
        return remote(part, part, send.at[send_index], recv.at[recv_index], 1 - core, chip)

    def begin():
        pl.when(is_high)(lambda: up(plane).start())
        pl.when(is_low)(lambda: down(plane, PLANES).start())
        side(plane, 5, line, first).start()
        side(plane, 9, line, second).start()

    def at_distance(distance, act):
        if distance == 0:
            act(plane, None)
            return
        pl.when(plane >= distance)(lambda: act(plane - distance, True))
        pl.when(plane + distance < PLANES)(lambda: act(plane + distance, False))

    def chain(distance):
        def act(at_plane, from_low):
            if from_low:
                up(at_plane).wait_recv()
                pl.when(is_high)(lambda: up(at_plane).start())
            else:
                down(at_plane, at_plane).wait_recv()
                pl.when(is_low)(lambda: down(at_plane, at_plane).start())
            side(at_plane, 5, line, first).start()
            side(at_plane, 9, line, second).start()
            across(at_plane, line).start()

        return partial(at_distance, distance, act)

    def near(distance):
        def act(at_plane, from_low):
            side(at_plane, 5, line_first, first).wait_recv()
            side(at_plane, 13, line_first, second).start()
            across(at_plane, line_first).start()

        return partial(at_distance, distance, act)

    def far(distance):
        def act(at_plane, from_low):
            side(at_plane, 9, line_second, second).wait_recv()
            across(at_plane, line_second).start()
            side(at_plane, 13, line_far, second).wait_recv()
            across(at_plane, line_far).start()

        return partial(at_distance, distance, act)

    def finish():
        all_of(15, 6, 17).wait_recv()

    def drain():
        def sent(index):
            copy(index, index, chip, 1 - core, chip).wait_send()

        for at_plane in range(PLANES):
            pl.when((plane >= at_plane) & is_high)(partial(sent, at_plane))
            pl.when((plane < at_plane) & is_low)(partial(sent, at_plane))
        pl.when(is_low)(partial(sent, PLANES))
        all_of(12, 5, 17).wait_send()
        all_of(15, 6, 17).wait_send()

    moves = [chain(1), near(0), chain(2), near(1), chain(3), far(0)]
    moves += [near(2), far(1), near(3), far(2), far(3)]
    return begin, moves, finish, drain


def gather_steps(buffer, send, recv):
    core, chip, first, second = place()
    plane, line = chip // LINES, chip % LINES
    line_first, line_second = first % LINES, second % LINES
    line_far = line_first + line_second - line
    half = buffer.shape[-1] // 2
    columns = pl.ds(pl.multiple_of(core * half, 128), half)
    others = pl.ds(pl.multiple_of((1 - core) * half, 128), half)

    def copy(index, part, to_core, to_chip):
        return remote(part, part, send.at[index], recv.at[index], to_core, to_chip)

    def own(at):
        return buffer.at[at, plane, line]

    def chip_part(at_plane, at_line, which):
        return buffer.at[:, at_plane, at_line, :, which]

    def line_part(at_line, which):
        return buffer.at[:, :, at_line, :, which]

    def start():
        copy(0, own(core), 1 - core, chip).start()

    def planes():
        copy(0, own(1 - core), 1 - core, chip).wait_recv()
        for step in range(1, PLANES):
            part = chip_part(plane, line, columns)
            copy(step, part, core, (chip + LINES * step) % CHIPS).start()

    def sides():
        for step in range(1, PLANES):
            part = chip_part((plane + PLANES - step) % PLANES, line, columns)
            copy(step, part, core, chip).wait_recv()
        copy(4, line_part(line, columns), core, first).start()
        copy(5, line_part(line, columns), core, second).start()
        for step in range(1, PLANES):
            part = chip_part((plane + PLANES - step) % PLANES, line, columns)
            copy(6 + step, part, 1 - core, chip).start()

    def corner():
        copy(4, line_part(line_first, columns), core, first).wait_recv()
        copy(6, line_part(line_first, columns), core, second).start()
        copy(10, line_part(line_first, columns), 1 - core, chip).start()
        copy(5, line_part(line_second, columns), core, second).wait_recv()
        copy(11, line_part(line_second, columns), 1 - core, chip).start()

    def last():
        copy(6, line_part(line_far, columns), core, second).wait_recv()
        copy(12, line_part(line_far, columns), 1 - core, chip).start()

    def finish():
        for step in range(1, PLANES):
            part = chip_part((plane + PLANES - step) % PLANES, line, others)
            copy(6 + step, part, 1 - core, chip).wait_recv()
        copy(10, line_part(line_second, others), 1 - core, chip).wait_recv()
        copy(11, line_part(line_first, others), 1 - core, chip).wait_recv()
        copy(12, line_part(line_far, others), 1 - core, chip).wait_recv()

    def drain():
        copy(0, own(core), 1 - core, chip).wait_send()
        for index in [1, 2, 3, 7, 8, 9]:
            copy(index, chip_part(plane, line, columns), 1 - core, chip).wait_send()
        for index in [4, 5, 6, 10, 11, 12]:
            copy(index, line_part(line, columns), 1 - core, chip).wait_send()

    return [start, planes, sides, corner, last, finish], drain


def iota(shape, axis):
    return lax.broadcasted_iota(jnp.int32, shape, axis)


def over(numbers, power):
    return lax.shift_right_arithmetic(numbers, jnp.full_like(numbers, power.bit_length() - 1))


def within(numbers, power):
    return numbers & (power - 1)


def as_column(row):
    parts = []
    for start in range(0, row.shape[1], 128):
        tile = jnp.broadcast_to(row[:, start : start + 128], (128, 128))
        parts.append(jnp.transpose(tile)[:, 0:1])
    return jnp.concatenate(parts, axis=0)


def as_row(column):
    parts = []
    for start in range(0, column.shape[0], 128):
        tile = jnp.broadcast_to(column[start : start + 128, :], (128, 128))
        parts.append(jnp.transpose(tile)[0:1, :])
    return jnp.concatenate(parts, axis=1)


def dot(left_side, right_side):
    return contract(left_side, right_side, 1, 0)


def dot_turned(left_side, right_side):
    return contract(left_side, right_side, 1, 1)


def norm_parts(inputs):
    centered = inputs - jnp.mean(inputs, axis=-1, keepdims=True)
    inverse = lax.rsqrt(jnp.mean(centered * centered, axis=-1, keepdims=True) + EPSILON)
    return centered * inverse, inverse


def norm_back_parts(grad_output, normed, inverse, ln_gain):
    grad_normed = grad_output * ln_gain
    first_term = jnp.mean(grad_normed, axis=-1, keepdims=True)
    second_term = jnp.mean(grad_normed * normed, axis=-1, keepdims=True)
    return (
        inverse * (grad_normed - first_term - normed * second_term),
        jnp.sum(grad_output * normed, axis=0, keepdims=True),
        jnp.sum(grad_output, axis=0, keepdims=True),
    )


def erf_parts(inputs):
    decay = jnp.exp(-0.5 * inputs * inputs)
    share = 1.0 / (1.0 + jnp.abs(inputs) * (0.3275911 * 0.5**0.5))
    terms = [1.061405429, -1.453152027, 1.421413741, -0.284496736, 0.254829592]
    series = 0.5 * terms[0]
    for term in terms[1:]:
        series = series * share + 0.5 * term
    tail = series * share * decay
    return jnp.where(inputs >= 0.0, 1.0 - tail, tail), decay


def gelu_parts(inputs):
    below, decay = erf_parts(inputs)
    return inputs * below, below + inputs * decay * ((2.0 * 3.141592653589793) ** -0.5)


def gelu(inputs):
    return inputs * erf_parts(inputs)[0]


def layer_kernel(names, *refs):
    r = SimpleNamespace(**dict(zip(names, refs, strict=True)))
    core, chip, _, _ = place()
    me = core * CHIPS + chip
    here = (core, chip // LINES, chip % LINES)
    scale = HEAD ** (-0.5)
    depth, deep = WIDTH // CHIPS, WIDE // CHIPS
    sentences = TOKENS // LONG

    for j in range(TOKENS // 128):
        r.ids[j : j + 1, :] = jnp.concatenate(
            [r.token_ids[2 * j : 2 * j + 1, :], r.token_ids[2 * j + 1 : 2 * j + 2, :]], axis=1
        )
    r.ids[TOKENS // 128 : 8, :] = jnp.zeros((8 - TOKENS // 128, 128), jnp.int32)
    greet()
    ahead = (iota((TOKENS, TOKENS), 0) < iota((TOKENS, TOKENS), 1)).astype(LOW)
    r.embedded[...] = ahead
    mine = pl.ds(pl.multiple_of(chip * depth, 16), depth)
    for index, shard in enumerate([r.wq, r.wk, r.wv, r.wo]):
        r.wa[mine, index * WIDTH : (index + 1) * WIDTH] = shard[...]
    r.wb[mine, :] = r.wup[...]
    r.wc[pl.ds(pl.multiple_of(chip * deep, 16), deep), :] = r.wdown[...]
    r.every_ids[me] = r.ids[...]
    enter()

    def peer(step):
        other = lax.rem(me + step, DEVICES)
        return other, lax.div(other, CHIPS), lax.rem(other, CHIPS)

    def ids_copy(step):
        other, to_core, to_chip = peer(step)
        return remote(r.ids, r.every_ids.at[me], r.one_send.at[0], r.one_recv.at[0], to_core, to_chip)

    def all_but_one(ref, index):
        part = ref.at[0 : DEVICES - 1]
        return remote(part, part, r.one_send.at[index], r.one_recv.at[index], 1 - core, chip)

    every(1, DEVICES, lambda step: ids_copy(step).start())

    def block(ref, rows, columns):
        def piece(at, carried):
            return ref.at[
                pl.ds(pl.multiple_of(at * rows, 16), rows),
                pl.ds(pl.multiple_of(carried * columns, 128), columns),
            ]

        def many(count):
            return ref.at[0 : count * rows, 0:columns]

        return piece, many

    begin_a, moves_a, finish_a, drain_a = weight_steps(
        *block(r.wa, depth, 2 * WIDTH), r.weight_send.at[0], r.weight_recv.at[0]
    )
    begin_b, moves_b, finish_b, drain_b = weight_steps(
        *block(r.wb, depth, WIDE // 2), r.weight_send.at[1], r.weight_recv.at[1]
    )
    begin_c, moves_c, finish_c, drain_c = weight_steps(
        *block(r.wc, deep, WIDTH // 2), r.weight_send.at[2], r.weight_recv.at[2]
    )
    begin_a()
    begin_b()

    def move(*steps):
        for moves, first_step in steps:
            moves[first_step]()
            moves[first_step + 1]()

    all_but_one(r.every_ids, 0).wait_recv()
    all_ids = jnp.concatenate([r.every_ids[:, j, :] for j in range(TOKENS // 128)], axis=1)
    all_owner = over(all_ids, VOCAB_ROWS)
    asked = all_owner == me
    ranks = dot(asked.astype(LOW), r.embedded[...])
    r.rank[...] = jnp.where(asked, ranks, -1.0)
    local_row = (all_ids - all_owner * VOCAB_ROWS + 1).astype(FULL)
    r.code[...] = local_row + (over(iota((DEVICES, TOKENS), 1), LONG) * 2048).astype(FULL)

    quarter_size = DEVICES // 4

    def rows_copy(other, quarter):
        return remote(
            r.rows.at[:, pl.ds(pl.multiple_of(other * PAD, 16), PAD), :],
            r.replies.at[:, pl.ds(pl.multiple_of(me * PAD, 16), PAD), :],
            r.rows_send.at[quarter],
            r.rows_recv.at[quarter],
            lax.div(other, CHIPS),
            lax.rem(other, CHIPS),
        )

    def rows_of(quarter):
        count = quarter_size - 1 if quarter == 3 else quarter_size
        part = r.replies.at[:, 0 : count * PAD, :]
        return remote(
            part, part, r.rows_send.at[quarter], r.rows_recv.at[quarter], 1 - core, chip
        )

    def pick(source):
        rank = r.rank[pl.ds(source, 1), :]
        code = r.code[pl.ds(source, 1), :]
        here_at = iota((CAPACITY, TOKENS), 0).astype(FULL) == rank
        found = jnp.sum(jnp.where(here_at, code, 0.0), axis=1, keepdims=True)
        sent = jnp.floor(found * (1.0 / 2048))
        row = found - sent * 2048.0 - 1.0
        chosen = (iota((CAPACITY, VOCAB_ROWS), 1).astype(FULL) == row).astype(LOW)
        at = pl.ds(pl.multiple_of(source * PAD, 16), PAD)
        source_sent = sent + (source * PAD).astype(FULL)
        for group in range(GROUPS):
            part = slice(group * PAD, (group + 1) * PAD)
            r.chosen[group, at, :] = chosen[part]
            r.found[group, at, 0:1] = row[part]
            r.found[group, at, 1:2] = source_sent[part]

    def quarter_rows(quarter):
        now = lax.rem(lax.div(me, quarter_size) + 1 + quarter, 4)

        def pick_two(index):
            pick(now * quarter_size + 2 * index)
            pick(now * quarter_size + 2 * index + 1)

        every(0, quarter_size // 2, pick_two)
        span = pl.ds(pl.multiple_of(now * quarter_size * PAD, 128), quarter_size * PAD)
        for start in range(0, WIDTH, BLOCK):
            lanes = slice(start, start + BLOCK)
            picked = r.chosen[:, span, :].reshape(GROUPS * quarter_size * PAD, VOCAB_ROWS)
            found_rows = dot(picked, r.table[:, lanes]).astype(LOW)
            r.rows[:, span, lanes] = found_rows.reshape(GROUPS, quarter_size * PAD, BLOCK)

        def send(index):
            other = now * quarter_size + lax.rem(lax.rem(me, quarter_size) + index, quarter_size)
            rows_copy(other, quarter).start()

        every(lax.div(quarter, 3), quarter_size, send)
        pl.when(quarter == 0)(partial(move, (moves_a, 0)))
        pl.when(quarter == 1)(partial(move, (moves_b, 0)))
        pl.when(quarter == 2)(partial(move, (moves_a, 2)))
        pl.when(quarter == 3)(partial(move, (moves_b, 2)))

    every(0, 4, quarter_rows)
    begin_c()
    own_at = pl.ds(pl.multiple_of(me * PAD, 16), PAD)
    r.replies[:, own_at, :] = r.rows[:, own_at, :]

    move((moves_a, 4))

    small_here = pl.ds(pl.multiple_of(chip * 128, 128), 128)
    lines = [r.bq, r.bv, r.bo, r.g1, r.s1, r.bdown, r.g2, r.s2]
    lines = [line[...].reshape(1, depth).astype(FULL) for line in lines]
    up_line = r.bup[...].reshape(1, deep).astype(FULL)
    lines += [up_line[:, part * depth : (part + 1) * depth] for part in range(deep // depth)]
    lines.append(jnp.zeros((PAD - len(lines), depth), FULL))
    own_small = jnp.concatenate(lines, axis=0)
    own_small = jnp.concatenate([own_small, jnp.zeros((PAD, 128 - depth), FULL)], axis=1)
    r.smalls[:, small_here] = own_small.astype(LOW)

    def small_copy(step):
        part = r.smalls.at[:, small_here]
        to_chip = lax.rem(chip + step, CHIPS)
        return remote(part, part, r.small_send.at[0], r.small_recv.at[0], core, to_chip)

    def all_smalls():
        part = r.smalls.at[:, 0 : (CHIPS - 1) * 128]
        return remote(part, part, r.small_send.at[0], r.small_recv.at[0], 1 - core, chip)

    every(1, CHIPS, lambda step: small_copy(step).start())
    move((moves_b, 4))

    own_row = jnp.concatenate([r.ids[j : j + 1, :] for j in range(TOKENS // 128)], axis=1)
    owner_row = over(own_row, VOCAB_ROWS).astype(FULL)
    owner_col = as_column(owner_row)
    earlier = (owner_row == owner_col) & (iota((TOKENS, TOKENS), 1) < iota((TOKENS, TOKENS), 0))
    own_rank = jnp.sum(earlier.astype(FULL), axis=1, keepdims=True)
    own_group = jnp.floor(own_rank * (1.0 / PAD))
    own_slot = own_group * SLOT_ROWS + owner_col * PAD + (own_rank - own_group * PAD)
    r.slot_col[...] = own_slot
    r.slot_line[0:1, :] = as_row(own_slot)
    move((moves_a, 6), (moves_c, 0))

    at_sent = over(iota((1, TOKENS), 1), LONG)
    lens = jnp.concatenate(
        [r.lens[...].reshape(1, sentences).astype(FULL), jnp.zeros((1, PAD - sentences), FULL)],
        axis=1,
    )
    spread_lens = dot(
        jnp.broadcast_to(lens, (8, PAD)).astype(LOW),
        (iota((PAD, TOKENS), 0) == over(iota((PAD, TOKENS), 1), LONG)).astype(LOW),
    )[0:1]
    valid_row = ((iota((1, TOKENS), 1) - at_sent * LONG).astype(FULL) < spread_lens).astype(FULL)
    r.valid_line[0:1, :] = valid_row
    r.valid_col[...] = as_column(valid_row)
    half_block = BLOCK // 2
    stacked_shape = (4 * half_block, half_block)
    same = within(over(iota(stacked_shape, 0), LONG), 2) == over(iota(stacked_shape, 1), LONG)
    r.block_bias[...] = jnp.where(same, 0.0, MASK_FLOOR)
    r.valid_bias[0:1, :] = (1.0 - valid_row) * MASK_FLOOR

    slots = r.slots[...].reshape(1, DEVICES * sentences)
    gap = jnp.full((1, PAD - sentences), -2, jnp.int32)
    slot_line = jnp.concatenate(
        [
            part
            for device in range(DEVICES)
            for part in (slots[:, device * sentences : (device + 1) * sentences], gap)
        ],
        axis=1,
    )
    side_line = within(slot_line, 2) + jnp.where(slot_line < 0, 8, 0)
    pair_line = over(slot_line, 2)
    pairs = r.langs.shape[0]
    lang_line = r.langs[...].reshape(1, pairs).astype(FULL)
    lang_line = jnp.concatenate([lang_line, jnp.full((1, -pairs % 128), -1.0, FULL)], axis=1)
    lang_col = as_column(lang_line)
    same_lang = jnp.sum(jnp.where(lang_col == lang_line, 1.0, 0.0), axis=1, keepdims=True)
    per_pair = 1.0 / (2.0 * LANGS * same_lang)
    at_pair = iota((lang_line.shape[1], SLOT_ROWS), 0) == pair_line
    weight_line = jnp.sum(jnp.where(at_pair, per_pair, 0.0), axis=0, keepdims=True)
    r.pairs[0:1, :] = weight_line
    r.pairs[1:2, :] = pair_line.astype(FULL)
    r.pairs[2:3, :] = side_line.astype(FULL)
    r.pairs_col[:, 0:1] = as_column(weight_line)
    r.pairs_col[:, 1:2] = as_column(pair_line.astype(FULL))
    r.pairs_col[:, 2:3] = as_column(side_line.astype(FULL))
    move((moves_b, 6), (moves_c, 2))

    all_smalls().wait_recv()
    smalls = r.smalls[...].astype(FULL)
    r.vectors[:, 0:WIDTH] = jnp.concatenate(
        [smalls[:, at * 128 : at * 128 + depth] for at in range(CHIPS)], axis=1
    )
    r.up_bias[0:1, :] = jnp.concatenate(
        [
            smalls[8 + part : 9 + part, at * 128 : at * 128 + depth]
            for at in range(CHIPS)
            for part in range(deep // depth)
        ],
        axis=1,
    )

    def vector(index):
        return r.vectors[index : index + 1, :]

    r.qkv_bias[0:1, 0:WIDTH] = vector(0)
    r.qkv_bias[0:1, WIDTH : 2 * WIDTH] = jnp.zeros((1, WIDTH), FULL)
    r.qkv_bias[0:1, 2 * WIDTH : 3 * WIDTH] = vector(1)

    move((moves_a, 8), (moves_b, 8), (moves_c, 4))

    def first_row(source):
        code = jnp.where(r.rank[pl.ds(source, 1), :] >= 0.0, r.code[pl.ds(source, 1), :], 0.0)
        at_first = iota((PAD, TOKENS), 1) == iota((PAD, TOKENS), 0) * LONG
        found = jnp.sum(jnp.where(at_first, code, 0.0), axis=1, keepdims=True)
        row = found - jnp.floor(found * (1.0 / 2048)) * 2048.0 - 1.0
        r.found[GROUPS, pl.ds(pl.multiple_of(source * PAD, 16), PAD), 0:1] = row

    every(0, DEVICES, first_row)
    for group in range(GROUPS + 1):
        named = as_row(r.found[group, :, 0:1])
        by_row = iota((VOCAB_ROWS, SLOT_ROWS), 0).astype(FULL) == named
        r.by_row[:, group * SLOT_ROWS : (group + 1) * SLOT_ROWS] = by_row.astype(LOW)

    def order(tile):
        at = pl.ds(pl.multiple_of(tile * BLOCK, BLOCK), BLOCK)
        lanes = iota((BLOCK, GROUPS * SLOT_ROWS), 1).astype(FULL)
        r.qkv[at, 0 : GROUPS * SLOT_ROWS] = (r.slot_col[at, :] == lanes).astype(LOW)

    every(0, TOKENS // BLOCK, order)
    for group in range(GROUPS):
        slot_at = iota((SLOT_ROWS, TOKENS), 0) + group * SLOT_ROWS
        named = (slot_at.astype(FULL) == r.slot_line[0:1, :]).astype(LOW)
        r.slot_hot[group] = named
    moves_a[10]()
    moves_b[10]()
    finish_a()
    for quarter in range(4):
        rows_of(quarter).wait_recv()

    def embed(tile):
        at = pl.ds(pl.multiple_of(tile * BLOCK, BLOCK), BLOCK)
        replies = r.replies[:, :, at].reshape(GROUPS * SLOT_ROWS, BLOCK)
        r.embedded[:, at] = dot(r.qkv[:, 0 : GROUPS * SLOT_ROWS], replies).astype(LOW)

    every(0, WIDTH // BLOCK, embed)

    def project(tile):
        at = pl.ds(pl.multiple_of(tile * BLOCK, BLOCK), BLOCK)
        r.qkv[:, at] = (dot(r.embedded[...], r.wa[:, at]) + r.qkv_bias[0:1, at]).astype(LOW)

    move((moves_c, 6))
    every(0, 9, project)

    row_sent = within(iota((PAIR_ROWS, WIDTH), 0), PAD)
    row_head = over(iota((PAIR_ROWS, WIDTH), 0), PAD)
    lane_block = over(iota((PAIR_ROWS, WIDTH), 1), HEAD)
    in_head = row_head == lane_block
    seen = (row_sent == lane_block) & (r.valid_line[0:1, :] > 0.0)
    firsts = (iota((PAD, TOKENS), 1) == iota((PAD, TOKENS), 0) * LONG).astype(LOW)
    real_row = iota((PAD, 1), 0) < sentences

    def spread(rows):
        return jnp.where(in_head, jnp.concatenate([rows] * HEADS, axis=0), jnp.zeros((), LOW))

    def fold(tall):
        tall = jnp.where(in_head, tall, 0.0)
        return sum(tall[head * PAD : (head + 1) * PAD] for head in range(HEADS))

    keys, values = slice(WIDTH, 2 * WIDTH), slice(2 * WIDTH, 3 * WIDTH)
    embedded_cls = dot(firsts, r.embedded[...]).astype(LOW)
    query_cls = (dot(embedded_cls, r.wa[:, 0:WIDTH]) + vector(0)).astype(LOW)
    cls_scores = dot_turned(spread(query_cls), r.qkv[:, keys]) * scale
    cls_scores = jnp.where(seen, cls_scores, MASK_FLOOR)
    cls_peak = jnp.max(cls_scores, axis=1, keepdims=True)
    cls_exp = jnp.where(seen, jnp.exp(cls_scores - cls_peak), 0.0)
    cls_total = jnp.sum(cls_exp, axis=1, keepdims=True)
    cls_probs = cls_exp / jnp.where(cls_total > 0.0, cls_total, 1.0)
    probs_low = cls_probs.astype(LOW)
    r.probs[...] = cls_probs
    context_cls = fold(dot(probs_low, r.qkv[:, values])).astype(LOW)
    first_cls = (
        embedded_cls.astype(FULL)
        + dot(context_cls, r.wa[:, 3 * WIDTH : 4 * WIDTH])
        + vector(2)
    )
    normed_one, inverse_one = norm_parts(first_cls)
    r.normed_one[...] = normed_one
    hidden_cls = normed_one * vector(3) + vector(4)
    hidden_cls_low = hidden_cls.astype(LOW)
    early_here = r.early.at[here]
    early_here[:, 0:WIDTH] = hidden_cls_low
    early_here[:, WIDTH : 2 * WIDTH] = query_cls
    steps_u, drain_u = gather_steps(r.units, r.gather_send.at[0], r.gather_recv.at[0])
    steps_e, drain_e = gather_steps(r.early, r.gather_send.at[1], r.gather_recv.at[1])
    steps_d, drain_d = gather_steps(r.downs, r.gather_send.at[2], r.gather_recv.at[2])
    steps_a, drain_a2 = gather_steps(r.attends, r.gather_send.at[3], r.gather_recv.at[3])
    steps_q, drain_q = gather_steps(r.queries, r.gather_send.at[4], r.gather_recv.at[4])
    steps_e[0]()

    def attend(unit):
        rows = pl.ds(pl.multiple_of(unit * half_block, half_block), half_block)
        lane_head = over(iota((half_block, BLOCK), 1), HEAD)
        bias = r.block_bias[...] + r.valid_bias[0:1, rows]

        def part(which, lane):
            return r.qkv[rows, which * WIDTH + lane : which * WIDTH + lane + BLOCK]

        for lane in range(0, WIDTH, BLOCK):
            query = part(0, lane) * jnp.asarray(scale, LOW)
            key, value = part(1, lane), part(2, lane)
            stacked = jnp.concatenate(
                [jnp.where(lane_head == head, query, jnp.zeros((), LOW)) for head in range(4)],
                axis=0,
            )
            scores = dot_turned(stacked, key) + bias
            shifted = jnp.exp(scores - jnp.max(scores, axis=1, keepdims=True))
            probs = shifted * (1.0 / jnp.sum(shifted, axis=1, keepdims=True))
            mixed = dot(probs.astype(LOW), value)
            result = mixed[0:half_block]
            for head in range(1, 4):
                result = jnp.where(
                    lane_head == head, mixed[head * half_block : (head + 1) * half_block], result
                )
            r.context[rows, lane : lane + BLOCK] = result.astype(LOW)

    def open_tile(tile):
        at = pl.ds(pl.multiple_of(tile * BLOCK, BLOCK), BLOCK)
        attended = dot(r.context[at, :], r.wa[:, 3 * WIDTH : 4 * WIDTH]) + vector(2)
        normed, _ = norm_parts(r.embedded[at, :].astype(FULL) + attended)
        hidden = normed * vector(3) + vector(4)
        r.context[at, :] = hidden.astype(LOW)
        r.table_full[at, :] = hidden + vector(5)

    most = SLOT_ROWS
    rest_at = pl.ds(most, TOKENS - most)

    def up_product(part):
        at = pl.ds(pl.multiple_of(part * BLOCK, BLOCK), BLOCK)
        return dot(r.context[...], r.wb[:, at]) + r.up_bias[0:1, at]

    def feed_up(part, last=False):
        active = gelu(r.tile_up[...]).astype(LOW)
        if not last:
            r.tile_up[...] = up_product(part + 1)
        lanes = pl.ds(pl.multiple_of(lax.rem(part, 4) * BLOCK, BLOCK), BLOCK)
        r.chosen[lax.div(part, 4), :, lanes] = active[:most]
        rest = pl.ds(pl.multiple_of(lax.div(part, 6) * BLOCK, BLOCK), BLOCK)
        lanes = pl.ds(pl.multiple_of(lax.rem(part, 6) * BLOCK, BLOCK), BLOCK)
        r.slopes[rest, lanes] = active[most:]

    def feed_down(part):
        lanes = pl.ds(pl.multiple_of(part * BLOCK, BLOCK), BLOCK)
        total = r.table_full[0:most, lanes]
        for group in range(GROUPS):
            rows = slice(group * VOCAB_ROWS, (group + 1) * VOCAB_ROWS)
            total = total + dot(r.chosen[group], r.wc[rows, lanes])
        r.table_full[0:most, lanes] = total

    def feed_rest(part):
        lanes = pl.ds(pl.multiple_of(part * BLOCK, BLOCK), BLOCK)
        low_part = dot(r.slopes[0:BLOCK, :], r.wc[0 : WIDE // 2, lanes])
        high_part = dot(r.slopes[BLOCK : 2 * BLOCK, :], r.wc[WIDE // 2 :, lanes])
        r.table_full[rest_at, lanes] += low_part + high_part

    def layer_copy(tile):
        at = pl.ds(pl.multiple_of(tile * BLOCK, BLOCK), BLOCK)
        return pltpu.make_async_copy(r.context.at[at], r.layer_out.at[at], r.out_sem.at[tile])

    def close_tile(tile):
        at = pl.ds(pl.multiple_of(tile * BLOCK, BLOCK), BLOCK)
        normed, _ = norm_parts(r.table_full[at, :])
        out = normed * vector(6) + vector(7)
        r.context[at, :] = (out * r.valid_col[at, :]).astype(LOW)
        layer_copy(tile).start()

    finish_b()
    r.hidden_cls[...] = hidden_cls_low

    def up_part(part):
        at = pl.ds(pl.multiple_of(part * WIDTH, BLOCK), WIDTH)
        active, slope = gelu_parts(dot(r.hidden_cls[...], r.wb[:, at]) + r.up_bias[0:1, at])
        r.active_cls[:, at] = active.astype(LOW)
        r.slope_cls[:, at] = slope

    every(0, WIDE // WIDTH, up_part)
    steps_e[1]()

    def attend_step(pair):
        attend(2 * pair)
        attend(2 * pair + 1)
        pl.when(pair == 0)(partial(move, (moves_c, 8)))
        pl.when(pair == 1)(moves_c[10])
        pl.when(pair == 2)(steps_e[2])

    every(0, 3, attend_step)
    finish_c()

    def pack_tall(target, first_row, act):
        def run(part):
            window = jnp.minimum(lax.div(part * 2 * depth, 128) * 128, WIDTH - BLOCK)
            shape = (BLOCK, BLOCK)
            lane = within(iota(shape, 1), 128)
            column = over(iota(shape, 1), 128) * depth + lane + (part * 2 * depth - window)
            select = ((iota(shape, 0) == column) & (lane < depth)).astype(LOW)
            taken = dot(r.tall[:, pl.ds(pl.multiple_of(window, 128), BLOCK)], select)

            def beside(low, high):
                return [
                    low[:, one * 128 : (one + 1) * 128]
                    + pltpu.roll(high[:, one * 128 : (one + 1) * 128], depth, 1)
                    for one in range(2)
                ]

            for half in range(CORES):
                base = half * PAIR_ROWS // 2
                both = beside(taken[base : base + 48], taken[base + 48 : base + 96])
                for one in range(2):
                    at = half * CHIPS + 2 * part + one
                    target[at, first_row : first_row + 48, :] = act(
                        2 * part + one, both[one]
                    ).astype(LOW)
            if first_row:
                left = beside(taken[PAIR_ROWS : PAIR_ROWS + PAD], taken[PAIR_ROWS + PAD :])
                for half in range(CORES):
                    for one in range(2):
                        target[half * CHIPS + 2 * part + one, 0:PAD, :] = left[one].astype(LOW)

        return run

    def pack_coefs(coefs):
        shape = (2 * PAIR_ROWS, GROUPS * 128)
        row, lane = iota(shape, 0), iota(shape, 1)
        kind = jnp.where(row >= PAIR_ROWS, PAD, 0)
        head = over(row, PAD) - jnp.where(row >= PAIR_ROWS, HEADS, 0)
        folds = head + kind + over(lane, 128) * 2 * PAD == within(lane, 128)
        lanes = contract(coefs, folds.astype(LOW), 0, 0).astype(LOW)
        total = None
        for group in range(GROUPS):
            part = dot(r.slot_hot[group], lanes[:, group * 128 : (group + 1) * 128])
            total = part if total is None else total + part
        return total.astype(LOW).reshape(DEVICES, PAD, 128)


    def down_part(part):
        at = pl.ds(pl.multiple_of(part * BLOCK, BLOCK), BLOCK)
        r.wide_cls[:, at] = dot(r.active_cls[...], r.wc[:, at])

    every(0, WIDTH // BLOCK, down_part)
    down_pre = r.wide_cls[:, 0:WIDTH] + vector(5)
    normed_two, inverse_two = norm_parts(hidden_cls + down_pre)
    summary = normed_two * vector(6) + vector(7)
    magnitude = jnp.sqrt(jnp.sum(summary * summary, axis=-1, keepdims=True) + EPSILON)
    unit = jnp.where(real_row, summary / magnitude, 0.0)
    r.units[here] = unit.astype(LOW)

    steps_u[0]()
    r.tall[0:PAIR_ROWS, :] = dot(probs_low, r.embedded[...]).astype(LOW)
    r.tall[PAIR_ROWS : PAIR_ROWS + PAD, :] = context_cls
    r.tall[PAIR_ROWS + PAD :, :] = embedded_cls
    pack_one = pack_tall(r.mail_one, PAD, lambda at, both: both)

    def pack_one_step(pair):
        pack_one(2 * pair)
        pack_one(2 * pair + 1)
        pl.when(pair == 0)(steps_u[1])
        pl.when(pair == 2)(steps_u[2])

    every(0, CHIPS // 4, pack_one_step)
    steps_u[3]()

    def post_one(box, got, index, step):
        other, to_core, to_chip = peer(step)
        remote(
            box.at[other], got.at[me], r.one_send.at[index], r.one_recv.at[index], to_core, to_chip
        ).start()

    r.got_one[me] = r.mail_one[me]

    def open_step(tile):
        open_tile(tile)
        pl.when(tile == 0)(steps_e[3])
        pl.when(tile == 2)(steps_u[4])

    def feed_step(steps, part):
        feed_up(part)
        for index in range(3):
            step = 3 * part + index + 1
            pl.when(step < DEVICES)(partial(post_one, r.mail_one, r.got_one, 1, step))
        for index, step in steps:
            pl.when(part == index)(step)

    first_parts, parts = 6, WIDE // BLOCK
    every(0, TOKENS // BLOCK, open_step)
    r.tile_up[...] = up_product(0)
    every(0, first_parts, partial(feed_step, [(1, steps_u[5]), (2, steps_e[4]), (5, steps_e[5])]))

    units = r.units[...].reshape(SLOT_ROWS, WIDTH)
    weight_row, pair_row, side_row = r.pairs[0:1, :], r.pairs[1:2, :], r.pairs[2:3, :]

    def pair_scores(rows, pair_col, side_col):
        opposite = side_col + side_row == 1.0
        partner = opposite & (pair_col == pair_row)
        raw = SCORE_SCALE * dot_turned(rows, units)
        shifted = jnp.where(partner, raw - SCORE_SCALE * MARGIN_WIDTH, raw)
        return jnp.where(opposite, shifted, MASK_FLOOR), partner

    every_score, every_partner = pair_scores(
        units, r.pairs_col[:, 1:2], r.pairs_col[:, 2:3]
    )
    peak_row = jnp.max(every_score, axis=0, keepdims=True)
    log_row = peak_row + jnp.log(
        jnp.sum(jnp.exp(every_score - peak_row), axis=0, keepdims=True)
    )
    picked_row = jnp.sum(jnp.where(every_partner, every_score, 0.0), axis=0, keepdims=True)
    r.loss[...] = jnp.sum(weight_row * (log_row - picked_row), axis=1, keepdims=True)

    rows_here = pl.ds(pl.multiple_of(me * PAD, 16), PAD)
    own_score, own_partner = pair_scores(
        r.units[here], r.pairs_col[rows_here, 1:2], r.pairs_col[rows_here, 2:3]
    )
    own_partner = own_partner.astype(FULL)
    own_peak = jnp.max(own_score, axis=1, keepdims=True)
    own_exp = jnp.exp(own_score - own_peak)
    own_share = own_exp / jnp.sum(own_exp, axis=1, keepdims=True)
    by_row = (r.pairs_col[rows_here, 0:1] * (own_share - own_partner)).astype(LOW)
    by_column = (weight_row * (jnp.exp(own_score - log_row) - own_partner)).astype(LOW)
    unit_grad = SCORE_SCALE * (dot(by_row, units) + dot(by_column, units))
    along = jnp.sum(unit * unit_grad, axis=-1, keepdims=True)
    summary_grad = (unit_grad - unit * along) / magnitude

    residual_grad, grad_g2, grad_s2 = norm_back_parts(
        summary_grad, normed_two, inverse_two, vector(6)
    )
    down_grad = residual_grad.astype(LOW)
    r.downs[here] = down_grad
    steps_d[0]()
    r.hidden_cls[...] = down_grad

    def up_back(part):
        at = pl.ds(pl.multiple_of(part * WIDTH, BLOCK), WIDTH)
        act_grad = dot_turned(r.hidden_cls[...], r.wc[at, :])
        r.active_cls[:, at] = (act_grad * r.slope_cls[:, at]).astype(LOW)

    every(0, WIDE // WIDTH, up_back)
    steps_d[1]()

    def hidden_back(part):
        at = pl.ds(pl.multiple_of(part * BLOCK, BLOCK), BLOCK)
        r.wide_cls[:, at] = dot_turned(r.active_cls[...], r.wb[at, :])

    every(0, WIDTH // BLOCK, hidden_back)
    hidden_grad = r.wide_cls[:, 0:WIDTH] + residual_grad
    first_grad, grad_g1, grad_s1 = norm_back_parts(
        hidden_grad, r.normed_one[...], inverse_one, vector(3)
    )
    attend_grad = first_grad.astype(LOW)
    context_grad = dot_turned(attend_grad, r.wa[:, 3 * WIDTH : 4 * WIDTH]).astype(LOW)
    attend_here = r.attends.at[here]
    attend_here[:, 0:WIDTH] = attend_grad
    attend_here[:, WIDTH : 2 * WIDTH] = context_grad
    steps_a[0]()
    steps_d[2]()
    context_tall = spread(context_grad)
    probs = r.probs[...]
    prob_grad = dot_turned(context_tall, r.qkv[:, values])
    inner = jnp.sum(probs * prob_grad, axis=1, keepdims=True)
    score_grad = (probs * (prob_grad - inner)).astype(LOW)
    steps_a[1]()
    r.mail_two[:, 48:64, :] = pack_coefs(jnp.concatenate([probs_low, score_grad], axis=0))
    r.got_two[me, 48:64, :] = r.mail_two[me, 48:64, :]
    query_grad = (fold(dot(score_grad, r.qkv[:, keys])) * scale).astype(LOW)
    probs_total = jnp.sum(probs_low.astype(FULL), axis=1, keepdims=True)
    grad_bvalue = jnp.sum(probs_total * context_tall.astype(FULL), axis=0, keepdims=True)
    grad_bquery = jnp.sum(query_grad.astype(FULL), axis=0, keepdims=True)
    r.queries[here] = query_grad
    own_sums = jnp.concatenate(
        [jnp.zeros((2 * depth, WIDTH), FULL)]
        + [grad_bquery, grad_bvalue, grad_g1, grad_s1, grad_g2, grad_s2]
        + [jnp.zeros((128 - 2 * depth - 6, WIDTH), FULL)],
        axis=0,
    )
    r.own_sums[...] = jnp.transpose(own_sums)
    steps_q[0]()
    steps_a[2]()
    r.tall[0:PAIR_ROWS, :] = (dot(score_grad, r.embedded[...]) * scale).astype(LOW)

    def with_sums(at, both):
        return both + r.own_sums[pl.ds(pl.multiple_of(at * depth, 16), depth), :]

    pack_two = pack_tall(r.mail_two, 0, with_sums)

    def send_two(at):
        remote(
            r.mail_two.at[at],
            r.got_two.at[me],
            r.one_send.at[2],
            r.one_recv.at[2],
            lax.div(at, CHIPS),
            lax.rem(at, CHIPS),
        ).start()

    def pack_two_step(step):
        pair = lax.rem(step + lax.div(chip, 4), CHIPS // 4)
        pack_two(2 * pair)
        pack_two(2 * pair + 1)
        for half in range(CORES):
            for one in range(4):
                at = half * CHIPS + 4 * pair + one
                pl.when(at != me)(partial(send_two, at))

    every(0, CHIPS // 4, pack_two_step)
    r.got_two[me, 0:48, :] = r.mail_two[me, 0:48, :]
    steps_q[1]()

    def all_rows(buffer, start, width=WIDTH):
        return buffer[:, :, :, :, start : start + width].reshape(SLOT_ROWS, width)

    quarter_rows_count = quarter_size * PAD

    def from_sent(quarter):
        span = pl.ds(pl.multiple_of(quarter * quarter_rows_count, 128), quarter_rows_count)
        shape = (GROUPS * quarter_rows_count, quarter_rows_count)
        lanes = (iota(shape, 1) + quarter * quarter_rows_count).astype(FULL)
        named = r.found[0:GROUPS, span, 1:2].reshape(GROUPS * quarter_rows_count, 1)
        return (named == lanes).astype(LOW), span

    def quarter_part(buffer, quarter, start):
        planes = pl.ds(lax.rem(quarter, 2) * 2, 2)
        part = buffer[lax.div(quarter, 2), planes, :, :, start : start + BLOCK]
        return part.reshape(quarter_rows_count, BLOCK)

    def widened(coefs, group, start, kind):
        lane_head = over(iota((128, BLOCK), 1) + start, HEAD)
        lanes = iota((128, BLOCK), 0) == lane_head + group * 2 * PAD + kind
        return dot(coefs, lanes.astype(LOW))

    half_wide = WIDE // 2

    def slope_tile(part):
        at = pl.ds(pl.multiple_of(core * half_wide + part * BLOCK, BLOCK), BLOCK)
        up_pre = dot(all_rows(r.early, 0), r.wb[:, at]) + r.up_bias[0:1, at]
        _, slope = gelu_parts(up_pre)
        r.slopes[:, pl.ds(pl.multiple_of(part * BLOCK, BLOCK), BLOCK)] = slope.astype(LOW)

    def slot_queries(quarter):
        sents, span = from_sent(quarter)
        for start in range(0, WIDTH, BLOCK):
            rows = dot(sents, quarter_part(r.early, quarter, WIDTH + start)).astype(LOW)
            rows = rows.reshape(GROUPS, quarter_rows_count, BLOCK)
            r.slot_query[:, span, start : start + BLOCK] = rows

    def activate():
        at = pl.ds(pl.multiple_of(chip // 2 * 2 * deep, 128), 2 * deep)
        up_pre = dot(all_rows(r.early, 0), r.wb[:, at]) + r.up_bias[0:1, at]
        r.active_turned[...] = jnp.transpose(gelu(up_pre)).astype(LOW)
        r.hidden_turned[...] = jnp.transpose(all_rows(r.early, 0))

    rest = [steps_d[3], steps_a[3], steps_q[2], steps_d[4], steps_a[4]]
    rest = [(first_parts + index, step) for index, step in enumerate(rest)]
    every(first_parts, parts - 1, partial(feed_step, rest))
    feed_up(parts - 1, last=True)

    def rest_step(part):
        feed_rest(part)
        for index, step in enumerate([steps_q[3], steps_d[5], steps_a[5]]):
            pl.when(part == index)(step)

    every(0, WIDTH // BLOCK, rest_step)
    steps_q[4]()

    def down_step(part):
        feed_down(part)
        for index, ends in enumerate([[drain_a, drain_b], [drain_c, drain_u], [drain_e]]):
            for end in ends:
                pl.when(part == index)(end)

    every(0, WIDTH // BLOCK, down_step)
    every(0, TOKENS // BLOCK, close_tile)
    every(0, 4, slot_queries)

    def slope_two(pair):
        slope_tile(2 * pair)
        slope_tile(2 * pair + 1)

    every(0, 3, slope_two)
    activate()

    all_but_one(r.got_one, 1).wait_recv()
    all_but_one(r.got_two, 2).wait_recv()
    def slot_probs(group):
        got = r.got_two[:, 48:64, :].reshape(SLOT_ROWS, 128)
        for start in range(0, WIDTH, BLOCK):
            r.replies[group, :, start : start + BLOCK] = widened(got, group, start, 0).astype(LOW)

    def slot_values(quarter):
        sents, span = from_sent(quarter)
        for start in range(0, WIDTH, BLOCK):
            lanes = slice(start, start + BLOCK)
            rows = dot(sents, quarter_part(r.attends, quarter, WIDTH + start))
            rows = rows.reshape(GROUPS, quarter_rows_count, BLOCK)
            rows = r.replies[:, span, lanes].astype(FULL) * rows
            r.replies[:, span, lanes] = rows.astype(LOW)

    every(0, GROUPS, slot_probs)
    every(0, 4, slot_values)

    def head_products(got, first_row, right, start, target):
        def one_head(head):
            lane = core * (WIDTH // 2) + lax.div(head, 2) * 128
            pair_rows = right[:, :, :, :, pl.ds(pl.multiple_of(start + lane, 128), 128)]
            row = pl.ds(pl.multiple_of(first_row + lax.rem(head, 3) * PAD, 16), PAD)
            block_rows = got[:, row, :].reshape(SLOT_ROWS, 128)
            r.product[...] = contract(block_rows, pair_rows.reshape(SLOT_ROWS, 128), 0, 0)
            part = r.product[pl.ds(pl.multiple_of(lax.div(head, 3) * depth, 16), depth), :]
            at = pl.ds(pl.multiple_of(lane, 128), 128)
            own_lanes = over(iota((depth, 128), 1), HEAD) == lax.rem(head, 2)
            target[:, at] = jnp.where(own_lanes, part, target[:, at])

        every(0, HEADS // 2, one_head)

    def half_of(ref, at_core):
        half = ref.shape[1] // 2
        return ref.at[:, pl.ds(pl.multiple_of(at_core * half, 128), half)]

    def half_copy(index, ref, at_core):
        part = half_of(ref, at_core)
        return remote(part, part, r.half_send.at[index], r.half_recv.at[index], 1 - core, chip)

    own_half = pl.ds(pl.multiple_of(core * (WIDTH // 2), 128), WIDTH // 2)
    r.g_wv[:, own_half] = jnp.zeros((depth, WIDTH // 2), FULL)
    r.g_wk[:, own_half] = jnp.zeros((depth, WIDTH // 2), FULL)
    head_products(r.got_one, PAD, r.attends, WIDTH, r.g_wv)
    half_copy(0, r.g_wv, core).start()

    downs = r.downs[...].reshape(SLOT_ROWS, WIDTH)
    attends = all_rows(r.attends, 0)

    def up_tile(part):
        at = pl.ds(pl.multiple_of(core * half_wide + part * BLOCK, BLOCK), BLOCK)
        slope = r.slopes[:, pl.ds(pl.multiple_of(part * BLOCK, BLOCK), BLOCK)].astype(FULL)
        up_all = (dot_turned(r.downs[...].reshape(SLOT_ROWS, WIDTH), r.wc[at, :]) * slope)
        up_all = up_all.astype(LOW)
        r.g_wup[0:depth, at] = dot(r.hidden_turned[mine, :], up_all)
        total = jnp.sum(up_all.astype(FULL), axis=0, keepdims=True)
        r.g_wup[depth : depth + 8, at] = jnp.broadcast_to(total, (8, BLOCK))

    every(0, half_wide // BLOCK, up_tile)
    half_copy(1, r.g_wup, core).start()
    r.g_wdown[...] = dot(r.active_turned[pl.ds(pl.multiple_of(chip % 2 * deep, 16), deep), :], downs)
    r.left_turned[...] = jnp.transpose(r.got_one[:, 0:PAD, :].reshape(SLOT_ROWS, 128))
    r.g_wo[...] = dot(r.left_turned[0:depth, :], attends)

    def own_part(rows, size):
        start = chip * size
        window = jnp.minimum(lax.div(start, 128) * 128, rows.shape[1] - BLOCK)
        part = rows[:, pl.ds(pl.multiple_of(window, 128), BLOCK)]
        return pltpu.roll(part, lax.rem(BLOCK + window - start, BLOCK), 1)

    for quarter in range(4):
        rows_of(quarter).wait_send()

    def slot_grads(group):
        got_scores = r.got_two[:, 48:64, :].reshape(SLOT_ROWS, 128)
        for start in range(0, WIDTH, BLOCK):
            lanes = slice(start, start + BLOCK)
            rows = r.slot_query[group, :, lanes].astype(FULL)
            rows = widened(got_scores, group, start, PAD) * rows * scale
            r.slot_query[group, :, lanes] = rows.astype(LOW)
        for start in range(0, WIDTH, BLOCK):
            lanes = slice(start, start + BLOCK)
            row_grad = dot_turned(r.slot_query[group], r.wa[lanes, keys])
            row_grad = row_grad + dot_turned(r.replies[group], r.wa[lanes, values])
            r.rows[group, :, lanes] = row_grad.astype(LOW)

    every(0, GROUPS, slot_grads)
    steps_q[5]()
    query_grads = all_rows(r.queries, 0)
    extra = dot_turned(query_grads, r.wa[:, 0:WIDTH]) + attends.astype(FULL)
    r.extra[...] = extra.astype(LOW)
    r.g_wq[...] = dot(r.left_turned[depth : 2 * depth, :], query_grads)

    half_rows = VOCAB_ROWS // 2

    def table_copy(tile):
        at = pl.ds(pl.multiple_of(tile * half_rows, BLOCK), half_rows)
        return pltpu.make_async_copy(
            r.table_full.at[at], r.table_grad.at[at], r.table_sem.at[tile]
        )

    def table_tile(tile):
        at = pl.ds(pl.multiple_of(tile * half_rows, BLOCK), half_rows)
        for start in range(0, WIDTH, BLOCK):
            lanes = slice(start, start + BLOCK)
            slot_rows = r.rows[:, :, lanes].reshape(GROUPS * SLOT_ROWS, BLOCK)
            r.table_full[at, lanes] = dot(r.by_row[at, 0 : GROUPS * SLOT_ROWS], slot_rows) + dot(
                r.by_row[at, GROUPS * SLOT_ROWS :], r.extra[:, lanes]
            )
        table_copy(tile).start()

    every(0, 2, table_tile)
    head_products(r.got_two, 0, r.early, WIDTH, r.g_wk)
    half_copy(2, r.g_wk, core).start()

    down_total = jnp.sum(downs.astype(FULL), axis=0, keepdims=True)
    attend_total = jnp.sum(attends.astype(FULL), axis=0, keepdims=True)
    sums = jnp.sum(r.got_two[:, 0:48, :].astype(FULL), axis=0)
    sums = jnp.concatenate([sums, jnp.zeros((128 - 48, 128), FULL)], axis=0)
    r.totals[...] = jnp.concatenate([attend_total, down_total, jnp.zeros((6, WIDTH), FULL)], axis=0)
    r.g_small[8:16, :] = own_part(r.totals, depth)
    r.g_small[0:8, 0:128] = jnp.transpose(sums)[2 * depth : 2 * depth + 8, :]
    r.g_small[0:8, 128:BLOCK] = jnp.zeros((8, BLOCK - 128), FULL)
    half_copy(1, r.g_wup, 1 - core).wait_recv()
    r.g_small[16:24, :] = own_part(r.g_wup.at[depth : depth + 8, :], deep)

    half_copy(0, r.g_wv, 1 - core).wait_recv()
    half_copy(2, r.g_wk, 1 - core).wait_recv()
    for index, ref in enumerate([r.g_wv, r.g_wup, r.g_wk]):
        half_copy(index, ref, core).wait_send()

    for index, ref in enumerate([r.every_ids, r.got_one, r.got_two]):
        all_but_one(ref, index).wait_send()
    all_smalls().wait_send()
    for end in [drain_d, drain_a2, drain_q]:
        end()
    every(0, TOKENS // BLOCK, lambda tile: layer_copy(tile).wait())
    every(0, 2, lambda tile: table_copy(tile).wait())


def layer(inputs):
    dma = pltpu.SemaphoreType.DMA
    vmem = pl.BlockSpec(memory_space=pltpu.VMEM)
    anywhere = pl.BlockSpec(memory_space=pl.ANY)
    depth, deep = WIDTH // CHIPS, WIDE // CHIPS

    def gathered(width):
        return pltpu.VMEM((CORES, PLANES, LINES, PAD, width), LOW)

    outputs = dict(
        layer_out=((TOKENS, WIDTH), LOW),
        table_grad=((VOCAB_ROWS, WIDTH), FULL),
        g_wq=((depth, WIDTH), FULL),
        g_wk=((depth, WIDTH), FULL),
        g_wv=((depth, WIDTH), FULL),
        g_wo=((depth, WIDTH), FULL),
        g_wup=((depth + 8, WIDE), FULL),
        g_wdown=((deep, WIDTH), FULL),
        g_small=((24, BLOCK), FULL),
        loss=((1, 1), FULL),
    )
    scratch = dict(
        ids=pltpu.VMEM((8, 128), jnp.int32),
        every_ids=pltpu.VMEM((DEVICES, 8, 128), jnp.int32),
        rank=pltpu.VMEM((DEVICES, TOKENS), FULL),
        code=pltpu.VMEM((DEVICES, TOKENS), FULL),
        found=pltpu.VMEM((GROUPS + 1, SLOT_ROWS, 2), FULL),
        block_bias=pltpu.VMEM((2 * BLOCK, BLOCK // 2), FULL),
        valid_bias=pltpu.VMEM((8, TOKENS), FULL),
        slot_col=pltpu.VMEM((TOKENS, 1), FULL),
        slot_line=pltpu.VMEM((8, TOKENS), FULL),
        valid_col=pltpu.VMEM((TOKENS, 1), FULL),
        valid_line=pltpu.VMEM((8, TOKENS), FULL),
        pairs=pltpu.VMEM((8, SLOT_ROWS), FULL),
        pairs_col=pltpu.VMEM((SLOT_ROWS, 128), FULL),
        vectors=pltpu.VMEM((PAD, WIDTH), FULL),
        up_bias=pltpu.VMEM((8, WIDE), FULL),
        qkv_bias=pltpu.VMEM((8, 3 * WIDTH), FULL),
        smalls=pltpu.VMEM((PAD, CHIPS * 128), LOW),
        wa=pltpu.VMEM((WIDTH, 4 * WIDTH), LOW),
        wb=pltpu.VMEM((WIDTH, WIDE), LOW),
        wc=pltpu.VMEM((WIDE, WIDTH), LOW),
        chosen=pltpu.VMEM((GROUPS, SLOT_ROWS, VOCAB_ROWS), LOW),
        by_row=pltpu.VMEM((VOCAB_ROWS, (GROUPS + 1) * SLOT_ROWS), LOW),
        rows=pltpu.VMEM((GROUPS, SLOT_ROWS, WIDTH), LOW),
        replies=pltpu.VMEM((GROUPS, SLOT_ROWS, WIDTH), LOW),
        slot_query=pltpu.VMEM((GROUPS, SLOT_ROWS, WIDTH), LOW),
        extra=pltpu.VMEM((SLOT_ROWS, WIDTH), LOW),
        hidden_cls=pltpu.VMEM((PAD, WIDTH), LOW),
        active_cls=pltpu.VMEM((PAD, WIDE), LOW),
        slope_cls=pltpu.VMEM((PAD, WIDE), FULL),
        wide_cls=pltpu.VMEM((PAD, WIDTH), FULL),
        tall=pltpu.VMEM((PAIR_ROWS + 2 * PAD, WIDTH), LOW),
        own_sums=pltpu.VMEM((WIDTH, 128), FULL),
        product=pltpu.VMEM((128, 128), FULL),
        slot_hot=pltpu.VMEM((GROUPS, SLOT_ROWS, TOKENS), LOW),
        tile_up=pltpu.VMEM((TOKENS, BLOCK), FULL),
        embedded=pltpu.VMEM((TOKENS, WIDTH), LOW),
        qkv=pltpu.VMEM((TOKENS, 3 * WIDTH), LOW),
        context=pltpu.VMEM((TOKENS, WIDTH), LOW),
        table_full=pltpu.VMEM((VOCAB_ROWS, WIDTH), FULL),
        probs=pltpu.VMEM((PAIR_ROWS, TOKENS), FULL),
        normed_one=pltpu.VMEM((PAD, WIDTH), FULL),
        units=gathered(WIDTH),
        early=gathered(2 * WIDTH),
        downs=gathered(WIDTH),
        attends=gathered(2 * WIDTH),
        queries=gathered(WIDTH),
        slopes=pltpu.VMEM((SLOT_ROWS, WIDE // 2), LOW),
        hidden_turned=pltpu.VMEM((WIDTH, SLOT_ROWS), LOW),
        active_turned=pltpu.VMEM((2 * deep, SLOT_ROWS), LOW),
        left_turned=pltpu.VMEM((128, SLOT_ROWS), LOW),
        totals=pltpu.VMEM((8, WIDTH), FULL),
        mail_one=pltpu.VMEM((DEVICES, 64, 128), LOW),
        got_one=pltpu.VMEM((DEVICES, 64, 128), LOW),
        mail_two=pltpu.VMEM((DEVICES, 64, 128), LOW),
        got_two=pltpu.VMEM((DEVICES, 64, 128), LOW),
        rows_send=dma((4,)),
        rows_recv=dma((4,)),
        one_send=dma((4,)),
        one_recv=dma((4,)),
        small_send=dma((1,)),
        small_recv=dma((1,)),
        weight_send=dma((3, 7)),
        weight_recv=dma((3, 18)),
        gather_send=dma((5, 13)),
        gather_recv=dma((5, 13)),
        half_send=dma((3,)),
        half_recv=dma((3,)),
        out_sem=dma((TOKENS // BLOCK,)),
        table_sem=dma((2,)),
    )
    names = INPUTS + OUTPUTS + list(scratch)
    return pl.pallas_call(
        partial(layer_kernel, names),
        out_shape=tuple(jax.ShapeDtypeStruct(*outputs[name]) for name in OUTPUTS),
        in_specs=[vmem] * len(INPUTS),
        out_specs=(anywhere, anywhere) + (vmem,) * (len(OUTPUTS) - 2),
        scratch_shapes=list(scratch.values()),
        compiler_params=pltpu.CompilerParams(
            collective_id=0, has_side_effects=True, vmem_limit_bytes=VMEM_LIMIT
        ),
        name="layer",
    )(*inputs)


def finish_kernel(count, *refs):
    large, (small, loss), outs = refs[:count], refs[count : count + 2], refs[count + 2 : -1]
    sems = refs[-1]
    copies = []
    for index, (source, target) in enumerate(zip(large, outs)):
        part = source if source.shape == target.shape else source.at[: target.shape[0]]
        copies.append(pltpu.make_async_copy(part, target, sems.at[index]))
        copies[-1].start()
    for row, target in zip([0, 1, 8, 2, 3, 16, 9, 4, 5], outs[count : count + 9]):
        size = target.shape[0]
        target[...] = small[row : row + 1, 0:size].reshape(size)
    outs[-1][...] = loss[...].reshape(1)
    for one in copies:
        one.wait()


def finish(results):
    vmem = pl.BlockSpec(memory_space=pltpu.VMEM)
    anywhere = pl.BlockSpec(memory_space=pl.ANY)
    depth, deep = WIDTH // CHIPS, WIDE // CHIPS
    count = len(results) - 2
    shapes = [(one.shape, one.dtype) for one in results[:count]]
    shapes[6] = ((depth, WIDE), FULL)
    shapes += [((depth,), FULL)] * 5 + [((deep,), FULL)] + [((depth,), FULL)] * 3
    shapes.append(((1,), FULL))
    return pl.pallas_call(
        partial(finish_kernel, count),
        out_shape=tuple(jax.ShapeDtypeStruct(*one) for one in shapes),
        in_specs=[vmem] * (count + 2),
        out_specs=(anywhere,) * count + (vmem,) * 10,
        scratch_shapes=[pltpu.SemaphoreType.DMA((count,))],
        name="finish",
    )(*results)


def block_body(
    table,
    token_ids,
    sent_lengths,
    pair_slot,
    pair_lang,
    *parameters,
):
    results = finish(layer((table, token_ids, sent_lengths, pair_slot, pair_lang) + parameters))
    layer_out, table_grad, g_wq, g_wk, g_wv, g_wo, g_wup, g_wdown = results[:8]
    g_bq, g_bv, g_bo, g_g1, g_s1, g_bup, g_bdown, g_g2, g_s2, loss = results[8:]
    return (
        layer_out.reshape(token_ids.shape + (WIDTH,)),
        loss.reshape(()),
        table_grad,
        g_wq,
        g_bq,
        g_wk,
        g_wv,
        g_bv,
        g_wo,
        g_bo,
        g_g1,
        g_s1,
        g_wup,
        g_bup,
        g_wdown,
        g_bdown,
        g_g2,
        g_s2,
    )


def solution(mesh):
    in_specs = (
        P(("dp", "fsdp"), None),
        P(("dp", "fsdp"), None),
        P(("dp", "fsdp")),
        P(),
        P(),
        P("fsdp", None),
        P("fsdp"),
        P("fsdp", None),
        P("fsdp", None),
        P("fsdp"),
        P("fsdp", None),
        P("fsdp"),
        P("fsdp"),
        P("fsdp"),
        P("fsdp", None),
        P("fsdp"),
        P("fsdp", None),
        P("fsdp"),
        P("fsdp"),
        P("fsdp"),
    )
    out_specs = (
        P(("dp", "fsdp"), None, None),
        P(),
        P(("dp", "fsdp"), None),
        P("fsdp", None),
        P("fsdp"),
        P("fsdp", None),
        P("fsdp", None),
        P("fsdp"),
        P("fsdp", None),
        P("fsdp"),
        P("fsdp"),
        P("fsdp"),
        P("fsdp", None),
        P("fsdp"),
        P("fsdp", None),
        P("fsdp"),
        P("fsdp"),
        P("fsdp"),
    )
    sizes = dict(mesh.shape)
    body = general_body
    if sizes["dp"] == CORES and sizes["fsdp"] == CHIPS:
        body = block_body
    return jax.shard_map(body, mesh=mesh, in_specs=in_specs, out_specs=out_specs, check_vma=False)
```

```python
from functools import partial
from types import SimpleNamespace

import jax
import jax.numpy as jnp
from jax import lax
from jax.experimental import pallas as pl
from jax.experimental.pallas import tpu as pltpu
from jax.sharding import PartitionSpec as P

HEADS = 12
HEAD = 64
LANGS = 109


EPSILON = 1e-06
SCORE_SCALE = 50.0
MARGIN_WIDTH = 0.3
MASK_FLOOR = -1000000000.0


def contract(left_side, right_side, left_dim, right_dim):
    return lax.dot_general(
        left_side,
        right_side,
        (((left_dim,), (right_dim,)), ((), ())),
        preferred_element_type=jnp.float32,
    )


def norm_rows(inputs, ln_gain, ln_shift):
    row_mean = jnp.mean(inputs, axis=-1, keepdims=True)
    centered = inputs - row_mean
    variance = jnp.mean(centered * centered, axis=-1, keepdims=True)
    inverse = lax.rsqrt(variance + EPSILON)
    normed = centered * inverse
    return (normed * ln_gain + ln_shift, normed, inverse)


def norm_back(grad_output, normed, inverse, ln_gain):
    grad_normed = grad_output * ln_gain
    first_term = jnp.mean(grad_normed, axis=-1, keepdims=True)
    second_term = jnp.mean(grad_normed * normed, axis=-1, keepdims=True)
    grad_input = inverse * (grad_normed - first_term - normed * second_term)
    return (grad_input, jnp.sum(grad_output * normed, axis=0), jnp.sum(grad_output, axis=0))


def general_body(
    table,
    token_ids,
    sent_lengths,
    pair_slot,
    pair_lang,
    w_query,
    b_query,
    w_key,
    w_value,
    b_value,
    w_out,
    b_out,
    ln1_gain,
    ln1_bias,
    w_up,
    b_up,
    w_down,
    b_down,
    ln2_gain,
    ln2_bias,
):
    sentences, length = token_ids.shape
    tokens = sentences * length
    vocab_rows, model_width = table.shape
    owners = lax.axis_size(("dp", "fsdp"))
    dp_count = lax.axis_size("dp")
    fsdp_count = lax.axis_size("fsdp")
    capacity = max(2, 2 * tokens // owners)
    device = lax.axis_index(("dp", "fsdp"))
    score_factor = HEAD ** (-0.5)
    flat_ids = token_ids.reshape(tokens)
    owner_of = flat_ids // vocab_rows
    member = (owner_of[:, None] == jnp.arange(owners, dtype=jnp.int32)[None, :]).astype(jnp.int32)
    owner_rank = jnp.sum(jnp.cumsum(member, axis=0) * member, axis=1) - 1
    slot_of = owner_of * capacity + owner_rank
    requests = jnp.full((owners * capacity,), -1, jnp.int32).at[slot_of].set(flat_ids)
    received = lax.all_to_all(
        lax.all_to_all(
            requests.reshape(dp_count, fsdp_count, capacity),
            "dp",
            split_axis=0,
            concat_axis=0,
            tiled=True,
        ),
        "fsdp",
        split_axis=1,
        concat_axis=1,
        tiled=True,
    )
    present = received >= 0
    local_rows = jnp.where(present, received - device * vocab_rows, 0)
    found_rows = jnp.where(present[..., None], table[local_rows], jnp.zeros((), table.dtype))
    replies = lax.all_to_all(
        lax.all_to_all(found_rows, "dp", split_axis=0, concat_axis=0, tiled=True),
        "fsdp",
        split_axis=1,
        concat_axis=1,
        tiled=True,
    )
    embedded = replies.reshape(owners * capacity, model_width)[slot_of]
    gathered = (
        lax.all_gather(w_query, "fsdp", axis=0, tiled=True),
        lax.all_gather(b_query, "fsdp", axis=0, tiled=True),
        lax.all_gather(w_key, "fsdp", axis=0, tiled=True),
        lax.all_gather(w_value, "fsdp", axis=0, tiled=True),
        lax.all_gather(b_value, "fsdp", axis=0, tiled=True),
        lax.all_gather(w_out, "fsdp", axis=0, tiled=True),
        lax.all_gather(b_out, "fsdp", axis=0, tiled=True),
        lax.all_gather(ln1_gain, "fsdp", axis=0, tiled=True),
        lax.all_gather(ln1_bias, "fsdp", axis=0, tiled=True),
        lax.all_gather(w_up, "fsdp", axis=0, tiled=True),
        lax.all_gather(b_up, "fsdp", axis=0, tiled=True),
        lax.all_gather(w_down, "fsdp", axis=0, tiled=True),
        lax.all_gather(b_down, "fsdp", axis=0, tiled=True),
        lax.all_gather(ln2_gain, "fsdp", axis=0, tiled=True),
        lax.all_gather(ln2_bias, "fsdp", axis=0, tiled=True),
    )
    (
        full_wq,
        full_bq,
        full_wk,
        full_wv,
        full_bv,
        full_wo,
        full_bo,
        full_g1,
        full_s1,
        full_wup,
        full_bup,
        full_wdown,
        full_bdown,
        full_g2,
        full_s2,
    ) = gathered
    valid_mask = jnp.arange(length, dtype=jnp.int32)[None, :] < sent_lengths[:, None]
    head_shape = (sentences, length, HEADS, HEAD)
    queries = (jnp.dot(embedded, full_wq, preferred_element_type=jnp.float32) + full_bq).astype(
        jnp.bfloat16
    )
    key_heads = (
        jnp.dot(embedded, full_wk, preferred_element_type=jnp.float32)
        .astype(jnp.bfloat16)
        .reshape(head_shape)
    )
    value_heads = (
        (jnp.dot(embedded, full_wv, preferred_element_type=jnp.float32) + full_bv)
        .astype(jnp.bfloat16)
        .reshape(head_shape)
    )
    query_heads = queries.reshape(head_shape)
    scores = (
        jnp.einsum("bqhd,bkhd->bhqk", query_heads, key_heads, preferred_element_type=jnp.float32)
        * score_factor
    )
    scores = jnp.where(valid_mask[:, None, None, :], scores, MASK_FLOOR)
    row_peak = jnp.max(scores, axis=-1, keepdims=True)
    shifted = jnp.exp(scores - row_peak)
    totals = jnp.sum(shifted, axis=-1, keepdims=True)
    attn_probs = (shifted / totals).astype(jnp.bfloat16)
    context = jnp.einsum(
        "bhqk,bkhd->bqhd", attn_probs, value_heads, preferred_element_type=jnp.float32
    )
    context = context.reshape(tokens, model_width).astype(jnp.bfloat16)
    attended = jnp.dot(context, full_wo, preferred_element_type=jnp.float32) + full_bo
    hidden, normed_one, inverse_one = norm_rows(
        embedded.astype(jnp.float32) + attended, full_g1, full_s1
    )
    hidden_low = hidden.astype(jnp.bfloat16)
    up_pre = jnp.dot(hidden_low, full_wup, preferred_element_type=jnp.float32) + full_bup
    activated = jax.nn.gelu(up_pre, approximate=False).astype(jnp.bfloat16)
    down_pre = jnp.dot(activated, full_wdown, preferred_element_type=jnp.float32) + full_bdown
    normed_out, normed_two, inverse_two = norm_rows(hidden + down_pre, full_g2, full_s2)
    layer_out = jnp.where(valid_mask.reshape(tokens)[:, None], normed_out, 0.0).astype(jnp.bfloat16)
    layer_out = layer_out.reshape(sentences, length, model_width)

    def first_rows(matrix):
        return matrix.reshape(sentences, length, matrix.shape[-1])[:, 0]

    summary = first_rows(normed_out)
    magnitude = jnp.sqrt(jnp.sum(summary * summary, axis=-1, keepdims=True) + EPSILON)
    unit_vector = summary / magnitude
    unit_low = unit_vector.astype(jnp.bfloat16)
    every_unit = lax.all_gather(unit_low, ("dp", "fsdp"), axis=0, tiled=True)
    every_side = pair_slot % 2
    every_pair = pair_slot // 2
    my_slots = lax.dynamic_slice_in_dim(pair_slot, device * sentences, sentences)
    my_side = my_slots % 2
    my_pair = my_slots // 2
    lang_onehot = (pair_lang[:, None] == jnp.arange(LANGS, dtype=jnp.int32)[None, :]).astype(
        jnp.float32
    )
    per_lang = jnp.sum(lang_onehot, axis=0)
    per_pair = 1.0 / (2.0 * LANGS * jnp.sum(lang_onehot * per_lang[None, :], axis=1))
    my_weight = jnp.take(per_pair, my_pair)
    opposite = my_side[:, None] != every_side[None, :]
    partner = opposite & (my_pair[:, None] == every_pair[None, :])
    raw_scores = SCORE_SCALE * contract(unit_low, every_unit, 1, 1)
    pair_scores = jnp.where(partner, raw_scores - SCORE_SCALE * MARGIN_WIDTH, raw_scores)
    pair_scores = jnp.where(opposite, pair_scores, MASK_FLOOR)
    pair_peak = jnp.max(pair_scores, axis=1, keepdims=True)
    pair_exp = jnp.exp(pair_scores - pair_peak)
    pair_total = jnp.sum(pair_exp, axis=1, keepdims=True)
    log_total = pair_peak[:, 0] + jnp.log(pair_total[:, 0])
    picked = jnp.sum(jnp.where(partner, pair_scores, 0.0), axis=1)
    loss_value = lax.psum(jnp.sum(my_weight * (log_total - picked)), ("dp", "fsdp"))
    coefficients = (
        my_weight[:, None] * (pair_exp / pair_total - partner.astype(jnp.float32))
    ).astype(jnp.bfloat16)
    unit_grad = SCORE_SCALE * contract(coefficients, every_unit, 1, 0)
    column_terms = SCORE_SCALE * contract(coefficients, unit_low, 0, 0)
    unit_grad = unit_grad + lax.psum_scatter(
        column_terms, ("dp", "fsdp"), scatter_dimension=0, tiled=True
    )
    along = jnp.sum(unit_vector * unit_grad, axis=-1, keepdims=True)
    summary_grad = (unit_grad - unit_vector * along) / magnitude
    again_weights = (
        lax.all_gather(w_query, "fsdp", axis=0, tiled=True),
        lax.all_gather(w_key, "fsdp", axis=0, tiled=True),
        lax.all_gather(w_value, "fsdp", axis=0, tiled=True),
        lax.all_gather(w_out, "fsdp", axis=0, tiled=True),
        lax.all_gather(ln1_gain, "fsdp", axis=0, tiled=True),
        lax.all_gather(w_up, "fsdp", axis=0, tiled=True),
        lax.all_gather(w_down, "fsdp", axis=0, tiled=True),
        lax.all_gather(ln2_gain, "fsdp", axis=0, tiled=True),
    )
    again_wq, again_wk, again_wv, again_wo, again_g1, again_wup, again_wdown, again_g2 = (
        again_weights
    )
    residual_grad, grad_g2, grad_s2 = norm_back(
        summary_grad, first_rows(normed_two), first_rows(inverse_two), again_g2
    )
    down_grad = residual_grad.astype(jnp.bfloat16)
    activated_cls = first_rows(activated)
    act_grad = contract(down_grad, again_wdown, 1, 1)
    gelu_value, gelu_pull = jax.vjp(partial(jax.nn.gelu, approximate=False), first_rows(up_pre))
    up_grad = gelu_pull(act_grad)[0].astype(jnp.bfloat16)
    hidden_cls = first_rows(hidden_low)
    hidden_grad = contract(up_grad, again_wup, 1, 1) + residual_grad
    first_grad, grad_g1, grad_s1 = norm_back(
        hidden_grad, first_rows(normed_one), first_rows(inverse_one), again_g1
    )
    attend_grad = first_grad.astype(jnp.bfloat16)
    context_cls = first_rows(context)
    context_grad = (
        contract(attend_grad, again_wo, 1, 1).astype(jnp.bfloat16).reshape(sentences, HEADS, HEAD)
    )
    query_cls = query_heads[:, 0]
    cls_scores = (
        jnp.einsum("bhd,bkhd->bhk", query_cls, key_heads, preferred_element_type=jnp.float32)
        * score_factor
    )
    cls_scores = jnp.where(valid_mask[:, None, :], cls_scores, MASK_FLOOR)
    cls_probs = jnp.exp(cls_scores - row_peak[:, :, 0]) / totals[:, :, 0]
    prob_grad = jnp.einsum(
        "bhd,bkhd->bhk", context_grad, value_heads, preferred_element_type=jnp.float32
    )
    score_grad = (
        cls_probs * (prob_grad - jnp.sum(cls_probs * prob_grad, axis=-1, keepdims=True))
    ).astype(jnp.bfloat16)
    query_grad = (
        (
            jnp.einsum("bhk,bkhd->bhd", score_grad, key_heads, preferred_element_type=jnp.float32)
            * score_factor
        )
        .astype(jnp.bfloat16)
        .reshape(sentences, model_width)
    )
    key_grad = (
        (
            jnp.einsum("bhk,bhd->bkhd", score_grad, query_cls, preferred_element_type=jnp.float32)
            * score_factor
        )
        .astype(jnp.bfloat16)
        .reshape(tokens, model_width)
    )
    value_grad = (
        jnp.einsum(
            "bhk,bhd->bkhd",
            cls_probs.astype(jnp.bfloat16),
            context_grad,
            preferred_element_type=jnp.float32,
        )
        .astype(jnp.bfloat16)
        .reshape(tokens, model_width)
    )
    embedded_cls = first_rows(embedded)
    grad_wkey = contract(embedded, key_grad, 0, 0)
    grad_wvalue = contract(embedded, value_grad, 0, 0)
    grad_bvalue = jnp.sum(value_grad, axis=0, dtype=jnp.float32)
    row_grads = contract(key_grad, again_wk, 1, 1) + contract(value_grad, again_wv, 1, 1)
    summary_extra = contract(query_grad, again_wq, 1, 1) + first_grad
    row_grads = (
        row_grads.reshape(sentences, length, model_width)
        .at[:, 0]
        .add(summary_extra)
        .reshape(tokens, model_width)
    )
    outgoing = jnp.zeros((owners * capacity, model_width), jnp.float32).at[slot_of].set(row_grads)
    incoming = lax.all_to_all(
        lax.all_to_all(
            outgoing.reshape(dp_count, fsdp_count, capacity, model_width).astype(jnp.bfloat16),
            "dp",
            split_axis=0,
            concat_axis=0,
            tiled=True,
        ),
        "fsdp",
        split_axis=1,
        concat_axis=1,
        tiled=True,
    ).astype(jnp.float32)
    incoming = jnp.where(
        present.reshape(owners * capacity)[:, None],
        incoming.reshape(owners * capacity, model_width),
        0.0,
    )
    table_grad = (
        jnp.zeros((vocab_rows, model_width), jnp.float32)
        .at[local_rows.reshape(owners * capacity)]
        .add(incoming)
    )
    grad_wquery = contract(embedded_cls, query_grad, 0, 0)
    grad_bquery = jnp.sum(query_grad, axis=0, dtype=jnp.float32)
    grad_wout = contract(context_cls, attend_grad, 0, 0)
    grad_bout = jnp.sum(attend_grad, axis=0, dtype=jnp.float32)
    grad_wup = contract(hidden_cls, up_grad, 0, 0)
    grad_bup = jnp.sum(up_grad, axis=0, dtype=jnp.float32)
    grad_wdown = contract(activated_cls, down_grad, 0, 0)
    grad_bdown = jnp.sum(down_grad, axis=0, dtype=jnp.float32)
    owned_grads = (
        lax.psum_scatter(
            grad_wquery.astype(jnp.bfloat16), "fsdp", scatter_dimension=0, tiled=True
        ).astype(jnp.float32),
        lax.psum_scatter(
            grad_bquery.astype(jnp.bfloat16), "fsdp", scatter_dimension=0, tiled=True
        ).astype(jnp.float32),
        lax.psum_scatter(
            grad_wkey.astype(jnp.bfloat16), "fsdp", scatter_dimension=0, tiled=True
        ).astype(jnp.float32),
        lax.psum_scatter(
            grad_wvalue.astype(jnp.bfloat16), "fsdp", scatter_dimension=0, tiled=True
        ).astype(jnp.float32),
        lax.psum_scatter(
            grad_bvalue.astype(jnp.bfloat16), "fsdp", scatter_dimension=0, tiled=True
        ).astype(jnp.float32),
        lax.psum_scatter(
            grad_wout.astype(jnp.bfloat16), "fsdp", scatter_dimension=0, tiled=True
        ).astype(jnp.float32),
        lax.psum_scatter(
            grad_bout.astype(jnp.bfloat16), "fsdp", scatter_dimension=0, tiled=True
        ).astype(jnp.float32),
        lax.psum_scatter(
            grad_g1.astype(jnp.bfloat16), "fsdp", scatter_dimension=0, tiled=True
        ).astype(jnp.float32),
        lax.psum_scatter(
            grad_s1.astype(jnp.bfloat16), "fsdp", scatter_dimension=0, tiled=True
        ).astype(jnp.float32),
        lax.psum_scatter(
            grad_wup.astype(jnp.bfloat16), "fsdp", scatter_dimension=0, tiled=True
        ).astype(jnp.float32),
        lax.psum_scatter(
            grad_bup.astype(jnp.bfloat16), "fsdp", scatter_dimension=0, tiled=True
        ).astype(jnp.float32),
        lax.psum_scatter(
            grad_wdown.astype(jnp.bfloat16), "fsdp", scatter_dimension=0, tiled=True
        ).astype(jnp.float32),
        lax.psum_scatter(
            grad_bdown.astype(jnp.bfloat16), "fsdp", scatter_dimension=0, tiled=True
        ).astype(jnp.float32),
        lax.psum_scatter(
            grad_g2.astype(jnp.bfloat16), "fsdp", scatter_dimension=0, tiled=True
        ).astype(jnp.float32),
        lax.psum_scatter(
            grad_s2.astype(jnp.bfloat16), "fsdp", scatter_dimension=0, tiled=True
        ).astype(jnp.float32),
    )
    summed = (
        lax.psum(owned_grads[0].astype(jnp.bfloat16), "dp").astype(jnp.float32),
        lax.psum(owned_grads[1].astype(jnp.bfloat16), "dp").astype(jnp.float32),
        lax.psum(owned_grads[2].astype(jnp.bfloat16), "dp").astype(jnp.float32),
        lax.psum(owned_grads[3].astype(jnp.bfloat16), "dp").astype(jnp.float32),
        lax.psum(owned_grads[4].astype(jnp.bfloat16), "dp").astype(jnp.float32),
        lax.psum(owned_grads[5].astype(jnp.bfloat16), "dp").astype(jnp.float32),
        lax.psum(owned_grads[6].astype(jnp.bfloat16), "dp").astype(jnp.float32),
        lax.psum(owned_grads[7].astype(jnp.bfloat16), "dp").astype(jnp.float32),
        lax.psum(owned_grads[8].astype(jnp.bfloat16), "dp").astype(jnp.float32),
        lax.psum(owned_grads[9].astype(jnp.bfloat16), "dp").astype(jnp.float32),
        lax.psum(owned_grads[10].astype(jnp.bfloat16), "dp").astype(jnp.float32),
        lax.psum(owned_grads[11].astype(jnp.bfloat16), "dp").astype(jnp.float32),
        lax.psum(owned_grads[12].astype(jnp.bfloat16), "dp").astype(jnp.float32),
        lax.psum(owned_grads[13].astype(jnp.bfloat16), "dp").astype(jnp.float32),
        lax.psum(owned_grads[14].astype(jnp.bfloat16), "dp").astype(jnp.float32),
    )
    return (
        layer_out,
        loss_value,
        table_grad,
        summed[0],
        summed[1],
        summed[2],
        summed[3],
        summed[4],
        summed[5],
        summed[6],
        summed[7],
        summed[8],
        summed[9],
        summed[10],
        summed[11],
        summed[12],
        summed[13],
        summed[14],
    )


CORES = 2
PLANES = 4
LINES = 4
CHIPS = PLANES * LINES
DEVICES = CORES * CHIPS
CAPACITY = 48
GROUPS = 3
PAD = 16
TOKENS = 768
WIDTH = 768
WIDE = 3072
VOCAB_ROWS = 1024
PAIR_ROWS = HEADS * PAD
SLOT_ROWS = DEVICES * PAD
LONG = 64
BLOCK = 256
MESH = pl.DeviceIdType.MESH
LOW = jnp.bfloat16
FULL = jnp.float32
VMEM_LIMIT = 62 * 1024 * 1024

INPUTS = ["table", "token_ids", "lens", "slots", "langs"]
INPUTS += ["wq", "bq", "wk", "wv", "bv", "wo", "bo", "g1", "s1", "wup", "bup", "wdown", "bdown"]
INPUTS += ["g2", "s2"]
OUTPUTS = ["layer_out", "table_grad", "g_wq", "g_wk", "g_wv", "g_wo", "g_wup", "g_wdown"]
OUTPUTS += ["g_small", "loss"]


def place():
    core = lax.axis_index("dp")
    chip = lax.axis_index("fsdp")
    along_x = chip + 1 - 2 * (chip % 2)
    along_y = chip + 2 - 4 * ((chip // 2) % 2)
    first = along_x + core * (along_y - along_x)
    second = along_y + core * (along_x - along_y)
    return core, chip, first, second


def greet():
    core, chip, _, _ = place()
    me = core * CHIPS + chip
    barrier = pltpu.get_barrier_semaphore()

    def signal(step):
        other = lax.rem(me + step, DEVICES)
        pl.semaphore_signal(
            barrier,
            inc=1,
            device_id=(lax.div(other, CHIPS), lax.rem(other, CHIPS)),
            device_id_type=MESH,
        )

    every(1, DEVICES, signal)


def enter():
    pl.semaphore_wait(pltpu.get_barrier_semaphore(), DEVICES - 1)


def remote(source, target, send_sem, recv_sem, core, chip):
    return pltpu.make_async_remote_copy(
        src_ref=source,
        dst_ref=target,
        send_sem=send_sem,
        recv_sem=recv_sem,
        device_id=(core, chip),
        device_id_type=MESH,
    )


def every(start, stop, act):
    def step(index, carry):
        act(index)
        return carry

    lax.fori_loop(start, stop, step, 0)


def weight_steps(piece, many, send, recv):
    core, chip, first, second = place()
    plane, line = chip // LINES, chip % LINES
    line_first, line_second = first % LINES, second % LINES
    line_far = line_first + line_second - line
    is_low, is_high = plane > 0, plane < PLANES - 1

    def copy(send_index, recv_index, at, to_core, to_chip, carried=core):
        part = piece(at, carried)
        return remote(part, part, send.at[send_index], recv.at[recv_index], to_core, to_chip)

    def up(at_plane):
        return copy(at_plane, at_plane, at_plane * LINES + line, core, chip + LINES)

    def down(at_plane, index):
        return copy(index, at_plane, at_plane * LINES + line, core, chip - LINES)

    def side(at_plane, base, at_line, target):
        return copy(5, base + at_plane, at_plane * LINES + at_line, core, target)

    def across(at_plane, at_line):
        return copy(6, 17, at_plane * LINES + at_line, 1 - core, chip)

    def all_of(count, send_index, recv_index):
        part = many(count)
        return remote(part, part, send.at[send_index], recv.at[recv_index], 1 - core, chip)

    def begin():
        pl.when(is_high)(lambda: up(plane).start())
        pl.when(is_low)(lambda: down(plane, PLANES).start())
        side(plane, 5, line, first).start()
        side(plane, 9, line, second).start()

    def at_distance(distance, act):
        if distance == 0:
            act(plane, None)
            return
        pl.when(plane >= distance)(lambda: act(plane - distance, True))
        pl.when(plane + distance < PLANES)(lambda: act(plane + distance, False))

    def chain(distance):
        def act(at_plane, from_low):
            if from_low:
                up(at_plane).wait_recv()
                pl.when(is_high)(lambda: up(at_plane).start())
            else:
                down(at_plane, at_plane).wait_recv()
                pl.when(is_low)(lambda: down(at_plane, at_plane).start())
            side(at_plane, 5, line, first).start()
            side(at_plane, 9, line, second).start()
            across(at_plane, line).start()

        return partial(at_distance, distance, act)

    def near(distance):
        def act(at_plane, from_low):
            side(at_plane, 5, line_first, first).wait_recv()
            side(at_plane, 13, line_first, second).start()
            across(at_plane, line_first).start()

        return partial(at_distance, distance, act)

    def far(distance):
        def act(at_plane, from_low):
            side(at_plane, 9, line_second, second).wait_recv()
            across(at_plane, line_second).start()
            side(at_plane, 13, line_far, second).wait_recv()
            across(at_plane, line_far).start()

        return partial(at_distance, distance, act)

    def finish():
        all_of(15, 6, 17).wait_recv()

    def drain():
        def sent(index):
            copy(index, index, chip, 1 - core, chip).wait_send()

        for at_plane in range(PLANES):
            pl.when((plane >= at_plane) & is_high)(partial(sent, at_plane))
            pl.when((plane < at_plane) & is_low)(partial(sent, at_plane))
        pl.when(is_low)(partial(sent, PLANES))
        all_of(12, 5, 17).wait_send()
        all_of(15, 6, 17).wait_send()

    moves = [chain(1), near(0), chain(2), near(1), chain(3), far(0)]
    moves += [near(2), far(1), near(3), far(2), far(3)]
    return begin, moves, finish, drain


def gather_steps(buffer, send, recv):
    core, chip, first, second = place()
    plane, line = chip // LINES, chip % LINES
    line_first, line_second = first % LINES, second % LINES
    line_far = line_first + line_second - line
    half = buffer.shape[-1] // 2
    columns = pl.ds(pl.multiple_of(core * half, 128), half)
    others = pl.ds(pl.multiple_of((1 - core) * half, 128), half)

    def copy(index, part, to_core, to_chip):
        return remote(part, part, send.at[index], recv.at[index], to_core, to_chip)

    def own(at):
        return buffer.at[at, plane, line]

    def chip_part(at_plane, at_line, which):
        return buffer.at[:, at_plane, at_line, :, which]

    def line_part(at_line, which):
        return buffer.at[:, :, at_line, :, which]

    def start():
        copy(0, own(core), 1 - core, chip).start()

    def planes():
        copy(0, own(1 - core), 1 - core, chip).wait_recv()
        for step in range(1, PLANES):
            part = chip_part(plane, line, columns)
            copy(step, part, core, (chip + LINES * step) % CHIPS).start()

    def sides():
        for step in range(1, PLANES):
            part = chip_part((plane + PLANES - step) % PLANES, line, columns)
            copy(step, part, core, chip).wait_recv()
        copy(4, line_part(line, columns), core, first).start()
        copy(5, line_part(line, columns), core, second).start()
        for step in range(1, PLANES):
            part = chip_part((plane + PLANES - step) % PLANES, line, columns)
            copy(6 + step, part, 1 - core, chip).start()

    def corner():
        copy(4, line_part(line_first, columns), core, first).wait_recv()
        copy(6, line_part(line_first, columns), core, second).start()
        copy(10, line_part(line_first, columns), 1 - core, chip).start()
        copy(5, line_part(line_second, columns), core, second).wait_recv()
        copy(11, line_part(line_second, columns), 1 - core, chip).start()

    def last():
        copy(6, line_part(line_far, columns), core, second).wait_recv()
        copy(12, line_part(line_far, columns), 1 - core, chip).start()

    def finish():
        for step in range(1, PLANES):
            part = chip_part((plane + PLANES - step) % PLANES, line, others)
            copy(6 + step, part, 1 - core, chip).wait_recv()
        copy(10, line_part(line_second, others), 1 - core, chip).wait_recv()
        copy(11, line_part(line_first, others), 1 - core, chip).wait_recv()
        copy(12, line_part(line_far, others), 1 - core, chip).wait_recv()

    def drain():
        copy(0, own(core), 1 - core, chip).wait_send()
        for index in [1, 2, 3, 7, 8, 9]:
            copy(index, chip_part(plane, line, columns), 1 - core, chip).wait_send()
        for index in [4, 5, 6, 10, 11, 12]:
            copy(index, line_part(line, columns), 1 - core, chip).wait_send()

    return [start, planes, sides, corner, last, finish], drain


def iota(shape, axis):
    return lax.broadcasted_iota(jnp.int32, shape, axis)


def over(numbers, power):
    return lax.shift_right_arithmetic(numbers, jnp.full_like(numbers, power.bit_length() - 1))


def within(numbers, power):
    return numbers & (power - 1)


def as_column(row):
    parts = []
    for start in range(0, row.shape[1], 128):
        tile = jnp.broadcast_to(row[:, start : start + 128], (128, 128))
        parts.append(jnp.transpose(tile)[:, 0:1])
    return jnp.concatenate(parts, axis=0)


def as_row(column):
    parts = []
    for start in range(0, column.shape[0], 128):
        tile = jnp.broadcast_to(column[start : start + 128, :], (128, 128))
        parts.append(jnp.transpose(tile)[0:1, :])
    return jnp.concatenate(parts, axis=1)


def dot(left_side, right_side):
    return contract(left_side, right_side, 1, 0)


def dot_turned(left_side, right_side):
    return contract(left_side, right_side, 1, 1)


def norm_parts(inputs):
    centered = inputs - jnp.mean(inputs, axis=-1, keepdims=True)
    inverse = lax.rsqrt(jnp.mean(centered * centered, axis=-1, keepdims=True) + EPSILON)
    return centered * inverse, inverse


def norm_back_parts(grad_output, normed, inverse, ln_gain):
    grad_normed = grad_output * ln_gain
    first_term = jnp.mean(grad_normed, axis=-1, keepdims=True)
    second_term = jnp.mean(grad_normed * normed, axis=-1, keepdims=True)
    return (
        inverse * (grad_normed - first_term - normed * second_term),
        jnp.sum(grad_output * normed, axis=0, keepdims=True),
        jnp.sum(grad_output, axis=0, keepdims=True),
    )


def erf_parts(inputs):
    decay = jnp.exp(-0.5 * inputs * inputs)
    share = 1.0 / (1.0 + jnp.abs(inputs) * (0.3275911 * 0.5**0.5))
    terms = [1.061405429, -1.453152027, 1.421413741, -0.284496736, 0.254829592]
    series = 0.5 * terms[0]
    for term in terms[1:]:
        series = series * share + 0.5 * term
    tail = series * share * decay
    return jnp.where(inputs >= 0.0, 1.0 - tail, tail), decay


def gelu_parts(inputs):
    below, decay = erf_parts(inputs)
    return inputs * below, below + inputs * decay * ((2.0 * 3.141592653589793) ** -0.5)


def gelu(inputs):
    return inputs * erf_parts(inputs)[0]


def layer_kernel(names, *refs):
    r = SimpleNamespace(**dict(zip(names, refs, strict=True)))
    core, chip, _, _ = place()
    me = core * CHIPS + chip
    here = (core, chip // LINES, chip % LINES)
    scale = HEAD ** (-0.5)
    depth, deep = WIDTH // CHIPS, WIDE // CHIPS
    sentences = TOKENS // LONG

    for j in range(TOKENS // 128):
        r.ids[j : j + 1, :] = jnp.concatenate(
            [r.token_ids[2 * j : 2 * j + 1, :], r.token_ids[2 * j + 1 : 2 * j + 2, :]], axis=1
        )
    r.ids[TOKENS // 128 : 8, :] = jnp.zeros((8 - TOKENS // 128, 128), jnp.int32)
    greet()
    ahead = (iota((TOKENS, TOKENS), 0) < iota((TOKENS, TOKENS), 1)).astype(LOW)
    r.embedded[...] = ahead
    mine = pl.ds(pl.multiple_of(chip * depth, 16), depth)
    for index, shard in enumerate([r.wq, r.wk, r.wv, r.wo]):
        r.wa[mine, index * WIDTH : (index + 1) * WIDTH] = shard[...]
    r.wb[mine, :] = r.wup[...]
    r.wc[pl.ds(pl.multiple_of(chip * deep, 16), deep), :] = r.wdown[...]
    r.every_ids[me] = r.ids[...]
    enter()

    def peer(step):
        other = lax.rem(me + step, DEVICES)
        return other, lax.div(other, CHIPS), lax.rem(other, CHIPS)

    def ids_copy(step):
        other, to_core, to_chip = peer(step)
        return remote(r.ids, r.every_ids.at[me], r.one_send.at[0], r.one_recv.at[0], to_core, to_chip)

    def all_but_one(ref, index):
        part = ref.at[0 : DEVICES - 1]
        return remote(part, part, r.one_send.at[index], r.one_recv.at[index], 1 - core, chip)

    every(1, DEVICES, lambda step: ids_copy(step).start())

    def block(ref, rows, columns):
        def piece(at, carried):
            return ref.at[
                pl.ds(pl.multiple_of(at * rows, 16), rows),
                pl.ds(pl.multiple_of(carried * columns, 128), columns),
            ]

        def many(count):
            return ref.at[0 : count * rows, 0:columns]

        return piece, many

    begin_a, moves_a, finish_a, drain_a = weight_steps(
        *block(r.wa, depth, 2 * WIDTH), r.weight_send.at[0], r.weight_recv.at[0]
    )
    begin_b, moves_b, finish_b, drain_b = weight_steps(
        *block(r.wb, depth, WIDE // 2), r.weight_send.at[1], r.weight_recv.at[1]
    )
    begin_c, moves_c, finish_c, drain_c = weight_steps(
        *block(r.wc, deep, WIDTH // 2), r.weight_send.at[2], r.weight_recv.at[2]
    )
    begin_a()
    begin_b()

    def move(*steps):
        for moves, first_step in steps:
            moves[first_step]()
            moves[first_step + 1]()

    all_but_one(r.every_ids, 0).wait_recv()
    all_ids = jnp.concatenate([r.every_ids[:, j, :] for j in range(TOKENS // 128)], axis=1)
    all_owner = over(all_ids, VOCAB_ROWS)
    asked = all_owner == me
    ranks = dot(asked.astype(LOW), r.embedded[...])
    r.rank[...] = jnp.where(asked, ranks, -1.0)
    local_row = (all_ids - all_owner * VOCAB_ROWS + 1).astype(FULL)
    r.code[...] = local_row + (over(iota((DEVICES, TOKENS), 1), LONG) * 2048).astype(FULL)

    quarter_size = DEVICES // 4

    def rows_copy(other, quarter):
        return remote(
            r.rows.at[:, pl.ds(pl.multiple_of(other * PAD, 16), PAD), :],
            r.replies.at[:, pl.ds(pl.multiple_of(me * PAD, 16), PAD), :],
            r.rows_send.at[quarter],
            r.rows_recv.at[quarter],
            lax.div(other, CHIPS),
            lax.rem(other, CHIPS),
        )

    def rows_of(quarter):
        count = quarter_size - 1 if quarter == 3 else quarter_size
        part = r.replies.at[:, 0 : count * PAD, :]
        return remote(
            part, part, r.rows_send.at[quarter], r.rows_recv.at[quarter], 1 - core, chip
        )

    def pick(source):
        rank = r.rank[pl.ds(source, 1), :]
        code = r.code[pl.ds(source, 1), :]
        here_at = iota((CAPACITY, TOKENS), 0).astype(FULL) == rank
        found = jnp.sum(jnp.where(here_at, code, 0.0), axis=1, keepdims=True)
        sent = jnp.floor(found * (1.0 / 2048))
        row = found - sent * 2048.0 - 1.0
        chosen = (iota((CAPACITY, VOCAB_ROWS), 1).astype(FULL) == row).astype(LOW)
        at = pl.ds(pl.multiple_of(source * PAD, 16), PAD)
        source_sent = sent + (source * PAD).astype(FULL)
        for group in range(GROUPS):
            part = slice(group * PAD, (group + 1) * PAD)
            r.chosen[group, at, :] = chosen[part]
            r.found[group, at, 0:1] = row[part]
            r.found[group, at, 1:2] = source_sent[part]

    def quarter_rows(quarter):
        now = lax.rem(lax.div(me, quarter_size) + 1 + quarter, 4)

        def pick_two(index):
            pick(now * quarter_size + 2 * index)
            pick(now * quarter_size + 2 * index + 1)

        every(0, quarter_size // 2, pick_two)
        span = pl.ds(pl.multiple_of(now * quarter_size * PAD, 128), quarter_size * PAD)
        for start in range(0, WIDTH, BLOCK):
            lanes = slice(start, start + BLOCK)
            picked = r.chosen[:, span, :].reshape(GROUPS * quarter_size * PAD, VOCAB_ROWS)
            found_rows = dot(picked, r.table[:, lanes]).astype(LOW)
            r.rows[:, span, lanes] = found_rows.reshape(GROUPS, quarter_size * PAD, BLOCK)

        def send(index):
            other = now * quarter_size + lax.rem(lax.rem(me, quarter_size) + index, quarter_size)
            rows_copy(other, quarter).start()

        every(lax.div(quarter, 3), quarter_size, send)
        pl.when(quarter == 0)(partial(move, (moves_a, 0)))
        pl.when(quarter == 1)(partial(move, (moves_b, 0)))
        pl.when(quarter == 2)(partial(move, (moves_a, 2)))
        pl.when(quarter == 3)(partial(move, (moves_b, 2)))

    every(0, 4, quarter_rows)
    begin_c()
    own_at = pl.ds(pl.multiple_of(me * PAD, 16), PAD)
    r.replies[:, own_at, :] = r.rows[:, own_at, :]

    move((moves_a, 4))

    small_here = pl.ds(pl.multiple_of(chip * 128, 128), 128)
    lines = [r.bq, r.bv, r.bo, r.g1, r.s1, r.bdown, r.g2, r.s2]
    lines = [line[...].reshape(1, depth).astype(FULL) for line in lines]
    up_line = r.bup[...].reshape(1, deep).astype(FULL)
    lines += [up_line[:, part * depth : (part + 1) * depth] for part in range(deep // depth)]
    lines.append(jnp.zeros((PAD - len(lines), depth), FULL))
    own_small = jnp.concatenate(lines, axis=0)
    own_small = jnp.concatenate([own_small, jnp.zeros((PAD, 128 - depth), FULL)], axis=1)
    r.smalls[:, small_here] = own_small.astype(LOW)

    def small_copy(step):
        part = r.smalls.at[:, small_here]
        to_chip = lax.rem(chip + step, CHIPS)
        return remote(part, part, r.small_send.at[0], r.small_recv.at[0], core, to_chip)

    def all_smalls():
        part = r.smalls.at[:, 0 : (CHIPS - 1) * 128]
        return remote(part, part, r.small_send.at[0], r.small_recv.at[0], 1 - core, chip)

    every(1, CHIPS, lambda step: small_copy(step).start())
    move((moves_b, 4))

    own_row = jnp.concatenate([r.ids[j : j + 1, :] for j in range(TOKENS // 128)], axis=1)
    owner_row = over(own_row, VOCAB_ROWS).astype(FULL)
    owner_col = as_column(owner_row)
    earlier = (owner_row == owner_col) & (iota((TOKENS, TOKENS), 1) < iota((TOKENS, TOKENS), 0))
    own_rank = jnp.sum(earlier.astype(FULL), axis=1, keepdims=True)
    own_group = jnp.floor(own_rank * (1.0 / PAD))
    own_slot = own_group * SLOT_ROWS + owner_col * PAD + (own_rank - own_group * PAD)
    r.slot_col[...] = own_slot
    r.slot_line[0:1, :] = as_row(own_slot)
    move((moves_a, 6), (moves_c, 0))

    at_sent = over(iota((1, TOKENS), 1), LONG)
    lens = jnp.concatenate(
        [r.lens[...].reshape(1, sentences).astype(FULL), jnp.zeros((1, PAD - sentences), FULL)],
        axis=1,
    )
    spread_lens = dot(
        jnp.broadcast_to(lens, (8, PAD)).astype(LOW),
        (iota((PAD, TOKENS), 0) == over(iota((PAD, TOKENS), 1), LONG)).astype(LOW),
    )[0:1]
    valid_row = ((iota((1, TOKENS), 1) - at_sent * LONG).astype(FULL) < spread_lens).astype(FULL)
    r.valid_line[0:1, :] = valid_row
    r.valid_col[...] = as_column(valid_row)
    half_block = BLOCK // 2
    stacked_shape = (4 * half_block, half_block)
    same = within(over(iota(stacked_shape, 0), LONG), 2) == over(iota(stacked_shape, 1), LONG)
    r.block_bias[...] = jnp.where(same, 0.0, MASK_FLOOR)
    r.valid_bias[0:1, :] = (1.0 - valid_row) * MASK_FLOOR

    slots = r.slots[...].reshape(1, DEVICES * sentences)
    gap = jnp.full((1, PAD - sentences), -2, jnp.int32)
    slot_line = jnp.concatenate(
        [
            part
            for device in range(DEVICES)
            for part in (slots[:, device * sentences : (device + 1) * sentences], gap)
        ],
        axis=1,
    )
    side_line = within(slot_line, 2) + jnp.where(slot_line < 0, 8, 0)
    pair_line = over(slot_line, 2)
    pairs = r.langs.shape[0]
    lang_line = r.langs[...].reshape(1, pairs).astype(FULL)
    lang_line = jnp.concatenate([lang_line, jnp.full((1, -pairs % 128), -1.0, FULL)], axis=1)
    lang_col = as_column(lang_line)
    same_lang = jnp.sum(jnp.where(lang_col == lang_line, 1.0, 0.0), axis=1, keepdims=True)
    per_pair = 1.0 / (2.0 * LANGS * same_lang)
    at_pair = iota((lang_line.shape[1], SLOT_ROWS), 0) == pair_line
    weight_line = jnp.sum(jnp.where(at_pair, per_pair, 0.0), axis=0, keepdims=True)
    r.pairs[0:1, :] = weight_line
    r.pairs[1:2, :] = pair_line.astype(FULL)
    r.pairs[2:3, :] = side_line.astype(FULL)
    r.pairs_col[:, 0:1] = as_column(weight_line)
    r.pairs_col[:, 1:2] = as_column(pair_line.astype(FULL))
    r.pairs_col[:, 2:3] = as_column(side_line.astype(FULL))
    move((moves_b, 6), (moves_c, 2))

    all_smalls().wait_recv()
    smalls = r.smalls[...].astype(FULL)
    r.vectors[:, 0:WIDTH] = jnp.concatenate(
        [smalls[:, at * 128 : at * 128 + depth] for at in range(CHIPS)], axis=1
    )
    r.up_bias[0:1, :] = jnp.concatenate(
        [
            smalls[8 + part : 9 + part, at * 128 : at * 128 + depth]
            for at in range(CHIPS)
            for part in range(deep // depth)
        ],
        axis=1,
    )

    def vector(index):
        return r.vectors[index : index + 1, :]

    r.qkv_bias[0:1, 0:WIDTH] = vector(0)
    r.qkv_bias[0:1, WIDTH : 2 * WIDTH] = jnp.zeros((1, WIDTH), FULL)
    r.qkv_bias[0:1, 2 * WIDTH : 3 * WIDTH] = vector(1)

    move((moves_a, 8), (moves_b, 8), (moves_c, 4))

    def first_row(source):
        code = jnp.where(r.rank[pl.ds(source, 1), :] >= 0.0, r.code[pl.ds(source, 1), :], 0.0)
        at_first = iota((PAD, TOKENS), 1) == iota((PAD, TOKENS), 0) * LONG
        found = jnp.sum(jnp.where(at_first, code, 0.0), axis=1, keepdims=True)
        row = found - jnp.floor(found * (1.0 / 2048)) * 2048.0 - 1.0
        r.found[GROUPS, pl.ds(pl.multiple_of(source * PAD, 16), PAD), 0:1] = row

    every(0, DEVICES, first_row)
    for group in range(GROUPS + 1):
        named = as_row(r.found[group, :, 0:1])
        by_row = iota((VOCAB_ROWS, SLOT_ROWS), 0).astype(FULL) == named
        r.by_row[:, group * SLOT_ROWS : (group + 1) * SLOT_ROWS] = by_row.astype(LOW)

    def order(tile):
        at = pl.ds(pl.multiple_of(tile * BLOCK, BLOCK), BLOCK)
        lanes = iota((BLOCK, GROUPS * SLOT_ROWS), 1).astype(FULL)
        r.qkv[at, 0 : GROUPS * SLOT_ROWS] = (r.slot_col[at, :] == lanes).astype(LOW)

    every(0, TOKENS // BLOCK, order)
    for group in range(GROUPS):
        slot_at = iota((SLOT_ROWS, TOKENS), 0) + group * SLOT_ROWS
        named = (slot_at.astype(FULL) == r.slot_line[0:1, :]).astype(LOW)
        r.slot_hot[group] = named
    moves_a[10]()
    moves_b[10]()
    finish_a()
    for quarter in range(4):
        rows_of(quarter).wait_recv()

    def embed(tile):
        at = pl.ds(pl.multiple_of(tile * BLOCK, BLOCK), BLOCK)
        replies = r.replies[:, :, at].reshape(GROUPS * SLOT_ROWS, BLOCK)
        r.embedded[:, at] = dot(r.qkv[:, 0 : GROUPS * SLOT_ROWS], replies).astype(LOW)

    every(0, WIDTH // BLOCK, embed)

    def project(tile):
        at = pl.ds(pl.multiple_of(tile * BLOCK, BLOCK), BLOCK)
        r.qkv[:, at] = (dot(r.embedded[...], r.wa[:, at]) + r.qkv_bias[0:1, at]).astype(LOW)

    move((moves_c, 6))
    every(0, 9, project)

    row_sent = within(iota((PAIR_ROWS, WIDTH), 0), PAD)
    row_head = over(iota((PAIR_ROWS, WIDTH), 0), PAD)
    lane_block = over(iota((PAIR_ROWS, WIDTH), 1), HEAD)
    in_head = row_head == lane_block
    seen = (row_sent == lane_block) & (r.valid_line[0:1, :] > 0.0)
    firsts = (iota((PAD, TOKENS), 1) == iota((PAD, TOKENS), 0) * LONG).astype(LOW)
    real_row = iota((PAD, 1), 0) < sentences

    def spread(rows):
        return jnp.where(in_head, jnp.concatenate([rows] * HEADS, axis=0), jnp.zeros((), LOW))

    def fold(tall):
        tall = jnp.where(in_head, tall, 0.0)
        return sum(tall[head * PAD : (head + 1) * PAD] for head in range(HEADS))

    keys, values = slice(WIDTH, 2 * WIDTH), slice(2 * WIDTH, 3 * WIDTH)
    embedded_cls = dot(firsts, r.embedded[...]).astype(LOW)
    query_cls = (dot(embedded_cls, r.wa[:, 0:WIDTH]) + vector(0)).astype(LOW)
    cls_scores = dot_turned(spread(query_cls), r.qkv[:, keys]) * scale
    cls_scores = jnp.where(seen, cls_scores, MASK_FLOOR)
    cls_peak = jnp.max(cls_scores, axis=1, keepdims=True)
    cls_exp = jnp.where(seen, jnp.exp(cls_scores - cls_peak), 0.0)
    cls_total = jnp.sum(cls_exp, axis=1, keepdims=True)
    cls_probs = cls_exp / jnp.where(cls_total > 0.0, cls_total, 1.0)
    probs_low = cls_probs.astype(LOW)
    r.probs[...] = cls_probs
    context_cls = fold(dot(probs_low, r.qkv[:, values])).astype(LOW)
    first_cls = (
        embedded_cls.astype(FULL)
        + dot(context_cls, r.wa[:, 3 * WIDTH : 4 * WIDTH])
        + vector(2)
    )
    normed_one, inverse_one = norm_parts(first_cls)
    r.normed_one[...] = normed_one
    hidden_cls = normed_one * vector(3) + vector(4)
    hidden_cls_low = hidden_cls.astype(LOW)
    early_here = r.early.at[here]
    early_here[:, 0:WIDTH] = hidden_cls_low
    early_here[:, WIDTH : 2 * WIDTH] = query_cls
    steps_u, drain_u = gather_steps(r.units, r.gather_send.at[0], r.gather_recv.at[0])
    steps_e, drain_e = gather_steps(r.early, r.gather_send.at[1], r.gather_recv.at[1])
    steps_d, drain_d = gather_steps(r.downs, r.gather_send.at[2], r.gather_recv.at[2])
    steps_a, drain_a2 = gather_steps(r.attends, r.gather_send.at[3], r.gather_recv.at[3])
    steps_q, drain_q = gather_steps(r.queries, r.gather_send.at[4], r.gather_recv.at[4])
    steps_e[0]()

    def attend(unit):
        rows = pl.ds(pl.multiple_of(unit * half_block, half_block), half_block)
        lane_head = over(iota((half_block, BLOCK), 1), HEAD)
        bias = r.block_bias[...] + r.valid_bias[0:1, rows]

        def part(which, lane):
            return r.qkv[rows, which * WIDTH + lane : which * WIDTH + lane + BLOCK]

        for lane in range(0, WIDTH, BLOCK):
            query = part(0, lane) * jnp.asarray(scale, LOW)
            key, value = part(1, lane), part(2, lane)
            stacked = jnp.concatenate(
                [jnp.where(lane_head == head, query, jnp.zeros((), LOW)) for head in range(4)],
                axis=0,
            )
            scores = dot_turned(stacked, key) + bias
            shifted = jnp.exp(scores - jnp.max(scores, axis=1, keepdims=True)).astype(LOW)
            mixed = dot(shifted, value)
            totals = dot(shifted, jnp.ones((half_block, BLOCK), LOW))
            result, total = mixed[0:half_block], totals[0:half_block]
            for head in range(1, 4):
                at = slice(head * half_block, (head + 1) * half_block)
                result = jnp.where(lane_head == head, mixed[at], result)
                total = jnp.where(lane_head == head, totals[at], total)
            r.context[rows, lane : lane + BLOCK] = (result / total).astype(LOW)

    def open_tile(tile):
        at = pl.ds(pl.multiple_of(tile * BLOCK, BLOCK), BLOCK)
        attended = dot(r.context[at, :], r.wa[:, 3 * WIDTH : 4 * WIDTH]) + vector(2)
        normed, _ = norm_parts(r.embedded[at, :].astype(FULL) + attended)
        hidden = normed * vector(3) + vector(4)
        r.context[at, :] = hidden.astype(LOW)
        r.table_full[at, :] = hidden + vector(5)

    most = SLOT_ROWS
    rest_at = pl.ds(most, TOKENS - most)

    def up_product(part):
        at = pl.ds(pl.multiple_of(part * BLOCK, BLOCK), BLOCK)
        return dot(r.context[...], r.wb[:, at]) + r.up_bias[0:1, at]

    def feed_up(part, last=False):
        active = gelu(r.tile_up[...]).astype(LOW)
        if not last:
            r.tile_up[...] = up_product(part + 1)
        lanes = pl.ds(pl.multiple_of(lax.rem(part, 4) * BLOCK, BLOCK), BLOCK)
        r.chosen[lax.div(part, 4), :, lanes] = active[:most]
        rest = pl.ds(pl.multiple_of(lax.div(part, 6) * BLOCK, BLOCK), BLOCK)
        lanes = pl.ds(pl.multiple_of(lax.rem(part, 6) * BLOCK, BLOCK), BLOCK)
        r.slopes[rest, lanes] = active[most:]

    def feed_down(part):
        lanes = pl.ds(pl.multiple_of(part * BLOCK, BLOCK), BLOCK)
        total = r.table_full[0:most, lanes]
        for group in range(GROUPS):
            rows = slice(group * VOCAB_ROWS, (group + 1) * VOCAB_ROWS)
            total = total + dot(r.chosen[group], r.wc[rows, lanes])
        r.table_full[0:most, lanes] = total

    def feed_rest(part):
        lanes = pl.ds(pl.multiple_of(part * BLOCK, BLOCK), BLOCK)
        low_part = dot(r.slopes[0:BLOCK, :], r.wc[0 : WIDE // 2, lanes])
        high_part = dot(r.slopes[BLOCK : 2 * BLOCK, :], r.wc[WIDE // 2 :, lanes])
        r.table_full[rest_at, lanes] += low_part + high_part

    def layer_copy(tile):
        at = pl.ds(pl.multiple_of(tile * BLOCK, BLOCK), BLOCK)
        return pltpu.make_async_copy(r.context.at[at], r.layer_out.at[at], r.out_sem.at[tile])

    def close_tile(tile):
        at = pl.ds(pl.multiple_of(tile * BLOCK, BLOCK), BLOCK)
        normed, _ = norm_parts(r.table_full[at, :])
        out = normed * vector(6) + vector(7)
        r.context[at, :] = (out * r.valid_col[at, :]).astype(LOW)
        layer_copy(tile).start()

    finish_b()
    r.hidden_cls[...] = hidden_cls_low

    def up_part(part):
        at = pl.ds(pl.multiple_of(part * WIDTH, BLOCK), WIDTH)
        active, slope = gelu_parts(dot(r.hidden_cls[...], r.wb[:, at]) + r.up_bias[0:1, at])
        r.active_cls[:, at] = active.astype(LOW)
        r.slope_cls[:, at] = slope

    every(0, WIDE // WIDTH, up_part)
    steps_e[1]()

    def attend_step(unit):
        attend(unit)
        pl.when(unit == 1)(partial(move, (moves_c, 8)))
        pl.when(unit == 3)(moves_c[10])
        pl.when(unit == 4)(steps_e[2])

    every(0, 6, attend_step)
    finish_c()

    def pack_tall(target, first_row, act):
        def run(part):
            window = jnp.minimum(lax.div(part * 2 * depth, 128) * 128, WIDTH - BLOCK)
            shape = (BLOCK, BLOCK)
            lane = within(iota(shape, 1), 128)
            column = over(iota(shape, 1), 128) * depth + lane + (part * 2 * depth - window)
            select = ((iota(shape, 0) == column) & (lane < depth)).astype(LOW)
            taken = dot(r.tall[:, pl.ds(pl.multiple_of(window, 128), BLOCK)], select)

            def beside(low, high):
                return [
                    low[:, one * 128 : (one + 1) * 128]
                    + pltpu.roll(high[:, one * 128 : (one + 1) * 128], depth, 1)
                    for one in range(2)
                ]

            for half in range(CORES):
                base = half * PAIR_ROWS // 2
                both = beside(taken[base : base + 48], taken[base + 48 : base + 96])
                for one in range(2):
                    at = half * CHIPS + 2 * part + one
                    target[at, first_row : first_row + 48, :] = act(
                        2 * part + one, both[one]
                    ).astype(LOW)
            if first_row:
                left = beside(taken[PAIR_ROWS : PAIR_ROWS + PAD], taken[PAIR_ROWS + PAD :])
                for half in range(CORES):
                    for one in range(2):
                        target[half * CHIPS + 2 * part + one, 0:PAD, :] = left[one].astype(LOW)

        return run

    def pack_coefs(coefs):
        shape = (2 * PAIR_ROWS, GROUPS * 128)
        row, lane = iota(shape, 0), iota(shape, 1)
        kind = jnp.where(row >= PAIR_ROWS, PAD, 0)
        head = over(row, PAD) - jnp.where(row >= PAIR_ROWS, HEADS, 0)
        folds = head + kind + over(lane, 128) * 2 * PAD == within(lane, 128)
        lanes = contract(coefs, folds.astype(LOW), 0, 0).astype(LOW)
        total = None
        for group in range(GROUPS):
            part = dot(r.slot_hot[group], lanes[:, group * 128 : (group + 1) * 128])
            total = part if total is None else total + part
        return total.astype(LOW).reshape(DEVICES, PAD, 128)


    def down_part(part):
        at = pl.ds(pl.multiple_of(part * BLOCK, BLOCK), BLOCK)
        r.wide_cls[:, at] = dot(r.active_cls[...], r.wc[:, at])

    every(0, WIDTH // BLOCK, down_part)
    down_pre = r.wide_cls[:, 0:WIDTH] + vector(5)
    normed_two, inverse_two = norm_parts(hidden_cls + down_pre)
    summary = normed_two * vector(6) + vector(7)
    magnitude = jnp.sqrt(jnp.sum(summary * summary, axis=-1, keepdims=True) + EPSILON)
    unit = jnp.where(real_row, summary / magnitude, 0.0)
    r.units[here] = unit.astype(LOW)

    steps_u[0]()
    r.tall[0:PAIR_ROWS, :] = dot(probs_low, r.embedded[...]).astype(LOW)
    r.tall[PAIR_ROWS : PAIR_ROWS + PAD, :] = context_cls
    r.tall[PAIR_ROWS + PAD :, :] = embedded_cls
    pack_one = pack_tall(r.mail_one, PAD, lambda at, both: both)

    def pack_one_step(part):
        pack_one(part)
        pl.when(part == 0)(steps_u[1])
        pl.when(part == 4)(steps_u[2])

    every(0, CHIPS // 2, pack_one_step)
    steps_u[3]()

    def post_one(box, got, index, step):
        other, to_core, to_chip = peer(step)
        remote(
            box.at[other], got.at[me], r.one_send.at[index], r.one_recv.at[index], to_core, to_chip
        ).start()

    r.got_one[me] = r.mail_one[me]

    def open_step(tile):
        open_tile(tile)
        pl.when(tile == 0)(steps_e[3])
        pl.when(tile == 2)(steps_u[4])

    def feed_step(steps, part):
        feed_up(part)
        for index in range(3):
            step = 3 * part + index + 1
            pl.when(step < DEVICES)(partial(post_one, r.mail_one, r.got_one, 1, step))
        for index, step in steps:
            pl.when(part == index)(step)

    first_parts, parts = 6, WIDE // BLOCK
    every(0, TOKENS // BLOCK, open_step)
    r.tile_up[...] = up_product(0)
    every(0, first_parts, partial(feed_step, [(1, steps_u[5]), (2, steps_e[4]), (5, steps_e[5])]))

    units = r.units[...].reshape(SLOT_ROWS, WIDTH)
    weight_row, pair_row, side_row = r.pairs[0:1, :], r.pairs[1:2, :], r.pairs[2:3, :]

    def pair_scores(rows, pair_col, side_col):
        opposite = side_col + side_row == 1.0
        partner = opposite & (pair_col == pair_row)
        raw = SCORE_SCALE * dot_turned(rows, units)
        shifted = jnp.where(partner, raw - SCORE_SCALE * MARGIN_WIDTH, raw)
        return jnp.where(opposite, shifted, MASK_FLOOR), partner

    every_score, every_partner = pair_scores(
        units, r.pairs_col[:, 1:2], r.pairs_col[:, 2:3]
    )
    peak_row = jnp.max(every_score, axis=0, keepdims=True)
    log_row = peak_row + jnp.log(
        jnp.sum(jnp.exp(every_score - peak_row), axis=0, keepdims=True)
    )
    picked_row = jnp.sum(jnp.where(every_partner, every_score, 0.0), axis=0, keepdims=True)
    r.loss[...] = jnp.sum(weight_row * (log_row - picked_row), axis=1, keepdims=True)

    rows_here = pl.ds(pl.multiple_of(me * PAD, 16), PAD)
    own_score, own_partner = pair_scores(
        r.units[here], r.pairs_col[rows_here, 1:2], r.pairs_col[rows_here, 2:3]
    )
    own_partner = own_partner.astype(FULL)
    own_peak = jnp.max(own_score, axis=1, keepdims=True)
    own_exp = jnp.exp(own_score - own_peak)
    own_share = own_exp / jnp.sum(own_exp, axis=1, keepdims=True)
    by_row = (r.pairs_col[rows_here, 0:1] * (own_share - own_partner)).astype(LOW)
    by_column = (weight_row * (jnp.exp(own_score - log_row) - own_partner)).astype(LOW)
    unit_grad = SCORE_SCALE * (dot(by_row, units) + dot(by_column, units))
    along = jnp.sum(unit * unit_grad, axis=-1, keepdims=True)
    summary_grad = (unit_grad - unit * along) / magnitude

    residual_grad, grad_g2, grad_s2 = norm_back_parts(
        summary_grad, normed_two, inverse_two, vector(6)
    )
    down_grad = residual_grad.astype(LOW)
    r.downs[here] = down_grad
    steps_d[0]()
    r.hidden_cls[...] = down_grad

    def up_back(part):
        at = pl.ds(pl.multiple_of(part * WIDTH, BLOCK), WIDTH)
        act_grad = dot_turned(r.hidden_cls[...], r.wc[at, :])
        r.active_cls[:, at] = (act_grad * r.slope_cls[:, at]).astype(LOW)

    every(0, WIDE // WIDTH, up_back)
    steps_d[1]()

    def hidden_back(part):
        at = pl.ds(pl.multiple_of(part * BLOCK, BLOCK), BLOCK)
        r.wide_cls[:, at] = dot_turned(r.active_cls[...], r.wb[at, :])

    every(0, WIDTH // BLOCK, hidden_back)
    hidden_grad = r.wide_cls[:, 0:WIDTH] + residual_grad
    first_grad, grad_g1, grad_s1 = norm_back_parts(
        hidden_grad, r.normed_one[...], inverse_one, vector(3)
    )
    attend_grad = first_grad.astype(LOW)
    context_grad = dot_turned(attend_grad, r.wa[:, 3 * WIDTH : 4 * WIDTH]).astype(LOW)
    attend_here = r.attends.at[here]
    attend_here[:, 0:WIDTH] = attend_grad
    attend_here[:, WIDTH : 2 * WIDTH] = context_grad
    steps_a[0]()
    steps_d[2]()
    context_tall = spread(context_grad)
    probs = r.probs[...]
    prob_grad = dot_turned(context_tall, r.qkv[:, values])
    inner = jnp.sum(probs * prob_grad, axis=1, keepdims=True)
    score_grad = (probs * (prob_grad - inner)).astype(LOW)
    steps_a[1]()
    r.mail_two[:, 48:64, :] = pack_coefs(jnp.concatenate([probs_low, score_grad], axis=0))
    r.got_two[me, 48:64, :] = r.mail_two[me, 48:64, :]
    query_grad = (fold(dot(score_grad, r.qkv[:, keys])) * scale).astype(LOW)
    probs_total = jnp.sum(probs_low.astype(FULL), axis=1, keepdims=True)
    grad_bvalue = jnp.sum(probs_total * context_tall.astype(FULL), axis=0, keepdims=True)
    grad_bquery = jnp.sum(query_grad.astype(FULL), axis=0, keepdims=True)
    r.queries[here] = query_grad
    own_sums = jnp.concatenate(
        [jnp.zeros((2 * depth, WIDTH), FULL)]
        + [grad_bquery, grad_bvalue, grad_g1, grad_s1, grad_g2, grad_s2]
        + [jnp.zeros((128 - 2 * depth - 6, WIDTH), FULL)],
        axis=0,
    )
    r.own_sums[...] = jnp.transpose(own_sums)
    steps_q[0]()
    steps_a[2]()
    r.tall[0:PAIR_ROWS, :] = (dot(score_grad, r.embedded[...]) * scale).astype(LOW)

    def with_sums(at, both):
        return both + r.own_sums[pl.ds(pl.multiple_of(at * depth, 16), depth), :]

    pack_two = pack_tall(r.mail_two, 0, with_sums)

    def send_two(at):
        remote(
            r.mail_two.at[at],
            r.got_two.at[me],
            r.one_send.at[2],
            r.one_recv.at[2],
            lax.div(at, CHIPS),
            lax.rem(at, CHIPS),
        ).start()

    def pack_two_step(step):
        part = lax.rem(step + lax.div(chip, 2), CHIPS // 2)
        pack_two(part)
        for half in range(CORES):
            for one in range(2):
                at = half * CHIPS + 2 * part + one
                pl.when(at != me)(partial(send_two, at))

    every(0, CHIPS // 2, pack_two_step)
    r.got_two[me, 0:48, :] = r.mail_two[me, 0:48, :]
    steps_q[1]()

    def all_rows(buffer, start, width=WIDTH):
        return buffer[:, :, :, :, start : start + width].reshape(SLOT_ROWS, width)

    quarter_rows_count = quarter_size * PAD

    def from_sent(quarter):
        span = pl.ds(pl.multiple_of(quarter * quarter_rows_count, 128), quarter_rows_count)
        shape = (GROUPS * quarter_rows_count, quarter_rows_count)
        lanes = (iota(shape, 1) + quarter * quarter_rows_count).astype(FULL)
        named = r.found[0:GROUPS, span, 1:2].reshape(GROUPS * quarter_rows_count, 1)
        return (named == lanes).astype(LOW), span

    def quarter_part(buffer, quarter, start):
        planes = pl.ds(lax.rem(quarter, 2) * 2, 2)
        part = buffer[lax.div(quarter, 2), planes, :, :, start : start + BLOCK]
        return part.reshape(quarter_rows_count, BLOCK)

    def widened(coefs, group, start, kind):
        lane_head = over(iota((128, BLOCK), 1) + start, HEAD)
        lanes = iota((128, BLOCK), 0) == lane_head + group * 2 * PAD + kind
        return dot(coefs, lanes.astype(LOW))

    half_wide = WIDE // 2

    def slope_tile(part):
        at = pl.ds(pl.multiple_of(core * half_wide + part * BLOCK, BLOCK), BLOCK)
        up_pre = dot(all_rows(r.early, 0), r.wb[:, at]) + r.up_bias[0:1, at]
        _, slope = gelu_parts(up_pre)
        r.slopes[:, pl.ds(pl.multiple_of(part * BLOCK, BLOCK), BLOCK)] = slope.astype(LOW)

    def slot_queries(quarter):
        sents, span = from_sent(quarter)
        for start in range(0, WIDTH, BLOCK):
            rows = dot(sents, quarter_part(r.early, quarter, WIDTH + start)).astype(LOW)
            rows = rows.reshape(GROUPS, quarter_rows_count, BLOCK)
            r.slot_query[:, span, start : start + BLOCK] = rows

    def activate():
        at = pl.ds(pl.multiple_of(chip // 2 * 2 * deep, 128), 2 * deep)
        up_pre = dot(all_rows(r.early, 0), r.wb[:, at]) + r.up_bias[0:1, at]
        r.active_turned[...] = jnp.transpose(gelu(up_pre)).astype(LOW)
        r.hidden_turned[...] = jnp.transpose(all_rows(r.early, 0))

    rest = [steps_d[3], steps_a[3], steps_q[2], steps_d[4], steps_a[4]]
    rest = [(first_parts + index, step) for index, step in enumerate(rest)]
    every(first_parts, parts - 1, partial(feed_step, rest))
    feed_up(parts - 1, last=True)

    def rest_step(part):
        feed_rest(part)
        for index, step in enumerate([steps_q[3], steps_d[5], steps_a[5]]):
            pl.when(part == index)(step)

    every(0, WIDTH // BLOCK, rest_step)
    steps_q[4]()

    def down_step(part):
        feed_down(part)
        for index, ends in enumerate([[drain_a, drain_b], [drain_c, drain_u], [drain_e]]):
            for end in ends:
                pl.when(part == index)(end)

    every(0, WIDTH // BLOCK, down_step)
    every(0, TOKENS // BLOCK, close_tile)
    every(0, 4, slot_queries)
    every(0, 6, slope_tile)
    activate()

    all_but_one(r.got_one, 1).wait_recv()
    all_but_one(r.got_two, 2).wait_recv()
    def slot_probs(group):
        got = r.got_two[:, 48:64, :].reshape(SLOT_ROWS, 128)
        for start in range(0, WIDTH, BLOCK):
            r.replies[group, :, start : start + BLOCK] = widened(got, group, start, 0).astype(LOW)

    def slot_values(quarter):
        sents, span = from_sent(quarter)
        for start in range(0, WIDTH, BLOCK):
            lanes = slice(start, start + BLOCK)
            rows = dot(sents, quarter_part(r.attends, quarter, WIDTH + start))
            rows = rows.reshape(GROUPS, quarter_rows_count, BLOCK)
            rows = r.replies[:, span, lanes].astype(FULL) * rows
            r.replies[:, span, lanes] = rows.astype(LOW)

    every(0, GROUPS, slot_probs)
    every(0, 4, slot_values)

    def head_products(got, first_row, right, start, target):
        def one_head(head):
            lane = core * (WIDTH // 2) + lax.div(head, 2) * 128
            pair_rows = right[:, :, :, :, pl.ds(pl.multiple_of(start + lane, 128), 128)]
            row = pl.ds(pl.multiple_of(first_row + lax.rem(head, 3) * PAD, 16), PAD)
            block_rows = got[:, row, :].reshape(SLOT_ROWS, 128)
            r.product[...] = contract(block_rows, pair_rows.reshape(SLOT_ROWS, 128), 0, 0)
            part = r.product[pl.ds(pl.multiple_of(lax.div(head, 3) * depth, 16), depth), :]
            at = pl.ds(pl.multiple_of(lane, 128), 128)
            own_lanes = over(iota((depth, 128), 1), HEAD) == lax.rem(head, 2)
            target[:, at] = jnp.where(own_lanes, part, target[:, at])

        every(0, HEADS // 2, one_head)

    def half_of(ref, at_core):
        half = ref.shape[1] // 2
        return ref.at[:, pl.ds(pl.multiple_of(at_core * half, 128), half)]

    def half_copy(index, ref, at_core):
        part = half_of(ref, at_core)
        return remote(part, part, r.half_send.at[index], r.half_recv.at[index], 1 - core, chip)

    own_half = pl.ds(pl.multiple_of(core * (WIDTH // 2), 128), WIDTH // 2)
    r.g_wv[:, own_half] = jnp.zeros((depth, WIDTH // 2), FULL)
    r.g_wk[:, own_half] = jnp.zeros((depth, WIDTH // 2), FULL)
    head_products(r.got_one, PAD, r.attends, WIDTH, r.g_wv)
    half_copy(0, r.g_wv, core).start()

    downs = r.downs[...].reshape(SLOT_ROWS, WIDTH)
    attends = all_rows(r.attends, 0)

    def up_tile(part):
        at = pl.ds(pl.multiple_of(core * half_wide + part * BLOCK, BLOCK), BLOCK)
        slope = r.slopes[:, pl.ds(pl.multiple_of(part * BLOCK, BLOCK), BLOCK)].astype(FULL)
        up_all = (dot_turned(r.downs[...].reshape(SLOT_ROWS, WIDTH), r.wc[at, :]) * slope)
        up_all = up_all.astype(LOW)
        r.g_wup[0:depth, at] = dot(r.hidden_turned[mine, :], up_all)
        total = jnp.sum(up_all.astype(FULL), axis=0, keepdims=True)
        r.g_wup[depth : depth + 8, at] = jnp.broadcast_to(total, (8, BLOCK))

    every(0, half_wide // BLOCK, up_tile)
    half_copy(1, r.g_wup, core).start()
    r.g_wdown[...] = dot(r.active_turned[pl.ds(pl.multiple_of(chip % 2 * deep, 16), deep), :], downs)
    r.left_turned[...] = jnp.transpose(r.got_one[:, 0:PAD, :].reshape(SLOT_ROWS, 128))
    r.g_wo[...] = dot(r.left_turned[0:depth, :], attends)

    def own_part(rows, size):
        start = chip * size
        window = jnp.minimum(lax.div(start, 128) * 128, rows.shape[1] - BLOCK)
        part = rows[:, pl.ds(pl.multiple_of(window, 128), BLOCK)]
        return pltpu.roll(part, lax.rem(BLOCK + window - start, BLOCK), 1)

    for quarter in range(4):
        rows_of(quarter).wait_send()

    def slot_grads(group):
        got_scores = r.got_two[:, 48:64, :].reshape(SLOT_ROWS, 128)
        for start in range(0, WIDTH, BLOCK):
            lanes = slice(start, start + BLOCK)
            rows = r.slot_query[group, :, lanes].astype(FULL)
            rows = widened(got_scores, group, start, PAD) * rows * scale
            r.slot_query[group, :, lanes] = rows.astype(LOW)
        for start in range(0, WIDTH, BLOCK):
            lanes = slice(start, start + BLOCK)
            row_grad = dot_turned(r.slot_query[group], r.wa[lanes, keys])
            row_grad = row_grad + dot_turned(r.replies[group], r.wa[lanes, values])
            r.rows[group, :, lanes] = row_grad.astype(LOW)

    every(0, GROUPS, slot_grads)
    steps_q[5]()
    query_grads = all_rows(r.queries, 0)
    extra = dot_turned(query_grads, r.wa[:, 0:WIDTH]) + attends.astype(FULL)
    r.extra[...] = extra.astype(LOW)
    r.g_wq[...] = dot(r.left_turned[depth : 2 * depth, :], query_grads)

    half_rows = VOCAB_ROWS // 2

    def table_copy(tile):
        at = pl.ds(pl.multiple_of(tile * half_rows, BLOCK), half_rows)
        return pltpu.make_async_copy(
            r.table_full.at[at], r.table_grad.at[at], r.table_sem.at[tile]
        )

    def table_tile(tile):
        at = pl.ds(pl.multiple_of(tile * half_rows, BLOCK), half_rows)
        for start in range(0, WIDTH, BLOCK):
            lanes = slice(start, start + BLOCK)
            slot_rows = r.rows[:, :, lanes].reshape(GROUPS * SLOT_ROWS, BLOCK)
            r.table_full[at, lanes] = dot(r.by_row[at, 0 : GROUPS * SLOT_ROWS], slot_rows) + dot(
                r.by_row[at, GROUPS * SLOT_ROWS :], r.extra[:, lanes]
            )
        table_copy(tile).start()

    every(0, 2, table_tile)
    head_products(r.got_two, 0, r.early, WIDTH, r.g_wk)
    half_copy(2, r.g_wk, core).start()

    down_total = jnp.sum(downs.astype(FULL), axis=0, keepdims=True)
    attend_total = jnp.sum(attends.astype(FULL), axis=0, keepdims=True)
    sums = jnp.sum(r.got_two[:, 0:48, :].astype(FULL), axis=0)
    sums = jnp.concatenate([sums, jnp.zeros((128 - 48, 128), FULL)], axis=0)
    r.totals[...] = jnp.concatenate([attend_total, down_total, jnp.zeros((6, WIDTH), FULL)], axis=0)
    r.g_small[8:16, :] = own_part(r.totals, depth)
    r.g_small[0:8, 0:128] = jnp.transpose(sums)[2 * depth : 2 * depth + 8, :]
    r.g_small[0:8, 128:BLOCK] = jnp.zeros((8, BLOCK - 128), FULL)
    half_copy(1, r.g_wup, 1 - core).wait_recv()
    r.g_small[16:24, :] = own_part(r.g_wup.at[depth : depth + 8, :], deep)

    half_copy(0, r.g_wv, 1 - core).wait_recv()
    half_copy(2, r.g_wk, 1 - core).wait_recv()
    for index, ref in enumerate([r.g_wv, r.g_wup, r.g_wk]):
        half_copy(index, ref, core).wait_send()

    for index, ref in enumerate([r.every_ids, r.got_one, r.got_two]):
        all_but_one(ref, index).wait_send()
    all_smalls().wait_send()
    for end in [drain_d, drain_a2, drain_q]:
        end()
    every(0, TOKENS // BLOCK, lambda tile: layer_copy(tile).wait())
    every(0, 2, lambda tile: table_copy(tile).wait())


def layer(inputs):
    dma = pltpu.SemaphoreType.DMA
    vmem = pl.BlockSpec(memory_space=pltpu.VMEM)
    anywhere = pl.BlockSpec(memory_space=pl.ANY)
    depth, deep = WIDTH // CHIPS, WIDE // CHIPS

    def gathered(width):
        return pltpu.VMEM((CORES, PLANES, LINES, PAD, width), LOW)

    outputs = dict(
        layer_out=((TOKENS, WIDTH), LOW),
        table_grad=((VOCAB_ROWS, WIDTH), FULL),
        g_wq=((depth, WIDTH), FULL),
        g_wk=((depth, WIDTH), FULL),
        g_wv=((depth, WIDTH), FULL),
        g_wo=((depth, WIDTH), FULL),
        g_wup=((depth + 8, WIDE), FULL),
        g_wdown=((deep, WIDTH), FULL),
        g_small=((24, BLOCK), FULL),
        loss=((1, 1), FULL),
    )
    scratch = dict(
        ids=pltpu.VMEM((8, 128), jnp.int32),
        every_ids=pltpu.VMEM((DEVICES, 8, 128), jnp.int32),
        rank=pltpu.VMEM((DEVICES, TOKENS), FULL),
        code=pltpu.VMEM((DEVICES, TOKENS), FULL),
        found=pltpu.VMEM((GROUPS + 1, SLOT_ROWS, 2), FULL),
        block_bias=pltpu.VMEM((2 * BLOCK, BLOCK // 2), FULL),
        valid_bias=pltpu.VMEM((8, TOKENS), FULL),
        slot_col=pltpu.VMEM((TOKENS, 1), FULL),
        slot_line=pltpu.VMEM((8, TOKENS), FULL),
        valid_col=pltpu.VMEM((TOKENS, 1), FULL),
        valid_line=pltpu.VMEM((8, TOKENS), FULL),
        pairs=pltpu.VMEM((8, SLOT_ROWS), FULL),
        pairs_col=pltpu.VMEM((SLOT_ROWS, 128), FULL),
        vectors=pltpu.VMEM((PAD, WIDTH), FULL),
        up_bias=pltpu.VMEM((8, WIDE), FULL),
        qkv_bias=pltpu.VMEM((8, 3 * WIDTH), FULL),
        smalls=pltpu.VMEM((PAD, CHIPS * 128), LOW),
        wa=pltpu.VMEM((WIDTH, 4 * WIDTH), LOW),
        wb=pltpu.VMEM((WIDTH, WIDE), LOW),
        wc=pltpu.VMEM((WIDE, WIDTH), LOW),
        chosen=pltpu.VMEM((GROUPS, SLOT_ROWS, VOCAB_ROWS), LOW),
        by_row=pltpu.VMEM((VOCAB_ROWS, (GROUPS + 1) * SLOT_ROWS), LOW),
        rows=pltpu.VMEM((GROUPS, SLOT_ROWS, WIDTH), LOW),
        replies=pltpu.VMEM((GROUPS, SLOT_ROWS, WIDTH), LOW),
        slot_query=pltpu.VMEM((GROUPS, SLOT_ROWS, WIDTH), LOW),
        extra=pltpu.VMEM((SLOT_ROWS, WIDTH), LOW),
        hidden_cls=pltpu.VMEM((PAD, WIDTH), LOW),
        active_cls=pltpu.VMEM((PAD, WIDE), LOW),
        slope_cls=pltpu.VMEM((PAD, WIDE), FULL),
        wide_cls=pltpu.VMEM((PAD, WIDTH), FULL),
        tall=pltpu.VMEM((PAIR_ROWS + 2 * PAD, WIDTH), LOW),
        own_sums=pltpu.VMEM((WIDTH, 128), FULL),
        product=pltpu.VMEM((128, 128), FULL),
        slot_hot=pltpu.VMEM((GROUPS, SLOT_ROWS, TOKENS), LOW),
        tile_up=pltpu.VMEM((TOKENS, BLOCK), FULL),
        embedded=pltpu.VMEM((TOKENS, WIDTH), LOW),
        qkv=pltpu.VMEM((TOKENS, 3 * WIDTH), LOW),
        context=pltpu.VMEM((TOKENS, WIDTH), LOW),
        table_full=pltpu.VMEM((VOCAB_ROWS, WIDTH), FULL),
        probs=pltpu.VMEM((PAIR_ROWS, TOKENS), FULL),
        normed_one=pltpu.VMEM((PAD, WIDTH), FULL),
        units=gathered(WIDTH),
        early=gathered(2 * WIDTH),
        downs=gathered(WIDTH),
        attends=gathered(2 * WIDTH),
        queries=gathered(WIDTH),
        slopes=pltpu.VMEM((SLOT_ROWS, WIDE // 2), LOW),
        hidden_turned=pltpu.VMEM((WIDTH, SLOT_ROWS), LOW),
        active_turned=pltpu.VMEM((2 * deep, SLOT_ROWS), LOW),
        left_turned=pltpu.VMEM((128, SLOT_ROWS), LOW),
        totals=pltpu.VMEM((8, WIDTH), FULL),
        mail_one=pltpu.VMEM((DEVICES, 64, 128), LOW),
        got_one=pltpu.VMEM((DEVICES, 64, 128), LOW),
        mail_two=pltpu.VMEM((DEVICES, 64, 128), LOW),
        got_two=pltpu.VMEM((DEVICES, 64, 128), LOW),
        rows_send=dma((4,)),
        rows_recv=dma((4,)),
        one_send=dma((4,)),
        one_recv=dma((4,)),
        small_send=dma((1,)),
        small_recv=dma((1,)),
        weight_send=dma((3, 7)),
        weight_recv=dma((3, 18)),
        gather_send=dma((5, 13)),
        gather_recv=dma((5, 13)),
        half_send=dma((3,)),
        half_recv=dma((3,)),
        out_sem=dma((TOKENS // BLOCK,)),
        table_sem=dma((2,)),
    )
    names = INPUTS + OUTPUTS + list(scratch)
    return pl.pallas_call(
        partial(layer_kernel, names),
        out_shape=tuple(jax.ShapeDtypeStruct(*outputs[name]) for name in OUTPUTS),
        in_specs=[vmem] * len(INPUTS),
        out_specs=(anywhere, anywhere) + (vmem,) * (len(OUTPUTS) - 2),
        scratch_shapes=list(scratch.values()),
        compiler_params=pltpu.CompilerParams(
            collective_id=0, has_side_effects=True, vmem_limit_bytes=VMEM_LIMIT
        ),
        name="layer",
    )(*inputs)


def finish_kernel(count, *refs):
    large, (small, loss), outs = refs[:count], refs[count : count + 2], refs[count + 2 : -1]
    sems = refs[-1]
    copies = []
    for index, (source, target) in enumerate(zip(large, outs)):
        part = source if source.shape == target.shape else source.at[: target.shape[0]]
        copies.append(pltpu.make_async_copy(part, target, sems.at[index]))
        copies[-1].start()
    for row, target in zip([0, 1, 8, 2, 3, 16, 9, 4, 5], outs[count : count + 9]):
        size = target.shape[0]
        target[...] = small[row : row + 1, 0:size].reshape(size)
    outs[-1][...] = loss[...].reshape(1)
    for one in copies:
        one.wait()


def finish(results):
    vmem = pl.BlockSpec(memory_space=pltpu.VMEM)
    anywhere = pl.BlockSpec(memory_space=pl.ANY)
    depth, deep = WIDTH // CHIPS, WIDE // CHIPS
    count = len(results) - 2
    shapes = [(one.shape, one.dtype) for one in results[:count]]
    shapes[6] = ((depth, WIDE), FULL)
    shapes += [((depth,), FULL)] * 5 + [((deep,), FULL)] + [((depth,), FULL)] * 3
    shapes.append(((1,), FULL))
    return pl.pallas_call(
        partial(finish_kernel, count),
        out_shape=tuple(jax.ShapeDtypeStruct(*one) for one in shapes),
        in_specs=[vmem] * (count + 2),
        out_specs=(anywhere,) * count + (vmem,) * 10,
        scratch_shapes=[pltpu.SemaphoreType.DMA((count,))],
        name="finish",
    )(*results)


def block_body(
    table,
    token_ids,
    sent_lengths,
    pair_slot,
    pair_lang,
    *parameters,
):
    results = finish(layer((table, token_ids, sent_lengths, pair_slot, pair_lang) + parameters))
    layer_out, table_grad, g_wq, g_wk, g_wv, g_wo, g_wup, g_wdown = results[:8]
    g_bq, g_bv, g_bo, g_g1, g_s1, g_bup, g_bdown, g_g2, g_s2, loss = results[8:]
    return (
        layer_out.reshape(token_ids.shape + (WIDTH,)),
        loss.reshape(()),
        table_grad,
        g_wq,
        g_bq,
        g_wk,
        g_wv,
        g_bv,
        g_wo,
        g_bo,
        g_g1,
        g_s1,
        g_wup,
        g_bup,
        g_wdown,
        g_bdown,
        g_g2,
        g_s2,
    )


def solution(mesh):
    in_specs = (
        P(("dp", "fsdp"), None),
        P(("dp", "fsdp"), None),
        P(("dp", "fsdp")),
        P(),
        P(),
        P("fsdp", None),
        P("fsdp"),
        P("fsdp", None),
        P("fsdp", None),
        P("fsdp"),
        P("fsdp", None),
        P("fsdp"),
        P("fsdp"),
        P("fsdp"),
        P("fsdp", None),
        P("fsdp"),
        P("fsdp", None),
        P("fsdp"),
        P("fsdp"),
        P("fsdp"),
    )
    out_specs = (
        P(("dp", "fsdp"), None, None),
        P(),
        P(("dp", "fsdp"), None),
        P("fsdp", None),
        P("fsdp"),
        P("fsdp", None),
        P("fsdp", None),
        P("fsdp"),
        P("fsdp", None),
        P("fsdp"),
        P("fsdp"),
        P("fsdp"),
        P("fsdp", None),
        P("fsdp"),
        P("fsdp", None),
        P("fsdp"),
        P("fsdp"),
        P("fsdp"),
    )
    sizes = dict(mesh.shape)
    body = general_body
    if sizes["dp"] == CORES and sizes["fsdp"] == CHIPS:
        body = block_body
    return jax.shard_map(body, mesh=mesh, in_specs=in_specs, out_specs=out_specs, check_vma=False)
```

```python
from functools import partial
from types import SimpleNamespace

import jax
import jax.numpy as jnp
from jax import lax
from jax.experimental import pallas as pl
from jax.experimental.pallas import tpu as pltpu
from jax.sharding import PartitionSpec as P

HEADS = 12
HEAD = 64
LANGS = 109


EPSILON = 1e-06
SCORE_SCALE = 50.0
MARGIN_WIDTH = 0.3
MASK_FLOOR = -1000000000.0


def contract(left_side, right_side, left_dim, right_dim):
    return lax.dot_general(
        left_side,
        right_side,
        (((left_dim,), (right_dim,)), ((), ())),
        preferred_element_type=jnp.float32,
    )


def norm_rows(inputs, ln_gain, ln_shift):
    row_mean = jnp.mean(inputs, axis=-1, keepdims=True)
    centered = inputs - row_mean
    variance = jnp.mean(centered * centered, axis=-1, keepdims=True)
    inverse = lax.rsqrt(variance + EPSILON)
    normed = centered * inverse
    return (normed * ln_gain + ln_shift, normed, inverse)


def norm_back(grad_output, normed, inverse, ln_gain):
    grad_normed = grad_output * ln_gain
    first_term = jnp.mean(grad_normed, axis=-1, keepdims=True)
    second_term = jnp.mean(grad_normed * normed, axis=-1, keepdims=True)
    grad_input = inverse * (grad_normed - first_term - normed * second_term)
    return (grad_input, jnp.sum(grad_output * normed, axis=0), jnp.sum(grad_output, axis=0))


def general_body(
    table,
    token_ids,
    sent_lengths,
    pair_slot,
    pair_lang,
    w_query,
    b_query,
    w_key,
    w_value,
    b_value,
    w_out,
    b_out,
    ln1_gain,
    ln1_bias,
    w_up,
    b_up,
    w_down,
    b_down,
    ln2_gain,
    ln2_bias,
):
    sentences, length = token_ids.shape
    tokens = sentences * length
    vocab_rows, model_width = table.shape
    owners = lax.axis_size(("dp", "fsdp"))
    dp_count = lax.axis_size("dp")
    fsdp_count = lax.axis_size("fsdp")
    capacity = max(2, 2 * tokens // owners)
    device = lax.axis_index(("dp", "fsdp"))
    score_factor = HEAD ** (-0.5)
    flat_ids = token_ids.reshape(tokens)
    owner_of = flat_ids // vocab_rows
    member = (owner_of[:, None] == jnp.arange(owners, dtype=jnp.int32)[None, :]).astype(jnp.int32)
    owner_rank = jnp.sum(jnp.cumsum(member, axis=0) * member, axis=1) - 1
    slot_of = owner_of * capacity + owner_rank
    requests = jnp.full((owners * capacity,), -1, jnp.int32).at[slot_of].set(flat_ids)
    received = lax.all_to_all(
        lax.all_to_all(
            requests.reshape(dp_count, fsdp_count, capacity),
            "dp",
            split_axis=0,
            concat_axis=0,
            tiled=True,
        ),
        "fsdp",
        split_axis=1,
        concat_axis=1,
        tiled=True,
    )
    present = received >= 0
    local_rows = jnp.where(present, received - device * vocab_rows, 0)
    found_rows = jnp.where(present[..., None], table[local_rows], jnp.zeros((), table.dtype))
    replies = lax.all_to_all(
        lax.all_to_all(found_rows, "dp", split_axis=0, concat_axis=0, tiled=True),
        "fsdp",
        split_axis=1,
        concat_axis=1,
        tiled=True,
    )
    embedded = replies.reshape(owners * capacity, model_width)[slot_of]
    gathered = (
        lax.all_gather(w_query, "fsdp", axis=0, tiled=True),
        lax.all_gather(b_query, "fsdp", axis=0, tiled=True),
        lax.all_gather(w_key, "fsdp", axis=0, tiled=True),
        lax.all_gather(w_value, "fsdp", axis=0, tiled=True),
        lax.all_gather(b_value, "fsdp", axis=0, tiled=True),
        lax.all_gather(w_out, "fsdp", axis=0, tiled=True),
        lax.all_gather(b_out, "fsdp", axis=0, tiled=True),
        lax.all_gather(ln1_gain, "fsdp", axis=0, tiled=True),
        lax.all_gather(ln1_bias, "fsdp", axis=0, tiled=True),
        lax.all_gather(w_up, "fsdp", axis=0, tiled=True),
        lax.all_gather(b_up, "fsdp", axis=0, tiled=True),
        lax.all_gather(w_down, "fsdp", axis=0, tiled=True),
        lax.all_gather(b_down, "fsdp", axis=0, tiled=True),
        lax.all_gather(ln2_gain, "fsdp", axis=0, tiled=True),
        lax.all_gather(ln2_bias, "fsdp", axis=0, tiled=True),
    )
    (
        full_wq,
        full_bq,
        full_wk,
        full_wv,
        full_bv,
        full_wo,
        full_bo,
        full_g1,
        full_s1,
        full_wup,
        full_bup,
        full_wdown,
        full_bdown,
        full_g2,
        full_s2,
    ) = gathered
    valid_mask = jnp.arange(length, dtype=jnp.int32)[None, :] < sent_lengths[:, None]
    head_shape = (sentences, length, HEADS, HEAD)
    queries = (jnp.dot(embedded, full_wq, preferred_element_type=jnp.float32) + full_bq).astype(
        jnp.bfloat16
    )
    key_heads = (
        jnp.dot(embedded, full_wk, preferred_element_type=jnp.float32)
        .astype(jnp.bfloat16)
        .reshape(head_shape)
    )
    value_heads = (
        (jnp.dot(embedded, full_wv, preferred_element_type=jnp.float32) + full_bv)
        .astype(jnp.bfloat16)
        .reshape(head_shape)
    )
    query_heads = queries.reshape(head_shape)
    scores = (
        jnp.einsum("bqhd,bkhd->bhqk", query_heads, key_heads, preferred_element_type=jnp.float32)
        * score_factor
    )
    scores = jnp.where(valid_mask[:, None, None, :], scores, MASK_FLOOR)
    row_peak = jnp.max(scores, axis=-1, keepdims=True)
    shifted = jnp.exp(scores - row_peak)
    totals = jnp.sum(shifted, axis=-1, keepdims=True)
    attn_probs = (shifted / totals).astype(jnp.bfloat16)
    context = jnp.einsum(
        "bhqk,bkhd->bqhd", attn_probs, value_heads, preferred_element_type=jnp.float32
    )
    context = context.reshape(tokens, model_width).astype(jnp.bfloat16)
    attended = jnp.dot(context, full_wo, preferred_element_type=jnp.float32) + full_bo
    hidden, normed_one, inverse_one = norm_rows(
        embedded.astype(jnp.float32) + attended, full_g1, full_s1
    )
    hidden_low = hidden.astype(jnp.bfloat16)
    up_pre = jnp.dot(hidden_low, full_wup, preferred_element_type=jnp.float32) + full_bup
    activated = jax.nn.gelu(up_pre, approximate=False).astype(jnp.bfloat16)
    down_pre = jnp.dot(activated, full_wdown, preferred_element_type=jnp.float32) + full_bdown
    normed_out, normed_two, inverse_two = norm_rows(hidden + down_pre, full_g2, full_s2)
    layer_out = jnp.where(valid_mask.reshape(tokens)[:, None], normed_out, 0.0).astype(jnp.bfloat16)
    layer_out = layer_out.reshape(sentences, length, model_width)

    def first_rows(matrix):
        return matrix.reshape(sentences, length, matrix.shape[-1])[:, 0]

    summary = first_rows(normed_out)
    magnitude = jnp.sqrt(jnp.sum(summary * summary, axis=-1, keepdims=True) + EPSILON)
    unit_vector = summary / magnitude
    unit_low = unit_vector.astype(jnp.bfloat16)
    every_unit = lax.all_gather(unit_low, ("dp", "fsdp"), axis=0, tiled=True)
    every_side = pair_slot % 2
    every_pair = pair_slot // 2
    my_slots = lax.dynamic_slice_in_dim(pair_slot, device * sentences, sentences)
    my_side = my_slots % 2
    my_pair = my_slots // 2
    lang_onehot = (pair_lang[:, None] == jnp.arange(LANGS, dtype=jnp.int32)[None, :]).astype(
        jnp.float32
    )
    per_lang = jnp.sum(lang_onehot, axis=0)
    per_pair = 1.0 / (2.0 * LANGS * jnp.sum(lang_onehot * per_lang[None, :], axis=1))
    my_weight = jnp.take(per_pair, my_pair)
    opposite = my_side[:, None] != every_side[None, :]
    partner = opposite & (my_pair[:, None] == every_pair[None, :])
    raw_scores = SCORE_SCALE * contract(unit_low, every_unit, 1, 1)
    pair_scores = jnp.where(partner, raw_scores - SCORE_SCALE * MARGIN_WIDTH, raw_scores)
    pair_scores = jnp.where(opposite, pair_scores, MASK_FLOOR)
    pair_peak = jnp.max(pair_scores, axis=1, keepdims=True)
    pair_exp = jnp.exp(pair_scores - pair_peak)
    pair_total = jnp.sum(pair_exp, axis=1, keepdims=True)
    log_total = pair_peak[:, 0] + jnp.log(pair_total[:, 0])
    picked = jnp.sum(jnp.where(partner, pair_scores, 0.0), axis=1)
    loss_value = lax.psum(jnp.sum(my_weight * (log_total - picked)), ("dp", "fsdp"))
    coefficients = (
        my_weight[:, None] * (pair_exp / pair_total - partner.astype(jnp.float32))
    ).astype(jnp.bfloat16)
    unit_grad = SCORE_SCALE * contract(coefficients, every_unit, 1, 0)
    column_terms = SCORE_SCALE * contract(coefficients, unit_low, 0, 0)
    unit_grad = unit_grad + lax.psum_scatter(
        column_terms, ("dp", "fsdp"), scatter_dimension=0, tiled=True
    )
    along = jnp.sum(unit_vector * unit_grad, axis=-1, keepdims=True)
    summary_grad = (unit_grad - unit_vector * along) / magnitude
    again_weights = (
        lax.all_gather(w_query, "fsdp", axis=0, tiled=True),
        lax.all_gather(w_key, "fsdp", axis=0, tiled=True),
        lax.all_gather(w_value, "fsdp", axis=0, tiled=True),
        lax.all_gather(w_out, "fsdp", axis=0, tiled=True),
        lax.all_gather(ln1_gain, "fsdp", axis=0, tiled=True),
        lax.all_gather(w_up, "fsdp", axis=0, tiled=True),
        lax.all_gather(w_down, "fsdp", axis=0, tiled=True),
        lax.all_gather(ln2_gain, "fsdp", axis=0, tiled=True),
    )
    again_wq, again_wk, again_wv, again_wo, again_g1, again_wup, again_wdown, again_g2 = (
        again_weights
    )
    residual_grad, grad_g2, grad_s2 = norm_back(
        summary_grad, first_rows(normed_two), first_rows(inverse_two), again_g2
    )
    down_grad = residual_grad.astype(jnp.bfloat16)
    activated_cls = first_rows(activated)
    act_grad = contract(down_grad, again_wdown, 1, 1)
    gelu_value, gelu_pull = jax.vjp(partial(jax.nn.gelu, approximate=False), first_rows(up_pre))
    up_grad = gelu_pull(act_grad)[0].astype(jnp.bfloat16)
    hidden_cls = first_rows(hidden_low)
    hidden_grad = contract(up_grad, again_wup, 1, 1) + residual_grad
    first_grad, grad_g1, grad_s1 = norm_back(
        hidden_grad, first_rows(normed_one), first_rows(inverse_one), again_g1
    )
    attend_grad = first_grad.astype(jnp.bfloat16)
    context_cls = first_rows(context)
    context_grad = (
        contract(attend_grad, again_wo, 1, 1).astype(jnp.bfloat16).reshape(sentences, HEADS, HEAD)
    )
    query_cls = query_heads[:, 0]
    cls_scores = (
        jnp.einsum("bhd,bkhd->bhk", query_cls, key_heads, preferred_element_type=jnp.float32)
        * score_factor
    )
    cls_scores = jnp.where(valid_mask[:, None, :], cls_scores, MASK_FLOOR)
    cls_probs = jnp.exp(cls_scores - row_peak[:, :, 0]) / totals[:, :, 0]
    prob_grad = jnp.einsum(
        "bhd,bkhd->bhk", context_grad, value_heads, preferred_element_type=jnp.float32
    )
    score_grad = (
        cls_probs * (prob_grad - jnp.sum(cls_probs * prob_grad, axis=-1, keepdims=True))
    ).astype(jnp.bfloat16)
    query_grad = (
        (
            jnp.einsum("bhk,bkhd->bhd", score_grad, key_heads, preferred_element_type=jnp.float32)
            * score_factor
        )
        .astype(jnp.bfloat16)
        .reshape(sentences, model_width)
    )
    key_grad = (
        (
            jnp.einsum("bhk,bhd->bkhd", score_grad, query_cls, preferred_element_type=jnp.float32)
            * score_factor
        )
        .astype(jnp.bfloat16)
        .reshape(tokens, model_width)
    )
    value_grad = (
        jnp.einsum(
            "bhk,bhd->bkhd",
            cls_probs.astype(jnp.bfloat16),
            context_grad,
            preferred_element_type=jnp.float32,
        )
        .astype(jnp.bfloat16)
        .reshape(tokens, model_width)
    )
    embedded_cls = first_rows(embedded)
    grad_wkey = contract(embedded, key_grad, 0, 0)
    grad_wvalue = contract(embedded, value_grad, 0, 0)
    grad_bvalue = jnp.sum(value_grad, axis=0, dtype=jnp.float32)
    row_grads = contract(key_grad, again_wk, 1, 1) + contract(value_grad, again_wv, 1, 1)
    summary_extra = contract(query_grad, again_wq, 1, 1) + first_grad
    row_grads = (
        row_grads.reshape(sentences, length, model_width)
        .at[:, 0]
        .add(summary_extra)
        .reshape(tokens, model_width)
    )
    outgoing = jnp.zeros((owners * capacity, model_width), jnp.float32).at[slot_of].set(row_grads)
    incoming = lax.all_to_all(
        lax.all_to_all(
            outgoing.reshape(dp_count, fsdp_count, capacity, model_width).astype(jnp.bfloat16),
            "dp",
            split_axis=0,
            concat_axis=0,
            tiled=True,
        ),
        "fsdp",
        split_axis=1,
        concat_axis=1,
        tiled=True,
    ).astype(jnp.float32)
    incoming = jnp.where(
        present.reshape(owners * capacity)[:, None],
        incoming.reshape(owners * capacity, model_width),
        0.0,
    )
    table_grad = (
        jnp.zeros((vocab_rows, model_width), jnp.float32)
        .at[local_rows.reshape(owners * capacity)]
        .add(incoming)
    )
    grad_wquery = contract(embedded_cls, query_grad, 0, 0)
    grad_bquery = jnp.sum(query_grad, axis=0, dtype=jnp.float32)
    grad_wout = contract(context_cls, attend_grad, 0, 0)
    grad_bout = jnp.sum(attend_grad, axis=0, dtype=jnp.float32)
    grad_wup = contract(hidden_cls, up_grad, 0, 0)
    grad_bup = jnp.sum(up_grad, axis=0, dtype=jnp.float32)
    grad_wdown = contract(activated_cls, down_grad, 0, 0)
    grad_bdown = jnp.sum(down_grad, axis=0, dtype=jnp.float32)
    owned_grads = (
        lax.psum_scatter(
            grad_wquery.astype(jnp.bfloat16), "fsdp", scatter_dimension=0, tiled=True
        ).astype(jnp.float32),
        lax.psum_scatter(
            grad_bquery.astype(jnp.bfloat16), "fsdp", scatter_dimension=0, tiled=True
        ).astype(jnp.float32),
        lax.psum_scatter(
            grad_wkey.astype(jnp.bfloat16), "fsdp", scatter_dimension=0, tiled=True
        ).astype(jnp.float32),
        lax.psum_scatter(
            grad_wvalue.astype(jnp.bfloat16), "fsdp", scatter_dimension=0, tiled=True
        ).astype(jnp.float32),
        lax.psum_scatter(
            grad_bvalue.astype(jnp.bfloat16), "fsdp", scatter_dimension=0, tiled=True
        ).astype(jnp.float32),
        lax.psum_scatter(
            grad_wout.astype(jnp.bfloat16), "fsdp", scatter_dimension=0, tiled=True
        ).astype(jnp.float32),
        lax.psum_scatter(
            grad_bout.astype(jnp.bfloat16), "fsdp", scatter_dimension=0, tiled=True
        ).astype(jnp.float32),
        lax.psum_scatter(
            grad_g1.astype(jnp.bfloat16), "fsdp", scatter_dimension=0, tiled=True
        ).astype(jnp.float32),
        lax.psum_scatter(
            grad_s1.astype(jnp.bfloat16), "fsdp", scatter_dimension=0, tiled=True
        ).astype(jnp.float32),
        lax.psum_scatter(
            grad_wup.astype(jnp.bfloat16), "fsdp", scatter_dimension=0, tiled=True
        ).astype(jnp.float32),
        lax.psum_scatter(
            grad_bup.astype(jnp.bfloat16), "fsdp", scatter_dimension=0, tiled=True
        ).astype(jnp.float32),
        lax.psum_scatter(
            grad_wdown.astype(jnp.bfloat16), "fsdp", scatter_dimension=0, tiled=True
        ).astype(jnp.float32),
        lax.psum_scatter(
            grad_bdown.astype(jnp.bfloat16), "fsdp", scatter_dimension=0, tiled=True
        ).astype(jnp.float32),
        lax.psum_scatter(
            grad_g2.astype(jnp.bfloat16), "fsdp", scatter_dimension=0, tiled=True
        ).astype(jnp.float32),
        lax.psum_scatter(
            grad_s2.astype(jnp.bfloat16), "fsdp", scatter_dimension=0, tiled=True
        ).astype(jnp.float32),
    )
    summed = (
        lax.psum(owned_grads[0].astype(jnp.bfloat16), "dp").astype(jnp.float32),
        lax.psum(owned_grads[1].astype(jnp.bfloat16), "dp").astype(jnp.float32),
        lax.psum(owned_grads[2].astype(jnp.bfloat16), "dp").astype(jnp.float32),
        lax.psum(owned_grads[3].astype(jnp.bfloat16), "dp").astype(jnp.float32),
        lax.psum(owned_grads[4].astype(jnp.bfloat16), "dp").astype(jnp.float32),
        lax.psum(owned_grads[5].astype(jnp.bfloat16), "dp").astype(jnp.float32),
        lax.psum(owned_grads[6].astype(jnp.bfloat16), "dp").astype(jnp.float32),
        lax.psum(owned_grads[7].astype(jnp.bfloat16), "dp").astype(jnp.float32),
        lax.psum(owned_grads[8].astype(jnp.bfloat16), "dp").astype(jnp.float32),
        lax.psum(owned_grads[9].astype(jnp.bfloat16), "dp").astype(jnp.float32),
        lax.psum(owned_grads[10].astype(jnp.bfloat16), "dp").astype(jnp.float32),
        lax.psum(owned_grads[11].astype(jnp.bfloat16), "dp").astype(jnp.float32),
        lax.psum(owned_grads[12].astype(jnp.bfloat16), "dp").astype(jnp.float32),
        lax.psum(owned_grads[13].astype(jnp.bfloat16), "dp").astype(jnp.float32),
        lax.psum(owned_grads[14].astype(jnp.bfloat16), "dp").astype(jnp.float32),
    )
    return (
        layer_out,
        loss_value,
        table_grad,
        summed[0],
        summed[1],
        summed[2],
        summed[3],
        summed[4],
        summed[5],
        summed[6],
        summed[7],
        summed[8],
        summed[9],
        summed[10],
        summed[11],
        summed[12],
        summed[13],
        summed[14],
    )


CORES = 2
PLANES = 4
LINES = 4
CHIPS = PLANES * LINES
DEVICES = CORES * CHIPS
CAPACITY = 48
GROUPS = 3
PAD = 16
TOKENS = 768
WIDTH = 768
WIDE = 3072
VOCAB_ROWS = 1024
PAIR_ROWS = HEADS * PAD
SLOT_ROWS = DEVICES * PAD
LONG = 64
BLOCK = 256
MESH = pl.DeviceIdType.MESH
LOW = jnp.bfloat16
FULL = jnp.float32
VMEM_LIMIT = 62 * 1024 * 1024

INPUTS = ["table", "token_ids", "lens", "slots", "langs"]
INPUTS += ["wq", "bq", "wk", "wv", "bv", "wo", "bo", "g1", "s1", "wup", "bup", "wdown", "bdown"]
INPUTS += ["g2", "s2"]
OUTPUTS = ["layer_out", "table_grad", "g_wq", "g_wk", "g_wv", "g_wo", "g_wup", "g_wdown"]
OUTPUTS += ["g_small", "loss"]


def place():
    core = lax.axis_index("dp")
    chip = lax.axis_index("fsdp")
    along_x = chip + 1 - 2 * (chip % 2)
    along_y = chip + 2 - 4 * ((chip // 2) % 2)
    first = along_x + core * (along_y - along_x)
    second = along_y + core * (along_x - along_y)
    return core, chip, first, second


def greet():
    core, chip, _, _ = place()
    me = core * CHIPS + chip
    barrier = pltpu.get_barrier_semaphore()

    def signal(step):
        other = lax.rem(me + step, DEVICES)
        pl.semaphore_signal(
            barrier,
            inc=1,
            device_id=(lax.div(other, CHIPS), lax.rem(other, CHIPS)),
            device_id_type=MESH,
        )

    every(1, DEVICES, signal)


def enter():
    pl.semaphore_wait(pltpu.get_barrier_semaphore(), DEVICES - 1)


def remote(source, target, send_sem, recv_sem, core, chip):
    return pltpu.make_async_remote_copy(
        src_ref=source,
        dst_ref=target,
        send_sem=send_sem,
        recv_sem=recv_sem,
        device_id=(core, chip),
        device_id_type=MESH,
    )


def every(start, stop, act):
    def step(index, carry):
        act(index)
        return carry

    lax.fori_loop(start, stop, step, 0)


def weight_steps(piece, many, send, recv):
    core, chip, first, second = place()
    plane, line = chip // LINES, chip % LINES
    line_first, line_second = first % LINES, second % LINES
    line_far = line_first + line_second - line
    is_low, is_high = plane > 0, plane < PLANES - 1

    def copy(send_index, recv_index, at, to_core, to_chip, carried=core):
        part = piece(at, carried)
        return remote(part, part, send.at[send_index], recv.at[recv_index], to_core, to_chip)

    def up(at_plane):
        return copy(at_plane, at_plane, at_plane * LINES + line, core, chip + LINES)

    def down(at_plane, index):
        return copy(index, at_plane, at_plane * LINES + line, core, chip - LINES)

    def side(at_plane, base, at_line, target):
        return copy(5, base + at_plane, at_plane * LINES + at_line, core, target)

    def across(at_plane, at_line):
        return copy(6, 17, at_plane * LINES + at_line, 1 - core, chip)

    def all_of(count, send_index, recv_index):
        part = many(count)
        return remote(part, part, send.at[send_index], recv.at[recv_index], 1 - core, chip)

    def begin():
        pl.when(is_high)(lambda: up(plane).start())
        pl.when(is_low)(lambda: down(plane, PLANES).start())
        side(plane, 5, line, first).start()
        side(plane, 9, line, second).start()

    def at_distance(distance, act):
        if distance == 0:
            act(plane, None)
            return
        pl.when(plane >= distance)(lambda: act(plane - distance, True))
        pl.when(plane + distance < PLANES)(lambda: act(plane + distance, False))

    def chain(distance):
        def act(at_plane, from_low):
            if from_low:
                up(at_plane).wait_recv()
                pl.when(is_high)(lambda: up(at_plane).start())
            else:
                down(at_plane, at_plane).wait_recv()
                pl.when(is_low)(lambda: down(at_plane, at_plane).start())
            side(at_plane, 5, line, first).start()
            side(at_plane, 9, line, second).start()
            across(at_plane, line).start()

        return partial(at_distance, distance, act)

    def near(distance):
        def act(at_plane, from_low):
            side(at_plane, 5, line_first, first).wait_recv()
            side(at_plane, 13, line_first, second).start()
            across(at_plane, line_first).start()

        return partial(at_distance, distance, act)

    def far(distance):
        def act(at_plane, from_low):
            side(at_plane, 9, line_second, second).wait_recv()
            across(at_plane, line_second).start()
            side(at_plane, 13, line_far, second).wait_recv()
            across(at_plane, line_far).start()

        return partial(at_distance, distance, act)

    def finish():
        all_of(15, 6, 17).wait_recv()

    def drain():
        def sent(index):
            copy(index, index, chip, 1 - core, chip).wait_send()

        for at_plane in range(PLANES):
            pl.when((plane >= at_plane) & is_high)(partial(sent, at_plane))
            pl.when((plane < at_plane) & is_low)(partial(sent, at_plane))
        pl.when(is_low)(partial(sent, PLANES))
        all_of(12, 5, 17).wait_send()
        all_of(15, 6, 17).wait_send()

    moves = [chain(1), near(0), chain(2), near(1), chain(3), far(0)]
    moves += [near(2), far(1), near(3), far(2), far(3)]
    return begin, moves, finish, drain


def gather_steps(buffer, send, recv):
    core, chip, first, second = place()
    plane, line = chip // LINES, chip % LINES
    line_first, line_second = first % LINES, second % LINES
    line_far = line_first + line_second - line
    half = buffer.shape[-1] // 2
    columns = pl.ds(pl.multiple_of(core * half, 128), half)
    others = pl.ds(pl.multiple_of((1 - core) * half, 128), half)

    def copy(index, part, to_core, to_chip):
        return remote(part, part, send.at[index], recv.at[index], to_core, to_chip)

    def own(at):
        return buffer.at[at, plane, line]

    def chip_part(at_plane, at_line, which):
        return buffer.at[:, at_plane, at_line, :, which]

    def line_part(at_line, which):
        return buffer.at[:, :, at_line, :, which]

    def start():
        copy(0, own(core), 1 - core, chip).start()

    def planes():
        copy(0, own(1 - core), 1 - core, chip).wait_recv()
        for step in range(1, PLANES):
            part = chip_part(plane, line, columns)
            copy(step, part, core, (chip + LINES * step) % CHIPS).start()

    def sides():
        for step in range(1, PLANES):
            part = chip_part((plane + PLANES - step) % PLANES, line, columns)
            copy(step, part, core, chip).wait_recv()
        copy(4, line_part(line, columns), core, first).start()
        copy(5, line_part(line, columns), core, second).start()
        for step in range(1, PLANES):
            part = chip_part((plane + PLANES - step) % PLANES, line, columns)
            copy(6 + step, part, 1 - core, chip).start()

    def corner():
        copy(4, line_part(line_first, columns), core, first).wait_recv()
        copy(6, line_part(line_first, columns), core, second).start()
        copy(10, line_part(line_first, columns), 1 - core, chip).start()
        copy(5, line_part(line_second, columns), core, second).wait_recv()
        copy(11, line_part(line_second, columns), 1 - core, chip).start()

    def last():
        copy(6, line_part(line_far, columns), core, second).wait_recv()
        copy(12, line_part(line_far, columns), 1 - core, chip).start()

    def finish():
        for step in range(1, PLANES):
            part = chip_part((plane + PLANES - step) % PLANES, line, others)
            copy(6 + step, part, 1 - core, chip).wait_recv()
        copy(10, line_part(line_second, others), 1 - core, chip).wait_recv()
        copy(11, line_part(line_first, others), 1 - core, chip).wait_recv()
        copy(12, line_part(line_far, others), 1 - core, chip).wait_recv()

    def drain():
        copy(0, own(core), 1 - core, chip).wait_send()
        for index in [1, 2, 3, 7, 8, 9]:
            copy(index, chip_part(plane, line, columns), 1 - core, chip).wait_send()
        for index in [4, 5, 6, 10, 11, 12]:
            copy(index, line_part(line, columns), 1 - core, chip).wait_send()

    return [start, planes, sides, corner, last, finish], drain


def iota(shape, axis):
    return lax.broadcasted_iota(jnp.int32, shape, axis)


def over(numbers, power):
    return lax.shift_right_arithmetic(numbers, jnp.full_like(numbers, power.bit_length() - 1))


def within(numbers, power):
    return numbers & (power - 1)


def as_column(row):
    parts = []
    for start in range(0, row.shape[1], 128):
        tile = jnp.broadcast_to(row[:, start : start + 128], (128, 128))
        parts.append(jnp.transpose(tile)[:, 0:1])
    return jnp.concatenate(parts, axis=0)


def as_row(column):
    parts = []
    for start in range(0, column.shape[0], 128):
        tile = jnp.broadcast_to(column[start : start + 128, :], (128, 128))
        parts.append(jnp.transpose(tile)[0:1, :])
    return jnp.concatenate(parts, axis=1)


def dot(left_side, right_side):
    return contract(left_side, right_side, 1, 0)


def dot_turned(left_side, right_side):
    return contract(left_side, right_side, 1, 1)


def norm_parts(inputs):
    centered = inputs - jnp.mean(inputs, axis=-1, keepdims=True)
    inverse = lax.rsqrt(jnp.mean(centered * centered, axis=-1, keepdims=True) + EPSILON)
    return centered * inverse, inverse


def norm_back_parts(grad_output, normed, inverse, ln_gain):
    grad_normed = grad_output * ln_gain
    first_term = jnp.mean(grad_normed, axis=-1, keepdims=True)
    second_term = jnp.mean(grad_normed * normed, axis=-1, keepdims=True)
    return (
        inverse * (grad_normed - first_term - normed * second_term),
        jnp.sum(grad_output * normed, axis=0, keepdims=True),
        jnp.sum(grad_output, axis=0, keepdims=True),
    )


def erf_parts(inputs):
    decay = jnp.exp(-0.5 * inputs * inputs)
    share = 1.0 / (1.0 + jnp.abs(inputs) * (0.3275911 * 0.5**0.5))
    terms = [1.061405429, -1.453152027, 1.421413741, -0.284496736, 0.254829592]
    series = 0.5 * terms[0]
    for term in terms[1:]:
        series = series * share + 0.5 * term
    tail = series * share * decay
    return jnp.where(inputs >= 0.0, 1.0 - tail, tail), decay


def gelu_parts(inputs):
    below, decay = erf_parts(inputs)
    return inputs * below, below + inputs * decay * ((2.0 * 3.141592653589793) ** -0.5)


def gelu(inputs):
    return inputs * erf_parts(inputs)[0]


def layer_kernel(names, *refs):
    r = SimpleNamespace(**dict(zip(names, refs, strict=True)))
    core, chip, _, _ = place()
    me = core * CHIPS + chip
    here = (core, chip // LINES, chip % LINES)
    scale = HEAD ** (-0.5)
    depth, deep = WIDTH // CHIPS, WIDE // CHIPS
    sentences = TOKENS // LONG

    for j in range(TOKENS // 128):
        r.ids[j : j + 1, :] = jnp.concatenate(
            [r.token_ids[2 * j : 2 * j + 1, :], r.token_ids[2 * j + 1 : 2 * j + 2, :]], axis=1
        )
    r.ids[TOKENS // 128 : 8, :] = jnp.zeros((8 - TOKENS // 128, 128), jnp.int32)
    greet()
    ahead = (iota((TOKENS, TOKENS), 0) < iota((TOKENS, TOKENS), 1)).astype(LOW)
    r.embedded[...] = ahead
    mine = pl.ds(pl.multiple_of(chip * depth, 16), depth)
    for index, shard in enumerate([r.wq, r.wk, r.wv, r.wo]):
        r.wa[mine, index * WIDTH : (index + 1) * WIDTH] = shard[...]
    r.wb[mine, :] = r.wup[...]
    r.wc[pl.ds(pl.multiple_of(chip * deep, 16), deep), :] = r.wdown[...]
    r.every_ids[me] = r.ids[...]
    enter()

    def peer(step):
        other = lax.rem(me + step, DEVICES)
        return other, lax.div(other, CHIPS), lax.rem(other, CHIPS)

    def ids_copy(step):
        other, to_core, to_chip = peer(step)
        return remote(r.ids, r.every_ids.at[me], r.one_send.at[0], r.one_recv.at[0], to_core, to_chip)

    def all_but_one(ref, index):
        part = ref.at[0 : DEVICES - 1]
        return remote(part, part, r.one_send.at[index], r.one_recv.at[index], 1 - core, chip)

    every(1, DEVICES, lambda step: ids_copy(step).start())

    def block(ref, rows, columns):
        def piece(at, carried):
            return ref.at[
                pl.ds(pl.multiple_of(at * rows, 16), rows),
                pl.ds(pl.multiple_of(carried * columns, 128), columns),
            ]

        def many(count):
            return ref.at[0 : count * rows, 0:columns]

        return piece, many

    begin_a, moves_a, finish_a, drain_a = weight_steps(
        *block(r.wa, depth, 2 * WIDTH), r.weight_send.at[0], r.weight_recv.at[0]
    )
    begin_b, moves_b, finish_b, drain_b = weight_steps(
        *block(r.wb, depth, WIDE // 2), r.weight_send.at[1], r.weight_recv.at[1]
    )
    begin_c, moves_c, finish_c, drain_c = weight_steps(
        *block(r.wc, deep, WIDTH // 2), r.weight_send.at[2], r.weight_recv.at[2]
    )
    begin_a()
    begin_b()

    def move(*steps):
        for moves, first_step in steps:
            moves[first_step]()
            moves[first_step + 1]()

    all_but_one(r.every_ids, 0).wait_recv()
    all_ids = jnp.concatenate([r.every_ids[:, j, :] for j in range(TOKENS // 128)], axis=1)
    all_owner = over(all_ids, VOCAB_ROWS)
    asked = all_owner == me
    ranks = dot(asked.astype(LOW), r.embedded[...])
    r.rank[...] = jnp.where(asked, ranks, -1.0)
    local_row = (all_ids - all_owner * VOCAB_ROWS + 1).astype(FULL)
    r.code[...] = local_row + (over(iota((DEVICES, TOKENS), 1), LONG) * 2048).astype(FULL)

    quarter_size = DEVICES // 4

    def rows_copy(other, quarter):
        return remote(
            r.rows.at[:, pl.ds(pl.multiple_of(other * PAD, 16), PAD), :],
            r.replies.at[:, pl.ds(pl.multiple_of(me * PAD, 16), PAD), :],
            r.rows_send.at[quarter],
            r.rows_recv.at[quarter],
            lax.div(other, CHIPS),
            lax.rem(other, CHIPS),
        )

    def rows_of(quarter):
        count = quarter_size - 1 if quarter == 3 else quarter_size
        part = r.replies.at[:, 0 : count * PAD, :]
        return remote(
            part, part, r.rows_send.at[quarter], r.rows_recv.at[quarter], 1 - core, chip
        )

    def pick(source):
        rank = r.rank[pl.ds(source, 1), :]
        code = r.code[pl.ds(source, 1), :]
        here_at = iota((CAPACITY, TOKENS), 0).astype(FULL) == rank
        found = jnp.sum(jnp.where(here_at, code, 0.0), axis=1, keepdims=True)
        sent = jnp.floor(found * (1.0 / 2048))
        row = found - sent * 2048.0 - 1.0
        chosen = (iota((CAPACITY, VOCAB_ROWS), 1).astype(FULL) == row).astype(LOW)
        at = pl.ds(pl.multiple_of(source * PAD, 16), PAD)
        source_sent = sent + (source * PAD).astype(FULL)
        for group in range(GROUPS):
            part = slice(group * PAD, (group + 1) * PAD)
            r.chosen[group, at, :] = chosen[part]
            r.found[group, at, 0:1] = row[part]
            r.found[group, at, 1:2] = source_sent[part]

    def quarter_rows(quarter):
        now = lax.rem(lax.div(me, quarter_size) + 1 + quarter, 4)

        def pick_two(index):
            pick(now * quarter_size + 2 * index)
            pick(now * quarter_size + 2 * index + 1)

        every(0, quarter_size // 2, pick_two)
        span = pl.ds(pl.multiple_of(now * quarter_size * PAD, 128), quarter_size * PAD)
        for start in range(0, WIDTH, BLOCK):
            lanes = slice(start, start + BLOCK)
            picked = r.chosen[:, span, :].reshape(GROUPS * quarter_size * PAD, VOCAB_ROWS)
            found_rows = dot(picked, r.table[:, lanes]).astype(LOW)
            r.rows[:, span, lanes] = found_rows.reshape(GROUPS, quarter_size * PAD, BLOCK)

        def send(index):
            other = now * quarter_size + lax.rem(lax.rem(me, quarter_size) + index, quarter_size)
            rows_copy(other, quarter).start()

        every(lax.div(quarter, 3), quarter_size, send)
        pl.when(quarter == 0)(partial(move, (moves_a, 0)))
        pl.when(quarter == 1)(partial(move, (moves_b, 0)))
        pl.when(quarter == 2)(partial(move, (moves_a, 2)))
        pl.when(quarter == 3)(partial(move, (moves_b, 2)))

    every(0, 4, quarter_rows)
    begin_c()
    own_at = pl.ds(pl.multiple_of(me * PAD, 16), PAD)
    r.replies[:, own_at, :] = r.rows[:, own_at, :]

    move((moves_a, 4))

    small_here = pl.ds(pl.multiple_of(chip * 128, 128), 128)
    lines = [r.bq, r.bv, r.bo, r.g1, r.s1, r.bdown, r.g2, r.s2]
    lines = [line[...].reshape(1, depth).astype(FULL) for line in lines]
    up_line = r.bup[...].reshape(1, deep).astype(FULL)
    lines += [up_line[:, part * depth : (part + 1) * depth] for part in range(deep // depth)]
    lines.append(jnp.zeros((PAD - len(lines), depth), FULL))
    own_small = jnp.concatenate(lines, axis=0)
    own_small = jnp.concatenate([own_small, jnp.zeros((PAD, 128 - depth), FULL)], axis=1)
    r.smalls[:, small_here] = own_small.astype(LOW)

    def small_copy(step):
        part = r.smalls.at[:, small_here]
        to_chip = lax.rem(chip + step, CHIPS)
        return remote(part, part, r.small_send.at[0], r.small_recv.at[0], core, to_chip)

    def all_smalls():
        part = r.smalls.at[:, 0 : (CHIPS - 1) * 128]
        return remote(part, part, r.small_send.at[0], r.small_recv.at[0], 1 - core, chip)

    every(1, CHIPS, lambda step: small_copy(step).start())
    move((moves_b, 4))

    own_row = jnp.concatenate([r.ids[j : j + 1, :] for j in range(TOKENS // 128)], axis=1)
    owner_row = over(own_row, VOCAB_ROWS).astype(FULL)
    owner_col = as_column(owner_row)
    earlier = (owner_row == owner_col) & (iota((TOKENS, TOKENS), 1) < iota((TOKENS, TOKENS), 0))
    own_rank = jnp.sum(earlier.astype(FULL), axis=1, keepdims=True)
    own_group = jnp.floor(own_rank * (1.0 / PAD))
    own_slot = own_group * SLOT_ROWS + owner_col * PAD + (own_rank - own_group * PAD)
    r.slot_col[...] = own_slot
    r.slot_line[0:1, :] = as_row(own_slot)
    move((moves_a, 6), (moves_c, 0))

    at_sent = over(iota((1, TOKENS), 1), LONG)
    lens = jnp.concatenate(
        [r.lens[...].reshape(1, sentences).astype(FULL), jnp.zeros((1, PAD - sentences), FULL)],
        axis=1,
    )
    spread_lens = dot(
        jnp.broadcast_to(lens, (8, PAD)).astype(LOW),
        (iota((PAD, TOKENS), 0) == over(iota((PAD, TOKENS), 1), LONG)).astype(LOW),
    )[0:1]
    valid_row = ((iota((1, TOKENS), 1) - at_sent * LONG).astype(FULL) < spread_lens).astype(FULL)
    r.valid_line[0:1, :] = valid_row
    r.valid_col[...] = as_column(valid_row)
    half_block = BLOCK // 2
    stacked_shape = (4 * half_block, half_block)
    same = within(over(iota(stacked_shape, 0), LONG), 2) == over(iota(stacked_shape, 1), LONG)
    r.block_bias[...] = jnp.where(same, 0.0, MASK_FLOOR)
    r.valid_bias[0:1, :] = (1.0 - valid_row) * MASK_FLOOR

    slots = r.slots[...].reshape(1, DEVICES * sentences)
    gap = jnp.full((1, PAD - sentences), -2, jnp.int32)
    slot_line = jnp.concatenate(
        [
            part
            for device in range(DEVICES)
            for part in (slots[:, device * sentences : (device + 1) * sentences], gap)
        ],
        axis=1,
    )
    side_line = within(slot_line, 2) + jnp.where(slot_line < 0, 8, 0)
    pair_line = over(slot_line, 2)
    pairs = r.langs.shape[0]
    lang_line = r.langs[...].reshape(1, pairs).astype(FULL)
    lang_line = jnp.concatenate([lang_line, jnp.full((1, -pairs % 128), -1.0, FULL)], axis=1)
    lang_col = as_column(lang_line)
    same_lang = jnp.sum(jnp.where(lang_col == lang_line, 1.0, 0.0), axis=1, keepdims=True)
    per_pair = 1.0 / (2.0 * LANGS * same_lang)
    at_pair = iota((lang_line.shape[1], SLOT_ROWS), 0) == pair_line
    weight_line = jnp.sum(jnp.where(at_pair, per_pair, 0.0), axis=0, keepdims=True)
    r.pairs[0:1, :] = weight_line
    r.pairs[1:2, :] = pair_line.astype(FULL)
    r.pairs[2:3, :] = side_line.astype(FULL)
    r.pairs_col[:, 0:1] = as_column(weight_line)
    r.pairs_col[:, 1:2] = as_column(pair_line.astype(FULL))
    r.pairs_col[:, 2:3] = as_column(side_line.astype(FULL))
    move((moves_b, 6), (moves_c, 2))

    all_smalls().wait_recv()
    smalls = r.smalls[...].astype(FULL)
    r.vectors[:, 0:WIDTH] = jnp.concatenate(
        [smalls[:, at * 128 : at * 128 + depth] for at in range(CHIPS)], axis=1
    )
    r.up_bias[0:1, :] = jnp.concatenate(
        [
            smalls[8 + part : 9 + part, at * 128 : at * 128 + depth]
            for at in range(CHIPS)
            for part in range(deep // depth)
        ],
        axis=1,
    )

    def vector(index):
        return r.vectors[index : index + 1, :]

    r.qkv_bias[0:1, 0:WIDTH] = vector(0)
    r.qkv_bias[0:1, WIDTH : 2 * WIDTH] = jnp.zeros((1, WIDTH), FULL)
    r.qkv_bias[0:1, 2 * WIDTH : 3 * WIDTH] = vector(1)

    move((moves_a, 8), (moves_b, 8), (moves_c, 4))

    def first_row(source):
        code = jnp.where(r.rank[pl.ds(source, 1), :] >= 0.0, r.code[pl.ds(source, 1), :], 0.0)
        at_first = iota((PAD, TOKENS), 1) == iota((PAD, TOKENS), 0) * LONG
        found = jnp.sum(jnp.where(at_first, code, 0.0), axis=1, keepdims=True)
        row = found - jnp.floor(found * (1.0 / 2048)) * 2048.0 - 1.0
        r.found[GROUPS, pl.ds(pl.multiple_of(source * PAD, 16), PAD), 0:1] = row

    every(0, DEVICES, first_row)
    for group in range(GROUPS + 1):
        named = as_row(r.found[group, :, 0:1])
        by_row = iota((VOCAB_ROWS, SLOT_ROWS), 0).astype(FULL) == named
        r.by_row[:, group * SLOT_ROWS : (group + 1) * SLOT_ROWS] = by_row.astype(LOW)

    def order(tile):
        at = pl.ds(pl.multiple_of(tile * BLOCK, BLOCK), BLOCK)
        lanes = iota((BLOCK, GROUPS * SLOT_ROWS), 1).astype(FULL)
        r.qkv[at, 0 : GROUPS * SLOT_ROWS] = (r.slot_col[at, :] == lanes).astype(LOW)

    every(0, TOKENS // BLOCK, order)
    for group in range(GROUPS):
        slot_at = iota((SLOT_ROWS, TOKENS), 0) + group * SLOT_ROWS
        named = (slot_at.astype(FULL) == r.slot_line[0:1, :]).astype(LOW)
        r.slot_hot[group] = named
    moves_a[10]()
    moves_b[10]()
    finish_a()
    for quarter in range(4):
        rows_of(quarter).wait_recv()

    def embed(tile):
        at = pl.ds(pl.multiple_of(tile * BLOCK, BLOCK), BLOCK)
        replies = r.replies[:, :, at].reshape(GROUPS * SLOT_ROWS, BLOCK)
        r.embedded[:, at] = dot(r.qkv[:, 0 : GROUPS * SLOT_ROWS], replies).astype(LOW)

    every(0, WIDTH // BLOCK, embed)

    def project(tile):
        at = pl.ds(pl.multiple_of(tile * BLOCK, BLOCK), BLOCK)
        r.qkv[:, at] = (dot(r.embedded[...], r.wa[:, at]) + r.qkv_bias[0:1, at]).astype(LOW)

    move((moves_c, 6))
    every(0, 9, project)

    row_sent = within(iota((PAIR_ROWS, WIDTH), 0), PAD)
    row_head = over(iota((PAIR_ROWS, WIDTH), 0), PAD)
    lane_block = over(iota((PAIR_ROWS, WIDTH), 1), HEAD)
    in_head = row_head == lane_block
    seen = (row_sent == lane_block) & (r.valid_line[0:1, :] > 0.0)
    firsts = (iota((PAD, TOKENS), 1) == iota((PAD, TOKENS), 0) * LONG).astype(LOW)
    real_row = iota((PAD, 1), 0) < sentences

    def spread(rows):
        return jnp.where(in_head, jnp.concatenate([rows] * HEADS, axis=0), jnp.zeros((), LOW))

    def fold(tall):
        tall = jnp.where(in_head, tall, 0.0)
        return sum(tall[head * PAD : (head + 1) * PAD] for head in range(HEADS))

    keys, values = slice(WIDTH, 2 * WIDTH), slice(2 * WIDTH, 3 * WIDTH)
    embedded_cls = dot(firsts, r.embedded[...]).astype(LOW)
    query_cls = (dot(embedded_cls, r.wa[:, 0:WIDTH]) + vector(0)).astype(LOW)
    cls_scores = dot_turned(spread(query_cls), r.qkv[:, keys]) * scale
    cls_scores = jnp.where(seen, cls_scores, MASK_FLOOR)
    cls_peak = jnp.max(cls_scores, axis=1, keepdims=True)
    cls_exp = jnp.where(seen, jnp.exp(cls_scores - cls_peak), 0.0)
    cls_total = jnp.sum(cls_exp, axis=1, keepdims=True)
    cls_probs = cls_exp / jnp.where(cls_total > 0.0, cls_total, 1.0)
    probs_low = cls_probs.astype(LOW)
    r.probs[...] = cls_probs
    context_cls = fold(dot(probs_low, r.qkv[:, values])).astype(LOW)
    first_cls = (
        embedded_cls.astype(FULL)
        + dot(context_cls, r.wa[:, 3 * WIDTH : 4 * WIDTH])
        + vector(2)
    )
    normed_one, inverse_one = norm_parts(first_cls)
    r.normed_one[...] = normed_one
    hidden_cls = normed_one * vector(3) + vector(4)
    hidden_cls_low = hidden_cls.astype(LOW)
    early_here = r.early.at[here]
    early_here[:, 0:WIDTH] = hidden_cls_low
    early_here[:, WIDTH : 2 * WIDTH] = query_cls
    steps_u, drain_u = gather_steps(r.units, r.gather_send.at[0], r.gather_recv.at[0])
    steps_e, drain_e = gather_steps(r.early, r.gather_send.at[1], r.gather_recv.at[1])
    steps_d, drain_d = gather_steps(r.downs, r.gather_send.at[2], r.gather_recv.at[2])
    steps_a, drain_a2 = gather_steps(r.attends, r.gather_send.at[3], r.gather_recv.at[3])
    steps_q, drain_q = gather_steps(r.queries, r.gather_send.at[4], r.gather_recv.at[4])
    steps_e[0]()

    def attend(unit):
        rows = pl.ds(pl.multiple_of(unit * half_block, half_block), half_block)
        lane_head = over(iota((half_block, BLOCK), 1), HEAD)
        bias = r.block_bias[...] + r.valid_bias[0:1, rows]

        def part(which, lane):
            return r.qkv[rows, which * WIDTH + lane : which * WIDTH + lane + BLOCK]

        for lane in range(0, WIDTH, BLOCK):
            query = part(0, lane) * jnp.asarray(scale, LOW)
            key, value = part(1, lane), part(2, lane)
            stacked = jnp.concatenate(
                [jnp.where(lane_head == head, query, jnp.zeros((), LOW)) for head in range(4)],
                axis=0,
            )
            scores = dot_turned(stacked, key) + bias
            shifted = jnp.exp(scores - jnp.max(scores, axis=1, keepdims=True))
            probs = shifted * (1.0 / jnp.sum(shifted, axis=1, keepdims=True))
            mixed = dot(probs.astype(LOW), value)
            result = mixed[0:half_block]
            for head in range(1, 4):
                result = jnp.where(
                    lane_head == head, mixed[head * half_block : (head + 1) * half_block], result
                )
            r.context[rows, lane : lane + BLOCK] = result.astype(LOW)

    def open_tile(tile):
        at = pl.ds(pl.multiple_of(tile * BLOCK, BLOCK), BLOCK)
        attended = dot(r.context[at, :], r.wa[:, 3 * WIDTH : 4 * WIDTH]) + vector(2)
        normed, _ = norm_parts(r.embedded[at, :].astype(FULL) + attended)
        hidden = normed * vector(3) + vector(4)
        r.context[at, :] = hidden.astype(LOW)
        r.table_full[at, :] = hidden + vector(5)

    most = SLOT_ROWS
    rest_at = pl.ds(most, TOKENS - most)

    def up_product(part):
        at = pl.ds(pl.multiple_of(part * BLOCK, BLOCK), BLOCK)
        return dot(r.context[...], r.wb[:, at]) + r.up_bias[0:1, at]

    def feed_up(part, last=False):
        active = gelu(r.tile_up[...]).astype(LOW)
        if not last:
            r.tile_up[...] = up_product(part + 1)
        lanes = pl.ds(pl.multiple_of(lax.rem(part, 4) * BLOCK, BLOCK), BLOCK)
        r.chosen[lax.div(part, 4), :, lanes] = active[:most]
        rest = pl.ds(pl.multiple_of(lax.div(part, 6) * BLOCK, BLOCK), BLOCK)
        lanes = pl.ds(pl.multiple_of(lax.rem(part, 6) * BLOCK, BLOCK), BLOCK)
        r.slopes[rest, lanes] = active[most:]

    def feed_down(part):
        lanes = pl.ds(pl.multiple_of(part * BLOCK, BLOCK), BLOCK)
        total = r.table_full[0:most, lanes]
        for group in range(GROUPS):
            rows = slice(group * VOCAB_ROWS, (group + 1) * VOCAB_ROWS)
            total = total + dot(r.chosen[group], r.wc[rows, lanes])
        r.table_full[0:most, lanes] = total

    def feed_rest(part):
        lanes = pl.ds(pl.multiple_of(part * BLOCK, BLOCK), BLOCK)
        low_part = dot(r.slopes[0:BLOCK, :], r.wc[0 : WIDE // 2, lanes])
        high_part = dot(r.slopes[BLOCK : 2 * BLOCK, :], r.wc[WIDE // 2 :, lanes])
        r.table_full[rest_at, lanes] += low_part + high_part

    def layer_copy(tile):
        at = pl.ds(pl.multiple_of(tile * BLOCK, BLOCK), BLOCK)
        return pltpu.make_async_copy(r.context.at[at], r.layer_out.at[at], r.out_sem.at[tile])

    def close_tile(tile):
        at = pl.ds(pl.multiple_of(tile * BLOCK, BLOCK), BLOCK)
        normed, _ = norm_parts(r.table_full[at, :])
        out = normed * vector(6) + vector(7)
        r.context[at, :] = (out * r.valid_col[at, :]).astype(LOW)
        layer_copy(tile).start()

    finish_b()
    r.hidden_cls[...] = hidden_cls_low

    def up_part(part):
        at = pl.ds(pl.multiple_of(part * WIDTH, BLOCK), WIDTH)
        active, slope = gelu_parts(dot(r.hidden_cls[...], r.wb[:, at]) + r.up_bias[0:1, at])
        r.active_cls[:, at] = active.astype(LOW)
        r.slope_cls[:, at] = slope

    every(0, WIDE // WIDTH, up_part)
    steps_e[1]()

    def attend_step(unit):
        attend(unit)
        pl.when(unit == 1)(partial(move, (moves_c, 8)))
        pl.when(unit == 3)(moves_c[10])
        pl.when(unit == 4)(steps_e[2])

    every(0, 6, attend_step)
    finish_c()

    def pack_tall(target, first_row, act):
        def run(part):
            window = jnp.minimum(lax.div(part * 2 * depth, 128) * 128, WIDTH - BLOCK)
            shape = (BLOCK, BLOCK)
            lane = within(iota(shape, 1), 128)
            column = over(iota(shape, 1), 128) * depth + lane + (part * 2 * depth - window)
            select = ((iota(shape, 0) == column) & (lane < depth)).astype(LOW)
            taken = dot(r.tall[:, pl.ds(pl.multiple_of(window, 128), BLOCK)], select)

            def beside(low, high):
                return [
                    low[:, one * 128 : (one + 1) * 128]
                    + pltpu.roll(high[:, one * 128 : (one + 1) * 128], depth, 1)
                    for one in range(2)
                ]

            for half in range(CORES):
                base = half * PAIR_ROWS // 2
                both = beside(taken[base : base + 48], taken[base + 48 : base + 96])
                for one in range(2):
                    at = half * CHIPS + 2 * part + one
                    target[at, first_row : first_row + 48, :] = act(
                        2 * part + one, both[one]
                    ).astype(LOW)
            if first_row:
                left = beside(taken[PAIR_ROWS : PAIR_ROWS + PAD], taken[PAIR_ROWS + PAD :])
                for half in range(CORES):
                    for one in range(2):
                        target[half * CHIPS + 2 * part + one, 0:PAD, :] = left[one].astype(LOW)

        return run

    def pack_coefs(coefs):
        shape = (2 * PAIR_ROWS, GROUPS * 128)
        row, lane = iota(shape, 0), iota(shape, 1)
        kind = jnp.where(row >= PAIR_ROWS, PAD, 0)
        head = over(row, PAD) - jnp.where(row >= PAIR_ROWS, HEADS, 0)
        folds = head + kind + over(lane, 128) * 2 * PAD == within(lane, 128)
        lanes = contract(coefs, folds.astype(LOW), 0, 0).astype(LOW)
        total = None
        for group in range(GROUPS):
            part = dot(r.slot_hot[group], lanes[:, group * 128 : (group + 1) * 128])
            total = part if total is None else total + part
        return total.astype(LOW).reshape(DEVICES, PAD, 128)


    def down_part(part):
        at = pl.ds(pl.multiple_of(part * BLOCK, BLOCK), BLOCK)
        r.wide_cls[:, at] = dot(r.active_cls[...], r.wc[:, at])

    every(0, WIDTH // BLOCK, down_part)
    down_pre = r.wide_cls[:, 0:WIDTH] + vector(5)
    normed_two, inverse_two = norm_parts(hidden_cls + down_pre)
    summary = normed_two * vector(6) + vector(7)
    magnitude = jnp.sqrt(jnp.sum(summary * summary, axis=-1, keepdims=True) + EPSILON)
    unit = jnp.where(real_row, summary / magnitude, 0.0)
    r.units[here] = unit.astype(LOW)

    steps_u[0]()
    r.tall[0:PAIR_ROWS, :] = dot(probs_low, r.embedded[...]).astype(LOW)
    r.tall[PAIR_ROWS : PAIR_ROWS + PAD, :] = context_cls
    r.tall[PAIR_ROWS + PAD :, :] = embedded_cls
    pack_one = pack_tall(r.mail_one, PAD, lambda at, both: both)

    def pack_one_step(part):
        pack_one(part)
        pl.when(part == 0)(steps_u[1])
        pl.when(part == 4)(steps_u[2])

    every(0, CHIPS // 2, pack_one_step)
    steps_u[3]()

    def post_one(box, got, index, step):
        other, to_core, to_chip = peer(step)
        remote(
            box.at[other], got.at[me], r.one_send.at[index], r.one_recv.at[index], to_core, to_chip
        ).start()

    r.got_one[me] = r.mail_one[me]

    def open_step(tile):
        open_tile(tile)
        pl.when(tile == 0)(steps_e[3])
        pl.when(tile == 2)(steps_u[4])

    def feed_step(steps, part):
        feed_up(part)
        for index in range(6):
            step = 6 * part + index + 1
            pl.when(step < DEVICES)(partial(post_one, r.mail_one, r.got_one, 1, step))
        for index, step in steps:
            pl.when(part == index)(step)

    first_parts, parts = 6, WIDE // BLOCK
    every(0, TOKENS // BLOCK, open_step)
    r.tile_up[...] = up_product(0)
    every(0, first_parts, partial(feed_step, [(1, steps_u[5]), (2, steps_e[4]), (5, steps_e[5])]))

    units = r.units[...].reshape(SLOT_ROWS, WIDTH)
    weight_row, pair_row, side_row = r.pairs[0:1, :], r.pairs[1:2, :], r.pairs[2:3, :]

    def pair_scores(rows, pair_col, side_col):
        opposite = side_col + side_row == 1.0
        partner = opposite & (pair_col == pair_row)
        raw = SCORE_SCALE * dot_turned(rows, units)
        shifted = jnp.where(partner, raw - SCORE_SCALE * MARGIN_WIDTH, raw)
        return jnp.where(opposite, shifted, MASK_FLOOR), partner

    every_score, every_partner = pair_scores(
        units, r.pairs_col[:, 1:2], r.pairs_col[:, 2:3]
    )
    peak_row = jnp.max(every_score, axis=0, keepdims=True)
    log_row = peak_row + jnp.log(
        jnp.sum(jnp.exp(every_score - peak_row), axis=0, keepdims=True)
    )
    picked_row = jnp.sum(jnp.where(every_partner, every_score, 0.0), axis=0, keepdims=True)
    r.loss[...] = jnp.sum(weight_row * (log_row - picked_row), axis=1, keepdims=True)

    rows_here = pl.ds(pl.multiple_of(me * PAD, 16), PAD)
    own_score, own_partner = pair_scores(
        r.units[here], r.pairs_col[rows_here, 1:2], r.pairs_col[rows_here, 2:3]
    )
    own_partner = own_partner.astype(FULL)
    own_peak = jnp.max(own_score, axis=1, keepdims=True)
    own_exp = jnp.exp(own_score - own_peak)
    own_share = own_exp / jnp.sum(own_exp, axis=1, keepdims=True)
    by_row = (r.pairs_col[rows_here, 0:1] * (own_share - own_partner)).astype(LOW)
    by_column = (weight_row * (jnp.exp(own_score - log_row) - own_partner)).astype(LOW)
    unit_grad = SCORE_SCALE * (dot(by_row, units) + dot(by_column, units))
    along = jnp.sum(unit * unit_grad, axis=-1, keepdims=True)
    summary_grad = (unit_grad - unit * along) / magnitude

    residual_grad, grad_g2, grad_s2 = norm_back_parts(
        summary_grad, normed_two, inverse_two, vector(6)
    )
    down_grad = residual_grad.astype(LOW)
    r.downs[here] = down_grad
    steps_d[0]()
    r.hidden_cls[...] = down_grad

    def up_back(part):
        at = pl.ds(pl.multiple_of(part * WIDTH, BLOCK), WIDTH)
        act_grad = dot_turned(r.hidden_cls[...], r.wc[at, :])
        r.active_cls[:, at] = (act_grad * r.slope_cls[:, at]).astype(LOW)

    every(0, WIDE // WIDTH, up_back)
    steps_d[1]()

    def hidden_back(part):
        at = pl.ds(pl.multiple_of(part * BLOCK, BLOCK), BLOCK)
        r.wide_cls[:, at] = dot_turned(r.active_cls[...], r.wb[at, :])

    every(0, WIDTH // BLOCK, hidden_back)
    hidden_grad = r.wide_cls[:, 0:WIDTH] + residual_grad
    first_grad, grad_g1, grad_s1 = norm_back_parts(
        hidden_grad, r.normed_one[...], inverse_one, vector(3)
    )
    attend_grad = first_grad.astype(LOW)
    context_grad = dot_turned(attend_grad, r.wa[:, 3 * WIDTH : 4 * WIDTH]).astype(LOW)
    attend_here = r.attends.at[here]
    attend_here[:, 0:WIDTH] = attend_grad
    attend_here[:, WIDTH : 2 * WIDTH] = context_grad
    steps_a[0]()
    steps_d[2]()
    context_tall = spread(context_grad)
    probs = r.probs[...]
    prob_grad = dot_turned(context_tall, r.qkv[:, values])
    inner = jnp.sum(probs * prob_grad, axis=1, keepdims=True)
    score_grad = (probs * (prob_grad - inner)).astype(LOW)
    steps_a[1]()
    r.mail_two[:, 48:64, :] = pack_coefs(jnp.concatenate([probs_low, score_grad], axis=0))
    r.got_two[me, 48:64, :] = r.mail_two[me, 48:64, :]
    query_grad = (fold(dot(score_grad, r.qkv[:, keys])) * scale).astype(LOW)
    probs_total = jnp.sum(probs_low.astype(FULL), axis=1, keepdims=True)
    grad_bvalue = jnp.sum(probs_total * context_tall.astype(FULL), axis=0, keepdims=True)
    grad_bquery = jnp.sum(query_grad.astype(FULL), axis=0, keepdims=True)
    r.queries[here] = query_grad
    own_sums = jnp.concatenate(
        [jnp.zeros((2 * depth, WIDTH), FULL)]
        + [grad_bquery, grad_bvalue, grad_g1, grad_s1, grad_g2, grad_s2]
        + [jnp.zeros((128 - 2 * depth - 6, WIDTH), FULL)],
        axis=0,
    )
    r.own_sums[...] = jnp.transpose(own_sums)
    steps_q[0]()
    steps_a[2]()
    r.tall[0:PAIR_ROWS, :] = (dot(score_grad, r.embedded[...]) * scale).astype(LOW)

    def with_sums(at, both):
        return both + r.own_sums[pl.ds(pl.multiple_of(at * depth, 16), depth), :]

    pack_two = pack_tall(r.mail_two, 0, with_sums)

    def send_two(at):
        remote(
            r.mail_two.at[at],
            r.got_two.at[me],
            r.one_send.at[2],
            r.one_recv.at[2],
            lax.div(at, CHIPS),
            lax.rem(at, CHIPS),
        ).start()

    def pack_two_step(step):
        part = lax.rem(step + lax.div(me, 4), CHIPS // 2)
        pack_two(part)
        for index in range(4):
            turn = lax.rem(index + me, 4)
            at = lax.div(turn, 2) * CHIPS + 2 * part + lax.rem(turn, 2)
            pl.when(at != me)(partial(send_two, at))

    every(0, CHIPS // 2, pack_two_step)
    r.got_two[me, 0:48, :] = r.mail_two[me, 0:48, :]
    steps_q[1]()

    def all_rows(buffer, start, width=WIDTH):
        return buffer[:, :, :, :, start : start + width].reshape(SLOT_ROWS, width)

    quarter_rows_count = quarter_size * PAD

    def from_sent(quarter):
        span = pl.ds(pl.multiple_of(quarter * quarter_rows_count, 128), quarter_rows_count)
        shape = (GROUPS * quarter_rows_count, quarter_rows_count)
        lanes = (iota(shape, 1) + quarter * quarter_rows_count).astype(FULL)
        named = r.found[0:GROUPS, span, 1:2].reshape(GROUPS * quarter_rows_count, 1)
        return (named == lanes).astype(LOW), span

    def quarter_part(buffer, quarter, start):
        planes = pl.ds(lax.rem(quarter, 2) * 2, 2)
        part = buffer[lax.div(quarter, 2), planes, :, :, start : start + BLOCK]
        return part.reshape(quarter_rows_count, BLOCK)

    def widened(coefs, group, start, kind):
        lane_head = over(iota((128, BLOCK), 1) + start, HEAD)
        lanes = iota((128, BLOCK), 0) == lane_head + group * 2 * PAD + kind
        return dot(coefs, lanes.astype(LOW))

    half_wide = WIDE // 2

    def slope_tile(part):
        at = pl.ds(pl.multiple_of(core * half_wide + part * BLOCK, BLOCK), BLOCK)
        up_pre = dot(all_rows(r.early, 0), r.wb[:, at]) + r.up_bias[0:1, at]
        _, slope = gelu_parts(up_pre)
        r.slopes[:, pl.ds(pl.multiple_of(part * BLOCK, BLOCK), BLOCK)] = slope.astype(LOW)

    def slot_queries(quarter):
        sents, span = from_sent(quarter)
        for start in range(0, WIDTH, BLOCK):
            rows = dot(sents, quarter_part(r.early, quarter, WIDTH + start)).astype(LOW)
            rows = rows.reshape(GROUPS, quarter_rows_count, BLOCK)
            r.slot_query[:, span, start : start + BLOCK] = rows

    def activate():
        at = pl.ds(pl.multiple_of(chip // 2 * 2 * deep, 128), 2 * deep)
        up_pre = dot(all_rows(r.early, 0), r.wb[:, at]) + r.up_bias[0:1, at]
        r.active_turned[...] = jnp.transpose(gelu(up_pre)).astype(LOW)
        r.hidden_turned[...] = jnp.transpose(all_rows(r.early, 0))

    rest = [steps_d[3], steps_a[3], steps_q[2], steps_d[4], steps_a[4]]
    rest = [(first_parts + index, step) for index, step in enumerate(rest)]
    every(first_parts, parts - 1, partial(feed_step, rest))
    feed_up(parts - 1, last=True)

    def rest_step(part):
        feed_rest(part)
        for index, step in enumerate([steps_q[3], steps_d[5], steps_a[5]]):
            pl.when(part == index)(step)

    every(0, WIDTH // BLOCK, rest_step)
    steps_q[4]()

    def down_step(part):
        feed_down(part)
        for index, ends in enumerate([[drain_a, drain_b], [drain_c, drain_u], [drain_e]]):
            for end in ends:
                pl.when(part == index)(end)

    every(0, WIDTH // BLOCK, down_step)
    every(0, TOKENS // BLOCK, close_tile)
    every(0, 4, slot_queries)
    every(0, 6, slope_tile)
    activate()

    all_but_one(r.got_one, 1).wait_recv()
    def slot_probs(group):
        got = r.got_two[:, 48:64, :].reshape(SLOT_ROWS, 128)
        for start in range(0, WIDTH, BLOCK):
            r.replies[group, :, start : start + BLOCK] = widened(got, group, start, 0).astype(LOW)

    def slot_values(quarter):
        sents, span = from_sent(quarter)
        for start in range(0, WIDTH, BLOCK):
            lanes = slice(start, start + BLOCK)
            rows = dot(sents, quarter_part(r.attends, quarter, WIDTH + start))
            rows = rows.reshape(GROUPS, quarter_rows_count, BLOCK)
            rows = r.replies[:, span, lanes].astype(FULL) * rows
            r.replies[:, span, lanes] = rows.astype(LOW)

    def head_products(got, first_row, right, start, target):
        def one_head(head):
            lane = core * (WIDTH // 2) + lax.div(head, 2) * 128
            pair_rows = right[:, :, :, :, pl.ds(pl.multiple_of(start + lane, 128), 128)]
            row = pl.ds(pl.multiple_of(first_row + lax.rem(head, 3) * PAD, 16), PAD)
            block_rows = got[:, row, :].reshape(SLOT_ROWS, 128)
            r.product[...] = contract(block_rows, pair_rows.reshape(SLOT_ROWS, 128), 0, 0)
            part = r.product[pl.ds(pl.multiple_of(lax.div(head, 3) * depth, 16), depth), :]
            at = pl.ds(pl.multiple_of(lane, 128), 128)
            own_lanes = over(iota((depth, 128), 1), HEAD) == lax.rem(head, 2)
            target[:, at] = jnp.where(own_lanes, part, target[:, at])

        every(0, HEADS // 2, one_head)

    def half_of(ref, at_core):
        half = ref.shape[1] // 2
        return ref.at[:, pl.ds(pl.multiple_of(at_core * half, 128), half)]

    def half_copy(index, ref, at_core):
        part = half_of(ref, at_core)
        return remote(part, part, r.half_send.at[index], r.half_recv.at[index], 1 - core, chip)

    own_half = pl.ds(pl.multiple_of(core * (WIDTH // 2), 128), WIDTH // 2)
    r.g_wv[:, own_half] = jnp.zeros((depth, WIDTH // 2), FULL)
    r.g_wk[:, own_half] = jnp.zeros((depth, WIDTH // 2), FULL)
    head_products(r.got_one, PAD, r.attends, WIDTH, r.g_wv)
    half_copy(0, r.g_wv, core).start()

    downs = r.downs[...].reshape(SLOT_ROWS, WIDTH)
    attends = all_rows(r.attends, 0)

    def up_tile(part):
        at = pl.ds(pl.multiple_of(core * half_wide + part * BLOCK, BLOCK), BLOCK)
        slope = r.slopes[:, pl.ds(pl.multiple_of(part * BLOCK, BLOCK), BLOCK)].astype(FULL)
        up_all = (dot_turned(r.downs[...].reshape(SLOT_ROWS, WIDTH), r.wc[at, :]) * slope)
        up_all = up_all.astype(LOW)
        r.g_wup[0:depth, at] = dot(r.hidden_turned[mine, :], up_all)
        total = jnp.sum(up_all.astype(FULL), axis=0, keepdims=True)
        r.g_wup[depth : depth + 8, at] = jnp.broadcast_to(total, (8, BLOCK))

    every(0, half_wide // BLOCK, up_tile)
    half_copy(1, r.g_wup, core).start()
    r.g_wdown[...] = dot(r.active_turned[pl.ds(pl.multiple_of(chip % 2 * deep, 16), deep), :], downs)
    r.left_turned[...] = jnp.transpose(r.got_one[:, 0:PAD, :].reshape(SLOT_ROWS, 128))
    r.g_wo[...] = dot(r.left_turned[0:depth, :], attends)

    def own_part(rows, size):
        start = chip * size
        window = jnp.minimum(lax.div(start, 128) * 128, rows.shape[1] - BLOCK)
        part = rows[:, pl.ds(pl.multiple_of(window, 128), BLOCK)]
        return pltpu.roll(part, lax.rem(BLOCK + window - start, BLOCK), 1)

    for quarter in range(4):
        rows_of(quarter).wait_send()
    all_but_one(r.got_two, 2).wait_recv()
    every(0, GROUPS, slot_probs)
    every(0, 4, slot_values)

    def slot_grads(group):
        got_scores = r.got_two[:, 48:64, :].reshape(SLOT_ROWS, 128)
        for start in range(0, WIDTH, BLOCK):
            lanes = slice(start, start + BLOCK)
            rows = r.slot_query[group, :, lanes].astype(FULL)
            rows = widened(got_scores, group, start, PAD) * rows * scale
            r.slot_query[group, :, lanes] = rows.astype(LOW)
        for start in range(0, WIDTH, BLOCK):
            lanes = slice(start, start + BLOCK)
            row_grad = dot_turned(r.slot_query[group], r.wa[lanes, keys])
            row_grad = row_grad + dot_turned(r.replies[group], r.wa[lanes, values])
            r.rows[group, :, lanes] = row_grad.astype(LOW)

    every(0, GROUPS, slot_grads)
    steps_q[5]()
    query_grads = all_rows(r.queries, 0)
    extra = dot_turned(query_grads, r.wa[:, 0:WIDTH]) + attends.astype(FULL)
    r.extra[...] = extra.astype(LOW)
    r.g_wq[...] = dot(r.left_turned[depth : 2 * depth, :], query_grads)

    half_rows = VOCAB_ROWS // 2

    def table_copy(tile):
        at = pl.ds(pl.multiple_of(tile * half_rows, BLOCK), half_rows)
        return pltpu.make_async_copy(
            r.table_full.at[at], r.table_grad.at[at], r.table_sem.at[tile]
        )

    def table_tile(tile):
        at = pl.ds(pl.multiple_of(tile * half_rows, BLOCK), half_rows)
        for start in range(0, WIDTH, BLOCK):
            lanes = slice(start, start + BLOCK)
            slot_rows = r.rows[:, :, lanes].reshape(GROUPS * SLOT_ROWS, BLOCK)
            r.table_full[at, lanes] = dot(r.by_row[at, 0 : GROUPS * SLOT_ROWS], slot_rows) + dot(
                r.by_row[at, GROUPS * SLOT_ROWS :], r.extra[:, lanes]
            )
        table_copy(tile).start()

    every(0, 2, table_tile)
    head_products(r.got_two, 0, r.early, WIDTH, r.g_wk)
    half_copy(2, r.g_wk, core).start()

    down_total = jnp.sum(downs.astype(FULL), axis=0, keepdims=True)
    attend_total = jnp.sum(attends.astype(FULL), axis=0, keepdims=True)
    sums = jnp.sum(r.got_two[:, 0:48, :].astype(FULL), axis=0)
    sums = jnp.concatenate([sums, jnp.zeros((128 - 48, 128), FULL)], axis=0)
    r.totals[...] = jnp.concatenate([attend_total, down_total, jnp.zeros((6, WIDTH), FULL)], axis=0)
    r.g_small[8:16, :] = own_part(r.totals, depth)
    r.g_small[0:8, 0:128] = jnp.transpose(sums)[2 * depth : 2 * depth + 8, :]
    r.g_small[0:8, 128:BLOCK] = jnp.zeros((8, BLOCK - 128), FULL)
    half_copy(1, r.g_wup, 1 - core).wait_recv()
    r.g_small[16:24, :] = own_part(r.g_wup.at[depth : depth + 8, :], deep)

    half_copy(0, r.g_wv, 1 - core).wait_recv()
    half_copy(2, r.g_wk, 1 - core).wait_recv()
    for index, ref in enumerate([r.g_wv, r.g_wup, r.g_wk]):
        half_copy(index, ref, core).wait_send()

    for index, ref in enumerate([r.every_ids, r.got_one, r.got_two]):
        all_but_one(ref, index).wait_send()
    all_smalls().wait_send()
    for end in [drain_d, drain_a2, drain_q]:
        end()
    every(0, TOKENS // BLOCK, lambda tile: layer_copy(tile).wait())
    every(0, 2, lambda tile: table_copy(tile).wait())


def layer(inputs):
    dma = pltpu.SemaphoreType.DMA
    vmem = pl.BlockSpec(memory_space=pltpu.VMEM)
    anywhere = pl.BlockSpec(memory_space=pl.ANY)
    depth, deep = WIDTH // CHIPS, WIDE // CHIPS

    def gathered(width):
        return pltpu.VMEM((CORES, PLANES, LINES, PAD, width), LOW)

    outputs = dict(
        layer_out=((TOKENS, WIDTH), LOW),
        table_grad=((VOCAB_ROWS, WIDTH), FULL),
        g_wq=((depth, WIDTH), FULL),
        g_wk=((depth, WIDTH), FULL),
        g_wv=((depth, WIDTH), FULL),
        g_wo=((depth, WIDTH), FULL),
        g_wup=((depth + 8, WIDE), FULL),
        g_wdown=((deep, WIDTH), FULL),
        g_small=((24, BLOCK), FULL),
        loss=((1, 1), FULL),
    )
    scratch = dict(
        ids=pltpu.VMEM((8, 128), jnp.int32),
        every_ids=pltpu.VMEM((DEVICES, 8, 128), jnp.int32),
        rank=pltpu.VMEM((DEVICES, TOKENS), FULL),
        code=pltpu.VMEM((DEVICES, TOKENS), FULL),
        found=pltpu.VMEM((GROUPS + 1, SLOT_ROWS, 2), FULL),
        block_bias=pltpu.VMEM((2 * BLOCK, BLOCK // 2), FULL),
        valid_bias=pltpu.VMEM((8, TOKENS), FULL),
        slot_col=pltpu.VMEM((TOKENS, 1), FULL),
        slot_line=pltpu.VMEM((8, TOKENS), FULL),
        valid_col=pltpu.VMEM((TOKENS, 1), FULL),
        valid_line=pltpu.VMEM((8, TOKENS), FULL),
        pairs=pltpu.VMEM((8, SLOT_ROWS), FULL),
        pairs_col=pltpu.VMEM((SLOT_ROWS, 128), FULL),
        vectors=pltpu.VMEM((PAD, WIDTH), FULL),
        up_bias=pltpu.VMEM((8, WIDE), FULL),
        qkv_bias=pltpu.VMEM((8, 3 * WIDTH), FULL),
        smalls=pltpu.VMEM((PAD, CHIPS * 128), LOW),
        wa=pltpu.VMEM((WIDTH, 4 * WIDTH), LOW),
        wb=pltpu.VMEM((WIDTH, WIDE), LOW),
        wc=pltpu.VMEM((WIDE, WIDTH), LOW),
        chosen=pltpu.VMEM((GROUPS, SLOT_ROWS, VOCAB_ROWS), LOW),
        by_row=pltpu.VMEM((VOCAB_ROWS, (GROUPS + 1) * SLOT_ROWS), LOW),
        rows=pltpu.VMEM((GROUPS, SLOT_ROWS, WIDTH), LOW),
        replies=pltpu.VMEM((GROUPS, SLOT_ROWS, WIDTH), LOW),
        slot_query=pltpu.VMEM((GROUPS, SLOT_ROWS, WIDTH), LOW),
        extra=pltpu.VMEM((SLOT_ROWS, WIDTH), LOW),
        hidden_cls=pltpu.VMEM((PAD, WIDTH), LOW),
        active_cls=pltpu.VMEM((PAD, WIDE), LOW),
        slope_cls=pltpu.VMEM((PAD, WIDE), FULL),
        wide_cls=pltpu.VMEM((PAD, WIDTH), FULL),
        tall=pltpu.VMEM((PAIR_ROWS + 2 * PAD, WIDTH), LOW),
        own_sums=pltpu.VMEM((WIDTH, 128), FULL),
        product=pltpu.VMEM((128, 128), FULL),
        slot_hot=pltpu.VMEM((GROUPS, SLOT_ROWS, TOKENS), LOW),
        tile_up=pltpu.VMEM((TOKENS, BLOCK), FULL),
        embedded=pltpu.VMEM((TOKENS, WIDTH), LOW),
        qkv=pltpu.VMEM((TOKENS, 3 * WIDTH), LOW),
        context=pltpu.VMEM((TOKENS, WIDTH), LOW),
        table_full=pltpu.VMEM((VOCAB_ROWS, WIDTH), FULL),
        probs=pltpu.VMEM((PAIR_ROWS, TOKENS), FULL),
        normed_one=pltpu.VMEM((PAD, WIDTH), FULL),
        units=gathered(WIDTH),
        early=gathered(2 * WIDTH),
        downs=gathered(WIDTH),
        attends=gathered(2 * WIDTH),
        queries=gathered(WIDTH),
        slopes=pltpu.VMEM((SLOT_ROWS, WIDE // 2), LOW),
        hidden_turned=pltpu.VMEM((WIDTH, SLOT_ROWS), LOW),
        active_turned=pltpu.VMEM((2 * deep, SLOT_ROWS), LOW),
        left_turned=pltpu.VMEM((128, SLOT_ROWS), LOW),
        totals=pltpu.VMEM((8, WIDTH), FULL),
        mail_one=pltpu.VMEM((DEVICES, 64, 128), LOW),
        got_one=pltpu.VMEM((DEVICES, 64, 128), LOW),
        mail_two=pltpu.VMEM((DEVICES, 64, 128), LOW),
        got_two=pltpu.VMEM((DEVICES, 64, 128), LOW),
        rows_send=dma((4,)),
        rows_recv=dma((4,)),
        one_send=dma((4,)),
        one_recv=dma((4,)),
        small_send=dma((1,)),
        small_recv=dma((1,)),
        weight_send=dma((3, 7)),
        weight_recv=dma((3, 18)),
        gather_send=dma((5, 13)),
        gather_recv=dma((5, 13)),
        half_send=dma((3,)),
        half_recv=dma((3,)),
        out_sem=dma((TOKENS // BLOCK,)),
        table_sem=dma((2,)),
    )
    names = INPUTS + OUTPUTS + list(scratch)
    return pl.pallas_call(
        partial(layer_kernel, names),
        out_shape=tuple(jax.ShapeDtypeStruct(*outputs[name]) for name in OUTPUTS),
        in_specs=[vmem] * len(INPUTS),
        out_specs=(anywhere, anywhere) + (vmem,) * (len(OUTPUTS) - 2),
        scratch_shapes=list(scratch.values()),
        compiler_params=pltpu.CompilerParams(
            collective_id=0, has_side_effects=True, vmem_limit_bytes=VMEM_LIMIT
        ),
        name="layer",
    )(*inputs)


def finish_kernel(count, *refs):
    large, (small, loss), outs = refs[:count], refs[count : count + 2], refs[count + 2 : -1]
    sems = refs[-1]
    copies = []
    for index, (source, target) in enumerate(zip(large, outs)):
        part = source if source.shape == target.shape else source.at[: target.shape[0]]
        copies.append(pltpu.make_async_copy(part, target, sems.at[index]))
        copies[-1].start()
    for row, target in zip([0, 1, 8, 2, 3, 16, 9, 4, 5], outs[count : count + 9]):
        size = target.shape[0]
        target[...] = small[row : row + 1, 0:size].reshape(size)
    outs[-1][...] = loss[...].reshape(1)
    for one in copies:
        one.wait()


def finish(results):
    vmem = pl.BlockSpec(memory_space=pltpu.VMEM)
    anywhere = pl.BlockSpec(memory_space=pl.ANY)
    depth, deep = WIDTH // CHIPS, WIDE // CHIPS
    count = len(results) - 2
    shapes = [(one.shape, one.dtype) for one in results[:count]]
    shapes[6] = ((depth, WIDE), FULL)
    shapes += [((depth,), FULL)] * 5 + [((deep,), FULL)] + [((depth,), FULL)] * 3
    shapes.append(((1,), FULL))
    return pl.pallas_call(
        partial(finish_kernel, count),
        out_shape=tuple(jax.ShapeDtypeStruct(*one) for one in shapes),
        in_specs=[vmem] * (count + 2),
        out_specs=(anywhere,) * count + (vmem,) * 10,
        scratch_shapes=[pltpu.SemaphoreType.DMA((count,))],
        name="finish",
    )(*results)


def block_body(
    table,
    token_ids,
    sent_lengths,
    pair_slot,
    pair_lang,
    *parameters,
):
    results = finish(layer((table, token_ids, sent_lengths, pair_slot, pair_lang) + parameters))
    layer_out, table_grad, g_wq, g_wk, g_wv, g_wo, g_wup, g_wdown = results[:8]
    g_bq, g_bv, g_bo, g_g1, g_s1, g_bup, g_bdown, g_g2, g_s2, loss = results[8:]
    return (
        layer_out.reshape(token_ids.shape + (WIDTH,)),
        loss.reshape(()),
        table_grad,
        g_wq,
        g_bq,
        g_wk,
        g_wv,
        g_bv,
        g_wo,
        g_bo,
        g_g1,
        g_s1,
        g_wup,
        g_bup,
        g_wdown,
        g_bdown,
        g_g2,
        g_s2,
    )


def solution(mesh):
    in_specs = (
        P(("dp", "fsdp"), None),
        P(("dp", "fsdp"), None),
        P(("dp", "fsdp")),
        P(),
        P(),
        P("fsdp", None),
        P("fsdp"),
        P("fsdp", None),
        P("fsdp", None),
        P("fsdp"),
        P("fsdp", None),
        P("fsdp"),
        P("fsdp"),
        P("fsdp"),
        P("fsdp", None),
        P("fsdp"),
        P("fsdp", None),
        P("fsdp"),
        P("fsdp"),
        P("fsdp"),
    )
    out_specs = (
        P(("dp", "fsdp"), None, None),
        P(),
        P(("dp", "fsdp"), None),
        P("fsdp", None),
        P("fsdp"),
        P("fsdp", None),
        P("fsdp", None),
        P("fsdp"),
        P("fsdp", None),
        P("fsdp"),
        P("fsdp"),
        P("fsdp"),
        P("fsdp", None),
        P("fsdp"),
        P("fsdp", None),
        P("fsdp"),
        P("fsdp"),
        P("fsdp"),
    )
    sizes = dict(mesh.shape)
    body = general_body
    if sizes["dp"] == CORES and sizes["fsdp"] == CHIPS:
        body = block_body
    return jax.shard_map(body, mesh=mesh, in_specs=in_specs, out_specs=out_specs, check_vma=False)
```

```python
from functools import partial
from types import SimpleNamespace

import jax
import jax.numpy as jnp
from jax import lax
from jax.experimental import pallas as pl
from jax.experimental.pallas import tpu as pltpu
from jax.sharding import PartitionSpec as P

HEADS = 12
HEAD = 64
LANGS = 109


EPSILON = 1e-06
SCORE_SCALE = 50.0
MARGIN_WIDTH = 0.3
MASK_FLOOR = -1000000000.0


def contract(left_side, right_side, left_dim, right_dim):
    return lax.dot_general(
        left_side,
        right_side,
        (((left_dim,), (right_dim,)), ((), ())),
        preferred_element_type=jnp.float32,
    )


def norm_rows(inputs, ln_gain, ln_shift):
    row_mean = jnp.mean(inputs, axis=-1, keepdims=True)
    centered = inputs - row_mean
    variance = jnp.mean(centered * centered, axis=-1, keepdims=True)
    inverse = lax.rsqrt(variance + EPSILON)
    normed = centered * inverse
    return (normed * ln_gain + ln_shift, normed, inverse)


def norm_back(grad_output, normed, inverse, ln_gain):
    grad_normed = grad_output * ln_gain
    first_term = jnp.mean(grad_normed, axis=-1, keepdims=True)
    second_term = jnp.mean(grad_normed * normed, axis=-1, keepdims=True)
    grad_input = inverse * (grad_normed - first_term - normed * second_term)
    return (grad_input, jnp.sum(grad_output * normed, axis=0), jnp.sum(grad_output, axis=0))


def general_body(
    table,
    token_ids,
    sent_lengths,
    pair_slot,
    pair_lang,
    w_query,
    b_query,
    w_key,
    w_value,
    b_value,
    w_out,
    b_out,
    ln1_gain,
    ln1_bias,
    w_up,
    b_up,
    w_down,
    b_down,
    ln2_gain,
    ln2_bias,
):
    sentences, length = token_ids.shape
    tokens = sentences * length
    vocab_rows, model_width = table.shape
    owners = lax.axis_size(("dp", "fsdp"))
    dp_count = lax.axis_size("dp")
    fsdp_count = lax.axis_size("fsdp")
    capacity = max(2, 2 * tokens // owners)
    device = lax.axis_index(("dp", "fsdp"))
    score_factor = HEAD ** (-0.5)
    flat_ids = token_ids.reshape(tokens)
    owner_of = flat_ids // vocab_rows
    member = (owner_of[:, None] == jnp.arange(owners, dtype=jnp.int32)[None, :]).astype(jnp.int32)
    owner_rank = jnp.sum(jnp.cumsum(member, axis=0) * member, axis=1) - 1
    slot_of = owner_of * capacity + owner_rank
    requests = jnp.full((owners * capacity,), -1, jnp.int32).at[slot_of].set(flat_ids)
    received = lax.all_to_all(
        lax.all_to_all(
            requests.reshape(dp_count, fsdp_count, capacity),
            "dp",
            split_axis=0,
            concat_axis=0,
            tiled=True,
        ),
        "fsdp",
        split_axis=1,
        concat_axis=1,
        tiled=True,
    )
    present = received >= 0
    local_rows = jnp.where(present, received - device * vocab_rows, 0)
    found_rows = jnp.where(present[..., None], table[local_rows], jnp.zeros((), table.dtype))
    replies = lax.all_to_all(
        lax.all_to_all(found_rows, "dp", split_axis=0, concat_axis=0, tiled=True),
        "fsdp",
        split_axis=1,
        concat_axis=1,
        tiled=True,
    )
    embedded = replies.reshape(owners * capacity, model_width)[slot_of]
    gathered = (
        lax.all_gather(w_query, "fsdp", axis=0, tiled=True),
        lax.all_gather(b_query, "fsdp", axis=0, tiled=True),
        lax.all_gather(w_key, "fsdp", axis=0, tiled=True),
        lax.all_gather(w_value, "fsdp", axis=0, tiled=True),
        lax.all_gather(b_value, "fsdp", axis=0, tiled=True),
        lax.all_gather(w_out, "fsdp", axis=0, tiled=True),
        lax.all_gather(b_out, "fsdp", axis=0, tiled=True),
        lax.all_gather(ln1_gain, "fsdp", axis=0, tiled=True),
        lax.all_gather(ln1_bias, "fsdp", axis=0, tiled=True),
        lax.all_gather(w_up, "fsdp", axis=0, tiled=True),
        lax.all_gather(b_up, "fsdp", axis=0, tiled=True),
        lax.all_gather(w_down, "fsdp", axis=0, tiled=True),
        lax.all_gather(b_down, "fsdp", axis=0, tiled=True),
        lax.all_gather(ln2_gain, "fsdp", axis=0, tiled=True),
        lax.all_gather(ln2_bias, "fsdp", axis=0, tiled=True),
    )
    (
        full_wq,
        full_bq,
        full_wk,
        full_wv,
        full_bv,
        full_wo,
        full_bo,
        full_g1,
        full_s1,
        full_wup,
        full_bup,
        full_wdown,
        full_bdown,
        full_g2,
        full_s2,
    ) = gathered
    valid_mask = jnp.arange(length, dtype=jnp.int32)[None, :] < sent_lengths[:, None]
    head_shape = (sentences, length, HEADS, HEAD)
    queries = (jnp.dot(embedded, full_wq, preferred_element_type=jnp.float32) + full_bq).astype(
        jnp.bfloat16
    )
    key_heads = (
        jnp.dot(embedded, full_wk, preferred_element_type=jnp.float32)
        .astype(jnp.bfloat16)
        .reshape(head_shape)
    )
    value_heads = (
        (jnp.dot(embedded, full_wv, preferred_element_type=jnp.float32) + full_bv)
        .astype(jnp.bfloat16)
        .reshape(head_shape)
    )
    query_heads = queries.reshape(head_shape)
    scores = (
        jnp.einsum("bqhd,bkhd->bhqk", query_heads, key_heads, preferred_element_type=jnp.float32)
        * score_factor
    )
    scores = jnp.where(valid_mask[:, None, None, :], scores, MASK_FLOOR)
    row_peak = jnp.max(scores, axis=-1, keepdims=True)
    shifted = jnp.exp(scores - row_peak)
    totals = jnp.sum(shifted, axis=-1, keepdims=True)
    attn_probs = (shifted / totals).astype(jnp.bfloat16)
    context = jnp.einsum(
        "bhqk,bkhd->bqhd", attn_probs, value_heads, preferred_element_type=jnp.float32
    )
    context = context.reshape(tokens, model_width).astype(jnp.bfloat16)
    attended = jnp.dot(context, full_wo, preferred_element_type=jnp.float32) + full_bo
    hidden, normed_one, inverse_one = norm_rows(
        embedded.astype(jnp.float32) + attended, full_g1, full_s1
    )
    hidden_low = hidden.astype(jnp.bfloat16)
    up_pre = jnp.dot(hidden_low, full_wup, preferred_element_type=jnp.float32) + full_bup
    activated = jax.nn.gelu(up_pre, approximate=False).astype(jnp.bfloat16)
    down_pre = jnp.dot(activated, full_wdown, preferred_element_type=jnp.float32) + full_bdown
    normed_out, normed_two, inverse_two = norm_rows(hidden + down_pre, full_g2, full_s2)
    layer_out = jnp.where(valid_mask.reshape(tokens)[:, None], normed_out, 0.0).astype(jnp.bfloat16)
    layer_out = layer_out.reshape(sentences, length, model_width)

    def first_rows(matrix):
        return matrix.reshape(sentences, length, matrix.shape[-1])[:, 0]

    summary = first_rows(normed_out)
    magnitude = jnp.sqrt(jnp.sum(summary * summary, axis=-1, keepdims=True) + EPSILON)
    unit_vector = summary / magnitude
    unit_low = unit_vector.astype(jnp.bfloat16)
    every_unit = lax.all_gather(unit_low, ("dp", "fsdp"), axis=0, tiled=True)
    every_side = pair_slot % 2
    every_pair = pair_slot // 2
    my_slots = lax.dynamic_slice_in_dim(pair_slot, device * sentences, sentences)
    my_side = my_slots % 2
    my_pair = my_slots // 2
    lang_onehot = (pair_lang[:, None] == jnp.arange(LANGS, dtype=jnp.int32)[None, :]).astype(
        jnp.float32
    )
    per_lang = jnp.sum(lang_onehot, axis=0)
    per_pair = 1.0 / (2.0 * LANGS * jnp.sum(lang_onehot * per_lang[None, :], axis=1))
    my_weight = jnp.take(per_pair, my_pair)
    opposite = my_side[:, None] != every_side[None, :]
    partner = opposite & (my_pair[:, None] == every_pair[None, :])
    raw_scores = SCORE_SCALE * contract(unit_low, every_unit, 1, 1)
    pair_scores = jnp.where(partner, raw_scores - SCORE_SCALE * MARGIN_WIDTH, raw_scores)
    pair_scores = jnp.where(opposite, pair_scores, MASK_FLOOR)
    pair_peak = jnp.max(pair_scores, axis=1, keepdims=True)
    pair_exp = jnp.exp(pair_scores - pair_peak)
    pair_total = jnp.sum(pair_exp, axis=1, keepdims=True)
    log_total = pair_peak[:, 0] + jnp.log(pair_total[:, 0])
    picked = jnp.sum(jnp.where(partner, pair_scores, 0.0), axis=1)
    loss_value = lax.psum(jnp.sum(my_weight * (log_total - picked)), ("dp", "fsdp"))
    coefficients = (
        my_weight[:, None] * (pair_exp / pair_total - partner.astype(jnp.float32))
    ).astype(jnp.bfloat16)
    unit_grad = SCORE_SCALE * contract(coefficients, every_unit, 1, 0)
    column_terms = SCORE_SCALE * contract(coefficients, unit_low, 0, 0)
    unit_grad = unit_grad + lax.psum_scatter(
        column_terms, ("dp", "fsdp"), scatter_dimension=0, tiled=True
    )
    along = jnp.sum(unit_vector * unit_grad, axis=-1, keepdims=True)
    summary_grad = (unit_grad - unit_vector * along) / magnitude
    again_weights = (
        lax.all_gather(w_query, "fsdp", axis=0, tiled=True),
        lax.all_gather(w_key, "fsdp", axis=0, tiled=True),
        lax.all_gather(w_value, "fsdp", axis=0, tiled=True),
        lax.all_gather(w_out, "fsdp", axis=0, tiled=True),
        lax.all_gather(ln1_gain, "fsdp", axis=0, tiled=True),
        lax.all_gather(w_up, "fsdp", axis=0, tiled=True),
        lax.all_gather(w_down, "fsdp", axis=0, tiled=True),
        lax.all_gather(ln2_gain, "fsdp", axis=0, tiled=True),
    )
    again_wq, again_wk, again_wv, again_wo, again_g1, again_wup, again_wdown, again_g2 = (
        again_weights
    )
    residual_grad, grad_g2, grad_s2 = norm_back(
        summary_grad, first_rows(normed_two), first_rows(inverse_two), again_g2
    )
    down_grad = residual_grad.astype(jnp.bfloat16)
    activated_cls = first_rows(activated)
    act_grad = contract(down_grad, again_wdown, 1, 1)
    gelu_value, gelu_pull = jax.vjp(partial(jax.nn.gelu, approximate=False), first_rows(up_pre))
    up_grad = gelu_pull(act_grad)[0].astype(jnp.bfloat16)
    hidden_cls = first_rows(hidden_low)
    hidden_grad = contract(up_grad, again_wup, 1, 1) + residual_grad
    first_grad, grad_g1, grad_s1 = norm_back(
        hidden_grad, first_rows(normed_one), first_rows(inverse_one), again_g1
    )
    attend_grad = first_grad.astype(jnp.bfloat16)
    context_cls = first_rows(context)
    context_grad = (
        contract(attend_grad, again_wo, 1, 1).astype(jnp.bfloat16).reshape(sentences, HEADS, HEAD)
    )
    query_cls = query_heads[:, 0]
    cls_scores = (
        jnp.einsum("bhd,bkhd->bhk", query_cls, key_heads, preferred_element_type=jnp.float32)
        * score_factor
    )
    cls_scores = jnp.where(valid_mask[:, None, :], cls_scores, MASK_FLOOR)
    cls_probs = jnp.exp(cls_scores - row_peak[:, :, 0]) / totals[:, :, 0]
    prob_grad = jnp.einsum(
        "bhd,bkhd->bhk", context_grad, value_heads, preferred_element_type=jnp.float32
    )
    score_grad = (
        cls_probs * (prob_grad - jnp.sum(cls_probs * prob_grad, axis=-1, keepdims=True))
    ).astype(jnp.bfloat16)
    query_grad = (
        (
            jnp.einsum("bhk,bkhd->bhd", score_grad, key_heads, preferred_element_type=jnp.float32)
            * score_factor
        )
        .astype(jnp.bfloat16)
        .reshape(sentences, model_width)
    )
    key_grad = (
        (
            jnp.einsum("bhk,bhd->bkhd", score_grad, query_cls, preferred_element_type=jnp.float32)
            * score_factor
        )
        .astype(jnp.bfloat16)
        .reshape(tokens, model_width)
    )
    value_grad = (
        jnp.einsum(
            "bhk,bhd->bkhd",
            cls_probs.astype(jnp.bfloat16),
            context_grad,
            preferred_element_type=jnp.float32,
        )
        .astype(jnp.bfloat16)
        .reshape(tokens, model_width)
    )
    embedded_cls = first_rows(embedded)
    grad_wkey = contract(embedded, key_grad, 0, 0)
    grad_wvalue = contract(embedded, value_grad, 0, 0)
    grad_bvalue = jnp.sum(value_grad, axis=0, dtype=jnp.float32)
    row_grads = contract(key_grad, again_wk, 1, 1) + contract(value_grad, again_wv, 1, 1)
    summary_extra = contract(query_grad, again_wq, 1, 1) + first_grad
    row_grads = (
        row_grads.reshape(sentences, length, model_width)
        .at[:, 0]
        .add(summary_extra)
        .reshape(tokens, model_width)
    )
    outgoing = jnp.zeros((owners * capacity, model_width), jnp.float32).at[slot_of].set(row_grads)
    incoming = lax.all_to_all(
        lax.all_to_all(
            outgoing.reshape(dp_count, fsdp_count, capacity, model_width).astype(jnp.bfloat16),
            "dp",
            split_axis=0,
            concat_axis=0,
            tiled=True,
        ),
        "fsdp",
        split_axis=1,
        concat_axis=1,
        tiled=True,
    ).astype(jnp.float32)
    incoming = jnp.where(
        present.reshape(owners * capacity)[:, None],
        incoming.reshape(owners * capacity, model_width),
        0.0,
    )
    table_grad = (
        jnp.zeros((vocab_rows, model_width), jnp.float32)
        .at[local_rows.reshape(owners * capacity)]
        .add(incoming)
    )
    grad_wquery = contract(embedded_cls, query_grad, 0, 0)
    grad_bquery = jnp.sum(query_grad, axis=0, dtype=jnp.float32)
    grad_wout = contract(context_cls, attend_grad, 0, 0)
    grad_bout = jnp.sum(attend_grad, axis=0, dtype=jnp.float32)
    grad_wup = contract(hidden_cls, up_grad, 0, 0)
    grad_bup = jnp.sum(up_grad, axis=0, dtype=jnp.float32)
    grad_wdown = contract(activated_cls, down_grad, 0, 0)
    grad_bdown = jnp.sum(down_grad, axis=0, dtype=jnp.float32)
    owned_grads = (
        lax.psum_scatter(
            grad_wquery.astype(jnp.bfloat16), "fsdp", scatter_dimension=0, tiled=True
        ).astype(jnp.float32),
        lax.psum_scatter(
            grad_bquery.astype(jnp.bfloat16), "fsdp", scatter_dimension=0, tiled=True
        ).astype(jnp.float32),
        lax.psum_scatter(
            grad_wkey.astype(jnp.bfloat16), "fsdp", scatter_dimension=0, tiled=True
        ).astype(jnp.float32),
        lax.psum_scatter(
            grad_wvalue.astype(jnp.bfloat16), "fsdp", scatter_dimension=0, tiled=True
        ).astype(jnp.float32),
        lax.psum_scatter(
            grad_bvalue.astype(jnp.bfloat16), "fsdp", scatter_dimension=0, tiled=True
        ).astype(jnp.float32),
        lax.psum_scatter(
            grad_wout.astype(jnp.bfloat16), "fsdp", scatter_dimension=0, tiled=True
        ).astype(jnp.float32),
        lax.psum_scatter(
            grad_bout.astype(jnp.bfloat16), "fsdp", scatter_dimension=0, tiled=True
        ).astype(jnp.float32),
        lax.psum_scatter(
            grad_g1.astype(jnp.bfloat16), "fsdp", scatter_dimension=0, tiled=True
        ).astype(jnp.float32),
        lax.psum_scatter(
            grad_s1.astype(jnp.bfloat16), "fsdp", scatter_dimension=0, tiled=True
        ).astype(jnp.float32),
        lax.psum_scatter(
            grad_wup.astype(jnp.bfloat16), "fsdp", scatter_dimension=0, tiled=True
        ).astype(jnp.float32),
        lax.psum_scatter(
            grad_bup.astype(jnp.bfloat16), "fsdp", scatter_dimension=0, tiled=True
        ).astype(jnp.float32),
        lax.psum_scatter(
            grad_wdown.astype(jnp.bfloat16), "fsdp", scatter_dimension=0, tiled=True
        ).astype(jnp.float32),
        lax.psum_scatter(
            grad_bdown.astype(jnp.bfloat16), "fsdp", scatter_dimension=0, tiled=True
        ).astype(jnp.float32),
        lax.psum_scatter(
            grad_g2.astype(jnp.bfloat16), "fsdp", scatter_dimension=0, tiled=True
        ).astype(jnp.float32),
        lax.psum_scatter(
            grad_s2.astype(jnp.bfloat16), "fsdp", scatter_dimension=0, tiled=True
        ).astype(jnp.float32),
    )
    summed = (
        lax.psum(owned_grads[0].astype(jnp.bfloat16), "dp").astype(jnp.float32),
        lax.psum(owned_grads[1].astype(jnp.bfloat16), "dp").astype(jnp.float32),
        lax.psum(owned_grads[2].astype(jnp.bfloat16), "dp").astype(jnp.float32),
        lax.psum(owned_grads[3].astype(jnp.bfloat16), "dp").astype(jnp.float32),
        lax.psum(owned_grads[4].astype(jnp.bfloat16), "dp").astype(jnp.float32),
        lax.psum(owned_grads[5].astype(jnp.bfloat16), "dp").astype(jnp.float32),
        lax.psum(owned_grads[6].astype(jnp.bfloat16), "dp").astype(jnp.float32),
        lax.psum(owned_grads[7].astype(jnp.bfloat16), "dp").astype(jnp.float32),
        lax.psum(owned_grads[8].astype(jnp.bfloat16), "dp").astype(jnp.float32),
        lax.psum(owned_grads[9].astype(jnp.bfloat16), "dp").astype(jnp.float32),
        lax.psum(owned_grads[10].astype(jnp.bfloat16), "dp").astype(jnp.float32),
        lax.psum(owned_grads[11].astype(jnp.bfloat16), "dp").astype(jnp.float32),
        lax.psum(owned_grads[12].astype(jnp.bfloat16), "dp").astype(jnp.float32),
        lax.psum(owned_grads[13].astype(jnp.bfloat16), "dp").astype(jnp.float32),
        lax.psum(owned_grads[14].astype(jnp.bfloat16), "dp").astype(jnp.float32),
    )
    return (
        layer_out,
        loss_value,
        table_grad,
        summed[0],
        summed[1],
        summed[2],
        summed[3],
        summed[4],
        summed[5],
        summed[6],
        summed[7],
        summed[8],
        summed[9],
        summed[10],
        summed[11],
        summed[12],
        summed[13],
        summed[14],
    )


CORES = 2
PLANES = 4
LINES = 4
CHIPS = PLANES * LINES
DEVICES = CORES * CHIPS
CAPACITY = 48
GROUPS = 3
PAD = 16
TOKENS = 768
WIDTH = 768
WIDE = 3072
VOCAB_ROWS = 1024
PAIR_ROWS = HEADS * PAD
SLOT_ROWS = DEVICES * PAD
LONG = 64
BLOCK = 256
MESH = pl.DeviceIdType.MESH
LOW = jnp.bfloat16
FULL = jnp.float32
VMEM_LIMIT = 62 * 1024 * 1024

INPUTS = ["table", "token_ids", "lens", "slots", "langs"]
INPUTS += ["wq", "bq", "wk", "wv", "bv", "wo", "bo", "g1", "s1", "wup", "bup", "wdown", "bdown"]
INPUTS += ["g2", "s2"]
OUTPUTS = ["layer_out", "table_grad", "g_wq", "g_wk", "g_wv", "g_wo", "g_wup", "g_wdown"]
OUTPUTS += ["g_small", "loss"]


def place():
    core = lax.axis_index("dp")
    chip = lax.axis_index("fsdp")
    along_x = chip + 1 - 2 * (chip % 2)
    along_y = chip + 2 - 4 * ((chip // 2) % 2)
    first = along_x + core * (along_y - along_x)
    second = along_y + core * (along_x - along_y)
    return core, chip, first, second


def greet():
    core, chip, _, _ = place()
    me = core * CHIPS + chip
    barrier = pltpu.get_barrier_semaphore()

    def signal(step):
        other = lax.rem(me + step, DEVICES)
        pl.semaphore_signal(
            barrier,
            inc=1,
            device_id=(lax.div(other, CHIPS), lax.rem(other, CHIPS)),
            device_id_type=MESH,
        )

    every(1, DEVICES, signal)


def enter():
    pl.semaphore_wait(pltpu.get_barrier_semaphore(), DEVICES - 1)


def remote(source, target, send_sem, recv_sem, core, chip):
    return pltpu.make_async_remote_copy(
        src_ref=source,
        dst_ref=target,
        send_sem=send_sem,
        recv_sem=recv_sem,
        device_id=(core, chip),
        device_id_type=MESH,
    )


def every(start, stop, act):
    def step(index, carry):
        act(index)
        return carry

    lax.fori_loop(start, stop, step, 0)


def weight_steps(piece, many, send, recv):
    core, chip, first, second = place()
    plane, line = chip // LINES, chip % LINES
    line_first, line_second = first % LINES, second % LINES
    line_far = line_first + line_second - line
    is_low, is_high = plane > 0, plane < PLANES - 1

    def copy(send_index, recv_index, at, to_core, to_chip, carried=core):
        part = piece(at, carried)
        return remote(part, part, send.at[send_index], recv.at[recv_index], to_core, to_chip)

    def up(at_plane):
        return copy(at_plane, at_plane, at_plane * LINES + line, core, chip + LINES)

    def down(at_plane, index):
        return copy(index, at_plane, at_plane * LINES + line, core, chip - LINES)

    def side(at_plane, base, at_line, target):
        return copy(5, base + at_plane, at_plane * LINES + at_line, core, target)

    def across(at_plane, at_line):
        return copy(6, 17, at_plane * LINES + at_line, 1 - core, chip)

    def all_of(count, send_index, recv_index):
        part = many(count)
        return remote(part, part, send.at[send_index], recv.at[recv_index], 1 - core, chip)

    def begin():
        pl.when(is_high)(lambda: up(plane).start())
        pl.when(is_low)(lambda: down(plane, PLANES).start())
        side(plane, 5, line, first).start()
        side(plane, 9, line, second).start()

    def at_distance(distance, act):
        if distance == 0:
            act(plane, None)
            return
        pl.when(plane >= distance)(lambda: act(plane - distance, True))
        pl.when(plane + distance < PLANES)(lambda: act(plane + distance, False))

    def chain(distance):
        def act(at_plane, from_low):
            if from_low:
                up(at_plane).wait_recv()
                pl.when(is_high)(lambda: up(at_plane).start())
            else:
                down(at_plane, at_plane).wait_recv()
                pl.when(is_low)(lambda: down(at_plane, at_plane).start())
            side(at_plane, 5, line, first).start()
            side(at_plane, 9, line, second).start()
            across(at_plane, line).start()

        return partial(at_distance, distance, act)

    def near(distance):
        def act(at_plane, from_low):
            side(at_plane, 5, line_first, first).wait_recv()
            side(at_plane, 13, line_first, second).start()
            across(at_plane, line_first).start()

        return partial(at_distance, distance, act)

    def far(distance):
        def act(at_plane, from_low):
            side(at_plane, 9, line_second, second).wait_recv()
            across(at_plane, line_second).start()
            side(at_plane, 13, line_far, second).wait_recv()
            across(at_plane, line_far).start()

        return partial(at_distance, distance, act)

    def finish():
        all_of(15, 6, 17).wait_recv()

    def drain():
        def sent(index):
            copy(index, index, chip, 1 - core, chip).wait_send()

        for at_plane in range(PLANES):
            pl.when((plane >= at_plane) & is_high)(partial(sent, at_plane))
            pl.when((plane < at_plane) & is_low)(partial(sent, at_plane))
        pl.when(is_low)(partial(sent, PLANES))
        all_of(12, 5, 17).wait_send()
        all_of(15, 6, 17).wait_send()

    moves = [chain(1), near(0), chain(2), near(1), chain(3), far(0)]
    moves += [near(2), far(1), near(3), far(2), far(3)]
    return begin, moves, finish, drain


def gather_steps(buffer, send, recv):
    core, chip, first, second = place()
    plane, line = chip // LINES, chip % LINES
    line_first, line_second = first % LINES, second % LINES
    line_far = line_first + line_second - line
    half = buffer.shape[-1] // 2
    columns = pl.ds(pl.multiple_of(core * half, 128), half)
    others = pl.ds(pl.multiple_of((1 - core) * half, 128), half)

    def copy(index, part, to_core, to_chip):
        return remote(part, part, send.at[index], recv.at[index], to_core, to_chip)

    def own(at):
        return buffer.at[at, plane, line]

    def chip_part(at_plane, at_line, which):
        return buffer.at[:, at_plane, at_line, :, which]

    def line_part(at_line, which):
        return buffer.at[:, :, at_line, :, which]

    def start():
        copy(0, own(core), 1 - core, chip).start()

    def planes():
        copy(0, own(1 - core), 1 - core, chip).wait_recv()
        for step in range(1, PLANES):
            part = chip_part(plane, line, columns)
            copy(step, part, core, (chip + LINES * step) % CHIPS).start()

    def sides():
        for step in range(1, PLANES):
            part = chip_part((plane + PLANES - step) % PLANES, line, columns)
            copy(step, part, core, chip).wait_recv()
        copy(4, line_part(line, columns), core, first).start()
        copy(5, line_part(line, columns), core, second).start()
        for step in range(1, PLANES):
            part = chip_part((plane + PLANES - step) % PLANES, line, columns)
            copy(6 + step, part, 1 - core, chip).start()

    def corner():
        copy(4, line_part(line_first, columns), core, first).wait_recv()
        copy(6, line_part(line_first, columns), core, second).start()
        copy(10, line_part(line_first, columns), 1 - core, chip).start()
        copy(5, line_part(line_second, columns), core, second).wait_recv()
        copy(11, line_part(line_second, columns), 1 - core, chip).start()

    def last():
        copy(6, line_part(line_far, columns), core, second).wait_recv()
        copy(12, line_part(line_far, columns), 1 - core, chip).start()

    def finish():
        for step in range(1, PLANES):
            part = chip_part((plane + PLANES - step) % PLANES, line, others)
            copy(6 + step, part, 1 - core, chip).wait_recv()
        copy(10, line_part(line_second, others), 1 - core, chip).wait_recv()
        copy(11, line_part(line_first, others), 1 - core, chip).wait_recv()
        copy(12, line_part(line_far, others), 1 - core, chip).wait_recv()

    def drain():
        copy(0, own(core), 1 - core, chip).wait_send()
        for index in [1, 2, 3, 7, 8, 9]:
            copy(index, chip_part(plane, line, columns), 1 - core, chip).wait_send()
        for index in [4, 5, 6, 10, 11, 12]:
            copy(index, line_part(line, columns), 1 - core, chip).wait_send()

    return [start, planes, sides, corner, last, finish], drain


def iota(shape, axis):
    return lax.broadcasted_iota(jnp.int32, shape, axis)


def over(numbers, power):
    return lax.shift_right_arithmetic(numbers, jnp.full_like(numbers, power.bit_length() - 1))


def within(numbers, power):
    return numbers & (power - 1)


def as_column(row):
    parts = []
    for start in range(0, row.shape[1], 128):
        tile = jnp.broadcast_to(row[:, start : start + 128], (128, 128))
        parts.append(jnp.transpose(tile)[:, 0:1])
    return jnp.concatenate(parts, axis=0)


def as_row(column):
    parts = []
    for start in range(0, column.shape[0], 128):
        tile = jnp.broadcast_to(column[start : start + 128, :], (128, 128))
        parts.append(jnp.transpose(tile)[0:1, :])
    return jnp.concatenate(parts, axis=1)


def dot(left_side, right_side):
    return contract(left_side, right_side, 1, 0)


def dot_turned(left_side, right_side):
    return contract(left_side, right_side, 1, 1)


def norm_parts(inputs):
    centered = inputs - jnp.mean(inputs, axis=-1, keepdims=True)
    inverse = lax.rsqrt(jnp.mean(centered * centered, axis=-1, keepdims=True) + EPSILON)
    return centered * inverse, inverse


def norm_back_parts(grad_output, normed, inverse, ln_gain):
    grad_normed = grad_output * ln_gain
    first_term = jnp.mean(grad_normed, axis=-1, keepdims=True)
    second_term = jnp.mean(grad_normed * normed, axis=-1, keepdims=True)
    return (
        inverse * (grad_normed - first_term - normed * second_term),
        jnp.sum(grad_output * normed, axis=0, keepdims=True),
        jnp.sum(grad_output, axis=0, keepdims=True),
    )


def erf_parts(inputs):
    decay = jnp.exp(-0.5 * inputs * inputs)
    share = 1.0 / (1.0 + jnp.abs(inputs) * (0.3275911 * 0.5**0.5))
    terms = [1.061405429, -1.453152027, 1.421413741, -0.284496736, 0.254829592]
    series = 0.5 * terms[0]
    for term in terms[1:]:
        series = series * share + 0.5 * term
    tail = series * share * decay
    return jnp.where(inputs >= 0.0, 1.0 - tail, tail), decay


def gelu_parts(inputs):
    below, decay = erf_parts(inputs)
    return inputs * below, below + inputs * decay * ((2.0 * 3.141592653589793) ** -0.5)


def gelu(inputs):
    return inputs * erf_parts(inputs)[0]


def layer_kernel(names, *refs):
    r = SimpleNamespace(**dict(zip(names, refs, strict=True)))
    core, chip, _, _ = place()
    me = core * CHIPS + chip
    here = (core, chip // LINES, chip % LINES)
    scale = HEAD ** (-0.5)
    depth, deep = WIDTH // CHIPS, WIDE // CHIPS
    sentences = TOKENS // LONG

    for j in range(TOKENS // 128):
        r.ids[j : j + 1, :] = jnp.concatenate(
            [r.token_ids[2 * j : 2 * j + 1, :], r.token_ids[2 * j + 1 : 2 * j + 2, :]], axis=1
        )
    r.ids[TOKENS // 128 : 8, :] = jnp.zeros((8 - TOKENS // 128, 128), jnp.int32)
    greet()
    ahead = (iota((TOKENS, TOKENS), 0) < iota((TOKENS, TOKENS), 1)).astype(LOW)
    r.embedded[...] = ahead
    mine = pl.ds(pl.multiple_of(chip * depth, 16), depth)
    for index, shard in enumerate([r.wq, r.wk, r.wv, r.wo]):
        r.wa[mine, index * WIDTH : (index + 1) * WIDTH] = shard[...]
    r.wb[mine, :] = r.wup[...]
    r.wc[pl.ds(pl.multiple_of(chip * deep, 16), deep), :] = r.wdown[...]
    r.every_ids[me] = r.ids[...]
    enter()

    def peer(step):
        other = lax.rem(me + step, DEVICES)
        return other, lax.div(other, CHIPS), lax.rem(other, CHIPS)

    def ids_copy(step):
        other, to_core, to_chip = peer(step)
        return remote(r.ids, r.every_ids.at[me], r.one_send.at[0], r.one_recv.at[0], to_core, to_chip)

    def all_but_one(ref, index):
        part = ref.at[0 : DEVICES - 1]
        return remote(part, part, r.one_send.at[index], r.one_recv.at[index], 1 - core, chip)

    every(1, DEVICES, lambda step: ids_copy(step).start())

    def block(ref, rows, columns):
        def piece(at, carried):
            return ref.at[
                pl.ds(pl.multiple_of(at * rows, 16), rows),
                pl.ds(pl.multiple_of(carried * columns, 128), columns),
            ]

        def many(count):
            return ref.at[0 : count * rows, 0:columns]

        return piece, many

    begin_a, moves_a, finish_a, drain_a = weight_steps(
        *block(r.wa, depth, 2 * WIDTH), r.weight_send.at[0], r.weight_recv.at[0]
    )
    begin_b, moves_b, finish_b, drain_b = weight_steps(
        *block(r.wb, depth, WIDE // 2), r.weight_send.at[1], r.weight_recv.at[1]
    )
    begin_c, moves_c, finish_c, drain_c = weight_steps(
        *block(r.wc, deep, WIDTH // 2), r.weight_send.at[2], r.weight_recv.at[2]
    )
    begin_a()
    begin_b()
    begin_c()

    def move(*steps):
        for moves, first_step in steps:
            moves[first_step]()
            moves[first_step + 1]()

    all_but_one(r.every_ids, 0).wait_recv()
    all_ids = jnp.concatenate([r.every_ids[:, j, :] for j in range(TOKENS // 128)], axis=1)
    all_owner = over(all_ids, VOCAB_ROWS)
    asked = all_owner == me
    ranks = dot(asked.astype(LOW), r.embedded[...])
    r.rank[...] = jnp.where(asked, ranks, -1.0)
    local_row = (all_ids - all_owner * VOCAB_ROWS + 1).astype(FULL)
    r.code[...] = local_row + (over(iota((DEVICES, TOKENS), 1), LONG) * 2048).astype(FULL)

    quarter_size = DEVICES // 4

    def rows_copy(other, quarter):
        return remote(
            r.rows.at[:, pl.ds(pl.multiple_of(other * PAD, 16), PAD), :],
            r.replies.at[:, pl.ds(pl.multiple_of(me * PAD, 16), PAD), :],
            r.rows_send.at[quarter],
            r.rows_recv.at[quarter],
            lax.div(other, CHIPS),
            lax.rem(other, CHIPS),
        )

    def rows_of(quarter):
        count = quarter_size - 1 if quarter == 3 else quarter_size
        part = r.replies.at[:, 0 : count * PAD, :]
        return remote(
            part, part, r.rows_send.at[quarter], r.rows_recv.at[quarter], 1 - core, chip
        )

    def pick(source):
        rank = r.rank[pl.ds(source, 1), :]
        code = r.code[pl.ds(source, 1), :]
        here_at = iota((CAPACITY, TOKENS), 0).astype(FULL) == rank
        found = jnp.sum(jnp.where(here_at, code, 0.0), axis=1, keepdims=True)
        sent = jnp.floor(found * (1.0 / 2048))
        row = found - sent * 2048.0 - 1.0
        chosen = (iota((CAPACITY, VOCAB_ROWS), 1).astype(FULL) == row).astype(LOW)
        at = pl.ds(pl.multiple_of(source * PAD, 16), PAD)
        source_sent = sent + (source * PAD).astype(FULL)
        for group in range(GROUPS):
            part = slice(group * PAD, (group + 1) * PAD)
            r.chosen[group, at, :] = chosen[part]
            r.found[group, at, 0:1] = row[part]
            r.found[group, at, 1:2] = source_sent[part]

    def quarter_rows(quarter):
        now = lax.rem(lax.div(me, quarter_size) + 1 + quarter, 4)

        def pick_two(index):
            pick(now * quarter_size + 2 * index)
            pick(now * quarter_size + 2 * index + 1)

        every(0, quarter_size // 2, pick_two)
        span = pl.ds(pl.multiple_of(now * quarter_size * PAD, 128), quarter_size * PAD)
        for start in range(0, WIDTH, BLOCK):
            lanes = slice(start, start + BLOCK)
            picked = r.chosen[:, span, :].reshape(GROUPS * quarter_size * PAD, VOCAB_ROWS)
            found_rows = dot(picked, r.table[:, lanes]).astype(LOW)
            r.rows[:, span, lanes] = found_rows.reshape(GROUPS, quarter_size * PAD, BLOCK)

        def send(index):
            other = now * quarter_size + lax.rem(lax.rem(me, quarter_size) + index, quarter_size)
            rows_copy(other, quarter).start()

        every(lax.div(quarter, 3), quarter_size, send)
        pl.when(quarter == 0)(partial(move, (moves_a, 0)))
        pl.when(quarter == 1)(partial(move, (moves_b, 0)))
        pl.when(quarter == 2)(partial(move, (moves_c, 0)))
        pl.when(quarter == 3)(partial(move, (moves_a, 2)))

    every(0, 4, quarter_rows)
    own_at = pl.ds(pl.multiple_of(me * PAD, 16), PAD)
    r.replies[:, own_at, :] = r.rows[:, own_at, :]

    move((moves_b, 2), (moves_c, 2))

    small_here = pl.ds(pl.multiple_of(chip * 128, 128), 128)
    lines = [r.bq, r.bv, r.bo, r.g1, r.s1, r.bdown, r.g2, r.s2]
    lines = [line[...].reshape(1, depth).astype(FULL) for line in lines]
    up_line = r.bup[...].reshape(1, deep).astype(FULL)
    lines += [up_line[:, part * depth : (part + 1) * depth] for part in range(deep // depth)]
    lines.append(jnp.zeros((PAD - len(lines), depth), FULL))
    own_small = jnp.concatenate(lines, axis=0)
    own_small = jnp.concatenate([own_small, jnp.zeros((PAD, 128 - depth), FULL)], axis=1)
    r.smalls[:, small_here] = own_small.astype(LOW)

    def small_copy(step):
        part = r.smalls.at[:, small_here]
        to_chip = lax.rem(chip + step, CHIPS)
        return remote(part, part, r.small_send.at[0], r.small_recv.at[0], core, to_chip)

    def all_smalls():
        part = r.smalls.at[:, 0 : (CHIPS - 1) * 128]
        return remote(part, part, r.small_send.at[0], r.small_recv.at[0], 1 - core, chip)

    every(1, CHIPS, lambda step: small_copy(step).start())
    move((moves_a, 4))

    own_row = jnp.concatenate([r.ids[j : j + 1, :] for j in range(TOKENS // 128)], axis=1)
    owner_row = over(own_row, VOCAB_ROWS).astype(FULL)
    owner_col = as_column(owner_row)
    earlier = (owner_row == owner_col) & (iota((TOKENS, TOKENS), 1) < iota((TOKENS, TOKENS), 0))
    own_rank = jnp.sum(earlier.astype(FULL), axis=1, keepdims=True)
    own_group = jnp.floor(own_rank * (1.0 / PAD))
    own_slot = own_group * SLOT_ROWS + owner_col * PAD + (own_rank - own_group * PAD)
    r.slot_col[...] = own_slot
    r.slot_line[0:1, :] = as_row(own_slot)
    move((moves_b, 4), (moves_c, 4))

    at_sent = over(iota((1, TOKENS), 1), LONG)
    lens = jnp.concatenate(
        [r.lens[...].reshape(1, sentences).astype(FULL), jnp.zeros((1, PAD - sentences), FULL)],
        axis=1,
    )
    spread_lens = dot(
        jnp.broadcast_to(lens, (8, PAD)).astype(LOW),
        (iota((PAD, TOKENS), 0) == over(iota((PAD, TOKENS), 1), LONG)).astype(LOW),
    )[0:1]
    valid_row = ((iota((1, TOKENS), 1) - at_sent * LONG).astype(FULL) < spread_lens).astype(FULL)
    r.valid_line[0:1, :] = valid_row
    r.valid_col[...] = as_column(valid_row)
    half_block = BLOCK // 2
    stacked_shape = (4 * half_block, half_block)
    same = within(over(iota(stacked_shape, 0), LONG), 2) == over(iota(stacked_shape, 1), LONG)
    r.block_bias[...] = jnp.where(same, 0.0, MASK_FLOOR)
    r.valid_bias[0:1, :] = (1.0 - valid_row) * MASK_FLOOR

    slots = r.slots[...].reshape(1, DEVICES * sentences)
    gap = jnp.full((1, PAD - sentences), -2, jnp.int32)
    slot_line = jnp.concatenate(
        [
            part
            for device in range(DEVICES)
            for part in (slots[:, device * sentences : (device + 1) * sentences], gap)
        ],
        axis=1,
    )
    side_line = within(slot_line, 2) + jnp.where(slot_line < 0, 8, 0)
    pair_line = over(slot_line, 2)
    pairs = r.langs.shape[0]
    lang_line = r.langs[...].reshape(1, pairs).astype(FULL)
    lang_line = jnp.concatenate([lang_line, jnp.full((1, -pairs % 128), -1.0, FULL)], axis=1)
    lang_col = as_column(lang_line)
    same_lang = jnp.sum(jnp.where(lang_col == lang_line, 1.0, 0.0), axis=1, keepdims=True)
    per_pair = 1.0 / (2.0 * LANGS * same_lang)
    at_pair = iota((lang_line.shape[1], SLOT_ROWS), 0) == pair_line
    weight_line = jnp.sum(jnp.where(at_pair, per_pair, 0.0), axis=0, keepdims=True)
    r.pairs[0:1, :] = weight_line
    r.pairs[1:2, :] = pair_line.astype(FULL)
    r.pairs[2:3, :] = side_line.astype(FULL)
    r.pairs_col[:, 0:1] = as_column(weight_line)
    r.pairs_col[:, 1:2] = as_column(pair_line.astype(FULL))
    r.pairs_col[:, 2:3] = as_column(side_line.astype(FULL))
    move((moves_a, 6))

    all_smalls().wait_recv()
    smalls = r.smalls[...].astype(FULL)
    r.vectors[:, 0:WIDTH] = jnp.concatenate(
        [smalls[:, at * 128 : at * 128 + depth] for at in range(CHIPS)], axis=1
    )
    r.up_bias[0:1, :] = jnp.concatenate(
        [
            smalls[8 + part : 9 + part, at * 128 : at * 128 + depth]
            for at in range(CHIPS)
            for part in range(deep // depth)
        ],
        axis=1,
    )

    def vector(index):
        return r.vectors[index : index + 1, :]

    r.qkv_bias[0:1, 0:WIDTH] = vector(0)
    r.qkv_bias[0:1, WIDTH : 2 * WIDTH] = jnp.zeros((1, WIDTH), FULL)
    r.qkv_bias[0:1, 2 * WIDTH : 3 * WIDTH] = vector(1)

    move((moves_b, 6), (moves_c, 6))

    def first_row(source):
        code = jnp.where(r.rank[pl.ds(source, 1), :] >= 0.0, r.code[pl.ds(source, 1), :], 0.0)
        at_first = iota((PAD, TOKENS), 1) == iota((PAD, TOKENS), 0) * LONG
        found = jnp.sum(jnp.where(at_first, code, 0.0), axis=1, keepdims=True)
        row = found - jnp.floor(found * (1.0 / 2048)) * 2048.0 - 1.0
        r.found[GROUPS, pl.ds(pl.multiple_of(source * PAD, 16), PAD), 0:1] = row

    every(0, DEVICES, first_row)
    for group in range(GROUPS + 1):
        named = as_row(r.found[group, :, 0:1])
        by_row = iota((VOCAB_ROWS, SLOT_ROWS), 0).astype(FULL) == named
        r.by_row[:, group * SLOT_ROWS : (group + 1) * SLOT_ROWS] = by_row.astype(LOW)

    def order(tile):
        at = pl.ds(pl.multiple_of(tile * BLOCK, BLOCK), BLOCK)
        lanes = iota((BLOCK, GROUPS * SLOT_ROWS), 1).astype(FULL)
        r.qkv[at, 0 : GROUPS * SLOT_ROWS] = (r.slot_col[at, :] == lanes).astype(LOW)

    every(0, TOKENS // BLOCK, order)
    for group in range(GROUPS):
        slot_at = iota((SLOT_ROWS, TOKENS), 0) + group * SLOT_ROWS
        named = (slot_at.astype(FULL) == r.slot_line[0:1, :]).astype(LOW)
        r.slot_hot[group] = named
    move((moves_a, 8), (moves_b, 8), (moves_c, 8))
    for moves in (moves_a, moves_b, moves_c):
        moves[10]()
    finish_a()
    for quarter in range(4):
        rows_of(quarter).wait_recv()

    def embed(tile):
        at = pl.ds(pl.multiple_of(tile * BLOCK, BLOCK), BLOCK)
        replies = r.replies[:, :, at].reshape(GROUPS * SLOT_ROWS, BLOCK)
        r.embedded[:, at] = dot(r.qkv[:, 0 : GROUPS * SLOT_ROWS], replies).astype(LOW)

    every(0, WIDTH // BLOCK, embed)

    def project(tile):
        at = pl.ds(pl.multiple_of(tile * BLOCK, BLOCK), BLOCK)
        r.qkv[:, at] = (dot(r.embedded[...], r.wa[:, at]) + r.qkv_bias[0:1, at]).astype(LOW)

    every(0, 9, project)

    row_sent = within(iota((PAIR_ROWS, WIDTH), 0), PAD)
    row_head = over(iota((PAIR_ROWS, WIDTH), 0), PAD)
    lane_block = over(iota((PAIR_ROWS, WIDTH), 1), HEAD)
    in_head = row_head == lane_block
    seen = (row_sent == lane_block) & (r.valid_line[0:1, :] > 0.0)
    firsts = (iota((PAD, TOKENS), 1) == iota((PAD, TOKENS), 0) * LONG).astype(LOW)
    real_row = iota((PAD, 1), 0) < sentences

    def spread(rows):
        return jnp.where(in_head, jnp.concatenate([rows] * HEADS, axis=0), jnp.zeros((), LOW))

    def fold(tall):
        tall = jnp.where(in_head, tall, 0.0)
        return sum(tall[head * PAD : (head + 1) * PAD] for head in range(HEADS))

    keys, values = slice(WIDTH, 2 * WIDTH), slice(2 * WIDTH, 3 * WIDTH)
    embedded_cls = dot(firsts, r.embedded[...]).astype(LOW)
    query_cls = (dot(embedded_cls, r.wa[:, 0:WIDTH]) + vector(0)).astype(LOW)
    cls_scores = dot_turned(spread(query_cls), r.qkv[:, keys]) * scale
    cls_scores = jnp.where(seen, cls_scores, MASK_FLOOR)
    cls_peak = jnp.max(cls_scores, axis=1, keepdims=True)
    cls_exp = jnp.where(seen, jnp.exp(cls_scores - cls_peak), 0.0)
    cls_total = jnp.sum(cls_exp, axis=1, keepdims=True)
    cls_probs = cls_exp / jnp.where(cls_total > 0.0, cls_total, 1.0)
    probs_low = cls_probs.astype(LOW)
    r.probs[...] = cls_probs
    context_cls = fold(dot(probs_low, r.qkv[:, values])).astype(LOW)
    first_cls = (
        embedded_cls.astype(FULL)
        + dot(context_cls, r.wa[:, 3 * WIDTH : 4 * WIDTH])
        + vector(2)
    )
    normed_one, inverse_one = norm_parts(first_cls)
    r.normed_one[...] = normed_one
    hidden_cls = normed_one * vector(3) + vector(4)
    hidden_cls_low = hidden_cls.astype(LOW)
    early_here = r.early.at[here]
    early_here[:, 0:WIDTH] = hidden_cls_low
    early_here[:, WIDTH : 2 * WIDTH] = query_cls
    steps_u, drain_u = gather_steps(r.units, r.gather_send.at[0], r.gather_recv.at[0])
    steps_e, drain_e = gather_steps(r.early, r.gather_send.at[1], r.gather_recv.at[1])
    steps_d, drain_d = gather_steps(r.downs, r.gather_send.at[2], r.gather_recv.at[2])
    steps_a, drain_a2 = gather_steps(r.attends, r.gather_send.at[3], r.gather_recv.at[3])
    steps_q, drain_q = gather_steps(r.queries, r.gather_send.at[4], r.gather_recv.at[4])
    steps_e[0]()

    def attend(unit):
        rows = pl.ds(pl.multiple_of(unit * half_block, half_block), half_block)
        lane_head = over(iota((half_block, BLOCK), 1), HEAD)
        bias = r.block_bias[...] + r.valid_bias[0:1, rows]

        def part(which, lane):
            return r.qkv[rows, which * WIDTH + lane : which * WIDTH + lane + BLOCK]

        for lane in range(0, WIDTH, BLOCK):
            query = part(0, lane) * jnp.asarray(scale, LOW)
            key, value = part(1, lane), part(2, lane)
            stacked = jnp.concatenate(
                [jnp.where(lane_head == head, query, jnp.zeros((), LOW)) for head in range(4)],
                axis=0,
            )
            scores = dot_turned(stacked, key) + bias
            shifted = jnp.exp(scores - jnp.max(scores, axis=1, keepdims=True))
            probs = shifted * (1.0 / jnp.sum(shifted, axis=1, keepdims=True))
            mixed = dot(probs.astype(LOW), value)
            result = mixed[0:half_block]
            for head in range(1, 4):
                result = jnp.where(
                    lane_head == head, mixed[head * half_block : (head + 1) * half_block], result
                )
            r.context[rows, lane : lane + BLOCK] = result.astype(LOW)

    def open_tile(tile):
        at = pl.ds(pl.multiple_of(tile * BLOCK, BLOCK), BLOCK)
        attended = dot(r.context[at, :], r.wa[:, 3 * WIDTH : 4 * WIDTH]) + vector(2)
        normed, _ = norm_parts(r.embedded[at, :].astype(FULL) + attended)
        hidden = normed * vector(3) + vector(4)
        r.context[at, :] = hidden.astype(LOW)
        r.table_full[at, :] = hidden + vector(5)

    most = SLOT_ROWS
    rest_at = pl.ds(most, TOKENS - most)

    def up_product(part):
        at = pl.ds(pl.multiple_of(part * BLOCK, BLOCK), BLOCK)
        return dot(r.context[...], r.wb[:, at]) + r.up_bias[0:1, at]

    def feed_up(part, last=False):
        active = gelu(r.tile_up[...]).astype(LOW)
        if not last:
            r.tile_up[...] = up_product(part + 1)
        lanes = pl.ds(pl.multiple_of(lax.rem(part, 4) * BLOCK, BLOCK), BLOCK)
        r.chosen[lax.div(part, 4), :, lanes] = active[:most]
        rest = pl.ds(pl.multiple_of(lax.div(part, 6) * BLOCK, BLOCK), BLOCK)
        lanes = pl.ds(pl.multiple_of(lax.rem(part, 6) * BLOCK, BLOCK), BLOCK)
        r.slopes[rest, lanes] = active[most:]

    def feed_down(part):
        lanes = pl.ds(pl.multiple_of(part * BLOCK, BLOCK), BLOCK)
        total = r.table_full[0:most, lanes]
        for group in range(GROUPS):
            rows = slice(group * VOCAB_ROWS, (group + 1) * VOCAB_ROWS)
            total = total + dot(r.chosen[group], r.wc[rows, lanes])
        r.table_full[0:most, lanes] = total

    def feed_rest(part):
        lanes = pl.ds(pl.multiple_of(part * BLOCK, BLOCK), BLOCK)
        low_part = dot(r.slopes[0:BLOCK, :], r.wc[0 : WIDE // 2, lanes])
        high_part = dot(r.slopes[BLOCK : 2 * BLOCK, :], r.wc[WIDE // 2 :, lanes])
        r.table_full[rest_at, lanes] += low_part + high_part

    def layer_copy(tile):
        at = pl.ds(pl.multiple_of(tile * BLOCK, BLOCK), BLOCK)
        return pltpu.make_async_copy(r.context.at[at], r.layer_out.at[at], r.out_sem.at[tile])

    def close_tile(tile):
        at = pl.ds(pl.multiple_of(tile * BLOCK, BLOCK), BLOCK)
        normed, _ = norm_parts(r.table_full[at, :])
        out = normed * vector(6) + vector(7)
        r.context[at, :] = (out * r.valid_col[at, :]).astype(LOW)
        layer_copy(tile).start()

    finish_b()
    r.hidden_cls[...] = hidden_cls_low

    def up_part(part):
        at = pl.ds(pl.multiple_of(part * WIDTH, BLOCK), WIDTH)
        active, slope = gelu_parts(dot(r.hidden_cls[...], r.wb[:, at]) + r.up_bias[0:1, at])
        r.active_cls[:, at] = active.astype(LOW)
        r.slope_cls[:, at] = slope

    every(0, WIDE // WIDTH, up_part)
    steps_e[1]()

    finish_c()

    def pack_tall(target, first_row, act):
        def run(part):
            window = jnp.minimum(lax.div(part * 2 * depth, 128) * 128, WIDTH - BLOCK)
            shape = (BLOCK, BLOCK)
            lane = within(iota(shape, 1), 128)
            column = over(iota(shape, 1), 128) * depth + lane + (part * 2 * depth - window)
            select = ((iota(shape, 0) == column) & (lane < depth)).astype(LOW)
            taken = dot(r.tall[:, pl.ds(pl.multiple_of(window, 128), BLOCK)], select)

            def beside(low, high):
                return [
                    low[:, one * 128 : (one + 1) * 128]
                    + pltpu.roll(high[:, one * 128 : (one + 1) * 128], depth, 1)
                    for one in range(2)
                ]

            for half in range(CORES):
                base = half * PAIR_ROWS // 2
                both = beside(taken[base : base + 48], taken[base + 48 : base + 96])
                for one in range(2):
                    at = half * CHIPS + 2 * part + one
                    target[at, first_row : first_row + 48, :] = act(
                        2 * part + one, both[one]
                    ).astype(LOW)
            if first_row:
                left = beside(taken[PAIR_ROWS : PAIR_ROWS + PAD], taken[PAIR_ROWS + PAD :])
                for half in range(CORES):
                    for one in range(2):
                        target[half * CHIPS + 2 * part + one, 0:PAD, :] = left[one].astype(LOW)

        return run

    def pack_coefs(coefs):
        shape = (2 * PAIR_ROWS, GROUPS * 128)
        row, lane = iota(shape, 0), iota(shape, 1)
        kind = jnp.where(row >= PAIR_ROWS, PAD, 0)
        head = over(row, PAD) - jnp.where(row >= PAIR_ROWS, HEADS, 0)
        folds = head + kind + over(lane, 128) * 2 * PAD == within(lane, 128)
        lanes = contract(coefs, folds.astype(LOW), 0, 0).astype(LOW)
        total = None
        for group in range(GROUPS):
            part = dot(r.slot_hot[group], lanes[:, group * 128 : (group + 1) * 128])
            total = part if total is None else total + part
        return total.astype(LOW).reshape(DEVICES, PAD, 128)


    def down_part(part):
        at = pl.ds(pl.multiple_of(part * BLOCK, BLOCK), BLOCK)
        r.wide_cls[:, at] = dot(r.active_cls[...], r.wc[:, at])

    every(0, WIDTH // BLOCK, down_part)
    down_pre = r.wide_cls[:, 0:WIDTH] + vector(5)
    normed_two, inverse_two = norm_parts(hidden_cls + down_pre)
    summary = normed_two * vector(6) + vector(7)
    magnitude = jnp.sqrt(jnp.sum(summary * summary, axis=-1, keepdims=True) + EPSILON)
    unit = jnp.where(real_row, summary / magnitude, 0.0)
    r.units[here] = unit.astype(LOW)

    steps_u[0]()
    r.tall[0:PAIR_ROWS, :] = dot(probs_low, r.embedded[...]).astype(LOW)
    r.tall[PAIR_ROWS : PAIR_ROWS + PAD, :] = context_cls
    r.tall[PAIR_ROWS + PAD :, :] = embedded_cls
    pack_one = pack_tall(r.mail_one, PAD, lambda at, both: both)

    def pack_one_step(part):
        pack_one(part)
        pl.when(part == 0)(steps_u[1])
        pl.when(part == 4)(steps_u[2])

    every(0, CHIPS // 2, pack_one_step)
    steps_u[3]()

    def post_one(box, got, index, step):
        other, to_core, to_chip = peer(step)
        remote(
            box.at[other], got.at[me], r.one_send.at[index], r.one_recv.at[index], to_core, to_chip
        ).start()

    r.got_one[me] = r.mail_one[me]

    def attend_step(unit):
        attend(unit)
        for index in range(8):
            step = 8 * (unit - 2) + index + 1
            pl.when((step > 0) & (step < DEVICES))(
                partial(post_one, r.mail_one, r.got_one, 1, step)
            )
        for index, step in [(0, steps_e[2]), (1, steps_u[4]), (3, steps_u[5]), (4, steps_e[3])]:
            pl.when(unit == index)(step)

    every(0, 6, attend_step)
    steps_e[4]()

    units = r.units[...].reshape(SLOT_ROWS, WIDTH)
    weight_row, pair_row, side_row = r.pairs[0:1, :], r.pairs[1:2, :], r.pairs[2:3, :]

    def pair_scores(rows, pair_col, side_col):
        opposite = side_col + side_row == 1.0
        partner = opposite & (pair_col == pair_row)
        raw = SCORE_SCALE * dot_turned(rows, units)
        shifted = jnp.where(partner, raw - SCORE_SCALE * MARGIN_WIDTH, raw)
        return jnp.where(opposite, shifted, MASK_FLOOR), partner

    every_score, every_partner = pair_scores(
        units, r.pairs_col[:, 1:2], r.pairs_col[:, 2:3]
    )
    peak_row = jnp.max(every_score, axis=0, keepdims=True)
    log_row = peak_row + jnp.log(
        jnp.sum(jnp.exp(every_score - peak_row), axis=0, keepdims=True)
    )
    picked_row = jnp.sum(jnp.where(every_partner, every_score, 0.0), axis=0, keepdims=True)
    r.loss[...] = jnp.sum(weight_row * (log_row - picked_row), axis=1, keepdims=True)

    rows_here = pl.ds(pl.multiple_of(me * PAD, 16), PAD)
    own_score, own_partner = pair_scores(
        r.units[here], r.pairs_col[rows_here, 1:2], r.pairs_col[rows_here, 2:3]
    )
    own_partner = own_partner.astype(FULL)
    own_peak = jnp.max(own_score, axis=1, keepdims=True)
    own_exp = jnp.exp(own_score - own_peak)
    own_share = own_exp / jnp.sum(own_exp, axis=1, keepdims=True)
    by_row = (r.pairs_col[rows_here, 0:1] * (own_share - own_partner)).astype(LOW)
    by_column = (weight_row * (jnp.exp(own_score - log_row) - own_partner)).astype(LOW)
    unit_grad = SCORE_SCALE * (dot(by_row, units) + dot(by_column, units))
    along = jnp.sum(unit * unit_grad, axis=-1, keepdims=True)
    summary_grad = (unit_grad - unit * along) / magnitude

    residual_grad, grad_g2, grad_s2 = norm_back_parts(
        summary_grad, normed_two, inverse_two, vector(6)
    )
    down_grad = residual_grad.astype(LOW)
    r.downs[here] = down_grad
    steps_d[0]()
    r.hidden_cls[...] = down_grad

    def up_back(part):
        at = pl.ds(pl.multiple_of(part * WIDTH, BLOCK), WIDTH)
        act_grad = dot_turned(r.hidden_cls[...], r.wc[at, :])
        r.active_cls[:, at] = (act_grad * r.slope_cls[:, at]).astype(LOW)

    every(0, WIDE // WIDTH, up_back)
    steps_d[1]()

    def hidden_back(part):
        at = pl.ds(pl.multiple_of(part * BLOCK, BLOCK), BLOCK)
        r.wide_cls[:, at] = dot_turned(r.active_cls[...], r.wb[at, :])

    every(0, WIDTH // BLOCK, hidden_back)
    hidden_grad = r.wide_cls[:, 0:WIDTH] + residual_grad
    first_grad, grad_g1, grad_s1 = norm_back_parts(
        hidden_grad, r.normed_one[...], inverse_one, vector(3)
    )
    attend_grad = first_grad.astype(LOW)
    context_grad = dot_turned(attend_grad, r.wa[:, 3 * WIDTH : 4 * WIDTH]).astype(LOW)
    attend_here = r.attends.at[here]
    attend_here[:, 0:WIDTH] = attend_grad
    attend_here[:, WIDTH : 2 * WIDTH] = context_grad
    steps_a[0]()
    steps_d[2]()
    context_tall = spread(context_grad)
    probs = r.probs[...]
    prob_grad = dot_turned(context_tall, r.qkv[:, values])
    inner = jnp.sum(probs * prob_grad, axis=1, keepdims=True)
    score_grad = (probs * (prob_grad - inner)).astype(LOW)
    steps_a[1]()
    r.mail_two[:, 48:64, :] = pack_coefs(jnp.concatenate([probs_low, score_grad], axis=0))
    r.got_two[me, 48:64, :] = r.mail_two[me, 48:64, :]
    query_grad = (fold(dot(score_grad, r.qkv[:, keys])) * scale).astype(LOW)
    probs_total = jnp.sum(probs_low.astype(FULL), axis=1, keepdims=True)
    grad_bvalue = jnp.sum(probs_total * context_tall.astype(FULL), axis=0, keepdims=True)
    grad_bquery = jnp.sum(query_grad.astype(FULL), axis=0, keepdims=True)
    r.queries[here] = query_grad
    own_sums = jnp.concatenate(
        [jnp.zeros((2 * depth, WIDTH), FULL)]
        + [grad_bquery, grad_bvalue, grad_g1, grad_s1, grad_g2, grad_s2]
        + [jnp.zeros((128 - 2 * depth - 6, WIDTH), FULL)],
        axis=0,
    )
    r.own_sums[...] = jnp.transpose(own_sums)
    steps_q[0]()
    steps_a[2]()
    r.tall[0:PAIR_ROWS, :] = (dot(score_grad, r.embedded[...]) * scale).astype(LOW)

    def with_sums(at, both):
        return both + r.own_sums[pl.ds(pl.multiple_of(at * depth, 16), depth), :]

    pack_two = pack_tall(r.mail_two, 0, with_sums)

    def send_two(at):
        remote(
            r.mail_two.at[at],
            r.got_two.at[me],
            r.one_send.at[2],
            r.one_recv.at[2],
            lax.div(at, CHIPS),
            lax.rem(at, CHIPS),
        ).start()

    def pack_two_step(step):
        part = lax.rem(step + lax.div(me, 4), CHIPS // 2)
        pack_two(part)
        for index in range(4):
            turn = lax.rem(index + me, 4)
            at = lax.div(turn, 2) * CHIPS + 2 * part + lax.rem(turn, 2)
            pl.when(at != me)(partial(send_two, at))

    every(0, CHIPS // 2, pack_two_step)
    r.got_two[me, 0:48, :] = r.mail_two[me, 0:48, :]
    steps_q[1]()

    def all_rows(buffer, start, width=WIDTH):
        return buffer[:, :, :, :, start : start + width].reshape(SLOT_ROWS, width)

    quarter_rows_count = quarter_size * PAD

    def from_sent(quarter):
        span = pl.ds(pl.multiple_of(quarter * quarter_rows_count, 128), quarter_rows_count)
        shape = (GROUPS * quarter_rows_count, quarter_rows_count)
        lanes = (iota(shape, 1) + quarter * quarter_rows_count).astype(FULL)
        named = r.found[0:GROUPS, span, 1:2].reshape(GROUPS * quarter_rows_count, 1)
        return (named == lanes).astype(LOW), span

    def quarter_part(buffer, quarter, start):
        planes = pl.ds(lax.rem(quarter, 2) * 2, 2)
        part = buffer[lax.div(quarter, 2), planes, :, :, start : start + BLOCK]
        return part.reshape(quarter_rows_count, BLOCK)

    def widened(coefs, group, start, kind):
        lane_head = over(iota((128, BLOCK), 1) + start, HEAD)
        lanes = iota((128, BLOCK), 0) == lane_head + group * 2 * PAD + kind
        return dot(coefs, lanes.astype(LOW))

    half_wide = WIDE // 2

    def slope_tile(part):
        at = pl.ds(pl.multiple_of(core * half_wide + part * BLOCK, BLOCK), BLOCK)
        up_pre = dot(all_rows(r.early, 0), r.wb[:, at]) + r.up_bias[0:1, at]
        _, slope = gelu_parts(up_pre)
        r.slopes[:, pl.ds(pl.multiple_of(part * BLOCK, BLOCK), BLOCK)] = slope.astype(LOW)

    def slot_queries(quarter):
        sents, span = from_sent(quarter)
        for start in range(0, WIDTH, BLOCK):
            rows = dot(sents, quarter_part(r.early, quarter, WIDTH + start)).astype(LOW)
            rows = rows.reshape(GROUPS, quarter_rows_count, BLOCK)
            r.slot_query[:, span, start : start + BLOCK] = rows

    def activate():
        at = pl.ds(pl.multiple_of(chip // 2 * 2 * deep, 128), 2 * deep)
        up_pre = dot(all_rows(r.early, 0), r.wb[:, at]) + r.up_bias[0:1, at]
        r.active_turned[...] = jnp.transpose(gelu(up_pre)).astype(LOW)
        r.hidden_turned[...] = jnp.transpose(all_rows(r.early, 0))

    steps_e[5]()

    def open_step(tile):
        open_tile(tile)
        pl.when(tile == 0)(steps_d[3])
        pl.when(tile == 2)(steps_a[3])

    def feed_step(part):
        feed_up(part)
        rest = [steps_q[2], steps_d[4], steps_a[4], steps_q[3], steps_d[5], steps_a[5], steps_q[4]]
        for index, step in enumerate(rest):
            pl.when(part == index + index // 5)(step)

    def down_step(part):
        feed_down(part)
        for index, ends in enumerate([[drain_a, drain_b], [drain_c, drain_u], [drain_e]]):
            for end in ends:
                pl.when(part == index)(end)

    every(0, TOKENS // BLOCK, open_step)
    r.tile_up[...] = up_product(0)
    every(0, WIDE // BLOCK - 1, feed_step)
    feed_up(WIDE // BLOCK - 1, last=True)
    every(0, WIDTH // BLOCK, feed_rest)
    every(0, WIDTH // BLOCK, down_step)
    every(0, TOKENS // BLOCK, close_tile)
    every(0, 4, slot_queries)
    every(0, 6, slope_tile)
    activate()

    all_but_one(r.got_one, 1).wait_recv()
    def slot_probs(group):
        got = r.got_two[:, 48:64, :].reshape(SLOT_ROWS, 128)
        for start in range(0, WIDTH, BLOCK):
            r.replies[group, :, start : start + BLOCK] = widened(got, group, start, 0).astype(LOW)

    def slot_values(quarter):
        sents, span = from_sent(quarter)
        for start in range(0, WIDTH, BLOCK):
            lanes = slice(start, start + BLOCK)
            rows = dot(sents, quarter_part(r.attends, quarter, WIDTH + start))
            rows = rows.reshape(GROUPS, quarter_rows_count, BLOCK)
            rows = r.replies[:, span, lanes].astype(FULL) * rows
            r.replies[:, span, lanes] = rows.astype(LOW)

    def head_products(got, first_row, right, start, target):
        def one_head(head):
            lane = core * (WIDTH // 2) + lax.div(head, 2) * 128
            pair_rows = right[:, :, :, :, pl.ds(pl.multiple_of(start + lane, 128), 128)]
            row = pl.ds(pl.multiple_of(first_row + lax.rem(head, 3) * PAD, 16), PAD)
            block_rows = got[:, row, :].reshape(SLOT_ROWS, 128)
            r.product[...] = contract(block_rows, pair_rows.reshape(SLOT_ROWS, 128), 0, 0)
            part = r.product[pl.ds(pl.multiple_of(lax.div(head, 3) * depth, 16), depth), :]
            at = pl.ds(pl.multiple_of(lane, 128), 128)
            own_lanes = over(iota((depth, 128), 1), HEAD) == lax.rem(head, 2)
            target[:, at] = jnp.where(own_lanes, part, target[:, at])

        every(0, HEADS // 2, one_head)

    def half_of(ref, at_core):
        half = ref.shape[1] // 2
        return ref.at[:, pl.ds(pl.multiple_of(at_core * half, 128), half)]

    def half_copy(index, ref, at_core):
        part = half_of(ref, at_core)
        return remote(part, part, r.half_send.at[index], r.half_recv.at[index], 1 - core, chip)

    own_half = pl.ds(pl.multiple_of(core * (WIDTH // 2), 128), WIDTH // 2)
    r.g_wv[:, own_half] = jnp.zeros((depth, WIDTH // 2), FULL)
    r.g_wk[:, own_half] = jnp.zeros((depth, WIDTH // 2), FULL)
    head_products(r.got_one, PAD, r.attends, WIDTH, r.g_wv)
    half_copy(0, r.g_wv, core).start()

    downs = r.downs[...].reshape(SLOT_ROWS, WIDTH)
    attends = all_rows(r.attends, 0)

    def up_tile(part):
        at = pl.ds(pl.multiple_of(core * half_wide + part * BLOCK, BLOCK), BLOCK)
        slope = r.slopes[:, pl.ds(pl.multiple_of(part * BLOCK, BLOCK), BLOCK)].astype(FULL)
        up_all = (dot_turned(r.downs[...].reshape(SLOT_ROWS, WIDTH), r.wc[at, :]) * slope)
        up_all = up_all.astype(LOW)
        r.g_wup[0:depth, at] = dot(r.hidden_turned[mine, :], up_all)
        total = jnp.sum(up_all.astype(FULL), axis=0, keepdims=True)
        r.g_wup[depth : depth + 8, at] = jnp.broadcast_to(total, (8, BLOCK))

    every(0, half_wide // BLOCK, up_tile)
    half_copy(1, r.g_wup, core).start()
    r.g_wdown[...] = dot(r.active_turned[pl.ds(pl.multiple_of(chip % 2 * deep, 16), deep), :], downs)
    r.left_turned[...] = jnp.transpose(r.got_one[:, 0:PAD, :].reshape(SLOT_ROWS, 128))
    r.g_wo[...] = dot(r.left_turned[0:depth, :], attends)

    def own_part(rows, size):
        start = chip * size
        window = jnp.minimum(lax.div(start, 128) * 128, rows.shape[1] - BLOCK)
        part = rows[:, pl.ds(pl.multiple_of(window, 128), BLOCK)]
        return pltpu.roll(part, lax.rem(BLOCK + window - start, BLOCK), 1)

    for quarter in range(4):
        rows_of(quarter).wait_send()
    all_but_one(r.got_two, 2).wait_recv()
    every(0, GROUPS, slot_probs)
    every(0, 4, slot_values)

    def slot_grads(group):
        got_scores = r.got_two[:, 48:64, :].reshape(SLOT_ROWS, 128)
        for start in range(0, WIDTH, BLOCK):
            lanes = slice(start, start + BLOCK)
            rows = r.slot_query[group, :, lanes].astype(FULL)
            rows = widened(got_scores, group, start, PAD) * rows * scale
            r.slot_query[group, :, lanes] = rows.astype(LOW)
        for start in range(0, WIDTH, BLOCK):
            lanes = slice(start, start + BLOCK)
            row_grad = dot_turned(r.slot_query[group], r.wa[lanes, keys])
            row_grad = row_grad + dot_turned(r.replies[group], r.wa[lanes, values])
            r.rows[group, :, lanes] = row_grad.astype(LOW)

    every(0, GROUPS, slot_grads)
    steps_q[5]()
    query_grads = all_rows(r.queries, 0)
    extra = dot_turned(query_grads, r.wa[:, 0:WIDTH]) + attends.astype(FULL)
    r.extra[...] = extra.astype(LOW)
    r.g_wq[...] = dot(r.left_turned[depth : 2 * depth, :], query_grads)

    half_rows = VOCAB_ROWS // 2

    def table_copy(tile):
        at = pl.ds(pl.multiple_of(tile * half_rows, BLOCK), half_rows)
        return pltpu.make_async_copy(
            r.table_full.at[at], r.table_grad.at[at], r.table_sem.at[tile]
        )

    def table_tile(tile):
        at = pl.ds(pl.multiple_of(tile * half_rows, BLOCK), half_rows)
        for start in range(0, WIDTH, BLOCK):
            lanes = slice(start, start + BLOCK)
            slot_rows = r.rows[:, :, lanes].reshape(GROUPS * SLOT_ROWS, BLOCK)
            r.table_full[at, lanes] = dot(r.by_row[at, 0 : GROUPS * SLOT_ROWS], slot_rows) + dot(
                r.by_row[at, GROUPS * SLOT_ROWS :], r.extra[:, lanes]
            )
        table_copy(tile).start()

    every(0, 2, table_tile)
    head_products(r.got_two, 0, r.early, WIDTH, r.g_wk)
    half_copy(2, r.g_wk, core).start()

    down_total = jnp.sum(downs.astype(FULL), axis=0, keepdims=True)
    attend_total = jnp.sum(attends.astype(FULL), axis=0, keepdims=True)
    sums = jnp.sum(r.got_two[:, 0:48, :].astype(FULL), axis=0)
    sums = jnp.concatenate([sums, jnp.zeros((128 - 48, 128), FULL)], axis=0)
    r.totals[...] = jnp.concatenate([attend_total, down_total, jnp.zeros((6, WIDTH), FULL)], axis=0)
    r.g_small[8:16, :] = own_part(r.totals, depth)
    r.g_small[0:8, 0:128] = jnp.transpose(sums)[2 * depth : 2 * depth + 8, :]
    r.g_small[0:8, 128:BLOCK] = jnp.zeros((8, BLOCK - 128), FULL)
    half_copy(1, r.g_wup, 1 - core).wait_recv()
    r.g_small[16:24, :] = own_part(r.g_wup.at[depth : depth + 8, :], deep)

    half_copy(0, r.g_wv, 1 - core).wait_recv()
    half_copy(2, r.g_wk, 1 - core).wait_recv()
    for index, ref in enumerate([r.g_wv, r.g_wup, r.g_wk]):
        half_copy(index, ref, core).wait_send()

    for index, ref in enumerate([r.every_ids, r.got_one, r.got_two]):
        all_but_one(ref, index).wait_send()
    all_smalls().wait_send()
    for end in [drain_d, drain_a2, drain_q]:
        end()
    every(0, TOKENS // BLOCK, lambda tile: layer_copy(tile).wait())
    every(0, 2, lambda tile: table_copy(tile).wait())


def layer(inputs):
    dma = pltpu.SemaphoreType.DMA
    vmem = pl.BlockSpec(memory_space=pltpu.VMEM)
    anywhere = pl.BlockSpec(memory_space=pl.ANY)
    depth, deep = WIDTH // CHIPS, WIDE // CHIPS

    def gathered(width):
        return pltpu.VMEM((CORES, PLANES, LINES, PAD, width), LOW)

    outputs = dict(
        layer_out=((TOKENS, WIDTH), LOW),
        table_grad=((VOCAB_ROWS, WIDTH), FULL),
        g_wq=((depth, WIDTH), FULL),
        g_wk=((depth, WIDTH), FULL),
        g_wv=((depth, WIDTH), FULL),
        g_wo=((depth, WIDTH), FULL),
        g_wup=((depth + 8, WIDE), FULL),
        g_wdown=((deep, WIDTH), FULL),
        g_small=((24, BLOCK), FULL),
        loss=((1, 1), FULL),
    )
    scratch = dict(
        ids=pltpu.VMEM((8, 128), jnp.int32),
        every_ids=pltpu.VMEM((DEVICES, 8, 128), jnp.int32),
        rank=pltpu.VMEM((DEVICES, TOKENS), FULL),
        code=pltpu.VMEM((DEVICES, TOKENS), FULL),
        found=pltpu.VMEM((GROUPS + 1, SLOT_ROWS, 2), FULL),
        block_bias=pltpu.VMEM((2 * BLOCK, BLOCK // 2), FULL),
        valid_bias=pltpu.VMEM((8, TOKENS), FULL),
        slot_col=pltpu.VMEM((TOKENS, 1), FULL),
        slot_line=pltpu.VMEM((8, TOKENS), FULL),
        valid_col=pltpu.VMEM((TOKENS, 1), FULL),
        valid_line=pltpu.VMEM((8, TOKENS), FULL),
        pairs=pltpu.VMEM((8, SLOT_ROWS), FULL),
        pairs_col=pltpu.VMEM((SLOT_ROWS, 128), FULL),
        vectors=pltpu.VMEM((PAD, WIDTH), FULL),
        up_bias=pltpu.VMEM((8, WIDE), FULL),
        qkv_bias=pltpu.VMEM((8, 3 * WIDTH), FULL),
        smalls=pltpu.VMEM((PAD, CHIPS * 128), LOW),
        wa=pltpu.VMEM((WIDTH, 4 * WIDTH), LOW),
        wb=pltpu.VMEM((WIDTH, WIDE), LOW),
        wc=pltpu.VMEM((WIDE, WIDTH), LOW),
        chosen=pltpu.VMEM((GROUPS, SLOT_ROWS, VOCAB_ROWS), LOW),
        by_row=pltpu.VMEM((VOCAB_ROWS, (GROUPS + 1) * SLOT_ROWS), LOW),
        rows=pltpu.VMEM((GROUPS, SLOT_ROWS, WIDTH), LOW),
        replies=pltpu.VMEM((GROUPS, SLOT_ROWS, WIDTH), LOW),
        slot_query=pltpu.VMEM((GROUPS, SLOT_ROWS, WIDTH), LOW),
        extra=pltpu.VMEM((SLOT_ROWS, WIDTH), LOW),
        hidden_cls=pltpu.VMEM((PAD, WIDTH), LOW),
        active_cls=pltpu.VMEM((PAD, WIDE), LOW),
        slope_cls=pltpu.VMEM((PAD, WIDE), FULL),
        wide_cls=pltpu.VMEM((PAD, WIDTH), FULL),
        tall=pltpu.VMEM((PAIR_ROWS + 2 * PAD, WIDTH), LOW),
        own_sums=pltpu.VMEM((WIDTH, 128), FULL),
        product=pltpu.VMEM((128, 128), FULL),
        slot_hot=pltpu.VMEM((GROUPS, SLOT_ROWS, TOKENS), LOW),
        tile_up=pltpu.VMEM((TOKENS, BLOCK), FULL),
        embedded=pltpu.VMEM((TOKENS, WIDTH), LOW),
        qkv=pltpu.VMEM((TOKENS, 3 * WIDTH), LOW),
        context=pltpu.VMEM((TOKENS, WIDTH), LOW),
        table_full=pltpu.VMEM((VOCAB_ROWS, WIDTH), FULL),
        probs=pltpu.VMEM((PAIR_ROWS, TOKENS), FULL),
        normed_one=pltpu.VMEM((PAD, WIDTH), FULL),
        units=gathered(WIDTH),
        early=gathered(2 * WIDTH),
        downs=gathered(WIDTH),
        attends=gathered(2 * WIDTH),
        queries=gathered(WIDTH),
        slopes=pltpu.VMEM((SLOT_ROWS, WIDE // 2), LOW),
        hidden_turned=pltpu.VMEM((WIDTH, SLOT_ROWS), LOW),
        active_turned=pltpu.VMEM((2 * deep, SLOT_ROWS), LOW),
        left_turned=pltpu.VMEM((128, SLOT_ROWS), LOW),
        totals=pltpu.VMEM((8, WIDTH), FULL),
        mail_one=pltpu.VMEM((DEVICES, 64, 128), LOW),
        got_one=pltpu.VMEM((DEVICES, 64, 128), LOW),
        mail_two=pltpu.VMEM((DEVICES, 64, 128), LOW),
        got_two=pltpu.VMEM((DEVICES, 64, 128), LOW),
        rows_send=dma((4,)),
        rows_recv=dma((4,)),
        one_send=dma((4,)),
        one_recv=dma((4,)),
        small_send=dma((1,)),
        small_recv=dma((1,)),
        weight_send=dma((3, 7)),
        weight_recv=dma((3, 18)),
        gather_send=dma((5, 13)),
        gather_recv=dma((5, 13)),
        half_send=dma((3,)),
        half_recv=dma((3,)),
        out_sem=dma((TOKENS // BLOCK,)),
        table_sem=dma((2,)),
    )
    names = INPUTS + OUTPUTS + list(scratch)
    return pl.pallas_call(
        partial(layer_kernel, names),
        out_shape=tuple(jax.ShapeDtypeStruct(*outputs[name]) for name in OUTPUTS),
        in_specs=[vmem] * len(INPUTS),
        out_specs=(anywhere, anywhere) + (vmem,) * (len(OUTPUTS) - 2),
        scratch_shapes=list(scratch.values()),
        compiler_params=pltpu.CompilerParams(
            collective_id=0, has_side_effects=True, vmem_limit_bytes=VMEM_LIMIT
        ),
        name="layer",
    )(*inputs)


def finish_kernel(count, *refs):
    large, (small, loss), outs = refs[:count], refs[count : count + 2], refs[count + 2 : -1]
    sems = refs[-1]
    copies = []
    for index, (source, target) in enumerate(zip(large, outs)):
        part = source if source.shape == target.shape else source.at[: target.shape[0]]
        copies.append(pltpu.make_async_copy(part, target, sems.at[index]))
        copies[-1].start()
    for row, target in zip([0, 1, 8, 2, 3, 16, 9, 4, 5], outs[count : count + 9]):
        size = target.shape[0]
        target[...] = small[row : row + 1, 0:size].reshape(size)
    outs[-1][...] = loss[...].reshape(1)
    for one in copies:
        one.wait()


def finish(results):
    vmem = pl.BlockSpec(memory_space=pltpu.VMEM)
    anywhere = pl.BlockSpec(memory_space=pl.ANY)
    depth, deep = WIDTH // CHIPS, WIDE // CHIPS
    count = len(results) - 2
    shapes = [(one.shape, one.dtype) for one in results[:count]]
    shapes[6] = ((depth, WIDE), FULL)
    shapes += [((depth,), FULL)] * 5 + [((deep,), FULL)] + [((depth,), FULL)] * 3
    shapes.append(((1,), FULL))
    return pl.pallas_call(
        partial(finish_kernel, count),
        out_shape=tuple(jax.ShapeDtypeStruct(*one) for one in shapes),
        in_specs=[vmem] * (count + 2),
        out_specs=(anywhere,) * count + (vmem,) * 10,
        scratch_shapes=[pltpu.SemaphoreType.DMA((count,))],
        name="finish",
    )(*results)


def block_body(
    table,
    token_ids,
    sent_lengths,
    pair_slot,
    pair_lang,
    *parameters,
):
    results = finish(layer((table, token_ids, sent_lengths, pair_slot, pair_lang) + parameters))
    layer_out, table_grad, g_wq, g_wk, g_wv, g_wo, g_wup, g_wdown = results[:8]
    g_bq, g_bv, g_bo, g_g1, g_s1, g_bup, g_bdown, g_g2, g_s2, loss = results[8:]
    return (
        layer_out.reshape(token_ids.shape + (WIDTH,)),
        loss.reshape(()),
        table_grad,
        g_wq,
        g_bq,
        g_wk,
        g_wv,
        g_bv,
        g_wo,
        g_bo,
        g_g1,
        g_s1,
        g_wup,
        g_bup,
        g_wdown,
        g_bdown,
        g_g2,
        g_s2,
    )


def solution(mesh):
    in_specs = (
        P(("dp", "fsdp"), None),
        P(("dp", "fsdp"), None),
        P(("dp", "fsdp")),
        P(),
        P(),
        P("fsdp", None),
        P("fsdp"),
        P("fsdp", None),
        P("fsdp", None),
        P("fsdp"),
        P("fsdp", None),
        P("fsdp"),
        P("fsdp"),
        P("fsdp"),
        P("fsdp", None),
        P("fsdp"),
        P("fsdp", None),
        P("fsdp"),
        P("fsdp"),
        P("fsdp"),
    )
    out_specs = (
        P(("dp", "fsdp"), None, None),
        P(),
        P(("dp", "fsdp"), None),
        P("fsdp", None),
        P("fsdp"),
        P("fsdp", None),
        P("fsdp", None),
        P("fsdp"),
        P("fsdp", None),
        P("fsdp"),
        P("fsdp"),
        P("fsdp"),
        P("fsdp", None),
        P("fsdp"),
        P("fsdp", None),
        P("fsdp"),
        P("fsdp"),
        P("fsdp"),
    )
    sizes = dict(mesh.shape)
    body = general_body
    if sizes["dp"] == CORES and sizes["fsdp"] == CHIPS:
        body = block_body
    return jax.shard_map(body, mesh=mesh, in_specs=in_specs, out_specs=out_specs, check_vma=False)
```

```python
from functools import partial
from types import SimpleNamespace

import jax
import jax.numpy as jnp
from jax import lax
from jax.experimental import pallas as pl
from jax.experimental.pallas import tpu as pltpu
from jax.sharding import PartitionSpec as P

HEADS = 12
HEAD = 64
LANGS = 109


EPSILON = 1e-06
SCORE_SCALE = 50.0
MARGIN_WIDTH = 0.3
MASK_FLOOR = -1000000000.0


def contract(left_side, right_side, left_dim, right_dim):
    return lax.dot_general(
        left_side,
        right_side,
        (((left_dim,), (right_dim,)), ((), ())),
        preferred_element_type=jnp.float32,
    )


def norm_rows(inputs, ln_gain, ln_shift):
    row_mean = jnp.mean(inputs, axis=-1, keepdims=True)
    centered = inputs - row_mean
    variance = jnp.mean(centered * centered, axis=-1, keepdims=True)
    inverse = lax.rsqrt(variance + EPSILON)
    normed = centered * inverse
    return (normed * ln_gain + ln_shift, normed, inverse)


def norm_back(grad_output, normed, inverse, ln_gain):
    grad_normed = grad_output * ln_gain
    first_term = jnp.mean(grad_normed, axis=-1, keepdims=True)
    second_term = jnp.mean(grad_normed * normed, axis=-1, keepdims=True)
    grad_input = inverse * (grad_normed - first_term - normed * second_term)
    return (grad_input, jnp.sum(grad_output * normed, axis=0), jnp.sum(grad_output, axis=0))


def general_body(
    table,
    token_ids,
    sent_lengths,
    pair_slot,
    pair_lang,
    w_query,
    b_query,
    w_key,
    w_value,
    b_value,
    w_out,
    b_out,
    ln1_gain,
    ln1_bias,
    w_up,
    b_up,
    w_down,
    b_down,
    ln2_gain,
    ln2_bias,
):
    sentences, length = token_ids.shape
    tokens = sentences * length
    vocab_rows, model_width = table.shape
    owners = lax.axis_size(("dp", "fsdp"))
    dp_count = lax.axis_size("dp")
    fsdp_count = lax.axis_size("fsdp")
    capacity = max(2, 2 * tokens // owners)
    device = lax.axis_index(("dp", "fsdp"))
    score_factor = HEAD ** (-0.5)
    flat_ids = token_ids.reshape(tokens)
    owner_of = flat_ids // vocab_rows
    member = (owner_of[:, None] == jnp.arange(owners, dtype=jnp.int32)[None, :]).astype(jnp.int32)
    owner_rank = jnp.sum(jnp.cumsum(member, axis=0) * member, axis=1) - 1
    slot_of = owner_of * capacity + owner_rank
    requests = jnp.full((owners * capacity,), -1, jnp.int32).at[slot_of].set(flat_ids)
    received = lax.all_to_all(
        lax.all_to_all(
            requests.reshape(dp_count, fsdp_count, capacity),
            "dp",
            split_axis=0,
            concat_axis=0,
            tiled=True,
        ),
        "fsdp",
        split_axis=1,
        concat_axis=1,
        tiled=True,
    )
    present = received >= 0
    local_rows = jnp.where(present, received - device * vocab_rows, 0)
    found_rows = jnp.where(present[..., None], table[local_rows], jnp.zeros((), table.dtype))
    replies = lax.all_to_all(
        lax.all_to_all(found_rows, "dp", split_axis=0, concat_axis=0, tiled=True),
        "fsdp",
        split_axis=1,
        concat_axis=1,
        tiled=True,
    )
    embedded = replies.reshape(owners * capacity, model_width)[slot_of]
    gathered = (
        lax.all_gather(w_query, "fsdp", axis=0, tiled=True),
        lax.all_gather(b_query, "fsdp", axis=0, tiled=True),
        lax.all_gather(w_key, "fsdp", axis=0, tiled=True),
        lax.all_gather(w_value, "fsdp", axis=0, tiled=True),
        lax.all_gather(b_value, "fsdp", axis=0, tiled=True),
        lax.all_gather(w_out, "fsdp", axis=0, tiled=True),
        lax.all_gather(b_out, "fsdp", axis=0, tiled=True),
        lax.all_gather(ln1_gain, "fsdp", axis=0, tiled=True),
        lax.all_gather(ln1_bias, "fsdp", axis=0, tiled=True),
        lax.all_gather(w_up, "fsdp", axis=0, tiled=True),
        lax.all_gather(b_up, "fsdp", axis=0, tiled=True),
        lax.all_gather(w_down, "fsdp", axis=0, tiled=True),
        lax.all_gather(b_down, "fsdp", axis=0, tiled=True),
        lax.all_gather(ln2_gain, "fsdp", axis=0, tiled=True),
        lax.all_gather(ln2_bias, "fsdp", axis=0, tiled=True),
    )
    (
        full_wq,
        full_bq,
        full_wk,
        full_wv,
        full_bv,
        full_wo,
        full_bo,
        full_g1,
        full_s1,
        full_wup,
        full_bup,
        full_wdown,
        full_bdown,
        full_g2,
        full_s2,
    ) = gathered
    valid_mask = jnp.arange(length, dtype=jnp.int32)[None, :] < sent_lengths[:, None]
    head_shape = (sentences, length, HEADS, HEAD)
    queries = (jnp.dot(embedded, full_wq, preferred_element_type=jnp.float32) + full_bq).astype(
        jnp.bfloat16
    )
    key_heads = (
        jnp.dot(embedded, full_wk, preferred_element_type=jnp.float32)
        .astype(jnp.bfloat16)
        .reshape(head_shape)
    )
    value_heads = (
        (jnp.dot(embedded, full_wv, preferred_element_type=jnp.float32) + full_bv)
        .astype(jnp.bfloat16)
        .reshape(head_shape)
    )
    query_heads = queries.reshape(head_shape)
    scores = (
        jnp.einsum("bqhd,bkhd->bhqk", query_heads, key_heads, preferred_element_type=jnp.float32)
        * score_factor
    )
    scores = jnp.where(valid_mask[:, None, None, :], scores, MASK_FLOOR)
    row_peak = jnp.max(scores, axis=-1, keepdims=True)
    shifted = jnp.exp(scores - row_peak)
    totals = jnp.sum(shifted, axis=-1, keepdims=True)
    attn_probs = (shifted / totals).astype(jnp.bfloat16)
    context = jnp.einsum(
        "bhqk,bkhd->bqhd", attn_probs, value_heads, preferred_element_type=jnp.float32
    )
    context = context.reshape(tokens, model_width).astype(jnp.bfloat16)
    attended = jnp.dot(context, full_wo, preferred_element_type=jnp.float32) + full_bo
    hidden, normed_one, inverse_one = norm_rows(
        embedded.astype(jnp.float32) + attended, full_g1, full_s1
    )
    hidden_low = hidden.astype(jnp.bfloat16)
    up_pre = jnp.dot(hidden_low, full_wup, preferred_element_type=jnp.float32) + full_bup
    activated = jax.nn.gelu(up_pre, approximate=False).astype(jnp.bfloat16)
    down_pre = jnp.dot(activated, full_wdown, preferred_element_type=jnp.float32) + full_bdown
    normed_out, normed_two, inverse_two = norm_rows(hidden + down_pre, full_g2, full_s2)
    layer_out = jnp.where(valid_mask.reshape(tokens)[:, None], normed_out, 0.0).astype(jnp.bfloat16)
    layer_out = layer_out.reshape(sentences, length, model_width)

    def first_rows(matrix):
        return matrix.reshape(sentences, length, matrix.shape[-1])[:, 0]

    summary = first_rows(normed_out)
    magnitude = jnp.sqrt(jnp.sum(summary * summary, axis=-1, keepdims=True) + EPSILON)
    unit_vector = summary / magnitude
    unit_low = unit_vector.astype(jnp.bfloat16)
    every_unit = lax.all_gather(unit_low, ("dp", "fsdp"), axis=0, tiled=True)
    every_side = pair_slot % 2
    every_pair = pair_slot // 2
    my_slots = lax.dynamic_slice_in_dim(pair_slot, device * sentences, sentences)
    my_side = my_slots % 2
    my_pair = my_slots // 2
    lang_onehot = (pair_lang[:, None] == jnp.arange(LANGS, dtype=jnp.int32)[None, :]).astype(
        jnp.float32
    )
    per_lang = jnp.sum(lang_onehot, axis=0)
    per_pair = 1.0 / (2.0 * LANGS * jnp.sum(lang_onehot * per_lang[None, :], axis=1))
    my_weight = jnp.take(per_pair, my_pair)
    opposite = my_side[:, None] != every_side[None, :]
    partner = opposite & (my_pair[:, None] == every_pair[None, :])
    raw_scores = SCORE_SCALE * contract(unit_low, every_unit, 1, 1)
    pair_scores = jnp.where(partner, raw_scores - SCORE_SCALE * MARGIN_WIDTH, raw_scores)
    pair_scores = jnp.where(opposite, pair_scores, MASK_FLOOR)
    pair_peak = jnp.max(pair_scores, axis=1, keepdims=True)
    pair_exp = jnp.exp(pair_scores - pair_peak)
    pair_total = jnp.sum(pair_exp, axis=1, keepdims=True)
    log_total = pair_peak[:, 0] + jnp.log(pair_total[:, 0])
    picked = jnp.sum(jnp.where(partner, pair_scores, 0.0), axis=1)
    loss_value = lax.psum(jnp.sum(my_weight * (log_total - picked)), ("dp", "fsdp"))
    coefficients = (
        my_weight[:, None] * (pair_exp / pair_total - partner.astype(jnp.float32))
    ).astype(jnp.bfloat16)
    unit_grad = SCORE_SCALE * contract(coefficients, every_unit, 1, 0)
    column_terms = SCORE_SCALE * contract(coefficients, unit_low, 0, 0)
    unit_grad = unit_grad + lax.psum_scatter(
        column_terms, ("dp", "fsdp"), scatter_dimension=0, tiled=True
    )
    along = jnp.sum(unit_vector * unit_grad, axis=-1, keepdims=True)
    summary_grad = (unit_grad - unit_vector * along) / magnitude
    again_weights = (
        lax.all_gather(w_query, "fsdp", axis=0, tiled=True),
        lax.all_gather(w_key, "fsdp", axis=0, tiled=True),
        lax.all_gather(w_value, "fsdp", axis=0, tiled=True),
        lax.all_gather(w_out, "fsdp", axis=0, tiled=True),
        lax.all_gather(ln1_gain, "fsdp", axis=0, tiled=True),
        lax.all_gather(w_up, "fsdp", axis=0, tiled=True),
        lax.all_gather(w_down, "fsdp", axis=0, tiled=True),
        lax.all_gather(ln2_gain, "fsdp", axis=0, tiled=True),
    )
    again_wq, again_wk, again_wv, again_wo, again_g1, again_wup, again_wdown, again_g2 = (
        again_weights
    )
    residual_grad, grad_g2, grad_s2 = norm_back(
        summary_grad, first_rows(normed_two), first_rows(inverse_two), again_g2
    )
    down_grad = residual_grad.astype(jnp.bfloat16)
    activated_cls = first_rows(activated)
    act_grad = contract(down_grad, again_wdown, 1, 1)
    gelu_value, gelu_pull = jax.vjp(partial(jax.nn.gelu, approximate=False), first_rows(up_pre))
    up_grad = gelu_pull(act_grad)[0].astype(jnp.bfloat16)
    hidden_cls = first_rows(hidden_low)
    hidden_grad = contract(up_grad, again_wup, 1, 1) + residual_grad
    first_grad, grad_g1, grad_s1 = norm_back(
        hidden_grad, first_rows(normed_one), first_rows(inverse_one), again_g1
    )
    attend_grad = first_grad.astype(jnp.bfloat16)
    context_cls = first_rows(context)
    context_grad = (
        contract(attend_grad, again_wo, 1, 1).astype(jnp.bfloat16).reshape(sentences, HEADS, HEAD)
    )
    query_cls = query_heads[:, 0]
    cls_scores = (
        jnp.einsum("bhd,bkhd->bhk", query_cls, key_heads, preferred_element_type=jnp.float32)
        * score_factor
    )
    cls_scores = jnp.where(valid_mask[:, None, :], cls_scores, MASK_FLOOR)
    cls_probs = jnp.exp(cls_scores - row_peak[:, :, 0]) / totals[:, :, 0]
    prob_grad = jnp.einsum(
        "bhd,bkhd->bhk", context_grad, value_heads, preferred_element_type=jnp.float32
    )
    score_grad = (
        cls_probs * (prob_grad - jnp.sum(cls_probs * prob_grad, axis=-1, keepdims=True))
    ).astype(jnp.bfloat16)
    query_grad = (
        (
            jnp.einsum("bhk,bkhd->bhd", score_grad, key_heads, preferred_element_type=jnp.float32)
            * score_factor
        )
        .astype(jnp.bfloat16)
        .reshape(sentences, model_width)
    )
    key_grad = (
        (
            jnp.einsum("bhk,bhd->bkhd", score_grad, query_cls, preferred_element_type=jnp.float32)
            * score_factor
        )
        .astype(jnp.bfloat16)
        .reshape(tokens, model_width)
    )
    value_grad = (
        jnp.einsum(
            "bhk,bhd->bkhd",
            cls_probs.astype(jnp.bfloat16),
            context_grad,
            preferred_element_type=jnp.float32,
        )
        .astype(jnp.bfloat16)
        .reshape(tokens, model_width)
    )
    embedded_cls = first_rows(embedded)
    grad_wkey = contract(embedded, key_grad, 0, 0)
    grad_wvalue = contract(embedded, value_grad, 0, 0)
    grad_bvalue = jnp.sum(value_grad, axis=0, dtype=jnp.float32)
    row_grads = contract(key_grad, again_wk, 1, 1) + contract(value_grad, again_wv, 1, 1)
    summary_extra = contract(query_grad, again_wq, 1, 1) + first_grad
    row_grads = (
        row_grads.reshape(sentences, length, model_width)
        .at[:, 0]
        .add(summary_extra)
        .reshape(tokens, model_width)
    )
    outgoing = jnp.zeros((owners * capacity, model_width), jnp.float32).at[slot_of].set(row_grads)
    incoming = lax.all_to_all(
        lax.all_to_all(
            outgoing.reshape(dp_count, fsdp_count, capacity, model_width).astype(jnp.bfloat16),
            "dp",
            split_axis=0,
            concat_axis=0,
            tiled=True,
        ),
        "fsdp",
        split_axis=1,
        concat_axis=1,
        tiled=True,
    ).astype(jnp.float32)
    incoming = jnp.where(
        present.reshape(owners * capacity)[:, None],
        incoming.reshape(owners * capacity, model_width),
        0.0,
    )
    table_grad = (
        jnp.zeros((vocab_rows, model_width), jnp.float32)
        .at[local_rows.reshape(owners * capacity)]
        .add(incoming)
    )
    grad_wquery = contract(embedded_cls, query_grad, 0, 0)
    grad_bquery = jnp.sum(query_grad, axis=0, dtype=jnp.float32)
    grad_wout = contract(context_cls, attend_grad, 0, 0)
    grad_bout = jnp.sum(attend_grad, axis=0, dtype=jnp.float32)
    grad_wup = contract(hidden_cls, up_grad, 0, 0)
    grad_bup = jnp.sum(up_grad, axis=0, dtype=jnp.float32)
    grad_wdown = contract(activated_cls, down_grad, 0, 0)
    grad_bdown = jnp.sum(down_grad, axis=0, dtype=jnp.float32)
    owned_grads = (
        lax.psum_scatter(
            grad_wquery.astype(jnp.bfloat16), "fsdp", scatter_dimension=0, tiled=True
        ).astype(jnp.float32),
        lax.psum_scatter(
            grad_bquery.astype(jnp.bfloat16), "fsdp", scatter_dimension=0, tiled=True
        ).astype(jnp.float32),
        lax.psum_scatter(
            grad_wkey.astype(jnp.bfloat16), "fsdp", scatter_dimension=0, tiled=True
        ).astype(jnp.float32),
        lax.psum_scatter(
            grad_wvalue.astype(jnp.bfloat16), "fsdp", scatter_dimension=0, tiled=True
        ).astype(jnp.float32),
        lax.psum_scatter(
            grad_bvalue.astype(jnp.bfloat16), "fsdp", scatter_dimension=0, tiled=True
        ).astype(jnp.float32),
        lax.psum_scatter(
            grad_wout.astype(jnp.bfloat16), "fsdp", scatter_dimension=0, tiled=True
        ).astype(jnp.float32),
        lax.psum_scatter(
            grad_bout.astype(jnp.bfloat16), "fsdp", scatter_dimension=0, tiled=True
        ).astype(jnp.float32),
        lax.psum_scatter(
            grad_g1.astype(jnp.bfloat16), "fsdp", scatter_dimension=0, tiled=True
        ).astype(jnp.float32),
        lax.psum_scatter(
            grad_s1.astype(jnp.bfloat16), "fsdp", scatter_dimension=0, tiled=True
        ).astype(jnp.float32),
        lax.psum_scatter(
            grad_wup.astype(jnp.bfloat16), "fsdp", scatter_dimension=0, tiled=True
        ).astype(jnp.float32),
        lax.psum_scatter(
            grad_bup.astype(jnp.bfloat16), "fsdp", scatter_dimension=0, tiled=True
        ).astype(jnp.float32),
        lax.psum_scatter(
            grad_wdown.astype(jnp.bfloat16), "fsdp", scatter_dimension=0, tiled=True
        ).astype(jnp.float32),
        lax.psum_scatter(
            grad_bdown.astype(jnp.bfloat16), "fsdp", scatter_dimension=0, tiled=True
        ).astype(jnp.float32),
        lax.psum_scatter(
            grad_g2.astype(jnp.bfloat16), "fsdp", scatter_dimension=0, tiled=True
        ).astype(jnp.float32),
        lax.psum_scatter(
            grad_s2.astype(jnp.bfloat16), "fsdp", scatter_dimension=0, tiled=True
        ).astype(jnp.float32),
    )
    summed = (
        lax.psum(owned_grads[0].astype(jnp.bfloat16), "dp").astype(jnp.float32),
        lax.psum(owned_grads[1].astype(jnp.bfloat16), "dp").astype(jnp.float32),
        lax.psum(owned_grads[2].astype(jnp.bfloat16), "dp").astype(jnp.float32),
        lax.psum(owned_grads[3].astype(jnp.bfloat16), "dp").astype(jnp.float32),
        lax.psum(owned_grads[4].astype(jnp.bfloat16), "dp").astype(jnp.float32),
        lax.psum(owned_grads[5].astype(jnp.bfloat16), "dp").astype(jnp.float32),
        lax.psum(owned_grads[6].astype(jnp.bfloat16), "dp").astype(jnp.float32),
        lax.psum(owned_grads[7].astype(jnp.bfloat16), "dp").astype(jnp.float32),
        lax.psum(owned_grads[8].astype(jnp.bfloat16), "dp").astype(jnp.float32),
        lax.psum(owned_grads[9].astype(jnp.bfloat16), "dp").astype(jnp.float32),
        lax.psum(owned_grads[10].astype(jnp.bfloat16), "dp").astype(jnp.float32),
        lax.psum(owned_grads[11].astype(jnp.bfloat16), "dp").astype(jnp.float32),
        lax.psum(owned_grads[12].astype(jnp.bfloat16), "dp").astype(jnp.float32),
        lax.psum(owned_grads[13].astype(jnp.bfloat16), "dp").astype(jnp.float32),
        lax.psum(owned_grads[14].astype(jnp.bfloat16), "dp").astype(jnp.float32),
    )
    return (
        layer_out,
        loss_value,
        table_grad,
        summed[0],
        summed[1],
        summed[2],
        summed[3],
        summed[4],
        summed[5],
        summed[6],
        summed[7],
        summed[8],
        summed[9],
        summed[10],
        summed[11],
        summed[12],
        summed[13],
        summed[14],
    )


CORES = 2
PLANES = 4
LINES = 4
CHIPS = PLANES * LINES
DEVICES = CORES * CHIPS
CAPACITY = 48
GROUPS = 3
PAD = 16
TOKENS = 768
WIDTH = 768
WIDE = 3072
VOCAB_ROWS = 1024
PAIR_ROWS = HEADS * PAD
SLOT_ROWS = DEVICES * PAD
LONG = 64
BLOCK = 256
MESH = pl.DeviceIdType.MESH
LOW = jnp.bfloat16
FULL = jnp.float32
VMEM_LIMIT = 62 * 1024 * 1024

INPUTS = ["table", "token_ids", "lens", "slots", "langs"]
INPUTS += ["wq", "bq", "wk", "wv", "bv", "wo", "bo", "g1", "s1", "wup", "bup", "wdown", "bdown"]
INPUTS += ["g2", "s2"]
OUTPUTS = ["layer_out", "table_grad", "g_wq", "g_wk", "g_wv", "g_wo", "g_wup", "g_wdown"]
OUTPUTS += ["g_small", "loss"]


def place():
    core = lax.axis_index("dp")
    chip = lax.axis_index("fsdp")
    along_x = chip + 1 - 2 * (chip % 2)
    along_y = chip + 2 - 4 * ((chip // 2) % 2)
    first = along_x + core * (along_y - along_x)
    second = along_y + core * (along_x - along_y)
    return core, chip, first, second


def greet():
    core, chip, _, _ = place()
    me = core * CHIPS + chip
    barrier = pltpu.get_barrier_semaphore()

    def signal(step):
        other = lax.rem(me + step, DEVICES)
        pl.semaphore_signal(
            barrier,
            inc=1,
            device_id=(lax.div(other, CHIPS), lax.rem(other, CHIPS)),
            device_id_type=MESH,
        )

    every(1, DEVICES, signal)


def enter():
    pl.semaphore_wait(pltpu.get_barrier_semaphore(), DEVICES - 1)


def remote(source, target, send_sem, recv_sem, core, chip):
    return pltpu.make_async_remote_copy(
        src_ref=source,
        dst_ref=target,
        send_sem=send_sem,
        recv_sem=recv_sem,
        device_id=(core, chip),
        device_id_type=MESH,
    )


def every(start, stop, act):
    def step(index, carry):
        act(index)
        return carry

    lax.fori_loop(start, stop, step, 0)


def weight_steps(piece, many, send, recv):
    core, chip, first, second = place()
    plane, line = chip // LINES, chip % LINES
    line_first, line_second = first % LINES, second % LINES
    line_far = line_first + line_second - line
    is_low, is_high = plane > 0, plane < PLANES - 1

    def copy(send_index, recv_index, at, to_core, to_chip, carried=core):
        part = piece(at, carried)
        return remote(part, part, send.at[send_index], recv.at[recv_index], to_core, to_chip)

    def up(at_plane):
        return copy(at_plane, at_plane, at_plane * LINES + line, core, chip + LINES)

    def down(at_plane, index):
        return copy(index, at_plane, at_plane * LINES + line, core, chip - LINES)

    def side(at_plane, base, at_line, target):
        return copy(5, base + at_plane, at_plane * LINES + at_line, core, target)

    def across(at_plane, at_line):
        return copy(6, 17, at_plane * LINES + at_line, 1 - core, chip)

    def all_of(count, send_index, recv_index):
        part = many(count)
        return remote(part, part, send.at[send_index], recv.at[recv_index], 1 - core, chip)

    def begin():
        pl.when(is_high)(lambda: up(plane).start())
        pl.when(is_low)(lambda: down(plane, PLANES).start())
        side(plane, 5, line, first).start()
        side(plane, 9, line, second).start()

    def at_distance(distance, act):
        if distance == 0:
            act(plane, None)
            return
        pl.when(plane >= distance)(lambda: act(plane - distance, True))
        pl.when(plane + distance < PLANES)(lambda: act(plane + distance, False))

    def chain(distance):
        def act(at_plane, from_low):
            if from_low:
                up(at_plane).wait_recv()
                pl.when(is_high)(lambda: up(at_plane).start())
            else:
                down(at_plane, at_plane).wait_recv()
                pl.when(is_low)(lambda: down(at_plane, at_plane).start())
            side(at_plane, 5, line, first).start()
            side(at_plane, 9, line, second).start()
            across(at_plane, line).start()

        return partial(at_distance, distance, act)

    def near(distance):
        def act(at_plane, from_low):
            side(at_plane, 5, line_first, first).wait_recv()
            side(at_plane, 13, line_first, second).start()
            across(at_plane, line_first).start()

        return partial(at_distance, distance, act)

    def far(distance):
        def act(at_plane, from_low):
            side(at_plane, 9, line_second, second).wait_recv()
            across(at_plane, line_second).start()
            side(at_plane, 13, line_far, second).wait_recv()
            across(at_plane, line_far).start()

        return partial(at_distance, distance, act)

    def finish():
        all_of(15, 6, 17).wait_recv()

    def drain():
        def sent(index):
            copy(index, index, chip, 1 - core, chip).wait_send()

        for at_plane in range(PLANES):
            pl.when((plane >= at_plane) & is_high)(partial(sent, at_plane))
            pl.when((plane < at_plane) & is_low)(partial(sent, at_plane))
        pl.when(is_low)(partial(sent, PLANES))
        all_of(12, 5, 17).wait_send()
        all_of(15, 6, 17).wait_send()

    moves = [chain(1), near(0), chain(2), near(1), chain(3), far(0)]
    moves += [near(2), far(1), near(3), far(2), far(3)]
    return begin, moves, finish, drain


def gather_steps(buffer, send, recv):
    core, chip, first, second = place()
    plane, line = chip // LINES, chip % LINES
    line_first, line_second = first % LINES, second % LINES
    line_far = line_first + line_second - line
    half = buffer.shape[-1] // 2
    columns = pl.ds(pl.multiple_of(core * half, 128), half)
    others = pl.ds(pl.multiple_of((1 - core) * half, 128), half)

    def copy(index, part, to_core, to_chip):
        return remote(part, part, send.at[index], recv.at[index], to_core, to_chip)

    def own(at):
        return buffer.at[at, plane, line]

    def chip_part(at_plane, at_line, which):
        return buffer.at[:, at_plane, at_line, :, which]

    def line_part(at_line, which):
        return buffer.at[:, :, at_line, :, which]

    def start():
        copy(0, own(core), 1 - core, chip).start()

    def planes():
        copy(0, own(1 - core), 1 - core, chip).wait_recv()
        for step in range(1, PLANES):
            part = chip_part(plane, line, columns)
            copy(step, part, core, (chip + LINES * step) % CHIPS).start()

    def sides():
        for step in range(1, PLANES):
            part = chip_part((plane + PLANES - step) % PLANES, line, columns)
            copy(step, part, core, chip).wait_recv()
        copy(4, line_part(line, columns), core, first).start()
        copy(5, line_part(line, columns), core, second).start()
        for step in range(1, PLANES):
            part = chip_part((plane + PLANES - step) % PLANES, line, columns)
            copy(6 + step, part, 1 - core, chip).start()

    def corner():
        copy(4, line_part(line_first, columns), core, first).wait_recv()
        copy(6, line_part(line_first, columns), core, second).start()
        copy(10, line_part(line_first, columns), 1 - core, chip).start()
        copy(5, line_part(line_second, columns), core, second).wait_recv()
        copy(11, line_part(line_second, columns), 1 - core, chip).start()

    def last():
        copy(6, line_part(line_far, columns), core, second).wait_recv()
        copy(12, line_part(line_far, columns), 1 - core, chip).start()

    def finish():
        for step in range(1, PLANES):
            part = chip_part((plane + PLANES - step) % PLANES, line, others)
            copy(6 + step, part, 1 - core, chip).wait_recv()
        copy(10, line_part(line_second, others), 1 - core, chip).wait_recv()
        copy(11, line_part(line_first, others), 1 - core, chip).wait_recv()
        copy(12, line_part(line_far, others), 1 - core, chip).wait_recv()

    def drain():
        copy(0, own(core), 1 - core, chip).wait_send()
        for index in [1, 2, 3, 7, 8, 9]:
            copy(index, chip_part(plane, line, columns), 1 - core, chip).wait_send()
        for index in [4, 5, 6, 10, 11, 12]:
            copy(index, line_part(line, columns), 1 - core, chip).wait_send()

    return [start, planes, sides, corner, last, finish], drain


def iota(shape, axis):
    return lax.broadcasted_iota(jnp.int32, shape, axis)


def over(numbers, power):
    return lax.shift_right_arithmetic(numbers, jnp.full_like(numbers, power.bit_length() - 1))


def within(numbers, power):
    return numbers & (power - 1)


def as_column(row):
    parts = []
    for start in range(0, row.shape[1], 128):
        tile = jnp.broadcast_to(row[:, start : start + 128], (128, 128))
        parts.append(jnp.transpose(tile)[:, 0:1])
    return jnp.concatenate(parts, axis=0)


def as_row(column):
    parts = []
    for start in range(0, column.shape[0], 128):
        tile = jnp.broadcast_to(column[start : start + 128, :], (128, 128))
        parts.append(jnp.transpose(tile)[0:1, :])
    return jnp.concatenate(parts, axis=1)


def dot(left_side, right_side):
    return contract(left_side, right_side, 1, 0)


def dot_turned(left_side, right_side):
    return contract(left_side, right_side, 1, 1)


def norm_parts(inputs):
    centered = inputs - jnp.mean(inputs, axis=-1, keepdims=True)
    inverse = lax.rsqrt(jnp.mean(centered * centered, axis=-1, keepdims=True) + EPSILON)
    return centered * inverse, inverse


def norm_back_parts(grad_output, normed, inverse, ln_gain):
    grad_normed = grad_output * ln_gain
    first_term = jnp.mean(grad_normed, axis=-1, keepdims=True)
    second_term = jnp.mean(grad_normed * normed, axis=-1, keepdims=True)
    return (
        inverse * (grad_normed - first_term - normed * second_term),
        jnp.sum(grad_output * normed, axis=0, keepdims=True),
        jnp.sum(grad_output, axis=0, keepdims=True),
    )


def erf_parts(inputs):
    decay = jnp.exp(-0.5 * inputs * inputs)
    share = 1.0 / (1.0 + jnp.abs(inputs) * (0.3275911 * 0.5**0.5))
    terms = [1.061405429, -1.453152027, 1.421413741, -0.284496736, 0.254829592]
    series = 0.5 * terms[0]
    for term in terms[1:]:
        series = series * share + 0.5 * term
    tail = series * share * decay
    return jnp.where(inputs >= 0.0, 1.0 - tail, tail), decay


def gelu_parts(inputs):
    below, decay = erf_parts(inputs)
    return inputs * below, below + inputs * decay * ((2.0 * 3.141592653589793) ** -0.5)


def gelu(inputs):
    return inputs * erf_parts(inputs)[0]


def layer_kernel(names, *refs):
    r = SimpleNamespace(**dict(zip(names, refs, strict=True)))
    core, chip, _, _ = place()
    me = core * CHIPS + chip
    here = (core, chip // LINES, chip % LINES)
    scale = HEAD ** (-0.5)
    depth, deep = WIDTH // CHIPS, WIDE // CHIPS
    sentences = TOKENS // LONG

    for j in range(TOKENS // 128):
        r.ids[j : j + 1, :] = jnp.concatenate(
            [r.token_ids[2 * j : 2 * j + 1, :], r.token_ids[2 * j + 1 : 2 * j + 2, :]], axis=1
        )
    r.ids[TOKENS // 128 : 8, :] = jnp.zeros((8 - TOKENS // 128, 128), jnp.int32)
    greet()
    ahead = (iota((TOKENS, TOKENS), 0) < iota((TOKENS, TOKENS), 1)).astype(LOW)
    r.embedded[...] = ahead
    mine = pl.ds(pl.multiple_of(chip * depth, 16), depth)
    for index, shard in enumerate([r.wq, r.wk, r.wv, r.wo]):
        r.wa[mine, index * WIDTH : (index + 1) * WIDTH] = shard[...]
    r.wb[mine, :] = r.wup[...]
    r.wc[pl.ds(pl.multiple_of(chip * deep, 16), deep), :] = r.wdown[...]
    r.every_ids[me] = r.ids[...]
    enter()

    def peer(step):
        other = lax.rem(me + step, DEVICES)
        return other, lax.div(other, CHIPS), lax.rem(other, CHIPS)

    def ids_copy(step):
        other, to_core, to_chip = peer(step)
        return remote(r.ids, r.every_ids.at[me], r.one_send.at[0], r.one_recv.at[0], to_core, to_chip)

    def all_but_one(ref, index):
        part = ref.at[0 : DEVICES - 1]
        return remote(part, part, r.one_send.at[index], r.one_recv.at[index], 1 - core, chip)

    every(1, DEVICES, lambda step: ids_copy(step).start())

    def block(ref, rows, columns):
        def piece(at, carried):
            return ref.at[
                pl.ds(pl.multiple_of(at * rows, 16), rows),
                pl.ds(pl.multiple_of(carried * columns, 128), columns),
            ]

        def many(count):
            return ref.at[0 : count * rows, 0:columns]

        return piece, many

    begin_a, moves_a, finish_a, drain_a = weight_steps(
        *block(r.wa, depth, 2 * WIDTH), r.weight_send.at[0], r.weight_recv.at[0]
    )
    begin_b, moves_b, finish_b, drain_b = weight_steps(
        *block(r.wb, depth, WIDE // 2), r.weight_send.at[1], r.weight_recv.at[1]
    )
    begin_c, moves_c, finish_c, drain_c = weight_steps(
        *block(r.wc, deep, WIDTH // 2), r.weight_send.at[2], r.weight_recv.at[2]
    )
    begin_a()
    begin_b()

    def move(*steps):
        for moves, first_step in steps:
            moves[first_step]()
            moves[first_step + 1]()

    all_but_one(r.every_ids, 0).wait_recv()
    all_ids = jnp.concatenate([r.every_ids[:, j, :] for j in range(TOKENS // 128)], axis=1)
    all_owner = over(all_ids, VOCAB_ROWS)
    asked = all_owner == me
    ranks = dot(asked.astype(LOW), r.embedded[...])
    r.rank[...] = jnp.where(asked, ranks, -1.0)
    local_row = (all_ids - all_owner * VOCAB_ROWS + 1).astype(FULL)
    r.code[...] = local_row + (over(iota((DEVICES, TOKENS), 1), LONG) * 2048).astype(FULL)

    quarter_size = DEVICES // 4

    def rows_copy(other, quarter):
        return remote(
            r.rows.at[:, pl.ds(pl.multiple_of(other * PAD, 16), PAD), :],
            r.replies.at[:, pl.ds(pl.multiple_of(me * PAD, 16), PAD), :],
            r.rows_send.at[quarter],
            r.rows_recv.at[quarter],
            lax.div(other, CHIPS),
            lax.rem(other, CHIPS),
        )

    def rows_of(quarter):
        count = quarter_size - 1 if quarter == 3 else quarter_size
        part = r.replies.at[:, 0 : count * PAD, :]
        return remote(
            part, part, r.rows_send.at[quarter], r.rows_recv.at[quarter], 1 - core, chip
        )

    def pick(source):
        rank = r.rank[pl.ds(source, 1), :]
        code = r.code[pl.ds(source, 1), :]
        here_at = iota((CAPACITY, TOKENS), 0).astype(FULL) == rank
        found = jnp.sum(jnp.where(here_at, code, 0.0), axis=1, keepdims=True)
        sent = jnp.floor(found * (1.0 / 2048))
        row = found - sent * 2048.0 - 1.0
        chosen = (iota((CAPACITY, VOCAB_ROWS), 1).astype(FULL) == row).astype(LOW)
        at = pl.ds(pl.multiple_of(source * PAD, 16), PAD)
        source_sent = sent + (source * PAD).astype(FULL)
        for group in range(GROUPS):
            part = slice(group * PAD, (group + 1) * PAD)
            r.chosen[group, at, :] = chosen[part]
            r.found[group, at, 0:1] = row[part]
            r.found[group, at, 1:2] = source_sent[part]

    def quarter_rows(quarter):
        now = lax.rem(lax.div(me, quarter_size) + 1 + quarter, 4)

        def pick_two(index):
            pick(now * quarter_size + 2 * index)
            pick(now * quarter_size + 2 * index + 1)

        every(0, quarter_size // 2, pick_two)
        span = pl.ds(pl.multiple_of(now * quarter_size * PAD, 128), quarter_size * PAD)
        for start in range(0, WIDTH, BLOCK):
            lanes = slice(start, start + BLOCK)
            picked = r.chosen[:, span, :].reshape(GROUPS * quarter_size * PAD, VOCAB_ROWS)
            found_rows = dot(picked, r.table[:, lanes]).astype(LOW)
            r.rows[:, span, lanes] = found_rows.reshape(GROUPS, quarter_size * PAD, BLOCK)

        def send(index):
            other = now * quarter_size + lax.rem(lax.rem(me, quarter_size) + index, quarter_size)
            rows_copy(other, quarter).start()

        every(lax.div(quarter, 3), quarter_size, send)
        pl.when(quarter == 0)(partial(move, (moves_a, 0)))
        pl.when(quarter == 1)(partial(move, (moves_b, 0)))
        pl.when(quarter == 2)(partial(move, (moves_a, 2)))
        pl.when(quarter == 3)(partial(move, (moves_b, 2)))

    every(0, 4, quarter_rows)
    begin_c()
    own_at = pl.ds(pl.multiple_of(me * PAD, 16), PAD)
    r.replies[:, own_at, :] = r.rows[:, own_at, :]

    move((moves_a, 4))

    small_here = pl.ds(pl.multiple_of(chip * 128, 128), 128)
    lines = [r.bq, r.bv, r.bo, r.g1, r.s1, r.bdown, r.g2, r.s2]
    lines = [line[...].reshape(1, depth).astype(FULL) for line in lines]
    up_line = r.bup[...].reshape(1, deep).astype(FULL)
    lines += [up_line[:, part * depth : (part + 1) * depth] for part in range(deep // depth)]
    lines.append(jnp.zeros((PAD - len(lines), depth), FULL))
    own_small = jnp.concatenate(lines, axis=0)
    own_small = jnp.concatenate([own_small, jnp.zeros((PAD, 128 - depth), FULL)], axis=1)
    r.smalls[:, small_here] = own_small.astype(LOW)

    def small_copy(step):
        part = r.smalls.at[:, small_here]
        to_chip = lax.rem(chip + step, CHIPS)
        return remote(part, part, r.small_send.at[0], r.small_recv.at[0], core, to_chip)

    def all_smalls():
        part = r.smalls.at[:, 0 : (CHIPS - 1) * 128]
        return remote(part, part, r.small_send.at[0], r.small_recv.at[0], 1 - core, chip)

    every(1, CHIPS, lambda step: small_copy(step).start())
    move((moves_b, 4))

    own_row = jnp.concatenate([r.ids[j : j + 1, :] for j in range(TOKENS // 128)], axis=1)
    owner_row = over(own_row, VOCAB_ROWS).astype(FULL)
    owner_col = as_column(owner_row)
    earlier = (owner_row == owner_col) & (iota((TOKENS, TOKENS), 1) < iota((TOKENS, TOKENS), 0))
    own_rank = jnp.sum(earlier.astype(FULL), axis=1, keepdims=True)
    own_group = jnp.floor(own_rank * (1.0 / PAD))
    own_slot = own_group * SLOT_ROWS + owner_col * PAD + (own_rank - own_group * PAD)
    r.slot_col[...] = own_slot
    r.slot_line[0:1, :] = as_row(own_slot)
    move((moves_a, 6), (moves_c, 0))

    at_sent = over(iota((1, TOKENS), 1), LONG)
    lens = jnp.concatenate(
        [r.lens[...].reshape(1, sentences).astype(FULL), jnp.zeros((1, PAD - sentences), FULL)],
        axis=1,
    )
    spread_lens = dot(
        jnp.broadcast_to(lens, (8, PAD)).astype(LOW),
        (iota((PAD, TOKENS), 0) == over(iota((PAD, TOKENS), 1), LONG)).astype(LOW),
    )[0:1]
    valid_row = ((iota((1, TOKENS), 1) - at_sent * LONG).astype(FULL) < spread_lens).astype(FULL)
    r.valid_line[0:1, :] = valid_row
    r.valid_col[...] = as_column(valid_row)
    half_block = BLOCK // 2
    stacked_shape = (4 * half_block, half_block)
    same = within(over(iota(stacked_shape, 0), LONG), 2) == over(iota(stacked_shape, 1), LONG)
    r.block_bias[...] = jnp.where(same, 0.0, MASK_FLOOR)
    r.valid_bias[0:1, :] = (1.0 - valid_row) * MASK_FLOOR

    slots = r.slots[...].reshape(1, DEVICES * sentences)
    gap = jnp.full((1, PAD - sentences), -2, jnp.int32)
    slot_line = jnp.concatenate(
        [
            part
            for device in range(DEVICES)
            for part in (slots[:, device * sentences : (device + 1) * sentences], gap)
        ],
        axis=1,
    )
    side_line = within(slot_line, 2) + jnp.where(slot_line < 0, 8, 0)
    pair_line = over(slot_line, 2)
    pairs = r.langs.shape[0]
    lang_line = r.langs[...].reshape(1, pairs).astype(FULL)
    lang_line = jnp.concatenate([lang_line, jnp.full((1, -pairs % 128), -1.0, FULL)], axis=1)
    lang_col = as_column(lang_line)
    same_lang = jnp.sum(jnp.where(lang_col == lang_line, 1.0, 0.0), axis=1, keepdims=True)
    per_pair = 1.0 / (2.0 * LANGS * same_lang)
    at_pair = iota((lang_line.shape[1], SLOT_ROWS), 0) == pair_line
    weight_line = jnp.sum(jnp.where(at_pair, per_pair, 0.0), axis=0, keepdims=True)
    r.pairs[0:1, :] = weight_line
    r.pairs[1:2, :] = pair_line.astype(FULL)
    r.pairs[2:3, :] = side_line.astype(FULL)
    r.pairs_col[:, 0:1] = as_column(weight_line)
    r.pairs_col[:, 1:2] = as_column(pair_line.astype(FULL))
    r.pairs_col[:, 2:3] = as_column(side_line.astype(FULL))
    move((moves_b, 6), (moves_c, 2))

    all_smalls().wait_recv()
    smalls = r.smalls[...].astype(FULL)
    r.vectors[:, 0:WIDTH] = jnp.concatenate(
        [smalls[:, at * 128 : at * 128 + depth] for at in range(CHIPS)], axis=1
    )
    r.up_bias[0:1, :] = jnp.concatenate(
        [
            smalls[8 + part : 9 + part, at * 128 : at * 128 + depth]
            for at in range(CHIPS)
            for part in range(deep // depth)
        ],
        axis=1,
    )

    def vector(index):
        return r.vectors[index : index + 1, :]

    r.qkv_bias[0:1, 0:WIDTH] = vector(0)
    r.qkv_bias[0:1, WIDTH : 2 * WIDTH] = jnp.zeros((1, WIDTH), FULL)
    r.qkv_bias[0:1, 2 * WIDTH : 3 * WIDTH] = vector(1)

    move((moves_a, 8), (moves_b, 8), (moves_c, 4))

    def first_row(source):
        code = jnp.where(r.rank[pl.ds(source, 1), :] >= 0.0, r.code[pl.ds(source, 1), :], 0.0)
        at_first = iota((PAD, TOKENS), 1) == iota((PAD, TOKENS), 0) * LONG
        found = jnp.sum(jnp.where(at_first, code, 0.0), axis=1, keepdims=True)
        row = found - jnp.floor(found * (1.0 / 2048)) * 2048.0 - 1.0
        r.found[GROUPS, pl.ds(pl.multiple_of(source * PAD, 16), PAD), 0:1] = row

    every(0, DEVICES, first_row)
    for group in range(GROUPS + 1):
        named = as_row(r.found[group, :, 0:1])
        by_row = iota((VOCAB_ROWS, SLOT_ROWS), 0).astype(FULL) == named
        r.by_row[:, group * SLOT_ROWS : (group + 1) * SLOT_ROWS] = by_row.astype(LOW)

    def order(tile):
        at = pl.ds(pl.multiple_of(tile * BLOCK, BLOCK), BLOCK)
        lanes = iota((BLOCK, GROUPS * SLOT_ROWS), 1).astype(FULL)
        r.qkv[at, 0 : GROUPS * SLOT_ROWS] = (r.slot_col[at, :] == lanes).astype(LOW)

    every(0, TOKENS // BLOCK, order)
    for group in range(GROUPS):
        slot_at = iota((SLOT_ROWS, TOKENS), 0) + group * SLOT_ROWS
        named = (slot_at.astype(FULL) == r.slot_line[0:1, :]).astype(LOW)
        r.slot_hot[group] = named
    moves_a[10]()
    moves_b[10]()
    finish_a()
    for quarter in range(4):
        rows_of(quarter).wait_recv()

    def embed(tile):
        at = pl.ds(pl.multiple_of(tile * BLOCK, BLOCK), BLOCK)
        replies = r.replies[:, :, at].reshape(GROUPS * SLOT_ROWS, BLOCK)
        r.embedded[:, at] = dot(r.qkv[:, 0 : GROUPS * SLOT_ROWS], replies).astype(LOW)

    every(0, WIDTH // BLOCK, embed)

    def project(tile):
        at = pl.ds(pl.multiple_of(tile * BLOCK, BLOCK), BLOCK)
        r.qkv[:, at] = (dot(r.embedded[...], r.wa[:, at]) + r.qkv_bias[0:1, at]).astype(LOW)

    move((moves_c, 6))
    every(0, 9, project)

    row_sent = within(iota((PAIR_ROWS, WIDTH), 0), PAD)
    row_head = over(iota((PAIR_ROWS, WIDTH), 0), PAD)
    lane_block = over(iota((PAIR_ROWS, WIDTH), 1), HEAD)
    in_head = row_head == lane_block
    seen = (row_sent == lane_block) & (r.valid_line[0:1, :] > 0.0)
    firsts = (iota((PAD, TOKENS), 1) == iota((PAD, TOKENS), 0) * LONG).astype(LOW)
    real_row = iota((PAD, 1), 0) < sentences

    def spread(rows):
        return jnp.where(in_head, jnp.concatenate([rows] * HEADS, axis=0), jnp.zeros((), LOW))

    def fold(tall):
        tall = jnp.where(in_head, tall, 0.0)
        return sum(tall[head * PAD : (head + 1) * PAD] for head in range(HEADS))

    keys, values = slice(WIDTH, 2 * WIDTH), slice(2 * WIDTH, 3 * WIDTH)
    embedded_cls = dot(firsts, r.embedded[...]).astype(LOW)
    query_cls = (dot(embedded_cls, r.wa[:, 0:WIDTH]) + vector(0)).astype(LOW)
    cls_scores = dot_turned(spread(query_cls), r.qkv[:, keys]) * scale
    cls_scores = jnp.where(seen, cls_scores, MASK_FLOOR)
    cls_peak = jnp.max(cls_scores, axis=1, keepdims=True)
    cls_exp = jnp.where(seen, jnp.exp(cls_scores - cls_peak), 0.0)
    cls_total = jnp.sum(cls_exp, axis=1, keepdims=True)
    cls_probs = cls_exp / jnp.where(cls_total > 0.0, cls_total, 1.0)
    probs_low = cls_probs.astype(LOW)
    r.probs[...] = cls_probs
    context_cls = fold(dot(probs_low, r.qkv[:, values])).astype(LOW)
    first_cls = (
        embedded_cls.astype(FULL)
        + dot(context_cls, r.wa[:, 3 * WIDTH : 4 * WIDTH])
        + vector(2)
    )
    normed_one, inverse_one = norm_parts(first_cls)
    r.normed_one[...] = normed_one
    hidden_cls = normed_one * vector(3) + vector(4)
    hidden_cls_low = hidden_cls.astype(LOW)
    early_here = r.early.at[here]
    early_here[:, 0:WIDTH] = hidden_cls_low
    early_here[:, WIDTH : 2 * WIDTH] = query_cls
    steps_u, drain_u = gather_steps(r.units, r.gather_send.at[0], r.gather_recv.at[0])
    steps_e, drain_e = gather_steps(r.early, r.gather_send.at[1], r.gather_recv.at[1])
    steps_d, drain_d = gather_steps(r.downs, r.gather_send.at[2], r.gather_recv.at[2])
    steps_a, drain_a2 = gather_steps(r.attends, r.gather_send.at[3], r.gather_recv.at[3])
    steps_q, drain_q = gather_steps(r.queries, r.gather_send.at[4], r.gather_recv.at[4])
    steps_e[0]()

    def attend(unit):
        rows = pl.ds(pl.multiple_of(unit * half_block, half_block), half_block)
        lane_head = over(iota((half_block, BLOCK), 1), HEAD)
        bias = r.block_bias[...] + r.valid_bias[0:1, rows]

        def part(which, lane):
            return r.qkv[rows, which * WIDTH + lane : which * WIDTH + lane + BLOCK]

        for lane in range(0, WIDTH, BLOCK):
            query = part(0, lane) * jnp.asarray(scale, LOW)
            key, value = part(1, lane), part(2, lane)
            stacked = jnp.concatenate(
                [jnp.where(lane_head == head, query, jnp.zeros((), LOW)) for head in range(4)],
                axis=0,
            )
            scores = dot_turned(stacked, key) + bias
            shifted = jnp.exp(scores - jnp.max(scores, axis=1, keepdims=True))
            probs = shifted * (1.0 / jnp.sum(shifted, axis=1, keepdims=True))
            mixed = dot(probs.astype(LOW), value)
            result = mixed[0:half_block]
            for head in range(1, 4):
                result = jnp.where(
                    lane_head == head, mixed[head * half_block : (head + 1) * half_block], result
                )
            r.context[rows, lane : lane + BLOCK] = result.astype(LOW)

    def open_tile(tile):
        at = pl.ds(pl.multiple_of(tile * BLOCK, BLOCK), BLOCK)
        attended = dot(r.context[at, :], r.wa[:, 3 * WIDTH : 4 * WIDTH]) + vector(2)
        normed, _ = norm_parts(r.embedded[at, :].astype(FULL) + attended)
        hidden = normed * vector(3) + vector(4)
        r.context[at, :] = hidden.astype(LOW)
        r.table_full[at, :] = hidden + vector(5)

    most = SLOT_ROWS
    rest_at = pl.ds(most, TOKENS - most)

    def up_product(part):
        at = pl.ds(pl.multiple_of(part * BLOCK, BLOCK), BLOCK)
        return dot(r.context[...], r.wb[:, at]) + r.up_bias[0:1, at]

    def feed_up(part, last=False):
        active = gelu(r.tile_up[...]).astype(LOW)
        if not last:
            r.tile_up[...] = up_product(part + 1)
        lanes = pl.ds(pl.multiple_of(lax.rem(part, 4) * BLOCK, BLOCK), BLOCK)
        r.chosen[lax.div(part, 4), :, lanes] = active[:most]
        rest = pl.ds(pl.multiple_of(lax.div(part, 6) * BLOCK, BLOCK), BLOCK)
        lanes = pl.ds(pl.multiple_of(lax.rem(part, 6) * BLOCK, BLOCK), BLOCK)
        r.slopes[rest, lanes] = active[most:]

    def feed_down(part):
        lanes = pl.ds(pl.multiple_of(part * BLOCK, BLOCK), BLOCK)
        total = r.table_full[0:most, lanes]
        for group in range(GROUPS):
            rows = slice(group * VOCAB_ROWS, (group + 1) * VOCAB_ROWS)
            total = total + dot(r.chosen[group], r.wc[rows, lanes])
        r.table_full[0:most, lanes] = total

    def feed_rest(part):
        lanes = pl.ds(pl.multiple_of(part * BLOCK, BLOCK), BLOCK)
        low_part = dot(r.slopes[0:BLOCK, :], r.wc[0 : WIDE // 2, lanes])
        high_part = dot(r.slopes[BLOCK : 2 * BLOCK, :], r.wc[WIDE // 2 :, lanes])
        r.table_full[rest_at, lanes] += low_part + high_part

    def layer_copy(tile):
        at = pl.ds(pl.multiple_of(tile * BLOCK, BLOCK), BLOCK)
        return pltpu.make_async_copy(r.context.at[at], r.layer_out.at[at], r.out_sem.at[tile])

    def close_tile(tile):
        at = pl.ds(pl.multiple_of(tile * BLOCK, BLOCK), BLOCK)
        normed, _ = norm_parts(r.table_full[at, :])
        out = normed * vector(6) + vector(7)
        r.context[at, :] = (out * r.valid_col[at, :]).astype(LOW)
        layer_copy(tile).start()

    finish_b()
    r.hidden_cls[...] = hidden_cls_low

    def up_part(part):
        at = pl.ds(pl.multiple_of(part * WIDTH, BLOCK), WIDTH)
        active, slope = gelu_parts(dot(r.hidden_cls[...], r.wb[:, at]) + r.up_bias[0:1, at])
        r.active_cls[:, at] = active.astype(LOW)
        r.slope_cls[:, at] = slope

    every(0, WIDE // WIDTH, up_part)
    steps_e[1]()

    def attend_step(unit):
        attend(unit)
        pl.when(unit == 1)(partial(move, (moves_c, 8)))
        pl.when(unit == 3)(moves_c[10])
        pl.when(unit == 4)(steps_e[2])

    every(0, 6, attend_step)
    finish_c()

    def pack_tall(target, first_row, act):
        def run(part):
            window = jnp.minimum(lax.div(part * 2 * depth, 128) * 128, WIDTH - BLOCK)
            shape = (BLOCK, BLOCK)
            lane = within(iota(shape, 1), 128)
            column = over(iota(shape, 1), 128) * depth + lane + (part * 2 * depth - window)
            select = ((iota(shape, 0) == column) & (lane < depth)).astype(LOW)
            taken = dot(r.tall[:, pl.ds(pl.multiple_of(window, 128), BLOCK)], select)

            def beside(low, high):
                return [
                    low[:, one * 128 : (one + 1) * 128]
                    + pltpu.roll(high[:, one * 128 : (one + 1) * 128], depth, 1)
                    for one in range(2)
                ]

            for half in range(CORES):
                base = half * PAIR_ROWS // 2
                both = beside(taken[base : base + 48], taken[base + 48 : base + 96])
                for one in range(2):
                    at = half * CHIPS + 2 * part + one
                    target[at, first_row : first_row + 48, :] = act(
                        2 * part + one, both[one]
                    ).astype(LOW)
            if first_row:
                left = beside(taken[PAIR_ROWS : PAIR_ROWS + PAD], taken[PAIR_ROWS + PAD :])
                for half in range(CORES):
                    for one in range(2):
                        target[half * CHIPS + 2 * part + one, 0:PAD, :] = left[one].astype(LOW)

        return run

    def pack_coefs(coefs):
        shape = (PAIR_ROWS, GROUPS * 128)
        folds = over(iota(shape, 0), PAD) + over(iota(shape, 1), 128) * PAD == within(
            iota(shape, 1), 128
        )
        lanes = contract(coefs, folds.astype(LOW), 0, 0).astype(LOW)
        total = None
        for group in range(GROUPS):
            part = dot(r.slot_hot[group], lanes[:, group * 128 : (group + 1) * 128])
            total = part if total is None else total + part
        return total.astype(LOW).reshape(DEVICES, PAD, 128)


    def down_part(part):
        at = pl.ds(pl.multiple_of(part * BLOCK, BLOCK), BLOCK)
        r.wide_cls[:, at] = dot(r.active_cls[...], r.wc[:, at])

    every(0, WIDTH // BLOCK, down_part)
    down_pre = r.wide_cls[:, 0:WIDTH] + vector(5)
    normed_two, inverse_two = norm_parts(hidden_cls + down_pre)
    summary = normed_two * vector(6) + vector(7)
    magnitude = jnp.sqrt(jnp.sum(summary * summary, axis=-1, keepdims=True) + EPSILON)
    unit = jnp.where(real_row, summary / magnitude, 0.0)
    r.units[here] = unit.astype(LOW)

    steps_u[0]()
    r.tall[0:PAIR_ROWS, :] = dot(probs_low, r.embedded[...]).astype(LOW)
    r.tall[PAIR_ROWS : PAIR_ROWS + PAD, :] = context_cls
    r.tall[PAIR_ROWS + PAD :, :] = embedded_cls
    pack_one = pack_tall(r.mail_one, PAD, lambda at, both: both)

    def pack_one_step(part):
        pack_one(part)
        pl.when(part == 0)(steps_u[1])
        pl.when(part == 4)(steps_u[2])

    every(0, CHIPS // 2, pack_one_step)
    r.mail_one[:, 64:80, :] = pack_coefs(probs_low)
    steps_u[3]()

    def post_one(box, got, index, step):
        other, to_core, to_chip = peer(step)
        remote(
            box.at[other], got.at[me], r.one_send.at[index], r.one_recv.at[index], to_core, to_chip
        ).start()

    r.got_one[me] = r.mail_one[me]

    def open_step(tile):
        open_tile(tile)
        pl.when(tile == 0)(steps_e[3])
        pl.when(tile == 2)(steps_u[4])

    def feed_step(steps, part):
        feed_up(part)
        for index in range(6):
            step = 6 * part + index + 1
            pl.when(step < DEVICES)(partial(post_one, r.mail_one, r.got_one, 1, step))
        for index, step in steps:
            pl.when(part == index)(step)

    first_parts, parts = 6, WIDE // BLOCK
    every(0, TOKENS // BLOCK, open_step)
    r.tile_up[...] = up_product(0)
    every(0, first_parts, partial(feed_step, [(1, steps_u[5]), (2, steps_e[4]), (5, steps_e[5])]))

    units = r.units[...].reshape(SLOT_ROWS, WIDTH)
    weight_row, pair_row, side_row = r.pairs[0:1, :], r.pairs[1:2, :], r.pairs[2:3, :]

    def pair_scores(rows, pair_col, side_col):
        opposite = side_col + side_row == 1.0
        partner = opposite & (pair_col == pair_row)
        raw = SCORE_SCALE * dot_turned(rows, units)
        shifted = jnp.where(partner, raw - SCORE_SCALE * MARGIN_WIDTH, raw)
        return jnp.where(opposite, shifted, MASK_FLOOR), partner

    every_score, every_partner = pair_scores(
        units, r.pairs_col[:, 1:2], r.pairs_col[:, 2:3]
    )
    peak_row = jnp.max(every_score, axis=0, keepdims=True)
    log_row = peak_row + jnp.log(
        jnp.sum(jnp.exp(every_score - peak_row), axis=0, keepdims=True)
    )
    picked_row = jnp.sum(jnp.where(every_partner, every_score, 0.0), axis=0, keepdims=True)
    r.loss[...] = jnp.sum(weight_row * (log_row - picked_row), axis=1, keepdims=True)

    rows_here = pl.ds(pl.multiple_of(me * PAD, 16), PAD)
    own_score, own_partner = pair_scores(
        r.units[here], r.pairs_col[rows_here, 1:2], r.pairs_col[rows_here, 2:3]
    )
    own_partner = own_partner.astype(FULL)
    own_peak = jnp.max(own_score, axis=1, keepdims=True)
    own_exp = jnp.exp(own_score - own_peak)
    own_share = own_exp / jnp.sum(own_exp, axis=1, keepdims=True)
    by_row = (r.pairs_col[rows_here, 0:1] * (own_share - own_partner)).astype(LOW)
    by_column = (weight_row * (jnp.exp(own_score - log_row) - own_partner)).astype(LOW)
    unit_grad = SCORE_SCALE * (dot(by_row, units) + dot(by_column, units))
    along = jnp.sum(unit * unit_grad, axis=-1, keepdims=True)
    summary_grad = (unit_grad - unit * along) / magnitude

    residual_grad, grad_g2, grad_s2 = norm_back_parts(
        summary_grad, normed_two, inverse_two, vector(6)
    )
    down_grad = residual_grad.astype(LOW)
    r.downs[here] = down_grad
    steps_d[0]()
    r.hidden_cls[...] = down_grad

    def up_back(part):
        at = pl.ds(pl.multiple_of(part * WIDTH, BLOCK), WIDTH)
        act_grad = dot_turned(r.hidden_cls[...], r.wc[at, :])
        r.active_cls[:, at] = (act_grad * r.slope_cls[:, at]).astype(LOW)

    every(0, WIDE // WIDTH, up_back)
    steps_d[1]()

    def hidden_back(part):
        at = pl.ds(pl.multiple_of(part * BLOCK, BLOCK), BLOCK)
        r.wide_cls[:, at] = dot_turned(r.active_cls[...], r.wb[at, :])

    every(0, WIDTH // BLOCK, hidden_back)
    hidden_grad = r.wide_cls[:, 0:WIDTH] + residual_grad
    first_grad, grad_g1, grad_s1 = norm_back_parts(
        hidden_grad, r.normed_one[...], inverse_one, vector(3)
    )
    attend_grad = first_grad.astype(LOW)
    context_grad = dot_turned(attend_grad, r.wa[:, 3 * WIDTH : 4 * WIDTH]).astype(LOW)
    attend_here = r.attends.at[here]
    attend_here[:, 0:WIDTH] = attend_grad
    attend_here[:, WIDTH : 2 * WIDTH] = context_grad
    steps_a[0]()
    steps_d[2]()
    context_tall = spread(context_grad)
    probs = r.probs[...]
    prob_grad = dot_turned(context_tall, r.qkv[:, values])
    inner = jnp.sum(probs * prob_grad, axis=1, keepdims=True)
    score_grad = (probs * (prob_grad - inner)).astype(LOW)
    steps_a[1]()
    r.mail_two[:, 48:64, :] = pack_coefs(score_grad)
    r.got_two[me, 48:64, :] = r.mail_two[me, 48:64, :]
    query_grad = (fold(dot(score_grad, r.qkv[:, keys])) * scale).astype(LOW)
    probs_total = jnp.sum(probs_low.astype(FULL), axis=1, keepdims=True)
    grad_bvalue = jnp.sum(probs_total * context_tall.astype(FULL), axis=0, keepdims=True)
    grad_bquery = jnp.sum(query_grad.astype(FULL), axis=0, keepdims=True)
    r.queries[here] = query_grad
    own_sums = jnp.concatenate(
        [jnp.zeros((2 * depth, WIDTH), FULL)]
        + [grad_bquery, grad_bvalue, grad_g1, grad_s1, grad_g2, grad_s2]
        + [jnp.zeros((128 - 2 * depth - 6, WIDTH), FULL)],
        axis=0,
    )
    r.own_sums[...] = jnp.transpose(own_sums)
    steps_q[0]()
    steps_a[2]()
    r.tall[0:PAIR_ROWS, :] = (dot(score_grad, r.embedded[...]) * scale).astype(LOW)

    def with_sums(at, both):
        return both + r.own_sums[pl.ds(pl.multiple_of(at * depth, 16), depth), :]

    pack_two = pack_tall(r.mail_two, 0, with_sums)

    def pack_two_step(step):
        part = lax.rem(step + lax.div(me, 4), CHIPS // 2)
        pack_two(part)
        for index in range(4):
            turn = lax.rem(index + me, 4)
            at = lax.div(turn, 2) * CHIPS + 2 * part + lax.rem(turn, 2)
            pl.when(at != me)(
                partial(post_one, r.mail_two, r.got_two, 2, lax.rem(at + DEVICES - me, DEVICES))
            )

    every(0, CHIPS // 2, pack_two_step)
    r.got_two[me, 0:48, :] = r.mail_two[me, 0:48, :]
    steps_q[1]()

    def all_rows(buffer, start, width=WIDTH):
        return buffer[:, :, :, :, start : start + width].reshape(SLOT_ROWS, width)

    quarter_rows_count = quarter_size * PAD

    def from_sent(quarter):
        span = pl.ds(pl.multiple_of(quarter * quarter_rows_count, 128), quarter_rows_count)
        shape = (GROUPS * quarter_rows_count, quarter_rows_count)
        lanes = (iota(shape, 1) + quarter * quarter_rows_count).astype(FULL)
        named = r.found[0:GROUPS, span, 1:2].reshape(GROUPS * quarter_rows_count, 1)
        return (named == lanes).astype(LOW), span

    def quarter_part(buffer, quarter, start):
        planes = pl.ds(lax.rem(quarter, 2) * 2, 2)
        part = buffer[lax.div(quarter, 2), planes, :, :, start : start + BLOCK]
        return part.reshape(quarter_rows_count, BLOCK)

    def widened(coefs, group, start):
        lanes = iota((128, BLOCK), 0) == over(iota((128, BLOCK), 1) + start, HEAD) + group * PAD
        return dot(coefs, lanes.astype(LOW))

    half_wide = WIDE // 2

    def slope_tile(part):
        at = pl.ds(pl.multiple_of(core * half_wide + part * BLOCK, BLOCK), BLOCK)
        up_pre = dot(all_rows(r.early, 0), r.wb[:, at]) + r.up_bias[0:1, at]
        _, slope = gelu_parts(up_pre)
        r.slopes[:, pl.ds(pl.multiple_of(part * BLOCK, BLOCK), BLOCK)] = slope.astype(LOW)

    def slot_queries(quarter):
        sents, span = from_sent(quarter)
        for start in range(0, WIDTH, BLOCK):
            rows = dot(sents, quarter_part(r.early, quarter, WIDTH + start)).astype(LOW)
            rows = rows.reshape(GROUPS, quarter_rows_count, BLOCK)
            r.slot_query[:, span, start : start + BLOCK] = rows

    def activate():
        at = pl.ds(pl.multiple_of(chip // 2 * 2 * deep, 128), 2 * deep)
        up_pre = dot(all_rows(r.early, 0), r.wb[:, at]) + r.up_bias[0:1, at]
        r.active_turned[...] = jnp.transpose(gelu(up_pre)).astype(LOW)
        r.hidden_turned[...] = jnp.transpose(all_rows(r.early, 0))

    rest = [steps_d[3], steps_a[3], steps_q[2], steps_d[4], steps_a[4]]
    rest = [(first_parts + index, step) for index, step in enumerate(rest)]
    every(first_parts, parts - 1, partial(feed_step, rest))
    feed_up(parts - 1, last=True)

    def rest_step(part):
        feed_rest(part)
        for index, step in enumerate([steps_q[3], steps_d[5], steps_a[5]]):
            pl.when(part == index)(step)

    every(0, WIDTH // BLOCK, rest_step)
    steps_q[4]()

    def down_step(part):
        feed_down(part)
        for index, ends in enumerate([[drain_a, drain_b], [drain_c, drain_u], [drain_e]]):
            for end in ends:
                pl.when(part == index)(end)

    every(0, WIDTH // BLOCK, down_step)
    every(0, TOKENS // BLOCK, close_tile)
    every(0, 4, slot_queries)
    every(0, 6, slope_tile)
    activate()

    all_but_one(r.got_one, 1).wait_recv()
    def slot_probs(group):
        got_probs = r.got_one[:, 64:80, :].reshape(SLOT_ROWS, 128)
        for start in range(0, WIDTH, BLOCK):
            r.replies[group, :, start : start + BLOCK] = widened(got_probs, group, start).astype(LOW)

    def slot_values(quarter):
        sents, span = from_sent(quarter)
        for start in range(0, WIDTH, BLOCK):
            lanes = slice(start, start + BLOCK)
            rows = dot(sents, quarter_part(r.attends, quarter, WIDTH + start))
            rows = rows.reshape(GROUPS, quarter_rows_count, BLOCK)
            rows = r.replies[:, span, lanes].astype(FULL) * rows
            r.replies[:, span, lanes] = rows.astype(LOW)

    every(0, GROUPS, slot_probs)
    every(0, 4, slot_values)

    def head_products(got, first_row, right, start, target):
        def one_head(head):
            lane = core * (WIDTH // 2) + lax.div(head, 2) * 128
            pair_rows = right[:, :, :, :, pl.ds(pl.multiple_of(start + lane, 128), 128)]
            row = pl.ds(pl.multiple_of(first_row + lax.rem(head, 3) * PAD, 16), PAD)
            block_rows = got[:, row, :].reshape(SLOT_ROWS, 128)
            r.product[...] = contract(block_rows, pair_rows.reshape(SLOT_ROWS, 128), 0, 0)
            part = r.product[pl.ds(pl.multiple_of(lax.div(head, 3) * depth, 16), depth), :]
            at = pl.ds(pl.multiple_of(lane, 128), 128)
            own_lanes = over(iota((depth, 128), 1), HEAD) == lax.rem(head, 2)
            target[:, at] = jnp.where(own_lanes, part, target[:, at])

        every(0, HEADS // 2, one_head)

    def half_of(ref, at_core):
        half = ref.shape[1] // 2
        return ref.at[:, pl.ds(pl.multiple_of(at_core * half, 128), half)]

    def half_copy(index, ref, at_core):
        part = half_of(ref, at_core)
        return remote(part, part, r.half_send.at[index], r.half_recv.at[index], 1 - core, chip)

    own_half = pl.ds(pl.multiple_of(core * (WIDTH // 2), 128), WIDTH // 2)
    r.g_wv[:, own_half] = jnp.zeros((depth, WIDTH // 2), FULL)
    r.g_wk[:, own_half] = jnp.zeros((depth, WIDTH // 2), FULL)
    head_products(r.got_one, PAD, r.attends, WIDTH, r.g_wv)
    half_copy(0, r.g_wv, core).start()

    downs = r.downs[...].reshape(SLOT_ROWS, WIDTH)
    attends = all_rows(r.attends, 0)

    def up_tile(part):
        at = pl.ds(pl.multiple_of(core * half_wide + part * BLOCK, BLOCK), BLOCK)
        slope = r.slopes[:, pl.ds(pl.multiple_of(part * BLOCK, BLOCK), BLOCK)].astype(FULL)
        up_all = (dot_turned(r.downs[...].reshape(SLOT_ROWS, WIDTH), r.wc[at, :]) * slope)
        up_all = up_all.astype(LOW)
        r.g_wup[0:depth, at] = dot(r.hidden_turned[mine, :], up_all)
        total = jnp.sum(up_all.astype(FULL), axis=0, keepdims=True)
        r.g_wup[depth : depth + 8, at] = jnp.broadcast_to(total, (8, BLOCK))

    every(0, half_wide // BLOCK, up_tile)
    half_copy(1, r.g_wup, core).start()
    r.g_wdown[...] = dot(r.active_turned[pl.ds(pl.multiple_of(chip % 2 * deep, 16), deep), :], downs)
    r.left_turned[...] = jnp.transpose(r.got_one[:, 0:PAD, :].reshape(SLOT_ROWS, 128))
    r.g_wo[...] = dot(r.left_turned[0:depth, :], attends)

    def own_part(rows, size):
        start = chip * size
        window = jnp.minimum(lax.div(start, 128) * 128, rows.shape[1] - BLOCK)
        part = rows[:, pl.ds(pl.multiple_of(window, 128), BLOCK)]
        return pltpu.roll(part, lax.rem(BLOCK + window - start, BLOCK), 1)

    for quarter in range(4):
        rows_of(quarter).wait_send()
    all_but_one(r.got_two, 2).wait_recv()

    def slot_grads(group):
        got_scores = r.got_two[:, 48:64, :].reshape(SLOT_ROWS, 128)
        for start in range(0, WIDTH, BLOCK):
            lanes = slice(start, start + BLOCK)
            rows = r.slot_query[group, :, lanes].astype(FULL)
            rows = widened(got_scores, group, start) * rows * scale
            r.slot_query[group, :, lanes] = rows.astype(LOW)
        for start in range(0, WIDTH, BLOCK):
            lanes = slice(start, start + BLOCK)
            row_grad = dot_turned(r.slot_query[group], r.wa[lanes, keys])
            row_grad = row_grad + dot_turned(r.replies[group], r.wa[lanes, values])
            r.rows[group, :, lanes] = row_grad.astype(LOW)

    every(0, GROUPS, slot_grads)
    steps_q[5]()
    query_grads = all_rows(r.queries, 0)
    extra = dot_turned(query_grads, r.wa[:, 0:WIDTH]) + attends.astype(FULL)
    r.extra[...] = extra.astype(LOW)
    r.g_wq[...] = dot(r.left_turned[depth : 2 * depth, :], query_grads)

    half_rows = VOCAB_ROWS // 2

    def table_copy(tile):
        at = pl.ds(pl.multiple_of(tile * half_rows, BLOCK), half_rows)
        return pltpu.make_async_copy(
            r.table_full.at[at], r.table_grad.at[at], r.table_sem.at[tile]
        )

    def table_tile(tile):
        at = pl.ds(pl.multiple_of(tile * half_rows, BLOCK), half_rows)
        for start in range(0, WIDTH, BLOCK):
            lanes = slice(start, start + BLOCK)
            slot_rows = r.rows[:, :, lanes].reshape(GROUPS * SLOT_ROWS, BLOCK)
            r.table_full[at, lanes] = dot(r.by_row[at, 0 : GROUPS * SLOT_ROWS], slot_rows) + dot(
                r.by_row[at, GROUPS * SLOT_ROWS :], r.extra[:, lanes]
            )
        table_copy(tile).start()

    every(0, 2, table_tile)
    head_products(r.got_two, 0, r.early, WIDTH, r.g_wk)
    half_copy(2, r.g_wk, core).start()

    down_total = jnp.sum(downs.astype(FULL), axis=0, keepdims=True)
    attend_total = jnp.sum(attends.astype(FULL), axis=0, keepdims=True)
    sums = jnp.sum(r.got_two[:, 0:48, :].astype(FULL), axis=0)
    sums = jnp.concatenate([sums, jnp.zeros((128 - 48, 128), FULL)], axis=0)
    r.totals[...] = jnp.concatenate([attend_total, down_total, jnp.zeros((6, WIDTH), FULL)], axis=0)
    r.g_small[8:16, :] = own_part(r.totals, depth)
    r.g_small[0:8, 0:128] = jnp.transpose(sums)[2 * depth : 2 * depth + 8, :]
    r.g_small[0:8, 128:BLOCK] = jnp.zeros((8, BLOCK - 128), FULL)
    half_copy(1, r.g_wup, 1 - core).wait_recv()
    r.g_small[16:24, :] = own_part(r.g_wup.at[depth : depth + 8, :], deep)

    half_copy(0, r.g_wv, 1 - core).wait_recv()
    half_copy(2, r.g_wk, 1 - core).wait_recv()
    for index, ref in enumerate([r.g_wv, r.g_wup, r.g_wk]):
        half_copy(index, ref, core).wait_send()

    for index, ref in enumerate([r.every_ids, r.got_one, r.got_two]):
        all_but_one(ref, index).wait_send()
    all_smalls().wait_send()
    for end in [drain_d, drain_a2, drain_q]:
        end()
    every(0, TOKENS // BLOCK, lambda tile: layer_copy(tile).wait())
    every(0, 2, lambda tile: table_copy(tile).wait())


def layer(inputs):
    dma = pltpu.SemaphoreType.DMA
    vmem = pl.BlockSpec(memory_space=pltpu.VMEM)
    anywhere = pl.BlockSpec(memory_space=pl.ANY)
    depth, deep = WIDTH // CHIPS, WIDE // CHIPS

    def gathered(width):
        return pltpu.VMEM((CORES, PLANES, LINES, PAD, width), LOW)

    outputs = dict(
        layer_out=((TOKENS, WIDTH), LOW),
        table_grad=((VOCAB_ROWS, WIDTH), FULL),
        g_wq=((depth, WIDTH), FULL),
        g_wk=((depth, WIDTH), FULL),
        g_wv=((depth, WIDTH), FULL),
        g_wo=((depth, WIDTH), FULL),
        g_wup=((depth + 8, WIDE), FULL),
        g_wdown=((deep, WIDTH), FULL),
        g_small=((24, BLOCK), FULL),
        loss=((1, 1), FULL),
    )
    scratch = dict(
        ids=pltpu.VMEM((8, 128), jnp.int32),
        every_ids=pltpu.VMEM((DEVICES, 8, 128), jnp.int32),
        rank=pltpu.VMEM((DEVICES, TOKENS), FULL),
        code=pltpu.VMEM((DEVICES, TOKENS), FULL),
        found=pltpu.VMEM((GROUPS + 1, SLOT_ROWS, 2), FULL),
        block_bias=pltpu.VMEM((2 * BLOCK, BLOCK // 2), FULL),
        valid_bias=pltpu.VMEM((8, TOKENS), FULL),
        slot_col=pltpu.VMEM((TOKENS, 1), FULL),
        slot_line=pltpu.VMEM((8, TOKENS), FULL),
        valid_col=pltpu.VMEM((TOKENS, 1), FULL),
        valid_line=pltpu.VMEM((8, TOKENS), FULL),
        pairs=pltpu.VMEM((8, SLOT_ROWS), FULL),
        pairs_col=pltpu.VMEM((SLOT_ROWS, 128), FULL),
        vectors=pltpu.VMEM((PAD, WIDTH), FULL),
        up_bias=pltpu.VMEM((8, WIDE), FULL),
        qkv_bias=pltpu.VMEM((8, 3 * WIDTH), FULL),
        smalls=pltpu.VMEM((PAD, CHIPS * 128), LOW),
        wa=pltpu.VMEM((WIDTH, 4 * WIDTH), LOW),
        wb=pltpu.VMEM((WIDTH, WIDE), LOW),
        wc=pltpu.VMEM((WIDE, WIDTH), LOW),
        chosen=pltpu.VMEM((GROUPS, SLOT_ROWS, VOCAB_ROWS), LOW),
        by_row=pltpu.VMEM((VOCAB_ROWS, (GROUPS + 1) * SLOT_ROWS), LOW),
        rows=pltpu.VMEM((GROUPS, SLOT_ROWS, WIDTH), LOW),
        replies=pltpu.VMEM((GROUPS, SLOT_ROWS, WIDTH), LOW),
        slot_query=pltpu.VMEM((GROUPS, SLOT_ROWS, WIDTH), LOW),
        extra=pltpu.VMEM((SLOT_ROWS, WIDTH), LOW),
        hidden_cls=pltpu.VMEM((PAD, WIDTH), LOW),
        active_cls=pltpu.VMEM((PAD, WIDE), LOW),
        slope_cls=pltpu.VMEM((PAD, WIDE), FULL),
        wide_cls=pltpu.VMEM((PAD, WIDTH), FULL),
        tall=pltpu.VMEM((PAIR_ROWS + 2 * PAD, WIDTH), LOW),
        own_sums=pltpu.VMEM((WIDTH, 128), FULL),
        product=pltpu.VMEM((128, 128), FULL),
        slot_hot=pltpu.VMEM((GROUPS, SLOT_ROWS, TOKENS), LOW),
        tile_up=pltpu.VMEM((TOKENS, BLOCK), FULL),
        embedded=pltpu.VMEM((TOKENS, WIDTH), LOW),
        qkv=pltpu.VMEM((TOKENS, 3 * WIDTH), LOW),
        context=pltpu.VMEM((TOKENS, WIDTH), LOW),
        table_full=pltpu.VMEM((VOCAB_ROWS, WIDTH), FULL),
        probs=pltpu.VMEM((PAIR_ROWS, TOKENS), FULL),
        normed_one=pltpu.VMEM((PAD, WIDTH), FULL),
        units=gathered(WIDTH),
        early=gathered(2 * WIDTH),
        downs=gathered(WIDTH),
        attends=gathered(2 * WIDTH),
        queries=gathered(WIDTH),
        slopes=pltpu.VMEM((SLOT_ROWS, WIDE // 2), LOW),
        hidden_turned=pltpu.VMEM((WIDTH, SLOT_ROWS), LOW),
        active_turned=pltpu.VMEM((2 * deep, SLOT_ROWS), LOW),
        left_turned=pltpu.VMEM((128, SLOT_ROWS), LOW),
        totals=pltpu.VMEM((8, WIDTH), FULL),
        mail_one=pltpu.VMEM((DEVICES, 80, 128), LOW),
        got_one=pltpu.VMEM((DEVICES, 80, 128), LOW),
        mail_two=pltpu.VMEM((DEVICES, 64, 128), LOW),
        got_two=pltpu.VMEM((DEVICES, 64, 128), LOW),
        rows_send=dma((4,)),
        rows_recv=dma((4,)),
        one_send=dma((4,)),
        one_recv=dma((4,)),
        small_send=dma((1,)),
        small_recv=dma((1,)),
        weight_send=dma((3, 7)),
        weight_recv=dma((3, 18)),
        gather_send=dma((5, 13)),
        gather_recv=dma((5, 13)),
        half_send=dma((3,)),
        half_recv=dma((3,)),
        out_sem=dma((TOKENS // BLOCK,)),
        table_sem=dma((2,)),
    )
    names = INPUTS + OUTPUTS + list(scratch)
    return pl.pallas_call(
        partial(layer_kernel, names),
        out_shape=tuple(jax.ShapeDtypeStruct(*outputs[name]) for name in OUTPUTS),
        in_specs=[vmem] * len(INPUTS),
        out_specs=(anywhere, anywhere) + (vmem,) * (len(OUTPUTS) - 2),
        scratch_shapes=list(scratch.values()),
        compiler_params=pltpu.CompilerParams(
            collective_id=0, has_side_effects=True, vmem_limit_bytes=VMEM_LIMIT
        ),
        name="layer",
    )(*inputs)


def finish_kernel(count, *refs):
    large, (small, loss), outs = refs[:count], refs[count : count + 2], refs[count + 2 : -1]
    sems = refs[-1]
    copies = []
    for index, (source, target) in enumerate(zip(large, outs)):
        part = source if source.shape == target.shape else source.at[: target.shape[0]]
        copies.append(pltpu.make_async_copy(part, target, sems.at[index]))
        copies[-1].start()
    for row, target in zip([0, 1, 8, 2, 3, 16, 9, 4, 5], outs[count : count + 9]):
        size = target.shape[0]
        target[...] = small[row : row + 1, 0:size].reshape(size)
    outs[-1][...] = loss[...].reshape(1)
    for one in copies:
        one.wait()


def finish(results):
    vmem = pl.BlockSpec(memory_space=pltpu.VMEM)
    anywhere = pl.BlockSpec(memory_space=pl.ANY)
    depth, deep = WIDTH // CHIPS, WIDE // CHIPS
    count = len(results) - 2
    shapes = [(one.shape, one.dtype) for one in results[:count]]
    shapes[6] = ((depth, WIDE), FULL)
    shapes += [((depth,), FULL)] * 5 + [((deep,), FULL)] + [((depth,), FULL)] * 3
    shapes.append(((1,), FULL))
    return pl.pallas_call(
        partial(finish_kernel, count),
        out_shape=tuple(jax.ShapeDtypeStruct(*one) for one in shapes),
        in_specs=[vmem] * (count + 2),
        out_specs=(anywhere,) * count + (vmem,) * 10,
        scratch_shapes=[pltpu.SemaphoreType.DMA((count,))],
        name="finish",
    )(*results)


def block_body(
    table,
    token_ids,
    sent_lengths,
    pair_slot,
    pair_lang,
    *parameters,
):
    results = finish(layer((table, token_ids, sent_lengths, pair_slot, pair_lang) + parameters))
    layer_out, table_grad, g_wq, g_wk, g_wv, g_wo, g_wup, g_wdown = results[:8]
    g_bq, g_bv, g_bo, g_g1, g_s1, g_bup, g_bdown, g_g2, g_s2, loss = results[8:]
    return (
        layer_out.reshape(token_ids.shape + (WIDTH,)),
        loss.reshape(()),
        table_grad,
        g_wq,
        g_bq,
        g_wk,
        g_wv,
        g_bv,
        g_wo,
        g_bo,
        g_g1,
        g_s1,
        g_wup,
        g_bup,
        g_wdown,
        g_bdown,
        g_g2,
        g_s2,
    )


def solution(mesh):
    in_specs = (
        P(("dp", "fsdp"), None),
        P(("dp", "fsdp"), None),
        P(("dp", "fsdp")),
        P(),
        P(),
        P("fsdp", None),
        P("fsdp"),
        P("fsdp", None),
        P("fsdp", None),
        P("fsdp"),
        P("fsdp", None),
        P("fsdp"),
        P("fsdp"),
        P("fsdp"),
        P("fsdp", None),
        P("fsdp"),
        P("fsdp", None),
        P("fsdp"),
        P("fsdp"),
        P("fsdp"),
    )
    out_specs = (
        P(("dp", "fsdp"), None, None),
        P(),
        P(("dp", "fsdp"), None),
        P("fsdp", None),
        P("fsdp"),
        P("fsdp", None),
        P("fsdp", None),
        P("fsdp"),
        P("fsdp", None),
        P("fsdp"),
        P("fsdp"),
        P("fsdp"),
        P("fsdp", None),
        P("fsdp"),
        P("fsdp", None),
        P("fsdp"),
        P("fsdp"),
        P("fsdp"),
    )
    sizes = dict(mesh.shape)
    body = general_body
    if sizes["dp"] == CORES and sizes["fsdp"] == CHIPS:
        body = block_body
    return jax.shard_map(body, mesh=mesh, in_specs=in_specs, out_specs=out_specs, check_vma=False)
```

```python
from functools import partial
from types import SimpleNamespace

import jax
import jax.numpy as jnp
from jax import lax
from jax.experimental import pallas as pl
from jax.experimental.pallas import tpu as pltpu
from jax.sharding import PartitionSpec as P

HEADS = 12
HEAD = 64
LANGS = 109


EPSILON = 1e-06
SCORE_SCALE = 50.0
MARGIN_WIDTH = 0.3
MASK_FLOOR = -1000000000.0


def contract(left_side, right_side, left_dim, right_dim):
    return lax.dot_general(
        left_side,
        right_side,
        (((left_dim,), (right_dim,)), ((), ())),
        preferred_element_type=jnp.float32,
    )


def norm_rows(inputs, ln_gain, ln_shift):
    row_mean = jnp.mean(inputs, axis=-1, keepdims=True)
    centered = inputs - row_mean
    variance = jnp.mean(centered * centered, axis=-1, keepdims=True)
    inverse = lax.rsqrt(variance + EPSILON)
    normed = centered * inverse
    return (normed * ln_gain + ln_shift, normed, inverse)


def norm_back(grad_output, normed, inverse, ln_gain):
    grad_normed = grad_output * ln_gain
    first_term = jnp.mean(grad_normed, axis=-1, keepdims=True)
    second_term = jnp.mean(grad_normed * normed, axis=-1, keepdims=True)
    grad_input = inverse * (grad_normed - first_term - normed * second_term)
    return (grad_input, jnp.sum(grad_output * normed, axis=0), jnp.sum(grad_output, axis=0))


def general_body(
    table,
    token_ids,
    sent_lengths,
    pair_slot,
    pair_lang,
    w_query,
    b_query,
    w_key,
    w_value,
    b_value,
    w_out,
    b_out,
    ln1_gain,
    ln1_bias,
    w_up,
    b_up,
    w_down,
    b_down,
    ln2_gain,
    ln2_bias,
):
    sentences, length = token_ids.shape
    tokens = sentences * length
    vocab_rows, model_width = table.shape
    owners = lax.axis_size(("dp", "fsdp"))
    dp_count = lax.axis_size("dp")
    fsdp_count = lax.axis_size("fsdp")
    capacity = max(2, 2 * tokens // owners)
    device = lax.axis_index(("dp", "fsdp"))
    score_factor = HEAD ** (-0.5)
    flat_ids = token_ids.reshape(tokens)
    owner_of = flat_ids // vocab_rows
    member = (owner_of[:, None] == jnp.arange(owners, dtype=jnp.int32)[None, :]).astype(jnp.int32)
    owner_rank = jnp.sum(jnp.cumsum(member, axis=0) * member, axis=1) - 1
    slot_of = owner_of * capacity + owner_rank
    requests = jnp.full((owners * capacity,), -1, jnp.int32).at[slot_of].set(flat_ids)
    received = lax.all_to_all(
        lax.all_to_all(
            requests.reshape(dp_count, fsdp_count, capacity),
            "dp",
            split_axis=0,
            concat_axis=0,
            tiled=True,
        ),
        "fsdp",
        split_axis=1,
        concat_axis=1,
        tiled=True,
    )
    present = received >= 0
    local_rows = jnp.where(present, received - device * vocab_rows, 0)
    found_rows = jnp.where(present[..., None], table[local_rows], jnp.zeros((), table.dtype))
    replies = lax.all_to_all(
        lax.all_to_all(found_rows, "dp", split_axis=0, concat_axis=0, tiled=True),
        "fsdp",
        split_axis=1,
        concat_axis=1,
        tiled=True,
    )
    embedded = replies.reshape(owners * capacity, model_width)[slot_of]
    gathered = (
        lax.all_gather(w_query, "fsdp", axis=0, tiled=True),
        lax.all_gather(b_query, "fsdp", axis=0, tiled=True),
        lax.all_gather(w_key, "fsdp", axis=0, tiled=True),
        lax.all_gather(w_value, "fsdp", axis=0, tiled=True),
        lax.all_gather(b_value, "fsdp", axis=0, tiled=True),
        lax.all_gather(w_out, "fsdp", axis=0, tiled=True),
        lax.all_gather(b_out, "fsdp", axis=0, tiled=True),
        lax.all_gather(ln1_gain, "fsdp", axis=0, tiled=True),
        lax.all_gather(ln1_bias, "fsdp", axis=0, tiled=True),
        lax.all_gather(w_up, "fsdp", axis=0, tiled=True),
        lax.all_gather(b_up, "fsdp", axis=0, tiled=True),
        lax.all_gather(w_down, "fsdp", axis=0, tiled=True),
        lax.all_gather(b_down, "fsdp", axis=0, tiled=True),
        lax.all_gather(ln2_gain, "fsdp", axis=0, tiled=True),
        lax.all_gather(ln2_bias, "fsdp", axis=0, tiled=True),
    )
    (
        full_wq,
        full_bq,
        full_wk,
        full_wv,
        full_bv,
        full_wo,
        full_bo,
        full_g1,
        full_s1,
        full_wup,
        full_bup,
        full_wdown,
        full_bdown,
        full_g2,
        full_s2,
    ) = gathered
    valid_mask = jnp.arange(length, dtype=jnp.int32)[None, :] < sent_lengths[:, None]
    head_shape = (sentences, length, HEADS, HEAD)
    queries = (jnp.dot(embedded, full_wq, preferred_element_type=jnp.float32) + full_bq).astype(
        jnp.bfloat16
    )
    key_heads = (
        jnp.dot(embedded, full_wk, preferred_element_type=jnp.float32)
        .astype(jnp.bfloat16)
        .reshape(head_shape)
    )
    value_heads = (
        (jnp.dot(embedded, full_wv, preferred_element_type=jnp.float32) + full_bv)
        .astype(jnp.bfloat16)
        .reshape(head_shape)
    )
    query_heads = queries.reshape(head_shape)
    scores = (
        jnp.einsum("bqhd,bkhd->bhqk", query_heads, key_heads, preferred_element_type=jnp.float32)
        * score_factor
    )
    scores = jnp.where(valid_mask[:, None, None, :], scores, MASK_FLOOR)
    row_peak = jnp.max(scores, axis=-1, keepdims=True)
    shifted = jnp.exp(scores - row_peak)
    totals = jnp.sum(shifted, axis=-1, keepdims=True)
    attn_probs = (shifted / totals).astype(jnp.bfloat16)
    context = jnp.einsum(
        "bhqk,bkhd->bqhd", attn_probs, value_heads, preferred_element_type=jnp.float32
    )
    context = context.reshape(tokens, model_width).astype(jnp.bfloat16)
    attended = jnp.dot(context, full_wo, preferred_element_type=jnp.float32) + full_bo
    hidden, normed_one, inverse_one = norm_rows(
        embedded.astype(jnp.float32) + attended, full_g1, full_s1
    )
    hidden_low = hidden.astype(jnp.bfloat16)
    up_pre = jnp.dot(hidden_low, full_wup, preferred_element_type=jnp.float32) + full_bup
    activated = jax.nn.gelu(up_pre, approximate=False).astype(jnp.bfloat16)
    down_pre = jnp.dot(activated, full_wdown, preferred_element_type=jnp.float32) + full_bdown
    normed_out, normed_two, inverse_two = norm_rows(hidden + down_pre, full_g2, full_s2)
    layer_out = jnp.where(valid_mask.reshape(tokens)[:, None], normed_out, 0.0).astype(jnp.bfloat16)
    layer_out = layer_out.reshape(sentences, length, model_width)

    def first_rows(matrix):
        return matrix.reshape(sentences, length, matrix.shape[-1])[:, 0]

    summary = first_rows(normed_out)
    magnitude = jnp.sqrt(jnp.sum(summary * summary, axis=-1, keepdims=True) + EPSILON)
    unit_vector = summary / magnitude
    unit_low = unit_vector.astype(jnp.bfloat16)
    every_unit = lax.all_gather(unit_low, ("dp", "fsdp"), axis=0, tiled=True)
    every_side = pair_slot % 2
    every_pair = pair_slot // 2
    my_slots = lax.dynamic_slice_in_dim(pair_slot, device * sentences, sentences)
    my_side = my_slots % 2
    my_pair = my_slots // 2
    lang_onehot = (pair_lang[:, None] == jnp.arange(LANGS, dtype=jnp.int32)[None, :]).astype(
        jnp.float32
    )
    per_lang = jnp.sum(lang_onehot, axis=0)
    per_pair = 1.0 / (2.0 * LANGS * jnp.sum(lang_onehot * per_lang[None, :], axis=1))
    my_weight = jnp.take(per_pair, my_pair)
    opposite = my_side[:, None] != every_side[None, :]
    partner = opposite & (my_pair[:, None] == every_pair[None, :])
    raw_scores = SCORE_SCALE * contract(unit_low, every_unit, 1, 1)
    pair_scores = jnp.where(partner, raw_scores - SCORE_SCALE * MARGIN_WIDTH, raw_scores)
    pair_scores = jnp.where(opposite, pair_scores, MASK_FLOOR)
    pair_peak = jnp.max(pair_scores, axis=1, keepdims=True)
    pair_exp = jnp.exp(pair_scores - pair_peak)
    pair_total = jnp.sum(pair_exp, axis=1, keepdims=True)
    log_total = pair_peak[:, 0] + jnp.log(pair_total[:, 0])
    picked = jnp.sum(jnp.where(partner, pair_scores, 0.0), axis=1)
    loss_value = lax.psum(jnp.sum(my_weight * (log_total - picked)), ("dp", "fsdp"))
    coefficients = (
        my_weight[:, None] * (pair_exp / pair_total - partner.astype(jnp.float32))
    ).astype(jnp.bfloat16)
    unit_grad = SCORE_SCALE * contract(coefficients, every_unit, 1, 0)
    column_terms = SCORE_SCALE * contract(coefficients, unit_low, 0, 0)
    unit_grad = unit_grad + lax.psum_scatter(
        column_terms, ("dp", "fsdp"), scatter_dimension=0, tiled=True
    )
    along = jnp.sum(unit_vector * unit_grad, axis=-1, keepdims=True)
    summary_grad = (unit_grad - unit_vector * along) / magnitude
    again_weights = (
        lax.all_gather(w_query, "fsdp", axis=0, tiled=True),
        lax.all_gather(w_key, "fsdp", axis=0, tiled=True),
        lax.all_gather(w_value, "fsdp", axis=0, tiled=True),
        lax.all_gather(w_out, "fsdp", axis=0, tiled=True),
        lax.all_gather(ln1_gain, "fsdp", axis=0, tiled=True),
        lax.all_gather(w_up, "fsdp", axis=0, tiled=True),
        lax.all_gather(w_down, "fsdp", axis=0, tiled=True),
        lax.all_gather(ln2_gain, "fsdp", axis=0, tiled=True),
    )
    again_wq, again_wk, again_wv, again_wo, again_g1, again_wup, again_wdown, again_g2 = (
        again_weights
    )
    residual_grad, grad_g2, grad_s2 = norm_back(
        summary_grad, first_rows(normed_two), first_rows(inverse_two), again_g2
    )
    down_grad = residual_grad.astype(jnp.bfloat16)
    activated_cls = first_rows(activated)
    act_grad = contract(down_grad, again_wdown, 1, 1)
    gelu_value, gelu_pull = jax.vjp(partial(jax.nn.gelu, approximate=False), first_rows(up_pre))
    up_grad = gelu_pull(act_grad)[0].astype(jnp.bfloat16)
    hidden_cls = first_rows(hidden_low)
    hidden_grad = contract(up_grad, again_wup, 1, 1) + residual_grad
    first_grad, grad_g1, grad_s1 = norm_back(
        hidden_grad, first_rows(normed_one), first_rows(inverse_one), again_g1
    )
    attend_grad = first_grad.astype(jnp.bfloat16)
    context_cls = first_rows(context)
    context_grad = (
        contract(attend_grad, again_wo, 1, 1).astype(jnp.bfloat16).reshape(sentences, HEADS, HEAD)
    )
    query_cls = query_heads[:, 0]
    cls_scores = (
        jnp.einsum("bhd,bkhd->bhk", query_cls, key_heads, preferred_element_type=jnp.float32)
        * score_factor
    )
    cls_scores = jnp.where(valid_mask[:, None, :], cls_scores, MASK_FLOOR)
    cls_probs = jnp.exp(cls_scores - row_peak[:, :, 0]) / totals[:, :, 0]
    prob_grad = jnp.einsum(
        "bhd,bkhd->bhk", context_grad, value_heads, preferred_element_type=jnp.float32
    )
    score_grad = (
        cls_probs * (prob_grad - jnp.sum(cls_probs * prob_grad, axis=-1, keepdims=True))
    ).astype(jnp.bfloat16)
    query_grad = (
        (
            jnp.einsum("bhk,bkhd->bhd", score_grad, key_heads, preferred_element_type=jnp.float32)
            * score_factor
        )
        .astype(jnp.bfloat16)
        .reshape(sentences, model_width)
    )
    key_grad = (
        (
            jnp.einsum("bhk,bhd->bkhd", score_grad, query_cls, preferred_element_type=jnp.float32)
            * score_factor
        )
        .astype(jnp.bfloat16)
        .reshape(tokens, model_width)
    )
    value_grad = (
        jnp.einsum(
            "bhk,bhd->bkhd",
            cls_probs.astype(jnp.bfloat16),
            context_grad,
            preferred_element_type=jnp.float32,
        )
        .astype(jnp.bfloat16)
        .reshape(tokens, model_width)
    )
    embedded_cls = first_rows(embedded)
    grad_wkey = contract(embedded, key_grad, 0, 0)
    grad_wvalue = contract(embedded, value_grad, 0, 0)
    grad_bvalue = jnp.sum(value_grad, axis=0, dtype=jnp.float32)
    row_grads = contract(key_grad, again_wk, 1, 1) + contract(value_grad, again_wv, 1, 1)
    summary_extra = contract(query_grad, again_wq, 1, 1) + first_grad
    row_grads = (
        row_grads.reshape(sentences, length, model_width)
        .at[:, 0]
        .add(summary_extra)
        .reshape(tokens, model_width)
    )
    outgoing = jnp.zeros((owners * capacity, model_width), jnp.float32).at[slot_of].set(row_grads)
    incoming = lax.all_to_all(
        lax.all_to_all(
            outgoing.reshape(dp_count, fsdp_count, capacity, model_width).astype(jnp.bfloat16),
            "dp",
            split_axis=0,
            concat_axis=0,
            tiled=True,
        ),
        "fsdp",
        split_axis=1,
        concat_axis=1,
        tiled=True,
    ).astype(jnp.float32)
    incoming = jnp.where(
        present.reshape(owners * capacity)[:, None],
        incoming.reshape(owners * capacity, model_width),
        0.0,
    )
    table_grad = (
        jnp.zeros((vocab_rows, model_width), jnp.float32)
        .at[local_rows.reshape(owners * capacity)]
        .add(incoming)
    )
    grad_wquery = contract(embedded_cls, query_grad, 0, 0)
    grad_bquery = jnp.sum(query_grad, axis=0, dtype=jnp.float32)
    grad_wout = contract(context_cls, attend_grad, 0, 0)
    grad_bout = jnp.sum(attend_grad, axis=0, dtype=jnp.float32)
    grad_wup = contract(hidden_cls, up_grad, 0, 0)
    grad_bup = jnp.sum(up_grad, axis=0, dtype=jnp.float32)
    grad_wdown = contract(activated_cls, down_grad, 0, 0)
    grad_bdown = jnp.sum(down_grad, axis=0, dtype=jnp.float32)
    owned_grads = (
        lax.psum_scatter(
            grad_wquery.astype(jnp.bfloat16), "fsdp", scatter_dimension=0, tiled=True
        ).astype(jnp.float32),
        lax.psum_scatter(
            grad_bquery.astype(jnp.bfloat16), "fsdp", scatter_dimension=0, tiled=True
        ).astype(jnp.float32),
        lax.psum_scatter(
            grad_wkey.astype(jnp.bfloat16), "fsdp", scatter_dimension=0, tiled=True
        ).astype(jnp.float32),
        lax.psum_scatter(
            grad_wvalue.astype(jnp.bfloat16), "fsdp", scatter_dimension=0, tiled=True
        ).astype(jnp.float32),
        lax.psum_scatter(
            grad_bvalue.astype(jnp.bfloat16), "fsdp", scatter_dimension=0, tiled=True
        ).astype(jnp.float32),
        lax.psum_scatter(
            grad_wout.astype(jnp.bfloat16), "fsdp", scatter_dimension=0, tiled=True
        ).astype(jnp.float32),
        lax.psum_scatter(
            grad_bout.astype(jnp.bfloat16), "fsdp", scatter_dimension=0, tiled=True
        ).astype(jnp.float32),
        lax.psum_scatter(
            grad_g1.astype(jnp.bfloat16), "fsdp", scatter_dimension=0, tiled=True
        ).astype(jnp.float32),
        lax.psum_scatter(
            grad_s1.astype(jnp.bfloat16), "fsdp", scatter_dimension=0, tiled=True
        ).astype(jnp.float32),
        lax.psum_scatter(
            grad_wup.astype(jnp.bfloat16), "fsdp", scatter_dimension=0, tiled=True
        ).astype(jnp.float32),
        lax.psum_scatter(
            grad_bup.astype(jnp.bfloat16), "fsdp", scatter_dimension=0, tiled=True
        ).astype(jnp.float32),
        lax.psum_scatter(
            grad_wdown.astype(jnp.bfloat16), "fsdp", scatter_dimension=0, tiled=True
        ).astype(jnp.float32),
        lax.psum_scatter(
            grad_bdown.astype(jnp.bfloat16), "fsdp", scatter_dimension=0, tiled=True
        ).astype(jnp.float32),
        lax.psum_scatter(
            grad_g2.astype(jnp.bfloat16), "fsdp", scatter_dimension=0, tiled=True
        ).astype(jnp.float32),
        lax.psum_scatter(
            grad_s2.astype(jnp.bfloat16), "fsdp", scatter_dimension=0, tiled=True
        ).astype(jnp.float32),
    )
    summed = (
        lax.psum(owned_grads[0].astype(jnp.bfloat16), "dp").astype(jnp.float32),
        lax.psum(owned_grads[1].astype(jnp.bfloat16), "dp").astype(jnp.float32),
        lax.psum(owned_grads[2].astype(jnp.bfloat16), "dp").astype(jnp.float32),
        lax.psum(owned_grads[3].astype(jnp.bfloat16), "dp").astype(jnp.float32),
        lax.psum(owned_grads[4].astype(jnp.bfloat16), "dp").astype(jnp.float32),
        lax.psum(owned_grads[5].astype(jnp.bfloat16), "dp").astype(jnp.float32),
        lax.psum(owned_grads[6].astype(jnp.bfloat16), "dp").astype(jnp.float32),
        lax.psum(owned_grads[7].astype(jnp.bfloat16), "dp").astype(jnp.float32),
        lax.psum(owned_grads[8].astype(jnp.bfloat16), "dp").astype(jnp.float32),
        lax.psum(owned_grads[9].astype(jnp.bfloat16), "dp").astype(jnp.float32),
        lax.psum(owned_grads[10].astype(jnp.bfloat16), "dp").astype(jnp.float32),
        lax.psum(owned_grads[11].astype(jnp.bfloat16), "dp").astype(jnp.float32),
        lax.psum(owned_grads[12].astype(jnp.bfloat16), "dp").astype(jnp.float32),
        lax.psum(owned_grads[13].astype(jnp.bfloat16), "dp").astype(jnp.float32),
        lax.psum(owned_grads[14].astype(jnp.bfloat16), "dp").astype(jnp.float32),
    )
    return (
        layer_out,
        loss_value,
        table_grad,
        summed[0],
        summed[1],
        summed[2],
        summed[3],
        summed[4],
        summed[5],
        summed[6],
        summed[7],
        summed[8],
        summed[9],
        summed[10],
        summed[11],
        summed[12],
        summed[13],
        summed[14],
    )


CORES = 2
PLANES = 4
LINES = 4
CHIPS = PLANES * LINES
DEVICES = CORES * CHIPS
CAPACITY = 48
GROUPS = 3
PAD = 16
TOKENS = 768
WIDTH = 768
WIDE = 3072
VOCAB_ROWS = 1024
PAIR_ROWS = HEADS * PAD
SLOT_ROWS = DEVICES * PAD
LONG = 64
BLOCK = 256
MESH = pl.DeviceIdType.MESH
LOW = jnp.bfloat16
FULL = jnp.float32
VMEM_LIMIT = 62 * 1024 * 1024

INPUTS = ["table", "token_ids", "lens", "slots", "langs"]
INPUTS += ["wq", "bq", "wk", "wv", "bv", "wo", "bo", "g1", "s1", "wup", "bup", "wdown", "bdown"]
INPUTS += ["g2", "s2"]
OUTPUTS = ["layer_out", "table_grad", "g_wq", "g_wk", "g_wv", "g_wo", "g_wup", "g_wdown"]
OUTPUTS += ["g_small", "loss"]


def place():
    core = lax.axis_index("dp")
    chip = lax.axis_index("fsdp")
    along_x = chip + 1 - 2 * (chip % 2)
    along_y = chip + 2 - 4 * ((chip // 2) % 2)
    first = along_x + core * (along_y - along_x)
    second = along_y + core * (along_x - along_y)
    return core, chip, first, second


def greet():
    core, chip, _, _ = place()
    me = core * CHIPS + chip
    barrier = pltpu.get_barrier_semaphore()

    def signal(step):
        other = lax.rem(me + step, DEVICES)
        pl.semaphore_signal(
            barrier,
            inc=1,
            device_id=(lax.div(other, CHIPS), lax.rem(other, CHIPS)),
            device_id_type=MESH,
        )

    every(1, DEVICES, signal)


def enter():
    pl.semaphore_wait(pltpu.get_barrier_semaphore(), DEVICES - 1)


def remote(source, target, send_sem, recv_sem, core, chip):
    return pltpu.make_async_remote_copy(
        src_ref=source,
        dst_ref=target,
        send_sem=send_sem,
        recv_sem=recv_sem,
        device_id=(core, chip),
        device_id_type=MESH,
    )


def every(start, stop, act):
    def step(index, carry):
        act(index)
        return carry

    lax.fori_loop(start, stop, step, 0)


def weight_steps(piece, many, send, recv):
    core, chip, first, second = place()
    plane, line = chip // LINES, chip % LINES
    line_first, line_second = first % LINES, second % LINES
    line_far = line_first + line_second - line
    is_low, is_high = plane > 0, plane < PLANES - 1

    def copy(send_index, recv_index, at, to_core, to_chip, carried=core):
        part = piece(at, carried)
        return remote(part, part, send.at[send_index], recv.at[recv_index], to_core, to_chip)

    def up(at_plane):
        return copy(at_plane, at_plane, at_plane * LINES + line, core, chip + LINES)

    def down(at_plane, index):
        return copy(index, at_plane, at_plane * LINES + line, core, chip - LINES)

    def side(at_plane, base, at_line, target):
        return copy(5, base + at_plane, at_plane * LINES + at_line, core, target)

    def across(at_plane, at_line):
        return copy(6, 17, at_plane * LINES + at_line, 1 - core, chip)

    def all_of(count, send_index, recv_index):
        part = many(count)
        return remote(part, part, send.at[send_index], recv.at[recv_index], 1 - core, chip)

    def begin():
        pl.when(is_high)(lambda: up(plane).start())
        pl.when(is_low)(lambda: down(plane, PLANES).start())
        side(plane, 5, line, first).start()
        side(plane, 9, line, second).start()

    def at_distance(distance, act):
        if distance == 0:
            act(plane, None)
            return
        pl.when(plane >= distance)(lambda: act(plane - distance, True))
        pl.when(plane + distance < PLANES)(lambda: act(plane + distance, False))

    def chain(distance):
        def act(at_plane, from_low):
            if from_low:
                up(at_plane).wait_recv()
                pl.when(is_high)(lambda: up(at_plane).start())
            else:
                down(at_plane, at_plane).wait_recv()
                pl.when(is_low)(lambda: down(at_plane, at_plane).start())
            side(at_plane, 5, line, first).start()
            side(at_plane, 9, line, second).start()
            across(at_plane, line).start()

        return partial(at_distance, distance, act)

    def near(distance):
        def act(at_plane, from_low):
            side(at_plane, 5, line_first, first).wait_recv()
            side(at_plane, 13, line_first, second).start()
            across(at_plane, line_first).start()

        return partial(at_distance, distance, act)

    def far(distance):
        def act(at_plane, from_low):
            side(at_plane, 9, line_second, second).wait_recv()
            across(at_plane, line_second).start()
            side(at_plane, 13, line_far, second).wait_recv()
            across(at_plane, line_far).start()

        return partial(at_distance, distance, act)

    def finish():
        all_of(15, 6, 17).wait_recv()

    def drain():
        def sent(index):
            copy(index, index, chip, 1 - core, chip).wait_send()

        for at_plane in range(PLANES):
            pl.when((plane >= at_plane) & is_high)(partial(sent, at_plane))
            pl.when((plane < at_plane) & is_low)(partial(sent, at_plane))
        pl.when(is_low)(partial(sent, PLANES))
        all_of(12, 5, 17).wait_send()
        all_of(15, 6, 17).wait_send()

    moves = [chain(1), near(0), chain(2), near(1), chain(3), far(0)]
    moves += [near(2), far(1), near(3), far(2), far(3)]
    return begin, moves, finish, drain


def gather_steps(buffer, send, recv):
    core, chip, first, second = place()
    plane, line = chip // LINES, chip % LINES
    line_first, line_second = first % LINES, second % LINES
    line_far = line_first + line_second - line
    half = buffer.shape[-1] // 2
    columns = pl.ds(pl.multiple_of(core * half, 128), half)
    others = pl.ds(pl.multiple_of((1 - core) * half, 128), half)

    def copy(index, part, to_core, to_chip):
        return remote(part, part, send.at[index], recv.at[index], to_core, to_chip)

    def own(at):
        return buffer.at[at, plane, line]

    def chip_part(at_plane, at_line, which):
        return buffer.at[:, at_plane, at_line, :, which]

    def line_part(at_line, which):
        return buffer.at[:, :, at_line, :, which]

    def start():
        copy(0, own(core), 1 - core, chip).start()

    def planes():
        copy(0, own(1 - core), 1 - core, chip).wait_recv()
        for step in range(1, PLANES):
            part = chip_part(plane, line, columns)
            copy(step, part, core, (chip + LINES * step) % CHIPS).start()

    def sides():
        for step in range(1, PLANES):
            part = chip_part((plane + PLANES - step) % PLANES, line, columns)
            copy(step, part, core, chip).wait_recv()
        copy(4, line_part(line, columns), core, first).start()
        copy(5, line_part(line, columns), core, second).start()
        for step in range(1, PLANES):
            part = chip_part((plane + PLANES - step) % PLANES, line, columns)
            copy(6 + step, part, 1 - core, chip).start()

    def corner():
        copy(4, line_part(line_first, columns), core, first).wait_recv()
        copy(6, line_part(line_first, columns), core, second).start()
        copy(10, line_part(line_first, columns), 1 - core, chip).start()
        copy(5, line_part(line_second, columns), core, second).wait_recv()
        copy(11, line_part(line_second, columns), 1 - core, chip).start()

    def last():
        copy(6, line_part(line_far, columns), core, second).wait_recv()
        copy(12, line_part(line_far, columns), 1 - core, chip).start()

    def finish():
        for step in range(1, PLANES):
            part = chip_part((plane + PLANES - step) % PLANES, line, others)
            copy(6 + step, part, 1 - core, chip).wait_recv()
        copy(10, line_part(line_second, others), 1 - core, chip).wait_recv()
        copy(11, line_part(line_first, others), 1 - core, chip).wait_recv()
        copy(12, line_part(line_far, others), 1 - core, chip).wait_recv()

    def drain():
        copy(0, own(core), 1 - core, chip).wait_send()
        for index in [1, 2, 3, 7, 8, 9]:
            copy(index, chip_part(plane, line, columns), 1 - core, chip).wait_send()
        for index in [4, 5, 6, 10, 11, 12]:
            copy(index, line_part(line, columns), 1 - core, chip).wait_send()

    return [start, planes, sides, corner, last, finish], drain


def iota(shape, axis):
    return lax.broadcasted_iota(jnp.int32, shape, axis)


def over(numbers, power):
    return lax.shift_right_arithmetic(numbers, jnp.full_like(numbers, power.bit_length() - 1))


def within(numbers, power):
    return numbers & (power - 1)


def as_column(row):
    parts = []
    for start in range(0, row.shape[1], 128):
        tile = jnp.broadcast_to(row[:, start : start + 128], (128, 128))
        parts.append(jnp.transpose(tile)[:, 0:1])
    return jnp.concatenate(parts, axis=0)


def as_row(column):
    parts = []
    for start in range(0, column.shape[0], 128):
        tile = jnp.broadcast_to(column[start : start + 128, :], (128, 128))
        parts.append(jnp.transpose(tile)[0:1, :])
    return jnp.concatenate(parts, axis=1)


def dot(left_side, right_side):
    return contract(left_side, right_side, 1, 0)


def dot_turned(left_side, right_side):
    return contract(left_side, right_side, 1, 1)


def norm_parts(inputs):
    centered = inputs - jnp.mean(inputs, axis=-1, keepdims=True)
    inverse = lax.rsqrt(jnp.mean(centered * centered, axis=-1, keepdims=True) + EPSILON)
    return centered * inverse, inverse


def norm_back_parts(grad_output, normed, inverse, ln_gain):
    grad_normed = grad_output * ln_gain
    first_term = jnp.mean(grad_normed, axis=-1, keepdims=True)
    second_term = jnp.mean(grad_normed * normed, axis=-1, keepdims=True)
    return (
        inverse * (grad_normed - first_term - normed * second_term),
        jnp.sum(grad_output * normed, axis=0, keepdims=True),
        jnp.sum(grad_output, axis=0, keepdims=True),
    )


def erf_parts(inputs):
    decay = jnp.exp(-0.5 * inputs * inputs)
    share = 1.0 / (1.0 + jnp.abs(inputs) * (0.3275911 * 0.5**0.5))
    terms = [1.061405429, -1.453152027, 1.421413741, -0.284496736, 0.254829592]
    series = 0.5 * terms[0]
    for term in terms[1:]:
        series = series * share + 0.5 * term
    tail = series * share * decay
    return jnp.where(inputs >= 0.0, 1.0 - tail, tail), decay


def gelu_parts(inputs):
    below, decay = erf_parts(inputs)
    return inputs * below, below + inputs * decay * ((2.0 * 3.141592653589793) ** -0.5)


def gelu(inputs):
    return inputs * erf_parts(inputs)[0]


def layer_kernel(names, *refs):
    r = SimpleNamespace(**dict(zip(names, refs, strict=True)))
    core, chip, _, _ = place()
    me = core * CHIPS + chip
    here = (core, chip // LINES, chip % LINES)
    scale = HEAD ** (-0.5)
    depth, deep = WIDTH // CHIPS, WIDE // CHIPS
    sentences = TOKENS // LONG

    for j in range(TOKENS // 128):
        r.ids[j : j + 1, :] = jnp.concatenate(
            [r.token_ids[2 * j : 2 * j + 1, :], r.token_ids[2 * j + 1 : 2 * j + 2, :]], axis=1
        )
    r.ids[TOKENS // 128 : 8, :] = jnp.zeros((8 - TOKENS // 128, 128), jnp.int32)
    greet()
    ahead = (iota((TOKENS, TOKENS), 0) < iota((TOKENS, TOKENS), 1)).astype(LOW)
    r.embedded[...] = ahead
    mine = pl.ds(pl.multiple_of(chip * depth, 16), depth)
    for index, shard in enumerate([r.wq, r.wk, r.wv, r.wo]):
        r.wa[mine, index * WIDTH : (index + 1) * WIDTH] = shard[...]
    r.wb[mine, :] = r.wup[...]
    r.wc[pl.ds(pl.multiple_of(chip * deep, 16), deep), :] = r.wdown[...]
    r.every_ids[me] = r.ids[...]
    enter()

    def peer(step):
        other = lax.rem(me + step, DEVICES)
        return other, lax.div(other, CHIPS), lax.rem(other, CHIPS)

    def ids_copy(step):
        other, to_core, to_chip = peer(step)
        return remote(r.ids, r.every_ids.at[me], r.one_send.at[0], r.one_recv.at[0], to_core, to_chip)

    def all_but_one(ref, index):
        part = ref.at[0 : DEVICES - 1]
        return remote(part, part, r.one_send.at[index], r.one_recv.at[index], 1 - core, chip)

    every(1, DEVICES, lambda step: ids_copy(step).start())

    def block(ref, rows, columns):
        def piece(at, carried):
            return ref.at[
                pl.ds(pl.multiple_of(at * rows, 16), rows),
                pl.ds(pl.multiple_of(carried * columns, 128), columns),
            ]

        def many(count):
            return ref.at[0 : count * rows, 0:columns]

        return piece, many

    begin_a, moves_a, finish_a, drain_a = weight_steps(
        *block(r.wa, depth, 2 * WIDTH), r.weight_send.at[0], r.weight_recv.at[0]
    )
    begin_b, moves_b, finish_b, drain_b = weight_steps(
        *block(r.wb, depth, WIDE // 2), r.weight_send.at[1], r.weight_recv.at[1]
    )
    begin_c, moves_c, finish_c, drain_c = weight_steps(
        *block(r.wc, deep, WIDTH // 2), r.weight_send.at[2], r.weight_recv.at[2]
    )
    begin_a()
    begin_b()

    def move(*steps):
        for moves, first_step in steps:
            moves[first_step]()
            moves[first_step + 1]()

    all_but_one(r.every_ids, 0).wait_recv()
    all_ids = jnp.concatenate([r.every_ids[:, j, :] for j in range(TOKENS // 128)], axis=1)
    all_owner = over(all_ids, VOCAB_ROWS)
    asked = all_owner == me
    ranks = dot(asked.astype(LOW), r.embedded[...])
    r.rank[...] = jnp.where(asked, ranks, -1.0)
    local_row = (all_ids - all_owner * VOCAB_ROWS + 1).astype(FULL)
    r.code[...] = local_row + (over(iota((DEVICES, TOKENS), 1), LONG) * 2048).astype(FULL)

    quarter_size = DEVICES // 4

    def rows_copy(other, quarter):
        return remote(
            r.rows.at[:, pl.ds(pl.multiple_of(other * PAD, 16), PAD), :],
            r.replies.at[:, pl.ds(pl.multiple_of(me * PAD, 16), PAD), :],
            r.rows_send.at[quarter],
            r.rows_recv.at[quarter],
            lax.div(other, CHIPS),
            lax.rem(other, CHIPS),
        )

    def rows_of(quarter):
        count = quarter_size - 1 if quarter == 3 else quarter_size
        part = r.replies.at[:, 0 : count * PAD, :]
        return remote(
            part, part, r.rows_send.at[quarter], r.rows_recv.at[quarter], 1 - core, chip
        )

    def pick(source):
        rank = r.rank[pl.ds(source, 1), :]
        code = r.code[pl.ds(source, 1), :]
        here_at = iota((CAPACITY, TOKENS), 0).astype(FULL) == rank
        found = jnp.sum(jnp.where(here_at, code, 0.0), axis=1, keepdims=True)
        sent = jnp.floor(found * (1.0 / 2048))
        row = found - sent * 2048.0 - 1.0
        chosen = (iota((CAPACITY, VOCAB_ROWS), 1).astype(FULL) == row).astype(LOW)
        at = pl.ds(pl.multiple_of(source * PAD, 16), PAD)
        source_sent = sent + (source * PAD).astype(FULL)
        for group in range(GROUPS):
            part = slice(group * PAD, (group + 1) * PAD)
            r.chosen[group, at, :] = chosen[part]
            r.found[group, at, 0:1] = row[part]
            r.found[group, at, 1:2] = source_sent[part]

    def quarter_rows(quarter):
        now = lax.rem(lax.div(me, quarter_size) + 1 + quarter, 4)

        def pick_two(index):
            pick(now * quarter_size + 2 * index)
            pick(now * quarter_size + 2 * index + 1)

        every(0, quarter_size // 2, pick_two)
        span = pl.ds(pl.multiple_of(now * quarter_size * PAD, 128), quarter_size * PAD)
        for start in range(0, WIDTH, BLOCK):
            lanes = slice(start, start + BLOCK)
            picked = r.chosen[:, span, :].reshape(GROUPS * quarter_size * PAD, VOCAB_ROWS)
            found_rows = dot(picked, r.table[:, lanes]).astype(LOW)
            r.rows[:, span, lanes] = found_rows.reshape(GROUPS, quarter_size * PAD, BLOCK)

        def send(index):
            other = now * quarter_size + lax.rem(lax.rem(me, quarter_size) + index, quarter_size)
            rows_copy(other, quarter).start()

        every(lax.div(quarter, 3), quarter_size, send)
        pl.when(quarter == 0)(partial(move, (moves_a, 0)))
        pl.when(quarter == 1)(partial(move, (moves_b, 0)))
        pl.when(quarter == 2)(partial(move, (moves_a, 2)))
        pl.when(quarter == 3)(partial(move, (moves_b, 2)))

    every(0, 4, quarter_rows)
    begin_c()
    own_at = pl.ds(pl.multiple_of(me * PAD, 16), PAD)
    r.replies[:, own_at, :] = r.rows[:, own_at, :]

    move((moves_a, 4))

    small_here = pl.ds(pl.multiple_of(chip * 128, 128), 128)
    lines = [r.bq, r.bv, r.bo, r.g1, r.s1, r.bdown, r.g2, r.s2]
    lines = [line[...].reshape(1, depth).astype(FULL) for line in lines]
    up_line = r.bup[...].reshape(1, deep).astype(FULL)
    lines += [up_line[:, part * depth : (part + 1) * depth] for part in range(deep // depth)]
    lines.append(jnp.zeros((PAD - len(lines), depth), FULL))
    own_small = jnp.concatenate(lines, axis=0)
    own_small = jnp.concatenate([own_small, jnp.zeros((PAD, 128 - depth), FULL)], axis=1)
    r.smalls[:, small_here] = own_small.astype(LOW)

    def small_copy(step):
        part = r.smalls.at[:, small_here]
        to_chip = lax.rem(chip + step, CHIPS)
        return remote(part, part, r.small_send.at[0], r.small_recv.at[0], core, to_chip)

    def all_smalls():
        part = r.smalls.at[:, 0 : (CHIPS - 1) * 128]
        return remote(part, part, r.small_send.at[0], r.small_recv.at[0], 1 - core, chip)

    every(1, CHIPS, lambda step: small_copy(step).start())
    move((moves_b, 4))

    own_row = jnp.concatenate([r.ids[j : j + 1, :] for j in range(TOKENS // 128)], axis=1)
    owner_row = over(own_row, VOCAB_ROWS).astype(FULL)
    owner_col = as_column(owner_row)
    earlier = (owner_row == owner_col) & (iota((TOKENS, TOKENS), 1) < iota((TOKENS, TOKENS), 0))
    own_rank = jnp.sum(earlier.astype(FULL), axis=1, keepdims=True)
    own_group = jnp.floor(own_rank * (1.0 / PAD))
    own_slot = own_group * SLOT_ROWS + owner_col * PAD + (own_rank - own_group * PAD)
    r.slot_col[...] = own_slot
    r.slot_line[0:1, :] = as_row(own_slot)
    move((moves_a, 6), (moves_c, 0))

    at_sent = over(iota((1, TOKENS), 1), LONG)
    lens = jnp.concatenate(
        [r.lens[...].reshape(1, sentences).astype(FULL), jnp.zeros((1, PAD - sentences), FULL)],
        axis=1,
    )
    spread_lens = dot(
        jnp.broadcast_to(lens, (8, PAD)).astype(LOW),
        (iota((PAD, TOKENS), 0) == over(iota((PAD, TOKENS), 1), LONG)).astype(LOW),
    )[0:1]
    valid_row = ((iota((1, TOKENS), 1) - at_sent * LONG).astype(FULL) < spread_lens).astype(FULL)
    r.valid_line[0:1, :] = valid_row
    r.valid_col[...] = as_column(valid_row)
    half_block = BLOCK // 2
    stacked_shape = (4 * half_block, half_block)
    same = within(over(iota(stacked_shape, 0), LONG), 2) == over(iota(stacked_shape, 1), LONG)
    r.block_bias[...] = jnp.where(same, 0.0, MASK_FLOOR)
    r.valid_bias[0:1, :] = (1.0 - valid_row) * MASK_FLOOR

    slots = r.slots[...].reshape(1, DEVICES * sentences)
    gap = jnp.full((1, PAD - sentences), -2, jnp.int32)
    slot_line = jnp.concatenate(
        [
            part
            for device in range(DEVICES)
            for part in (slots[:, device * sentences : (device + 1) * sentences], gap)
        ],
        axis=1,
    )
    side_line = within(slot_line, 2) + jnp.where(slot_line < 0, 8, 0)
    pair_line = over(slot_line, 2)
    pairs = r.langs.shape[0]
    lang_line = r.langs[...].reshape(1, pairs).astype(FULL)
    lang_line = jnp.concatenate([lang_line, jnp.full((1, -pairs % 128), -1.0, FULL)], axis=1)
    lang_col = as_column(lang_line)
    same_lang = jnp.sum(jnp.where(lang_col == lang_line, 1.0, 0.0), axis=1, keepdims=True)
    per_pair = 1.0 / (2.0 * LANGS * same_lang)
    at_pair = iota((lang_line.shape[1], SLOT_ROWS), 0) == pair_line
    weight_line = jnp.sum(jnp.where(at_pair, per_pair, 0.0), axis=0, keepdims=True)
    r.pairs[0:1, :] = weight_line
    r.pairs[1:2, :] = pair_line.astype(FULL)
    r.pairs[2:3, :] = side_line.astype(FULL)
    r.pairs_col[:, 0:1] = as_column(weight_line)
    r.pairs_col[:, 1:2] = as_column(pair_line.astype(FULL))
    r.pairs_col[:, 2:3] = as_column(side_line.astype(FULL))
    move((moves_b, 6), (moves_c, 2))

    all_smalls().wait_recv()
    smalls = r.smalls[...].astype(FULL)
    r.vectors[:, 0:WIDTH] = jnp.concatenate(
        [smalls[:, at * 128 : at * 128 + depth] for at in range(CHIPS)], axis=1
    )
    r.up_bias[0:1, :] = jnp.concatenate(
        [
            smalls[8 + part : 9 + part, at * 128 : at * 128 + depth]
            for at in range(CHIPS)
            for part in range(deep // depth)
        ],
        axis=1,
    )

    def vector(index):
        return r.vectors[index : index + 1, :]

    r.qkv_bias[0:1, 0:WIDTH] = vector(0)
    r.qkv_bias[0:1, WIDTH : 2 * WIDTH] = jnp.zeros((1, WIDTH), FULL)
    r.qkv_bias[0:1, 2 * WIDTH : 3 * WIDTH] = vector(1)

    move((moves_a, 8), (moves_b, 8), (moves_c, 4))

    def first_row(source):
        code = jnp.where(r.rank[pl.ds(source, 1), :] >= 0.0, r.code[pl.ds(source, 1), :], 0.0)
        at_first = iota((PAD, TOKENS), 1) == iota((PAD, TOKENS), 0) * LONG
        found = jnp.sum(jnp.where(at_first, code, 0.0), axis=1, keepdims=True)
        row = found - jnp.floor(found * (1.0 / 2048)) * 2048.0 - 1.0
        r.found[GROUPS, pl.ds(pl.multiple_of(source * PAD, 16), PAD), 0:1] = row

    every(0, DEVICES, first_row)
    for group in range(GROUPS + 1):
        named = as_row(r.found[group, :, 0:1])
        by_row = iota((VOCAB_ROWS, SLOT_ROWS), 0).astype(FULL) == named
        r.by_row[:, group * SLOT_ROWS : (group + 1) * SLOT_ROWS] = by_row.astype(LOW)

    def order(tile):
        at = pl.ds(pl.multiple_of(tile * BLOCK, BLOCK), BLOCK)
        lanes = iota((BLOCK, GROUPS * SLOT_ROWS), 1).astype(FULL)
        r.qkv[at, 0 : GROUPS * SLOT_ROWS] = (r.slot_col[at, :] == lanes).astype(LOW)

    every(0, TOKENS // BLOCK, order)
    for group in range(GROUPS):
        slot_at = iota((SLOT_ROWS, TOKENS), 0) + group * SLOT_ROWS
        named = (slot_at.astype(FULL) == r.slot_line[0:1, :]).astype(LOW)
        r.slot_hot[group] = named
    moves_a[10]()
    moves_b[10]()
    finish_a()
    for quarter in range(4):
        rows_of(quarter).wait_recv()

    def embed(tile):
        at = pl.ds(pl.multiple_of(tile * BLOCK, BLOCK), BLOCK)
        replies = r.replies[:, :, at].reshape(GROUPS * SLOT_ROWS, BLOCK)
        r.embedded[:, at] = dot(r.qkv[:, 0 : GROUPS * SLOT_ROWS], replies).astype(LOW)

    every(0, WIDTH // BLOCK, embed)

    def project(tile):
        at = pl.ds(pl.multiple_of(tile * BLOCK, BLOCK), BLOCK)
        r.qkv[:, at] = (dot(r.embedded[...], r.wa[:, at]) + r.qkv_bias[0:1, at]).astype(LOW)

    move((moves_c, 6))
    every(0, 9, project)

    row_sent = within(iota((PAIR_ROWS, WIDTH), 0), PAD)
    row_head = over(iota((PAIR_ROWS, WIDTH), 0), PAD)
    lane_block = over(iota((PAIR_ROWS, WIDTH), 1), HEAD)
    in_head = row_head == lane_block
    seen = (row_sent == lane_block) & (r.valid_line[0:1, :] > 0.0)
    firsts = (iota((PAD, TOKENS), 1) == iota((PAD, TOKENS), 0) * LONG).astype(LOW)
    real_row = iota((PAD, 1), 0) < sentences

    def spread(rows):
        return jnp.where(in_head, jnp.concatenate([rows] * HEADS, axis=0), jnp.zeros((), LOW))

    def fold(tall):
        tall = jnp.where(in_head, tall, 0.0)
        return sum(tall[head * PAD : (head + 1) * PAD] for head in range(HEADS))

    keys, values = slice(WIDTH, 2 * WIDTH), slice(2 * WIDTH, 3 * WIDTH)
    embedded_cls = dot(firsts, r.embedded[...]).astype(LOW)
    query_cls = (dot(embedded_cls, r.wa[:, 0:WIDTH]) + vector(0)).astype(LOW)
    cls_scores = dot_turned(spread(query_cls), r.qkv[:, keys]) * scale
    cls_scores = jnp.where(seen, cls_scores, MASK_FLOOR)
    cls_peak = jnp.max(cls_scores, axis=1, keepdims=True)
    cls_exp = jnp.where(seen, jnp.exp(cls_scores - cls_peak), 0.0)
    cls_total = jnp.sum(cls_exp, axis=1, keepdims=True)
    cls_probs = cls_exp / jnp.where(cls_total > 0.0, cls_total, 1.0)
    probs_low = cls_probs.astype(LOW)
    r.probs[...] = cls_probs
    context_cls = fold(dot(probs_low, r.qkv[:, values])).astype(LOW)
    first_cls = (
        embedded_cls.astype(FULL)
        + dot(context_cls, r.wa[:, 3 * WIDTH : 4 * WIDTH])
        + vector(2)
    )
    normed_one, inverse_one = norm_parts(first_cls)
    r.normed_one[...] = normed_one
    hidden_cls = normed_one * vector(3) + vector(4)
    hidden_cls_low = hidden_cls.astype(LOW)
    early_here = r.early.at[here]
    early_here[:, 0:WIDTH] = hidden_cls_low
    early_here[:, WIDTH : 2 * WIDTH] = query_cls
    steps_u, drain_u = gather_steps(r.units, r.gather_send.at[0], r.gather_recv.at[0])
    steps_e, drain_e = gather_steps(r.early, r.gather_send.at[1], r.gather_recv.at[1])
    steps_d, drain_d = gather_steps(r.downs, r.gather_send.at[2], r.gather_recv.at[2])
    steps_a, drain_a2 = gather_steps(r.attends, r.gather_send.at[3], r.gather_recv.at[3])
    steps_q, drain_q = gather_steps(r.queries, r.gather_send.at[4], r.gather_recv.at[4])
    steps_e[0]()

    def attend(unit):
        rows = pl.ds(pl.multiple_of(unit * half_block, half_block), half_block)
        lane_head = over(iota((half_block, BLOCK), 1), HEAD)
        bias = r.block_bias[...] + r.valid_bias[0:1, rows]

        def part(which, lane):
            return r.qkv[rows, which * WIDTH + lane : which * WIDTH + lane + BLOCK]

        for lane in range(0, WIDTH, BLOCK):
            query = part(0, lane) * jnp.asarray(scale, LOW)
            key, value = part(1, lane), part(2, lane)
            stacked = jnp.concatenate(
                [jnp.where(lane_head == head, query, jnp.zeros((), LOW)) for head in range(4)],
                axis=0,
            )
            scores = dot_turned(stacked, key) + bias
            shifted = jnp.exp(scores - jnp.max(scores, axis=1, keepdims=True))
            probs = shifted * (1.0 / jnp.sum(shifted, axis=1, keepdims=True))
            mixed = dot(probs.astype(LOW), value)
            result = mixed[0:half_block]
            for head in range(1, 4):
                result = jnp.where(
                    lane_head == head, mixed[head * half_block : (head + 1) * half_block], result
                )
            r.context[rows, lane : lane + BLOCK] = result.astype(LOW)

    def open_tile(tile):
        at = pl.ds(pl.multiple_of(tile * BLOCK, BLOCK), BLOCK)
        attended = dot(r.context[at, :], r.wa[:, 3 * WIDTH : 4 * WIDTH]) + vector(2)
        normed, _ = norm_parts(r.embedded[at, :].astype(FULL) + attended)
        hidden = normed * vector(3) + vector(4)
        r.context[at, :] = hidden.astype(LOW)
        r.table_full[at, :] = hidden + vector(5)

    most = SLOT_ROWS
    rest_at = pl.ds(most, TOKENS - most)

    def up_product(part):
        at = pl.ds(pl.multiple_of(part * BLOCK, BLOCK), BLOCK)
        return dot(r.context[...], r.wb[:, at]) + r.up_bias[0:1, at]

    def feed_up(part, last=False):
        active = gelu(r.tile_up[...]).astype(LOW)
        if not last:
            r.tile_up[...] = up_product(part + 1)
        lanes = pl.ds(pl.multiple_of(lax.rem(part, 4) * BLOCK, BLOCK), BLOCK)
        r.chosen[lax.div(part, 4), :, lanes] = active[:most]
        rest = pl.ds(pl.multiple_of(lax.div(part, 6) * BLOCK, BLOCK), BLOCK)
        lanes = pl.ds(pl.multiple_of(lax.rem(part, 6) * BLOCK, BLOCK), BLOCK)
        r.slopes[rest, lanes] = active[most:]

    def feed_down(part):
        lanes = pl.ds(pl.multiple_of(part * BLOCK, BLOCK), BLOCK)
        total = r.table_full[0:most, lanes]
        for group in range(GROUPS):
            rows = slice(group * VOCAB_ROWS, (group + 1) * VOCAB_ROWS)
            total = total + dot(r.chosen[group], r.wc[rows, lanes])
        r.table_full[0:most, lanes] = total

    def feed_rest(part):
        lanes = pl.ds(pl.multiple_of(part * BLOCK, BLOCK), BLOCK)
        low_part = dot(r.slopes[0:BLOCK, :], r.wc[0 : WIDE // 2, lanes])
        high_part = dot(r.slopes[BLOCK : 2 * BLOCK, :], r.wc[WIDE // 2 :, lanes])
        r.table_full[rest_at, lanes] += low_part + high_part

    def layer_copy(tile):
        at = pl.ds(pl.multiple_of(tile * BLOCK, BLOCK), BLOCK)
        return pltpu.make_async_copy(r.context.at[at], r.layer_out.at[at], r.out_sem.at[tile])

    def close_tile(tile):
        at = pl.ds(pl.multiple_of(tile * BLOCK, BLOCK), BLOCK)
        normed, _ = norm_parts(r.table_full[at, :])
        out = normed * vector(6) + vector(7)
        r.context[at, :] = (out * r.valid_col[at, :]).astype(LOW)
        layer_copy(tile).start()

    finish_b()
    r.hidden_cls[...] = hidden_cls_low

    def up_part(part):
        at = pl.ds(pl.multiple_of(part * WIDTH, BLOCK), WIDTH)
        active, slope = gelu_parts(dot(r.hidden_cls[...], r.wb[:, at]) + r.up_bias[0:1, at])
        r.active_cls[:, at] = active.astype(LOW)
        r.slope_cls[:, at] = slope

    every(0, WIDE // WIDTH, up_part)
    steps_e[1]()

    def attend_step(unit):
        attend(unit)
        pl.when(unit == 1)(partial(move, (moves_c, 8)))
        pl.when(unit == 3)(moves_c[10])
        pl.when(unit == 4)(steps_e[2])

    every(0, 6, attend_step)
    finish_c()

    def pack_tall(target, first_row, act):
        def run(part):
            window = jnp.minimum(lax.div(part * 2 * depth, 128) * 128, WIDTH - BLOCK)
            shape = (BLOCK, BLOCK)
            lane = within(iota(shape, 1), 128)
            column = over(iota(shape, 1), 128) * depth + lane + (part * 2 * depth - window)
            select = ((iota(shape, 0) == column) & (lane < depth)).astype(LOW)
            taken = dot(r.tall[:, pl.ds(pl.multiple_of(window, 128), BLOCK)], select)

            def beside(low, high):
                return [
                    low[:, one * 128 : (one + 1) * 128]
                    + pltpu.roll(high[:, one * 128 : (one + 1) * 128], depth, 1)
                    for one in range(2)
                ]

            for half in range(CORES):
                base = half * PAIR_ROWS // 2
                both = beside(taken[base : base + 48], taken[base + 48 : base + 96])
                for one in range(2):
                    at = half * CHIPS + 2 * part + one
                    target[at, first_row : first_row + 48, :] = act(
                        2 * part + one, both[one]
                    ).astype(LOW)
            if first_row:
                left = beside(taken[PAIR_ROWS : PAIR_ROWS + PAD], taken[PAIR_ROWS + PAD :])
                for half in range(CORES):
                    for one in range(2):
                        target[half * CHIPS + 2 * part + one, 0:PAD, :] = left[one].astype(LOW)

        return run

    def pack_coefs(coefs):
        shape = (PAIR_ROWS, GROUPS * 128)
        folds = over(iota(shape, 0), PAD) + over(iota(shape, 1), 128) * PAD == within(
            iota(shape, 1), 128
        )
        lanes = contract(coefs, folds.astype(LOW), 0, 0).astype(LOW)
        total = None
        for group in range(GROUPS):
            part = dot(r.slot_hot[group], lanes[:, group * 128 : (group + 1) * 128])
            total = part if total is None else total + part
        return total.astype(LOW).reshape(DEVICES, PAD, 128)


    def down_part(part):
        at = pl.ds(pl.multiple_of(part * BLOCK, BLOCK), BLOCK)
        r.wide_cls[:, at] = dot(r.active_cls[...], r.wc[:, at])

    every(0, WIDTH // BLOCK, down_part)
    down_pre = r.wide_cls[:, 0:WIDTH] + vector(5)
    normed_two, inverse_two = norm_parts(hidden_cls + down_pre)
    summary = normed_two * vector(6) + vector(7)
    magnitude = jnp.sqrt(jnp.sum(summary * summary, axis=-1, keepdims=True) + EPSILON)
    unit = jnp.where(real_row, summary / magnitude, 0.0)
    r.units[here] = unit.astype(LOW)

    steps_u[0]()
    r.tall[0:PAIR_ROWS, :] = dot(probs_low, r.embedded[...]).astype(LOW)
    r.tall[PAIR_ROWS : PAIR_ROWS + PAD, :] = context_cls
    r.tall[PAIR_ROWS + PAD :, :] = embedded_cls
    pack_one = pack_tall(r.mail_one, PAD, lambda at, both: both)

    def pack_one_step(part):
        pack_one(part)
        pl.when(part == 0)(steps_u[1])
        pl.when(part == 4)(steps_u[2])

    every(0, CHIPS // 2, pack_one_step)
    r.mail_one[:, 64:80, :] = pack_coefs(probs_low)
    steps_u[3]()

    def post_one(box, got, index, step):
        other, to_core, to_chip = peer(step)
        remote(
            box.at[other], got.at[me], r.one_send.at[index], r.one_recv.at[index], to_core, to_chip
        ).start()

    def post(box, got, index):
        every(1, DEVICES, partial(post_one, box, got, index))
        got[me] = box[me]


    r.got_one[me] = r.mail_one[me]

    def open_step(tile):
        open_tile(tile)
        pl.when(tile == 0)(steps_e[3])
        pl.when(tile == 2)(steps_u[4])

    def feed_step(steps, part):
        feed_up(part)
        for index in range(4):
            step = 4 * part + index + 1
            pl.when(step < DEVICES)(partial(post_one, r.mail_one, r.got_one, 1, step))
        for index, step in steps:
            pl.when(part == index)(step)

    first_parts, parts = 4, WIDE // BLOCK
    every(0, TOKENS // BLOCK, open_step)
    r.tile_up[...] = up_product(0)
    every(0, first_parts, partial(feed_step, [(1, steps_u[5]), (2, steps_e[4]), (3, steps_e[5])]))

    units = r.units[...].reshape(SLOT_ROWS, WIDTH)
    weight_row, pair_row, side_row = r.pairs[0:1, :], r.pairs[1:2, :], r.pairs[2:3, :]

    def pair_scores(rows, pair_col, side_col):
        opposite = side_col + side_row == 1.0
        partner = opposite & (pair_col == pair_row)
        raw = SCORE_SCALE * dot_turned(rows, units)
        shifted = jnp.where(partner, raw - SCORE_SCALE * MARGIN_WIDTH, raw)
        return jnp.where(opposite, shifted, MASK_FLOOR), partner

    every_score, every_partner = pair_scores(
        units, r.pairs_col[:, 1:2], r.pairs_col[:, 2:3]
    )
    peak_row = jnp.max(every_score, axis=0, keepdims=True)
    log_row = peak_row + jnp.log(
        jnp.sum(jnp.exp(every_score - peak_row), axis=0, keepdims=True)
    )
    picked_row = jnp.sum(jnp.where(every_partner, every_score, 0.0), axis=0, keepdims=True)
    r.loss[...] = jnp.sum(weight_row * (log_row - picked_row), axis=1, keepdims=True)

    rows_here = pl.ds(pl.multiple_of(me * PAD, 16), PAD)
    own_score, own_partner = pair_scores(
        r.units[here], r.pairs_col[rows_here, 1:2], r.pairs_col[rows_here, 2:3]
    )
    own_partner = own_partner.astype(FULL)
    own_peak = jnp.max(own_score, axis=1, keepdims=True)
    own_exp = jnp.exp(own_score - own_peak)
    own_share = own_exp / jnp.sum(own_exp, axis=1, keepdims=True)
    by_row = (r.pairs_col[rows_here, 0:1] * (own_share - own_partner)).astype(LOW)
    by_column = (weight_row * (jnp.exp(own_score - log_row) - own_partner)).astype(LOW)
    unit_grad = SCORE_SCALE * (dot(by_row, units) + dot(by_column, units))
    along = jnp.sum(unit * unit_grad, axis=-1, keepdims=True)
    summary_grad = (unit_grad - unit * along) / magnitude

    residual_grad, grad_g2, grad_s2 = norm_back_parts(
        summary_grad, normed_two, inverse_two, vector(6)
    )
    down_grad = residual_grad.astype(LOW)
    r.downs[here] = down_grad
    steps_d[0]()
    r.hidden_cls[...] = down_grad

    def up_back(part):
        at = pl.ds(pl.multiple_of(part * WIDTH, BLOCK), WIDTH)
        act_grad = dot_turned(r.hidden_cls[...], r.wc[at, :])
        r.active_cls[:, at] = (act_grad * r.slope_cls[:, at]).astype(LOW)

    every(0, WIDE // WIDTH, up_back)
    steps_d[1]()

    def hidden_back(part):
        at = pl.ds(pl.multiple_of(part * BLOCK, BLOCK), BLOCK)
        r.wide_cls[:, at] = dot_turned(r.active_cls[...], r.wb[at, :])

    every(0, WIDTH // BLOCK, hidden_back)
    hidden_grad = r.wide_cls[:, 0:WIDTH] + residual_grad
    first_grad, grad_g1, grad_s1 = norm_back_parts(
        hidden_grad, r.normed_one[...], inverse_one, vector(3)
    )
    attend_grad = first_grad.astype(LOW)
    context_grad = dot_turned(attend_grad, r.wa[:, 3 * WIDTH : 4 * WIDTH]).astype(LOW)
    attend_here = r.attends.at[here]
    attend_here[:, 0:WIDTH] = attend_grad
    attend_here[:, WIDTH : 2 * WIDTH] = context_grad
    steps_a[0]()
    steps_d[2]()
    context_tall = spread(context_grad)
    probs = r.probs[...]
    prob_grad = dot_turned(context_tall, r.qkv[:, values])
    inner = jnp.sum(probs * prob_grad, axis=1, keepdims=True)
    score_grad = (probs * (prob_grad - inner)).astype(LOW)
    steps_a[1]()
    r.mail_two[:, 48:64, :] = pack_coefs(score_grad)
    query_grad = (fold(dot(score_grad, r.qkv[:, keys])) * scale).astype(LOW)
    probs_total = jnp.sum(probs_low.astype(FULL), axis=1, keepdims=True)
    grad_bvalue = jnp.sum(probs_total * context_tall.astype(FULL), axis=0, keepdims=True)
    grad_bquery = jnp.sum(query_grad.astype(FULL), axis=0, keepdims=True)
    r.queries[here] = query_grad
    own_sums = jnp.concatenate(
        [jnp.zeros((2 * depth, WIDTH), FULL)]
        + [grad_bquery, grad_bvalue, grad_g1, grad_s1, grad_g2, grad_s2]
        + [jnp.zeros((128 - 2 * depth - 6, WIDTH), FULL)],
        axis=0,
    )
    r.own_sums[...] = jnp.transpose(own_sums)
    steps_q[0]()
    steps_a[2]()
    r.tall[0:PAIR_ROWS, :] = (dot(score_grad, r.embedded[...]) * scale).astype(LOW)

    def with_sums(at, both):
        return both + r.own_sums[pl.ds(pl.multiple_of(at * depth, 16), depth), :]

    every(0, CHIPS // 2, pack_tall(r.mail_two, 0, with_sums))
    steps_q[1]()
    post(r.mail_two, r.got_two, 2)

    def all_rows(buffer, start, width=WIDTH):
        return buffer[:, :, :, :, start : start + width].reshape(SLOT_ROWS, width)

    quarter_rows_count = quarter_size * PAD

    def from_sent(quarter):
        span = pl.ds(pl.multiple_of(quarter * quarter_rows_count, 128), quarter_rows_count)
        shape = (GROUPS * quarter_rows_count, quarter_rows_count)
        lanes = (iota(shape, 1) + quarter * quarter_rows_count).astype(FULL)
        named = r.found[0:GROUPS, span, 1:2].reshape(GROUPS * quarter_rows_count, 1)
        return (named == lanes).astype(LOW), span

    def quarter_part(buffer, quarter, start):
        planes = pl.ds(lax.rem(quarter, 2) * 2, 2)
        part = buffer[lax.div(quarter, 2), planes, :, :, start : start + BLOCK]
        return part.reshape(quarter_rows_count, BLOCK)

    def widened(coefs, group, start):
        lanes = iota((128, BLOCK), 0) == over(iota((128, BLOCK), 1) + start, HEAD) + group * PAD
        return dot(coefs, lanes.astype(LOW))

    half_wide = WIDE // 2

    def slope_tile(part):
        at = pl.ds(pl.multiple_of(core * half_wide + part * BLOCK, BLOCK), BLOCK)
        up_pre = dot(all_rows(r.early, 0), r.wb[:, at]) + r.up_bias[0:1, at]
        _, slope = gelu_parts(up_pre)
        r.slopes[:, pl.ds(pl.multiple_of(part * BLOCK, BLOCK), BLOCK)] = slope.astype(LOW)

    def slot_queries(quarter):
        sents, span = from_sent(quarter)
        for start in range(0, WIDTH, BLOCK):
            rows = dot(sents, quarter_part(r.early, quarter, WIDTH + start)).astype(LOW)
            rows = rows.reshape(GROUPS, quarter_rows_count, BLOCK)
            r.slot_query[:, span, start : start + BLOCK] = rows

    def activate():
        at = pl.ds(pl.multiple_of(chip // 2 * 2 * deep, 128), 2 * deep)
        up_pre = dot(all_rows(r.early, 0), r.wb[:, at]) + r.up_bias[0:1, at]
        r.active_turned[...] = jnp.transpose(gelu(up_pre)).astype(LOW)
        r.hidden_turned[...] = jnp.transpose(all_rows(r.early, 0))

    rest = [steps_d[3], steps_a[3], steps_q[2], steps_d[4], steps_a[4]]
    rest = [(first_parts + index, step) for index, step in enumerate(rest)]
    every(first_parts, parts - 1, partial(feed_step, rest))
    feed_up(parts - 1, last=True)

    def rest_step(part):
        feed_rest(part)
        for index, step in enumerate([steps_q[3], steps_d[5], steps_a[5]]):
            pl.when(part == index)(step)

    every(0, WIDTH // BLOCK, rest_step)
    steps_q[4]()
    every(0, WIDTH // BLOCK, feed_down)
    every(0, TOKENS // BLOCK, close_tile)
    every(0, 4, slot_queries)
    every(0, 6, slope_tile)
    activate()

    all_but_one(r.got_one, 1).wait_recv()
    def slot_probs(group):
        got_probs = r.got_one[:, 64:80, :].reshape(SLOT_ROWS, 128)
        for start in range(0, WIDTH, BLOCK):
            r.replies[group, :, start : start + BLOCK] = widened(got_probs, group, start).astype(LOW)

    def slot_values(quarter):
        sents, span = from_sent(quarter)
        for start in range(0, WIDTH, BLOCK):
            lanes = slice(start, start + BLOCK)
            rows = dot(sents, quarter_part(r.attends, quarter, WIDTH + start))
            rows = rows.reshape(GROUPS, quarter_rows_count, BLOCK)
            rows = r.replies[:, span, lanes].astype(FULL) * rows
            r.replies[:, span, lanes] = rows.astype(LOW)

    every(0, GROUPS, slot_probs)
    every(0, 4, slot_values)

    def head_products(got, first_row, right, start, target):
        def one_head(head):
            lane = core * (WIDTH // 2) + lax.div(head, 2) * 128
            pair_rows = right[:, :, :, :, pl.ds(pl.multiple_of(start + lane, 128), 128)]
            row = pl.ds(pl.multiple_of(first_row + lax.rem(head, 3) * PAD, 16), PAD)
            block_rows = got[:, row, :].reshape(SLOT_ROWS, 128)
            r.product[...] = contract(block_rows, pair_rows.reshape(SLOT_ROWS, 128), 0, 0)
            part = r.product[pl.ds(pl.multiple_of(lax.div(head, 3) * depth, 16), depth), :]
            at = pl.ds(pl.multiple_of(lane, 128), 128)
            own_lanes = over(iota((depth, 128), 1), HEAD) == lax.rem(head, 2)
            target[:, at] = jnp.where(own_lanes, part, target[:, at])

        every(0, HEADS // 2, one_head)

    def half_of(ref, at_core):
        half = ref.shape[1] // 2
        return ref.at[:, pl.ds(pl.multiple_of(at_core * half, 128), half)]

    def half_copy(index, ref, at_core):
        part = half_of(ref, at_core)
        return remote(part, part, r.half_send.at[index], r.half_recv.at[index], 1 - core, chip)

    own_half = pl.ds(pl.multiple_of(core * (WIDTH // 2), 128), WIDTH // 2)
    r.g_wv[:, own_half] = jnp.zeros((depth, WIDTH // 2), FULL)
    r.g_wk[:, own_half] = jnp.zeros((depth, WIDTH // 2), FULL)
    head_products(r.got_one, PAD, r.attends, WIDTH, r.g_wv)
    half_copy(0, r.g_wv, core).start()

    downs = r.downs[...].reshape(SLOT_ROWS, WIDTH)
    attends = all_rows(r.attends, 0)

    def up_tile(part):
        at = pl.ds(pl.multiple_of(core * half_wide + part * BLOCK, BLOCK), BLOCK)
        slope = r.slopes[:, pl.ds(pl.multiple_of(part * BLOCK, BLOCK), BLOCK)].astype(FULL)
        up_all = (dot_turned(r.downs[...].reshape(SLOT_ROWS, WIDTH), r.wc[at, :]) * slope)
        up_all = up_all.astype(LOW)
        r.g_wup[0:depth, at] = dot(r.hidden_turned[mine, :], up_all)
        total = jnp.sum(up_all.astype(FULL), axis=0, keepdims=True)
        r.g_wup[depth : depth + 8, at] = jnp.broadcast_to(total, (8, BLOCK))

    every(0, half_wide // BLOCK, up_tile)
    half_copy(1, r.g_wup, core).start()
    r.g_wdown[...] = dot(r.active_turned[pl.ds(pl.multiple_of(chip % 2 * deep, 16), deep), :], downs)
    r.left_turned[...] = jnp.transpose(r.got_one[:, 0:PAD, :].reshape(SLOT_ROWS, 128))
    r.g_wo[...] = dot(r.left_turned[0:depth, :], attends)
    own_lanes = (iota((WIDTH, 128), 0) == chip * depth + iota((WIDTH, 128), 1)).astype(LOW)

    def own_part(rows, select):
        total = None
        for _ in range(3):
            part = rows.astype(LOW)
            rows = rows - part.astype(FULL)
            picked = dot(part, select)
            total = picked if total is None else total + picked
        return total

    for quarter in range(4):
        rows_of(quarter).wait_send()
    all_but_one(r.got_two, 2).wait_recv()

    def slot_grads(group):
        got_scores = r.got_two[:, 48:64, :].reshape(SLOT_ROWS, 128)
        for start in range(0, WIDTH, BLOCK):
            lanes = slice(start, start + BLOCK)
            rows = r.slot_query[group, :, lanes].astype(FULL)
            rows = widened(got_scores, group, start) * rows * scale
            r.slot_query[group, :, lanes] = rows.astype(LOW)
        for start in range(0, WIDTH, BLOCK):
            lanes = slice(start, start + BLOCK)
            row_grad = dot_turned(r.slot_query[group], r.wa[lanes, keys])
            row_grad = row_grad + dot_turned(r.replies[group], r.wa[lanes, values])
            r.rows[group, :, lanes] = row_grad.astype(LOW)

    every(0, GROUPS, slot_grads)
    steps_q[5]()
    query_grads = all_rows(r.queries, 0)
    extra = dot_turned(query_grads, r.wa[:, 0:WIDTH]) + attends.astype(FULL)
    r.extra[...] = extra.astype(LOW)
    r.g_wq[...] = dot(r.left_turned[depth : 2 * depth, :], query_grads)

    half_rows = VOCAB_ROWS // 2

    def table_copy(tile):
        at = pl.ds(pl.multiple_of(tile * half_rows, BLOCK), half_rows)
        return pltpu.make_async_copy(
            r.table_full.at[at], r.table_grad.at[at], r.table_sem.at[tile]
        )

    def table_tile(tile):
        at = pl.ds(pl.multiple_of(tile * half_rows, BLOCK), half_rows)
        for start in range(0, WIDTH, BLOCK):
            lanes = slice(start, start + BLOCK)
            slot_rows = r.rows[:, :, lanes].reshape(GROUPS * SLOT_ROWS, BLOCK)
            r.table_full[at, lanes] = dot(r.by_row[at, 0 : GROUPS * SLOT_ROWS], slot_rows) + dot(
                r.by_row[at, GROUPS * SLOT_ROWS :], r.extra[:, lanes]
            )
        table_copy(tile).start()

    every(0, 2, table_tile)
    head_products(r.got_two, 0, r.early, WIDTH, r.g_wk)
    half_copy(2, r.g_wk, core).start()

    down_total = jnp.sum(downs.astype(FULL), axis=0, keepdims=True)
    attend_total = jnp.sum(attends.astype(FULL), axis=0, keepdims=True)
    sums = jnp.sum(r.got_two[:, 0:48, :].astype(FULL), axis=0)
    sums = jnp.concatenate([sums, jnp.zeros((128 - 48, 128), FULL)], axis=0)
    stacked = jnp.concatenate([attend_total, down_total, jnp.zeros((6, WIDTH), FULL)], axis=0)
    r.g_small[8:16, 0:128] = own_part(stacked, own_lanes)
    r.g_small[0:8, 0:128] = jnp.transpose(sums)[2 * depth : 2 * depth + 8, :]
    r.g_small[0:16, 128:BLOCK] = jnp.zeros((PAD, BLOCK - 128), FULL)
    half_copy(1, r.g_wup, 1 - core).wait_recv()
    up_lanes = (iota((WIDE, BLOCK), 0) == chip * deep + iota((WIDE, BLOCK), 1)).astype(LOW)
    r.g_small[16:24, :] = own_part(r.g_wup[depth : depth + 8, :], up_lanes)

    half_copy(0, r.g_wv, 1 - core).wait_recv()
    half_copy(2, r.g_wk, 1 - core).wait_recv()
    for index, ref in enumerate([r.g_wv, r.g_wup, r.g_wk]):
        half_copy(index, ref, core).wait_send()

    for index, ref in enumerate([r.every_ids, r.got_one, r.got_two]):
        all_but_one(ref, index).wait_send()
    all_smalls().wait_send()
    for end in [drain_a, drain_b, drain_c, drain_u, drain_e, drain_d, drain_a2, drain_q]:
        end()
    every(0, TOKENS // BLOCK, lambda tile: layer_copy(tile).wait())
    every(0, 2, lambda tile: table_copy(tile).wait())


def layer(inputs):
    dma = pltpu.SemaphoreType.DMA
    vmem = pl.BlockSpec(memory_space=pltpu.VMEM)
    anywhere = pl.BlockSpec(memory_space=pl.ANY)
    depth, deep = WIDTH // CHIPS, WIDE // CHIPS

    def gathered(width):
        return pltpu.VMEM((CORES, PLANES, LINES, PAD, width), LOW)

    outputs = dict(
        layer_out=((TOKENS, WIDTH), LOW),
        table_grad=((VOCAB_ROWS, WIDTH), FULL),
        g_wq=((depth, WIDTH), FULL),
        g_wk=((depth, WIDTH), FULL),
        g_wv=((depth, WIDTH), FULL),
        g_wo=((depth, WIDTH), FULL),
        g_wup=((depth + 8, WIDE), FULL),
        g_wdown=((deep, WIDTH), FULL),
        g_small=((24, BLOCK), FULL),
        loss=((1, 1), FULL),
    )
    scratch = dict(
        ids=pltpu.VMEM((8, 128), jnp.int32),
        every_ids=pltpu.VMEM((DEVICES, 8, 128), jnp.int32),
        rank=pltpu.VMEM((DEVICES, TOKENS), FULL),
        code=pltpu.VMEM((DEVICES, TOKENS), FULL),
        found=pltpu.VMEM((GROUPS + 1, SLOT_ROWS, 2), FULL),
        block_bias=pltpu.VMEM((2 * BLOCK, BLOCK // 2), FULL),
        valid_bias=pltpu.VMEM((8, TOKENS), FULL),
        slot_col=pltpu.VMEM((TOKENS, 1), FULL),
        slot_line=pltpu.VMEM((8, TOKENS), FULL),
        valid_col=pltpu.VMEM((TOKENS, 1), FULL),
        valid_line=pltpu.VMEM((8, TOKENS), FULL),
        pairs=pltpu.VMEM((8, SLOT_ROWS), FULL),
        pairs_col=pltpu.VMEM((SLOT_ROWS, 128), FULL),
        vectors=pltpu.VMEM((PAD, WIDTH), FULL),
        up_bias=pltpu.VMEM((8, WIDE), FULL),
        qkv_bias=pltpu.VMEM((8, 3 * WIDTH), FULL),
        smalls=pltpu.VMEM((PAD, CHIPS * 128), LOW),
        wa=pltpu.VMEM((WIDTH, 4 * WIDTH), LOW),
        wb=pltpu.VMEM((WIDTH, WIDE), LOW),
        wc=pltpu.VMEM((WIDE, WIDTH), LOW),
        chosen=pltpu.VMEM((GROUPS, SLOT_ROWS, VOCAB_ROWS), LOW),
        by_row=pltpu.VMEM((VOCAB_ROWS, (GROUPS + 1) * SLOT_ROWS), LOW),
        rows=pltpu.VMEM((GROUPS, SLOT_ROWS, WIDTH), LOW),
        replies=pltpu.VMEM((GROUPS, SLOT_ROWS, WIDTH), LOW),
        slot_query=pltpu.VMEM((GROUPS, SLOT_ROWS, WIDTH), LOW),
        extra=pltpu.VMEM((SLOT_ROWS, WIDTH), LOW),
        hidden_cls=pltpu.VMEM((PAD, WIDTH), LOW),
        active_cls=pltpu.VMEM((PAD, WIDE), LOW),
        slope_cls=pltpu.VMEM((PAD, WIDE), FULL),
        wide_cls=pltpu.VMEM((PAD, WIDTH), FULL),
        tall=pltpu.VMEM((PAIR_ROWS + 2 * PAD, WIDTH), LOW),
        own_sums=pltpu.VMEM((WIDTH, 128), FULL),
        product=pltpu.VMEM((128, 128), FULL),
        slot_hot=pltpu.VMEM((GROUPS, SLOT_ROWS, TOKENS), LOW),
        tile_up=pltpu.VMEM((TOKENS, BLOCK), FULL),
        embedded=pltpu.VMEM((TOKENS, WIDTH), LOW),
        qkv=pltpu.VMEM((TOKENS, 3 * WIDTH), LOW),
        context=pltpu.VMEM((TOKENS, WIDTH), LOW),
        table_full=pltpu.VMEM((VOCAB_ROWS, WIDTH), FULL),
        probs=pltpu.VMEM((PAIR_ROWS, TOKENS), FULL),
        normed_one=pltpu.VMEM((PAD, WIDTH), FULL),
        units=gathered(WIDTH),
        early=gathered(2 * WIDTH),
        downs=gathered(WIDTH),
        attends=gathered(2 * WIDTH),
        queries=gathered(WIDTH),
        slopes=pltpu.VMEM((SLOT_ROWS, WIDE // 2), LOW),
        hidden_turned=pltpu.VMEM((WIDTH, SLOT_ROWS), LOW),
        active_turned=pltpu.VMEM((2 * deep, SLOT_ROWS), LOW),
        left_turned=pltpu.VMEM((128, SLOT_ROWS), LOW),
        mail_one=pltpu.VMEM((DEVICES, 80, 128), LOW),
        got_one=pltpu.VMEM((DEVICES, 80, 128), LOW),
        mail_two=pltpu.VMEM((DEVICES, 64, 128), LOW),
        got_two=pltpu.VMEM((DEVICES, 64, 128), LOW),
        rows_send=dma((4,)),
        rows_recv=dma((4,)),
        one_send=dma((4,)),
        one_recv=dma((4,)),
        small_send=dma((1,)),
        small_recv=dma((1,)),
        weight_send=dma((3, 7)),
        weight_recv=dma((3, 18)),
        gather_send=dma((5, 13)),
        gather_recv=dma((5, 13)),
        half_send=dma((3,)),
        half_recv=dma((3,)),
        out_sem=dma((TOKENS // BLOCK,)),
        table_sem=dma((2,)),
    )
    names = INPUTS + OUTPUTS + list(scratch)
    return pl.pallas_call(
        partial(layer_kernel, names),
        out_shape=tuple(jax.ShapeDtypeStruct(*outputs[name]) for name in OUTPUTS),
        in_specs=[vmem] * len(INPUTS),
        out_specs=(anywhere, anywhere) + (vmem,) * (len(OUTPUTS) - 2),
        scratch_shapes=list(scratch.values()),
        compiler_params=pltpu.CompilerParams(
            collective_id=0, has_side_effects=True, vmem_limit_bytes=VMEM_LIMIT
        ),
        name="layer",
    )(*inputs)


def finish_kernel(count, *refs):
    large, (small, loss), outs = refs[:count], refs[count : count + 2], refs[count + 2 : -1]
    sems = refs[-1]
    copies = []
    for index, (source, target) in enumerate(zip(large, outs)):
        part = source if source.shape == target.shape else source.at[: target.shape[0]]
        copies.append(pltpu.make_async_copy(part, target, sems.at[index]))
        copies[-1].start()
    for row, target in zip([0, 1, 8, 2, 3, 16, 9, 4, 5], outs[count : count + 9]):
        size = target.shape[0]
        target[...] = small[row : row + 1, 0:size].reshape(size)
    outs[-1][...] = loss[...].reshape(1)
    for one in copies:
        one.wait()


def finish(results):
    vmem = pl.BlockSpec(memory_space=pltpu.VMEM)
    anywhere = pl.BlockSpec(memory_space=pl.ANY)
    depth, deep = WIDTH // CHIPS, WIDE // CHIPS
    count = len(results) - 2
    shapes = [(one.shape, one.dtype) for one in results[:count]]
    shapes[6] = ((depth, WIDE), FULL)
    shapes += [((depth,), FULL)] * 5 + [((deep,), FULL)] + [((depth,), FULL)] * 3
    shapes.append(((1,), FULL))
    return pl.pallas_call(
        partial(finish_kernel, count),
        out_shape=tuple(jax.ShapeDtypeStruct(*one) for one in shapes),
        in_specs=[vmem] * (count + 2),
        out_specs=(anywhere,) * count + (vmem,) * 10,
        scratch_shapes=[pltpu.SemaphoreType.DMA((count,))],
        name="finish",
    )(*results)


def block_body(
    table,
    token_ids,
    sent_lengths,
    pair_slot,
    pair_lang,
    *parameters,
):
    results = finish(layer((table, token_ids, sent_lengths, pair_slot, pair_lang) + parameters))
    layer_out, table_grad, g_wq, g_wk, g_wv, g_wo, g_wup, g_wdown = results[:8]
    g_bq, g_bv, g_bo, g_g1, g_s1, g_bup, g_bdown, g_g2, g_s2, loss = results[8:]
    return (
        layer_out.reshape(token_ids.shape + (WIDTH,)),
        loss.reshape(()),
        table_grad,
        g_wq,
        g_bq,
        g_wk,
        g_wv,
        g_bv,
        g_wo,
        g_bo,
        g_g1,
        g_s1,
        g_wup,
        g_bup,
        g_wdown,
        g_bdown,
        g_g2,
        g_s2,
    )


def solution(mesh):
    in_specs = (
        P(("dp", "fsdp"), None),
        P(("dp", "fsdp"), None),
        P(("dp", "fsdp")),
        P(),
        P(),
        P("fsdp", None),
        P("fsdp"),
        P("fsdp", None),
        P("fsdp", None),
        P("fsdp"),
        P("fsdp", None),
        P("fsdp"),
        P("fsdp"),
        P("fsdp"),
        P("fsdp", None),
        P("fsdp"),
        P("fsdp", None),
        P("fsdp"),
        P("fsdp"),
        P("fsdp"),
    )
    out_specs = (
        P(("dp", "fsdp"), None, None),
        P(),
        P(("dp", "fsdp"), None),
        P("fsdp", None),
        P("fsdp"),
        P("fsdp", None),
        P("fsdp", None),
        P("fsdp"),
        P("fsdp", None),
        P("fsdp"),
        P("fsdp"),
        P("fsdp"),
        P("fsdp", None),
        P("fsdp"),
        P("fsdp", None),
        P("fsdp"),
        P("fsdp"),
        P("fsdp"),
    )
    sizes = dict(mesh.shape)
    body = general_body
    if sizes["dp"] == CORES and sizes["fsdp"] == CHIPS:
        body = block_body
    return jax.shard_map(body, mesh=mesh, in_specs=in_specs, out_specs=out_specs, check_vma=False)
```
